32 devices in a mesh: batch: 4 (over y, core), seq: 8 (over z, x).
Axes of the slice: x: 2, y: 2, z: 4, core: 2. Of those that a mesh axis runs over, the one named last changes fastest.
Arguments:
- block_input: bfloat16 [4, 2048, 2048], P('batch', 'seq'), may hold values from -6 to 6
- out_grad: bfloat16 [4, 2048, 2048], P('batch', 'seq'), may hold values from -10 to 10
- norm_gains: float32 [2, 2048], P(None, ('batch', 'seq')), may hold values from 0 to 6
- mixer_weight: float32 [2048, 7680], P(('batch', 'seq')), may hold values from -1 to 1
- gate_weight: float32 [2560, 320], P(('batch', 'seq')), may hold values from -0.25 to 0.25
- chan_params: float32 [8, 2560], P(None, ('batch', 'seq')), may hold values from -3 to 16
- mlp_weight: float32 [2048, 18432], P(('batch', 'seq')), may hold values from -1 to 1
- first_gains: float32 [2, 2048], P(None, ('batch', 'seq')), may hold values from -0.00061035156 to 0.00061035156
- first_mixer: float32 [2048, 7680], P(('batch', 'seq')), may hold values from -0.00021362305 to 0.00021362305
- first_gate: float32 [2560, 320], P(('batch', 'seq')), may hold values from -0.00021362305 to 0.00021362305
- first_chan: float32 [8, 2560], P(None, ('batch', 'seq')), may hold values from -0.00061035156 to 0.00061035156
- first_mlp: float32 [2048, 18432], P(('batch', 'seq')), may hold values from -0.00021362305 to 0.00021362305
- second_gains: float32 [2, 2048], P(None, ('batch', 'seq')), may hold values from 1.10454215e-11 to 1.6568132e-10
- second_mixer: float32 [2048, 7680], P(('batch', 'seq')), may hold values from 9.204517e-12 to 1.4727228e-10
- second_gate: float32 [2560, 320], P(('batch', 'seq')), may hold values from 9.204517e-12 to 1.4727228e-10
- second_chan: float32 [8, 2560], P(None, ('batch', 'seq')), may hold values from 8.284066e-11 to 1.3254505e-09
- second_mlp: float32 [2048, 18432], P(('batch', 'seq')), may hold values from 9.204517e-12 to 1.4727228e-10
Outputs:
- block_output: bfloat16 [4, 2048, 2048], P('batch', 'seq')
- input_grad: float32 [4, 2048, 2048], P('batch', 'seq')
- grad_norm: float32 [], replicated
- new_first_gains: float32 [2, 2048], P(None, ('batch', 'seq'))
- new_second_gains: float32 [2, 2048], P(None, ('batch', 'seq'))
- new_gains: float32 [2, 2048], P(None, ('batch', 'seq'))
- new_first_mixer: float32 [2048, 7680], P(('batch', 'seq'))
- new_second_mixer: float32 [2048, 7680], P(('batch', 'seq'))
- new_mixer: float32 [2048, 7680], P(('batch', 'seq'))
- new_first_gate: float32 [2560, 320], P(('batch', 'seq'))
- new_second_gate: float32 [2560, 320], P(('batch', 'seq'))
- new_gate: float32 [2560, 320], P(('batch', 'seq'))
- new_first_chan: float32 [8, 2560], P(None, ('batch', 'seq'))
- new_second_chan: float32 [8, 2560], P(None, ('batch', 'seq'))
- new_chan: float32 [8, 2560], P(None, ('batch', 'seq'))
- new_first_mlp: float32 [2048, 18432], P(('batch', 'seq'))
- new_second_mlp: float32 [2048, 18432], P(('batch', 'seq'))
- new_mlp: float32 [2048, 18432], P(('batch', 'seq'))
The draws below stay inside these ranges and needn't reach their ends.
All inputs are finite; a program needn't handle non-finite values.
Results may differ from the reference program's by a relative error of at most 0.017.
Values may be sent and summed in bfloat16 or wider, within the bound.
A program may use at most 704 MiB of HBM per device.

```python
import math
import jax
import jax.numpy as jnp
from jax import lax

D = 2048
R = 2560
F = 6144
CONV = 4
STEP = 10
HEAD_DIM = 160
LEN = 2048
SEQS = 4
PARAMS = 54321152


def column_scaled(key, row_count, first_cols, first_scale, last_cols, last_scale):
    noise_values = jnp.clip(jax.random.normal(key, (row_count, first_cols + last_cols), jnp.float32), -5.0, 5.0)
    column_index = jnp.arange(first_cols + last_cols)
    column_scale = jnp.where(column_index < first_cols, first_scale, last_scale)
    return noise_values * column_scale


def draw_mixer_weight(key, part):
    key = jax.random.fold_in(key, 1)
    return column_scaled(key, D, 2 * R, D ** (-0.5), R, 2.0 * R ** (-0.5))


def draw_mlp_weight(key, part):
    key = jax.random.fold_in(key, 5)
    return column_scaled(key, D, 2 * F, D ** (-0.5), F, 0.5 * F ** (-0.5))


def draw_norm_gains(key, part):
    key = jax.random.fold_in(key, 2)
    position = jnp.arange(D, dtype=jnp.float32) / (D - 1)
    rising = 1.0 + 2.0 * position
    noise_values = jax.random.uniform(key, (2, D), jnp.float32, 0.8, 1.2)
    return rising * noise_values


def draw_out_grad(key, part):
    key = jax.random.fold_in(key, 3)
    position = jnp.arange(D, dtype=jnp.float32) / (D - 1)
    noise_values = jnp.clip(jax.random.normal(key, (SEQS, LEN, D), jnp.float32), -5.0, 5.0)
    return (noise_values * (0.5 + position)).astype(jnp.bfloat16)


def draw_chan_params(key, part):
    key = jax.random.fold_in(key, 4)
    key_list = jax.random.split(key, 5)
    tap_scale = jnp.array([0.6, 0.4, 0.3, 0.2], jnp.float32)[:, None]
    taps = jnp.clip(jax.random.normal(key_list[0], (4, R), jnp.float32), -4.0, 4.0) * tap_scale
    bias_scale = jnp.array([0.3, 0.6, 0.6], jnp.float32)[:, None]
    biases = jnp.clip(jax.random.normal(key_list[1], (3, R), jnp.float32), -4.0, 4.0) * bias_scale
    slow_share = 0.5
    slow_mask = jax.random.bernoulli(key_list[2], slow_share, (R,))
    slow_rate = jnp.exp(jax.random.uniform(key_list[3], (R,), jnp.float32, jnp.log(0.5 / LEN), jnp.log(3.0 / LEN)))
    fast_rate = jnp.exp(jax.random.uniform(key_list[4], (R,), jnp.float32, jnp.log(0.03), jnp.log(0.1)))
    rate_values = jnp.where(slow_mask, slow_rate, fast_rate) / 8.0
    lambda_row = -jnp.log(jnp.expm1(rate_values))
    return jnp.concatenate([taps, biases, lambda_row[None, :]], axis=0)


def block_scale(rng, dims, shards, least, high):
    factor_of = 1.0
    for dim, shards_of in shards:
        steps = jax.random.uniform(jax.random.fold_in(jax.random.fold_in(rng, 6), dim), (shards_of,), jnp.float32, least / len(shards), high / len(shards))
        factor_of = factor_of * jnp.repeat(jnp.exp(steps), dims[dim] // shards_of).reshape((-1,) + (1,) * (len(dims) - 1 - dim))
    return factor_of


def gaussian(key, extent, width, most, cuts=(), kind=jnp.bfloat16):
    values = width * jax.random.normal(key, extent, jnp.float32)
    if cuts:
        values = values * block_scale(key, extent, cuts, -0.22, 0.18)
    return jnp.clip(values, -most, most).astype(kind)


def setup_inputs(seed: int = 0) -> dict:
    splits = jax.random.split(jax.random.key(seed), 18)
    return {
        "block_input": gaussian(splits[0], (SEQS, LEN, D), 1.0, 6.0, ((0, 4), (1, 8))),
        "out_grad": draw_out_grad(jax.random.fold_in(splits[17], 71), 0),
        "norm_gains": draw_norm_gains(jax.random.fold_in(splits[17], 71), 0),
        "mixer_weight": draw_mixer_weight(jax.random.fold_in(splits[17], 71), 0),
        "gate_weight": gaussian(splits[4], (R, 2 * HEAD_DIM), (4 * HEAD_DIM) ** -0.5, 0.25, ((0, 32),), jnp.float32),
        "chan_params": draw_chan_params(jax.random.fold_in(splits[17], 71), 0),
        "mlp_weight": draw_mlp_weight(jax.random.fold_in(splits[17], 71), 0),
        "first_gains": gaussian(splits[7], (2, D), (0.33 / PARAMS ** 0.5), 0.00061035156, ((1, 32),), jnp.float32),
        "first_mixer": gaussian(splits[8], (D, 3 * R), (0.11 / PARAMS ** 0.5), 0.00021362305, ((0, 32),), jnp.float32),
        "first_gate": gaussian(splits[9], (R, 2 * HEAD_DIM), (0.11 / PARAMS ** 0.5), 0.00021362305, ((0, 32),), jnp.float32),
        "first_chan": gaussian(splits[10], (CONV + 4, R), (0.33 / PARAMS ** 0.5), 0.00061035156, ((1, 32),), jnp.float32),
        "first_mlp": gaussian(splits[11], (D, 3 * F), (0.11 / PARAMS ** 0.5), 0.00021362305, ((0, 32),), jnp.float32),
        "second_gains": jnp.clip(jnp.exp(math.log(1.6568131588901025e-10) - 2.7080502 * jax.random.uniform(splits[12], (2, D), jnp.float32) ** block_scale(splits[12], (2, D), ((1, 32),), -0.2, 0.2)), 1.1045421521860277e-11, 1.6568131588901025e-10),
        "second_mixer": jnp.clip(jnp.exp(math.log(1.472722777062785e-10) - 2.7725887 * jax.random.uniform(splits[13], (D, 3 * R), jnp.float32) ** block_scale(splits[13], (D, 3 * R), ((0, 32),), -0.2, 0.2)), 9.204517356642405e-12, 1.472722777062785e-10),
        "second_gate": jnp.clip(jnp.exp(math.log(1.472722777062785e-10) - 2.7725887 * jax.random.uniform(splits[14], (R, 2 * HEAD_DIM), jnp.float32) ** block_scale(splits[14], (R, 2 * HEAD_DIM), ((0, 32),), -0.2, 0.2)), 9.204517356642405e-12, 1.472722777062785e-10),
        "second_chan": jnp.clip(jnp.exp(math.log(1.325450527112082e-09) - 2.7725887 * jax.random.uniform(splits[15], (CONV + 4, R), jnp.float32) ** block_scale(splits[15], (CONV + 4, R), ((1, 32),), -0.2, 0.2)), 8.284065794450512e-11, 1.325450527112082e-09),
        "second_mlp": jnp.clip(jnp.exp(math.log(1.472722777062785e-10) - 2.7725887 * jax.random.uniform(splits[16], (D, 3 * F), jnp.float32) ** block_scale(splits[16], (D, 3 * F), ((0, 32),), -0.2, 0.2)), 9.204517356642405e-12, 1.472722777062785e-10),
    }


norm_eps = 1e-06
clip_limit = 1.0
beta_first = 0.9
beta_second = 0.999
adam_eps = 1e-08
rate_matrix = 0.05
rate_gains = 0.8
rate_channel = 2.0
decay_matrix = 0.1
highest = lax.Precision.HIGHEST

@jax.custom_vjp
def low(v):
    return lax.optimization_barrier(v.astype(jnp.bfloat16)).astype(jnp.float32)

@jax.custom_vjp
def low_back(v):
    return v

def low_keep(v):
    return (low(v), None)

def low_pass(kept, grad):
    return (grad,)

def back_keep(v):
    return (v, None)

def back_low(kept, grad):
    return (low(grad),)
low.defvjp(low_keep, low_pass)
low_back.defvjp(back_keep, back_low)

def product(left, right):
    return jnp.dot(left, right, precision=highest, preferred_element_type=jnp.float32)

def rms_scale(values, gain):
    inverse = lax.rsqrt(lax.optimization_barrier(jnp.mean(values * values, axis=-1, keepdims=True)) + norm_eps)
    return values * inverse * gain

def coefficients(conv_value, pre_recur, pre_input, lambda_row):
    recur_gate = jax.nn.sigmoid(pre_recur)
    input_gate = jax.nn.sigmoid(pre_input)
    log_decay = -8.0 * jax.nn.softplus(-lambda_row) * recur_gate
    decays = jnp.exp(log_decay)
    scale_in = jnp.sqrt(-jnp.expm1(2.0 * log_decay))
    return (decays, scale_in * input_gate * conv_value)

def gelu_product(gate_up):
    half_width = gate_up.shape[1] // 2
    return jax.nn.gelu(gate_up[:, :half_width]) * gate_up[:, half_width:]

def block_step(params, carry, x_block):
    norm_pair, mixer_rows, gate_rows, channel, feed_rows = params
    lru_state, conv_tail = carry
    tokens = x_block.shape[0]
    lru_width = channel.shape[1]
    hidden_width = feed_rows.shape[1] // 3
    head_dim = gate_rows.shape[1] // 2
    head_count = lru_width // head_dim
    normed_one = low(rms_scale(x_block, norm_pair[0]))
    branch_gate = low_back(product(normed_one, mixer_rows[:, :lru_width]))
    branch_conv = low(low_back(product(normed_one, mixer_rows[:, lru_width:2 * lru_width])))
    extended = jnp.concatenate([conv_tail, branch_conv], axis=0)
    conv_sum = channel[4]
    for tap_index in range(4):
        conv_sum = conv_sum + channel[tap_index] * extended[3 - tap_index:3 - tap_index + tokens]
    conv_value = low(low_back(conv_sum))
    gate_pre = jnp.einsum('thi,hij->thj', conv_value.reshape(tokens, head_count, head_dim), gate_rows.reshape(head_count, head_dim, 2 * head_dim), precision=highest)
    pre_recur = low_back(gate_pre[:, :, :head_dim].reshape(tokens, lru_width) + channel[5])
    pre_input = low_back(gate_pre[:, :, head_dim:].reshape(tokens, lru_width) + channel[6])
    decays, drive_terms = coefficients(conv_value, pre_recur, pre_input, channel[7])

    def advance(running, paired):
        running = paired[0] * running + paired[1]
        return (running, running)
    lru_state, states = lax.scan(advance, lru_state, (decays, drive_terms))
    mixed_rows = low(states * jax.nn.gelu(branch_gate))
    mixer_out = low_back(product(mixed_rows, mixer_rows[:, 2 * lru_width:].T))
    residual = x_block + mixer_out
    normed_two = low(rms_scale(residual, norm_pair[1]))
    gate_up = low_back(product(normed_two, feed_rows[:, :2 * hidden_width]))
    hidden_rows = low(gelu_product(gate_up))
    mlp_out = low_back(product(hidden_rows, feed_rows[:, 2 * hidden_width:].T))
    return ((lru_state, branch_conv[tokens - 3:]), residual + mlp_out)

def forward(inputs, norm_gains, mixer_weight, gate_weight, chan_params, mlp_weight):
    params = (low(norm_gains), low(mixer_weight), low(gate_weight), low(chan_params), low(mlp_weight))
    seq_count, length, model_width = inputs.shape
    block_rows = math.gcd(length, 512)
    lru_width = chan_params.shape[1]
    blocks = inputs.reshape(seq_count, length // block_rows, block_rows, model_width)

    def run_block(carry, x_block):
        return block_step(params, carry, x_block)
    checked = jax.checkpoint(run_block)

    def run_sequence(unused, seq_blocks):
        initial = (jnp.zeros((lru_width,), jnp.float32), jnp.zeros((3, lru_width), jnp.float32))
        final_carry, outputs = lax.scan(checked, initial, seq_blocks)
        return (unused, outputs)
    unused_end, outputs = lax.scan(run_sequence, jnp.zeros((), jnp.float32), blocks)
    return outputs.reshape(seq_count, length, model_width)

def adam_step(weight, grad, first, second, factor, rate, decay_rate):
    clipped = grad * factor
    first_new = beta_first * first + (1.0 - beta_first) * clipped
    second_new = beta_second * second + (1.0 - beta_second) * clipped * clipped
    first_hat = first_new / (1.0 - beta_first ** STEP)
    second_hat = second_new / (1.0 - beta_second ** STEP)
    weight_new = weight - rate * (first_hat / (jnp.sqrt(second_hat) + adam_eps) + decay_rate * weight)
    return (first_new, second_new, weight_new)

def reference(block_input, out_grad, norm_gains, mixer_weight, gate_weight, chan_params, mlp_weight, first_gains, first_mixer, first_gate, first_chan, first_mlp, second_gains, second_mixer, second_gate, second_chan, second_mlp):
    inputs = block_input.astype(jnp.float32)
    cotangent = out_grad.astype(jnp.float32)
    outputs, pullback = jax.vjp(forward, inputs, norm_gains, mixer_weight, gate_weight, chan_params, mlp_weight)
    grads = pullback(cotangent)
    squares = jnp.zeros((), jnp.float32)
    for grad_part in grads[1:]:
        squares = squares + jnp.sum(grad_part * grad_part)
    grad_norm = jnp.sqrt(squares)
    factor = clip_limit / jnp.maximum(grad_norm, clip_limit)
    gains_up = adam_step(norm_gains, grads[1], first_gains, second_gains, factor, rate_gains, 0.0)
    mixer_up = adam_step(mixer_weight, grads[2], first_mixer, second_mixer, factor, rate_matrix, decay_matrix)
    gate_up = adam_step(gate_weight, grads[3], first_gate, second_gate, factor, rate_matrix, decay_matrix)
    chan_up = adam_step(chan_params, grads[4], first_chan, second_chan, factor, rate_channel, 0.0)
    mlp_up = adam_step(mlp_weight, grads[5], first_mlp, second_mlp, factor, rate_matrix, decay_matrix)
    return (outputs.astype(jnp.bfloat16), grads[0], grad_norm, gains_up[0], gains_up[1], gains_up[2], mixer_up[0], mixer_up[1], mixer_up[2], gate_up[0], gate_up[1], gate_up[2], chan_up[0], chan_up[1], chan_up[2], mlp_up[0], mlp_up[1], mlp_up[2])
```

```python
import functools
import math

import jax
import jax.numpy as jnp
from jax import lax
from jax.experimental import pallas as pl
from jax.experimental.pallas import tpu as pltpu
from jax.sharding import PartitionSpec as P

STEP = 10
norm_eps = 1e-06
clip_limit = 1.0
beta_first = 0.9
beta_second = 0.999
adam_eps = 1e-08
rate_matrix = 0.05
rate_gains = 0.8
rate_channel = 2.0
decay_matrix = 0.1

MESH = pl.DeviceIdType.MESH
F32 = jnp.float32
BF16 = jnp.bfloat16
ANY = pl.BlockSpec(memory_space=pl.ANY)
VM = pl.BlockSpec(memory_space=pltpu.VMEM)
FLIPS = [(fy, fc, fx) for fy in (0, 1) for fc in (0, 1) for fx in (0, 1) if fy + fc + fx]
GELU_SCALE = math.sqrt(2.0 / math.pi)


def place():
    b = lax.axis_index("batch")
    s = lax.axis_index("seq")
    y, z = b // 2, s // 2
    return y, b - 2 * y, z, s - 2 * z


def device(y, c, z, x):
    return (y * 2 + c, z * 2 + x)


def rank(y, c, x):
    return (y * 2 + c) * 2 + x


def flip(v, f):
    return 1 - v if f else v


def greet(peers):
    barrier = pltpu.get_barrier_semaphore()
    for peer in peers:
        pl.semaphore_signal(barrier, inc=1, device_id=peer, device_id_type=MESH)
    pl.semaphore_wait(barrier, len(peers))


def remote(src, dst, send, recv, to):
    copy = pltpu.make_async_remote_copy(
        src_ref=src, dst_ref=dst, send_sem=send, recv_sem=recv, device_id=to, device_id_type=MESH
    )
    copy.start()
    return copy


def params(collective_id, vmem=None):
    return pltpu.CompilerParams(
        collective_id=collective_id, has_side_effects=True, vmem_limit_bytes=vmem
    )


DMA = pltpu.SemaphoreType.DMA


def gather_kernel(a, o, loc, ss, rs):
    y, c, z, x = place()
    to_x, to_y, to_c = device(y, c, z, 1 - x), device(1 - y, c, z, x), device(y, 1 - c, z, x)
    greet((to_x, to_y, to_c))
    me, bx, by, bd = rank(y, c, x), rank(y, c, 1 - x), rank(1 - y, c, x), rank(1 - y, c, 1 - x)
    half = a.shape[0] // 2
    lo, hi = pl.ds(0, half), pl.ds(half, half)
    done = []

    def send(src, dst, k, to):
        copy = remote(src, dst, ss.at[k], rs.at[k], to)
        done.append(copy)
        return copy

    s0 = send(a.at[lo], o.at[me, lo], 0, to_x)
    s1 = send(a.at[hi], o.at[me, hi], 1, to_y)
    s2 = send(a.at[hi], o.at[me, hi], 2, to_x)
    s3 = send(a.at[lo], o.at[me, lo], 3, to_y)
    s4 = send(a, o.at[me], 4, to_c)
    own = pltpu.make_async_copy(a, o.at[me], loc)
    own.start()

    def pass_on(block, part, k):
        return send(o.at[block, part], o.at[block, part], k, to_c)

    s0.wait_recv()
    s5 = send(o.at[bx, lo], o.at[bx, lo], 5, to_y)
    last = [s4, pass_on(bx, lo, 7)]
    s1.wait_recv()
    s6 = send(o.at[by, hi], o.at[by, hi], 6, to_x)
    last.append(pass_on(by, hi, 8))
    s2.wait_recv()
    last.append(pass_on(bx, hi, 9))
    s3.wait_recv()
    last.append(pass_on(by, lo, 10))
    s5.wait_recv()
    last.append(pass_on(bd, lo, 11))
    s6.wait_recv()
    last.append(pass_on(bd, hi, 12))
    for copy in last:
        copy.wait_recv()
    for copy in done:
        copy.wait_send()
    own.wait()


def plane_gather(a, collective_id):
    rows, width = a.shape
    out = pl.pallas_call(
        gather_kernel,
        out_shape=jax.ShapeDtypeStruct((8, rows, width), a.dtype),
        in_specs=[ANY],
        out_specs=ANY,
        scratch_shapes=[DMA, DMA((13,)), DMA((13,))],
        compiler_params=params(collective_id),
        cost_estimate=pl.CostEstimate(flops=0, bytes_accessed=120 * 2**20, transcendentals=0),
    )(a)
    return out.reshape(8 * rows, width)


def scatter_kernel(p, o, mine, sib, part, got, loc, ss, rs):
    y, c, z, x = place()
    to_x, to_y, to_c = device(y, c, z, 1 - x), device(1 - y, c, z, x), device(y, 1 - c, z, x)
    greet((to_x, to_y, to_c))
    half = o.shape[0] // 2
    step = 16
    cut = (pl.ds(0, half), pl.ds(half, half))
    where = ((1 - y, 1 - x), (1 - y, x), (y, 1 - x), (y, x))
    order = [(0, 0), (0, 1), (1, 0), (2, 1), (2, 0), (1, 1), (3, 0), (3, 1)]
    from_c, own, sends = {}, {}, []
    for n, (t, h) in enumerate(order):
        ty, tx = where[t]
        own[t, h] = pltpu.make_async_copy(
            p.at[rank(ty, c, tx), cut[h]], mine.at[t, h], loc.at[n]
        )
        own[t, h].start()
        from_c[t, h] = remote(
            p.at[rank(ty, 1 - c, tx), cut[h]], sib.at[t, h], ss.at[n], rs.at[n], to_c
        )
        sends.append(from_c[t, h])

    def add(dst, t, h, extra):
        own[t, h].wait()
        from_c[t, h].wait_recv()

        @pl.loop(0, half // step)
        def _(i):
            at = pl.ds(pl.multiple_of(i * step, step), step)
            total = mine[t, h, at].astype(F32) + sib[t, h, at].astype(F32)
            for ref in extra:
                total = total + ref[at].astype(F32)
            dst[at] = total.astype(dst.dtype)

    def send(k, slot, to):
        copy = remote(part.at[k], got.at[slot], ss.at[8 + k], rs.at[8 + slot], to)
        sends.append(copy)
        return copy

    def arrival(slot):
        return pltpu.make_async_remote_copy(
            src_ref=part.at[0], dst_ref=got.at[slot], send_sem=ss.at[8], recv_sem=rs.at[8 + slot],
            device_id=to_x, device_id_type=MESH,
        )

    add(part.at[0], 0, 0, ())
    send(0, 1, to_y)
    add(part.at[1], 0, 1, ())
    send(1, 3, to_x)
    add(part.at[2], 1, 0, ())
    send(2, 0, to_y)
    add(part.at[3], 2, 1, ())
    send(3, 2, to_x)
    arrival(1).wait_recv()
    add(part.at[4], 2, 0, (got.at[1],))
    send(4, 4, to_x)
    arrival(3).wait_recv()
    add(part.at[5], 1, 1, (got.at[3],))
    send(5, 5, to_y)
    arrival(0).wait_recv()
    arrival(4).wait_recv()
    add(o.at[cut[0]], 3, 0, (got.at[0], got.at[4]))
    arrival(2).wait_recv()
    arrival(5).wait_recv()
    add(o.at[cut[1]], 3, 1, (got.at[2], got.at[5]))
    for copy in sends:
        copy.wait_send()


def plane_scatter(p, collective_id):
    width = p.shape[1]
    rows = p.shape[0] // 8
    half = rows // 2
    return pl.pallas_call(
        scatter_kernel,
        out_shape=jax.ShapeDtypeStruct((rows, width), F32),
        in_specs=[ANY],
        out_specs=VM,
        scratch_shapes=[
            pltpu.VMEM((4, 2, half, width), BF16),
            pltpu.VMEM((4, 2, half, width), BF16),
            pltpu.VMEM((6, half, width), BF16),
            pltpu.VMEM((6, half, width), BF16),
            DMA((8,)),
            DMA((14,)),
            DMA((14,)),
        ],
        compiler_params=params(collective_id, 40 * 2**20),
        cost_estimate=pl.CostEstimate(flops=0, bytes_accessed=140 * 2**20, transcendentals=0),
    )(p.reshape(8, rows, width))


def exchange_steps(a, o, loc, ss, rs):
    y, c, z, x = place()
    me = rank(y, c, x)
    copies = []
    for n, (fy, fc, fx) in enumerate(FLIPS):
        ty, tc, tx = flip(y, fy), flip(c, fc), flip(x, fx)
        copies.append(
            remote(a.at[rank(ty, tc, tx)], o.at[me], ss.at[n], rs.at[n], device(ty, tc, z, tx))
        )
    own = pltpu.make_async_copy(a.at[me], o.at[me], loc)
    own.start()
    return copies, own


def plane_peers():
    y, c, z, x = place()
    return [device(flip(y, fy), flip(c, fc), z, flip(x, fx)) for fy, fc, fx in FLIPS]


def line_peers(length):
    y, c, z, x = place()
    return [device(y, c, lax.rem(z + k, length), x) for k in range(1, length)]


def exchange_kernel(a, o, loc, ss, rs):
    greet(plane_peers())
    copies, own = exchange_steps(a, o, loc, ss, rs)
    for copy in copies:
        copy.wait()
    own.wait()


def plane_exchange(a, collective_id):
    return pl.pallas_call(
        exchange_kernel,
        out_shape=jax.ShapeDtypeStruct(a.shape, a.dtype),
        in_specs=[ANY],
        out_specs=ANY,
        scratch_shapes=[DMA, DMA((7,)), DMA((7,))],
        compiler_params=params(collective_id),
        cost_estimate=pl.CostEstimate(flops=0, bytes_accessed=80 * 2**20, transcendentals=0),
    )(a)


def first_kernel(length, wm, gn, gp, wm_o, gn_o, gp_o, loc, ss, rs, line_s, line_r, gain_s, gain_r, move_s, move_r):
    y, c, z, x = place()
    s = 2 * z + x
    me = rank(y, c, x)
    line = line_peers(length)
    plane = plane_peers()
    to_z, to_x = lax.rem(s, length), s // length
    moves = jnp.where(jnp.logical_and(to_z == z, to_x == x), 0, 1)
    src = x * length + z
    from_z = src // 2
    from_x = src - 2 * from_z
    barrier = pltpu.get_barrier_semaphore()
    for peer in line + plane:
        pl.semaphore_signal(barrier, inc=1, device_id=peer, device_id_type=MESH)

    @pl.when(moves == 1)
    def _():
        pl.semaphore_signal(barrier, inc=1, device_id=device(y, c, to_z, to_x), device_id_type=MESH)
        pl.semaphore_signal(barrier, inc=1, device_id=device(y, c, from_z, from_x), device_id_type=MESH)

    pl.semaphore_wait(barrier, len(line) + len(plane) + 2 * moves)

    copies, own = exchange_steps(wm, wm_o, loc.at[0], ss, rs)
    gain_own = pltpu.make_async_copy(gn, gn_o.at[me, z], loc.at[1])
    gain_own.start()
    gains = [
        remote(gn, gn_o.at[me, z], line_s.at[0, k], line_r.at[0, k], line[k]) for k in range(length - 1)
    ]

    @pl.when(moves == 1)
    def _():
        copy = remote(gp, gp_o.at[to_z], move_s, move_r, device(y, c, to_z, to_x))
        copy.wait()

    @pl.when(moves == 0)
    def _():
        copy = pltpu.make_async_copy(gp, gp_o.at[z], loc.at[2])
        copy.start()
        copy.wait()

    gates = [
        remote(gp_o.at[z], gp_o.at[z], line_s.at[1, k], line_r.at[1, k], line[k])
        for k in range(length - 1)
    ]
    gain_own.wait()
    for copy in gains:
        copy.wait()
    spread = [
        remote(gn_o.at[me], gn_o.at[me], gain_s.at[n], gain_r.at[n], plane[n]) for n in range(7)
    ]
    for copy in spread + gates + copies:
        copy.wait()
    own.wait()


def first(wm, gn, gp, length, collective_id):
    return pl.pallas_call(
        functools.partial(first_kernel, length),
        out_shape=(
            jax.ShapeDtypeStruct(wm.shape, wm.dtype),
            jax.ShapeDtypeStruct((8, length) + gn.shape, gn.dtype),
            jax.ShapeDtypeStruct((length,) + gp.shape, gp.dtype),
        ),
        in_specs=[ANY] * 3,
        out_specs=(ANY,) * 3,
        scratch_shapes=[
            DMA((3,)), DMA((7,)), DMA((7,)), DMA((2, length)), DMA((2, length)),
            DMA((7,)), DMA((7,)), DMA, DMA,
        ],
        compiler_params=params(collective_id),
    )(wm, gn, gp)


def last_kernel(
    length, wm, gn, gp, sq, wm_o, gn_o, gp_o, sq_o,
    gn_in, gn_mid, gn_got, gn_fin, gp_got, gp_sum, gp_fin, sq_plane, sq_line, sq_mid,
    loc, ss, rs, gs, gr, ls, lr, move_s, move_r,
):
    y, c, z, x = place()
    s = 2 * z + x
    me = rank(y, c, x)
    line = line_peers(length)
    plane = plane_peers()
    owner = x * length + z
    to_z = owner // 2
    to_x = owner - 2 * to_z
    from_z, from_x = lax.rem(s, length), s // length
    moves = jnp.where(jnp.logical_and(to_z == z, to_x == x), 0, 1)
    barrier = pltpu.get_barrier_semaphore()
    for peer in line + plane:
        pl.semaphore_signal(barrier, inc=1, device_id=peer, device_id_type=MESH)

    @pl.when(moves == 1)
    def _():
        pl.semaphore_signal(barrier, inc=1, device_id=device(y, c, to_z, to_x), device_id_type=MESH)
        pl.semaphore_signal(barrier, inc=1, device_id=device(y, c, from_z, from_x), device_id_type=MESH)

    pl.semaphore_wait(barrier, len(line) + len(plane) + 2 * moves)

    gain = []
    for n, (fy, fc, fx) in enumerate(FLIPS):
        to = rank(flip(y, fy), flip(c, fc), flip(x, fx))
        gain.append(remote(gn.at[to], gn_in.at[n], gs.at[0, n], gr.at[0, n], plane[n]))
    gate = [
        remote(gp.at[k + 1], gp_got.at[k], ls.at[0, k], lr.at[0, k], line[k]) for k in range(length - 1)
    ]
    copies, own = exchange_steps(wm, wm_o, loc, ss, rs)
    for copy in gain:
        copy.wait()
    total = gn[me]
    for n in range(7):
        total = total + gn_in[n]
    gn_mid[...] = total
    gain_line = [
        remote(gn_mid.at[k + 1], gn_got.at[k], ls.at[1, k], lr.at[1, k], line[k])
        for k in range(length - 1)
    ]
    for copy in gate:
        copy.wait()
    total = gp[0]
    for k in range(length - 1):
        total = total + gp_got[k]
    gp_sum[...] = total

    @pl.when(moves == 1)
    def _():
        copy = remote(gp_sum, gp_fin, move_s, move_r, device(y, c, to_z, to_x))
        copy.wait()

    @pl.when(moves == 0)
    def _():
        gp_fin[...] = gp_sum[...]

    for copy in gain_line:
        copy.wait()
    total = gn_mid[0]
    for k in range(length - 1):
        total = total + gn_got[k]
    gn_o[...] = total
    gates = gp_fin[...]
    gp_o[...] = gates

    def tiles(v):
        v = v * v
        if v.shape[0] > 8:
            v = jnp.sum(v.reshape(v.shape[0] // 8, 8, v.shape[1]), axis=0)
        part = v[:, :128]
        for n in range(1, v.shape[1] // 128):
            part = part + v[:, n * 128 : (n + 1) * 128]
        return part

    sq_plane[me] = sq[...] + tiles(total) + tiles(gates)
    sums = [
        remote(sq_plane.at[me], sq_plane.at[me], gs.at[1, n], gr.at[1, n], plane[n]) for n in range(7)
    ]
    for copy in sums:
        copy.wait()
    total = sq_plane[0]
    for n in range(1, 8):
        total = total + sq_plane[n]
    sq_line[z] = total
    sums = [
        remote(sq_line.at[z], sq_line.at[z], ls.at[2, k], lr.at[2, k], line[k])
        for k in range(length - 1)
    ]
    for copy in sums:
        copy.wait()
    total = sq_line[0]
    for n in range(1, length):
        total = total + sq_line[n]
    sq_o[...] = total
    for copy in copies:
        copy.wait()
    own.wait()


def last(wm, gn, gp, sq, length, collective_id):
    small, rows = gn.shape[2:], gp.shape[1:]
    return pl.pallas_call(
        functools.partial(last_kernel, length),
        out_shape=(
            jax.ShapeDtypeStruct(wm.shape, wm.dtype),
            jax.ShapeDtypeStruct(small, F32),
            jax.ShapeDtypeStruct(rows, F32),
            jax.ShapeDtypeStruct((8, 128), F32),
        ),
        in_specs=[ANY, VM, VM, VM],
        out_specs=(ANY, VM, VM, VM),
        scratch_shapes=[
            pltpu.VMEM((7, length) + small, F32),
            pltpu.VMEM((length,) + small, F32),
            pltpu.VMEM((length,) + small, F32),
            pltpu.VMEM(small, F32),
            pltpu.VMEM((length,) + rows, F32),
            pltpu.VMEM(rows, F32),
            pltpu.VMEM(rows, F32),
            pltpu.VMEM((8, 8, 128), F32),
            pltpu.VMEM((length, 8, 128), F32),
            pltpu.VMEM((8, 128), F32),
            DMA, DMA((7,)), DMA((7,)), DMA((2, 7)), DMA((2, 7)),
            DMA((3, length)), DMA((3, length)), DMA, DMA,
        ],
        compiler_params=params(collective_id, 24 * 2**20),
    )(wm, gn, gp, sq)


def minus_expm1(v):
    series = 1.0 + v * (1.0 / 8.0)
    for n in (7.0, 6.0, 5.0, 4.0, 3.0, 2.0):
        series = 1.0 + series * v * (1.0 / n)
    return jnp.where(v > -0.5, -v * series, 1.0 - jnp.exp(v))


def gelu_parts(v):
    inner = jnp.tanh(GELU_SCALE * (v + 0.044715 * v * v * v))
    return 0.5 * v * (1.0 + inner), inner


def gelu_slope(v, inner):
    return 0.5 * (1.0 + inner) + 0.5 * v * (1.0 - inner * inner) * GELU_SCALE * (
        1.0 + 3.0 * 0.044715 * v * v
    )


CHUNK = 64


def forward_kernel(
    length, proj, gate, chan, mixed, decay_o, width_o, recur_o, enter_o, conv_o, xe, se, ends_o,
    pre, loc_h, ends, carry, hs, hr, es, er,
):
    y, c, z, x = place()
    line = line_peers(length)
    greet(line)
    seqs, span, rc = mixed.shape
    chunks = span // CHUNK

    @pl.loop(0, seqs * chunks)
    def _(i):
        b = i // chunks
        r = pl.multiple_of((i - b * chunks) * CHUNK, CHUNK)
        xe[b, pl.ds(r + 8, CHUNK)] = proj[b, pl.ds(r, CHUNK), rc:].astype(BF16).astype(F32)

    ahead = device(y, c, lax.rem(z + 1, length), x)
    halo = remote(xe.at[:, pl.ds(span, 8)], xe.at[:, pl.ds(0, 8)], hs, hr, ahead)
    halo.wait()

    @pl.when(z == 0)
    def _():
        xe[:, 0:8] = jnp.zeros((seqs, 8, rc), F32)

    @pl.loop(0, seqs * chunks)
    def _(i):
        b = i // chunks
        r = pl.multiple_of((i - b * chunks) * CHUNK, CHUNK)
        at = pl.ds(r, CHUNK)
        window = xe[b, pl.ds(r, CHUNK + 8)]
        total = chan[4:5] + chan[0:1] * window[8:]
        for k in (1, 2, 3):
            total = total + chan[k : k + 1] * pltpu.roll(window, k, 0)[8:]
        low = total.astype(BF16)
        conv_o[b, at] = low
        value = low.astype(F32)
        gates = jnp.dot(low, gate[...], preferred_element_type=F32)
        recur = jax.nn.sigmoid(gates[:, :rc] + chan[5:6])
        enter = jax.nn.sigmoid(gates[:, rc:] + chan[6:7])
        log_decay = -chan[7:8] * recur
        decay = jnp.exp(log_decay)
        width = jnp.sqrt(minus_expm1(2.0 * log_decay))
        recur_o[b, at] = recur
        enter_o[b, at] = enter
        decay_o[b, at] = decay
        width_o[b, at] = width
        loc_h[b, at] = width * enter * value

    row = lax.broadcasted_iota(jnp.int32, (8, rc), 0)

    def tile(i, held):
        at = pl.ds(pl.multiple_of(i * 8, 8), 8)
        new = []
        for b in range(seqs):
            a, h = decay_o[b, at], loc_h[b, at]
            for n in (1, 2, 4):
                keep = row >= n
                h = h + jnp.where(keep, a * pltpu.roll(h, n, 0), 0.0)
                a = jnp.where(keep, a * pltpu.roll(a, n, 0), a)
            h = h + a * held[b][1]
            a = a * held[b][0]
            loc_h[b, at] = h
            pre[b, at] = a
            new.append((a[7:8], h[7:8]))
        return tuple(new)

    one, zero = jnp.ones((1, rc), F32), jnp.zeros((1, rc), F32)
    final = lax.fori_loop(0, span // 8, tile, ((one, zero),) * seqs)
    for b in range(seqs):
        ends[z, 0, b] = jnp.broadcast_to(final[b][0], (8, rc))
        ends[z, 1, b] = jnp.broadcast_to(final[b][1], (8, rc))
        ends_o[b] = jnp.broadcast_to(final[b][0], (8, rc))
    moves = [remote(ends.at[z], ends.at[z], es.at[k], er.at[k], line[k]) for k in range(length - 1)]
    for copy in moves:
        copy.wait()
    carry[...] = jnp.zeros_like(carry)
    for k in range(length):
        carry[...] = jnp.where(k < z, ends[k, 0] * carry[...] + ends[k, 1], carry[...])

    for b in range(seqs):
        se[b, 0:8] = carry[b]

    @pl.loop(0, seqs * chunks)
    def _(i):
        b = i // chunks
        r = pl.multiple_of((i - b * chunks) * CHUNK, CHUNK)
        at = pl.ds(r, CHUNK)
        state = loc_h[b, at] + pre[b, at] * carry[b, 0:1]
        se[b, pl.ds(r + 8, CHUNK)] = state
        gelu, _ = gelu_parts(proj[b, at, :rc])
        mixed[b, at] = (state * gelu).astype(BF16)


def recur_forward(proj, gate, chan, length, collective_id):
    seqs, span, rc = proj.shape[0], proj.shape[1], proj.shape[2] // 2
    full = jax.ShapeDtypeStruct((seqs, span, rc), F32)
    longer = jax.ShapeDtypeStruct((seqs, span + 8, rc), F32)
    low = jax.ShapeDtypeStruct((seqs, span, rc), BF16)
    return pl.pallas_call(
        functools.partial(forward_kernel, length),
        out_shape=(
            low, full, full, full, full, low, longer, longer,
            jax.ShapeDtypeStruct((seqs, 8, rc), F32),
        ),
        in_specs=[VM] * 3,
        out_specs=(VM,) * 9,
        scratch_shapes=[
            pltpu.VMEM((seqs, span, rc), F32),
            pltpu.VMEM((seqs, span, rc), F32),
            pltpu.VMEM((length, 2, seqs, 8, rc), F32),
            pltpu.VMEM((seqs, 8, rc), F32),
            DMA, DMA, DMA((length,)), DMA((length,)),
        ],
        compiler_params=params(collective_id, 56 * 2**20),
        cost_estimate=pl.CostEstimate(
            flops=2 * seqs * span * rc * rc * 2, bytes_accessed=100 * 2**20, transcendentals=0
        ),
    )(proj, gate, chan)


def backward_kernel(
    length, dmix, gate, chan, decay, width, recur, enter, conv, xe, se, ends_f, proj,
    dproj, dgate, gchan, suffix, grad, de, ends, carry, hs, hr, es, er,
):
    y, c, z, x = place()
    line = line_peers(length)
    greet(line)
    seqs, span, rc = decay.shape
    chunks = span // CHUNK

    @pl.loop(0, seqs * chunks)
    def _(i):
        b = i // chunks
        r = pl.multiple_of((i - b * chunks) * CHUNK, CHUNK)
        at = pl.ds(r, CHUNK)
        branch = proj[b, at]
        gelu, inner = gelu_parts(branch)
        above = dmix[b, at]
        state = se[b, pl.ds(r + 8, CHUNK)]
        grad[b, at] = above * gelu
        dproj[b, at, :rc] = (above * state * gelu_slope(branch, inner)).astype(BF16)

    row = lax.broadcasted_iota(jnp.int32, (8, rc), 0)

    def tile(i, held):
        at = pl.ds(pl.multiple_of(span - 8 - i * 8, 8), 8)
        new = []
        for b in range(seqs):
            product, total, following = held[b]
            plain, h = decay[b, at], grad[b, at]
            a = jnp.where(row == 7, following, pltpu.roll(plain, 7, 0))
            for n in (1, 2, 4):
                keep = row < 8 - n
                h = h + jnp.where(keep, a * pltpu.roll(h, 8 - n, 0), 0.0)
                a = jnp.where(keep, a * pltpu.roll(a, 8 - n, 0), a)
            h = h + a * total
            a = a * product
            grad[b, at] = h
            suffix[b, at] = a
            new.append((a[0:1], h[0:1], plain[0:1]))
        return tuple(new)

    one, zero = jnp.ones((1, rc), F32), jnp.zeros((1, rc), F32)
    final = lax.fori_loop(0, span // 8, tile, ((one, zero, one),) * seqs)
    for b in range(seqs):
        ends[z, 0, b] = ends_f[b]
        ends[z, 1, b] = jnp.broadcast_to(final[b][1] * final[b][2], (8, rc))
    moves = [remote(ends.at[z], ends.at[z], es.at[k], er.at[k], line[k]) for k in range(length - 1)]
    for copy in moves:
        copy.wait()
    carry[...] = jnp.zeros_like(carry)
    for k in reversed(range(length)):
        carry[...] = jnp.where(k > z, ends[k, 0] * carry[...] + ends[k, 1], carry[...])

    gchan[...] = jnp.zeros_like(gchan)

    def fold(v):
        return jnp.sum(v.reshape(v.shape[0] // 8, 8, v.shape[1]), axis=0)

    @pl.loop(0, seqs * chunks)
    def _(i):
        b = i // chunks
        r = pl.multiple_of((i - b * chunks) * CHUNK, CHUNK)
        at = pl.ds(r, CHUNK)
        g = grad[b, at] + suffix[b, at] * carry[b, 0:1]
        a, w, ra, ri = decay[b, at], width[b, at], recur[b, at], enter[b, at]
        value = conv[b, at].astype(F32)
        before = pltpu.roll(se[b, pl.ds(r, CHUNK + 8)], 1, 0)[8:]
        dla = g * before * a - g * ri * value * (a * a) / w
        slope = dla * ra * (1.0 - ra)
        dpa = (-chan[7:8] * slope).astype(BF16)
        dpi = (g * w * value * ri * (1.0 - ri)).astype(BF16)
        dgate[b, at, :rc] = dpa
        dgate[b, at, rc:] = dpi
        gchan[5] += fold(dpa.astype(F32))
        gchan[6] += fold(dpi.astype(F32))
        gchan[7] += fold(dla * ra)
        back = lax.dot_general(
            dgate[b, at], gate[...], (((1,), (1,)), ((), ())), preferred_element_type=F32
        )
        dcv = (g * w * ri + back).astype(BF16).astype(F32)
        de[b, at] = dcv
        gchan[4] += fold(dcv)

    behind = device(y, c, lax.rem(z + length - 1, length), x)
    halo = remote(de.at[:, pl.ds(0, 8)], de.at[:, pl.ds(span, 8)], hs, hr, behind)
    halo.wait()

    @pl.when(z == length - 1)
    def _():
        de[:, span:] = jnp.zeros((seqs, 8, rc), F32)

    @pl.loop(0, seqs * chunks)
    def _(i):
        b = i // chunks
        r = pl.multiple_of((i - b * chunks) * CHUNK, CHUNK)
        at = pl.ds(r, CHUNK)
        window = de[b, pl.ds(r, CHUNK + 8)]
        inputs = xe[b, pl.ds(r, CHUNK + 8)]
        dcv = window[:CHUNK]
        total = chan[0:1] * dcv
        gchan[0] += fold(dcv * inputs[8:])
        for k in (1, 2, 3):
            total = total + chan[k : k + 1] * pltpu.roll(window, CHUNK + 8 - k, 0)[:CHUNK]
            gchan[k] += fold(dcv * pltpu.roll(inputs, k, 0)[8:])
        dproj[b, at, rc:] = total.astype(BF16)


def recur_backward(dmix, gate, chan, kept, proj, length, collective_id):
    decay, width, recur, enter, conv, xe, se, ends = kept
    seqs, span, rc = decay.shape
    wide = jax.ShapeDtypeStruct((seqs, span, 2 * rc), BF16)
    return pl.pallas_call(
        functools.partial(backward_kernel, length),
        grid=(1,),
        out_shape=(wide, wide, jax.ShapeDtypeStruct((8, 8, rc), F32)),
        in_specs=[VM] * 11 + [pl.BlockSpec((seqs, span, rc), lambda i: (0, 0, 0))],
        out_specs=(VM,) * 3,
        scratch_shapes=[
            pltpu.VMEM((seqs, span, rc), F32),
            pltpu.VMEM((seqs, span, rc), F32),
            pltpu.VMEM((seqs, span + 8, rc), F32),
            pltpu.VMEM((length, 2, seqs, 8, rc), F32),
            pltpu.VMEM((seqs, 8, rc), F32),
            DMA, DMA, DMA((length,)), DMA((length,)),
        ],
        compiler_params=params(collective_id, 60 * 2**20),
        cost_estimate=pl.CostEstimate(
            flops=2 * seqs * span * rc * rc * 2, bytes_accessed=120 * 2**20, transcendentals=0
        ),
    )(dmix, gate, chan, decay, width, recur, enter, conv, xe, se, ends, proj)


def routes(length, senders):
    pairs = [(z, z + 1) for z in range(length - 1) if z in senders]
    return [(2 * a + x, 2 * b + x) for a, b in pairs for x in range(2)]


def line_gather(block, length):
    up_routes = routes(length, range(length))
    down_routes = [(b, a) for a, b in up_routes]
    up = down = block
    ups, downs = [], []
    for _ in range(length - 1):
        up = lax.ppermute(up, "seq", up_routes)
        down = lax.ppermute(down, "seq", down_routes)
        ups.append(up)
        downs.append(down)
    z = lax.axis_index("seq") // 2
    blocks = [block]
    for k in range(1, length):
        blocks.append(jnp.where(z + k < length, downs[k - 1], ups[length - k - 1]))
    return blocks


def line_scatter(blocks, length):
    up = down = None
    for hop in range(1, length):
        up_routes = routes(length, range(hop))
        down_routes = [
            (2 * (length - 1 - a // 2) + a % 2, 2 * (length - 1 - b // 2) + b % 2) for a, b in up_routes
        ]
        up_block, down_block = blocks[length - hop], blocks[hop]
        if up is not None:
            up_block = (up_block.astype(F32) + up.astype(F32)).astype(BF16)
            down_block = (down_block.astype(F32) + down.astype(F32)).astype(BF16)
        up = lax.ppermute(up_block, "seq", up_routes)
        down = lax.ppermute(down_block, "seq", down_routes)
    return blocks[0].astype(F32) + up.astype(F32) + down.astype(F32)


def contract_last(left, right):
    return lax.dot_general(
        left, right, (((1,), (1,)), ((), ())), preferred_element_type=F32
    )


def contract_first(left, right):
    return lax.dot_general(
        left, right, (((0,), (0,)), ((), ())), preferred_element_type=F32
    )


def adam_step(weight, grad, first, second, factor, rate, decay_rate):
    clipped = grad * factor
    first_new = beta_first * first + (1.0 - beta_first) * clipped
    second_new = beta_second * second + (1.0 - beta_second) * clipped * clipped
    first_hat = first_new / (1.0 - beta_first**STEP)
    second_hat = second_new / (1.0 - beta_second**STEP)
    weight_new = weight - rate * (
        first_hat / (jnp.sqrt(second_hat) + adam_eps) + decay_rate * weight
    )
    return (first_new, second_new, weight_new)


def normalize(values, gain):
    inverse = lax.rsqrt(jnp.mean(values * values, axis=-1, keepdims=True) + norm_eps)
    scaled = values * inverse
    return (scaled, inverse, (scaled * gain).astype(BF16))


def normalize_back(grad_normed, scaled, inverse, gain):
    grad_scaled = grad_normed * gain
    gain_grad = jnp.sum(grad_normed * scaled, axis=0)
    inner = jnp.mean(grad_scaled * scaled, axis=-1, keepdims=True)
    return (inverse * (grad_scaled - scaled * inner), gain_grad)


def on_device(
    block_input,
    out_grad,
    norm_gains,
    mixer_weight,
    gate_weight,
    chan_params,
    mlp_weight,
    first_gains,
    first_mixer,
    first_gate,
    first_chan,
    first_mlp,
    second_gains,
    second_mixer,
    second_gate,
    second_chan,
    second_mlp,
):
    length = lax.axis_size("seq") // 2
    z = lax.axis_index("seq") // 2
    tokens, model = block_input.shape[1:]
    share = mixer_weight.shape[0]
    pair = 2 * share
    lru = mixer_weight.shape[1] // 3
    hidden = mlp_weight.shape[1] // 3
    r8, f8 = lru // 8, hidden // 8
    rc = -(-r8 // 128) * 128
    head = gate_weight.shape[1] // 2
    heads = r8 // head
    gate_rows = gate_weight.shape[0]
    gate_pad = -(-gate_rows // 16) * 16

    def turned(v):
        lead = v.shape[:-1]
        v = v.reshape(lead + (4, length, pair)).swapaxes(-2, -3)
        return jnp.roll(v, -z, axis=-3).reshape(lead + (model,))

    def turned_back(v):
        lead = v.shape[:-1]
        v = jnp.roll(v.reshape(lead + (length, 4, pair)), z, axis=-3)
        return v.swapaxes(-2, -3).reshape(lead + (model,))

    mixer_out = (
        mixer_weight.astype(BF16).reshape(share, 3, 8, r8).transpose(2, 0, 1, 3).reshape(8, share, 3 * r8)
    )
    mlp_out = (
        mlp_weight.astype(BF16).reshape(share, 3, 8, f8).transpose(2, 0, 1, 3).reshape(8, share, 3 * f8)
    )
    gains_out = jnp.pad(norm_gains, ((0, 6), (0, 128 - share)))
    gate_out = jnp.pad(
        jnp.concatenate([gate_weight, chan_params.T], axis=1).astype(BF16),
        ((0, gate_pad - gate_rows), (0, rc - 2 * head - 8)),
    )
    mixer_in, gains_in, gate_in = first(mixer_out, gains_out, gate_out, length, 1)
    gains = gains_in[:, :, :2, :share].astype(BF16).astype(F32)
    gains = gains.reshape(4, 2, length, 2, share).transpose(3, 0, 2, 1, 4).reshape(2, model)
    gains = turned(gains)
    gate_own = gate_in[:, :gate_rows].reshape(r8, rc)
    chan = gate_own[:, 2 * head : 2 * head + 8].astype(F32).T
    lam = chan[7]
    fill = jnp.concatenate([jnp.zeros((7, rc - r8), F32), jnp.ones((1, rc - r8), F32)])
    chan = jnp.concatenate([chan[:7], 8.0 * jax.nn.softplus(-lam)[None]])
    chan = jnp.concatenate([chan, fill], axis=1)
    gate = jnp.zeros((rc, 2, rc), BF16)
    for h in range(heads):
        at = slice(h * head, (h + 1) * head)
        block = gate_own[at, : 2 * head].reshape(head, 2, head)
        gate = gate.at[at, :, at].set(block)
    gate = gate.reshape(rc, 2 * rc)

    mixer_blocks = line_gather(mixer_in.reshape(8 * share, 3 * r8), length)
    inputs = turned(block_input[0].astype(F32))
    cotangent_low = turned(out_grad[0])
    cotangent = cotangent_low.astype(F32)
    scaled_one, inverse_one, normed_one = normalize(inputs, gains[0])
    normed_one = plane_gather(normed_one, 2)
    mlp_in = plane_exchange(mlp_out, 3)
    mlp_blocks = line_gather(mlp_in.reshape(8 * share, 3 * f8), length)
    grad_out = plane_gather(cotangent_low, 4)

    mixer_full = jnp.concatenate(mixer_blocks)
    parts = [jnp.pad(mixer_full[:, n * r8 : (n + 1) * r8], ((0, 0), (0, rc - r8))) for n in range(3)]
    mixer_first = jnp.concatenate(parts[:2], axis=1)
    mixer_last = parts[2]
    span = 2 * tokens
    projected = jnp.dot(normed_one, mixer_first, preferred_element_type=F32)
    projected = projected.reshape(4, span, 2 * rc)
    mixed, *kept = recur_forward(projected, gate, chan, length, 5)
    mixed = mixed.reshape(4 * span, rc)
    mixer_sum = plane_scatter(contract_last(mixed, mixer_last).astype(BF16), 6)
    residual = inputs + mixer_sum
    scaled_two, inverse_two, normed_two = normalize(residual, gains[1])
    normed_two = plane_gather(normed_two, 7)

    mlp_full = jnp.concatenate(mlp_blocks)
    mlp_gate, mlp_up, mlp_down = (mlp_full[:, n * f8 : (n + 1) * f8] for n in range(3))
    gg = jnp.dot(normed_two, mlp_gate, preferred_element_type=F32)
    uu = jnp.dot(normed_two, mlp_up, preferred_element_type=F32)
    dhid = jnp.dot(grad_out, mlp_down, preferred_element_type=F32)
    gelu, inner = gelu_parts(gg)
    hid = (gelu * uu).astype(BF16)
    dgg = (dhid * uu * gelu_slope(gg, inner)).astype(BF16)
    duu = (dhid * gelu).astype(BF16)
    dnormed_two = contract_last(dgg, mlp_gate) + contract_last(duu, mlp_up)
    dnormed_two = plane_scatter(dnormed_two.astype(BF16), 8)

    def line_sum(term):
        term = term.astype(BF16)
        rows = term.shape[0] // length
        return line_scatter([term[k * rows : (k + 1) * rows] for k in range(length)], length)

    down_grad = line_sum(contract_first(grad_out, hid))
    gate_grad = line_sum(contract_first(normed_two, dgg))
    up_grad = line_sum(contract_first(normed_two, duu))
    mlp_sum = plane_scatter(contract_last(hid, mlp_down).astype(BF16), 9)
    block_output = turned_back((residual + mlp_sum).astype(BF16))

    grad_from_second, gain_two_grad = normalize_back(dnormed_two, scaled_two, inverse_two, gains[1])
    grad_residual = cotangent + grad_from_second
    dmz = plane_gather(grad_residual.astype(BF16), 10)
    dmix = jnp.dot(dmz, mixer_last, preferred_element_type=F32).reshape(4, span, rc)
    out_grad_sum = line_sum(contract_first(dmz, mixed)[:, :r8])
    dproj, dgate, chan_grad = recur_backward(dmix, gate, chan, kept, projected, length, 11)
    dproj = dproj.reshape(4 * span, 2 * rc)
    dgate = dgate.reshape(4 * span, 2 * rc)
    dnormed_one = plane_scatter(contract_last(dproj, mixer_first).astype(BF16), 12)
    first_grad = contract_first(normed_one, dproj)
    proj_grad_sum = line_sum(
        jnp.concatenate([first_grad[:, :r8], first_grad[:, rc : rc + r8]], axis=1)
    )
    gate_full_grad = contract_first(kept[4].reshape(4 * span, rc), dgate)

    grad_from_first, gain_one_grad = normalize_back(dnormed_one, scaled_one, inverse_one, gains[0])
    input_grad = turned_back(grad_residual + grad_from_first)

    mlp_sums = [gate_grad, up_grad, down_grad]
    mixer_sums = [proj_grad_sum, out_grad_sum]
    squares = sum(jnp.sum(g * g) for g in mlp_sums + mixer_sums)
    mlp_back = jnp.stack([g.astype(BF16).reshape(8, share, f8) for g in mlp_sums], axis=2)
    mlp_back = plane_exchange(mlp_back.reshape(8, share, 3 * f8), 13)
    mixer_back = jnp.concatenate([g.astype(BF16).reshape(8, share, -1) for g in mixer_sums], axis=2)

    gains_back = jnp.stack([gain_one_grad, gain_two_grad])
    gains_back = gains_back.reshape(2, length, 8, share).transpose(2, 1, 0, 3)
    gains_back = jnp.pad(gains_back, ((0, 0), (0, 0), (0, 6), (0, 128 - share)))
    blocks = []
    for h in range(heads):
        at = slice(h * head, (h + 1) * head)
        blocks.append(
            jnp.concatenate([gate_full_grad[at, at], gate_full_grad[at, rc + h * head : rc + (h + 1) * head]], axis=1)
        )
    gate_grad_own = jnp.concatenate(blocks)
    chan_grad = jnp.sum(chan_grad, axis=1)[:, :r8]
    chan_grad = jnp.concatenate([chan_grad[:7], (8.0 * jax.nn.sigmoid(-lam) * chan_grad[7])[None]])
    gate_back = jnp.concatenate([gate_grad_own, chan_grad.T], axis=1).reshape(length, gate_rows, 2 * head + 8)
    gate_back = jnp.pad(
        gate_back, ((0, 0), (0, gate_pad - gate_rows), (0, rc - 2 * head - 8))
    )
    gate_back = jnp.roll(gate_back, -z, axis=0)
    squares_in = jnp.zeros((8, 128), F32).at[0, 0].set(squares)
    mixer_back, gains_sum, gate_sum, squares_sum = last(
        mixer_back, gains_back, gate_back, squares_in, length, 14
    )

    grad_norm = jnp.sqrt(jnp.sum(squares_sum))
    factor = clip_limit / jnp.maximum(grad_norm, clip_limit)
    mixer_grad = mixer_back.astype(F32).reshape(8, share, 3, r8).transpose(1, 2, 0, 3).reshape(share, 3 * lru)
    mlp_grad = mlp_back.astype(F32).reshape(8, share, 3, f8).transpose(1, 2, 0, 3).reshape(share, 3 * hidden)
    gains_up = adam_step(
        norm_gains, gains_sum[:2, :share], first_gains, second_gains, factor, rate_gains, 0.0
    )
    mixer_up = adam_step(
        mixer_weight, mixer_grad, first_mixer, second_mixer, factor, rate_matrix, decay_matrix
    )
    gate_up = adam_step(
        gate_weight, gate_sum[:gate_rows, : 2 * head], first_gate, second_gate, factor, rate_matrix, decay_matrix
    )
    chan_up = adam_step(
        chan_params, gate_sum[:gate_rows, 2 * head : 2 * head + 8].T, first_chan, second_chan, factor,
        rate_channel, 0.0,
    )
    mlp_up = adam_step(
        mlp_weight, mlp_grad, first_mlp, second_mlp, factor, rate_matrix, decay_matrix
    )
    return (
        block_output[None],
        input_grad[None],
        grad_norm,
        *gains_up,
        *mixer_up,
        *gate_up,
        *chan_up,
        *mlp_up,
    )


def solution(mesh):
    rows = P(("batch", "seq"), None)
    columns = P(None, ("batch", "seq"))
    data = P("batch", "seq", None)
    weights = (columns, rows, rows, columns, rows)
    in_specs = (data, data) + weights * 3
    triples = tuple(spec for spec in weights for _ in range(3))
    return jax.shard_map(
        on_device,
        mesh=mesh,
        in_specs=in_specs,
        out_specs=(data, data, P()) + triples,
        check_vma=False,
    )
```

```python
import functools
import math

import jax
import jax.numpy as jnp
from jax import lax
from jax.experimental import pallas as pl
from jax.experimental.pallas import tpu as pltpu
from jax.sharding import PartitionSpec as P

STEP = 10
norm_eps = 1e-06
clip_limit = 1.0
beta_first = 0.9
beta_second = 0.999
adam_eps = 1e-08
rate_matrix = 0.05
rate_gains = 0.8
rate_channel = 2.0
decay_matrix = 0.1

MESH = pl.DeviceIdType.MESH
F32 = jnp.float32
BF16 = jnp.bfloat16
ANY = pl.BlockSpec(memory_space=pl.ANY)
VM = pl.BlockSpec(memory_space=pltpu.VMEM)
FLIPS = [(fy, fc, fx) for fy in (0, 1) for fc in (0, 1) for fx in (0, 1) if fy + fc + fx]
GELU_SCALE = math.sqrt(2.0 / math.pi)


def place():
    b = lax.axis_index("batch")
    s = lax.axis_index("seq")
    y, z = b // 2, s // 2
    return y, b - 2 * y, z, s - 2 * z


def device(y, c, z, x):
    return (y * 2 + c, z * 2 + x)


def rank(y, c, x):
    return (y * 2 + c) * 2 + x


def flip(v, f):
    return 1 - v if f else v


def greet(peers):
    barrier = pltpu.get_barrier_semaphore()
    for peer in peers:
        pl.semaphore_signal(barrier, inc=1, device_id=peer, device_id_type=MESH)
    pl.semaphore_wait(barrier, len(peers))


def remote(src, dst, send, recv, to):
    copy = pltpu.make_async_remote_copy(
        src_ref=src, dst_ref=dst, send_sem=send, recv_sem=recv, device_id=to, device_id_type=MESH
    )
    copy.start()
    return copy


def params(collective_id, vmem=None):
    return pltpu.CompilerParams(
        collective_id=collective_id, has_side_effects=True, vmem_limit_bytes=vmem
    )


DMA = pltpu.SemaphoreType.DMA


def gather_peers():
    y, c, z, x = place()
    return [device(y, c, z, 1 - x), device(1 - y, c, z, x), device(y, 1 - c, z, x)]


class Gather:
    def __init__(self, a, o, loc, ss, rs):
        y, c, z, x = place()
        self.to_x, self.to_y, self.to_c = gather_peers()
        self.me, self.bx = rank(y, c, x), rank(y, c, 1 - x)
        self.by, self.bd = rank(1 - y, c, x), rank(1 - y, c, 1 - x)
        half = a.shape[0] // 2
        self.lo, self.hi = pl.ds(0, half), pl.ds(half, half)
        self.a, self.o, self.loc, self.ss, self.rs = a, o, loc, ss, rs
        self.done = []

    def send(self, src, dst, k, to):
        copy = remote(src, dst, self.ss.at[k], self.rs.at[k], to)
        self.done.append(copy)
        return copy

    def relay(self, block, part, k, to):
        return self.send(self.o.at[block, part], self.o.at[block, part], k, to)

    def begin(self):
        a, o, me, lo, hi = self.a, self.o, self.me, self.lo, self.hi
        self.s0 = self.send(a.at[lo], o.at[me, lo], 0, self.to_x)
        self.s1 = self.send(a.at[hi], o.at[me, hi], 1, self.to_y)
        self.s2 = self.send(a.at[hi], o.at[me, hi], 2, self.to_x)
        self.s3 = self.send(a.at[lo], o.at[me, lo], 3, self.to_y)
        self.s4 = self.send(a, o.at[me], 4, self.to_c)
        self.own = pltpu.make_async_copy(a, o.at[me], self.loc)
        self.own.start()

    def middle(self):
        self.s0.wait_recv()
        self.s5 = self.relay(self.bx, self.lo, 5, self.to_y)
        self.last = [self.s4, self.relay(self.bx, self.lo, 7, self.to_c)]
        self.s1.wait_recv()
        self.s6 = self.relay(self.by, self.hi, 6, self.to_x)
        self.last.append(self.relay(self.by, self.hi, 8, self.to_c))

    def end(self):
        self.s2.wait_recv()
        self.last.append(self.relay(self.bx, self.hi, 9, self.to_c))
        self.s3.wait_recv()
        self.last.append(self.relay(self.by, self.lo, 10, self.to_c))
        self.s5.wait_recv()
        self.last.append(self.relay(self.bd, self.lo, 11, self.to_c))
        self.s6.wait_recv()
        self.last.append(self.relay(self.bd, self.hi, 12, self.to_c))
        for copy in self.last:
            copy.wait_recv()
        for copy in self.done:
            copy.wait_send()
        self.own.wait()


class Hop:
    def __init__(self, kind, hop, length, refs, ss, rs):
        y, c, z, x = place()
        self.kind, self.hop, self.length, self.z = kind, hop, length, z
        self.up = device(y, c, lax.rem(z + 1, length), x)
        self.down = device(y, c, lax.rem(z + length - 1, length), x)
        self.ss, self.rs = ss, rs
        if kind == "gather":
            self.line = LineGather(refs[0], length, ss, rs)
            return
        n = len(refs) // (3 if hop == 1 else 4)
        if hop == 1:
            up, down = [r.at[length - 1] for r in refs[:n]], [r.at[1] for r in refs[:n]]
        else:
            up, down = refs[:n], refs[n : 2 * n]
        self.pairs = tuple(zip(up, refs[-2 * n : -n])), tuple(zip(down, refs[-n:]))

    def peers(self):
        return [self.up, self.down]

    def when(self, up, down, act):
        for way, condition in enumerate((up, down)):

            @pl.when(condition)
            def _():
                for n, (src, dst) in enumerate(self.pairs[way]):
                    act(
                        pltpu.make_async_remote_copy(
                            src, dst, self.ss.at[way, n], self.rs.at[way, n],
                            device_id=(self.up, self.down)[way], device_id_type=MESH,
                        )
                    )

    def sending(self):
        return self.z <= self.hop - 1, self.z >= self.length - self.hop

    def start(self):
        if self.kind == "gather":
            self.line.start(self.hop)
        else:
            self.when(*self.sending(), lambda copy: copy.start())

    def finish(self):
        if self.kind == "gather":
            self.line.arrive(self.hop)
            self.line.sends(self.hop, lambda copy: copy.wait_send())
            return
        z, last = self.z, self.length - 1
        self.when(
            jnp.logical_and(z >= 1, z <= self.hop),
            jnp.logical_and(z <= last - 1, z >= last - self.hop),
            lambda copy: copy.wait_recv(),
        )
        self.when(*self.sending(), lambda copy: copy.wait_send())


def hop_results(carried):
    kind, hop, operands = carried
    shapes = [v.shape[1:] if kind == "scatter" and hop == 1 else v.shape for v in operands]
    shapes = [jax.ShapeDtypeStruct(shape, v.dtype) for shape, v in zip(shapes, operands)]
    return shapes * 2 if kind == "scatter" and hop == 1 else shapes


def call_carrying(body, operands, in_specs, out_shapes, out_specs, scratch, carried, length, **kwargs):
    if carried is None:
        results = pl.pallas_call(
            functools.partial(body, None), out_shape=tuple(out_shapes), in_specs=list(in_specs),
            out_specs=tuple(out_specs), scratch_shapes=list(scratch), **kwargs,
        )(*operands)
        return results, ()
    kind, hop, extra = carried
    more = hop_results(carried)
    ins, outs = len(operands), len(out_shapes)

    def kernel(*refs):
        hop_in, rest = refs[ins : ins + len(extra)], refs[ins + len(extra) :]
        hop_out, (ss, rs) = rest[outs : outs + len(more)], rest[-2:]
        used = hop_out if kind == "gather" else tuple(hop_in) + tuple(hop_out)
        body(
            Hop(kind, hop, length, used, ss, rs), *refs[:ins], *rest[:outs], *rest[outs + len(more) : -2]
        )

    results = pl.pallas_call(
        kernel,
        out_shape=tuple(out_shapes) + tuple(more),
        in_specs=list(in_specs) + [ANY] * len(extra),
        out_specs=tuple(out_specs) + (ANY,) * len(more),
        scratch_shapes=list(scratch) + [DMA((2, length)), DMA((2, length))],
        input_output_aliases={ins: outs} if kind == "gather" else {},
        **kwargs,
    )(*operands, *extra)
    return results[:outs], results[outs:]


def gather_kernel(hop, a, o, loc, ss, rs):
    greet(gather_peers() + (hop.peers() if hop else []))
    steps = Gather(a, o, loc, ss, rs)
    steps.begin()
    if hop:
        hop.start()
    steps.middle()
    steps.end()
    if hop:
        hop.finish()


def plane_gather(a, collective_id, carried=None, length=0):
    rows, width = a.shape
    (out,), more = call_carrying(
        gather_kernel, [a], [ANY], [jax.ShapeDtypeStruct((8, rows, width), a.dtype)], [ANY],
        [DMA, DMA((13,)), DMA((13,))], carried, length,
        compiler_params=params(collective_id),
        cost_estimate=pl.CostEstimate(flops=0, bytes_accessed=120 * 2**20, transcendentals=0),
    )
    return out.reshape(8 * rows, width), more


def scatter_kernel(hop, p, o, mine, sib, part, got, loc, ss, rs):
    greet(gather_peers() + (hop.peers() if hop else []))
    if hop:
        hop.start()
    scatter_steps(p, o, mine, sib, part, got, loc, ss, rs)
    if hop:
        hop.finish()


def scatter_steps(p, o, mine, sib, part, got, loc, ss, rs, mark=lambda: None):
    y, c, z, x = place()
    to_x, to_y, to_c = gather_peers()
    half = o.shape[0] // 2
    step = 16
    cut = (pl.ds(0, half), pl.ds(half, half))
    where = ((1 - y, 1 - x), (1 - y, x), (y, 1 - x), (y, x))
    order = [(0, 0), (0, 1), (1, 0), (2, 1), (2, 0), (1, 1), (3, 0), (3, 1)]
    from_c, own, sends = {}, {}, []
    for n, (t, h) in enumerate(order):
        ty, tx = where[t]
        own[t, h] = pltpu.make_async_copy(
            p.at[rank(ty, c, tx), cut[h]], mine.at[t, h], loc.at[n]
        )
        own[t, h].start()
        from_c[t, h] = remote(
            p.at[rank(ty, 1 - c, tx), cut[h]], sib.at[t, h], ss.at[n], rs.at[n], to_c
        )
        sends.append(from_c[t, h])

    def add(dst, t, h, extra):
        own[t, h].wait()
        from_c[t, h].wait_recv()

        @pl.loop(0, half // step)
        def _(i):
            at = pl.ds(pl.multiple_of(i * step, step), step)
            total = mine[t, h, at].astype(F32) + sib[t, h, at].astype(F32)
            for ref in extra:
                total = total + ref[at].astype(F32)
            dst[at] = total.astype(dst.dtype)

    def send(k, slot, to):
        copy = remote(part.at[k], got.at[slot], ss.at[8 + k], rs.at[8 + slot], to)
        sends.append(copy)
        return copy

    def arrival(slot):
        return pltpu.make_async_remote_copy(
            src_ref=part.at[0], dst_ref=got.at[slot], send_sem=ss.at[8], recv_sem=rs.at[8 + slot],
            device_id=to_x, device_id_type=MESH,
        )

    add(part.at[0], 0, 0, ())
    send(0, 1, to_y)
    add(part.at[1], 0, 1, ())
    send(1, 3, to_x)
    add(part.at[2], 1, 0, ())
    send(2, 0, to_y)
    add(part.at[3], 2, 1, ())
    send(3, 2, to_x)
    arrival(1).wait_recv()
    add(part.at[4], 2, 0, (got.at[1],))
    send(4, 4, to_x)
    arrival(3).wait_recv()
    add(part.at[5], 1, 1, (got.at[3],))
    send(5, 5, to_y)
    mark()
    arrival(0).wait_recv()
    arrival(4).wait_recv()
    add(o.at[cut[0]], 3, 0, (got.at[0], got.at[4]))
    arrival(2).wait_recv()
    arrival(5).wait_recv()
    add(o.at[cut[1]], 3, 1, (got.at[2], got.at[5]))
    for copy in sends:
        copy.wait_send()


def scatter_scratch(half, width):
    return [
        pltpu.VMEM((4, 2, half, width), BF16),
        pltpu.VMEM((4, 2, half, width), BF16),
        pltpu.VMEM((6, half, width), BF16),
        pltpu.VMEM((6, half, width), BF16),
        DMA((8,)),
        DMA((14,)),
        DMA((14,)),
    ]


def plane_scatter(p, collective_id, carried=None, length=0):
    width = p.shape[1]
    rows = p.shape[0] // 8
    (out,), more = call_carrying(
        scatter_kernel, [p.reshape(8, rows, width)], [ANY],
        [jax.ShapeDtypeStruct((rows, width), F32)], [VM],
        scatter_scratch(rows // 2, width), carried, length,
        compiler_params=params(collective_id, 40 * 2**20),
        cost_estimate=pl.CostEstimate(flops=0, bytes_accessed=140 * 2**20, transcendentals=0),
    )
    return out, more


def exchange_steps(a, o, loc, ss, rs):
    y, c, z, x = place()
    me = rank(y, c, x)
    copies = []
    for n, (fy, fc, fx) in enumerate(FLIPS):
        ty, tc, tx = flip(y, fy), flip(c, fc), flip(x, fx)
        copies.append(
            remote(a.at[rank(ty, tc, tx)], o.at[me], ss.at[n], rs.at[n], device(ty, tc, z, tx))
        )
    own = pltpu.make_async_copy(a.at[me], o.at[me], loc)
    own.start()
    return copies, own


def plane_peers():
    y, c, z, x = place()
    return [device(flip(y, fy), flip(c, fc), z, flip(x, fx)) for fy, fc, fx in FLIPS]


def line_peers(length):
    y, c, z, x = place()
    return [device(y, c, lax.rem(z + k, length), x) for k in range(1, length)]


class LineGather:
    def __init__(self, buf, length, ss, rs):
        y, c, z, x = place()
        self.z, self.length, self.buf, self.ss, self.rs = z, length, buf, ss, rs
        self.up = device(y, c, lax.rem(z + 1, length), x)
        self.down = device(y, c, lax.rem(z + length - 1, length), x)

    def copy(self, hop, upward):
        length, buf = self.length, self.buf
        src, dst = ((length - hop + 1) % length, length - hop) if upward else (hop - 1, hop)
        way = 0 if upward else 1
        return pltpu.make_async_remote_copy(
            src_ref=buf.at[src], dst_ref=buf.at[dst], send_sem=self.ss.at[way, hop - 1],
            recv_sem=self.rs.at[way, hop - 1], device_id=self.up if upward else self.down,
            device_id_type=MESH,
        )

    def sends(self, hop, act):
        z, length = self.z, self.length

        @pl.when(jnp.logical_and(z + 1 < length, z >= hop - 1))
        def _():
            act(self.copy(hop, True))

        @pl.when(jnp.logical_and(z >= 1, z + hop - 1 < length))
        def _():
            act(self.copy(hop, False))

    def start(self, hop):
        self.sends(hop, lambda copy: copy.start())

    def arrive(self, hop):
        z, length = self.z, self.length

        @pl.when(z >= hop)
        def _():
            self.copy(hop, True).wait_recv()

        @pl.when(z + hop < length)
        def _():
            self.copy(hop, False).wait_recv()

    def finish(self):
        for hop in range(1, self.length):
            self.sends(hop, lambda copy: copy.wait_send())


class LineScatter:
    def __init__(self, g, total, up_mine, down_mine, up_got, down_got, loc, ss, rs):
        y, c, z, x = place()
        self.length = length = g.shape[0]
        self.g, self.total = g, total
        self.mine, self.got = (up_mine, down_mine), (up_got, down_got)
        self.loc, self.ss, self.rs = loc, ss, rs
        self.to = (device(y, c, lax.rem(z + 1, length), x), device(y, c, lax.rem(z + length - 1, length), x))
        self.far = (z, length - 1 - z)

    def load(self, way, hop):
        k = self.length - hop if way == 0 else hop
        return pltpu.make_async_copy(self.g.at[k], self.mine[way].at[hop - 1], self.loc.at[way, hop - 1])

    def load_own(self):
        return pltpu.make_async_copy(self.g.at[0], self.total, self.loc.at[0, self.length - 1])

    def copy(self, way, hop):
        return pltpu.make_async_remote_copy(
            src_ref=self.mine[way].at[hop - 1], dst_ref=self.got[way].at[hop - 1],
            send_sem=self.ss.at[way, hop - 1], recv_sem=self.rs.at[way, hop - 1],
            device_id=self.to[way], device_id_type=MESH,
        )

    def begin(self):
        for hop in range(1, self.length):
            for way in (0, 1):
                self.load(way, hop).start()
        self.load_own().start()

    def add(self, dst, src):
        @pl.loop(0, dst.shape[0] // 16)
        def _(i):
            at = pl.ds(pl.multiple_of(i * 16, 16), 16)
            dst[at] = (dst[at].astype(F32) + src[at].astype(F32)).astype(dst.dtype)

    def start(self, hop):
        for way in (0, 1):
            far = self.far[way]
            self.load(way, hop).wait()
            if hop > 1:

                @pl.when(jnp.logical_and(far >= 1, far <= hop - 1))
                def _():
                    self.copy(way, hop - 1).wait_recv()
                    self.add(self.mine[way].at[hop - 1], self.got[way].at[hop - 2])

            @pl.when(far <= hop - 1)
            def _():
                self.copy(way, hop).start()

    def end(self, result):
        last = self.length - 1
        self.load_own().wait()
        for way in (0, 1):

            @pl.when(self.far[way] >= 1)
            def _():
                self.copy(way, last).wait_recv()

        def each(act):
            @pl.loop(0, result.shape[0] // 16)
            def _(i):
                act(pl.ds(pl.multiple_of(i * 16, 16), 16))

        def own(at):
            result[at] = self.total[at].astype(F32)

        each(own)
        for way in (0, 1):

            @pl.when(self.far[way] >= 1)
            def _():
                def more(at):
                    result[at] += self.got[way][last - 1, at].astype(F32)

                each(more)

        for hop in range(1, self.length):
            for way in (0, 1):

                @pl.when(self.far[way] <= hop - 1)
                def _():
                    self.copy(way, hop).wait_send()


def closing_kernel(p, e, g, o, e_o, g_o, *scratch):
    scatter_refs, exchange_refs, line_refs = scratch[:7], scratch[7:10], scratch[10:]
    length = g.shape[0]
    greet(plane_peers() + line_peers(length))
    line = LineScatter(g, *line_refs)
    line.begin()
    line.start(1)
    hops = list(range(2, length))

    def mark():
        if hops:
            line.start(hops.pop(0))

    scatter_steps(p, o, *scatter_refs, mark=mark)
    copies, own = exchange_steps(e, e_o, *exchange_refs)
    while hops:
        mark()
    line.end(g_o)
    for copy in copies:
        copy.wait()
    own.wait()


def closing(p, e, g, collective_id):
    rows, width = p.shape[0] // 8, p.shape[1]
    length = g.shape[0]
    hops = (length - 1,) + g.shape[1:]
    return pl.pallas_call(
        closing_kernel,
        out_shape=(
            jax.ShapeDtypeStruct((rows, width), F32),
            jax.ShapeDtypeStruct(e.shape, e.dtype),
            jax.ShapeDtypeStruct(g.shape[1:], F32),
        ),
        in_specs=[ANY] * 3,
        out_specs=(VM, ANY, VM),
        scratch_shapes=scatter_scratch(rows // 2, width)
        + [DMA, DMA((7,)), DMA((7,)), pltpu.VMEM(g.shape[1:], BF16)]
        + [pltpu.VMEM(hops, BF16)] * 4
        + [DMA((2, length))] * 3,
        compiler_params=params(collective_id, 56 * 2**20),
        cost_estimate=pl.CostEstimate(flops=0, bytes_accessed=250 * 2**20, transcendentals=0),
    )(p.reshape(8, rows, width), e, g)


def first_kernel(
    length, inputs, mixer_w, mlp_w, gn, gp, normed_o, wm_o, wf_o, gains_o, gp_o,
    normed, gn_all, wm, wf, loc, ms, mr, fs, fr, line_s, line_r, gain_s, gain_r, move_s, move_r,
    gather_s, gather_r, hop_s, hop_r,
):
    y, c, z, x = place()
    s = 2 * z + x
    me = rank(y, c, x)
    rows, width = inputs.shape
    pair = width // (4 * length)
    line = line_peers(length)
    plane = plane_peers()
    to_z, to_x = lax.rem(s, length), s // length
    moves = jnp.where(jnp.logical_and(to_z == z, to_x == x), 0, 1)
    src = x * length + z
    from_z = src // 2
    from_x = src - 2 * from_z
    barrier = pltpu.get_barrier_semaphore()
    for peer in line + plane:
        pl.semaphore_signal(barrier, inc=1, device_id=peer, device_id_type=MESH)

    @pl.when(moves == 1)
    def _():
        pl.semaphore_signal(barrier, inc=1, device_id=device(y, c, to_z, to_x), device_id_type=MESH)
        pl.semaphore_signal(barrier, inc=1, device_id=device(y, c, from_z, from_x), device_id_type=MESH)

    pl.semaphore_wait(barrier, len(line) + len(plane) + 2 * moves)

    gn_all[me, z] = gn[...]
    gains = [
        remote(gn, gn_all.at[me, z], line_s.at[0, k], line_r.at[0, k], line[k]) for k in range(length - 1)
    ]
    for pack, source in ((wm, mixer_w), (wf, mlp_w)):
        part = pack.shape[2] // 3
        for t in range(8):
            for j in range(3):
                start = (j * 8 + t) * part
                pack[t, :, j * part : (j + 1) * part] = source[:, start : start + part].astype(BF16)
        if pack is wm:
            for copy in gains:
                copy.wait()
            spread = [
                remote(gn_all.at[me], gn_all.at[me], gain_s.at[n], gain_r.at[n], plane[n])
                for n in range(7)
            ]
            mixer, mixer_own = exchange_steps(wm, wm_o.at[0], loc.at[0], ms, mr)

    @pl.when(moves == 1)
    def _():
        copy = remote(gp, gp_o.at[to_z], move_s, move_r, device(y, c, to_z, to_x))
        copy.wait()

    @pl.when(moves == 0)
    def _():
        copy = pltpu.make_async_copy(gp, gp_o.at[z], loc.at[2])
        copy.start()
        copy.wait()

    gates = [
        remote(gp_o.at[z], gp_o.at[z], line_s.at[1, k], line_r.at[1, k], line[k])
        for k in range(length - 1)
    ]
    for copy in spread:
        copy.wait()
    for k in range(length):
        other = lax.rem(z + k, length)
        for b in range(4):
            at = slice((4 * k + b) * pair, (4 * k + b + 1) * pair)
            gains_o[:, at] = (gn_all[2 * b, other] + gn_all[2 * b + 1, other])[:, :pair]

    @pl.loop(0, rows // 16)
    def _(i):
        at = pl.ds(pl.multiple_of(i * 16, 16), 16)
        v = inputs[at].astype(F32)
        inverse = lax.rsqrt(jnp.sum(v * v, axis=-1, keepdims=True) * (1.0 / width) + norm_eps)
        normed[at] = (v * inverse * gains_o[0:1]).astype(BF16)

    gather = Gather(normed, normed_o, loc.at[1], gather_s, gather_r)
    gather.begin()
    for copy in mixer:
        copy.wait()
    mixer_own.wait()
    hops = LineGather(wm_o, length, hop_s, hop_r)
    hops.start(1)
    feed, feed_own = exchange_steps(wf, wf_o.at[0], loc.at[3], fs, fr)
    gather.middle()
    hops.arrive(1)
    if length > 2:
        hops.start(2)
    gather.end()
    for hop in range(2, length):
        hops.arrive(hop)
        if hop + 1 < length:
            hops.start(hop + 1)
    for copy in feed + gates:
        copy.wait()
    feed_own.wait()
    hops.finish()


def first(inputs, mixer, mlp, gn, gp, length, collective_id):
    rows, width = inputs.shape
    share = mixer.shape[0]
    wm, wf = (8, share, mixer.shape[1] // 8), (8, share, mlp.shape[1] // 8)
    return pl.pallas_call(
        functools.partial(first_kernel, length),
        out_shape=(
            jax.ShapeDtypeStruct((8, rows, width), BF16),
            jax.ShapeDtypeStruct((length,) + wm, BF16),
            jax.ShapeDtypeStruct((length,) + wf, BF16),
            jax.ShapeDtypeStruct((8, width), F32),
            jax.ShapeDtypeStruct((length,) + gp.shape, gp.dtype),
        ),
        in_specs=[VM, VM, VM, VM, ANY],
        out_specs=(ANY, ANY, ANY, VM, ANY),
        scratch_shapes=[
            pltpu.VMEM((rows, width), BF16),
            pltpu.VMEM((8, length, 8, 128), F32),
            pltpu.VMEM(wm, BF16),
            pltpu.VMEM(wf, BF16),
            DMA((4,)), DMA((7,)), DMA((7,)), DMA((7,)), DMA((7,)),
            DMA((2, length)), DMA((2, length)), DMA((7,)), DMA((7,)), DMA, DMA,
            DMA((13,)), DMA((13,)), DMA((2, length)), DMA((2, length)),
        ],
        compiler_params=params(collective_id, 40 * 2**20),
        cost_estimate=pl.CostEstimate(flops=0, bytes_accessed=300 * 2**20, transcendentals=0),
    )(inputs, mixer, mlp, gn, gp)


def last_kernel(
    length, wm, gn, gp, sq, wm_o, gn_o, gp_o, sq_o,
    gn_in, gn_mid, gn_got, gn_fin, gp_got, gp_sum, gp_fin, sq_plane, sq_line, sq_mid,
    loc, ss, rs, gs, gr, ls, lr, move_s, move_r,
):
    y, c, z, x = place()
    s = 2 * z + x
    me = rank(y, c, x)
    line = line_peers(length)
    plane = plane_peers()
    owner = x * length + z
    to_z = owner // 2
    to_x = owner - 2 * to_z
    from_z, from_x = lax.rem(s, length), s // length
    moves = jnp.where(jnp.logical_and(to_z == z, to_x == x), 0, 1)
    barrier = pltpu.get_barrier_semaphore()
    for peer in line + plane:
        pl.semaphore_signal(barrier, inc=1, device_id=peer, device_id_type=MESH)

    @pl.when(moves == 1)
    def _():
        pl.semaphore_signal(barrier, inc=1, device_id=device(y, c, to_z, to_x), device_id_type=MESH)
        pl.semaphore_signal(barrier, inc=1, device_id=device(y, c, from_z, from_x), device_id_type=MESH)

    pl.semaphore_wait(barrier, len(line) + len(plane) + 2 * moves)

    gain = []
    for n, (fy, fc, fx) in enumerate(FLIPS):
        to = rank(flip(y, fy), flip(c, fc), flip(x, fx))
        gain.append(remote(gn.at[to], gn_in.at[n], gs.at[0, n], gr.at[0, n], plane[n]))
    gate = [
        remote(gp.at[k + 1], gp_got.at[k], ls.at[0, k], lr.at[0, k], line[k]) for k in range(length - 1)
    ]
    copies, own = exchange_steps(wm, wm_o, loc, ss, rs)
    for copy in gain:
        copy.wait()
    total = gn[me]
    for n in range(7):
        total = total + gn_in[n]
    gn_mid[...] = total
    gain_line = [
        remote(gn_mid.at[k + 1], gn_got.at[k], ls.at[1, k], lr.at[1, k], line[k])
        for k in range(length - 1)
    ]
    for copy in gate:
        copy.wait()
    total = gp[0]
    for k in range(length - 1):
        total = total + gp_got[k]
    gp_sum[...] = total

    @pl.when(moves == 1)
    def _():
        copy = remote(gp_sum, gp_fin, move_s, move_r, device(y, c, to_z, to_x))
        copy.wait()

    @pl.when(moves == 0)
    def _():
        gp_fin[...] = gp_sum[...]

    for copy in gain_line:
        copy.wait()
    total = gn_mid[0]
    for k in range(length - 1):
        total = total + gn_got[k]
    gn_o[...] = total
    gates = gp_fin[...]
    gp_o[...] = gates

    def tiles(v):
        v = v * v
        if v.shape[0] > 8:
            v = jnp.sum(v.reshape(v.shape[0] // 8, 8, v.shape[1]), axis=0)
        part = v[:, :128]
        for n in range(1, v.shape[1] // 128):
            part = part + v[:, n * 128 : (n + 1) * 128]
        return part

    sq_plane[me] = sq[...] + tiles(total) + tiles(gates)
    sums = [
        remote(sq_plane.at[me], sq_plane.at[me], gs.at[1, n], gr.at[1, n], plane[n]) for n in range(7)
    ]
    for copy in sums:
        copy.wait()
    total = sq_plane[0]
    for n in range(1, 8):
        total = total + sq_plane[n]
    sq_line[z] = total
    sums = [
        remote(sq_line.at[z], sq_line.at[z], ls.at[2, k], lr.at[2, k], line[k])
        for k in range(length - 1)
    ]
    for copy in sums:
        copy.wait()
    total = sq_line[0]
    for n in range(1, length):
        total = total + sq_line[n]
    sq_o[...] = total
    for copy in copies:
        copy.wait()
    own.wait()


def last(wm, gn, gp, sq, length, collective_id):
    small, rows = gn.shape[2:], gp.shape[1:]
    return pl.pallas_call(
        functools.partial(last_kernel, length),
        out_shape=(
            jax.ShapeDtypeStruct(wm.shape, wm.dtype),
            jax.ShapeDtypeStruct(small, F32),
            jax.ShapeDtypeStruct(rows, F32),
            jax.ShapeDtypeStruct((8, 128), F32),
        ),
        in_specs=[ANY, VM, VM, VM],
        out_specs=(ANY, VM, VM, VM),
        scratch_shapes=[
            pltpu.VMEM((7, length) + small, F32),
            pltpu.VMEM((length,) + small, F32),
            pltpu.VMEM((length,) + small, F32),
            pltpu.VMEM(small, F32),
            pltpu.VMEM((length,) + rows, F32),
            pltpu.VMEM(rows, F32),
            pltpu.VMEM(rows, F32),
            pltpu.VMEM((8, 8, 128), F32),
            pltpu.VMEM((length, 8, 128), F32),
            pltpu.VMEM((8, 128), F32),
            DMA, DMA((7,)), DMA((7,)), DMA((2, 7)), DMA((2, 7)),
            DMA((3, length)), DMA((3, length)), DMA, DMA,
        ],
        compiler_params=params(collective_id, 24 * 2**20),
    )(wm, gn, gp, sq)


def minus_expm1(v):
    series = 1.0 + v * (1.0 / 8.0)
    for n in (7.0, 6.0, 5.0, 4.0, 3.0, 2.0):
        series = 1.0 + series * v * (1.0 / n)
    return jnp.where(v > -0.5, -v * series, 1.0 - jnp.exp(v))


def gelu_parts(v):
    inner = jnp.tanh(GELU_SCALE * (v + 0.044715 * v * v * v))
    return 0.5 * v * (1.0 + inner), inner


def gelu_slope(v, inner):
    return 0.5 * (1.0 + inner) + 0.5 * v * (1.0 - inner * inner) * GELU_SCALE * (
        1.0 + 3.0 * 0.044715 * v * v
    )


CHUNK = 64


def forward_kernel(
    hop, length, proj, gate, chan, above, mixed, decay_o, width_o, recur_o, enter_o, conv_o, xe, se, ends_o, above_o,
    pre, loc_h, ends, carry, hs, hr, es, er, gather_l, gather_s, gather_r,
):
    y, c, z, x = place()
    line = line_peers(length)
    greet(line + gather_peers())
    seqs, span, rc = mixed.shape
    chunks = span // CHUNK
    gather = Gather(above, above_o, gather_l, gather_s, gather_r)
    ahead = device(y, c, lax.rem(z + 1, length), x)
    for b in range(seqs):
        xe[b, span : span + 8] = proj[b, span - 8 : span, rc:].astype(BF16).astype(F32)
    halo = remote(xe.at[:, pl.ds(span, 8)], xe.at[:, pl.ds(0, 8)], hs, hr, ahead)
    halo.wait_send()
    gather.begin()
    if hop:
        hop.start()

    @pl.loop(0, seqs * chunks)
    def _(i):
        b = i // chunks
        r = pl.multiple_of((i - b * chunks) * CHUNK, CHUNK)
        xe[b, pl.ds(r + 8, CHUNK)] = proj[b, pl.ds(r, CHUNK), rc:].astype(BF16).astype(F32)

    halo.wait_recv()

    @pl.when(z == 0)
    def _():
        xe[:, 0:8] = jnp.zeros((seqs, 8, rc), F32)

    @pl.loop(0, seqs * chunks)
    def _(i):
        b = i // chunks
        r = pl.multiple_of((i - b * chunks) * CHUNK, CHUNK)
        at = pl.ds(r, CHUNK)
        window = xe[b, pl.ds(r, CHUNK + 8)]
        total = chan[4:5] + chan[0:1] * window[8:]
        for k in (1, 2, 3):
            total = total + chan[k : k + 1] * pltpu.roll(window, k, 0)[8:]
        low = total.astype(BF16)
        conv_o[b, at] = low
        value = low.astype(F32)
        gates = jnp.dot(low, gate[...], preferred_element_type=F32)
        recur = jax.nn.sigmoid(gates[:, :rc] + chan[5:6])
        enter = jax.nn.sigmoid(gates[:, rc:] + chan[6:7])
        log_decay = -chan[7:8] * recur
        decay = jnp.exp(log_decay)
        width = jnp.sqrt(minus_expm1(2.0 * log_decay))
        recur_o[b, at] = recur
        enter_o[b, at] = enter
        decay_o[b, at] = decay
        width_o[b, at] = width
        loc_h[b, at] = width * enter * value

    gather.middle()
    row = lax.broadcasted_iota(jnp.int32, (8, rc), 0)

    def tile(i, held):
        at = pl.ds(pl.multiple_of(i * 8, 8), 8)
        new = []
        for b in range(seqs):
            a, h = decay_o[b, at], loc_h[b, at]
            for n in (1, 2, 4):
                keep = row >= n
                h = h + jnp.where(keep, a * pltpu.roll(h, n, 0), 0.0)
                a = jnp.where(keep, a * pltpu.roll(a, n, 0), a)
            h = h + a * held[b][1]
            a = a * held[b][0]
            loc_h[b, at] = h
            pre[b, at] = a
            new.append((a[7:8], h[7:8]))
        return tuple(new)

    one, zero = jnp.ones((1, rc), F32), jnp.zeros((1, rc), F32)
    final = lax.fori_loop(0, span // 8, tile, ((one, zero),) * seqs)
    for b in range(seqs):
        ends[z, 0, b] = jnp.broadcast_to(final[b][0], (8, rc))
        ends[z, 1, b] = jnp.broadcast_to(final[b][1], (8, rc))
        ends_o[b] = jnp.broadcast_to(final[b][0], (8, rc))
    moves = [remote(ends.at[z], ends.at[z], es.at[k], er.at[k], line[k]) for k in range(length - 1)]
    for copy in moves:
        copy.wait()
    carry[...] = jnp.zeros_like(carry)
    for k in range(length):
        carry[...] = jnp.where(k < z, ends[k, 0] * carry[...] + ends[k, 1], carry[...])

    for b in range(seqs):
        se[b, 0:8] = carry[b]

    @pl.loop(0, seqs * chunks)
    def _(i):
        b = i // chunks
        r = pl.multiple_of((i - b * chunks) * CHUNK, CHUNK)
        at = pl.ds(r, CHUNK)
        state = loc_h[b, at] + pre[b, at] * carry[b, 0:1]
        se[b, pl.ds(r + 8, CHUNK)] = state
        gelu, _ = gelu_parts(proj[b, at, :rc])
        mixed[b, at] = (state * gelu).astype(BF16)

    gather.end()
    if hop:
        hop.finish()


def recur_forward(proj, gate, chan, above, length, collective_id, carried):
    seqs, span, rc = proj.shape[0], proj.shape[1], proj.shape[2] // 2
    full = jax.ShapeDtypeStruct((seqs, span, rc), F32)
    longer = jax.ShapeDtypeStruct((seqs, span + 8, rc), F32)
    low = jax.ShapeDtypeStruct((seqs, span, rc), BF16)
    return call_carrying(
        lambda hop, *refs: forward_kernel(hop, length, *refs),
        [proj, gate, chan, above],
        [VM, VM, VM, ANY],
        (
            low, full, full, full, full, low, longer, longer,
            jax.ShapeDtypeStruct((seqs, 8, rc), F32),
            jax.ShapeDtypeStruct((8,) + above.shape, above.dtype),
        ),
        (VM,) * 9 + (ANY,),
        [
            pltpu.VMEM((seqs, span, rc), F32),
            pltpu.VMEM((seqs, span, rc), F32),
            pltpu.VMEM((length, 2, seqs, 8, rc), F32),
            pltpu.VMEM((seqs, 8, rc), F32),
            DMA, DMA, DMA((length,)), DMA((length,)),
            DMA, DMA((13,)), DMA((13,)),
        ],
        carried,
        length,
        compiler_params=params(collective_id, 56 * 2**20),
        cost_estimate=pl.CostEstimate(
            flops=2 * seqs * span * rc * rc * 2, bytes_accessed=100 * 2**20, transcendentals=0
        ),
    )


def backward_kernel(
    length, dmix, gate, chan, decay, width, recur, enter, conv, xe, se, ends_f, proj,
    dproj, dgate, gchan, suffix, grad, de, ends, carry, hs, hr, es, er,
):
    y, c, z, x = place()
    line = line_peers(length)
    greet(line)
    seqs, span, rc = decay.shape
    chunks = span // CHUNK

    @pl.loop(0, seqs * chunks)
    def _(i):
        b = i // chunks
        r = pl.multiple_of((i - b * chunks) * CHUNK, CHUNK)
        at = pl.ds(r, CHUNK)
        branch = proj[b, at]
        gelu, inner = gelu_parts(branch)
        above = dmix[b, at]
        state = se[b, pl.ds(r + 8, CHUNK)]
        grad[b, at] = above * gelu
        dproj[b, at, :rc] = (above * state * gelu_slope(branch, inner)).astype(BF16)

    row = lax.broadcasted_iota(jnp.int32, (8, rc), 0)

    def tile(i, held):
        at = pl.ds(pl.multiple_of(span - 8 - i * 8, 8), 8)
        new = []
        for b in range(seqs):
            product, total, following = held[b]
            plain, h = decay[b, at], grad[b, at]
            a = jnp.where(row == 7, following, pltpu.roll(plain, 7, 0))
            for n in (1, 2, 4):
                keep = row < 8 - n
                h = h + jnp.where(keep, a * pltpu.roll(h, 8 - n, 0), 0.0)
                a = jnp.where(keep, a * pltpu.roll(a, 8 - n, 0), a)
            h = h + a * total
            a = a * product
            grad[b, at] = h
            suffix[b, at] = a
            new.append((a[0:1], h[0:1], plain[0:1]))
        return tuple(new)

    one, zero = jnp.ones((1, rc), F32), jnp.zeros((1, rc), F32)
    final = lax.fori_loop(0, span // 8, tile, ((one, zero, one),) * seqs)
    for b in range(seqs):
        ends[z, 0, b] = ends_f[b]
        ends[z, 1, b] = jnp.broadcast_to(final[b][1] * final[b][2], (8, rc))
    moves = [remote(ends.at[z], ends.at[z], es.at[k], er.at[k], line[k]) for k in range(length - 1)]
    for copy in moves:
        copy.wait()
    carry[...] = jnp.zeros_like(carry)
    for k in reversed(range(length)):
        carry[...] = jnp.where(k > z, ends[k, 0] * carry[...] + ends[k, 1], carry[...])

    gchan[...] = jnp.zeros_like(gchan)

    def fold(v):
        return jnp.sum(v.reshape(v.shape[0] // 8, 8, v.shape[1]), axis=0)

    @pl.loop(0, seqs * chunks)
    def _(i):
        b = i // chunks
        r = pl.multiple_of((i - b * chunks) * CHUNK, CHUNK)
        at = pl.ds(r, CHUNK)
        g = grad[b, at] + suffix[b, at] * carry[b, 0:1]
        a, w, ra, ri = decay[b, at], width[b, at], recur[b, at], enter[b, at]
        value = conv[b, at].astype(F32)
        before = pltpu.roll(se[b, pl.ds(r, CHUNK + 8)], 1, 0)[8:]
        dla = g * before * a - g * ri * value * (a * a) / w
        slope = dla * ra * (1.0 - ra)
        dpa = (-chan[7:8] * slope).astype(BF16)
        dpi = (g * w * value * ri * (1.0 - ri)).astype(BF16)
        dgate[b, at, :rc] = dpa
        dgate[b, at, rc:] = dpi
        gchan[5] += fold(dpa.astype(F32))
        gchan[6] += fold(dpi.astype(F32))
        gchan[7] += fold(dla * ra)
        back = lax.dot_general(
            dgate[b, at], gate[...], (((1,), (1,)), ((), ())), preferred_element_type=F32
        )
        dcv = (g * w * ri + back).astype(BF16).astype(F32)
        de[b, at] = dcv
        gchan[4] += fold(dcv)

    behind = device(y, c, lax.rem(z + length - 1, length), x)
    halo = remote(de.at[:, pl.ds(0, 8)], de.at[:, pl.ds(span, 8)], hs, hr, behind)
    halo.wait()

    @pl.when(z == length - 1)
    def _():
        de[:, span:] = jnp.zeros((seqs, 8, rc), F32)

    @pl.loop(0, seqs * chunks)
    def _(i):
        b = i // chunks
        r = pl.multiple_of((i - b * chunks) * CHUNK, CHUNK)
        at = pl.ds(r, CHUNK)
        window = de[b, pl.ds(r, CHUNK + 8)]
        inputs = xe[b, pl.ds(r, CHUNK + 8)]
        dcv = window[:CHUNK]
        total = chan[0:1] * dcv
        gchan[0] += fold(dcv * inputs[8:])
        for k in (1, 2, 3):
            total = total + chan[k : k + 1] * pltpu.roll(window, CHUNK + 8 - k, 0)[:CHUNK]
            gchan[k] += fold(dcv * pltpu.roll(inputs, k, 0)[8:])
        dproj[b, at, rc:] = total.astype(BF16)


def recur_backward(dmix, gate, chan, kept, proj, length, collective_id):
    decay, width, recur, enter, conv, xe, se, ends = kept
    seqs, span, rc = decay.shape
    wide = jax.ShapeDtypeStruct((seqs, span, 2 * rc), BF16)
    return pl.pallas_call(
        functools.partial(backward_kernel, length),
        grid=(1,),
        out_shape=(wide, wide, jax.ShapeDtypeStruct((8, 8, rc), F32)),
        in_specs=[VM] * 11 + [pl.BlockSpec((seqs, span, rc), lambda i: (0, 0, 0))],
        out_specs=(VM,) * 3,
        scratch_shapes=[
            pltpu.VMEM((seqs, span, rc), F32),
            pltpu.VMEM((seqs, span, rc), F32),
            pltpu.VMEM((seqs, span + 8, rc), F32),
            pltpu.VMEM((length, 2, seqs, 8, rc), F32),
            pltpu.VMEM((seqs, 8, rc), F32),
            DMA, DMA, DMA((length,)), DMA((length,)),
        ],
        compiler_params=params(collective_id, 60 * 2**20),
        cost_estimate=pl.CostEstimate(
            flops=2 * seqs * span * rc * rc * 2, bytes_accessed=120 * 2**20, transcendentals=0
        ),
    )(dmix, gate, chan, decay, width, recur, enter, conv, xe, se, ends, proj)


def routes(length, senders):
    pairs = [(z, z + 1) for z in range(length - 1) if z in senders]
    return [(2 * a + x, 2 * b + x) for a, b in pairs for x in range(2)]


def line_gather(block, length):
    up_routes = routes(length, range(length))
    down_routes = [(b, a) for a, b in up_routes]
    up = down = block
    ups, downs = [], []
    for _ in range(length - 1):
        up = lax.ppermute(up, "seq", up_routes)
        down = lax.ppermute(down, "seq", down_routes)
        ups.append(up)
        downs.append(down)
    z = lax.axis_index("seq") // 2
    blocks = [block]
    for k in range(1, length):
        blocks.append(jnp.where(z + k < length, downs[k - 1], ups[length - k - 1]))
    return blocks


def line_scatter(blocks, length):
    up = down = None
    for hop in range(1, length):
        up_routes = routes(length, range(hop))
        down_routes = [
            (2 * (length - 1 - a // 2) + a % 2, 2 * (length - 1 - b // 2) + b % 2) for a, b in up_routes
        ]
        up_block, down_block = blocks[length - hop], blocks[hop]
        if up is not None:
            up_block = (up_block.astype(F32) + up.astype(F32)).astype(BF16)
            down_block = (down_block.astype(F32) + down.astype(F32)).astype(BF16)
        up = lax.ppermute(up_block, "seq", up_routes)
        down = lax.ppermute(down_block, "seq", down_routes)
    return blocks[0].astype(F32) + up.astype(F32) + down.astype(F32)


def contract_last(left, right):
    return lax.dot_general(
        left, right, (((1,), (1,)), ((), ())), preferred_element_type=F32
    )


def contract_first(left, right):
    return lax.dot_general(
        left, right, (((0,), (0,)), ((), ())), preferred_element_type=F32
    )


def adam_step(weight, grad, first, second, factor, rate, decay_rate):
    clipped = grad * factor
    first_new = beta_first * first + (1.0 - beta_first) * clipped
    second_new = beta_second * second + (1.0 - beta_second) * clipped * clipped
    first_hat = first_new / (1.0 - beta_first**STEP)
    second_hat = second_new / (1.0 - beta_second**STEP)
    weight_new = weight - rate * (
        first_hat / (jnp.sqrt(second_hat) + adam_eps) + decay_rate * weight
    )
    return (first_new, second_new, weight_new)


def adam_kernel(rate, decay_rate, factor, w, g, m, v, m_o, v_o, w_o):
    first_new, second_new, weight_new = adam_step(
        w[...], g[0].astype(F32), m[...], v[...], factor[0:1, 0:1], rate, decay_rate
    )
    m_o[...] = first_new
    v_o[...] = second_new
    w_o[...] = weight_new


def adam_blocks(weight, grad, first, second, factor, rate, decay_rate):
    rows, part = grad.shape[1], grad.shape[2] // 3
    block = pl.BlockSpec((rows, part), lambda t, j: (0, j * 8 + t))
    shape = jax.ShapeDtypeStruct(weight.shape, F32)
    return pl.pallas_call(
        functools.partial(adam_kernel, rate, decay_rate),
        grid=(8, 3),
        out_shape=(shape,) * 3,
        in_specs=[
            pl.BlockSpec((8, 128), lambda t, j: (0, 0)),
            block,
            pl.BlockSpec((1, rows, part), lambda t, j: (t, 0, j)),
            block,
            block,
        ],
        out_specs=(block,) * 3,
        cost_estimate=pl.CostEstimate(flops=0, bytes_accessed=7 * 4 * weight.size, transcendentals=0),
    )(jnp.full((8, 128), factor), weight, grad, first, second)


def normalize(values, gain):
    inverse = lax.rsqrt(jnp.mean(values * values, axis=-1, keepdims=True) + norm_eps)
    scaled = values * inverse
    return (scaled, inverse, (scaled * gain).astype(BF16))


def normalize_back(grad_normed, scaled, inverse, gain):
    grad_scaled = grad_normed * gain
    gain_grad = jnp.sum(grad_normed * scaled, axis=0)
    inner = jnp.mean(grad_scaled * scaled, axis=-1, keepdims=True)
    return (inverse * (grad_scaled - scaled * inner), gain_grad)


def on_device(
    block_input,
    out_grad,
    norm_gains,
    mixer_weight,
    gate_weight,
    chan_params,
    mlp_weight,
    first_gains,
    first_mixer,
    first_gate,
    first_chan,
    first_mlp,
    second_gains,
    second_mixer,
    second_gate,
    second_chan,
    second_mlp,
):
    length = lax.axis_size("seq") // 2
    z = lax.axis_index("seq") // 2
    tokens, model = block_input.shape[1:]
    share = mixer_weight.shape[0]
    pair = 2 * share
    lru = mixer_weight.shape[1] // 3
    hidden = mlp_weight.shape[1] // 3
    r8, f8 = lru // 8, hidden // 8
    rc = -(-r8 // 128) * 128
    head = gate_weight.shape[1] // 2
    heads = r8 // head
    gate_rows = gate_weight.shape[0]
    gate_pad = -(-gate_rows // 16) * 16

    def turned(v):
        lead = v.shape[:-1]
        v = v.reshape(lead + (4, length, pair)).swapaxes(-2, -3)
        return jnp.roll(v, -z, axis=-3).reshape(lead + (model,))

    def turned_back(v):
        lead = v.shape[:-1]
        v = jnp.roll(v.reshape(lead + (length, 4, pair)), z, axis=-3)
        return v.swapaxes(-2, -3).reshape(lead + (model,))

    x = lax.axis_index("seq") - 2 * z
    low_gains = norm_gains.astype(BF16).astype(F32)
    gains_out = jnp.where(
        x == 0,
        jnp.pad(low_gains, ((0, 6), (0, 128 - share))),
        jnp.pad(low_gains, ((0, 6), (share, 128 - 2 * share))),
    )
    gate_out = jnp.pad(
        jnp.concatenate([gate_weight, chan_params.T], axis=1).astype(BF16),
        ((0, gate_pad - gate_rows), (0, rc - 2 * head - 8)),
    )
    inputs_low = turned(block_input[0])
    normed_one, mixer_in, mlp_full, gains, gate_in = first(
        inputs_low, mixer_weight, mlp_weight, gains_out, gate_out, length, 1
    )
    normed_one = normed_one.reshape(8 * tokens, model)
    inputs = inputs_low.astype(F32)
    inverse_one = lax.rsqrt(jnp.mean(inputs * inputs, axis=-1, keepdims=True) + norm_eps)
    scaled_one = inputs * inverse_one
    gate_own = gate_in[:, :gate_rows].reshape(r8, rc)
    chan = gate_own[:, 2 * head : 2 * head + 8].astype(F32).T
    lam = chan[7]
    fill = jnp.concatenate([jnp.zeros((7, rc - r8), F32), jnp.ones((1, rc - r8), F32)])
    chan = jnp.concatenate([chan[:7], 8.0 * jax.nn.softplus(-lam)[None]])
    chan = jnp.concatenate([chan, fill], axis=1)
    gate = []
    for h in range(heads):
        block = gate_own[h * head : (h + 1) * head, : 2 * head]
        at = ((0, 0), (h * head, rc - (h + 1) * head))
        gate.append(
            jnp.concatenate([jnp.pad(block[:, :head], at), jnp.pad(block[:, head:], at)], axis=1)
        )
    gate = jnp.pad(jnp.concatenate(gate), ((0, rc - r8), (0, 0)))

    cotangent_low = turned(out_grad[0])
    cotangent = cotangent_low.astype(F32)
    carried = length == 4
    if not carried:
        mlp_full = jnp.concatenate(line_gather(mlp_full[0].reshape(8 * share, 3 * f8), length))

    def carry_gather(hop):
        return ("gather", hop, (mlp_full,)) if carried else None

    mixer_full = mixer_in.reshape(model, 3 * r8)
    parts = [jnp.pad(mixer_full[:, n * r8 : (n + 1) * r8], ((0, 0), (0, rc - r8))) for n in range(3)]
    mixer_first = jnp.concatenate(parts[:2], axis=1)
    mixer_last = parts[2]
    span = 2 * tokens
    projected = jnp.dot(normed_one, mixer_first, preferred_element_type=F32)
    projected = projected.reshape(4, span, 2 * rc)
    (mixed, *kept, grad_out), more = recur_forward(
        projected, gate, chan, cotangent_low, length, 5, carry_gather(1)
    )
    (mlp_full,) = more or (mlp_full,)
    grad_out = grad_out.reshape(8 * tokens, model)
    mixed = mixed.reshape(4 * span, rc)
    mixer_sum, more = plane_scatter(
        contract_last(mixed, mixer_last).astype(BF16), 6, carry_gather(2), length
    )
    (mlp_full,) = more or (mlp_full,)
    residual = inputs + mixer_sum
    scaled_two, inverse_two, normed_two = normalize(residual, gains[1])
    normed_two, more = plane_gather(normed_two, 7, carry_gather(3), length)
    (mlp_full,) = more or (mlp_full,)
    mlp_full = mlp_full.reshape(model, 3 * f8)
    mlp_gate, mlp_up, mlp_down = (mlp_full[:, n * f8 : (n + 1) * f8] for n in range(3))
    gg = jnp.dot(normed_two, mlp_gate, preferred_element_type=F32)
    uu = jnp.dot(normed_two, mlp_up, preferred_element_type=F32)
    dhid = jnp.dot(grad_out, mlp_down, preferred_element_type=F32)
    gelu, inner = gelu_parts(gg)
    hid = (gelu * uu).astype(BF16)
    dgg = (dhid * uu * gelu_slope(gg, inner)).astype(BF16)
    duu = (dhid * gelu).astype(BF16)
    dnormed_two = contract_last(dgg, mlp_gate) + contract_last(duu, mlp_up)

    def terms(v):
        return v.astype(BF16).reshape(length, 8 * share, f8)

    mlp_terms = [
        terms(contract_first(normed_two, dgg)),
        terms(contract_first(normed_two, duu)),
        terms(contract_first(grad_out, hid)),
    ]

    def carry_scatter(hop, got):
        if not carried:
            return None
        if hop == 1:
            return ("scatter", 1, mlp_terms)
        return ("scatter", hop, add_got(got, length - hop, hop))

    def add_got(got, up, down):
        sums = []
        for n, term in enumerate(mlp_terms):
            below = jnp.where(z >= 1, got[n].astype(F32), 0.0)
            sums.append((term[up].astype(F32) + below).astype(BF16))
        for n, term in enumerate(mlp_terms):
            above = jnp.where(z <= length - 2, got[3 + n].astype(F32), 0.0)
            sums.append((term[down].astype(F32) + above).astype(BF16))
        return sums

    dnormed_two, got = plane_scatter(dnormed_two.astype(BF16), 8, carry_scatter(1, None), length)
    grad_from_second, gain_two_grad = normalize_back(dnormed_two, scaled_two, inverse_two, gains[1])
    grad_residual = cotangent + grad_from_second
    dmz, got = plane_gather(grad_residual.astype(BF16), 10, carry_scatter(2, got), length)
    mlp_sum, got = plane_scatter(
        contract_last(hid, mlp_down).astype(BF16), 9, carry_scatter(3, got), length
    )
    block_output = turned_back((residual + mlp_sum).astype(BF16))
    if carried:
        mlp_sums = [
            mlp_terms[n][0].astype(F32)
            + jnp.where(z >= 1, got[n].astype(F32), 0.0)
            + jnp.where(z <= length - 2, got[3 + n].astype(F32), 0.0)
            for n in range(3)
        ]
    else:
        mlp_sums = [line_scatter([term[k] for k in range(length)], length) for term in mlp_terms]
    mlp_back = jnp.concatenate([g.astype(BF16).reshape(8, share, f8) for g in mlp_sums], axis=2)

    dmix = jnp.dot(dmz, mixer_last, preferred_element_type=F32).reshape(4, span, rc)
    dproj, dgate, chan_grad = recur_backward(dmix, gate, chan, kept, projected, length, 11)
    dproj = dproj.reshape(4 * span, 2 * rc)
    dgate = dgate.reshape(4 * span, 2 * rc)
    proj_grad = contract_first(normed_one, dproj)
    last_grad = contract_first(dmz, mixed)
    mixer_terms = jnp.concatenate(
        [proj_grad[:, :r8], proj_grad[:, rc : rc + r8], last_grad[:, :r8]], axis=1
    )
    mixer_terms = mixer_terms.astype(BF16).reshape(length, 8 * share, 3 * r8)
    dnormed_one, mlp_back, mixer_sums = closing(
        contract_last(dproj, mixer_first).astype(BF16), mlp_back, mixer_terms, 12
    )
    gate_full_grad = contract_first(kept[4].reshape(4 * span, rc), dgate)

    grad_from_first, gain_one_grad = normalize_back(dnormed_one, scaled_one, inverse_one, gains[0])
    input_grad = turned_back(grad_residual + grad_from_first)

    squares = sum(jnp.sum(g * g) for g in mlp_sums + [mixer_sums])
    mixer_back = mixer_sums.astype(BF16).reshape(8, share, 3 * r8)

    gains_back = jnp.stack([gain_one_grad, gain_two_grad])
    gains_back = gains_back.reshape(2, length, 8, share).transpose(2, 1, 0, 3)
    gains_back = jnp.pad(gains_back, ((0, 0), (0, 0), (0, 6), (0, 128 - share)))
    blocks = []
    for h in range(heads):
        at = slice(h * head, (h + 1) * head)
        blocks.append(
            jnp.concatenate([gate_full_grad[at, at], gate_full_grad[at, rc + h * head : rc + (h + 1) * head]], axis=1)
        )
    gate_grad_own = jnp.concatenate(blocks)
    chan_grad = jnp.sum(chan_grad, axis=1)[:, :r8]
    chan_grad = jnp.concatenate([chan_grad[:7], (8.0 * jax.nn.sigmoid(-lam) * chan_grad[7])[None]])
    gate_back = jnp.concatenate([gate_grad_own, chan_grad.T], axis=1).reshape(length, gate_rows, 2 * head + 8)
    gate_back = jnp.pad(
        gate_back, ((0, 0), (0, gate_pad - gate_rows), (0, rc - 2 * head - 8))
    )
    gate_back = jnp.roll(gate_back, -z, axis=0)
    squares_in = jnp.zeros((8, 128), F32).at[0, 0].set(squares)
    mixer_back, gains_sum, gate_sum, squares_sum = last(
        mixer_back, gains_back, gate_back, squares_in, length, 14
    )

    grad_norm = jnp.sqrt(jnp.sum(squares_sum))
    factor = clip_limit / jnp.maximum(grad_norm, clip_limit)
    mixer_grad = mixer_back.astype(F32).reshape(8, share, 3, r8).transpose(1, 2, 0, 3).reshape(share, 3 * lru)
    gains_up = adam_step(
        norm_gains, gains_sum[:2, :share], first_gains, second_gains, factor, rate_gains, 0.0
    )
    mixer_up = adam_step(
        mixer_weight, mixer_grad, first_mixer, second_mixer, factor, rate_matrix, decay_matrix
    )
    gate_up = adam_step(
        gate_weight, gate_sum[:gate_rows, : 2 * head], first_gate, second_gate, factor, rate_matrix, decay_matrix
    )
    chan_up = adam_step(
        chan_params, gate_sum[:gate_rows, 2 * head : 2 * head + 8].T, first_chan, second_chan, factor,
        rate_channel, 0.0,
    )
    mlp_up = adam_blocks(
        mlp_weight, mlp_back, first_mlp, second_mlp, factor, rate_matrix, decay_matrix
    )
    return (
        block_output[None],
        input_grad[None],
        grad_norm,
        *gains_up,
        *mixer_up,
        *gate_up,
        *chan_up,
        *mlp_up,
    )


def solution(mesh):
    rows = P(("batch", "seq"), None)
    columns = P(None, ("batch", "seq"))
    data = P("batch", "seq", None)
    weights = (columns, rows, rows, columns, rows)
    in_specs = (data, data) + weights * 3
    triples = tuple(spec for spec in weights for _ in range(3))
    return jax.shard_map(
        on_device,
        mesh=mesh,
        in_specs=in_specs,
        out_specs=(data, data, P()) + triples,
        check_vma=False,
    )
```

```python
import functools
import math

import jax
import jax.numpy as jnp
from jax import lax
from jax.experimental import pallas as pl
from jax.experimental.pallas import tpu as pltpu
from jax.sharding import PartitionSpec as P

STEP = 10
norm_eps = 1e-06
clip_limit = 1.0
beta_first = 0.9
beta_second = 0.999
adam_eps = 1e-08
rate_matrix = 0.05
rate_gains = 0.8
rate_channel = 2.0
decay_matrix = 0.1

MESH = pl.DeviceIdType.MESH
F32 = jnp.float32
BF16 = jnp.bfloat16
ANY = pl.BlockSpec(memory_space=pl.ANY)
VM = pl.BlockSpec(memory_space=pltpu.VMEM)
FLIPS = [(fy, fc, fx) for fy in (0, 1) for fc in (0, 1) for fx in (0, 1) if fy + fc + fx]
GELU_SCALE = math.sqrt(2.0 / math.pi)


def place():
    b = lax.axis_index("batch")
    s = lax.axis_index("seq")
    y, z = b // 2, s // 2
    return y, b - 2 * y, z, s - 2 * z


def device(y, c, z, x):
    return (y * 2 + c, z * 2 + x)


def rank(y, c, x):
    return (y * 2 + c) * 2 + x


def flip(v, f):
    return 1 - v if f else v


def greet(peers):
    barrier = pltpu.get_barrier_semaphore()
    for peer in peers:
        pl.semaphore_signal(barrier, inc=1, device_id=peer, device_id_type=MESH)
    pl.semaphore_wait(barrier, len(peers))


def remote(src, dst, send, recv, to):
    copy = pltpu.make_async_remote_copy(
        src_ref=src, dst_ref=dst, send_sem=send, recv_sem=recv, device_id=to, device_id_type=MESH
    )
    copy.start()
    return copy


def params(collective_id, vmem=None):
    return pltpu.CompilerParams(
        collective_id=collective_id, has_side_effects=True, vmem_limit_bytes=vmem
    )


DMA = pltpu.SemaphoreType.DMA


def gather_peers():
    y, c, z, x = place()
    return [device(y, c, z, 1 - x), device(1 - y, c, z, x), device(y, 1 - c, z, x)]


class Gather:
    def __init__(self, a, o, loc, ss, rs):
        y, c, z, x = place()
        self.to_x, self.to_y, self.to_c = gather_peers()
        self.me, self.bx = rank(y, c, x), rank(y, c, 1 - x)
        self.by, self.bd = rank(1 - y, c, x), rank(1 - y, c, 1 - x)
        half = a.shape[0] // 2
        self.lo, self.hi = pl.ds(0, half), pl.ds(half, half)
        self.a, self.o, self.loc, self.ss, self.rs = a, o, loc, ss, rs
        self.done = []

    def send(self, src, dst, k, to):
        copy = remote(src, dst, self.ss.at[k], self.rs.at[k], to)
        self.done.append(copy)
        return copy

    def relay(self, block, part, k, to):
        return self.send(self.o.at[block, part], self.o.at[block, part], k, to)

    def begin(self):
        a, o, me, lo, hi = self.a, self.o, self.me, self.lo, self.hi
        self.s0 = self.send(a.at[lo], o.at[me, lo], 0, self.to_x)
        self.s1 = self.send(a.at[hi], o.at[me, hi], 1, self.to_y)
        self.s2 = self.send(a.at[hi], o.at[me, hi], 2, self.to_x)
        self.s3 = self.send(a.at[lo], o.at[me, lo], 3, self.to_y)
        self.s4 = self.send(a, o.at[me], 4, self.to_c)
        self.own = pltpu.make_async_copy(a, o.at[me], self.loc)
        self.own.start()

    def middle(self):
        self.s0.wait_recv()
        self.s5 = self.relay(self.bx, self.lo, 5, self.to_y)
        self.last = [self.s4, self.relay(self.bx, self.lo, 7, self.to_c)]
        self.s1.wait_recv()
        self.s6 = self.relay(self.by, self.hi, 6, self.to_x)
        self.last.append(self.relay(self.by, self.hi, 8, self.to_c))

    def end(self, mark=lambda: None):
        self.s2.wait_recv()
        self.last.append(self.relay(self.bx, self.hi, 9, self.to_c))
        self.s3.wait_recv()
        self.last.append(self.relay(self.by, self.lo, 10, self.to_c))
        mark()
        self.s5.wait_recv()
        self.last.append(self.relay(self.bd, self.lo, 11, self.to_c))
        self.s6.wait_recv()
        self.last.append(self.relay(self.bd, self.hi, 12, self.to_c))
        for copy in self.last:
            copy.wait_recv()
        for copy in self.done:
            copy.wait_send()
        self.own.wait()


def scatter_steps(p, o, mine, sib, part, got, loc, ss, rs, mark=lambda name: None):
    y, c, z, x = place()
    to_x, to_y, to_c = gather_peers()
    half = o.shape[0] // 2
    step = 16
    cut = (pl.ds(0, half), pl.ds(half, half))
    where = ((1 - y, 1 - x), (1 - y, x), (y, 1 - x), (y, x))
    order = [(0, 0), (0, 1), (1, 0), (2, 1), (2, 0), (1, 1), (3, 0), (3, 1)]
    from_c, own, sends = {}, {}, []
    for n, (t, h) in enumerate(order):
        ty, tx = where[t]
        own[t, h] = pltpu.make_async_copy(
            p.at[rank(ty, c, tx), cut[h]], mine.at[t, h], loc.at[n]
        )
        own[t, h].start()
        from_c[t, h] = remote(
            p.at[rank(ty, 1 - c, tx), cut[h]], sib.at[t, h], ss.at[n], rs.at[n], to_c
        )
        sends.append(from_c[t, h])

    def add(dst, t, h, extra):
        own[t, h].wait()
        from_c[t, h].wait_recv()

        @pl.loop(0, half // step)
        def _(i):
            at = pl.ds(pl.multiple_of(i * step, step), step)
            total = mine[t, h, at].astype(F32) + sib[t, h, at].astype(F32)
            for ref in extra:
                total = total + ref[at].astype(F32)
            dst[at] = total.astype(dst.dtype)

    def send(k, slot, to):
        copy = remote(part.at[k], got.at[slot], ss.at[8 + k], rs.at[8 + slot], to)
        sends.append(copy)
        return copy

    def arrival(slot):
        return pltpu.make_async_remote_copy(
            src_ref=part.at[0], dst_ref=got.at[slot], send_sem=ss.at[8], recv_sem=rs.at[8 + slot],
            device_id=to_x, device_id_type=MESH,
        )

    add(part.at[0], 0, 0, ())
    send(0, 1, to_y)
    add(part.at[1], 0, 1, ())
    send(1, 3, to_x)
    add(part.at[2], 1, 0, ())
    send(2, 0, to_y)
    add(part.at[3], 2, 1, ())
    send(3, 2, to_x)
    arrival(1).wait_recv()
    add(part.at[4], 2, 0, (got.at[1],))
    send(4, 4, to_x)
    mark("early")
    arrival(3).wait_recv()
    add(part.at[5], 1, 1, (got.at[3],))
    send(5, 5, to_y)
    mark("late")
    arrival(0).wait_recv()
    arrival(4).wait_recv()
    add(o.at[cut[0]], 3, 0, (got.at[0], got.at[4]))
    arrival(2).wait_recv()
    arrival(5).wait_recv()
    add(o.at[cut[1]], 3, 1, (got.at[2], got.at[5]))
    for copy in sends:
        copy.wait_send()


def scatter_scratch(half, width):
    return [
        pltpu.VMEM((4, 2, half, width), BF16),
        pltpu.VMEM((4, 2, half, width), BF16),
        pltpu.VMEM((6, half, width), BF16),
        pltpu.VMEM((6, half, width), BF16),
        DMA((8,)),
        DMA((14,)),
        DMA((14,)),
    ]


def exchange_steps(a, o, loc, ss, rs, columns=None):
    y, c, z, x = place()
    me = rank(y, c, x)
    dst = o.at[me] if columns is None else o.at[me, :, columns]
    copies = []
    for n, (fy, fc, fx) in enumerate(FLIPS):
        ty, tc, tx = flip(y, fy), flip(c, fc), flip(x, fx)
        copies.append(remote(a.at[rank(ty, tc, tx)], dst, ss.at[n], rs.at[n], device(ty, tc, z, tx)))
    own = pltpu.make_async_copy(a.at[me], dst, loc)
    own.start()
    return copies, own


def plane_peers():
    y, c, z, x = place()
    return [device(flip(y, fy), flip(c, fc), z, flip(x, fx)) for fy, fc, fx in FLIPS]


def line_peers(length):
    y, c, z, x = place()
    return [device(y, c, lax.rem(z + k, length), x) for k in range(1, length)]


class LineGather:
    def __init__(self, buf, length, ss, rs):
        y, c, z, x = place()
        self.z, self.length, self.buf, self.ss, self.rs = z, length, buf, ss, rs
        self.up = device(y, c, lax.rem(z + 1, length), x)
        self.down = device(y, c, lax.rem(z + length - 1, length), x)

    def copy(self, hop, upward):
        length, buf = self.length, self.buf
        src, dst = ((length - hop + 1) % length, length - hop) if upward else (hop - 1, hop)
        way = 0 if upward else 1
        return pltpu.make_async_remote_copy(
            src_ref=buf.at[src], dst_ref=buf.at[dst], send_sem=self.ss.at[way, hop - 1],
            recv_sem=self.rs.at[way, hop - 1], device_id=self.up if upward else self.down,
            device_id_type=MESH,
        )

    def sends(self, hop, act):
        z, length = self.z, self.length

        @pl.when(jnp.logical_and(z + 1 < length, z >= hop - 1))
        def _():
            act(self.copy(hop, True))

        @pl.when(jnp.logical_and(z >= 1, z + hop - 1 < length))
        def _():
            act(self.copy(hop, False))

    def start(self, hop):
        self.sends(hop, lambda copy: copy.start())

    def arrive(self, hop):
        z, length = self.z, self.length

        @pl.when(z >= hop)
        def _():
            self.copy(hop, True).wait_recv()

        @pl.when(z + hop < length)
        def _():
            self.copy(hop, False).wait_recv()

    def finish(self):
        for hop in range(1, self.length):
            self.sends(hop, lambda copy: copy.wait_send())


class LineScatter:
    def __init__(self, sources, length, total, up_mine, down_mine, up_got, down_got, loc, ss, rs):
        y, c, z, x = place()
        self.sources, self.length, self.total = sources, length, total
        self.mine, self.got = (up_mine, down_mine), (up_got, down_got)
        self.loc, self.ss, self.rs = loc, ss, rs
        self.to = (device(y, c, lax.rem(z + 1, length), x), device(y, c, lax.rem(z + length - 1, length), x))
        self.far = (z, length - 1 - z)

    def loads(self, way, hop):
        k = 0 if hop == 0 else self.length - hop if way == 0 else hop
        copies, at = [], 0
        for n, (ref, first, columns) in enumerate(self.sources):
            dst = self.mine[way].at[hop - 1] if hop else self.total
            copies.append(
                pltpu.make_async_copy(
                    ref.at[k, :, pl.ds(first, columns)], dst.at[:, pl.ds(at, columns)],
                    self.loc.at[way, hop, n],
                )
            )
            at += columns
        return copies

    def copy(self, way, hop):
        return pltpu.make_async_remote_copy(
            src_ref=self.mine[way].at[hop - 1], dst_ref=self.got[way].at[hop - 1],
            send_sem=self.ss.at[way, hop - 1], recv_sem=self.rs.at[way, hop - 1],
            device_id=self.to[way], device_id_type=MESH,
        )

    def begin(self):
        for hop in range(1, self.length):
            for way in (0, 1):
                for copy in self.loads(way, hop):
                    copy.start()
        for copy in self.loads(0, 0):
            copy.start()
        self.next = 1
        self.start()

    def start(self):
        hop = self.next
        if hop >= self.length:
            return
        self.next += 1
        for way in (0, 1):
            far = self.far[way]
            for copy in self.loads(way, hop):
                copy.wait()
            if hop > 1:

                @pl.when(jnp.logical_and(far >= 1, far <= hop - 1))
                def _():
                    self.copy(way, hop - 1).wait_recv()
                    dst, src = self.mine[way].at[hop - 1], self.got[way].at[hop - 2]

                    @pl.loop(0, dst.shape[0] // 16)
                    def _(i):
                        at = pl.ds(pl.multiple_of(i * 16, 16), 16)
                        dst[at] = (dst[at].astype(F32) + src[at].astype(F32)).astype(dst.dtype)

            @pl.when(far <= hop - 1)
            def _():
                self.copy(way, hop).start()

    def end(self, result, squares):
        while self.next < self.length:
            self.start()
        last = self.length - 1
        for copy in self.loads(0, 0):
            copy.wait()
        squares[...] = jnp.zeros_like(squares)

        def finish(ways):
            for way in ways:
                self.copy(way, last).wait_recv()

            @pl.loop(0, result.shape[0] // 16)
            def _(i):
                at = pl.ds(pl.multiple_of(i * 16, 16), 16)
                total = self.total[at].astype(F32)
                for way in ways:
                    total = total + self.got[way][last - 1, at].astype(F32)
                result[at] = total.astype(result.dtype)
                squares[...] += tile_of_squares(total)

        above, below = self.far[0] >= 1, self.far[1] >= 1
        pl.when(jnp.logical_and(above, below))(lambda: finish((0, 1)))
        pl.when(jnp.logical_not(above))(lambda: finish((1,)))
        pl.when(jnp.logical_not(below))(lambda: finish((0,)))
        for hop in range(1, self.length):
            for way in (0, 1):

                @pl.when(self.far[way] <= hop - 1)
                def _():
                    self.copy(way, hop).wait_send()


def fold(v):
    return jnp.sum(v.reshape(v.shape[0] // 8, 8, v.shape[1]), axis=0)


def tile_of_squares(v):
    v = fold(v * v)
    part = v[:, :128]
    for n in range(1, v.shape[1] // 128):
        part = part + v[:, n * 128 : (n + 1) * 128]
    if v.shape[1] % 128:
        rest = v[:, v.shape[1] // 128 * 128 :]
        part = part + jnp.concatenate([rest, jnp.zeros((8, 128 - rest.shape[1]), F32)], axis=1)
    return part


def line_scratch(length, rows, columns, sources):
    slots = pltpu.VMEM((length - 1, rows, columns), BF16)
    return [pltpu.VMEM((rows, columns), BF16)] + [slots] * 4 + [
        DMA((2, length, sources)), DMA((2, length)), DMA((2, length))
    ]


LINE_REFS = 8
SCATTER_REFS = 7
TILE = jax.ShapeDtypeStruct((8, 128), F32)


def line_neighbours(length):
    y, c, z, x = place()
    return [device(y, c, lax.rem(z + 1, length), x), device(y, c, lax.rem(z + length - 1, length), x)]


def rows_loop(rows, body):
    @pl.loop(0, rows // 16)
    def _(i):
        body(pl.ds(pl.multiple_of(i * 16, 16), 16))


def turned_tiles(length, pair):
    _, _, z, _ = place()
    for k in range(length):
        for b in range(4):
            yield k * 4 + b, pl.multiple_of((b * length + lax.rem(z + k, length)) * pair, pair)


def load_turned(ref, at, length, pair):
    if pair % 128:
        return ref[at]
    return jnp.concatenate([ref[at, pl.ds(src, pair)] for _, src in turned_tiles(length, pair)], axis=1)


def store_turned(ref, at, value, length, pair):
    if pair % 128:
        ref[at] = value
        return
    for n, dst in turned_tiles(length, pair):
        ref[at, pl.ds(dst, pair)] = value[:, n * pair : (n + 1) * pair]


def inverse_rms(v):
    return lax.rsqrt(jnp.sum(v * v, axis=-1, keepdims=True) * (1.0 / v.shape[-1]) + norm_eps)


def norm_rows_back(v, gain, grad):
    inverse = inverse_rms(v)
    scaled = v * inverse
    moved = grad * gain
    inner = jnp.sum(moved * scaled, axis=-1, keepdims=True) * (1.0 / v.shape[-1])
    return inverse * (moved - scaled * inner), fold(grad * scaled)


def middle_kernel(length, p, inputs, gains, w_in, residual, normed_o, w, *scratch):
    scatter_refs, (low, loc, gs, gr, hs, hr) = scratch[:SCATTER_REFS], scratch[SCATTER_REFS:]
    greet(gather_peers() + line_neighbours(length))
    hops = LineGather(w, length, hs, hr)
    hops.start(1)
    started = [1]

    def advance(name=None):
        if name != "early" and started[0] < length - 1:
            hops.arrive(started[0])
            started[0] += 1
            hops.start(started[0])

    scatter_steps(p, residual, *scatter_refs)

    def body(at):
        v = inputs[at].astype(F32) + residual[at]
        residual[at] = v
        low[at] = (v * inverse_rms(v) * gains[1:2]).astype(BF16)

    rows_loop(low.shape[0], body)
    gather = Gather(low, normed_o, loc, gs, gr)
    gather.begin()
    advance()
    gather.middle()
    gather.end(advance)
    while started[0] < length - 1:
        advance()
    hops.arrive(length - 1)
    hops.finish()


def middle(p, inputs, gains, w, length, collective_id):
    rows, width = inputs.shape
    return pl.pallas_call(
        functools.partial(middle_kernel, length),
        out_shape=(
            jax.ShapeDtypeStruct((rows, width), F32),
            jax.ShapeDtypeStruct((8, rows, width), BF16),
            jax.ShapeDtypeStruct(w.shape, w.dtype),
        ),
        in_specs=[ANY, VM, VM, ANY],
        out_specs=(VM, ANY, ANY),
        scratch_shapes=scatter_scratch(rows // 2, width)
        + [pltpu.VMEM((rows, width), BF16), DMA, DMA((13,)), DMA((13,)), DMA((2, length)), DMA((2, length))],
        input_output_aliases={3: 2},
        compiler_params=params(collective_id, 40 * 2**20),
        cost_estimate=pl.CostEstimate(flops=0, bytes_accessed=300 * 2**20, transcendentals=0),
    )(p.reshape(8, rows, width), inputs, gains, w)


def turn_kernel(length, cuts, p, residual, above, gains, *refs):
    terms, refs = refs[: len(cuts)], refs[len(cuts) :]
    back, gain, low_o, sums, squares, *scratch = refs
    scatter_refs, (total, low, loc, gs, gr), line_refs = (
        scratch[:SCATTER_REFS], scratch[SCATTER_REFS : SCATTER_REFS + 5], scratch[SCATTER_REFS + 5 :]
    )
    greet(gather_peers() + line_neighbours(length))
    line = LineScatter([(ref, *cut) for ref, cut in zip(terms, cuts)], length, *line_refs)
    line.begin()
    scatter_steps(p, total, *scatter_refs, mark=lambda name: line.start() if name == "late" else None)
    gain[...] = jnp.zeros_like(gain)

    def body(at):
        grad, gain_part = norm_rows_back(residual[at], gains[1:2], total[at])
        grad = above[at].astype(F32) + grad
        back[at] = grad
        low[at] = grad.astype(BF16)
        gain[...] += gain_part

    rows_loop(low.shape[0], body)
    gather = Gather(low, low_o, loc, gs, gr)
    gather.begin()
    gather.middle()
    line.start()
    gather.end()
    line.end(sums, squares)


def turn(p, residual, above, gains, terms, cuts, length, collective_id):
    rows, width = residual.shape
    line_rows, columns = terms[0].shape[1], sum(cut[1] for cut in cuts)
    return pl.pallas_call(
        functools.partial(turn_kernel, length, cuts),
        out_shape=(
            jax.ShapeDtypeStruct((rows, width), F32),
            jax.ShapeDtypeStruct((8, width), F32),
            jax.ShapeDtypeStruct((8, rows, width), BF16),
            jax.ShapeDtypeStruct((line_rows, columns), BF16),
            TILE,
        ),
        in_specs=[ANY, VM, VM, VM] + [ANY] * len(terms),
        out_specs=(VM, VM, ANY, VM, VM),
        scratch_shapes=scatter_scratch(rows // 2, width)
        + [pltpu.VMEM((rows, width), F32), pltpu.VMEM((rows, width), BF16), DMA, DMA((13,)), DMA((13,))]
        + line_scratch(length, line_rows, columns, len(cuts)),
        compiler_params=params(collective_id, 56 * 2**20),
        cost_estimate=pl.CostEstimate(flops=0, bytes_accessed=300 * 2**20, transcendentals=0),
    )(p.reshape(8, rows, width), residual, above, gains, *terms)


def output_kernel(length, cuts, p, residual, *refs):
    terms, refs = refs[: len(cuts)], refs[len(cuts) :]
    out, sums, squares, *scratch = refs
    scatter_refs, total, line_refs = (
        scratch[:SCATTER_REFS], scratch[SCATTER_REFS], scratch[SCATTER_REFS + 1 :]
    )
    greet(gather_peers() + line_neighbours(length))
    line = LineScatter([(ref, *cut) for ref, cut in zip(terms, cuts)], length, *line_refs)
    line.begin()
    scatter_steps(p, total, *scatter_refs, mark=lambda name: line.start())
    pair = out.shape[1] // (4 * length)

    def body(at):
        store_turned(out, at, (residual[at] + total[at]).astype(BF16), length, pair)

    rows_loop(out.shape[0], body)
    line.end(sums, squares)


def output(p, residual, terms, cuts, length, collective_id):
    rows, width = residual.shape
    line_rows, columns = terms[0].shape[1], sum(cut[1] for cut in cuts)
    return pl.pallas_call(
        functools.partial(output_kernel, length, cuts),
        out_shape=(
            jax.ShapeDtypeStruct((rows, width), BF16),
            jax.ShapeDtypeStruct((line_rows, columns), BF16),
            TILE,
        ),
        in_specs=[ANY, VM] + [ANY] * len(terms),
        out_specs=(VM, VM, VM),
        scratch_shapes=scatter_scratch(rows // 2, width)
        + [pltpu.VMEM((rows, width), F32)]
        + line_scratch(length, line_rows, columns, len(cuts)),
        compiler_params=params(collective_id, 48 * 2**20),
        cost_estimate=pl.CostEstimate(flops=0, bytes_accessed=150 * 2**20, transcendentals=0),
    )(p.reshape(8, rows, width), residual, *terms)


def closing_kernel(length, parts, p, g, *refs):
    blocks, refs = refs[:parts], refs[parts:]
    o, e_o, sums, squares, *scratch = refs
    scatter_refs, (loc, es, er), line_refs = (
        scratch[:SCATTER_REFS], scratch[SCATTER_REFS : SCATTER_REFS + 3], scratch[SCATTER_REFS + 3 :]
    )
    greet(plane_peers() + line_neighbours(length))
    line = LineScatter([(g, 0, g.shape[2])], length, *line_refs)
    line.begin()
    scatter_steps(p, o, *scatter_refs, mark=lambda name: line.start() if name == "late" else None)
    moves, at = [], 0
    for n, block in enumerate(blocks):
        columns = block.shape[2]
        moves.append(
            exchange_steps(block, e_o, loc.at[n], es.at[n], er.at[n], pl.ds(at, columns))
        )
        at += columns
    line.end(sums, squares)
    for copies, own in moves:
        for copy in copies:
            copy.wait()
        own.wait()


def closing(p, blocks, g, length, collective_id):
    rows, width = p.shape[0] // 8, p.shape[1]
    share = blocks[0].shape[0] // 8
    blocks = [block.reshape(8, share, block.shape[1]) for block in blocks]
    columns = sum(block.shape[2] for block in blocks)
    parts = len(blocks)
    return pl.pallas_call(
        functools.partial(closing_kernel, length, parts),
        out_shape=(
            jax.ShapeDtypeStruct((rows, width), F32),
            jax.ShapeDtypeStruct((8, share, columns), BF16),
            jax.ShapeDtypeStruct(g.shape[1:], BF16),
            TILE,
        ),
        in_specs=[ANY] * (2 + parts),
        out_specs=(VM, ANY, VM, VM),
        scratch_shapes=scatter_scratch(rows // 2, width)
        + [DMA((parts,)), DMA((parts, 7)), DMA((parts, 7))]
        + line_scratch(length, g.shape[1], g.shape[2], 1),
        compiler_params=params(collective_id, 56 * 2**20),
        cost_estimate=pl.CostEstimate(flops=0, bytes_accessed=250 * 2**20, transcendentals=0),
    )(p.reshape(8, rows, width), g, *blocks)


def first_kernel(
    length, inputs, above, mixer_w, mlp_w, gn, gp,
    normed_o, wm_o, wf_o, wd_o, gains_o, gp_o, inputs_o, above_o,
    normed, gn_all, wm, wf, wd, loc, ms, mr, fs, fr, line_s, line_r, gain_s, gain_r, move_s, move_r,
    gather_s, gather_r, hop_s, hop_r,
):
    y, c, z, x = place()
    s = 2 * z + x
    me = rank(y, c, x)
    rows, width = inputs.shape
    pair = width // (4 * length)
    line = line_peers(length)
    plane = plane_peers()
    to_z, to_x = lax.rem(s, length), s // length
    moves = jnp.where(jnp.logical_and(to_z == z, to_x == x), 0, 1)
    src = x * length + z
    from_z = src // 2
    from_x = src - 2 * from_z
    barrier = pltpu.get_barrier_semaphore()
    for peer in line + plane:
        pl.semaphore_signal(barrier, inc=1, device_id=peer, device_id_type=MESH)

    @pl.when(moves == 1)
    def _():
        pl.semaphore_signal(barrier, inc=1, device_id=device(y, c, to_z, to_x), device_id_type=MESH)
        pl.semaphore_signal(barrier, inc=1, device_id=device(y, c, from_z, from_x), device_id_type=MESH)

    pl.semaphore_wait(barrier, len(line) + len(plane) + 2 * moves)

    gn_all[me, z] = gn[...]
    gains = [
        remote(gn, gn_all.at[me, z], line_s.at[0, k], line_r.at[0, k], line[k]) for k in range(length - 1)
    ]
    for pack, source, js in ((wm, mixer_w, (0, 1, 2)), (wf, mlp_w, (0, 1)), (wd, mlp_w, (2,))):
        part = pack.shape[2] // len(js)
        for t in range(8):
            for n, j in enumerate(js):
                start = (j * 8 + t) * part
                pack[t, :, n * part : (n + 1) * part] = source[:, start : start + part].astype(BF16)
        if pack is wm:
            for copy in gains:
                copy.wait()
            spread = [
                remote(gn_all.at[me], gn_all.at[me], gain_s.at[n], gain_r.at[n], plane[n])
                for n in range(7)
            ]
            mixer, mixer_own = exchange_steps(wm, wm_o.at[0], loc.at[0], ms, mr)

    @pl.when(moves == 1)
    def _():
        copy = remote(gp, gp_o.at[to_z], move_s, move_r, device(y, c, to_z, to_x))
        copy.wait()

    @pl.when(moves == 0)
    def _():
        copy = pltpu.make_async_copy(gp, gp_o.at[z], loc.at[2])
        copy.start()
        copy.wait()

    gates = [
        remote(gp_o.at[z], gp_o.at[z], line_s.at[1, k], line_r.at[1, k], line[k])
        for k in range(length - 1)
    ]
    for copy in spread:
        copy.wait()
    for k in range(length):
        other = lax.rem(z + k, length)
        for b in range(4):
            at = slice((4 * k + b) * pair, (4 * k + b + 1) * pair)
            tile = (gn_all[2 * b, other] + gn_all[2 * b + 1, other])[:, :pair]
            gains_o[:, at] = tile.astype(BF16).astype(F32)

    def body(at):
        v = load_turned(inputs, at, length, pair)
        inputs_o[at] = v
        v = v.astype(F32)
        normed[at] = (v * inverse_rms(v) * gains_o[0:1]).astype(BF16)

    rows_loop(rows, body)

    gather = Gather(normed, normed_o, loc.at[1], gather_s, gather_r)
    gather.begin()
    for copy in mixer:
        copy.wait()
    mixer_own.wait()
    hops = LineGather(wm_o, length, hop_s, hop_r)
    hops.start(1)
    down, down_own = exchange_steps(wd, wd_o.at[0], loc.at[4], fs.at[1], fr.at[1])
    feed, feed_own = exchange_steps(wf, wf_o.at[0], loc.at[3], fs.at[0], fr.at[0])
    gather.middle()

    def turn_rows(at):
        above_o[at] = load_turned(above, at, length, pair)

    rows_loop(rows, turn_rows)
    hops.arrive(1)
    if length > 2:
        hops.start(2)
    gather.end()
    for hop in range(2, length):
        hops.arrive(hop)
        if hop + 1 < length:
            hops.start(hop + 1)
    for copy in down + feed + gates:
        copy.wait()
    down_own.wait()
    feed_own.wait()
    hops.finish()


def first(inputs, above, mixer, mlp, gn, gp, length, collective_id):
    rows, width = inputs.shape
    share = mixer.shape[0]
    wm, wf, wd = ((8, share, n) for n in (mixer.shape[1] // 8, mlp.shape[1] // 12, mlp.shape[1] // 24))
    low = jax.ShapeDtypeStruct((rows, width), BF16)
    return pl.pallas_call(
        functools.partial(first_kernel, length),
        out_shape=(
            jax.ShapeDtypeStruct((8, rows, width), BF16),
            jax.ShapeDtypeStruct((length,) + wm, BF16),
            jax.ShapeDtypeStruct((length,) + wf, BF16),
            jax.ShapeDtypeStruct((length,) + wd, BF16),
            jax.ShapeDtypeStruct((8, width), F32),
            jax.ShapeDtypeStruct((length,) + gp.shape, gp.dtype),
            low,
            low,
        ),
        in_specs=[VM] * 5 + [ANY],
        out_specs=(ANY, ANY, ANY, ANY, VM, ANY, VM, VM),
        scratch_shapes=[
            pltpu.VMEM((rows, width), BF16),
            pltpu.VMEM((8, length, 8, 128), F32),
            pltpu.VMEM(wm, BF16),
            pltpu.VMEM(wf, BF16),
            pltpu.VMEM(wd, BF16),
            DMA((5,)), DMA((7,)), DMA((7,)), DMA((2, 7)), DMA((2, 7)),
            DMA((2, length)), DMA((2, length)), DMA((7,)), DMA((7,)), DMA, DMA,
            DMA((13,)), DMA((13,)), DMA((2, length)), DMA((2, length)),
        ],
        compiler_params=params(collective_id, 40 * 2**20),
        cost_estimate=pl.CostEstimate(flops=0, bytes_accessed=300 * 2**20, transcendentals=0),
    )(inputs, above, mixer, mlp, gn, gp)


def last_kernel(
    length, share, heads_columns, wm, total, inputs, back, gains, gain_two, gp, sq,
    gw, gm, gv, pw, pm, pv,
    wm_o, grad_o, gm_o, gv_o, gw_o, pm_o, pv_o, pw_o, norm_o, factor_o,
    gain, row_sums, gn, gn_in, gn_mid, gn_got, gp_got, gp_sum, gp_fin, sq_plane, sq_line,
    loc, ss, rs, gs, gr, ls, lr, move_s, move_r,
):
    y, c, z, x = place()
    s = 2 * z + x
    me = rank(y, c, x)
    line = line_peers(length)
    plane = plane_peers()
    owner = x * length + z
    to_z = owner // 2
    to_x = owner - 2 * to_z
    from_z, from_x = lax.rem(s, length), s // length
    moves = jnp.where(jnp.logical_and(to_z == z, to_x == x), 0, 1)
    barrier = pltpu.get_barrier_semaphore()
    for peer in line + plane:
        pl.semaphore_signal(barrier, inc=1, device_id=peer, device_id_type=MESH)

    @pl.when(moves == 1)
    def _():
        pl.semaphore_signal(barrier, inc=1, device_id=device(y, c, to_z, to_x), device_id_type=MESH)
        pl.semaphore_signal(barrier, inc=1, device_id=device(y, c, from_z, from_x), device_id_type=MESH)

    pl.semaphore_wait(barrier, len(line) + len(plane) + 2 * moves)

    gate = [
        remote(gp.at[k + 1], gp_got.at[k], ls.at[0, k], lr.at[0, k], line[k]) for k in range(length - 1)
    ]
    rows, width = inputs.shape
    pair = width // (4 * length)
    gain[...] = jnp.zeros_like(gain)

    def body(at):
        grad, gain_part = norm_rows_back(inputs[at].astype(F32), gains[0:1], total[at])
        store_turned(grad_o, at, back[at] + grad, length, pair)
        gain[...] += gain_part

    rows_loop(rows, body)
    row = lax.broadcasted_iota(jnp.int32, (8, width), 0)
    ones = jnp.sum(gain[...], axis=0, keepdims=True)
    twos = jnp.sum(gain_two[...], axis=0, keepdims=True)
    row_sums[...] = jnp.where(row == 0, ones, jnp.where(row == 1, twos, 0.0))
    if pair < 128:
        gn[...] = jnp.zeros_like(gn)
    for k in range(length):
        for b in range(4):
            gn[b, k, :, :pair] = row_sums[:, (4 * k + b) * pair : (4 * k + b + 1) * pair]
    sends = []
    for n, (fy, fc, fx) in enumerate(FLIPS):
        to = flip(y, fy) * 2 + flip(c, fc)
        sends.append(remote(gn.at[to], gn_in.at[n], gs.at[0, n], gr.at[0, n], plane[n]))
    copies, own = exchange_steps(wm, wm_o, loc, ss, rs)
    for copy in gate:
        copy.wait()
    sums = gp[0]
    for k in range(length - 1):
        sums = sums + gp_got[k]
    gp_sum[...] = sums
    for copy in sends:
        copy.wait()
    sums = gn[2 * y + c]
    for n in range(7):
        sums = sums + gn_in[n]
    gn_mid[...] = sums
    sends = [
        remote(gn_mid.at[k + 1], gn_got.at[k], ls.at[1, k], lr.at[1, k], line[k])
        for k in range(length - 1)
    ]

    @pl.when(moves == 1)
    def _():
        copy = remote(gp_sum, gp_fin, move_s, move_r, device(y, c, to_z, to_x))
        copy.wait()

    @pl.when(moves == 0)
    def _():
        gp_fin[...] = gp_sum[...]

    for copy in sends:
        copy.wait()
    sums = gn_mid[0]
    for k in range(length - 1):
        sums = sums + gn_got[k]
    lane = lax.broadcasted_iota(jnp.int32, (8, 128), 1)
    mine = jnp.logical_and(lane >= x * share, lane < (x + 1) * share)
    gain_sum = jnp.where(mine, sums, 0.0)
    gate_sum = gp_fin[...]
    sq_plane[me] = sq[...] + gain_sum * gain_sum + tile_of_squares(gate_sum)
    sends = [
        remote(sq_plane.at[me], sq_plane.at[me], gs.at[1, n], gr.at[1, n], plane[n]) for n in range(7)
    ]
    for copy in sends:
        copy.wait()
    sums = sq_plane[0]
    for n in range(1, 8):
        sums = sums + sq_plane[n]
    sq_line[z] = sums
    sends = [
        remote(sq_line.at[z], sq_line.at[z], ls.at[2, k], lr.at[2, k], line[k])
        for k in range(length - 1)
    ]
    for copy in sends:
        copy.wait()
    sums = sq_line[0]
    for n in range(1, length):
        sums = sums + sq_line[n]
    sums = jnp.sum(jnp.sum(sums, axis=0, keepdims=True), axis=1, keepdims=True)
    norm = jnp.broadcast_to(jnp.sqrt(sums), (8, 128))
    factor = clip_limit / jnp.maximum(norm, clip_limit)
    norm_o[...] = norm
    factor_o[...] = factor
    gm_o[...], gv_o[...], gw_o[...] = adam_step(
        gw[...], gain_sum, gm[...], gv[...], factor, rate_gains, 0.0
    )
    column = lax.broadcasted_iota(jnp.int32, gate_sum.shape, 1)
    matrix = column < heads_columns
    pm_o[...], pv_o[...], pw_o[...] = adam_step(
        pw[...], gate_sum, pm[...], pv[...], factor[0:1, 0:1],
        jnp.where(matrix, rate_matrix, rate_channel), jnp.where(matrix, decay_matrix, 0.0),
    )
    for copy in copies:
        copy.wait()
    own.wait()


def last(wm, total, inputs, back, gains, gain_two, gp, sq, gain_state, gate_state, share, columns, length, collective_id):
    rows, width = inputs.shape
    tile, pack = TILE, jax.ShapeDtypeStruct(gp.shape[1:], F32)
    return pl.pallas_call(
        functools.partial(last_kernel, length, share, columns),
        out_shape=(
            jax.ShapeDtypeStruct(wm.shape, wm.dtype),
            jax.ShapeDtypeStruct((rows, width), F32),
            tile, tile, tile, pack, pack, pack, tile, tile,
        ),
        in_specs=[ANY] + [VM] * 13,
        out_specs=(ANY,) + (VM,) * 9,
        scratch_shapes=[
            pltpu.VMEM((8, width), F32),
            pltpu.VMEM((8, width), F32),
            pltpu.VMEM((4, length, 8, 128), F32),
            pltpu.VMEM((7, length, 8, 128), F32),
            pltpu.VMEM((length, 8, 128), F32),
            pltpu.VMEM((length, 8, 128), F32),
            pltpu.VMEM(gp.shape, F32),
            pltpu.VMEM(gp.shape[1:], F32),
            pltpu.VMEM(gp.shape[1:], F32),
            pltpu.VMEM((8, 8, 128), F32),
            pltpu.VMEM((length, 8, 128), F32),
            DMA, DMA((7,)), DMA((7,)), DMA((2, 7)), DMA((2, 7)),
            DMA((3, length)), DMA((3, length)), DMA, DMA,
        ],
        compiler_params=params(collective_id, 32 * 2**20),
    )(wm, total, inputs, back, gains, gain_two, gp, sq, *gain_state, *gate_state)


def minus_expm1(v):
    series = 1.0 + v * (1.0 / 8.0)
    for n in (7.0, 6.0, 5.0, 4.0, 3.0, 2.0):
        series = 1.0 + series * v * (1.0 / n)
    return jnp.where(v > -0.5, -v * series, 1.0 - jnp.exp(v))


def gelu_parts(v):
    inner = jnp.tanh(GELU_SCALE * (v + 0.044715 * v * v * v))
    return 0.5 * v * (1.0 + inner), inner


def gelu_slope(v, inner):
    return 0.5 * (1.0 + inner) + 0.5 * v * (1.0 - inner * inner) * GELU_SCALE * (
        1.0 + 3.0 * 0.044715 * v * v
    )


CHUNK = 64


def forward_kernel(
    length, proj, gate, chan, above, w_in, mixed, decay_o, width_o, recur_o, enter_o, conv_o, xe, se, ends_o, above_o, w,
    pre, loc_h, ends, carry, hs, hr, es, er, gather_l, gather_s, gather_r, hop_s, hop_r,
):
    y, c, z, x = place()
    line = line_peers(length)
    greet(line + gather_peers())
    seqs, span, rc = mixed.shape
    chunks = span // CHUNK
    gather = Gather(above, above_o, gather_l, gather_s, gather_r)
    ahead = device(y, c, lax.rem(z + 1, length), x)
    for b in range(seqs):
        xe[b, span : span + 8] = proj[b, span - 8 : span, rc:].astype(BF16).astype(F32)
    halo = remote(xe.at[:, pl.ds(span, 8)], xe.at[:, pl.ds(0, 8)], hs, hr, ahead)
    halo.wait_send()
    hops = LineGather(w, length, hop_s, hop_r)
    hops.start(1)
    gather.begin()

    @pl.loop(0, seqs * chunks)
    def _(i):
        b = i // chunks
        r = pl.multiple_of((i - b * chunks) * CHUNK, CHUNK)
        xe[b, pl.ds(r + 8, CHUNK)] = proj[b, pl.ds(r, CHUNK), rc:].astype(BF16).astype(F32)

    halo.wait_recv()

    @pl.when(z == 0)
    def _():
        xe[:, 0:8] = jnp.zeros((seqs, 8, rc), F32)

    def coefficients(i):
        b = i // chunks
        r = pl.multiple_of((i - b * chunks) * CHUNK, CHUNK)
        at = pl.ds(r, CHUNK)
        window = xe[b, pl.ds(r, CHUNK + 8)]
        total = chan[4:5] + chan[0:1] * window[8:]
        for k in (1, 2, 3):
            total = total + chan[k : k + 1] * pltpu.roll(window, k, 0)[8:]
        low = total.astype(BF16)
        conv_o[b, at] = low
        value = low.astype(F32)
        gates = jnp.dot(low, gate[...], preferred_element_type=F32)
        recur = jax.nn.sigmoid(gates[:, :rc] + chan[5:6])
        enter = jax.nn.sigmoid(gates[:, rc:] + chan[6:7])
        log_decay = -chan[7:8] * recur
        decay = jnp.exp(log_decay)
        width = jnp.sqrt(minus_expm1(2.0 * log_decay))
        recur_o[b, at] = recur
        enter_o[b, at] = enter
        decay_o[b, at] = decay
        width_o[b, at] = width
        loc_h[b, at] = width * enter * value

    half = seqs * chunks // 2
    pl.loop(0, half)(coefficients)
    gather.middle()
    hops.arrive(1)
    if length > 2:
        hops.start(2)
    pl.loop(half, seqs * chunks)(coefficients)
    row = lax.broadcasted_iota(jnp.int32, (8, rc), 0)

    def tile(i, held):
        at = pl.ds(pl.multiple_of(i * 8, 8), 8)
        new = []
        for b in range(seqs):
            a, h = decay_o[b, at], loc_h[b, at]
            for n in (1, 2, 4):
                keep = row >= n
                h = h + jnp.where(keep, a * pltpu.roll(h, n, 0), 0.0)
                a = jnp.where(keep, a * pltpu.roll(a, n, 0), a)
            h = h + a * held[b][1]
            a = a * held[b][0]
            loc_h[b, at] = h
            pre[b, at] = a
            new.append((a[7:8], h[7:8]))
        return tuple(new)

    one, zero = jnp.ones((1, rc), F32), jnp.zeros((1, rc), F32)
    final = lax.fori_loop(0, span // 8, tile, ((one, zero),) * seqs)
    for b in range(seqs):
        ends[z, 0, b] = jnp.broadcast_to(final[b][0], (8, rc))
        ends[z, 1, b] = jnp.broadcast_to(final[b][1], (8, rc))
        ends_o[b] = jnp.broadcast_to(final[b][0], (8, rc))
    moves = [remote(ends.at[z], ends.at[z], es.at[k], er.at[k], line[k]) for k in range(length - 1)]
    for copy in moves:
        copy.wait()
    if length > 3:
        hops.arrive(2)
        hops.start(3)
    carry[...] = jnp.zeros_like(carry)
    for k in range(length):
        carry[...] = jnp.where(k < z, ends[k, 0] * carry[...] + ends[k, 1], carry[...])

    for b in range(seqs):
        se[b, 0:8] = carry[b]

    @pl.loop(0, seqs * chunks)
    def _(i):
        b = i // chunks
        r = pl.multiple_of((i - b * chunks) * CHUNK, CHUNK)
        at = pl.ds(r, CHUNK)
        state = loc_h[b, at] + pre[b, at] * carry[b, 0:1]
        se[b, pl.ds(r + 8, CHUNK)] = state
        gelu, _ = gelu_parts(proj[b, at, :rc])
        mixed[b, at] = (state * gelu).astype(BF16)

    gather.end()
    for hop in range(min(3, length - 1), length):
        hops.arrive(hop)
        if hop + 1 < length:
            hops.start(hop + 1)
    hops.finish()


def recur_forward(proj, gate, chan, above, w, length, collective_id):
    seqs, span, rc = proj.shape[0], proj.shape[1], proj.shape[2] // 2
    full = jax.ShapeDtypeStruct((seqs, span, rc), F32)
    longer = jax.ShapeDtypeStruct((seqs, span + 8, rc), F32)
    low = jax.ShapeDtypeStruct((seqs, span, rc), BF16)
    return pl.pallas_call(
        functools.partial(forward_kernel, length),
        out_shape=(
            low, full, full, full, full, low, longer, longer,
            jax.ShapeDtypeStruct((seqs, 8, rc), F32),
            jax.ShapeDtypeStruct((8,) + above.shape, above.dtype),
            jax.ShapeDtypeStruct(w.shape, w.dtype),
        ),
        in_specs=[VM, VM, VM, ANY, ANY],
        out_specs=(VM,) * 9 + (ANY, ANY),
        scratch_shapes=[
            pltpu.VMEM((seqs, span, rc), F32),
            pltpu.VMEM((seqs, span, rc), F32),
            pltpu.VMEM((length, 2, seqs, 8, rc), F32),
            pltpu.VMEM((seqs, 8, rc), F32),
            DMA, DMA, DMA((length,)), DMA((length,)),
            DMA, DMA((13,)), DMA((13,)), DMA((2, length)), DMA((2, length)),
        ],
        input_output_aliases={4: 10},
        compiler_params=params(collective_id, 56 * 2**20),
        cost_estimate=pl.CostEstimate(
            flops=2 * seqs * span * rc * rc * 2, bytes_accessed=100 * 2**20, transcendentals=0
        ),
    )(proj, gate, chan, above, w)


def backward_kernel(
    length, cuts, dmix, gate, chan, decay, width, recur, enter, conv, xe, se, ends_f, proj, *refs
):
    terms, refs = refs[: len(cuts)], refs[len(cuts) :]
    dproj, dgate, gchan, sums, squares, suffix, grad, de, ends, carry, hs, hr, es, er, *line_refs = refs
    y, c, z, x = place()
    line = line_peers(length)
    greet(line)
    scatter = LineScatter([(ref, *cut) for ref, cut in zip(terms, cuts)], length, *line_refs)
    scatter.begin()
    seqs, span, rc = decay.shape
    chunks = span // CHUNK

    @pl.loop(0, seqs * chunks)
    def _(i):
        b = i // chunks
        r = pl.multiple_of((i - b * chunks) * CHUNK, CHUNK)
        at = pl.ds(r, CHUNK)
        branch = proj[b, at]
        gelu, inner = gelu_parts(branch)
        above = dmix[b, at]
        state = se[b, pl.ds(r + 8, CHUNK)]
        grad[b, at] = above * gelu
        dproj[b, at, :rc] = (above * state * gelu_slope(branch, inner)).astype(BF16)

    row = lax.broadcasted_iota(jnp.int32, (8, rc), 0)

    def tile(i, held):
        at = pl.ds(pl.multiple_of(span - 8 - i * 8, 8), 8)
        new = []
        for b in range(seqs):
            product, total, following = held[b]
            plain, h = decay[b, at], grad[b, at]
            a = jnp.where(row == 7, following, pltpu.roll(plain, 7, 0))
            for n in (1, 2, 4):
                keep = row < 8 - n
                h = h + jnp.where(keep, a * pltpu.roll(h, 8 - n, 0), 0.0)
                a = jnp.where(keep, a * pltpu.roll(a, 8 - n, 0), a)
            h = h + a * total
            a = a * product
            grad[b, at] = h
            suffix[b, at] = a
            new.append((a[0:1], h[0:1], plain[0:1]))
        return tuple(new)

    one, zero = jnp.ones((1, rc), F32), jnp.zeros((1, rc), F32)
    final = lax.fori_loop(0, span // 8, tile, ((one, zero, one),) * seqs)
    for b in range(seqs):
        ends[z, 0, b] = ends_f[b]
        ends[z, 1, b] = jnp.broadcast_to(final[b][1] * final[b][2], (8, rc))
    moves = [remote(ends.at[z], ends.at[z], es.at[k], er.at[k], line[k]) for k in range(length - 1)]
    for copy in moves:
        copy.wait()
    scatter.start()
    carry[...] = jnp.zeros_like(carry)
    for k in reversed(range(length)):
        carry[...] = jnp.where(k > z, ends[k, 0] * carry[...] + ends[k, 1], carry[...])

    gchan[...] = jnp.zeros_like(gchan)

    @pl.loop(0, seqs * chunks)
    def _(i):
        b = i // chunks
        r = pl.multiple_of((i - b * chunks) * CHUNK, CHUNK)
        at = pl.ds(r, CHUNK)
        g = grad[b, at] + suffix[b, at] * carry[b, 0:1]
        a, w, ra, ri = decay[b, at], width[b, at], recur[b, at], enter[b, at]
        value = conv[b, at].astype(F32)
        before = pltpu.roll(se[b, pl.ds(r, CHUNK + 8)], 1, 0)[8:]
        dla = g * before * a - g * ri * value * (a * a) / w
        slope = dla * ra * (1.0 - ra)
        dpa = (-chan[7:8] * slope).astype(BF16)
        dpi = (g * w * value * ri * (1.0 - ri)).astype(BF16)
        dgate[b, at, :rc] = dpa
        dgate[b, at, rc:] = dpi
        gchan[5] += fold(dpa.astype(F32))
        gchan[6] += fold(dpi.astype(F32))
        gchan[7] += fold(dla * ra)
        back = lax.dot_general(
            dgate[b, at], gate[...], (((1,), (1,)), ((), ())), preferred_element_type=F32
        )
        dcv = (g * w * ri + back).astype(BF16).astype(F32)
        de[b, at] = dcv
        gchan[4] += fold(dcv)

    behind = device(y, c, lax.rem(z + length - 1, length), x)
    halo = remote(de.at[:, pl.ds(0, 8)], de.at[:, pl.ds(span, 8)], hs, hr, behind)
    halo.wait()
    scatter.start()

    @pl.when(z == length - 1)
    def _():
        de[:, span:] = jnp.zeros((seqs, 8, rc), F32)

    @pl.loop(0, seqs * chunks)
    def _(i):
        b = i // chunks
        r = pl.multiple_of((i - b * chunks) * CHUNK, CHUNK)
        at = pl.ds(r, CHUNK)
        window = de[b, pl.ds(r, CHUNK + 8)]
        inputs = xe[b, pl.ds(r, CHUNK + 8)]
        dcv = window[:CHUNK]
        total = chan[0:1] * dcv
        gchan[0] += fold(dcv * inputs[8:])
        for k in (1, 2, 3):
            total = total + chan[k : k + 1] * pltpu.roll(window, CHUNK + 8 - k, 0)[:CHUNK]
            gchan[k] += fold(dcv * pltpu.roll(inputs, k, 0)[8:])
        dproj[b, at, rc:] = total.astype(BF16)

    scatter.end(sums, squares)


def recur_backward(dmix, gate, chan, kept, proj, terms, cuts, length, collective_id):
    decay, width, recur, enter, conv, xe, se, ends = kept
    seqs, span, rc = decay.shape
    wide = jax.ShapeDtypeStruct((seqs, span, 2 * rc), BF16)
    line_rows, columns = terms[0].shape[1], sum(cut[1] for cut in cuts)
    return pl.pallas_call(
        functools.partial(backward_kernel, length, cuts),
        grid=(1,),
        out_shape=(
            wide, wide, jax.ShapeDtypeStruct((8, 8, rc), F32),
            jax.ShapeDtypeStruct((line_rows, columns), BF16), TILE,
        ),
        in_specs=[VM] * 11 + [pl.BlockSpec((seqs, span, rc), lambda i: (0, 0, 0))] + [ANY] * len(terms),
        out_specs=(VM,) * 5,
        scratch_shapes=[
            pltpu.VMEM((seqs, span, rc), F32),
            pltpu.VMEM((seqs, span, rc), F32),
            pltpu.VMEM((seqs, span + 8, rc), F32),
            pltpu.VMEM((length, 2, seqs, 8, rc), F32),
            pltpu.VMEM((seqs, 8, rc), F32),
            DMA, DMA, DMA((length,)), DMA((length,)),
        ]
        + line_scratch(length, line_rows, columns, len(cuts)),
        compiler_params=params(collective_id, 62 * 2**20),
        cost_estimate=pl.CostEstimate(
            flops=2 * seqs * span * rc * rc * 2, bytes_accessed=120 * 2**20, transcendentals=0
        ),
    )(dmix, gate, chan, decay, width, recur, enter, conv, xe, se, ends, proj, *terms)


def contract_last(left, right):
    return lax.dot_general(
        left, right, (((1,), (1,)), ((), ())), preferred_element_type=F32
    )


def contract_first(left, right):
    return lax.dot_general(
        left, right, (((0,), (0,)), ((), ())), preferred_element_type=F32
    )


def adam_step(weight, grad, first, second, factor, rate, decay_rate):
    clipped = grad * factor
    first_new = beta_first * first + (1.0 - beta_first) * clipped
    second_new = beta_second * second + (1.0 - beta_second) * clipped * clipped
    first_hat = first_new / (1.0 - beta_first**STEP)
    second_hat = second_new / (1.0 - beta_second**STEP)
    weight_new = weight - rate * (
        first_hat / (jnp.sqrt(second_hat) + adam_eps) + decay_rate * weight
    )
    return (first_new, second_new, weight_new)


def adam_kernel(rate, decay_rate, factor, w, g, m, v, m_o, v_o, w_o):
    first_new, second_new, weight_new = adam_step(
        w[...], g[0].astype(F32), m[...], v[...], factor[0:1, 0:1], rate, decay_rate
    )
    m_o[...] = first_new
    v_o[...] = second_new
    w_o[...] = weight_new


def adam_blocks(weight, grad, first, second, factor, rate, decay_rate):
    rows, part = grad.shape[1], grad.shape[2] // 3
    block = pl.BlockSpec((rows, part), lambda t, j: (0, j * 8 + t))
    shape = jax.ShapeDtypeStruct(weight.shape, F32)
    return pl.pallas_call(
        functools.partial(adam_kernel, rate, decay_rate),
        grid=(8, 3),
        out_shape=(shape,) * 3,
        in_specs=[
            pl.BlockSpec((8, 128), lambda t, j: (0, 0)),
            block,
            pl.BlockSpec((1, rows, part), lambda t, j: (t, 0, j)),
            block,
            block,
        ],
        out_specs=(block,) * 3,
        cost_estimate=pl.CostEstimate(flops=0, bytes_accessed=7 * 4 * weight.size, transcendentals=0),
    )(factor, weight, grad, first, second)


def adam_pairs_kernel(rate, decay_rate, factor, w, g, m, v, m_o, v_o, w_o):
    part = g.shape[2] // 3
    for j in range(3):

        @pl.when(pl.program_id(1) == j)
        def _():
            at = slice(j * part, (j + 1) * part)
            grad = jnp.concatenate([g[0, :, at].astype(F32), g[1, :, at].astype(F32)], axis=1)
            first_new, second_new, weight_new = adam_step(
                w[...], grad, m[...], v[...], factor[0:1, 0:1], rate, decay_rate
            )
            m_o[...] = first_new
            v_o[...] = second_new
            w_o[...] = weight_new


def adam_pairs(weight, grad, first, second, factor, rate, decay_rate):
    rows, part = grad.shape[1], grad.shape[2] // 3
    block = pl.BlockSpec((rows, 2 * part), lambda t, j: (0, j * 4 + t))
    shape = jax.ShapeDtypeStruct(weight.shape, F32)
    return pl.pallas_call(
        functools.partial(adam_pairs_kernel, rate, decay_rate),
        grid=(4, 3),
        out_shape=(shape,) * 3,
        in_specs=[
            pl.BlockSpec((8, 128), lambda t, j: (0, 0)),
            block,
            pl.BlockSpec((2, rows, 3 * part), lambda t, j: (t, 0, 0)),
            block,
            block,
        ],
        out_specs=(block,) * 3,
        cost_estimate=pl.CostEstimate(flops=0, bytes_accessed=7 * 4 * weight.size, transcendentals=0),
    )(factor, weight, grad, first, second)


def on_device(
    block_input,
    out_grad,
    norm_gains,
    mixer_weight,
    gate_weight,
    chan_params,
    mlp_weight,
    first_gains,
    first_mixer,
    first_gate,
    first_chan,
    first_mlp,
    second_gains,
    second_mixer,
    second_gate,
    second_chan,
    second_mlp,
):
    length = lax.axis_size("seq") // 2
    z = lax.axis_index("seq") // 2
    tokens, model = block_input.shape[1:]
    share = mixer_weight.shape[0]
    pair = 2 * share
    lru = mixer_weight.shape[1] // 3
    hidden = mlp_weight.shape[1] // 3
    r8, f8 = lru // 8, hidden // 8
    rc = -(-r8 // 128) * 128
    head = gate_weight.shape[1] // 2
    heads = r8 // head
    gate_rows = gate_weight.shape[0]
    gate_pad = -(-gate_rows // 16) * 16

    x = lax.axis_index("seq") - 2 * z
    batch = lax.axis_index("batch")
    plain = pair % 128 == 0

    def turned(v):
        if plain:
            return v
        v = v.reshape(v.shape[0], 4, length, pair).swapaxes(1, 2)
        return jnp.roll(v, -z, axis=1).reshape(v.shape[0], model)

    def turned_back(v):
        if plain:
            return v
        v = jnp.roll(v.reshape(v.shape[0], length, 4, pair), z, axis=1)
        return v.swapaxes(1, 2).reshape(v.shape[0], model)

    def gain_tile(v):
        return jnp.where(
            x == 0,
            jnp.pad(v, ((0, 6), (0, 128 - share))),
            jnp.pad(v, ((0, 6), (share, 128 - 2 * share))),
        )

    def gain_rows(v):
        return jnp.where(x == 0, v[:2, :share], v[:2, share : 2 * share])

    def gate_pack(rows, channels):
        pack = jnp.concatenate([rows, channels.T], axis=1)
        return jnp.pad(pack, ((0, gate_pad - gate_rows), (0, rc - 2 * head - 8)))

    gain_state = [gain_tile(v) for v in (norm_gains, first_gains, second_gains)]
    gate_state = [
        gate_pack(*pair_of)
        for pair_of in ((gate_weight, chan_params), (first_gate, first_chan), (second_gate, second_chan))
    ]
    normed_one, mixer_full, mlp_gu, mlp_down, gains, gate_in, inputs, above = first(
        turned(block_input[0]),
        turned(out_grad[0]),
        mixer_weight,
        mlp_weight,
        gain_state[0],
        gate_state[0].astype(BF16),
        length,
        1,
    )
    normed_one = normed_one.reshape(8 * tokens, model)
    gate_own = gate_in[:, :gate_rows].reshape(r8, rc)
    chan = gate_own[:, 2 * head : 2 * head + 8].astype(F32).T
    lam = chan[7]
    fill = jnp.concatenate([jnp.zeros((7, rc - r8), F32), jnp.ones((1, rc - r8), F32)])
    chan = jnp.concatenate([chan[:7], 8.0 * jax.nn.softplus(-lam)[None]])
    chan = jnp.concatenate([chan, fill], axis=1)
    gate = []
    for h in range(heads):
        block = gate_own[h * head : (h + 1) * head, : 2 * head]
        at = ((0, 0), (h * head, rc - (h + 1) * head))
        gate.append(
            jnp.concatenate([jnp.pad(block[:, :head], at), jnp.pad(block[:, head:], at)], axis=1)
        )
    gate = jnp.pad(jnp.concatenate(gate), ((0, rc - r8), (0, 0)))

    mixer_full = mixer_full.reshape(model, 3 * r8)
    parts = [jnp.pad(mixer_full[:, n * r8 : (n + 1) * r8], ((0, 0), (0, rc - r8))) for n in range(3)]
    mixer_first = jnp.concatenate(parts[:2], axis=1)
    mixer_last = parts[2]
    span = 2 * tokens
    projected = jnp.dot(normed_one, mixer_first, preferred_element_type=F32)
    projected = projected.reshape(4, span, 2 * rc)
    mixed, *kept, grad_out, mlp_down = recur_forward(projected, gate, chan, above, mlp_down, length, 2)
    grad_out = grad_out.reshape(8 * tokens, model)
    mixed = mixed.reshape(4 * span, rc)
    residual, normed_two, mlp_gu = middle(
        contract_last(mixed, mixer_last).astype(BF16), inputs, gains, mlp_gu, length, 3
    )
    normed_two = normed_two.reshape(8 * tokens, model)
    mlp_gu = mlp_gu.reshape(model, 2 * f8)
    mlp_gate, mlp_up = mlp_gu[:, :f8], mlp_gu[:, f8:]
    mlp_down = mlp_down.reshape(model, f8)
    gg = jnp.dot(normed_two, mlp_gate, preferred_element_type=F32)
    uu = jnp.dot(normed_two, mlp_up, preferred_element_type=F32)
    dhid = jnp.dot(grad_out, mlp_down, preferred_element_type=F32)
    gelu, inner = gelu_parts(gg)
    hid = (gelu * uu).astype(BF16)
    dgg = (dhid * uu * gelu_slope(gg, inner)).astype(BF16)
    duu = (dhid * gelu).astype(BF16)
    dnormed_two = contract_last(dgg, mlp_gate) + contract_last(duu, mlp_up)

    def terms(v):
        return v.astype(BF16).reshape(length, 8 * share, f8)

    gate_terms = terms(contract_first(normed_two, dgg))
    up_terms = terms(contract_first(normed_two, duu))
    down_terms = terms(contract_first(grad_out, hid))
    up_cut = f8 // 256 * 128
    down_cut = f8 // 384 * 128

    grad_residual, gain_two, dmz, sums_one, squares_one = turn(
        dnormed_two.astype(BF16), residual, above, gains,
        (gate_terms, up_terms), ((0, f8), (0, up_cut)), length, 4,
    )
    dmz = dmz.reshape(8 * tokens, model)
    block_output, sums_two, squares_two = output(
        contract_last(hid, mlp_down).astype(BF16), residual,
        (up_terms, down_terms), ((up_cut, f8 - up_cut), (0, down_cut)), length, 5,
    )
    dmix = jnp.dot(dmz, mixer_last, preferred_element_type=F32).reshape(4, span, rc)
    dproj, dgate, chan_grad, sums_three, squares_three = recur_backward(
        dmix, gate, chan, kept, projected, (down_terms,), ((down_cut, f8 - down_cut),), length, 6
    )
    dproj = dproj.reshape(4 * span, 2 * rc)
    dgate = dgate.reshape(4 * span, 2 * rc)
    proj_grad = contract_first(normed_one, dproj)
    last_grad = contract_first(dmz, mixed)
    mixer_terms = jnp.concatenate(
        [proj_grad[:, :r8], proj_grad[:, rc : rc + r8], last_grad[:, :r8]], axis=1
    )
    mixer_terms = mixer_terms.astype(BF16).reshape(length, 8 * share, 3 * r8)
    dnormed_one, mlp_back, mixer_sums, squares_four = closing(
        contract_last(dproj, mixer_first).astype(BF16), (sums_one, sums_two, sums_three), mixer_terms,
        length, 7,
    )

    gate_full_grad = contract_first(kept[4].reshape(4 * span, rc), dgate)
    blocks = []
    for h in range(heads):
        at = slice(h * head, (h + 1) * head)
        blocks.append(
            jnp.concatenate([gate_full_grad[at, at], gate_full_grad[at, rc + h * head : rc + (h + 1) * head]], axis=1)
        )
    gate_grad_own = jnp.concatenate(blocks)
    chan_grad = jnp.sum(chan_grad, axis=1)[:, :r8]
    chan_grad = jnp.concatenate([chan_grad[:7], (8.0 * jax.nn.sigmoid(-lam) * chan_grad[7])[None]])
    gate_back = jnp.concatenate([gate_grad_own, chan_grad.T], axis=1).reshape(length, gate_rows, 2 * head + 8)
    gate_back = jnp.pad(
        gate_back, ((0, 0), (0, gate_pad - gate_rows), (0, rc - 2 * head - 8))
    )
    gate_back = jnp.roll(gate_back, -z, axis=0)
    mixer_back, input_grad, *small, norm, factor = last(
        mixer_sums.reshape(8, share, 3 * r8), dnormed_one, inputs, grad_residual, gains, gain_two,
        gate_back, squares_one + squares_two + squares_three + squares_four, gain_state, gate_state,
        share, 2 * head, length, 8,
    )
    gains_up = [gain_rows(v) for v in small[:3]]
    gate_up = [v[:gate_rows, : 2 * head] for v in small[3:]]
    chan_up = [v[:gate_rows, 2 * head : 2 * head + 8].T for v in small[3:]]
    mixer_up = adam_pairs(
        mixer_weight, mixer_back, first_mixer, second_mixer, factor, rate_matrix, decay_matrix
    )
    mlp_up = adam_blocks(
        mlp_weight, mlp_back, first_mlp, second_mlp, factor, rate_matrix, decay_matrix
    )
    return (
        turned_back(block_output)[None],
        turned_back(input_grad)[None],
        norm[0, 0],
        *gains_up,
        *mixer_up,
        *gate_up,
        *chan_up,
        *mlp_up,
    )


def solution(mesh):
    rows = P(("batch", "seq"), None)
    columns = P(None, ("batch", "seq"))
    data = P("batch", "seq", None)
    weights = (columns, rows, rows, columns, rows)
    in_specs = (data, data) + weights * 3
    triples = tuple(spec for spec in weights for _ in range(3))
    return jax.shard_map(
        on_device,
        mesh=mesh,
        in_specs=in_specs,
        out_specs=(data, data, P()) + triples,
        check_vma=False,
    )
```

```python
import functools
import math

import jax
import jax.numpy as jnp
from jax import lax
from jax.experimental import pallas as pl
from jax.experimental.pallas import tpu as pltpu
from jax.sharding import PartitionSpec as P

STEP = 10
norm_eps = 1e-06
clip_limit = 1.0
beta_first = 0.9
beta_second = 0.999
adam_eps = 1e-08
rate_matrix = 0.05
rate_gains = 0.8
rate_channel = 2.0
decay_matrix = 0.1

MESH = pl.DeviceIdType.MESH
F32 = jnp.float32
BF16 = jnp.bfloat16
ANY = pl.BlockSpec(memory_space=pl.ANY)
VM = pl.BlockSpec(memory_space=pltpu.VMEM)
FLIPS = [(fy, fc, fx) for fy in (0, 1) for fc in (0, 1) for fx in (0, 1) if fy + fc + fx]
GELU_SCALE = math.sqrt(2.0 / math.pi)


def place():
    b = lax.axis_index("batch")
    s = lax.axis_index("seq")
    y, z = b // 2, s // 2
    return y, b - 2 * y, z, s - 2 * z


def device(y, c, z, x):
    return (y * 2 + c, z * 2 + x)


def rank(y, c, x):
    return (y * 2 + c) * 2 + x


def flip(v, f):
    return 1 - v if f else v


def greet(peers):
    barrier = pltpu.get_barrier_semaphore()
    for peer in peers:
        pl.semaphore_signal(barrier, inc=1, device_id=peer, device_id_type=MESH)
    pl.semaphore_wait(barrier, len(peers))


def remote(src, dst, send, recv, to):
    copy = pltpu.make_async_remote_copy(
        src_ref=src, dst_ref=dst, send_sem=send, recv_sem=recv, device_id=to, device_id_type=MESH
    )
    copy.start()
    return copy


def params(collective_id, vmem=None):
    return pltpu.CompilerParams(
        collective_id=collective_id, has_side_effects=True, vmem_limit_bytes=vmem
    )


DMA = pltpu.SemaphoreType.DMA


def gather_peers():
    y, c, z, x = place()
    return [device(y, c, z, 1 - x), device(1 - y, c, z, x), device(y, 1 - c, z, x)]


class Gather:
    def __init__(self, a, o, loc, ss, rs):
        y, c, z, x = place()
        self.to_x, self.to_y, self.to_c = gather_peers()
        self.me, self.bx = rank(y, c, x), rank(y, c, 1 - x)
        self.by, self.bd = rank(1 - y, c, x), rank(1 - y, c, 1 - x)
        half = a.shape[0] // 2
        self.lo, self.hi = pl.ds(0, half), pl.ds(half, half)
        self.a, self.o, self.loc, self.ss, self.rs = a, o, loc, ss, rs
        self.done, self.last = [], []

    def send(self, src, dst, k, to):
        copy = remote(src, dst, self.ss.at[k], self.rs.at[k], to)
        self.done.append(copy)
        return copy

    def relay(self, block, part, k, to):
        return self.send(self.o.at[block, part], self.o.at[block, part], k, to)

    def begin_half(self, half):
        a, o, me = self.a, self.o, self.me
        part = (self.lo, self.hi)[half]
        if half == 0:
            self.s0 = self.send(a.at[part], o.at[me, part], 0, self.to_x)
            self.s3 = self.send(a.at[part], o.at[me, part], 3, self.to_y)
        else:
            self.s1 = self.send(a.at[part], o.at[me, part], 1, self.to_y)
            self.s2 = self.send(a.at[part], o.at[me, part], 2, self.to_x)
        self.last.append(self.send(a.at[part], o.at[me, part], (4, 13)[half], self.to_c))
        if half == 1:
            self.own = pltpu.make_async_copy(a, o.at[me], self.loc)
            self.own.start()

    def begin(self):
        self.begin_half(0)
        self.begin_half(1)

    def middle(self):
        self.s0.wait_recv()
        self.s5 = self.relay(self.bx, self.lo, 5, self.to_y)
        self.last.append(self.relay(self.bx, self.lo, 7, self.to_c))
        self.s1.wait_recv()
        self.s6 = self.relay(self.by, self.hi, 6, self.to_x)
        self.last.append(self.relay(self.by, self.hi, 8, self.to_c))

    def relays(self, mark=lambda: None):
        self.s2.wait_recv()
        self.last.append(self.relay(self.bx, self.hi, 9, self.to_c))
        self.s3.wait_recv()
        self.last.append(self.relay(self.by, self.lo, 10, self.to_c))
        mark()
        self.s5.wait_recv()
        self.last.append(self.relay(self.bd, self.lo, 11, self.to_c))
        self.s6.wait_recv()
        self.last.append(self.relay(self.bd, self.hi, 12, self.to_c))

    def finish(self):
        for copy in self.last:
            copy.wait_recv()
        for copy in self.done:
            copy.wait_send()
        self.own.wait()

    def end(self, mark=lambda: None):
        self.relays(mark)
        self.finish()


def scatter_steps(p, o, mine, sib, part, got, loc, ss, rs):
    y, c, z, x = place()
    to_x, to_y, to_c = gather_peers()
    half = o.shape[0] // 2
    step = 16
    cut = (pl.ds(0, half), pl.ds(half, half))
    where = ((1 - y, 1 - x), (1 - y, x), (y, 1 - x), (y, x))
    order = [(0, 0), (0, 1), (1, 0), (2, 1), (2, 0), (1, 1), (3, 0), (3, 1)]
    from_c, own, sends = {}, {}, []
    for n, (t, h) in enumerate(order):
        ty, tx = where[t]
        own[t, h] = pltpu.make_async_copy(
            p.at[rank(ty, c, tx), cut[h]], mine.at[t, h], loc.at[n]
        )
        own[t, h].start()
        from_c[t, h] = remote(
            p.at[rank(ty, 1 - c, tx), cut[h]], sib.at[t, h], ss.at[n], rs.at[n], to_c
        )
        sends.append(from_c[t, h])
    yield "begun"

    def add(dst, t, h, extra):
        own[t, h].wait()
        from_c[t, h].wait_recv()

        @pl.loop(0, half // step)
        def _(i):
            at = pl.ds(pl.multiple_of(i * step, step), step)
            total = mine[t, h, at].astype(F32) + sib[t, h, at].astype(F32)
            for ref in extra:
                total = total + ref[at].astype(F32)
            dst[at] = total.astype(dst.dtype)

    def send(k, slot, to):
        copy = remote(part.at[k], got.at[slot], ss.at[8 + k], rs.at[8 + slot], to)
        sends.append(copy)
        return copy

    def arrival(slot):
        return pltpu.make_async_remote_copy(
            src_ref=part.at[0], dst_ref=got.at[slot], send_sem=ss.at[8], recv_sem=rs.at[8 + slot],
            device_id=to_x, device_id_type=MESH,
        )

    add(part.at[0], 0, 0, ())
    send(0, 1, to_y)
    add(part.at[1], 0, 1, ())
    send(1, 3, to_x)
    add(part.at[2], 1, 0, ())
    send(2, 0, to_y)
    add(part.at[3], 2, 1, ())
    send(3, 2, to_x)
    yield "sent"
    arrival(1).wait_recv()
    add(part.at[4], 2, 0, (got.at[1],))
    send(4, 4, to_x)
    yield "early"
    arrival(3).wait_recv()
    add(part.at[5], 1, 1, (got.at[3],))
    send(5, 5, to_y)
    yield "late"
    arrival(0).wait_recv()
    arrival(4).wait_recv()
    add(o.at[cut[0]], 3, 0, (got.at[0], got.at[4]))
    yield "low half"
    arrival(2).wait_recv()
    arrival(5).wait_recv()
    add(o.at[cut[1]], 3, 1, (got.at[2], got.at[5]))
    yield "high half"
    for copy in sends:
        copy.wait_send()


def scatter_scratch(half, width):
    return [
        pltpu.VMEM((4, 2, half, width), BF16),
        pltpu.VMEM((4, 2, half, width), BF16),
        pltpu.VMEM((6, half, width), BF16),
        pltpu.VMEM((6, half, width), BF16),
        DMA((8,)),
        DMA((14,)),
        DMA((14,)),
    ]


def exchange_steps(a, o, loc, ss, rs, columns=None):
    y, c, z, x = place()
    me = rank(y, c, x)
    dst = o.at[me] if columns is None else o.at[me, :, columns]
    copies = []
    for n, (fy, fc, fx) in enumerate(FLIPS):
        ty, tc, tx = flip(y, fy), flip(c, fc), flip(x, fx)
        copies.append(remote(a.at[rank(ty, tc, tx)], dst, ss.at[n], rs.at[n], device(ty, tc, z, tx)))
    own = pltpu.make_async_copy(a.at[me], dst, loc)
    own.start()
    return copies, own


def plane_peers():
    y, c, z, x = place()
    return [device(flip(y, fy), flip(c, fc), z, flip(x, fx)) for fy, fc, fx in FLIPS]


def line_peers(length):
    y, c, z, x = place()
    return [device(y, c, lax.rem(z + k, length), x) for k in range(1, length)]


class LineGather:
    def __init__(self, buf, length, ss, rs):
        y, c, z, x = place()
        self.z, self.length, self.buf, self.ss, self.rs = z, length, buf, ss, rs
        self.up = device(y, c, lax.rem(z + 1, length), x)
        self.down = device(y, c, lax.rem(z + length - 1, length), x)

    def copy(self, hop, upward):
        length, buf = self.length, self.buf
        src, dst = ((length - hop + 1) % length, length - hop) if upward else (hop - 1, hop)
        way = 0 if upward else 1
        return pltpu.make_async_remote_copy(
            src_ref=buf.at[src], dst_ref=buf.at[dst], send_sem=self.ss.at[way, hop - 1],
            recv_sem=self.rs.at[way, hop - 1], device_id=self.up if upward else self.down,
            device_id_type=MESH,
        )

    def sends(self, hop, act):
        z, length = self.z, self.length

        @pl.when(jnp.logical_and(z + 1 < length, z >= hop - 1))
        def _():
            act(self.copy(hop, True))

        @pl.when(jnp.logical_and(z >= 1, z + hop - 1 < length))
        def _():
            act(self.copy(hop, False))

    def start(self, hop):
        self.sends(hop, lambda copy: copy.start())

    def arrive(self, hop):
        z, length = self.z, self.length

        @pl.when(z >= hop)
        def _():
            self.copy(hop, True).wait_recv()

        @pl.when(z + hop < length)
        def _():
            self.copy(hop, False).wait_recv()

    def finish(self):
        for hop in range(1, self.length):
            self.sends(hop, lambda copy: copy.wait_send())


class LineScatter:
    def __init__(self, sources, length, total, up_mine, down_mine, up_got, down_got, loc, ss, rs):
        y, c, z, x = place()
        self.sources, self.length, self.total = sources, length, total
        self.mine, self.got = (up_mine, down_mine), (up_got, down_got)
        self.loc, self.ss, self.rs = loc, ss, rs
        self.to = (device(y, c, lax.rem(z + 1, length), x), device(y, c, lax.rem(z + length - 1, length), x))
        self.far = (z, length - 1 - z)
        self.next = 1

    def loads(self, way, hop):
        k = 0 if hop == 0 else self.length - hop if way == 0 else hop
        copies, at = [], 0
        for n, (ref, first, columns) in enumerate(self.sources):
            dst = self.term(way, hop) if hop else self.total
            copies.append(
                pltpu.make_async_copy(
                    ref.at[k, :, pl.ds(first, columns)], dst.at[:, pl.ds(at, columns)],
                    self.loc.at[way, hop, n],
                )
            )
            at += columns
        return copies

    def term(self, way, hop):
        return self.mine[way].at[hop - 1]

    def copy(self, way, hop):
        return pltpu.make_async_remote_copy(
            src_ref=self.term(way, hop), dst_ref=self.got[way].at[hop - 1],
            send_sem=self.ss.at[way, hop - 1], recv_sem=self.rs.at[way, hop - 1],
            device_id=self.to[way], device_id_type=MESH,
        )

    def load(self, hops):
        for hop in hops:
            for way in (0, 1) if hop else (0,):
                for copy in self.loads(way, hop):
                    copy.start()

    def start(self):
        hop = self.next
        if hop >= self.length:
            return
        self.next += 1
        for way in (0, 1):
            far = self.far[way]
            for copy in self.loads(way, hop):
                copy.wait()
            if hop > 1:

                @pl.when(jnp.logical_and(far >= 1, far <= hop - 1))
                def _():
                    self.copy(way, hop - 1).wait_recv()
                    dst, src = self.term(way, hop), self.got[way].at[hop - 2]

                    def add(at):
                        dst[at] = dst[at] + src[at]

                    rows_loop(dst.shape[0], add, unroll=4)

            @pl.when(far <= hop - 1)
            def _():
                self.copy(way, hop).start()

    def end(self, result, first_column, squares):
        last = self.length - 1
        for copy in self.loads(0, 0):
            copy.wait()
        columns = pl.ds(first_column, self.total.shape[1])

        def finish(ways):
            for way in ways:
                self.copy(way, last).wait_recv()

            def add(at):
                total = self.total[at].astype(F32)
                for way in ways:
                    total = total + self.got[way][last - 1, at].astype(F32)
                result[at, columns] = total.astype(result.dtype)
                squares[...] += tile_of_squares(total)

            rows_loop(result.shape[0], add)

        above, below = self.far[0] >= 1, self.far[1] >= 1
        pl.when(jnp.logical_and(above, below))(lambda: finish((0, 1)))
        pl.when(jnp.logical_not(above))(lambda: finish((1,)))
        pl.when(jnp.logical_not(below))(lambda: finish((0,)))
        for hop in range(1, self.length):
            for way in (0, 1):

                @pl.when(self.far[way] <= hop - 1)
                def _():
                    self.copy(way, hop).wait_send()


class HeldLine(LineScatter):
    def __init__(self, g, up_got, down_got, ss, rs):
        y, c, z, x = place()
        self.length = length = g.shape[0]
        self.sources, self.g, self.total = (), g, g.at[0]
        self.got, self.ss, self.rs = (up_got, down_got), ss, rs
        self.to = line_neighbours(length)
        self.far = (z, length - 1 - z)
        self.next = 1

    def term(self, way, hop):
        return self.g.at[self.length - hop if way == 0 else hop]


def chains_of(cuts):
    whole = sum(cut[2] for cut in cuts)
    left = -(-whole // 256) * 128
    lists = [], []
    for which, first_column, columns in cuts:
        taken = min(columns, left)
        if taken:
            lists[0].append((which, first_column, taken))
        if columns > taken:
            lists[1].append((which, first_column + taken, columns - taken))
        left -= taken
    return lists


class Lines:
    def __init__(self, terms, cuts, length, refs):
        self.chains, self.length = [], length
        for n, cut in enumerate(chains_of(cuts)):
            sources = [(terms[which], first_column, columns) for which, first_column, columns in cut]
            self.chains.append(
                LineScatter(sources, length, *refs[n * LINE_REFS : (n + 1) * LINE_REFS])
            )
        self.queue = [chain for _ in range(1, length) for chain in self.chains]

    def begin(self):
        for chain in self.chains:
            chain.load((1,))
        self.start()
        self.start()
        for chain in self.chains:
            chain.load((*range(2, self.length), 0))

    def start(self):
        if self.queue:
            self.queue.pop(0).start()

    def end(self, result, squares):
        while self.queue:
            self.start()
        squares[...] = jnp.zeros_like(squares)
        at = 0
        for chain in self.chains:
            chain.end(result, at, squares)
            at += chain.total.shape[1]


def lines_scratch(length, rows, cuts):
    return sum(
        (line_scratch(length, rows, sum(cut[2] for cut in chain), len(chain)) for chain in chains_of(cuts)), []
    )


def fold(v):
    return jnp.sum(v.reshape(v.shape[0] // 8, 8, v.shape[1]), axis=0)


def tile_of_squares(v):
    v = fold(v * v)
    part = v[:, :128]
    for n in range(1, v.shape[1] // 128):
        part = part + v[:, n * 128 : (n + 1) * 128]
    if v.shape[1] % 128:
        rest = v[:, v.shape[1] // 128 * 128 :]
        part = part + jnp.concatenate([rest, jnp.zeros((8, 128 - rest.shape[1]), F32)], axis=1)
    return part


def line_scratch(length, rows, columns, sources):
    slots = pltpu.VMEM((length - 1, rows, columns), BF16)
    return [pltpu.VMEM((rows, columns), BF16)] + [slots] * 4 + [
        DMA((2, length, sources)), DMA((2, length)), DMA((2, length))
    ]


LINE_REFS = 8
SCATTER_REFS = 7
TILE = jax.ShapeDtypeStruct((8, 128), F32)


def line_neighbours(length):
    y, c, z, x = place()
    return [device(y, c, lax.rem(z + 1, length), x), device(y, c, lax.rem(z + length - 1, length), x)]


def rows_loop(rows, body, start=0, unroll=2):
    @pl.loop(start // 16, (start + rows) // 16, unroll=unroll)
    def _(i):
        body(pl.ds(pl.multiple_of(i * 16, 16), 16))


def turned_tiles(length, pair):
    _, _, z, _ = place()
    for k in range(length):
        for b in range(4):
            yield k * 4 + b, pl.multiple_of((b * length + lax.rem(z + k, length)) * pair, pair)


def load_turned(ref, at, length, pair):
    if pair % 128:
        return ref[at]
    return jnp.concatenate([ref[at, pl.ds(src, pair)] for _, src in turned_tiles(length, pair)], axis=1)


def store_turned(ref, at, value, length, pair):
    if pair % 128:
        ref[at] = value
        return
    for n, dst in turned_tiles(length, pair):
        ref[at, pl.ds(dst, pair)] = value[:, n * pair : (n + 1) * pair]


def inverse_rms(v):
    return lax.rsqrt(jnp.sum(v * v, axis=-1, keepdims=True) * (1.0 / v.shape[-1]) + norm_eps)


def norm_rows_back(v, gain, grad):
    inverse = inverse_rms(v)
    scaled = v * inverse
    moved = grad * gain
    inner = jnp.sum(moved * scaled, axis=-1, keepdims=True) * (1.0 / v.shape[-1])
    return inverse * (moved - scaled * inner), fold(grad * scaled)


def middle_kernel(length, p, inputs, gains, w_in, residual, normed_o, w, *scratch):
    scatter_refs, (low, loc, gs, gr, hs, hr) = scratch[:SCATTER_REFS], scratch[SCATTER_REFS:]
    greet(gather_peers() + line_neighbours(length))
    hops = LineGather(w, length, hs, hr)
    hops.start(1)
    started = [1]

    def advance():
        if started[0] < length - 1:
            hops.arrive(started[0])
            started[0] += 1
            hops.start(started[0])

    def body(at):
        v = inputs[at].astype(F32) + residual[at]
        residual[at] = v
        low[at] = (v * inverse_rms(v) * gains[1:2]).astype(BF16)

    half = low.shape[0] // 2
    gather = Gather(low, normed_o, loc, gs, gr)
    for name in scatter_steps(p, residual, *scatter_refs):
        if name == "low half":
            rows_loop(half, body)
            gather.begin_half(0)
        if name == "high half":
            rows_loop(half, body, half)
            gather.begin_half(1)
            advance()
    gather.middle()
    gather.end(advance)
    while started[0] < length - 1:
        advance()
    hops.arrive(length - 1)
    hops.finish()


def middle(p, inputs, gains, w, length, collective_id):
    rows, width = inputs.shape
    return pl.pallas_call(
        functools.partial(middle_kernel, length),
        out_shape=(
            jax.ShapeDtypeStruct((rows, width), F32),
            jax.ShapeDtypeStruct((8, rows, width), BF16),
            jax.ShapeDtypeStruct(w.shape, w.dtype),
        ),
        in_specs=[ANY, VM, VM, ANY],
        out_specs=(VM, ANY, ANY),
        scratch_shapes=scatter_scratch(rows // 2, width)
        + [pltpu.VMEM((rows, width), BF16), DMA, DMA((14,)), DMA((14,)), DMA((2, length)), DMA((2, length))],
        input_output_aliases={3: 2},
        compiler_params=params(collective_id, 40 * 2**20),
        cost_estimate=pl.CostEstimate(flops=0, bytes_accessed=300 * 2**20, transcendentals=0),
    )(p.reshape(8, rows, width), inputs, gains, w)


def turn_kernel(length, cuts, p, residual, above, gains, *refs):
    parts = 1 + max(cut[0] for cut in cuts)
    terms, refs = refs[:parts], refs[parts:]
    back, gain, low_o, sums, squares, *scratch = refs
    scatter_refs, (total, low, loc, gs, gr), line_refs = (
        scratch[:SCATTER_REFS], scratch[SCATTER_REFS : SCATTER_REFS + 5], scratch[SCATTER_REFS + 5 :]
    )
    greet(gather_peers() + line_neighbours(length))
    line = Lines(terms, cuts, length, line_refs)
    line.begin()
    gain[...] = jnp.zeros_like(gain)

    def body(at):
        grad, gain_part = norm_rows_back(residual[at], gains[1:2], total[at])
        grad = above[at].astype(F32) + grad
        back[at] = grad
        low[at] = grad.astype(BF16)
        gain[...] += gain_part

    half = low.shape[0] // 2
    gather = Gather(low, low_o, loc, gs, gr)
    for name in scatter_steps(p, total, *scatter_refs):
        if name in ("early", "late"):
            line.start()
        if name == "low half":
            rows_loop(half, body)
            gather.begin_half(0)
        if name == "high half":
            rows_loop(half, body, half)
            gather.begin_half(1)
            line.start()
    gather.middle()
    line.start()
    gather.end()
    line.end(sums, squares)


def turn(p, residual, above, gains, terms, cuts, length, collective_id):
    rows, width = residual.shape
    line_rows, columns = terms[0].shape[1], sum(cut[2] for cut in cuts)
    return pl.pallas_call(
        functools.partial(turn_kernel, length, cuts),
        out_shape=(
            jax.ShapeDtypeStruct((rows, width), F32),
            jax.ShapeDtypeStruct((8, width), F32),
            jax.ShapeDtypeStruct((8, rows, width), BF16),
            jax.ShapeDtypeStruct((line_rows, columns), BF16),
            TILE,
        ),
        in_specs=[ANY, VM, VM, VM] + [ANY] * len(terms),
        out_specs=(VM, VM, ANY, VM, VM),
        scratch_shapes=scatter_scratch(rows // 2, width)
        + [pltpu.VMEM((rows, width), F32), pltpu.VMEM((rows, width), BF16), DMA, DMA((14,)), DMA((14,))]
        + lines_scratch(length, line_rows, cuts),
        compiler_params=params(collective_id, 56 * 2**20),
        cost_estimate=pl.CostEstimate(flops=0, bytes_accessed=300 * 2**20, transcendentals=0),
    )(p.reshape(8, rows, width), residual, above, gains, *terms)


def closing_kernel(
    length, cut, part, x_in, dmz_in, dproj, mixed, first_w, q, residual, terms, block,
    o, out, e_o, sums, squares,
    x_part, dmz_part, g, back, total, up_got, down_got, ls, lr, load_s, free, loc, es, er, *scratch,
):
    scatter_refs, line_refs = scratch[:SCATTER_REFS], scratch[SCATTER_REFS:]
    greet(plane_peers() + line_neighbours(length))
    model, rc = first_w.shape[0], mixed.shape[1]
    tokens = dproj.shape[0]
    columns = x_part.shape[2]
    steps = model // columns
    rows = tokens // steps
    line_rows = g.shape[1]

    def loads(i, slot):
        at = pl.ds(pl.multiple_of(i * columns, columns), columns)
        return (
            pltpu.make_async_copy(x_in.at[:, at], x_part.at[slot], load_s.at[0, slot]),
            pltpu.make_async_copy(dmz_in.at[:, at], dmz_part.at[slot], load_s.at[1, slot]),
        )

    group = steps // 4
    order = (3, 1, 2, 0)

    def fetch(i, slot):
        for copy in loads(i, slot):
            copy.start()

    fetch(order[0] * group, 0)
    rest = LineScatter([(terms, *cut)], length, *line_refs)
    rest.load((1,))
    rest.start()
    rest.load((*range(2, length), 0))
    line = HeldLine(g, up_got, down_got, ls, lr)
    output = scatter_steps(q, total, *scatter_refs)
    next(output)
    copies, own = exchange_steps(block, e_o, loc, es, er)

    def compute(n):
        @pl.loop(0, group)
        def _(j):
            count = n * group + j
            slot = count - count // 2 * 2
            i = order[n] * group + j

            @pl.when(j + 1 < group)
            def _():
                fetch(i + 1, 1 - slot)

            if n < 3:

                @pl.when(j + 1 == group)
                def _():
                    fetch(order[n + 1] * group, 1 - slot)

            for copy in loads(i, slot):
                copy.wait()
            front = contract_first(x_part[slot], dproj[...])
            tail = contract_first(dmz_part[slot], mixed[...])
            k = i * columns // line_rows
            at = pl.ds(pl.multiple_of(i * columns - k * line_rows, columns), columns)
            g[k, at] = jnp.concatenate(
                [front[:, :part], front[:, rc : rc + part], tail[:, :part]], axis=1
            ).astype(BF16)
            block_of = i * rows // 256
            at = pl.ds(pl.multiple_of(i * rows - block_of * 256, rows), rows)
            mine = dproj[pl.ds(pl.multiple_of(i * rows, rows), rows)]
            for first_column in range(0, model, 512):
                cols = slice(first_column, first_column + 512)
                back[block_of, at, cols] = contract_last(mine, first_w[cols]).astype(BF16)

    compute(0)
    next(output)
    compute(1)
    if length == 4:
        line.start()
    next(output)
    rest.start()
    compute(2)
    next(output)
    compute(3)
    if length != 4:
        line.start()
    while rest.next < length:
        rest.start()
    for _ in output:
        pass
    for peer in gather_peers():
        pl.semaphore_signal(free, inc=1, device_id=peer, device_id_type=MESH)
    line.start()
    pl.semaphore_wait(free, 3)
    incoming = scatter_steps(back, o, *scatter_refs)
    next(incoming)
    pair = out.shape[1] // (4 * length)

    def body(at):
        store_turned(out, at, (residual[at] + total[at]).astype(BF16), length, pair)

    rows_loop(out.shape[0], body)
    squares[...] = jnp.zeros_like(squares)
    rest.end(sums, 0, squares)
    for name in incoming:
        if name == "early" and line.next < length:
            line.start()
    while line.next < length:
        line.start()
    line.end(sums, cut[1], squares)
    for copy in copies:
        copy.wait()
    own.wait()


def closing(x, dmz, dproj, mixed, first_w, q, residual, terms, cut, block, part, length, collective_id):
    rows, width = residual.shape
    tokens, model = x.shape
    share = block.shape[0] // 8
    block = block.reshape(8, share, block.shape[1])
    line_rows = terms.shape[1]
    columns = min(256, line_rows)
    held = pltpu.VMEM((length - 1, line_rows, 3 * part), BF16)
    return pl.pallas_call(
        functools.partial(closing_kernel, length, cut, part),
        out_shape=(
            jax.ShapeDtypeStruct((rows, width), F32),
            jax.ShapeDtypeStruct((rows, width), BF16),
            jax.ShapeDtypeStruct(block.shape, BF16),
            jax.ShapeDtypeStruct((line_rows, cut[1] + 3 * part), BF16),
            TILE,
        ),
        in_specs=[ANY, ANY, VM, VM, VM, ANY, VM, ANY, ANY],
        out_specs=(VM, VM, ANY, VM, VM),
        scratch_shapes=[
            pltpu.VMEM((2, tokens, columns), BF16),
            pltpu.VMEM((2, tokens, columns), BF16),
            pltpu.VMEM((length, line_rows, 3 * part), BF16),
            pltpu.VMEM((8, rows, width), BF16),
            pltpu.VMEM((rows, width), F32),
            held, held,
            DMA((2, length)), DMA((2, length)), DMA((2, 2)), pltpu.SemaphoreType.REGULAR,
            DMA, DMA((7,)), DMA((7,)),
        ]
        + scatter_scratch(rows // 2, width)
        + line_scratch(length, line_rows, cut[1], 1),
        compiler_params=params(collective_id, 63 * 2**20),
        cost_estimate=pl.CostEstimate(
            flops=10 * tokens * model * dproj.shape[1] // 2, bytes_accessed=350 * 2**20, transcendentals=0
        ),
    )(x, dmz, dproj, mixed, first_w, q.reshape(8, rows, width), residual, terms, block)


def first_kernel(
    length, inputs, above, mixer_w, mlp_w, gains_w, gate_w, chan_w,
    normed_o, wm_o, wf_o, wd_o, gains_o, gp_o, inputs_o, above_o,
    gn, gp, normed, gn_all, wm, wf, wd, loc, ms, mr, fs, fr, line_s, line_r, gain_s, gain_r, move_s, move_r,
    gather_s, gather_r, hop_s, hop_r,
):
    y, c, z, x = place()
    s = 2 * z + x
    me = rank(y, c, x)
    rows, width = inputs.shape
    pair = width // (4 * length)
    line = line_peers(length)
    plane = plane_peers()
    to_z, to_x = lax.rem(s, length), s // length
    moves = jnp.where(jnp.logical_and(to_z == z, to_x == x), 0, 1)
    src = x * length + z
    from_z = src // 2
    from_x = src - 2 * from_z
    barrier = pltpu.get_barrier_semaphore()
    for peer in line + plane:
        pl.semaphore_signal(barrier, inc=1, device_id=peer, device_id_type=MESH)

    @pl.when(moves == 1)
    def _():
        pl.semaphore_signal(barrier, inc=1, device_id=device(y, c, to_z, to_x), device_id_type=MESH)
        pl.semaphore_signal(barrier, inc=1, device_id=device(y, c, from_z, from_x), device_id_type=MESH)

    pl.semaphore_wait(barrier, len(line) + len(plane) + 2 * moves)

    share = gains_w.shape[1]
    gn[...] = jnp.zeros_like(gn)
    for n in (0, 1):

        @pl.when(x == n)
        def _():
            gn[:2, n * share : (n + 1) * share] = gains_w[...]

    gp[...] = jnp.zeros_like(gp)
    channels = contract_first(chan_w[...].astype(BF16), unit(8))
    gp[: gate_w.shape[0]] = jnp.concatenate(
        [
            gate_w[...],
            channels,
            jnp.zeros((gate_w.shape[0], gp.shape[1] - gate_w.shape[1] - 8), F32),
        ],
        axis=1,
    ).astype(BF16)
    gn_all[me, z] = gn[...]
    gains = [
        remote(gn, gn_all.at[me, z], line_s.at[0, k], line_r.at[0, k], line[k]) for k in range(length - 1)
    ]
    gate_move = pltpu.make_async_remote_copy(
        src_ref=gp, dst_ref=gp_o.at[to_z], send_sem=move_s, recv_sem=move_r,
        device_id=device(y, c, to_z, to_x), device_id_type=MESH,
    )
    gate_stay = pltpu.make_async_copy(gp, gp_o.at[z], loc.at[2])
    pl.when(moves == 1)(lambda: gate_move.start())
    pl.when(moves == 0)(lambda: gate_stay.start())

    def fill(pack, source, js):
        part = pack.shape[2] // len(js)
        for t in range(8):
            for n, j in enumerate(js):
                start = (j * 8 + t) * part
                pack[t, :, n * part : (n + 1) * part] = source[:, start : start + part].astype(BF16)

    fill(wm, mixer_w, (0, 1, 2))
    mixer, mixer_own = exchange_steps(wm, wm_o.at[0], loc.at[0], ms, mr)
    for copy in gains:
        copy.wait()
    spread = [
        remote(gn_all.at[me], gn_all.at[me], gain_s.at[n], gain_r.at[n], plane[n]) for n in range(7)
    ]
    pl.when(moves == 1)(lambda: gate_move.wait())
    pl.when(moves == 0)(lambda: gate_stay.wait())
    gates = [
        remote(gp_o.at[z], gp_o.at[z], line_s.at[1, k], line_r.at[1, k], line[k])
        for k in range(length - 1)
    ]
    fill(wd, mlp_w, (2,))
    down, down_own = exchange_steps(wd, wd_o.at[0], loc.at[4], fs.at[1], fr.at[1])
    fill(wf, mlp_w, (0, 1))
    feed, feed_own = exchange_steps(wf, wf_o.at[0], loc.at[3], fs.at[0], fr.at[0])
    for copy in spread:
        copy.wait()
    for k in range(length):
        other = lax.rem(z + k, length)
        for b in range(4):
            at = slice((4 * k + b) * pair, (4 * k + b + 1) * pair)
            tile = (gn_all[2 * b, other] + gn_all[2 * b + 1, other])[:, :pair]
            gains_o[:, at] = tile.astype(BF16).astype(F32)
    for copy in mixer:
        copy.wait()
    mixer_own.wait()
    hops = LineGather(wm_o, length, hop_s, hop_r)
    hops.start(1)

    def body(at):
        v = load_turned(inputs, at, length, pair)
        inputs_o[at] = v
        v = v.astype(F32)
        normed[at] = (v * inverse_rms(v) * gains_o[0:1]).astype(BF16)
        above_o[at] = load_turned(above, at, length, pair)

    half = rows // 2
    gather = Gather(normed, normed_o, loc.at[1], gather_s, gather_r)
    rows_loop(half, body)
    gather.begin_half(0)
    rows_loop(half, body, half)
    gather.begin_half(1)
    hops.arrive(1)
    if length > 2:
        hops.start(2)
    gather.middle()
    if length > 3:
        hops.arrive(2)
        hops.start(3)
    gather.relays()
    for hop in range(min(3, length - 1), length):
        hops.arrive(hop)
        if hop + 1 < length:
            hops.start(hop + 1)
    gather.finish()
    for copy in down + feed + gates:
        copy.wait()
    down_own.wait()
    feed_own.wait()
    hops.finish()


def unit(n):
    return (
        lax.broadcasted_iota(jnp.int32, (n, n), 0) == lax.broadcasted_iota(jnp.int32, (n, n), 1)
    ).astype(BF16)


def first(inputs, above, mixer, mlp, gains, gate, chan, rc, length, collective_id):
    rows, width = inputs.shape
    pack = (-(-gate.shape[0] // 16) * 16, rc)
    share = mixer.shape[0]
    wm, wf, wd = ((8, share, n) for n in (mixer.shape[1] // 8, mlp.shape[1] // 12, mlp.shape[1] // 24))
    low = jax.ShapeDtypeStruct((rows, width), BF16)
    return pl.pallas_call(
        functools.partial(first_kernel, length),
        out_shape=(
            jax.ShapeDtypeStruct((8, rows, width), BF16),
            jax.ShapeDtypeStruct((length,) + wm, BF16),
            jax.ShapeDtypeStruct((length,) + wf, BF16),
            jax.ShapeDtypeStruct((length,) + wd, BF16),
            jax.ShapeDtypeStruct((8, width), F32),
            jax.ShapeDtypeStruct((length,) + pack, BF16),
            low,
            low,
        ),
        in_specs=[VM] * 7,
        out_specs=(ANY, ANY, ANY, ANY, VM, ANY, VM, VM),
        scratch_shapes=[
            pltpu.VMEM((8, 128), F32),
            pltpu.VMEM(pack, BF16),
            pltpu.VMEM((rows, width), BF16),
            pltpu.VMEM((8, length, 8, 128), F32),
            pltpu.VMEM(wm, BF16),
            pltpu.VMEM(wf, BF16),
            pltpu.VMEM(wd, BF16),
            DMA((5,)), DMA((7,)), DMA((7,)), DMA((2, 7)), DMA((2, 7)),
            DMA((2, length)), DMA((2, length)), DMA((7,)), DMA((7,)), DMA, DMA,
            DMA((14,)), DMA((14,)), DMA((2, length)), DMA((2, length)),
        ],
        compiler_params=params(collective_id, 40 * 2**20),
        cost_estimate=pl.CostEstimate(flops=0, bytes_accessed=300 * 2**20, transcendentals=0),
    )(inputs, above, mixer, mlp, gains, gate, chan)


def last_kernel(
    length, wm, total, inputs, back, gains, gain_two, gp, sq,
    gains_w, gains_m, gains_v, gate_w, gate_m, gate_v, chan_w, chan_m, chan_v,
    wm_o, grad_o, gains_mo, gains_vo, gains_wo, gate_mo, gate_vo, gate_wo, chan_mo, chan_vo, chan_wo,
    norm_o, factor_o,
    gain, row_sums, gn, gn_in, gn_mid, gn_got, gp_got, gp_sum, gp_fin, sq_plane, sq_line,
    loc, ss, rs, gs, gr, ls, lr, move_s, move_r,
):
    y, c, z, x = place()
    s = 2 * z + x
    me = rank(y, c, x)
    line = line_peers(length)
    plane = plane_peers()
    owner = x * length + z
    to_z = owner // 2
    to_x = owner - 2 * to_z
    from_z, from_x = lax.rem(s, length), s // length
    moves = jnp.where(jnp.logical_and(to_z == z, to_x == x), 0, 1)
    barrier = pltpu.get_barrier_semaphore()
    for peer in line + plane:
        pl.semaphore_signal(barrier, inc=1, device_id=peer, device_id_type=MESH)

    @pl.when(moves == 1)
    def _():
        pl.semaphore_signal(barrier, inc=1, device_id=device(y, c, to_z, to_x), device_id_type=MESH)
        pl.semaphore_signal(barrier, inc=1, device_id=device(y, c, from_z, from_x), device_id_type=MESH)

    pl.semaphore_wait(barrier, len(line) + len(plane) + 2 * moves)

    gate = [
        remote(gp.at[k + 1], gp_got.at[k], ls.at[0, k], lr.at[0, k], line[k]) for k in range(length - 1)
    ]
    rows, width = inputs.shape
    pair = width // (4 * length)
    gain[...] = jnp.zeros_like(gain)

    def body(at):
        grad, gain_part = norm_rows_back(inputs[at].astype(F32), gains[0:1], total[at])
        store_turned(grad_o, at, back[at] + grad, length, pair)
        gain[...] += gain_part

    rows_loop(rows, body)
    row = lax.broadcasted_iota(jnp.int32, (8, width), 0)
    ones = jnp.sum(gain[...], axis=0, keepdims=True)
    twos = jnp.sum(gain_two[...], axis=0, keepdims=True)
    row_sums[...] = jnp.where(row == 0, ones, jnp.where(row == 1, twos, 0.0))
    if pair < 128:
        gn[...] = jnp.zeros_like(gn)
    for k in range(length):
        for b in range(4):
            gn[b, k, :, :pair] = row_sums[:, (4 * k + b) * pair : (4 * k + b + 1) * pair]
    sends = []
    for n, (fy, fc, fx) in enumerate(FLIPS):
        to = flip(y, fy) * 2 + flip(c, fc)
        sends.append(remote(gn.at[to], gn_in.at[n], gs.at[0, n], gr.at[0, n], plane[n]))
    copies, own = exchange_steps(wm, wm_o, loc, ss, rs)
    for copy in gate:
        copy.wait()
    sums = gp[0]
    for k in range(length - 1):
        sums = sums + gp_got[k]
    gp_sum[...] = sums
    for copy in sends:
        copy.wait()
    sums = gn[2 * y + c]
    for n in range(7):
        sums = sums + gn_in[n]
    gn_mid[...] = sums
    sends = [
        remote(gn_mid.at[k + 1], gn_got.at[k], ls.at[1, k], lr.at[1, k], line[k])
        for k in range(length - 1)
    ]

    @pl.when(moves == 1)
    def _():
        copy = remote(gp_sum, gp_fin, move_s, move_r, device(y, c, to_z, to_x))
        copy.wait()

    @pl.when(moves == 0)
    def _():
        gp_fin[...] = gp_sum[...]

    for copy in sends:
        copy.wait()
    sums = gn_mid[0]
    for k in range(length - 1):
        sums = sums + gn_got[k]
    share = gains_w.shape[1]
    lane = lax.broadcasted_iota(jnp.int32, (8, 128), 1)
    mine = jnp.logical_and(lane >= x * share, lane < (x + 1) * share)
    gain_sum = jnp.where(mine, sums, 0.0)
    gate_sum = gp_fin[...]
    sq_plane[me] = sq[...] + gain_sum * gain_sum + tile_of_squares(gate_sum)
    sends = [
        remote(sq_plane.at[me], sq_plane.at[me], gs.at[1, n], gr.at[1, n], plane[n]) for n in range(7)
    ]
    for copy in sends:
        copy.wait()
    sums = sq_plane[0]
    for n in range(1, 8):
        sums = sums + sq_plane[n]
    sq_line[z] = sums
    sends = [
        remote(sq_line.at[z], sq_line.at[z], ls.at[2, k], lr.at[2, k], line[k])
        for k in range(length - 1)
    ]
    for copy in sends:
        copy.wait()
    sums = sq_line[0]
    for n in range(1, length):
        sums = sums + sq_line[n]
    sums = jnp.sum(jnp.sum(sums, axis=0, keepdims=True), axis=1, keepdims=True)
    norm = jnp.broadcast_to(jnp.sqrt(sums), (8, 128))
    factor = clip_limit / jnp.maximum(norm, clip_limit)
    norm_o[...] = norm
    factor_o[...] = factor
    gain_own = jnp.where(x == 0, gain_sum[:2, :share], gain_sum[:2, share : 2 * share])
    one = factor[0:1, 0:1]
    gains_mo[...], gains_vo[...], gains_wo[...] = adam_step(
        gains_w[...], gain_own, gains_m[...], gains_v[...], one, rate_gains, 0.0
    )
    gate_rows, columns = gate_w.shape
    gate_mo[...], gate_vo[...], gate_wo[...] = adam_step(
        gate_w[...], gate_sum[:gate_rows, :columns], gate_m[...], gate_v[...], one, rate_matrix, decay_matrix
    )
    channels = lax.dot_general(
        unit(8).astype(F32), gate_sum[:gate_rows, columns : columns + 8], (((1,), (1,)), ((), ())),
        precision=lax.Precision.HIGHEST, preferred_element_type=F32,
    )
    chan_mo[...], chan_vo[...], chan_wo[...] = adam_step(
        chan_w[...], channels, chan_m[...], chan_v[...], one, rate_channel, 0.0
    )
    for copy in copies:
        copy.wait()
    own.wait()


def last(wm, total, inputs, back, gains, gain_two, gp, sq, small, length, collective_id):
    rows, width = inputs.shape
    states = [jax.ShapeDtypeStruct(v.shape, F32) for v in small]
    return pl.pallas_call(
        functools.partial(last_kernel, length),
        out_shape=(
            jax.ShapeDtypeStruct(wm.shape, wm.dtype),
            jax.ShapeDtypeStruct((rows, width), F32),
            *states, TILE, TILE,
        ),
        in_specs=[ANY] + [VM] * 16,
        out_specs=(ANY,) + (VM,) * 12,
        scratch_shapes=[
            pltpu.VMEM((8, width), F32),
            pltpu.VMEM((8, width), F32),
            pltpu.VMEM((4, length, 8, 128), F32),
            pltpu.VMEM((7, length, 8, 128), F32),
            pltpu.VMEM((length, 8, 128), F32),
            pltpu.VMEM((length, 8, 128), F32),
            pltpu.VMEM(gp.shape, F32),
            pltpu.VMEM(gp.shape[1:], F32),
            pltpu.VMEM(gp.shape[1:], F32),
            pltpu.VMEM((8, 8, 128), F32),
            pltpu.VMEM((length, 8, 128), F32),
            DMA, DMA((7,)), DMA((7,)), DMA((2, 7)), DMA((2, 7)),
            DMA((3, length)), DMA((3, length)), DMA, DMA,
        ],
        compiler_params=params(collective_id, 32 * 2**20),
    )(wm, total, inputs, back, gains, gain_two, gp, sq, *small)


def minus_expm1(v):
    series = 1.0 + v * (1.0 / 8.0)
    for n in (7.0, 6.0, 5.0, 4.0, 3.0, 2.0):
        series = 1.0 + series * v * (1.0 / n)
    return jnp.where(v > -0.5, -v * series, 1.0 - jnp.exp(v))


def gelu_parts(v):
    inner = jnp.tanh(GELU_SCALE * (v + 0.044715 * v * v * v))
    return 0.5 * v * (1.0 + inner), inner


def gelu_slope(v, inner):
    return 0.5 * (1.0 + inner) + 0.5 * v * (1.0 - inner * inner) * GELU_SCALE * (
        1.0 + 3.0 * 0.044715 * v * v
    )


CHUNK = 64


def forward_kernel(
    length, proj, gate, chan, above, w_in, mixed, decay_o, width_o, recur_o, enter_o, conv_o, xe, se, ends_o, above_o, w,
    pre, loc_h, ends, carry, hs, hr, es, er, gather_l, gather_s, gather_r, hop_s, hop_r,
    keep_s, *kept,
):
    keeps = [
        pltpu.make_async_copy(src, dst, keep_s.at[n])
        for n, (src, dst) in enumerate(
            zip(kept, (decay_o, width_o, recur_o, enter_o, conv_o, xe, se))
        )
    ]
    decay_o, width_o, recur_o, enter_o, conv_o, xe, se = kept
    y, c, z, x = place()
    line = line_peers(length)
    greet(line + gather_peers())
    seqs, span, rc = mixed.shape
    chunks = span // CHUNK
    gather = Gather(above, above_o, gather_l, gather_s, gather_r)
    ahead = device(y, c, lax.rem(z + 1, length), x)
    for b in range(seqs):
        xe[b, span : span + 8] = proj[b, span - 8 : span, rc:].astype(BF16).astype(F32)
    halo = remote(xe.at[:, pl.ds(span, 8)], xe.at[:, pl.ds(0, 8)], hs, hr, ahead)
    halo.wait_send()
    hops = LineGather(w, length, hop_s, hop_r)
    hops.start(1)
    gather.begin()

    @pl.loop(0, seqs * chunks)
    def _(i):
        b = i // chunks
        r = pl.multiple_of((i - b * chunks) * CHUNK, CHUNK)
        xe[b, pl.ds(r + 8, CHUNK)] = proj[b, pl.ds(r, CHUNK), rc:].astype(BF16).astype(F32)

    halo.wait_recv()

    @pl.when(z == 0)
    def _():
        xe[:, 0:8] = jnp.zeros((seqs, 8, rc), F32)

    def coefficients(i):
        b = i // chunks
        r = pl.multiple_of((i - b * chunks) * CHUNK, CHUNK)
        at = pl.ds(r, CHUNK)
        window = xe[b, pl.ds(r, CHUNK + 8)]
        total = chan[4:5] + chan[0:1] * window[8:]
        for k in (1, 2, 3):
            total = total + chan[k : k + 1] * pltpu.roll(window, k, 0)[8:]
        low = total.astype(BF16)
        conv_o[b, at] = low
        value = low.astype(F32)
        gates = jnp.dot(low, gate[...], preferred_element_type=F32)
        recur = jax.nn.sigmoid(gates[:, :rc] + chan[5:6])
        enter = jax.nn.sigmoid(gates[:, rc:] + chan[6:7])
        log_decay = -chan[7:8] * recur
        decay = jnp.exp(log_decay)
        width = jnp.sqrt(minus_expm1(2.0 * log_decay))
        recur_o[b, at] = recur
        enter_o[b, at] = enter
        decay_o[b, at] = decay
        width_o[b, at] = width
        loc_h[b, at] = width * enter * value

    half = seqs * chunks // 2
    pl.loop(0, half)(coefficients)
    hops.arrive(1)
    if length > 2:
        hops.start(2)
    pl.loop(half, seqs * chunks)(coefficients)
    for copy in keeps[:-1]:
        copy.start()
    row = lax.broadcasted_iota(jnp.int32, (8, rc), 0)

    def tile(i, held):
        at = pl.ds(pl.multiple_of(i * 8, 8), 8)
        new = []
        for b in range(seqs):
            a, h = decay_o[b, at], loc_h[b, at]
            for n in (1, 2, 4):
                keep = row >= n
                h = h + jnp.where(keep, a * pltpu.roll(h, n, 0), 0.0)
                a = jnp.where(keep, a * pltpu.roll(a, n, 0), a)
            h = h + a * held[b][1]
            a = a * held[b][0]
            loc_h[b, at] = h
            pre[b, at] = a
            new.append((a[7:8], h[7:8]))
        return tuple(new)

    one, zero = jnp.ones((1, rc), F32), jnp.zeros((1, rc), F32)
    final = lax.fori_loop(0, span // 8, tile, ((one, zero),) * seqs)
    for b in range(seqs):
        ends[z, 0, b] = jnp.broadcast_to(final[b][0], (8, rc))
        ends[z, 1, b] = jnp.broadcast_to(final[b][1], (8, rc))
        ends_o[b] = jnp.broadcast_to(final[b][0], (8, rc))
    moves = [remote(ends.at[z], ends.at[z], es.at[k], er.at[k], line[k]) for k in range(length - 1)]
    for copy in moves:
        copy.wait()
    if length > 3:
        hops.arrive(2)
        hops.start(3)
    gather.middle()
    carry[...] = jnp.zeros_like(carry)
    for k in range(length):
        carry[...] = jnp.where(k < z, ends[k, 0] * carry[...] + ends[k, 1], carry[...])

    for b in range(seqs):
        se[b, 0:8] = carry[b]

    @pl.loop(0, seqs * chunks)
    def _(i):
        b = i // chunks
        r = pl.multiple_of((i - b * chunks) * CHUNK, CHUNK)
        at = pl.ds(r, CHUNK)
        state = loc_h[b, at] + pre[b, at] * carry[b, 0:1]
        se[b, pl.ds(r + 8, CHUNK)] = state
        gelu, _ = gelu_parts(proj[b, at, :rc])
        mixed[b, at] = (state * gelu).astype(BF16)

    keeps[-1].start()
    gather.end()
    for hop in range(min(3, length - 1), length):
        hops.arrive(hop)
        if hop + 1 < length:
            hops.start(hop + 1)
    hops.finish()
    for copy in keeps:
        copy.wait()


def recur_forward(proj, gate, chan, above, w, length, collective_id):
    seqs, span, rc = proj.shape[0], proj.shape[1], proj.shape[2] // 2
    full = jax.ShapeDtypeStruct((seqs, span, rc), F32)
    longer = jax.ShapeDtypeStruct((seqs, span + 8, rc), F32)
    low = jax.ShapeDtypeStruct((seqs, span, rc), BF16)
    return pl.pallas_call(
        functools.partial(forward_kernel, length),
        out_shape=(
            low, full, full, full, full, low, longer, longer,
            jax.ShapeDtypeStruct((seqs, 8, rc), F32),
            jax.ShapeDtypeStruct((8,) + above.shape, above.dtype),
            jax.ShapeDtypeStruct(w.shape, w.dtype),
        ),
        in_specs=[VM, VM, VM, ANY, ANY],
        out_specs=(VM,) + (ANY,) * 7 + (VM, ANY, ANY),
        scratch_shapes=[
            pltpu.VMEM((seqs, span, rc), F32),
            pltpu.VMEM((seqs, span, rc), F32),
            pltpu.VMEM((length, 2, seqs, 8, rc), F32),
            pltpu.VMEM((seqs, 8, rc), F32),
            DMA, DMA, DMA((length,)), DMA((length,)),
            DMA, DMA((14,)), DMA((14,)), DMA((2, length)), DMA((2, length)),
            DMA((7,)),
            *[pltpu.VMEM(v.shape, v.dtype) for v in (full, full, full, full, low, longer, longer)],
        ],
        input_output_aliases={4: 10},
        compiler_params=params(collective_id, 56 * 2**20),
        cost_estimate=pl.CostEstimate(
            flops=2 * seqs * span * rc * rc * 2, bytes_accessed=100 * 2**20, transcendentals=0
        ),
    )(proj, gate, chan, above, w)


def backward_kernel(
    length, cuts, dmix, gate, chan, decay, width, recur, enter, conv, xe, se, ends_f, proj, block, *refs
):
    parts = 1 + max(cut[0] for cut in cuts)
    terms, refs = refs[:parts], refs[parts:]
    dproj, dgate, gchan, sums, squares, block_o, *refs = refs
    suffix, grad, de, ends, carry, hs, hr, es, er, keep_s, move_l, move_s, move_r, *refs = refs
    kept, line_refs = refs[:8], refs[8:]
    loads = [
        pltpu.make_async_copy(src, dst, keep_s.at[n])
        for n, (src, dst) in enumerate(
            zip((dmix, proj.at[:, :, pl.ds(0, decay.shape[2])], se, decay, width, recur, enter, conv, xe), (de.at[:, pl.ds(0, decay.shape[1])], *kept))
        )
    ]
    proj, se, decay, width, recur, enter, conv, xe = kept
    y, c, z, x = place()
    line = line_peers(length)
    greet(line + plane_peers())
    scatter = Lines(terms, cuts, length, line_refs)
    scatter.begin()
    for copy in loads:
        copy.start()
    moves, own = exchange_steps(block, block_o, move_l, move_s, move_r)
    seqs, span, rc = decay.shape
    chunks = span // CHUNK
    for copy in loads[:3]:
        copy.wait()

    @pl.loop(0, seqs * chunks)
    def _(i):
        b = i // chunks
        r = pl.multiple_of((i - b * chunks) * CHUNK, CHUNK)
        at = pl.ds(r, CHUNK)
        branch = proj[b, at]
        gelu, inner = gelu_parts(branch)
        above = de[b, at]
        state = se[b, pl.ds(r + 8, CHUNK)]
        grad[b, at] = above * gelu
        dproj[b, at, :rc] = (above * state * gelu_slope(branch, inner)).astype(BF16)

    loads[3].wait()
    row = lax.broadcasted_iota(jnp.int32, (8, rc), 0)

    def tile(i, held):
        at = pl.ds(pl.multiple_of(span - 8 - i * 8, 8), 8)
        new = []
        for b in range(seqs):
            product, total, following = held[b]
            plain, h = decay[b, at], grad[b, at]
            a = jnp.where(row == 7, following, pltpu.roll(plain, 7, 0))
            for n in (1, 2, 4):
                keep = row < 8 - n
                h = h + jnp.where(keep, a * pltpu.roll(h, 8 - n, 0), 0.0)
                a = jnp.where(keep, a * pltpu.roll(a, 8 - n, 0), a)
            h = h + a * total
            a = a * product
            grad[b, at] = h
            suffix[b, at] = a
            new.append((a[0:1], h[0:1], plain[0:1]))
        return tuple(new)

    one, zero = jnp.ones((1, rc), F32), jnp.zeros((1, rc), F32)
    final = lax.fori_loop(0, span // 8, tile, ((one, zero, one),) * seqs)
    for b in range(seqs):
        ends[z, 0, b] = ends_f[b]
        ends[z, 1, b] = jnp.broadcast_to(final[b][1] * final[b][2], (8, rc))
    tails = [remote(ends.at[z], ends.at[z], es.at[k], er.at[k], line[k]) for k in range(length - 1)]
    for copy in tails:
        copy.wait()
    scatter.start()
    scatter.start()
    for copy in loads[4:]:
        copy.wait()
    carry[...] = jnp.zeros_like(carry)
    for k in reversed(range(length)):
        carry[...] = jnp.where(k > z, ends[k, 0] * carry[...] + ends[k, 1], carry[...])

    gchan[...] = jnp.zeros_like(gchan)

    @pl.loop(0, seqs * chunks)
    def _(i):
        b = i // chunks
        r = pl.multiple_of((i - b * chunks) * CHUNK, CHUNK)
        at = pl.ds(r, CHUNK)
        g = grad[b, at] + suffix[b, at] * carry[b, 0:1]
        a, w, ra, ri = decay[b, at], width[b, at], recur[b, at], enter[b, at]
        value = conv[b, at].astype(F32)
        before = pltpu.roll(se[b, pl.ds(r, CHUNK + 8)], 1, 0)[8:]
        dla = g * before * a - g * ri * value * (a * a) / w
        slope = dla * ra * (1.0 - ra)
        dpa = (-chan[7:8] * slope).astype(BF16)
        dpi = (g * w * value * ri * (1.0 - ri)).astype(BF16)
        dgate[b, at, :rc] = dpa
        dgate[b, at, rc:] = dpi
        gchan[5] += fold(dpa.astype(F32))
        gchan[6] += fold(dpi.astype(F32))
        gchan[7] += fold(dla * ra)
        back = lax.dot_general(
            dgate[b, at], gate[...], (((1,), (1,)), ((), ())), preferred_element_type=F32
        )
        dcv = (g * w * ri + back).astype(BF16).astype(F32)
        de[b, at] = dcv
        gchan[4] += fold(dcv)

    behind = device(y, c, lax.rem(z + length - 1, length), x)
    halo = remote(de.at[:, pl.ds(0, 8)], de.at[:, pl.ds(span, 8)], hs, hr, behind)
    halo.wait()
    scatter.start()
    scatter.start()

    @pl.when(z == length - 1)
    def _():
        de[:, span:] = jnp.zeros((seqs, 8, rc), F32)

    @pl.loop(0, seqs * chunks)
    def _(i):
        b = i // chunks
        r = pl.multiple_of((i - b * chunks) * CHUNK, CHUNK)
        at = pl.ds(r, CHUNK)
        window = de[b, pl.ds(r, CHUNK + 8)]
        inputs = xe[b, pl.ds(r, CHUNK + 8)]
        dcv = window[:CHUNK]
        total = chan[0:1] * dcv
        gchan[0] += fold(dcv * inputs[8:])
        for k in (1, 2, 3):
            total = total + chan[k : k + 1] * pltpu.roll(window, CHUNK + 8 - k, 0)[:CHUNK]
            gchan[k] += fold(dcv * pltpu.roll(inputs, k, 0)[8:])
        dproj[b, at, rc:] = total.astype(BF16)

    scatter.end(sums, squares)
    for copy in moves:
        copy.wait()
    own.wait()


def recur_backward(dmix, gate, chan, kept, proj, block, terms, cuts, length, collective_id):
    decay, width, recur, enter, conv, xe, se, ends = kept
    seqs, span, rc = decay.shape
    wide = jax.ShapeDtypeStruct((seqs, span, 2 * rc), BF16)
    line_rows, columns = terms[0].shape[1], sum(cut[2] for cut in cuts)
    return pl.pallas_call(
        functools.partial(backward_kernel, length, cuts),
        out_shape=(
            wide, wide, jax.ShapeDtypeStruct((8, 8, rc), F32),
            jax.ShapeDtypeStruct((line_rows, columns), BF16), TILE,
            jax.ShapeDtypeStruct(block.shape, BF16),
        ),
        in_specs=[ANY, VM, VM] + [ANY] * 7 + [VM] + [ANY] * (2 + len(terms)),
        out_specs=(VM,) * 5 + (ANY,),
        scratch_shapes=[
            pltpu.VMEM((seqs, span, rc), F32),
            pltpu.VMEM((seqs, span, rc), F32),
            pltpu.VMEM((seqs, span + 8, rc), F32),
            pltpu.VMEM((length, 2, seqs, 8, rc), F32),
            pltpu.VMEM((seqs, 8, rc), F32),
            DMA, DMA, DMA((length,)), DMA((length,)),
            DMA((9,)), DMA, DMA((7,)), DMA((7,)),
            *[
                pltpu.VMEM(shape, dtype)
                for shape, dtype in (
                    (decay.shape, F32), (se.shape, F32), (decay.shape, F32), (decay.shape, F32),
                    (decay.shape, F32), (decay.shape, F32), (decay.shape, BF16), (xe.shape, F32),
                )
            ],
        ]
        + lines_scratch(length, line_rows, cuts),
        compiler_params=params(collective_id, 62 * 2**20),
        cost_estimate=pl.CostEstimate(
            flops=2 * seqs * span * rc * rc * 2, bytes_accessed=120 * 2**20, transcendentals=0
        ),
    )(dmix, gate, chan, decay, width, recur, enter, conv, xe, se, ends, proj, block, *terms)


def contract_last(left, right):
    return lax.dot_general(
        left, right, (((1,), (1,)), ((), ())), preferred_element_type=F32
    )


def contract_first(left, right):
    return lax.dot_general(
        left, right, (((0,), (0,)), ((), ())), preferred_element_type=F32
    )


def resident(shape):
    return pl.BlockSpec(shape, lambda i: (0, 0), pipeline_mode=pl.Buffered(1))


def feed_kernel(cut, x, above, gate_up, down, hid, dgate, dup, out, back):
    f = hid.shape[1]
    for first_column in range(0, f, cut):
        at = slice(first_column, first_column + cut)
        gg = jnp.dot(x[...], gate_up[:, at], preferred_element_type=F32)
        uu = jnp.dot(x[...], gate_up[:, f + first_column : f + first_column + cut], preferred_element_type=F32)
        dhid = jnp.dot(above[...], down[:, at], preferred_element_type=F32)
        gelu, inner = gelu_parts(gg)
        hid[:, at] = (gelu * uu).astype(BF16)
        dgate[:, at] = (dhid * uu * gelu_slope(gg, inner)).astype(BF16)
        dup[:, at] = (dhid * gelu).astype(BF16)
    for first_column in range(0, x.shape[1], 512):
        at = slice(first_column, first_column + 512)
        out[:, at] = contract_last(hid[...], down[at]).astype(BF16)
        both = contract_last(dgate[...], gate_up[at, :f]) + contract_last(dup[...], gate_up[at, f:])
        back[:, at] = both.astype(BF16)


def feed_forward_back(x, above, gate_up, down):
    tokens, model = x.shape
    f = down.shape[1]
    rows = 256

    def block(width):
        return pl.BlockSpec((rows, width), lambda i: (i, 0))

    return pl.pallas_call(
        functools.partial(feed_kernel, 256),
        grid=(tokens // rows,),
        out_shape=tuple(jax.ShapeDtypeStruct((tokens, n), BF16) for n in (f, f, f, model, model)),
        in_specs=[block(model), block(model), resident(gate_up.shape), resident(down.shape)],
        out_specs=tuple(block(n) for n in (f, f, f, model, model)),
        compiler_params=pltpu.CompilerParams(vmem_limit_bytes=48 * 2**20),
        cost_estimate=pl.CostEstimate(
            flops=12 * tokens * model * f, bytes_accessed=40 * 2**20, transcendentals=0
        ),
    )(x, above, gate_up, down)


def feed_grads_kernel(x, above, hid, dgate, dup, gate_o, up_o, down_o):
    gate_o[...] = contract_first(x[...], dgate[...]).astype(BF16)
    up_o[...] = contract_first(x[...], dup[...]).astype(BF16)
    down_o[...] = contract_first(above[...], hid[...]).astype(BF16)


def feed_grads(x, above, hid, dgate, dup):
    tokens, model = x.shape
    f = hid.shape[1]
    columns = pl.BlockSpec((tokens, 256), lambda i: (0, i))
    return pl.pallas_call(
        feed_grads_kernel,
        grid=(model // 256,),
        out_shape=(jax.ShapeDtypeStruct((model, f), BF16),) * 3,
        in_specs=[columns, columns] + [resident(hid.shape)] * 3,
        out_specs=(pl.BlockSpec((256, f), lambda i: (i, 0)),) * 3,
        compiler_params=pltpu.CompilerParams(vmem_limit_bytes=48 * 2**20),
        cost_estimate=pl.CostEstimate(
            flops=6 * tokens * model * f, bytes_accessed=40 * 2**20, transcendentals=0
        ),
    )(x, above, hid, dgate, dup)


def adam_step(weight, grad, first, second, factor, rate, decay_rate):
    clipped = grad * factor
    first_new = beta_first * first + (1.0 - beta_first) * clipped
    second_new = beta_second * second + (1.0 - beta_second) * clipped * clipped
    first_hat = first_new / (1.0 - beta_first**STEP)
    second_hat = second_new / (1.0 - beta_second**STEP)
    weight_new = weight - rate * (
        first_hat / (jnp.sqrt(second_hat) + adam_eps) + decay_rate * weight
    )
    return (first_new, second_new, weight_new)


def adam_kernel(rate, decay_rate, sources, factor, w, m, v, *refs):
    grads, (m_o, v_o, w_o) = refs[: len(sources)], refs[len(sources) :]
    parts = []
    for ref, pieces in zip(grads, sources):
        for first, columns, at, stride in pieces:
            for t in range(8):
                parts.append((at + t * stride, ref[t, :, first : first + columns].astype(F32)))
    parts.sort(key=lambda part: part[0])
    grad = jnp.concatenate([part for _, part in parts], axis=1)
    first_new, second_new, weight_new = adam_step(
        w[...], grad, m[...], v[...], factor[0:1, 0:1], rate, decay_rate
    )
    m_o[...] = first_new
    v_o[...] = second_new
    w_o[...] = weight_new


def adam_rows(weight, grads, sources, first, second, factor, rate, decay_rate):
    rows, width = weight.shape
    step = min(rows, 16)
    block = pl.BlockSpec((step, width), lambda i: (i, 0))
    shape = jax.ShapeDtypeStruct(weight.shape, F32)
    return pl.pallas_call(
        functools.partial(adam_kernel, rate, decay_rate, sources),
        grid=(rows // step,),
        out_shape=(shape,) * 3,
        in_specs=[pl.BlockSpec((8, 128), lambda i: (0, 0)), block, block, block]
        + [pl.BlockSpec((8, step, g.shape[2]), lambda i: (0, i, 0)) for g in grads],
        out_specs=(block,) * 3,
        compiler_params=pltpu.CompilerParams(vmem_limit_bytes=48 * 2**20),
        cost_estimate=pl.CostEstimate(flops=0, bytes_accessed=7 * 4 * weight.size, transcendentals=0),
    )(factor, weight, first, second, *grads)


def on_device(
    block_input,
    out_grad,
    norm_gains,
    mixer_weight,
    gate_weight,
    chan_params,
    mlp_weight,
    first_gains,
    first_mixer,
    first_gate,
    first_chan,
    first_mlp,
    second_gains,
    second_mixer,
    second_gate,
    second_chan,
    second_mlp,
):
    length = lax.axis_size("seq") // 2
    z = lax.axis_index("seq") // 2
    tokens, model = block_input.shape[1:]
    share = mixer_weight.shape[0]
    pair = 2 * share
    lru = mixer_weight.shape[1] // 3
    hidden = mlp_weight.shape[1] // 3
    r8, f8 = lru // 8, hidden // 8
    rc = -(-r8 // 128) * 128
    head = gate_weight.shape[1] // 2
    heads = r8 // head
    gate_rows = gate_weight.shape[0]
    gate_pad = -(-gate_rows // 16) * 16

    x = lax.axis_index("seq") - 2 * z
    batch = lax.axis_index("batch")
    plain = pair % 128 == 0

    def turned(v):
        if plain:
            return v
        v = v.reshape(v.shape[0], 4, length, pair).swapaxes(1, 2)
        return jnp.roll(v, -z, axis=1).reshape(v.shape[0], model)

    def turned_back(v):
        if plain:
            return v
        v = jnp.roll(v.reshape(v.shape[0], length, 4, pair), z, axis=1)
        return v.swapaxes(1, 2).reshape(v.shape[0], model)

    normed_one, mixer_full, mlp_gu, mlp_down, gains, gate_in, inputs, above = first(
        turned(block_input[0]),
        turned(out_grad[0]),
        mixer_weight,
        mlp_weight,
        norm_gains,
        gate_weight,
        chan_params,
        rc,
        length,
        1,
    )
    normed_one = normed_one.reshape(8 * tokens, model)
    gate_own = gate_in[:, :gate_rows].reshape(r8, rc)
    chan = gate_own[:, 2 * head : 2 * head + 8].astype(F32).T
    lam = chan[7]
    fill = jnp.concatenate([jnp.zeros((7, rc - r8), F32), jnp.ones((1, rc - r8), F32)])
    chan = jnp.concatenate([chan[:7], 8.0 * jax.nn.softplus(-lam)[None]])
    chan = jnp.concatenate([chan, fill], axis=1)
    gate = []
    for h in range(heads):
        block = gate_own[h * head : (h + 1) * head, : 2 * head]
        at = ((0, 0), (h * head, rc - (h + 1) * head))
        gate.append(
            jnp.concatenate([jnp.pad(block[:, :head], at), jnp.pad(block[:, head:], at)], axis=1)
        )
    gate = jnp.pad(jnp.concatenate(gate), ((0, rc - r8), (0, 0)))

    mixer_full = mixer_full.reshape(model, 3 * r8)
    parts = [jnp.pad(mixer_full[:, n * r8 : (n + 1) * r8], ((0, 0), (0, rc - r8))) for n in range(3)]
    mixer_first = jnp.concatenate(parts[:2], axis=1)
    mixer_last = parts[2]
    span = 2 * tokens
    projected = jnp.dot(normed_one, mixer_first, preferred_element_type=F32)
    projected = projected.reshape(4, span, 2 * rc)
    mixed, *kept, grad_out, mlp_down = recur_forward(projected, gate, chan, above, mlp_down, length, 2)
    grad_out = grad_out.reshape(8 * tokens, model)
    mixed = mixed.reshape(4 * span, rc)
    residual, normed_two, mlp_gu = middle(
        contract_last(mixed, mixer_last).astype(BF16), inputs, gains, mlp_gu, length, 3
    )
    normed_two = normed_two.reshape(8 * tokens, model)
    mlp_gu = mlp_gu.reshape(model, 2 * f8)
    mlp_down = mlp_down.reshape(model, f8)
    hid, dgg, duu, mlp_part, dnormed_two = feed_forward_back(normed_two, grad_out, mlp_gu, mlp_down)
    gate_terms, up_terms, down_terms = (
        v.reshape(length, 8 * share, f8) for v in feed_grads(normed_two, grad_out, hid, dgg, duu)
    )
    up_cut, down_cut = f8 // 384 * 256, f8 // 384 * 256

    grad_residual, gain_two, dmz, sums_one, squares_one = turn(
        dnormed_two, residual, above, gains,
        (gate_terms, up_terms), ((0, 0, f8), (1, 0, up_cut)), length, 4,
    )
    dmz = dmz.reshape(8 * tokens, model)
    dmix = jnp.dot(dmz, mixer_last, preferred_element_type=F32).reshape(4, span, rc)
    dproj, dgate, chan_grad, sums_two, squares_two, back_one = recur_backward(
        dmix, gate, chan, kept, projected, sums_one.reshape(8, share, sums_one.shape[1]),
        (up_terms, down_terms), ((0, up_cut, f8 - up_cut), (1, 0, down_cut)), length, 6,
    )
    dproj = dproj.reshape(4 * span, 2 * rc)
    dgate = dgate.reshape(4 * span, 2 * rc)
    dnormed_one, block_output, back_two, rest_sums, squares_three = closing(
        normed_one, dmz, dproj, mixed, mixer_first, mlp_part, residual,
        down_terms, (down_cut, f8 - down_cut), sums_two, r8, length, 7,
    )

    gate_full_grad = contract_first(kept[4].reshape(4 * span, rc), dgate)
    blocks = []
    for h in range(heads):
        at = slice(h * head, (h + 1) * head)
        blocks.append(
            jnp.concatenate([gate_full_grad[at, at], gate_full_grad[at, rc + h * head : rc + (h + 1) * head]], axis=1)
        )
    gate_grad_own = jnp.concatenate(blocks)
    chan_grad = jnp.sum(chan_grad, axis=1)[:, :r8]
    chan_grad = jnp.concatenate([chan_grad[:7], (8.0 * jax.nn.sigmoid(-lam) * chan_grad[7])[None]])
    gate_back = jnp.concatenate([gate_grad_own, chan_grad.T], axis=1).reshape(length, gate_rows, 2 * head + 8)
    gate_back = jnp.pad(
        gate_back, ((0, 0), (0, gate_pad - gate_rows), (0, rc - 2 * head - 8))
    )
    gate_back = jnp.roll(gate_back, -z, axis=0)
    rest_back, input_grad, *small, norm, factor = last(
        rest_sums.reshape(8, share, rest_sums.shape[1]), dnormed_one, inputs, grad_residual, gains, gain_two,
        gate_back, squares_one + squares_two + squares_three,
        (
            norm_gains, first_gains, second_gains, gate_weight, first_gate, second_gate,
            chan_params, first_chan, second_chan,
        ),
        length, 8,
    )
    gains_up, gate_up, chan_up = small[:3], small[3:6], small[6:]
    rest = f8 - down_cut
    mixer_up = adam_rows(
        mixer_weight, (rest_back,), ([(rest + n * r8, r8, n * lru, r8) for n in range(3)],),
        first_mixer, second_mixer, factor, rate_matrix, decay_matrix,
    )
    mlp_up = adam_rows(
        mlp_weight, (back_one, back_two, rest_back),
        (
            [(0, f8, 0, f8), (f8, up_cut, hidden, f8)],
            [(0, f8 - up_cut, hidden + up_cut, f8), (f8 - up_cut, down_cut, 2 * hidden, f8)],
            [(0, rest, 2 * hidden + down_cut, f8)],
        ),
        first_mlp, second_mlp, factor, rate_matrix, decay_matrix,
    )
    return (
        turned_back(block_output)[None],
        turned_back(input_grad)[None],
        norm[0, 0],
        *gains_up,
        *mixer_up,
        *gate_up,
        *chan_up,
        *mlp_up,
    )


def solution(mesh):
    rows = P(("batch", "seq"), None)
    columns = P(None, ("batch", "seq"))
    data = P("batch", "seq", None)
    weights = (columns, rows, rows, columns, rows)
    in_specs = (data, data) + weights * 3
    triples = tuple(spec for spec in weights for _ in range(3))
    return jax.shard_map(
        on_device,
        mesh=mesh,
        in_specs=in_specs,
        out_specs=(data, data, P()) + triples,
        check_vma=False,
    )
```

```python
import functools
import math

import jax
import jax.numpy as jnp
from jax import lax
from jax.experimental import pallas as pl
from jax.experimental.pallas import tpu as pltpu
from jax.sharding import PartitionSpec as P

STEP = 10
norm_eps = 1e-06
clip_limit = 1.0
beta_first = 0.9
beta_second = 0.999
adam_eps = 1e-08
rate_matrix = 0.05
rate_gains = 0.8
rate_channel = 2.0
decay_matrix = 0.1

MESH = pl.DeviceIdType.MESH
F32 = jnp.float32
BF16 = jnp.bfloat16
ANY = pl.BlockSpec(memory_space=pl.ANY)
VM = pl.BlockSpec(memory_space=pltpu.VMEM)
FLIPS = [(fy, fc, fx) for fy in (0, 1) for fc in (0, 1) for fx in (0, 1) if fy + fc + fx]
GELU_SCALE = math.sqrt(2.0 / math.pi)


def place():
    b = lax.axis_index("batch")
    s = lax.axis_index("seq")
    y, z = b // 2, s // 2
    return y, b - 2 * y, z, s - 2 * z


def device(y, c, z, x):
    return (y * 2 + c, z * 2 + x)


def rank(y, c, x):
    return (y * 2 + c) * 2 + x


def flip(v, f):
    return 1 - v if f else v


def greet(peers):
    barrier = pltpu.get_barrier_semaphore()
    for peer in peers:
        pl.semaphore_signal(barrier, inc=1, device_id=peer, device_id_type=MESH)
    pl.semaphore_wait(barrier, len(peers))


def remote(src, dst, send, recv, to):
    copy = pltpu.make_async_remote_copy(
        src_ref=src, dst_ref=dst, send_sem=send, recv_sem=recv, device_id=to, device_id_type=MESH
    )
    copy.start()
    return copy


VMEM_BYTES = 63 * 2**20


def params(collective_id):
    return pltpu.CompilerParams(
        collective_id=collective_id, has_side_effects=True, vmem_limit_bytes=VMEM_BYTES
    )


DMA = pltpu.SemaphoreType.DMA


def gather_peers():
    y, c, z, x = place()
    return [device(y, c, z, 1 - x), device(1 - y, c, z, x), device(y, 1 - c, z, x)]


class Gather:
    def __init__(self, a, o, loc, ss, rs):
        y, c, z, x = place()
        self.to_x, self.to_y, self.to_c = gather_peers()
        self.me, self.bx = rank(y, c, x), rank(y, c, 1 - x)
        self.by, self.bd = rank(1 - y, c, x), rank(1 - y, c, 1 - x)
        half = a.shape[0] // 2
        self.lo, self.hi = pl.ds(0, half), pl.ds(half, half)
        self.a, self.o, self.loc, self.ss, self.rs = a, o, loc, ss, rs
        self.done, self.last = [], []

    def send(self, src, dst, k, to):
        copy = remote(src, dst, self.ss.at[k], self.rs.at[k], to)
        self.done.append(copy)
        return copy

    def relay(self, block, part, k, to):
        return self.send(self.o.at[block, part], self.o.at[block, part], k, to)

    def begin_half(self, half):
        a, o, me = self.a, self.o, self.me
        part = (self.lo, self.hi)[half]
        if half == 0:
            self.s0 = self.send(a.at[part], o.at[me, part], 0, self.to_x)
            self.s3 = self.send(a.at[part], o.at[me, part], 3, self.to_y)
        else:
            self.s1 = self.send(a.at[part], o.at[me, part], 1, self.to_y)
            self.s2 = self.send(a.at[part], o.at[me, part], 2, self.to_x)
        self.last.append(self.send(a.at[part], o.at[me, part], (4, 13)[half], self.to_c))
        if half == 1:
            self.own = pltpu.make_async_copy(a, o.at[me], self.loc)
            self.own.start()

    def begin(self):
        self.begin_half(0)
        self.begin_half(1)

    def middle(self):
        self.s0.wait_recv()
        self.s5 = self.relay(self.bx, self.lo, 5, self.to_y)
        self.last.append(self.relay(self.bx, self.lo, 7, self.to_c))
        self.s1.wait_recv()
        self.s6 = self.relay(self.by, self.hi, 6, self.to_x)
        self.last.append(self.relay(self.by, self.hi, 8, self.to_c))

    def relays(self, mark=lambda: None):
        self.s2.wait_recv()
        self.last.append(self.relay(self.bx, self.hi, 9, self.to_c))
        self.s3.wait_recv()
        self.last.append(self.relay(self.by, self.lo, 10, self.to_c))
        mark()
        self.s5.wait_recv()
        self.last.append(self.relay(self.bd, self.lo, 11, self.to_c))
        self.s6.wait_recv()
        self.last.append(self.relay(self.bd, self.hi, 12, self.to_c))

    def finish(self):
        for copy in self.last:
            copy.wait_recv()
        for copy in self.done:
            copy.wait_send()
        self.own.wait()

    def end(self, mark=lambda: None):
        self.relays(mark)
        self.finish()


def scatter_steps(p, o, mine, sib, part, got, loc, ss, rs):
    y, c, z, x = place()
    to_x, to_y, to_c = gather_peers()
    half = o.shape[0] // 2
    step = 16
    cut = (pl.ds(0, half), pl.ds(half, half))
    where = ((1 - y, 1 - x), (1 - y, x), (y, 1 - x), (y, x))
    order = [(0, 0), (0, 1), (1, 0), (2, 1), (2, 0), (1, 1), (3, 0), (3, 1)]
    from_c, own, sends = {}, {}, []
    for n, (t, h) in enumerate(order):
        ty, tx = where[t]
        own[t, h] = pltpu.make_async_copy(
            p.at[rank(ty, c, tx), cut[h]], mine.at[t, h], loc.at[n]
        )
        own[t, h].start()
        from_c[t, h] = remote(
            p.at[rank(ty, 1 - c, tx), cut[h]], sib.at[t, h], ss.at[n], rs.at[n], to_c
        )
        sends.append(from_c[t, h])
    yield "begun"

    def add(dst, t, h, extra):
        own[t, h].wait()
        from_c[t, h].wait_recv()

        @pl.loop(0, half // step)
        def _(i):
            at = pl.ds(pl.multiple_of(i * step, step), step)
            total = mine[t, h, at].astype(F32) + sib[t, h, at].astype(F32)
            for ref in extra:
                total = total + ref[at].astype(F32)
            dst[at] = total.astype(dst.dtype)

    def send(k, slot, to):
        copy = remote(part.at[k], got.at[slot], ss.at[8 + k], rs.at[8 + slot], to)
        sends.append(copy)
        return copy

    def arrival(slot):
        return pltpu.make_async_remote_copy(
            src_ref=part.at[0], dst_ref=got.at[slot], send_sem=ss.at[8], recv_sem=rs.at[8 + slot],
            device_id=to_x, device_id_type=MESH,
        )

    add(part.at[0], 0, 0, ())
    send(0, 1, to_y)
    add(part.at[1], 0, 1, ())
    send(1, 3, to_x)
    add(part.at[2], 1, 0, ())
    send(2, 0, to_y)
    add(part.at[3], 2, 1, ())
    send(3, 2, to_x)
    yield "sent"
    arrival(1).wait_recv()
    add(part.at[4], 2, 0, (got.at[1],))
    send(4, 4, to_x)
    yield "early"
    arrival(3).wait_recv()
    add(part.at[5], 1, 1, (got.at[3],))
    send(5, 5, to_y)
    yield "late"
    arrival(0).wait_recv()
    arrival(4).wait_recv()
    add(o.at[cut[0]], 3, 0, (got.at[0], got.at[4]))
    yield "low half"
    arrival(2).wait_recv()
    arrival(5).wait_recv()
    add(o.at[cut[1]], 3, 1, (got.at[2], got.at[5]))
    yield "high half"
    for copy in sends:
        copy.wait_send()


def scatter_scratch(half, width):
    return [
        pltpu.VMEM((4, 2, half, width), BF16),
        pltpu.VMEM((4, 2, half, width), BF16),
        pltpu.VMEM((6, half, width), BF16),
        pltpu.VMEM((6, half, width), BF16),
        DMA((8,)),
        DMA((14,)),
        DMA((14,)),
    ]


def exchange_steps(a, o, loc, ss, rs, columns=None):
    y, c, z, x = place()
    me = rank(y, c, x)
    dst = o.at[me] if columns is None else o.at[me, :, columns]
    copies = []
    for n, (fy, fc, fx) in enumerate(FLIPS):
        ty, tc, tx = flip(y, fy), flip(c, fc), flip(x, fx)
        copies.append(remote(a.at[rank(ty, tc, tx)], dst, ss.at[n], rs.at[n], device(ty, tc, z, tx)))
    own = pltpu.make_async_copy(a.at[me], dst, loc)
    own.start()
    return copies, own


def plane_peers():
    y, c, z, x = place()
    return [device(flip(y, fy), flip(c, fc), z, flip(x, fx)) for fy, fc, fx in FLIPS]


def line_peers(length):
    y, c, z, x = place()
    return [device(y, c, lax.rem(z + k, length), x) for k in range(1, length)]


class LineGather:
    def __init__(self, buf, length, ss, rs):
        y, c, z, x = place()
        self.z, self.length, self.buf, self.ss, self.rs = z, length, buf, ss, rs
        self.up = device(y, c, lax.rem(z + 1, length), x)
        self.down = device(y, c, lax.rem(z + length - 1, length), x)

    def copy(self, hop, upward):
        length, buf = self.length, self.buf
        src, dst = ((length - hop + 1) % length, length - hop) if upward else (hop - 1, hop)
        way = 0 if upward else 1
        return pltpu.make_async_remote_copy(
            src_ref=buf.at[src], dst_ref=buf.at[dst], send_sem=self.ss.at[way, hop - 1],
            recv_sem=self.rs.at[way, hop - 1], device_id=self.up if upward else self.down,
            device_id_type=MESH,
        )

    def sends(self, hop, act):
        z, length = self.z, self.length

        @pl.when(jnp.logical_and(z + 1 < length, z >= hop - 1))
        def _():
            act(self.copy(hop, True))

        @pl.when(jnp.logical_and(z >= 1, z + hop - 1 < length))
        def _():
            act(self.copy(hop, False))

    def start(self, hop):
        self.sends(hop, lambda copy: copy.start())

    def start_piece(self, n):
        for way, last, dst in ((0, self.z + 1 < self.length, self.length - 1), (1, self.z >= 1, 1)):

            @pl.when(last)
            def _():
                remote(
                    self.buf.at[0, n], self.buf.at[dst, n], self.ss.at[way, 0], self.rs.at[way, 0],
                    (self.up, self.down)[way],
                )

    def arrive(self, hop):
        z, length = self.z, self.length

        @pl.when(z >= hop)
        def _():
            self.copy(hop, True).wait_recv()

        @pl.when(z + hop < length)
        def _():
            self.copy(hop, False).wait_recv()

    def finish(self, first_hop=1, last_hop=None):
        for hop in range(first_hop, (last_hop or self.length - 1) + 1):
            self.sends(hop, lambda copy: copy.wait_send())


class LineScatter:
    def __init__(self, sources, length, total, up_mine, down_mine, up_got, down_got, loc, ss, rs):
        y, c, z, x = place()
        self.sources, self.length, self.total = sources, length, total
        self.mine, self.got = (up_mine, down_mine), (up_got, down_got)
        self.loc, self.ss, self.rs = loc, ss, rs
        self.to = (device(y, c, lax.rem(z + 1, length), x), device(y, c, lax.rem(z + length - 1, length), x))
        self.far = (z, length - 1 - z)
        self.next = 1

    def loads(self, way, hop):
        k = 0 if hop == 0 else self.length - hop if way == 0 else hop
        copies, at = [], 0
        for n, (ref, first, columns) in enumerate(self.sources):
            dst = self.term(way, hop) if hop else self.total
            copies.append(
                pltpu.make_async_copy(
                    ref.at[k, :, pl.ds(first, columns)], dst.at[:, pl.ds(at, columns)],
                    self.loc.at[way, hop, n],
                )
            )
            at += columns
        return copies

    def term(self, way, hop):
        return self.mine[way].at[hop - 1]

    def copy(self, way, hop):
        return pltpu.make_async_remote_copy(
            src_ref=self.term(way, hop), dst_ref=self.got[way].at[hop - 1],
            send_sem=self.ss.at[way, hop - 1], recv_sem=self.rs.at[way, hop - 1],
            device_id=self.to[way], device_id_type=MESH,
        )

    def load(self, hops):
        for hop in hops:
            for way in (0, 1) if hop else (0,):
                for copy in self.loads(way, hop):
                    copy.start()

    def start(self):
        hop = self.next
        if hop >= self.length:
            return
        self.next += 1
        for way in (0, 1):
            far = self.far[way]
            for copy in self.loads(way, hop):
                copy.wait()
            if hop > 1:

                @pl.when(jnp.logical_and(far >= 1, far <= hop - 1))
                def _():
                    self.copy(way, hop - 1).wait_recv()
                    dst, src = self.term(way, hop), self.got[way].at[hop - 2]

                    def add(at):
                        dst[at] = dst[at] + src[at]

                    rows_loop(dst.shape[0], add, unroll=4)

            @pl.when(far <= hop - 1)
            def _():
                self.copy(way, hop).start()

    def end(self, result, first_column, squares):
        last = self.length - 1
        for copy in self.loads(0, 0):
            copy.wait()
        columns = pl.ds(first_column, self.total.shape[1])

        def finish(ways):
            for way in ways:
                self.copy(way, last).wait_recv()

            def add(at):
                total = self.total[at].astype(F32)
                for way in ways:
                    total = total + self.got[way][last - 1, at].astype(F32)
                result[at, columns] = total.astype(result.dtype)
                squares[...] += tile_of_squares(total)

            rows_loop(result.shape[0], add)

        above, below = self.far[0] >= 1, self.far[1] >= 1
        pl.when(jnp.logical_and(above, below))(lambda: finish((0, 1)))
        pl.when(jnp.logical_not(above))(lambda: finish((1,)))
        pl.when(jnp.logical_not(below))(lambda: finish((0,)))
        for hop in range(1, self.length):
            for way in (0, 1):

                @pl.when(self.far[way] <= hop - 1)
                def _():
                    self.copy(way, hop).wait_send()


class HeldLine(LineScatter):
    def __init__(self, g, first_column, up_got, down_got, ss, rs):
        y, c, z, x = place()
        self.length = length = g.shape[0]
        self.columns = pl.ds(first_column, up_got.shape[2])
        self.sources, self.g, self.total = (), g, g.at[0, :, self.columns]
        self.got, self.ss, self.rs = (up_got, down_got), ss, rs
        self.to = line_neighbours(length)
        self.far = (z, length - 1 - z)
        self.next = 1

    def term(self, way, hop):
        return self.g.at[self.length - hop if way == 0 else hop, :, self.columns]


def chains_of(cuts):
    whole = sum(cut[2] for cut in cuts)
    left = -(-whole // 256) * 128
    lists = [], []
    for which, first_column, columns in cuts:
        taken = min(columns, left)
        if taken:
            lists[0].append((which, first_column, taken))
        if columns > taken:
            lists[1].append((which, first_column + taken, columns - taken))
        left -= taken
    return lists


class Lines:
    def __init__(self, terms, cuts, length, refs):
        self.chains, self.length = [], length
        for n, cut in enumerate(chains_of(cuts)):
            sources = [(terms[which], first_column, columns) for which, first_column, columns in cut]
            self.chains.append(
                LineScatter(sources, length, *refs[n * LINE_REFS : (n + 1) * LINE_REFS])
            )
        self.queue = [chain for _ in range(1, length) for chain in self.chains]

    def begin(self):
        for chain in self.chains:
            chain.load((1,))
        self.start()
        self.start()
        for chain in self.chains:
            chain.load((*range(2, self.length), 0))

    def start(self):
        if self.queue:
            self.queue.pop(0).start()

    def end(self, result, squares):
        while self.queue:
            self.start()
        squares[...] = jnp.zeros_like(squares)
        at = 0
        for chain in self.chains:
            chain.end(result, at, squares)
            at += chain.total.shape[1]


def lines_scratch(length, rows, cuts):
    return sum(
        (line_scratch(length, rows, sum(cut[2] for cut in chain), len(chain)) for chain in chains_of(cuts)), []
    )


def fold(v):
    return jnp.sum(v.reshape(v.shape[0] // 8, 8, v.shape[1]), axis=0)


def tile_of_squares(v):
    v = fold(v * v)
    part = v[:, :128]
    for n in range(1, v.shape[1] // 128):
        part = part + v[:, n * 128 : (n + 1) * 128]
    if v.shape[1] % 128:
        rest = v[:, v.shape[1] // 128 * 128 :]
        part = part + jnp.concatenate([rest, jnp.zeros((8, 128 - rest.shape[1]), F32)], axis=1)
    return part


def line_scratch(length, rows, columns, sources):
    slots = pltpu.VMEM((length - 1, rows, columns), BF16)
    return [pltpu.VMEM((rows, columns), BF16)] + [slots] * 4 + [
        DMA((2, length, sources)), DMA((2, length)), DMA((2, length))
    ]


LINE_REFS = 8
SCATTER_REFS = 7
TILE = jax.ShapeDtypeStruct((8, 128), F32)


def line_neighbours(length):
    y, c, z, x = place()
    return [device(y, c, lax.rem(z + 1, length), x), device(y, c, lax.rem(z + length - 1, length), x)]


def rows_loop(rows, body, start=0, unroll=2):
    @pl.loop(start // 16, (start + rows) // 16, unroll=unroll)
    def _(i):
        body(pl.ds(pl.multiple_of(i * 16, 16), 16))


def turned_tiles(length, pair):
    _, _, z, _ = place()
    for k in range(length):
        for b in range(4):
            yield k * 4 + b, pl.multiple_of((b * length + lax.rem(z + k, length)) * pair, pair)


def load_turned(ref, at, length, pair):
    if pair % 128:
        return ref[at]
    return jnp.concatenate([ref[at, pl.ds(src, pair)] for _, src in turned_tiles(length, pair)], axis=1)


def store_turned(ref, at, value, length, pair):
    if pair % 128:
        ref[at] = value
        return
    for n, dst in turned_tiles(length, pair):
        ref[at, pl.ds(dst, pair)] = value[:, n * pair : (n + 1) * pair]


def inverse_rms(v):
    return lax.rsqrt(jnp.sum(v * v, axis=-1, keepdims=True) * (1.0 / v.shape[-1]) + norm_eps)


def norm_rows_back(v, gain, grad):
    inverse = inverse_rms(v)
    scaled = v * inverse
    moved = grad * gain
    inner = jnp.sum(moved * scaled, axis=-1, keepdims=True) * (1.0 / v.shape[-1])
    return inverse * (moved - scaled * inner), fold(grad * scaled)


def middle_kernel(length, mixed, mixer, inputs, gains, w_in, late_in, residual, normed_o, w, late, *scratch):
    scatter_refs, (p, low, loc, gs, gr, hs, hr, late_s, late_r) = scratch[:SCATTER_REFS], scratch[SCATTER_REFS:]
    greet(gather_peers() + line_neighbours(length))
    hops = LineGather(w, length, hs, hr)
    hops.start(1)
    late_hops = LineGather(late, length, late_s, late_r)
    late_hops.start(1)
    started = [1]
    part = mixed.shape[1]
    rows, width = low.shape

    @pl.loop(0, 4)
    def _(i):
        mine = mixed[pl.ds(pl.multiple_of(i * 2 * rows, rows), 2 * rows)]
        for first_column in range(0, width, 512):
            at = slice(first_column, first_column + 512)
            both = contract_last(mine, mixer[at, 2 * part :]).astype(BF16)
            p[pl.ds(2 * i, 2), :, at] = both.reshape(2, rows, 512)

    def advance():
        if started[0] < length - 1:
            hops.arrive(started[0])
            started[0] += 1
            hops.start(started[0])

    def body(at):
        v = inputs[at].astype(F32) + residual[at]
        residual[at] = v
        low[at] = (v * inverse_rms(v) * gains[1:2]).astype(BF16)

    half = low.shape[0] // 2
    gather = Gather(low, normed_o, loc, gs, gr)
    for name in scatter_steps(p, residual, *scatter_refs):
        if name == "late":
            advance()
        if name == "low half":
            rows_loop(half, body)
            gather.begin_half(0)
        if name == "high half":
            rows_loop(half, body, half)
            gather.begin_half(1)
    gather.middle()
    advance()
    gather.end()
    while started[0] < length - 1:
        advance()
    hops.arrive(length - 1)
    hops.finish()
    late_hops.arrive(1)
    late_hops.finish(1, 1)


def middle(mixed, mixer, inputs, gains, w, late, length, collective_id):
    rows, width = inputs.shape
    return pl.pallas_call(
        functools.partial(middle_kernel, length),
        out_shape=(
            jax.ShapeDtypeStruct((rows, width), F32),
            jax.ShapeDtypeStruct((8, rows, width), BF16),
            jax.ShapeDtypeStruct(w.shape, w.dtype),
            jax.ShapeDtypeStruct(late.shape, late.dtype),
        ),
        in_specs=[VM, VM, VM, VM, ANY, ANY],
        out_specs=(VM, ANY, ANY, ANY),
        scratch_shapes=scatter_scratch(rows // 2, width)
        + [pltpu.VMEM((8, rows, width), BF16), pltpu.VMEM((rows, width), BF16), DMA, DMA((14,)), DMA((14,))]
        + [DMA((2, length))] * 4,
        input_output_aliases={4: 2, 5: 3},
        compiler_params=params(collective_id),
        cost_estimate=pl.CostEstimate(flops=0, bytes_accessed=300 * 2**20, transcendentals=0),
    )(mixed, mixer, inputs, gains, w, late)


def turn_kernel(length, cuts, p, residual, above, gains, mixer, *refs):
    parts = 1 + max(cut[0] for cut in cuts)
    terms, refs = refs[:parts], refs[parts:]
    back, gain, low_o, dmix, sums, squares, *scratch = refs
    scatter_refs, (total, low, loc, gs, gr, parts_in, load_s), line_refs = (
        scratch[:SCATTER_REFS], scratch[SCATTER_REFS : SCATTER_REFS + 7], scratch[SCATTER_REFS + 7 :]
    )
    greet(gather_peers() + line_neighbours(length))
    line = Lines(terms, cuts, length, line_refs)
    line.begin()
    gain[...] = jnp.zeros_like(gain)

    def body(at):
        grad, gain_part = norm_rows_back(residual[at], gains[1:2], total[at])
        grad = above[at].astype(F32) + grad
        back[at] = grad
        low[at] = grad.astype(BF16)
        gain[...] += gain_part

    half = low.shape[0] // 2
    gather = Gather(low, low_o, loc, gs, gr)
    for name in scatter_steps(p, total, *scatter_refs):
        if name in ("early", "late"):
            line.start()
        if name == "low half":
            rows_loop(half, body)
            gather.begin_half(0)
        if name == "high half":
            rows_loop(half, body, half)
            gather.begin_half(1)
            line.start()
    gather.middle()
    line.start()
    gather.end()
    rows = low.shape[0]
    part = mixer.shape[1] // 3

    def load(n, slot):
        return pltpu.make_async_copy(low_o.at[pl.ds(2 * n, 2)], parts_in.at[slot], load_s.at[slot])

    load(0, 0).start()

    @pl.loop(0, 4)
    def _(n):
        slot = n - n // 2 * 2

        @pl.when(n + 1 < 4)
        def _():
            load(n + 1, 1 - slot).start()

        load(n, slot).wait()
        lines = parts_in[slot].reshape(2 * rows, parts_in.shape[3])
        mix = jnp.dot(lines, mixer[:, 2 * part :], preferred_element_type=F32)
        none = jnp.zeros((2 * rows, dmix.shape[1] - part), F32)
        dmix[pl.ds(pl.multiple_of(n * 2 * rows, rows), 2 * rows)] = jnp.concatenate([mix, none], axis=1)

    line.end(sums, squares)


def turn(p, residual, above, gains, mixer, rc, terms, cuts, length, collective_id):
    rows, width = residual.shape
    line_rows, columns = terms[0].shape[1], sum(cut[2] for cut in cuts)
    return pl.pallas_call(
        functools.partial(turn_kernel, length, cuts),
        out_shape=(
            jax.ShapeDtypeStruct((rows, width), F32),
            jax.ShapeDtypeStruct((8, width), F32),
            jax.ShapeDtypeStruct((8, rows, width), BF16),
            jax.ShapeDtypeStruct((8 * rows, rc), F32),
            jax.ShapeDtypeStruct((line_rows, columns), BF16),
            TILE,
        ),
        in_specs=[ANY, VM, VM, VM, VM] + [ANY] * len(terms),
        out_specs=(VM, VM, ANY, VM, VM, VM),
        scratch_shapes=scatter_scratch(rows // 2, width)
        + [pltpu.VMEM((rows, width), F32), pltpu.VMEM((rows, width), BF16), DMA, DMA((14,)), DMA((14,))]
        + [pltpu.VMEM((2, 2, rows, width), BF16), DMA((2,))]
        + lines_scratch(length, line_rows, cuts),
        compiler_params=params(collective_id),
        cost_estimate=pl.CostEstimate(flops=0, bytes_accessed=300 * 2**20, transcendentals=0),
    )(p.reshape(8, rows, width), residual, above, gains, mixer, *terms)


def closing_kernel(
    length, cut, part, x_in, dmz_in, dproj, mixed, mixer, q, residual, terms, block,
    o, out, e_o, sums, squares,
    x_part, dmz_part, g, back, total, up_a, down_a, up_b, down_b, ls, lr, load_s, free, loc, es, er, *scratch,
):
    scatter_refs, line_refs = scratch[:SCATTER_REFS], scratch[SCATTER_REFS:]
    greet(plane_peers() + line_neighbours(length))
    model = mixer.shape[0]
    tokens = dproj.shape[0]
    columns = x_part.shape[2]
    steps = model // columns
    rows = tokens // steps
    line_rows = g.shape[1]

    def loads(i, slot):
        at = pl.ds(pl.multiple_of(i * columns, columns), columns)
        return (
            pltpu.make_async_copy(x_in.at[:, at], x_part.at[slot], load_s.at[0, slot]),
            pltpu.make_async_copy(dmz_in.at[:, at], dmz_part.at[slot], load_s.at[1, slot]),
        )

    group = steps // 4
    order = (3, 1, 2, 0)

    def fetch(i, slot):
        for copy in loads(i, slot):
            copy.start()

    fetch(order[0] * group, 0)
    rest = LineScatter([(terms, *cut)], length, *line_refs)
    rest.load((1,))
    rest.start()
    rest.load((*range(2, length), 0))
    split = up_a.shape[2]
    line_a = HeldLine(g, 0, up_a, down_a, ls.at[0], lr.at[0])
    line_b = HeldLine(g, split, up_b, down_b, ls.at[1], lr.at[1])
    queue = [chain for _ in range(1, length) for chain in (line_a, line_b)]

    def advance(times=1):
        for _ in range(times):
            if queue:
                queue.pop(0).start()

    output = scatter_steps(q, total, *scatter_refs)
    next(output)
    copies, own = exchange_steps(block, e_o, loc, es, er)

    def compute(n):
        @pl.loop(0, group)
        def _(j):
            count = n * group + j
            slot = count - count // 2 * 2
            i = order[n] * group + j

            @pl.when(j + 1 < group)
            def _():
                fetch(i + 1, 1 - slot)

            if n < 3:

                @pl.when(j + 1 == group)
                def _():
                    fetch(order[n + 1] * group, 1 - slot)

            for copy in loads(i, slot):
                copy.wait()
            front = contract_first(x_part[slot], dproj[...])
            tail = contract_first(dmz_part[slot], mixed[...])
            k = i * columns // line_rows
            at = pl.ds(pl.multiple_of(i * columns - k * line_rows, columns), columns)
            g[k, at] = jnp.concatenate([front, tail], axis=1).astype(BF16)
            block_of = i * rows // 256
            at = pl.ds(pl.multiple_of(i * rows - block_of * 256, rows), rows)
            mine = dproj[pl.ds(pl.multiple_of(i * rows, rows), rows)]
            for first_column in range(0, model, 512):
                cols = slice(first_column, first_column + 512)
                back[block_of, at, cols] = contract_last(mine, mixer[cols, : 2 * part]).astype(BF16)

    compute(0)
    next(output)
    rest.start()
    compute(1)
    while rest.next < length:
        rest.start()
    if length == 4:
        advance(2)
    next(output)
    compute(2)
    next(output)
    compute(3)
    advance(1 if length == 4 else 2)
    for _ in output:
        pass
    for peer in gather_peers():
        pl.semaphore_signal(free, inc=1, device_id=peer, device_id_type=MESH)
    advance()
    pl.semaphore_wait(free, 3)
    incoming = scatter_steps(back, o, *scatter_refs)
    next(incoming)
    pair = out.shape[1] // (4 * length)

    def body(at):
        store_turned(out, at, (residual[at] + total[at]).astype(BF16), length, pair)

    rows_loop(out.shape[0], body)
    squares[...] = jnp.zeros_like(squares)
    rest.end(sums, 0, squares)
    for name in incoming:
        if name in ("sent", "late"):
            advance()
    while queue:
        advance()
    line_a.end(sums, cut[1], squares)
    line_b.end(sums, cut[1] + split, squares)
    for copy in copies:
        copy.wait()
    own.wait()


def closing(x, dmz, dproj, mixed, mixer, q, residual, terms, cut, block, part, length, collective_id):
    rows, width = residual.shape
    tokens, model = x.shape
    share = block.shape[0] // 8
    block = block.reshape(8, share, block.shape[1])
    line_rows = terms.shape[1]
    columns = min(256, line_rows)
    split = -(-3 * part // 256) * 128
    held_a, held_b = (pltpu.VMEM((length - 1, line_rows, n), BF16) for n in (split, 3 * part - split))
    return pl.pallas_call(
        functools.partial(closing_kernel, length, cut, part),
        out_shape=(
            jax.ShapeDtypeStruct((rows, width), F32),
            jax.ShapeDtypeStruct((rows, width), BF16),
            jax.ShapeDtypeStruct(block.shape, BF16),
            jax.ShapeDtypeStruct((line_rows, cut[1] + 3 * part), BF16),
            TILE,
        ),
        in_specs=[ANY, ANY, VM, VM, VM, ANY, VM, ANY, ANY],
        out_specs=(VM, VM, ANY, VM, VM),
        scratch_shapes=[
            pltpu.VMEM((2, tokens, columns), BF16),
            pltpu.VMEM((2, tokens, columns), BF16),
            pltpu.VMEM((length, line_rows, 3 * part), BF16),
            pltpu.VMEM((8, rows, width), BF16),
            pltpu.VMEM((rows, width), F32),
            held_a, held_a, held_b, held_b,
            DMA((2, 2, length)), DMA((2, 2, length)), DMA((2, 2)), pltpu.SemaphoreType.REGULAR,
            DMA, DMA((7,)), DMA((7,)),
        ]
        + scatter_scratch(rows // 2, width)
        + line_scratch(length, line_rows, cut[1], 1),
        compiler_params=params(collective_id),
        cost_estimate=pl.CostEstimate(
            flops=10 * tokens * model * dproj.shape[1] // 2, bytes_accessed=350 * 2**20, transcendentals=0
        ),
    )(x, dmz, dproj, mixed, mixer, q.reshape(8, rows, width), residual, terms, block)


def first_kernel(
    length, inputs_in, above_in, mixer_in, mlp_in, gains_in, gate_in, chan_in,
    normed_o, wm_o, wf_o, wd_o, w2, gains_o, gp_o, inputs_o, above_o,
    inputs, above, mixer_w, mlp_w, gains_w, gate_w, chan_w, load_s,
    gn, gp, normed, gn_all, wm, wf, wd, loc, ms, mr, fs, fr, line_s, line_r, gain_s, gain_r, move_s, move_r,
    gather_s, gather_r, hop_s, hop_r,
):
    loads = [
        pltpu.make_async_copy(src, dst, load_s.at[n])
        for n, (src, dst) in enumerate(
            (
                (gains_in, gains_w), (gate_in, gate_w), (chan_in, chan_w), (mixer_in, mixer_w),
                (mlp_in, mlp_w), (inputs_in, inputs), (above_in, above),
            )
        )
    ]
    for copy in loads:
        copy.start()
    y, c, z, x = place()
    s = 2 * z + x
    me = rank(y, c, x)
    rows, width = inputs.shape
    pair = width // (4 * length)
    line = line_peers(length)
    plane = plane_peers()
    to_z, to_x = lax.rem(s, length), s // length
    moves = jnp.where(jnp.logical_and(to_z == z, to_x == x), 0, 1)
    src = x * length + z
    from_z = src // 2
    from_x = src - 2 * from_z
    barrier = pltpu.get_barrier_semaphore()
    for peer in line + plane:
        pl.semaphore_signal(barrier, inc=1, device_id=peer, device_id_type=MESH)

    @pl.when(moves == 1)
    def _():
        pl.semaphore_signal(barrier, inc=1, device_id=device(y, c, to_z, to_x), device_id_type=MESH)
        pl.semaphore_signal(barrier, inc=1, device_id=device(y, c, from_z, from_x), device_id_type=MESH)

    pl.semaphore_wait(barrier, len(line) + len(plane) + 2 * moves)

    for copy in loads[:3]:
        copy.wait()
    share = gains_w.shape[1]
    gn[...] = jnp.zeros_like(gn)
    for n in (0, 1):

        @pl.when(x == n)
        def _():
            gn[:2, n * share : (n + 1) * share] = gains_w[...]

    gp[...] = jnp.zeros_like(gp)
    channels = contract_first(chan_w[...].astype(BF16), unit(8))
    gp[: gate_w.shape[0]] = jnp.concatenate(
        [
            gate_w[...],
            channels,
            jnp.zeros((gate_w.shape[0], gp.shape[1] - gate_w.shape[1] - 8), F32),
        ],
        axis=1,
    ).astype(BF16)
    gn_all[me, z] = gn[...]
    gains = [
        remote(gn, gn_all.at[me, z], line_s.at[0, k], line_r.at[0, k], line[k]) for k in range(length - 1)
    ]
    gate_move = pltpu.make_async_remote_copy(
        src_ref=gp, dst_ref=gp_o.at[to_z], send_sem=move_s, recv_sem=move_r,
        device_id=device(y, c, to_z, to_x), device_id_type=MESH,
    )
    gate_stay = pltpu.make_async_copy(gp, gp_o.at[z], loc.at[2])
    pl.when(moves == 1)(lambda: gate_move.start())
    pl.when(moves == 0)(lambda: gate_stay.start())

    def fill(pack, source, js, offset=0):
        part = pack.shape[2] // len(js)
        whole = source.shape[1] // 24
        for t in range(8):
            for n, j in enumerate(js):
                start = (j * 8 + t) * whole + offset
                pack[t, :, n * part : (n + 1) * part] = source[:, start : start + part].astype(BF16)

    loads[3].wait()
    fill(wm, mixer_w, (0, 1, 2))
    mixer, mixer_own = exchange_steps(wm, wm_o.at[0], loc.at[0], ms, mr)
    for copy in gains:
        copy.wait()
    spread = [
        remote(gn_all.at[me], gn_all.at[me], gain_s.at[n], gain_r.at[n], plane[n]) for n in range(7)
    ]
    pl.when(moves == 1)(lambda: gate_move.wait())
    pl.when(moves == 0)(lambda: gate_stay.wait())
    gates = [
        remote(gp_o.at[z], gp_o.at[z], line_s.at[1, k], line_r.at[1, k], line[k])
        for k in range(length - 1)
    ]
    hops = LineGather(wm_o, length, hop_s, hop_r)
    mixer_own.wait()
    hops.start_piece(me)

    def pass_piece(n):
        fy, fc, fx = FLIPS[n]
        mixer[n].wait_recv()
        hops.start_piece(rank(flip(y, fy), flip(c, fc), flip(x, fx)))

    pass_piece(1)
    loads[4].wait()
    fill(wd, mlp_w, (2,))
    down, down_own = exchange_steps(wd, wd_o.at[0], loc.at[4], fs.at[1], fr.at[1])
    fill(wf, mlp_w, (0, 1))
    feed, feed_own = exchange_steps(wf, wf_o.at[0], loc.at[3], fs.at[0], fr.at[0])
    for n in (0, 2, 3, 5, 4, 6):
        pass_piece(n)
    fill(w2, mlp_w, (0, 1, 2), wd.shape[2])
    for copy in spread:
        copy.wait()
    for k in range(length):
        other = lax.rem(z + k, length)
        for b in range(4):
            at = slice((4 * k + b) * pair, (4 * k + b + 1) * pair)
            tile = (gn_all[2 * b, other] + gn_all[2 * b + 1, other])[:, :pair]
            gains_o[:, at] = tile.astype(BF16).astype(F32)
    for copy in mixer:
        copy.wait_send()

    def body(at):
        v = load_turned(inputs, at, length, pair)
        inputs_o[at] = v
        v = v.astype(F32)
        normed[at] = (v * inverse_rms(v) * gains_o[0:1]).astype(BF16)
        above_o[at] = load_turned(above, at, length, pair)

    for copy in loads[5:]:
        copy.wait()
    half = rows // 2
    gather = Gather(normed, normed_o, loc.at[1], gather_s, gather_r)
    rows_loop(half, body)
    gather.begin_half(0)
    rows_loop(half, body, half)
    gather.begin_half(1)
    hops.arrive(1)
    if length > 2:
        hops.start(2)
    gather.middle()
    if length > 3:
        hops.arrive(2)
        hops.start(3)
    gather.relays()
    for hop in range(min(3, length - 1), length):
        hops.arrive(hop)
        if hop + 1 < length:
            hops.start(hop + 1)
    gather.finish()
    for copy in down + feed + gates:
        copy.wait()
    down_own.wait()
    feed_own.wait()
    hops.finish()


def early(f8):
    return f8 // 384 * 256


def unit(n):
    return (
        lax.broadcasted_iota(jnp.int32, (n, n), 0) == lax.broadcasted_iota(jnp.int32, (n, n), 1)
    ).astype(BF16)


def first(inputs, above, mixer, mlp, gains, gate, chan, rc, length, collective_id):
    rows, width = inputs.shape
    pack = (-(-gate.shape[0] // 16) * 16, rc)
    share = mixer.shape[0]
    f8 = mlp.shape[1] // 24
    wm, wf, wd, w2 = (
        (8, share, n) for n in (mixer.shape[1] // 8, 2 * early(f8), early(f8), 3 * (f8 - early(f8)))
    )
    low = jax.ShapeDtypeStruct((rows, width), BF16)
    return pl.pallas_call(
        functools.partial(first_kernel, length),
        out_shape=(
            jax.ShapeDtypeStruct((8, rows, width), BF16),
            jax.ShapeDtypeStruct((length,) + wm, BF16),
            jax.ShapeDtypeStruct((length,) + wf, BF16),
            jax.ShapeDtypeStruct((length,) + wd, BF16),
            jax.ShapeDtypeStruct(w2, BF16),
            jax.ShapeDtypeStruct((8, width), F32),
            jax.ShapeDtypeStruct((length,) + pack, BF16),
            low,
            low,
        ),
        in_specs=[ANY] * 7,
        out_specs=(ANY, ANY, ANY, ANY, VM, VM, ANY, VM, VM),
        scratch_shapes=[
            *[pltpu.VMEM(v.shape, v.dtype) for v in (inputs, above, mixer, mlp, gains, gate, chan)],
            DMA((7,)),
            pltpu.VMEM((8, 128), F32),
            pltpu.VMEM(pack, BF16),
            pltpu.VMEM((rows, width), BF16),
            pltpu.VMEM((8, length, 8, 128), F32),
            pltpu.VMEM(wm, BF16),
            pltpu.VMEM(wf, BF16),
            pltpu.VMEM(wd, BF16),
            DMA((5,)), DMA((7,)), DMA((7,)), DMA((2, 7)), DMA((2, 7)),
            DMA((2, length)), DMA((2, length)), DMA((7,)), DMA((7,)), DMA, DMA,
            DMA((14,)), DMA((14,)), DMA((2, length)), DMA((2, length)),
        ],
        compiler_params=params(collective_id),
        cost_estimate=pl.CostEstimate(flops=0, bytes_accessed=300 * 2**20, transcendentals=0),
    )(inputs, above, mixer, mlp, gains, gate, chan)


def last_kernel(
    length, share, wm, total, inputs, back, gains, gain_two, gp, sq_one, sq_two, sq_three,
    wm_o, grad_o, gains_o, gates_o,
    norm_o, factor_o,
    gain, row_sums, gn, gn_in, gn_mid, gn_got, gp_got, gp_sum, gp_fin, sq_plane, sq_line,
    loc, ss, rs, gs, gr, ls, lr, move_s, move_r,
):
    y, c, z, x = place()
    s = 2 * z + x
    me = rank(y, c, x)
    line = line_peers(length)
    plane = plane_peers()
    owner = x * length + z
    to_z = owner // 2
    to_x = owner - 2 * to_z
    from_z, from_x = lax.rem(s, length), s // length
    moves = jnp.where(jnp.logical_and(to_z == z, to_x == x), 0, 1)
    barrier = pltpu.get_barrier_semaphore()
    for peer in line + plane:
        pl.semaphore_signal(barrier, inc=1, device_id=peer, device_id_type=MESH)

    @pl.when(moves == 1)
    def _():
        pl.semaphore_signal(barrier, inc=1, device_id=device(y, c, to_z, to_x), device_id_type=MESH)
        pl.semaphore_signal(barrier, inc=1, device_id=device(y, c, from_z, from_x), device_id_type=MESH)

    pl.semaphore_wait(barrier, len(line) + len(plane) + 2 * moves)

    gate = [
        remote(gp.at[lax.rem(z + k + 1, length)], gp_got.at[k], ls.at[0, k], lr.at[0, k], line[k])
        for k in range(length - 1)
    ]
    rows, width = inputs.shape
    pair = width // (4 * length)
    gain[...] = jnp.zeros_like(gain)

    def body(at):
        grad, gain_part = norm_rows_back(inputs[at].astype(F32), gains[0:1], total[at])
        store_turned(grad_o, at, back[at] + grad, length, pair)
        gain[...] += gain_part

    rows_loop(rows, body)
    row = lax.broadcasted_iota(jnp.int32, (8, width), 0)
    ones = jnp.sum(gain[...], axis=0, keepdims=True)
    twos = jnp.sum(gain_two[...], axis=0, keepdims=True)
    row_sums[...] = jnp.where(row == 0, ones, jnp.where(row == 1, twos, 0.0))
    if pair < 128:
        gn[...] = jnp.zeros_like(gn)
    for k in range(length):
        for b in range(4):
            gn[b, k, :, :pair] = row_sums[:, (4 * k + b) * pair : (4 * k + b + 1) * pair]
    sends = []
    for n, (fy, fc, fx) in enumerate(FLIPS):
        to = flip(y, fy) * 2 + flip(c, fc)
        sends.append(remote(gn.at[to], gn_in.at[n], gs.at[0, n], gr.at[0, n], plane[n]))
    copies, own = exchange_steps(wm, wm_o, loc, ss, rs)
    for copy in gate:
        copy.wait()
    sums = gp[z]
    for k in range(length - 1):
        sums = sums + gp_got[k]
    gp_sum[...] = sums
    for copy in sends:
        copy.wait()
    sums = gn[2 * y + c]
    for n in range(7):
        sums = sums + gn_in[n]
    gn_mid[...] = sums
    sends = [
        remote(gn_mid.at[k + 1], gn_got.at[k], ls.at[1, k], lr.at[1, k], line[k])
        for k in range(length - 1)
    ]

    @pl.when(moves == 1)
    def _():
        copy = remote(gp_sum, gp_fin, move_s, move_r, device(y, c, to_z, to_x))
        copy.wait()

    @pl.when(moves == 0)
    def _():
        gp_fin[...] = gp_sum[...]

    for copy in sends:
        copy.wait()
    sums = gn_mid[0]
    for k in range(length - 1):
        sums = sums + gn_got[k]
    lane = lax.broadcasted_iota(jnp.int32, (8, 128), 1)
    mine = jnp.logical_and(lane >= x * share, lane < (x + 1) * share)
    gain_sum = jnp.where(mine, sums, 0.0)
    gate_sum = gp_fin[...]
    sq_plane[me] = sq_one[...] + sq_two[...] + sq_three[...] + gain_sum * gain_sum + tile_of_squares(gate_sum)
    sends = [
        remote(sq_plane.at[me], sq_plane.at[me], gs.at[1, n], gr.at[1, n], plane[n]) for n in range(7)
    ]
    for copy in sends:
        copy.wait()
    sums = sq_plane[0]
    for n in range(1, 8):
        sums = sums + sq_plane[n]
    sq_line[z] = sums
    sends = [
        remote(sq_line.at[z], sq_line.at[z], ls.at[2, k], lr.at[2, k], line[k])
        for k in range(length - 1)
    ]
    for copy in sends:
        copy.wait()
    sums = sq_line[0]
    for n in range(1, length):
        sums = sums + sq_line[n]
    sums = jnp.sum(jnp.sum(sums, axis=0, keepdims=True), axis=1, keepdims=True)
    norm = jnp.broadcast_to(jnp.sqrt(sums), (8, 128))
    factor = clip_limit / jnp.maximum(norm, clip_limit)
    norm_o[...] = norm
    factor_o[...] = factor
    gains_o[...] = jnp.where(x == 0, gain_sum[:2, :share], gain_sum[:2, share : 2 * share])
    gates_o[...] = gate_sum
    for copy in copies:
        copy.wait()
    own.wait()


def last(wm, total, inputs, back, gains, gain_two, gp, squares, length, collective_id):
    rows, width = inputs.shape
    share = wm.shape[1]
    return pl.pallas_call(
        functools.partial(last_kernel, length, share),
        out_shape=(
            jax.ShapeDtypeStruct(wm.shape, wm.dtype),
            jax.ShapeDtypeStruct((rows, width), F32),
            jax.ShapeDtypeStruct((2, share), F32),
            jax.ShapeDtypeStruct(gp.shape[1:], F32),
            TILE, TILE,
        ),
        in_specs=[ANY] + [VM] * 9,
        out_specs=(ANY,) + (VM,) * 5,
        scratch_shapes=[
            pltpu.VMEM((8, width), F32),
            pltpu.VMEM((8, width), F32),
            pltpu.VMEM((4, length, 8, 128), F32),
            pltpu.VMEM((7, length, 8, 128), F32),
            pltpu.VMEM((length, 8, 128), F32),
            pltpu.VMEM((length, 8, 128), F32),
            pltpu.VMEM(gp.shape, F32),
            pltpu.VMEM(gp.shape[1:], F32),
            pltpu.VMEM(gp.shape[1:], F32),
            pltpu.VMEM((8, 8, 128), F32),
            pltpu.VMEM((length, 8, 128), F32),
            DMA, DMA((7,)), DMA((7,)), DMA((2, 7)), DMA((2, 7)),
            DMA((3, length)), DMA((3, length)), DMA, DMA,
        ],
        compiler_params=params(collective_id),
    )(wm, total, inputs, back, gains, gain_two, gp, *squares)


def minus_expm1(v):
    series = 1.0 + v * (1.0 / 8.0)
    for n in (7.0, 6.0, 5.0, 4.0, 3.0, 2.0):
        series = 1.0 + series * v * (1.0 / n)
    return jnp.where(v > -0.5, -v * series, 1.0 - jnp.exp(v))


def gelu_parts(v):
    inner = jnp.tanh(GELU_SCALE * (v + 0.044715 * v * v * v))
    return 0.5 * v * (1.0 + inner), inner


def gelu_slope(v, inner):
    return 0.5 * (1.0 + inner) + 0.5 * v * (1.0 - inner * inner) * GELU_SCALE * (
        1.0 + 3.0 * 0.044715 * v * v
    )


CHUNK = 64


def forward_kernel(
    length, x_in, mixer, gate, chan, above, w2, w_in,
    mixed, branch_o, decay_o, width_o, recur_o, enter_o, conv_o, xe_o, se_o, ends_o, above_o, w2_o, w,
    x_part, pre, loc_h, ends, carry, hs, hr, es, er, gather_l, gather_s, gather_r, hop_s, hop_r, load_s, keep_s, w2_l, w2_s, w2_r,
    branch, decay_k, width_k, recur_k, enter_k, conv_k, xe, se,
):
    keeps = [
        pltpu.make_async_copy(src, dst, keep_s.at[n])
        for n, (src, dst) in enumerate(
            (
                (branch, branch_o), (decay_k, decay_o), (width_k, width_o), (recur_k, recur_o),
                (enter_k, enter_o), (conv_k, conv_o), (xe, xe_o), (se, se_o),
            )
        )
    ]
    y, c, z, x = place()
    line = line_peers(length)
    seqs, span, rc = branch.shape
    part = mixed.shape[2]
    rows = x_part.shape[1]
    chunks = span // CHUNK

    def load(n, slot):
        half = 1 - n // seqs
        b = n - n // seqs * seqs
        at = pl.ds(pl.multiple_of((b * 2 + half) * rows, rows), rows)
        return pltpu.make_async_copy(x_in.at[at], x_part.at[slot], load_s.at[slot])

    load(0, 0).start()
    greet(line + plane_peers())
    hops = LineGather(w, length, hop_s, hop_r)
    hops.start(1)
    gather = Gather(above, above_o, gather_l, gather_s, gather_r)
    gather.begin()
    shares, share_own = exchange_steps(w2, w2_o.at[0], w2_l, w2_s, w2_r)

    def project(n):
        slot = n - n // 2 * 2

        @pl.when(n + 1 < 2 * seqs)
        def _():
            load(n + 1, 1 - slot).start()

        load(n, slot).wait()
        both = jnp.dot(x_part[slot], mixer[:, : 2 * part], preferred_element_type=F32)
        none = jnp.zeros((rows, rc - part), F32)
        half = 1 - n // seqs
        b = n - n // seqs * seqs
        at = pl.multiple_of(half * rows, rows)
        branch[b, pl.ds(at, rows)] = jnp.concatenate([both[:, :part], none], axis=1)
        low = both[:, part:].astype(BF16).astype(F32)
        xe[b, pl.ds(at + 8, rows)] = jnp.concatenate([low, none], axis=1)

    pl.loop(0, seqs)(project)
    ahead = device(y, c, lax.rem(z + 1, length), x)
    halo = remote(xe.at[:, pl.ds(span, 8)], xe.at[:, pl.ds(0, 8)], hs, hr, ahead)
    pl.loop(seqs, 2 * seqs)(project)

    def coefficients(b, chunk):
        r = pl.multiple_of(chunk * CHUNK, CHUNK)
        at = pl.ds(r, CHUNK)
        window = xe[b, pl.ds(r, CHUNK + 8)]
        total = chan[4:5] + chan[0:1] * window[8:]
        for k in (1, 2, 3):
            total = total + chan[k : k + 1] * pltpu.roll(window, k, 0)[8:]
        low = total.astype(BF16)
        conv_k[b, at] = low
        value = low.astype(F32)
        gates = jnp.dot(low, gate[...], preferred_element_type=F32)
        recur = jax.nn.sigmoid(gates[:, :rc] + chan[5:6])
        enter = jax.nn.sigmoid(gates[:, rc:] + chan[6:7])
        log_decay = -chan[7:8] * recur
        decay = jnp.exp(log_decay)
        width = jnp.sqrt(minus_expm1(2.0 * log_decay))
        recur_k[b, at] = recur
        enter_k[b, at] = enter
        decay_k[b, at] = decay
        width_k[b, at] = width
        loc_h[b, at] = width * enter * value

    def later_chunks(i):
        b = i // (chunks - 1)
        coefficients(b, 1 + i - b * (chunks - 1))

    many = seqs * (chunks - 1)
    pl.loop(0, many // 2)(later_chunks)
    hops.arrive(1)
    if length > 2:
        hops.start(2)
    pl.loop(many // 2, many)(later_chunks)
    halo.wait()

    @pl.when(z == 0)
    def _():
        xe[:, 0:8] = jnp.zeros((seqs, 8, rc), F32)

    @pl.loop(0, seqs)
    def _(b):
        coefficients(b, 0)

    for copy in keeps[:-1]:
        copy.start()
    row = lax.broadcasted_iota(jnp.int32, (8, rc), 0)

    def tile(i, held):
        at = pl.ds(pl.multiple_of(i * 8, 8), 8)
        new = []
        for b in range(seqs):
            a, h = decay_k[b, at], loc_h[b, at]
            for n in (1, 2, 4):
                keep = row >= n
                h = h + jnp.where(keep, a * pltpu.roll(h, n, 0), 0.0)
                a = jnp.where(keep, a * pltpu.roll(a, n, 0), a)
            h = h + a * held[b][1]
            a = a * held[b][0]
            loc_h[b, at] = h
            pre[b, at] = a
            new.append((a[7:8], h[7:8]))
        return tuple(new)

    one, zero = jnp.ones((1, rc), F32), jnp.zeros((1, rc), F32)
    final = lax.fori_loop(0, span // 8, tile, ((one, zero),) * seqs)
    for b in range(seqs):
        ends[z, 0, b] = jnp.broadcast_to(final[b][0], (8, rc))
        ends[z, 1, b] = jnp.broadcast_to(final[b][1], (8, rc))
        ends_o[b] = jnp.broadcast_to(final[b][0], (8, rc))
    moves = [remote(ends.at[z], ends.at[z], es.at[k], er.at[k], line[k]) for k in range(length - 1)]
    if length > 3:
        hops.arrive(2)
        hops.start(3)
    for copy in moves:
        copy.wait()
    gather.middle()
    carry[...] = jnp.zeros_like(carry)
    for k in range(length):
        carry[...] = jnp.where(k < z, ends[k, 0] * carry[...] + ends[k, 1], carry[...])

    for b in range(seqs):
        se[b, 0:8] = carry[b]

    @pl.loop(0, seqs * chunks)
    def _(i):
        b = i // chunks
        r = pl.multiple_of((i - b * chunks) * CHUNK, CHUNK)
        at = pl.ds(r, CHUNK)
        state = loc_h[b, at] + pre[b, at] * carry[b, 0:1]
        se[b, pl.ds(r + 8, CHUNK)] = state
        gelu, _ = gelu_parts(branch[b, at])
        mixed[b, at] = (state * gelu)[:, :part].astype(BF16)

    keeps[-1].start()
    gather.end()
    for hop in range(min(3, length - 1), length):
        hops.arrive(hop)
        if hop + 1 < length:
            hops.start(hop + 1)
    hops.finish()
    for copy in keeps + shares:
        copy.wait()
    share_own.wait()


def recur_forward(x, mixer, gate, chan, above, w2, w, length, collective_id):
    rc = gate.shape[0]
    part = mixer.shape[1] // 3
    rows = x.shape[0] // 8
    seqs, span = 4, 2 * rows
    full = jax.ShapeDtypeStruct((seqs, span, rc), F32)
    longer = jax.ShapeDtypeStruct((seqs, span + 8, rc), F32)
    kept = (full, full, full, full, full, jax.ShapeDtypeStruct((seqs, span, rc), BF16), longer, longer)
    return pl.pallas_call(
        functools.partial(forward_kernel, length),
        out_shape=(
            jax.ShapeDtypeStruct((seqs, span, part), BF16),
            *kept,
            jax.ShapeDtypeStruct((seqs, 8, rc), F32),
            jax.ShapeDtypeStruct((8,) + above.shape, above.dtype),
            jax.ShapeDtypeStruct((length,) + w2.shape, w2.dtype),
            jax.ShapeDtypeStruct(w.shape, w.dtype),
        ),
        in_specs=[ANY, VM, VM, VM, ANY, ANY, ANY],
        out_specs=(VM,) + (ANY,) * 8 + (VM, ANY, ANY, ANY),
        scratch_shapes=[
            pltpu.VMEM((2, rows, x.shape[1]), BF16),
            pltpu.VMEM((seqs, span, rc), F32),
            pltpu.VMEM((seqs, span, rc), F32),
            pltpu.VMEM((length, 2, seqs, 8, rc), F32),
            pltpu.VMEM((seqs, 8, rc), F32),
            DMA, DMA, DMA((length,)), DMA((length,)),
            DMA, DMA((14,)), DMA((14,)), DMA((2, length)), DMA((2, length)),
            DMA((2,)), DMA((8,)), DMA, DMA((7,)), DMA((7,)),
            *[pltpu.VMEM(v.shape, v.dtype) for v in kept],
        ],
        input_output_aliases={6: 12},
        compiler_params=params(collective_id),
        cost_estimate=pl.CostEstimate(
            flops=2 * seqs * span * rc * rc * 2, bytes_accessed=100 * 2**20, transcendentals=0
        ),
    )(x, mixer, gate, chan, above, w2, w)


def backward_kernel(
    length, cuts, head, dmix, gate, chan, decay, width, recur, enter, conv, xe, se, ends_f, proj, block, *refs
):
    parts = 1 + max(cut[0] for cut in cuts)
    terms, refs = refs[:parts], refs[parts:]
    dproj, gates_o, sums, squares, block_o, *refs = refs
    dgate, gchan, *refs = refs
    suffix, grad, de, ends, carry, hs, hr, es, er, keep_s, move_l, move_s, move_r, *refs = refs
    kept, line_refs = refs[:8], refs[8:]
    loads = [
        pltpu.make_async_copy(src, dst, keep_s.at[n])
        for n, (src, dst) in enumerate(
            zip((dmix, proj, se, decay, width, recur, enter, conv, xe), (de.at[:, pl.ds(0, decay.shape[1])], *kept))
        )
    ]
    proj, se, decay, width, recur, enter, conv, xe = kept
    y, c, z, x = place()
    line = line_peers(length)
    greet(line + plane_peers())
    scatter = Lines(terms, cuts, length, line_refs)
    scatter.begin()
    for copy in loads:
        copy.start()
    moves, own = exchange_steps(block, block_o, move_l, move_s, move_r)
    seqs, span, rc = decay.shape
    part = dproj.shape[2] // 2
    chunks = span // CHUNK
    for copy in loads[:3]:
        copy.wait()

    @pl.loop(0, seqs * chunks)
    def _(i):
        b = i // chunks
        r = pl.multiple_of((i - b * chunks) * CHUNK, CHUNK)
        at = pl.ds(r, CHUNK)
        branch = proj[b, at]
        gelu, inner = gelu_parts(branch)
        above = de[b, at]
        state = se[b, pl.ds(r + 8, CHUNK)]
        grad[b, at] = above * gelu
        proj[b, at] = above * state * gelu_slope(branch, inner)

    loads[3].wait()
    row = lax.broadcasted_iota(jnp.int32, (8, rc), 0)

    def tile(i, held):
        at = pl.ds(pl.multiple_of(span - 8 - i * 8, 8), 8)
        new = []
        for b in range(seqs):
            product, total, following = held[b]
            plain, h = decay[b, at], grad[b, at]
            a = jnp.where(row == 7, following, pltpu.roll(plain, 7, 0))
            for n in (1, 2, 4):
                keep = row < 8 - n
                h = h + jnp.where(keep, a * pltpu.roll(h, 8 - n, 0), 0.0)
                a = jnp.where(keep, a * pltpu.roll(a, 8 - n, 0), a)
            h = h + a * total
            a = a * product
            grad[b, at] = h
            suffix[b, at] = a
            new.append((a[0:1], h[0:1], plain[0:1]))
        return tuple(new)

    one, zero = jnp.ones((1, rc), F32), jnp.zeros((1, rc), F32)
    final = lax.fori_loop(0, span // 8, tile, ((one, zero, one),) * seqs)
    for b in range(seqs):
        ends[z, 0, b] = ends_f[b]
        ends[z, 1, b] = jnp.broadcast_to(final[b][1] * final[b][2], (8, rc))
    tails = [remote(ends.at[z], ends.at[z], es.at[k], er.at[k], line[k]) for k in range(length - 1)]
    for copy in tails:
        copy.wait()
    scatter.start()
    scatter.start()
    for copy in loads[4:]:
        copy.wait()
    carry[...] = jnp.zeros_like(carry)
    for k in reversed(range(length)):
        carry[...] = jnp.where(k > z, ends[k, 0] * carry[...] + ends[k, 1], carry[...])

    gchan[...] = jnp.zeros_like(gchan)

    @pl.loop(0, seqs * chunks)
    def _(i):
        b = i // chunks
        r = pl.multiple_of((i - b * chunks) * CHUNK, CHUNK)
        at = pl.ds(r, CHUNK)
        g = grad[b, at] + suffix[b, at] * carry[b, 0:1]
        a, w, ra, ri = decay[b, at], width[b, at], recur[b, at], enter[b, at]
        value = conv[b, at].astype(F32)
        before = pltpu.roll(se[b, pl.ds(r, CHUNK + 8)], 1, 0)[8:]
        dla = g * before * a - g * ri * value * (a * a) / w
        slope = dla * ra * (1.0 - ra)
        dpa = (-chan[7:8] * slope).astype(BF16)
        dpi = (g * w * value * ri * (1.0 - ri)).astype(BF16)
        dgate[b, at, :rc] = dpa
        dgate[b, at, rc:] = dpi
        gchan[5] += fold(dpa.astype(F32))
        gchan[6] += fold(dpi.astype(F32))
        gchan[7] += fold(dla * ra)
        back = lax.dot_general(
            dgate[b, at], gate[...], (((1,), (1,)), ((), ())), preferred_element_type=F32
        )
        dcv = (g * w * ri + back).astype(BF16).astype(F32)
        de[b, at] = dcv
        gchan[4] += fold(dcv)

    behind = device(y, c, lax.rem(z + length - 1, length), x)
    halo = remote(de.at[:, pl.ds(0, 8)], de.at[:, pl.ds(span, 8)], hs, hr, behind)
    halo.wait()
    scatter.start()
    scatter.start()
    low = conv[...].reshape(seqs * span, rc)
    recur_grad, enter_grad = (
        contract_first(low, dgate[:, :, at].reshape(seqs * span, rc)) for at in (slice(0, rc), slice(rc, 2 * rc))
    )

    @pl.when(z == length - 1)
    def _():
        de[:, span:] = jnp.zeros((seqs, 8, rc), F32)

    @pl.loop(0, seqs * chunks)
    def _(i):
        b = i // chunks
        r = pl.multiple_of((i - b * chunks) * CHUNK, CHUNK)
        at = pl.ds(r, CHUNK)
        window = de[b, pl.ds(r, CHUNK + 8)]
        inputs = xe[b, pl.ds(r, CHUNK + 8)]
        dcv = window[:CHUNK]
        total = chan[0:1] * dcv
        gchan[0] += fold(dcv * inputs[8:])
        for k in (1, 2, 3):
            total = total + chan[k : k + 1] * pltpu.roll(window, CHUNK + 8 - k, 0)[:CHUNK]
            gchan[k] += fold(dcv * pltpu.roll(inputs, k, 0)[8:])
        dproj[b, at] = jnp.concatenate([proj[b, at, :part], total[:, :part]], axis=1).astype(BF16)

    rates = 8.0 * minus_expm1(chan[7:8] * (-1.0 / 8.0))
    channels = [jnp.sum(gchan[n], axis=0, keepdims=True) for n in range(8)]
    channels[7] = channels[7] * rates
    channels = lax.dot_general(
        jnp.concatenate(channels), unit(8).astype(F32), (((0,), (0,)), ((), ())),
        precision=lax.Precision.HIGHEST, preferred_element_type=F32,
    )
    blocks = []
    for first_row in range(0, part, head):
        at = slice(first_row, first_row + head)
        blocks.append(jnp.concatenate([recur_grad[at, at], enter_grad[at, at]], axis=1))
    pack = jnp.concatenate(
        [jnp.concatenate(blocks), channels[:part], jnp.zeros((part, rc - 2 * head - 8), F32)], axis=1
    )
    rows = part // length
    if rows < gates_o.shape[1]:
        gates_o[...] = jnp.zeros_like(gates_o)
    for n in range(length):
        gates_o[n, :rows] = pack[n * rows : (n + 1) * rows]
    scatter.end(sums, squares)
    for copy in moves:
        copy.wait()
    own.wait()


def recur_backward(dmix, gate, chan, kept, part, head, block, terms, cuts, length, collective_id):
    proj, decay, width, recur, enter, conv, xe, se, ends = kept
    seqs, span, rc = decay.shape
    gate_pad = -(-(part // length) // 16) * 16
    line_rows, columns = terms[0].shape[1], sum(cut[2] for cut in cuts)
    return pl.pallas_call(
        functools.partial(backward_kernel, length, cuts, head),
        out_shape=(
            jax.ShapeDtypeStruct((seqs, span, 2 * part), BF16),
            jax.ShapeDtypeStruct((length, gate_pad, rc), F32),
            jax.ShapeDtypeStruct((line_rows, columns), BF16), TILE,
            jax.ShapeDtypeStruct(block.shape, BF16),
        ),
        in_specs=[ANY, VM, VM] + [ANY] * 7 + [VM] + [ANY] * (2 + len(terms)),
        out_specs=(VM,) * 4 + (ANY,),
        scratch_shapes=[
            pltpu.VMEM((seqs, span, 2 * rc), BF16),
            pltpu.VMEM((8, 8, rc), F32),
            pltpu.VMEM((seqs, span, rc), F32),
            pltpu.VMEM((seqs, span, rc), F32),
            pltpu.VMEM((seqs, span + 8, rc), F32),
            pltpu.VMEM((length, 2, seqs, 8, rc), F32),
            pltpu.VMEM((seqs, 8, rc), F32),
            DMA, DMA, DMA((length,)), DMA((length,)),
            DMA((9,)), DMA, DMA((7,)), DMA((7,)),
            *[
                pltpu.VMEM(shape, dtype)
                for shape, dtype in (
                    (decay.shape, F32), (se.shape, F32), (decay.shape, F32), (decay.shape, F32),
                    (decay.shape, F32), (decay.shape, F32), (decay.shape, BF16), (xe.shape, F32),
                )
            ],
        ]
        + lines_scratch(length, line_rows, cuts),
        compiler_params=params(collective_id),
        cost_estimate=pl.CostEstimate(
            flops=2 * seqs * span * rc * rc * 2, bytes_accessed=120 * 2**20, transcendentals=0
        ),
    )(dmix, gate, chan, decay, width, recur, enter, conv, xe, se, ends, proj, block, *terms)


def contract_last(left, right):
    return lax.dot_general(
        left, right, (((1,), (1,)), ((), ())), preferred_element_type=F32
    )


def contract_first(left, right):
    return lax.dot_general(
        left, right, (((0,), (0,)), ((), ())), preferred_element_type=F32
    )


def resident(shape):
    return pl.BlockSpec(shape, lambda i: (0, 0), pipeline_mode=pl.Buffered(1))


def feed_forward(x, above, gate_up, down, hid, dgate, dup):
    f = hid.shape[1]
    for first_column in range(0, f, 256):
        at = slice(first_column, first_column + 256)
        gg = jnp.dot(x[...], gate_up[:, at], preferred_element_type=F32)
        uu = jnp.dot(x[...], gate_up[:, f + first_column : f + first_column + 256], preferred_element_type=F32)
        dhid = jnp.dot(above[...], down[:, at], preferred_element_type=F32)
        gelu, inner = gelu_parts(gg)
        hid[:, at] = (gelu * uu).astype(BF16)
        dgate[:, at] = (dhid * uu * gelu_slope(gg, inner)).astype(BF16)
        dup[:, at] = (dhid * gelu).astype(BF16)


def grads_compute(x, above, hid, dgate, dup, gate_o, up_o, down_o):
    gate_o[...] = contract_first(x[...], dgate[...]).astype(BF16)
    up_o[...] = contract_first(x[...], dup[...]).astype(BF16)
    down_o[...] = contract_first(above[...], hid[...]).astype(BF16)


def with_hops(length, first_hop, last_hop, buf, ss, rs, steps, compute):
    i = pl.program_id(0)
    hops = LineGather(buf, length, ss, rs)

    @pl.when(i == 0)
    def _():
        greet(line_neighbours(length))
        hops.start(first_hop)

    @pl.when(i == steps // 2)
    def _():
        for hop in range(first_hop, last_hop):
            hops.arrive(hop)
            hops.start(hop + 1)

    compute()

    @pl.when(i == steps - 1)
    def _():
        hops.arrive(last_hop)
        hops.finish(first_hop, last_hop)


def early_feed_kernel(length, x, above, gate_up, down, w_in, hid, dgate, dup, w, ss, rs):
    with_hops(
        length, 2, length - 2, w, ss, rs, 8,
        lambda: feed_forward(x, above, gate_up, down, hid, dgate, dup),
    )


def early_feed(x, above, gate_up, down, w, length, collective_id):
    tokens, model = x.shape
    f = down.shape[1]

    def block(width):
        return pl.BlockSpec((tokens // 8, width), lambda i: (i, 0))

    return pl.pallas_call(
        functools.partial(early_feed_kernel, length),
        grid=(8,),
        out_shape=(jax.ShapeDtypeStruct((tokens, f), BF16),) * 3 + (jax.ShapeDtypeStruct(w.shape, w.dtype),),
        in_specs=[block(model), block(model), resident(gate_up.shape), resident(down.shape), ANY],
        out_specs=(block(f),) * 3 + (ANY,),
        scratch_shapes=[DMA((2, length)), DMA((2, length))],
        input_output_aliases={4: 3},
        compiler_params=params(collective_id),
        cost_estimate=pl.CostEstimate(flops=6 * tokens * model * f, bytes_accessed=30 * 2**20, transcendentals=0),
    )(x, above, gate_up, down, w)


def late_feed_kernel(
    x, above, hid_one, dgate_one, dup_one, gate_up, down, late, hid, dgate, dup, out, back
):
    f, g = down.shape[1], hid.shape[1]
    feed_forward(x, above, late.at[:, : 2 * g], late.at[:, 2 * g :], hid, dgate, dup)
    for first_column in range(0, x.shape[1], 512):
        at = slice(first_column, first_column + 512)
        ahead = contract_last(hid_one[...], down[at]) + contract_last(hid[...], late[at, 2 * g :])
        out[:, at] = ahead.astype(BF16)
        both = contract_last(dgate_one[...], gate_up[at, :f]) + contract_last(dup_one[...], gate_up[at, f:])
        both = both + contract_last(dgate[...], late[at, :g]) + contract_last(dup[...], late[at, g : 2 * g])
        back[:, at] = both.astype(BF16)


def late_feed(x, above, early_units, gate_up, down, late):
    tokens, model = x.shape
    f, g = down.shape[1], late.shape[1] // 3

    def block(width):
        return pl.BlockSpec((tokens // 8, width), lambda i: (i, 0))

    widths = (g, g, g, model, model)
    return pl.pallas_call(
        late_feed_kernel,
        grid=(8,),
        out_shape=tuple(jax.ShapeDtypeStruct((tokens, n), BF16) for n in widths),
        in_specs=[block(model), block(model)]
        + [block(f)] * 3
        + [resident(v.shape) for v in (gate_up, down, late)],
        out_specs=tuple(block(n) for n in widths),
        compiler_params=pltpu.CompilerParams(vmem_limit_bytes=VMEM_BYTES),
        cost_estimate=pl.CostEstimate(
            flops=6 * tokens * model * (f + 2 * g), bytes_accessed=60 * 2**20, transcendentals=0
        ),
    )(x, above, *early_units, gate_up, down, late)


def early_grads_kernel(length, x, above, hid, dgate, dup, w_in, gate_o, up_o, down_o, w, ss, rs):
    with_hops(
        length, length - 1, length - 1, w, ss, rs, 8,
        lambda: grads_compute(x, above, hid, dgate, dup, gate_o, up_o, down_o),
    )


def feed_grads(x, above, hid, dgate, dup, w=None, length=0, collective_id=None):
    tokens, model = x.shape
    f = hid.shape[1]
    columns = pl.BlockSpec((tokens, model // 8), lambda i: (0, i))
    in_specs = [columns, columns] + [resident(hid.shape)] * 3
    shapes = (jax.ShapeDtypeStruct((model, f), BF16),) * 3
    out_specs = (pl.BlockSpec((model // 8, f), lambda i: (i, 0)),) * 3
    cost = pl.CostEstimate(flops=6 * tokens * model * f, bytes_accessed=40 * 2**20, transcendentals=0)
    if w is None:
        return pl.pallas_call(
            grads_compute,
            grid=(8,),
            out_shape=shapes,
            in_specs=in_specs,
            out_specs=out_specs,
            compiler_params=pltpu.CompilerParams(vmem_limit_bytes=VMEM_BYTES),
            cost_estimate=cost,
        )(x, above, hid, dgate, dup)
    return pl.pallas_call(
        functools.partial(early_grads_kernel, length),
        grid=(8,),
        out_shape=shapes + (jax.ShapeDtypeStruct(w.shape, w.dtype),),
        in_specs=in_specs + [ANY],
        out_specs=out_specs + (ANY,),
        scratch_shapes=[DMA((2, length)), DMA((2, length))],
        input_output_aliases={5: 3},
        compiler_params=params(collective_id),
        cost_estimate=cost,
    )(x, above, hid, dgate, dup, w)


def adam_step(weight, grad, first, second, factor, rate, decay_rate):
    clipped = grad * factor
    first_new = beta_first * first + (1.0 - beta_first) * clipped
    second_new = beta_second * second + (1.0 - beta_second) * clipped * clipped
    first_hat = first_new / (1.0 - beta_first**STEP)
    second_hat = second_new / (1.0 - beta_second**STEP)
    weight_new = weight - rate * (
        first_hat / (jnp.sqrt(second_hat) + adam_eps) + decay_rate * weight
    )
    return (first_new, second_new, weight_new)


def small_steps(factor, refs, outs):
    gains_sum, gates_sum, *states = refs
    rows, columns = states[3].shape
    channels = lax.dot_general(
        unit(8).astype(F32), gates_sum[:rows, columns : columns + 8], (((1,), (1,)), ((), ())),
        precision=lax.Precision.HIGHEST, preferred_element_type=F32,
    )
    grads = gains_sum[...], gates_sum[:rows, :columns], channels
    rates = (rate_gains, 0.0), (rate_matrix, decay_matrix), (rate_channel, 0.0)
    for n in range(3):
        w, m, v = states[3 * n : 3 * n + 3]
        results = adam_step(w[...], grads[n], m[...], v[...], factor, *rates[n])
        for out, result in zip(outs[3 * n : 3 * n + 3], results):
            out[...] = result


def adam_kernel(rate, decay_rate, sources, factor, w, m, v, *refs):
    grads, refs = refs[: len(sources)], refs[len(sources) :]
    if len(refs) > 3:
        small, refs = refs[:11], refs[11:]
        pl.when(pl.program_id(0) == 0)(lambda: small_steps(factor[0:1, 0:1], small, refs[3:]))
    m_o, v_o, w_o = refs[:3]
    parts = []
    for ref, pieces in zip(grads, sources):
        for first, columns, at, stride in pieces:
            for t in range(8):
                parts.append((at + t * stride, ref[t, :, first : first + columns].astype(F32)))
    parts.sort(key=lambda part: part[0])
    grad = jnp.concatenate([part for _, part in parts], axis=1)
    first_new, second_new, weight_new = adam_step(
        w[...], grad, m[...], v[...], factor[0:1, 0:1], rate, decay_rate
    )
    m_o[...] = first_new
    v_o[...] = second_new
    w_o[...] = weight_new


def adam_rows(weight, grads, sources, first, second, factor, rate, decay_rate, small=()):
    rows, width = weight.shape
    step = min(rows, 16)
    block = pl.BlockSpec((step, width), lambda i: (i, 0))
    shape = jax.ShapeDtypeStruct(weight.shape, F32)

    def whole(v):
        return pl.BlockSpec(v.shape, lambda i: (0, 0))

    results = pl.pallas_call(
        functools.partial(adam_kernel, rate, decay_rate, sources),
        grid=(rows // step,),
        out_shape=(shape,) * 3 + tuple(jax.ShapeDtypeStruct(v.shape, F32) for v in small[2:]),
        in_specs=[pl.BlockSpec((8, 128), lambda i: (0, 0)), block, block, block]
        + [pl.BlockSpec((8, step, g.shape[2]), lambda i: (0, i, 0)) for g in grads]
        + [whole(v) for v in small],
        out_specs=(block,) * 3 + tuple(whole(v) for v in small[2:]),
        compiler_params=pltpu.CompilerParams(vmem_limit_bytes=VMEM_BYTES),
        cost_estimate=pl.CostEstimate(flops=0, bytes_accessed=7 * 4 * weight.size, transcendentals=0),
    )(factor, weight, first, second, *grads, *small)
    return (*results[:3], results[3:]) if small else results


def on_device(
    block_input,
    out_grad,
    norm_gains,
    mixer_weight,
    gate_weight,
    chan_params,
    mlp_weight,
    first_gains,
    first_mixer,
    first_gate,
    first_chan,
    first_mlp,
    second_gains,
    second_mixer,
    second_gate,
    second_chan,
    second_mlp,
):
    length = lax.axis_size("seq") // 2
    z = lax.axis_index("seq") // 2
    tokens, model = block_input.shape[1:]
    share = mixer_weight.shape[0]
    pair = 2 * share
    lru = mixer_weight.shape[1] // 3
    hidden = mlp_weight.shape[1] // 3
    r8, f8 = lru // 8, hidden // 8
    rc = -(-r8 // 128) * 128
    head = gate_weight.shape[1] // 2
    heads = r8 // head
    gate_rows = gate_weight.shape[0]
    gate_pad = -(-gate_rows // 16) * 16

    x = lax.axis_index("seq") - 2 * z
    batch = lax.axis_index("batch")
    plain = pair % 128 == 0

    def turned(v):
        if plain:
            return v
        v = v.reshape(v.shape[0], 4, length, pair).swapaxes(1, 2)
        return jnp.roll(v, -z, axis=1).reshape(v.shape[0], model)

    def turned_back(v):
        if plain:
            return v
        v = jnp.roll(v.reshape(v.shape[0], length, 4, pair), z, axis=1)
        return v.swapaxes(1, 2).reshape(v.shape[0], model)

    normed_one, mixer_full, mlp_gu, mlp_down, late_pack, gains, gate_in, inputs, above = first(
        turned(block_input[0]),
        turned(out_grad[0]),
        mixer_weight,
        mlp_weight,
        norm_gains,
        gate_weight,
        chan_params,
        rc,
        length,
        1,
    )
    normed_one = normed_one.reshape(8 * tokens, model)
    gate_own = gate_in[:, :gate_rows].reshape(r8, rc)
    chan = gate_own[:, 2 * head : 2 * head + 8].astype(F32).T
    lam = chan[7]
    fill = jnp.concatenate([jnp.zeros((7, rc - r8), F32), jnp.ones((1, rc - r8), F32)])
    chan = jnp.concatenate([chan[:7], 8.0 * jax.nn.softplus(-lam)[None]])
    chan = jnp.concatenate([chan, fill], axis=1)
    gate = []
    for h in range(heads):
        block = gate_own[h * head : (h + 1) * head, : 2 * head]
        at = ((0, 0), (h * head, rc - (h + 1) * head))
        gate.append(
            jnp.concatenate([jnp.pad(block[:, :head], at), jnp.pad(block[:, head:], at)], axis=1)
        )
    gate = jnp.pad(jnp.concatenate(gate), ((0, rc - r8), (0, 0)))

    mixer_full = mixer_full.reshape(model, 3 * r8)
    mixed, *kept, grad_out, late, mlp_down = recur_forward(
        normed_one, mixer_full, gate, chan, above, late_pack, mlp_down, length, 2
    )
    grad_out = grad_out.reshape(8 * tokens, model)
    mixed = mixed.reshape(8 * tokens, r8)
    residual, normed_two, mlp_gu, late = middle(mixed, mixer_full, inputs, gains, mlp_gu, late, length, 3)
    normed_two = normed_two.reshape(8 * tokens, model)
    h1 = early(f8)
    h2 = f8 - h1
    mlp_gu = mlp_gu.reshape(model, 2 * h1)
    mlp_down = mlp_down.reshape(model, h1)
    *early_units, late = early_feed(normed_two, grad_out, mlp_gu, mlp_down, late, length, 9)
    *early_terms, late = feed_grads(
        normed_two, grad_out, *early_units, w=late, length=length, collective_id=10
    )
    late = late.reshape(model, 3 * h2)
    *late_units, mlp_part, dnormed_two = late_feed(
        normed_two, grad_out, early_units, mlp_gu, mlp_down, late
    )
    late_terms = feed_grads(normed_two, grad_out, *late_units)
    gate_one, up_one, down_one = (v.reshape(length, 8 * share, h1) for v in early_terms)
    gate_two, up_two, down_two = (v.reshape(length, 8 * share, h2) for v in late_terms)
    down_cut = h1 // 2

    grad_residual, gain_two, dmz, dmix, sums_one, squares_one = turn(
        dnormed_two, residual, above, gains, mixer_full, rc,
        (gate_one, up_one, down_one), ((0, 0, h1), (1, 0, h1), (2, 0, down_cut)), length, 4,
    )
    dmz = dmz.reshape(8 * tokens, model)
    span = 2 * tokens
    dmix = dmix.reshape(4, span, rc)
    dproj, gate_back, sums_two, squares_two, back_one = recur_backward(
        dmix, gate, chan, kept, r8, head, sums_one.reshape(8, share, sums_one.shape[1]),
        (down_one, gate_two, up_two), ((0, down_cut, h1 - down_cut), (1, 0, h2), (2, 0, h2)), length, 6,
    )
    dproj = dproj.reshape(4 * span, 2 * r8)
    dnormed_one, block_output, back_two, rest_sums, squares_three = closing(
        normed_one, dmz, dproj, mixed, mixer_full, mlp_part, residual,
        down_two, (0, h2), sums_two, r8, length, 7,
    )

    rest_back, input_grad, gains_sum, gates_sum, norm, factor = last(
        rest_sums.reshape(8, share, rest_sums.shape[1]), dnormed_one, inputs, grad_residual, gains, gain_two,
        gate_back, (squares_one, squares_two, squares_three), length, 8,
    )
    *mixer_up, small = adam_rows(
        mixer_weight, (rest_back,), ([(h2 + n * r8, r8, n * lru, r8) for n in range(3)],),
        first_mixer, second_mixer, factor, rate_matrix, decay_matrix,
        (
            gains_sum, gates_sum, norm_gains, first_gains, second_gains, gate_weight, first_gate, second_gate,
            chan_params, first_chan, second_chan,
        ),
    )
    gains_up, gate_up, chan_up = small[:3], small[3:6], small[6:]
    mlp_up = adam_rows(
        mlp_weight, (back_one, back_two, rest_back),
        (
            [(0, h1, 0, f8), (h1, h1, hidden, f8), (2 * h1, down_cut, 2 * hidden, f8)],
            [
                (0, h1 - down_cut, 2 * hidden + down_cut, f8),
                (h1 - down_cut, h2, h1, f8),
                (h1 - down_cut + h2, h2, hidden + h1, f8),
            ],
            [(0, h2, 2 * hidden + h1, f8)],
        ),
        first_mlp, second_mlp, factor, rate_matrix, decay_matrix,
    )
    return (
        turned_back(block_output)[None],
        turned_back(input_grad)[None],
        norm[0, 0],
        *gains_up,
        *mixer_up,
        *gate_up,
        *chan_up,
        *mlp_up,
    )


def solution(mesh):
    rows = P(("batch", "seq"), None)
    columns = P(None, ("batch", "seq"))
    data = P("batch", "seq", None)
    weights = (columns, rows, rows, columns, rows)
    in_specs = (data, data) + weights * 3
    triples = tuple(spec for spec in weights for _ in range(3))
    return jax.shard_map(
        on_device,
        mesh=mesh,
        in_specs=in_specs,
        out_specs=(data, data, P()) + triples,
        check_vma=False,
    )
```

```python
import functools
import math

import jax
import jax.numpy as jnp
from jax import lax
from jax.experimental import pallas as pl
from jax.experimental.pallas import tpu as pltpu
from jax.sharding import PartitionSpec as P

STEP = 10
norm_eps = 1e-06
clip_limit = 1.0
beta_first = 0.9
beta_second = 0.999
adam_eps = 1e-08
rate_matrix = 0.05
rate_gains = 0.8
rate_channel = 2.0
decay_matrix = 0.1

MESH = pl.DeviceIdType.MESH
F32 = jnp.float32
BF16 = jnp.bfloat16
ANY = pl.BlockSpec(memory_space=pl.ANY)
VM = pl.BlockSpec(memory_space=pltpu.VMEM)
FLIPS = [(fy, fc, fx) for fy in (0, 1) for fc in (0, 1) for fx in (0, 1) if fy + fc + fx]
GELU_SCALE = math.sqrt(2.0 / math.pi)


def place():
    b = lax.axis_index("batch")
    s = lax.axis_index("seq")
    y, z = b // 2, s // 2
    return y, b - 2 * y, z, s - 2 * z


def device(y, c, z, x):
    return (y * 2 + c, z * 2 + x)


def rank(y, c, x):
    return (y * 2 + c) * 2 + x


def flip(v, f):
    return 1 - v if f else v


def greet(peers):
    barrier = pltpu.get_barrier_semaphore()
    for peer in peers:
        pl.semaphore_signal(barrier, inc=1, device_id=peer, device_id_type=MESH)
    pl.semaphore_wait(barrier, len(peers))


def remote(src, dst, send, recv, to):
    copy = pltpu.make_async_remote_copy(
        src_ref=src, dst_ref=dst, send_sem=send, recv_sem=recv, device_id=to, device_id_type=MESH
    )
    copy.start()
    return copy


VMEM_BYTES = 63 * 2**20


def params(collective_id):
    return pltpu.CompilerParams(
        collective_id=collective_id, has_side_effects=True, vmem_limit_bytes=VMEM_BYTES
    )


DMA = pltpu.SemaphoreType.DMA


def gather_peers():
    y, c, z, x = place()
    return [device(y, c, z, 1 - x), device(1 - y, c, z, x), device(y, 1 - c, z, x)]


class Gather:
    def __init__(self, a, o, loc, ss, rs):
        y, c, z, x = place()
        self.to_x, self.to_y, self.to_c = gather_peers()
        self.me, self.bx = rank(y, c, x), rank(y, c, 1 - x)
        self.by, self.bd = rank(1 - y, c, x), rank(1 - y, c, 1 - x)
        half = a.shape[0] // 2
        self.lo, self.hi = pl.ds(0, half), pl.ds(half, half)
        self.a, self.o, self.loc, self.ss, self.rs = a, o, loc, ss, rs
        self.done, self.last = [], []

    def send(self, src, dst, k, to):
        copy = remote(src, dst, self.ss.at[k], self.rs.at[k], to)
        self.done.append(copy)
        return copy

    def relay(self, block, part, k, to):
        return self.send(self.o.at[block, part], self.o.at[block, part], k, to)

    def begin_half(self, half):
        a, o, me = self.a, self.o, self.me
        part = (self.lo, self.hi)[half]
        if half == 0:
            self.s0 = self.send(a.at[part], o.at[me, part], 0, self.to_x)
            self.s3 = self.send(a.at[part], o.at[me, part], 3, self.to_y)
        else:
            self.s1 = self.send(a.at[part], o.at[me, part], 1, self.to_y)
            self.s2 = self.send(a.at[part], o.at[me, part], 2, self.to_x)
        self.last.append(self.send(a.at[part], o.at[me, part], (4, 13)[half], self.to_c))
        if half == 1:
            self.own = pltpu.make_async_copy(a, o.at[me], self.loc)
            self.own.start()

    def begin(self):
        self.begin_half(0)
        self.begin_half(1)

    def middle(self):
        self.s0.wait_recv()
        self.s5 = self.relay(self.bx, self.lo, 5, self.to_y)
        self.last.append(self.relay(self.bx, self.lo, 7, self.to_c))
        self.s1.wait_recv()
        self.s6 = self.relay(self.by, self.hi, 6, self.to_x)
        self.last.append(self.relay(self.by, self.hi, 8, self.to_c))

    def relays(self, mark=lambda: None):
        self.s2.wait_recv()
        self.last.append(self.relay(self.bx, self.hi, 9, self.to_c))
        self.s3.wait_recv()
        self.last.append(self.relay(self.by, self.lo, 10, self.to_c))
        mark()
        self.s5.wait_recv()
        self.last.append(self.relay(self.bd, self.lo, 11, self.to_c))
        self.s6.wait_recv()
        self.last.append(self.relay(self.bd, self.hi, 12, self.to_c))

    def finish(self, skip=0, own=True):
        for copy in self.last[skip:]:
            copy.wait_recv()
        for copy in self.done:
            copy.wait_send()
        if own:
            self.own.wait()

    def end(self, mark=lambda: None):
        self.relays(mark)
        self.finish()


def scatter_steps(p, o, mine, sib, part, got, loc, ss, rs, prepare=None):
    y, c, z, x = place()
    to_x, to_y, to_c = gather_peers()
    half = o.shape[0] // 2
    step = 16
    cut = (pl.ds(0, half), pl.ds(half, half))
    where = ((1 - y, 1 - x), (1 - y, x), (y, 1 - x), (y, x))
    order = [(0, 0), (0, 1), (1, 0), (2, 1), (2, 0), (1, 1), (3, 0), (3, 1)]
    from_c, own, sends = {}, {}, []
    for n, (t, h) in enumerate(order):
        ty, tx = where[t]
        if prepare and all(key[0] != t for key in own):
            prepare(rank(ty, c, tx))
            prepare(rank(ty, 1 - c, tx))
        own[t, h] = pltpu.make_async_copy(
            p.at[rank(ty, c, tx), cut[h]], mine.at[t, h], loc.at[n]
        )
        own[t, h].start()
        from_c[t, h] = remote(
            p.at[rank(ty, 1 - c, tx), cut[h]], sib.at[t, h], ss.at[n], rs.at[n], to_c
        )
        sends.append(from_c[t, h])
    yield "begun"

    def add(dst, t, h, extra):
        own[t, h].wait()
        from_c[t, h].wait_recv()

        @pl.loop(0, half // step)
        def _(i):
            at = pl.ds(pl.multiple_of(i * step, step), step)
            total = mine[t, h, at].astype(F32) + sib[t, h, at].astype(F32)
            for ref in extra:
                total = total + ref[at].astype(F32)
            dst[at] = total.astype(dst.dtype)

    def send(k, slot, to):
        copy = remote(part.at[k], got.at[slot], ss.at[8 + k], rs.at[8 + slot], to)
        sends.append(copy)
        return copy

    def arrival(slot):
        return pltpu.make_async_remote_copy(
            src_ref=part.at[0], dst_ref=got.at[slot], send_sem=ss.at[8], recv_sem=rs.at[8 + slot],
            device_id=to_x, device_id_type=MESH,
        )

    add(part.at[0], 0, 0, ())
    send(0, 1, to_y)
    add(part.at[1], 0, 1, ())
    send(1, 3, to_x)
    add(part.at[2], 1, 0, ())
    send(2, 0, to_y)
    add(part.at[3], 2, 1, ())
    send(3, 2, to_x)
    yield "sent"
    arrival(1).wait_recv()
    add(part.at[4], 2, 0, (got.at[1],))
    send(4, 4, to_x)
    yield "early"
    arrival(3).wait_recv()
    add(part.at[5], 1, 1, (got.at[3],))
    send(5, 5, to_y)
    yield "late"
    arrival(0).wait_recv()
    arrival(4).wait_recv()
    add(o.at[cut[0]], 3, 0, (got.at[0], got.at[4]))
    yield "low half"
    arrival(2).wait_recv()
    arrival(5).wait_recv()
    add(o.at[cut[1]], 3, 1, (got.at[2], got.at[5]))
    yield "high half"
    for copy in sends:
        copy.wait_send()


def scatter_scratch(half, width):
    return [
        pltpu.VMEM((4, 2, half, width), BF16),
        pltpu.VMEM((4, 2, half, width), BF16),
        pltpu.VMEM((6, half, width), BF16),
        pltpu.VMEM((6, half, width), BF16),
        DMA((8,)),
        DMA((14,)),
        DMA((14,)),
    ]


def exchange_steps(a, o, loc, ss, rs, columns=None):
    y, c, z, x = place()
    me = rank(y, c, x)
    dst = o.at[me] if columns is None else o.at[me, :, columns]
    copies = []
    for n, (fy, fc, fx) in enumerate(FLIPS):
        ty, tc, tx = flip(y, fy), flip(c, fc), flip(x, fx)
        copies.append(remote(a.at[rank(ty, tc, tx)], dst, ss.at[n], rs.at[n], device(ty, tc, z, tx)))
    own = pltpu.make_async_copy(a.at[me], dst, loc)
    own.start()
    return copies, own


def plane_peers():
    y, c, z, x = place()
    return [device(flip(y, fy), flip(c, fc), z, flip(x, fx)) for fy, fc, fx in FLIPS]


def line_peers(length):
    y, c, z, x = place()
    return [device(y, c, lax.rem(z + k, length), x) for k in range(1, length)]


class LineGather:
    def __init__(self, buf, length, ss, rs):
        y, c, z, x = place()
        self.z, self.length, self.buf, self.ss, self.rs = z, length, buf, ss, rs
        self.up = device(y, c, lax.rem(z + 1, length), x)
        self.down = device(y, c, lax.rem(z + length - 1, length), x)

    def copy(self, hop, upward):
        length, buf = self.length, self.buf
        src, dst = ((length - hop + 1) % length, length - hop) if upward else (hop - 1, hop)
        way = 0 if upward else 1
        return pltpu.make_async_remote_copy(
            src_ref=buf.at[src], dst_ref=buf.at[dst], send_sem=self.ss.at[way, hop - 1],
            recv_sem=self.rs.at[way, hop - 1], device_id=self.up if upward else self.down,
            device_id_type=MESH,
        )

    def sends(self, hop, act):
        z, length = self.z, self.length

        @pl.when(jnp.logical_and(z + 1 < length, z >= hop - 1))
        def _():
            act(self.copy(hop, True))

        @pl.when(jnp.logical_and(z >= 1, z + hop - 1 < length))
        def _():
            act(self.copy(hop, False))

    def start(self, hop):
        self.sends(hop, lambda copy: copy.start())

    def start_piece(self, n):
        for way, last, dst in ((0, self.z + 1 < self.length, self.length - 1), (1, self.z >= 1, 1)):

            @pl.when(last)
            def _():
                remote(
                    self.buf.at[0, n], self.buf.at[dst, n], self.ss.at[way, 0], self.rs.at[way, 0],
                    (self.up, self.down)[way],
                )

    def arrive(self, hop):
        z, length = self.z, self.length

        @pl.when(z >= hop)
        def _():
            self.copy(hop, True).wait_recv()

        @pl.when(z + hop < length)
        def _():
            self.copy(hop, False).wait_recv()

    def finish(self, first_hop=1, last_hop=None):
        for hop in range(first_hop, (last_hop or self.length - 1) + 1):
            self.sends(hop, lambda copy: copy.wait_send())


class LineScatter:
    def __init__(self, sources, length, total, up_mine, down_mine, up_got, down_got, loc, ss, rs):
        y, c, z, x = place()
        self.sources, self.length, self.total = sources, length, total
        self.mine, self.got = (up_mine, down_mine), (up_got, down_got)
        self.loc, self.ss, self.rs = loc, ss, rs
        self.to = (device(y, c, lax.rem(z + 1, length), x), device(y, c, lax.rem(z + length - 1, length), x))
        self.far = (z, length - 1 - z)
        self.next = 1

    def loads(self, way, hop):
        k = 0 if hop == 0 else self.length - hop if way == 0 else hop
        copies, at = [], 0
        for n, (ref, first, columns) in enumerate(self.sources):
            dst = self.term(way, hop) if hop else self.total
            copies.append(
                pltpu.make_async_copy(
                    ref.at[k, :, pl.ds(first, columns)], dst.at[:, pl.ds(at, columns)],
                    self.loc.at[way, hop, n],
                )
            )
            at += columns
        return copies

    def term(self, way, hop):
        return self.mine[way].at[hop - 1]

    def copy(self, way, hop):
        return pltpu.make_async_remote_copy(
            src_ref=self.term(way, hop), dst_ref=self.got[way].at[hop - 1],
            send_sem=self.ss.at[way, hop - 1], recv_sem=self.rs.at[way, hop - 1],
            device_id=self.to[way], device_id_type=MESH,
        )

    def load(self, hops):
        for hop in hops:
            for way in (0, 1) if hop else (0,):
                for copy in self.loads(way, hop):
                    copy.start()

    def start(self):
        hop = self.next
        if hop >= self.length:
            return
        self.next += 1
        for way in (0, 1):
            far = self.far[way]
            for copy in self.loads(way, hop):
                copy.wait()
            if hop > 1:

                @pl.when(jnp.logical_and(far >= 1, far <= hop - 1))
                def _():
                    self.copy(way, hop - 1).wait_recv()
                    dst, src = self.term(way, hop), self.got[way].at[hop - 2]

                    def add(at):
                        dst[at] = dst[at] + src[at]

                    rows_loop(dst.shape[0], add, unroll=4)

            @pl.when(far <= hop - 1)
            def _():
                self.copy(way, hop).start()

    def end(self, result, first_column, squares):
        last = self.length - 1
        for copy in self.loads(0, 0):
            copy.wait()
        columns = pl.ds(first_column, self.total.shape[1])

        def finish(ways):
            for way in ways:
                self.copy(way, last).wait_recv()

            def add(at):
                total = self.total[at].astype(F32)
                for way in ways:
                    total = total + self.got[way][last - 1, at].astype(F32)
                result[at, columns] = total.astype(result.dtype)
                squares[...] += tile_of_squares(total)

            rows_loop(result.shape[0], add)

        above, below = self.far[0] >= 1, self.far[1] >= 1
        pl.when(jnp.logical_and(above, below))(lambda: finish((0, 1)))
        pl.when(jnp.logical_not(above))(lambda: finish((1,)))
        pl.when(jnp.logical_not(below))(lambda: finish((0,)))
        for hop in range(1, self.length):
            for way in (0, 1):

                @pl.when(self.far[way] <= hop - 1)
                def _():
                    self.copy(way, hop).wait_send()


class HeldLine(LineScatter):
    def __init__(self, g, first_column, up_got, down_got, ss, rs):
        y, c, z, x = place()
        self.length = length = g.shape[0]
        self.columns = pl.ds(first_column, up_got.shape[2])
        self.sources, self.g, self.total = (), g, g.at[0, :, self.columns]
        self.got, self.ss, self.rs = (up_got, down_got), ss, rs
        self.to = line_neighbours(length)
        self.far = (z, length - 1 - z)
        self.next = 1

    def term(self, way, hop):
        return self.g.at[self.length - hop if way == 0 else hop, :, self.columns]


def chains_of(cuts):
    whole = sum(cut[2] for cut in cuts)
    left = -(-whole // 256) * 128
    lists = [], []
    for which, first_column, columns in cuts:
        taken = min(columns, left)
        if taken:
            lists[0].append((which, first_column, taken))
        if columns > taken:
            lists[1].append((which, first_column + taken, columns - taken))
        left -= taken
    return lists


class Lines:
    def __init__(self, terms, cuts, length, refs):
        self.chains, self.length = [], length
        for n, cut in enumerate(chains_of(cuts)):
            sources = [(terms[which], first_column, columns) for which, first_column, columns in cut]
            self.chains.append(
                LineScatter(sources, length, *refs[n * LINE_REFS : (n + 1) * LINE_REFS])
            )
        self.queue = [chain for _ in range(1, length) for chain in self.chains]

    def begin(self):
        for chain in self.chains:
            chain.load((1,))
        self.start()
        self.start()
        for chain in self.chains:
            chain.load((*range(2, self.length), 0))

    def start(self):
        if self.queue:
            self.queue.pop(0).start()

    def end(self, result, squares):
        while self.queue:
            self.start()
        squares[...] = jnp.zeros_like(squares)
        at = 0
        for chain in self.chains:
            chain.end(result, at, squares)
            at += chain.total.shape[1]


def lines_scratch(length, rows, cuts):
    return sum(
        (line_scratch(length, rows, sum(cut[2] for cut in chain), len(chain)) for chain in chains_of(cuts)), []
    )


def fold(v):
    return jnp.sum(v.reshape(v.shape[0] // 8, 8, v.shape[1]), axis=0)


def tile_of_squares(v):
    v = fold(v * v)
    part = v[:, :128]
    for n in range(1, v.shape[1] // 128):
        part = part + v[:, n * 128 : (n + 1) * 128]
    if v.shape[1] % 128:
        rest = v[:, v.shape[1] // 128 * 128 :]
        part = part + jnp.concatenate([rest, jnp.zeros((8, 128 - rest.shape[1]), F32)], axis=1)
    return part


def line_scratch(length, rows, columns, sources):
    slots = pltpu.VMEM((length - 1, rows, columns), BF16)
    return [pltpu.VMEM((rows, columns), BF16)] + [slots] * 4 + [
        DMA((2, length, sources)), DMA((2, length)), DMA((2, length))
    ]


def starts(copies):
    for copy in copies:
        copy.start()
    return copies


def waits(copies):
    for copy in copies:
        copy.wait()


def local_copies(pairs, sems):
    return [pltpu.make_async_copy(src, dst, sems.at[n]) for n, (src, dst) in enumerate(pairs)]


def held(*arrays):
    return [pltpu.VMEM(v.shape, v.dtype) for v in arrays]


LINE_REFS = 8
SCATTER_REFS = 7
TILE = jax.ShapeDtypeStruct((8, 128), F32)


def line_neighbours(length):
    y, c, z, x = place()
    return [device(y, c, lax.rem(z + 1, length), x), device(y, c, lax.rem(z + length - 1, length), x)]


def rows_loop(rows, body, start=0, unroll=2):
    @pl.loop(start // 16, (start + rows) // 16, unroll=unroll)
    def _(i):
        body(pl.ds(pl.multiple_of(i * 16, 16), 16))


def turned_tiles(length, pair):
    _, _, z, _ = place()
    for k in range(length):
        for b in range(4):
            yield k * 4 + b, pl.multiple_of((b * length + lax.rem(z + k, length)) * pair, pair)


def load_turned(ref, at, length, pair):
    if pair % 128:
        return ref[at]
    return jnp.concatenate([ref[at, pl.ds(src, pair)] for _, src in turned_tiles(length, pair)], axis=1)


def store_turned(ref, at, value, length, pair):
    if pair % 128:
        ref[at] = value
        return
    for n, dst in turned_tiles(length, pair):
        ref[at, pl.ds(dst, pair)] = value[:, n * pair : (n + 1) * pair]


def inverse_rms(v):
    return lax.rsqrt(jnp.sum(v * v, axis=-1, keepdims=True) * (1.0 / v.shape[-1]) + norm_eps)


def norm_rows_back(v, gain, grad):
    inverse = inverse_rms(v)
    scaled = v * inverse
    moved = grad * gain
    inner = jnp.sum(moved * scaled, axis=-1, keepdims=True) * (1.0 / v.shape[-1])
    return inverse * (moved - scaled * inner), fold(grad * scaled)


def middle_kernel(length, mixed_in, mixer_in, inputs_in, gains_in, w_in, late_in, residual_o, normed_o, w, late, *scratch):
    scatter_refs, (p, low, loc, gs, gr, hs, hr, late_s, late_r, *scratch) = scratch[:SCATTER_REFS], scratch[SCATTER_REFS:]
    mixed, mixer, inputs, gains, residual, load_s, keep_s = scratch
    loads = starts(
        local_copies(
            ((mixed_in, mixed), (mixer_in, mixer), (inputs_in, inputs), (gains_in, gains)), load_s
        )
    )
    greet(gather_peers() + line_neighbours(length))
    hops = LineGather(w, length, hs, hr)
    hops.start(1)
    late_hops = LineGather(late, length, late_s, late_r)
    late_hops.start(1)
    started = [1]
    part = mixed.shape[1]
    rows, width = low.shape

    waits(loads[:2])

    def prepare(i):
        mine = mixed[pl.ds(pl.multiple_of(i * rows, rows), rows)]
        for first_column in range(0, width, 512):
            at = slice(first_column, first_column + 512)
            p[i, :, at] = contract_last(mine, mixer[at, 2 * part :]).astype(BF16)

    def advance():
        if started[0] < length - 1:
            hops.arrive(started[0])
            started[0] += 1
            hops.start(started[0])

    def body(at):
        v = inputs[at].astype(F32) + residual[at]
        residual[at] = v
        low[at] = (v * inverse_rms(v) * gains[1:2]).astype(BF16)

    half = low.shape[0] // 2
    gather = Gather(low, normed_o, loc, gs, gr)
    for name in scatter_steps(p, residual, *scatter_refs, prepare=prepare):
        if name == "late":
            advance()
        if name == "low half":
            waits(loads[2:])
            rows_loop(half, body)
            gather.begin_half(0)
        if name == "high half":
            rows_loop(half, body, half)
            gather.begin_half(1)
    keeps = starts(local_copies(((residual, residual_o),), keep_s))
    gather.middle()
    advance()
    gather.end()
    waits(keeps)
    while started[0] < length - 1:
        advance()
    hops.arrive(length - 1)
    hops.finish()
    late_hops.arrive(1)
    late_hops.finish(1, 1)


def middle(mixed, mixer, inputs, gains, w, late, length, collective_id):
    rows, width = inputs.shape
    return pl.pallas_call(
        functools.partial(middle_kernel, length),
        out_shape=(
            jax.ShapeDtypeStruct((rows, width), F32),
            jax.ShapeDtypeStruct((8, rows, width), BF16),
            jax.ShapeDtypeStruct(w.shape, w.dtype),
            jax.ShapeDtypeStruct(late.shape, late.dtype),
        ),
        in_specs=[ANY] * 6,
        out_specs=(ANY,) * 4,
        scratch_shapes=scatter_scratch(rows // 2, width)
        + [pltpu.VMEM((8, rows, width), BF16), pltpu.VMEM((rows, width), BF16), DMA, DMA((14,)), DMA((14,))]
        + [DMA((2, length))] * 4
        + held(mixed, mixer, inputs, gains)
        + [pltpu.VMEM((rows, width), F32), DMA((4,)), DMA((1,))],
        input_output_aliases={4: 2, 5: 3},
        compiler_params=params(collective_id),
        cost_estimate=pl.CostEstimate(flops=0, bytes_accessed=300 * 2**20, transcendentals=0),
    )(mixed, mixer, inputs, gains, w, late)


def turn_kernel(length, cuts, p, residual_in, above_in, gains_in, mixer_in, *refs):
    parts = 1 + max(cut[0] for cut in cuts)
    terms, refs = refs[:parts], refs[parts:]
    back_o, gain, low_o, dmix_o, sums, squares, *scratch = refs
    scatter_refs, scratch = scratch[:SCATTER_REFS], scratch[SCATTER_REFS:]
    total, low, loc, gs, gr, parts_in, load_s, residual, above, gains, mixer, back, dmix, in_s, keep_s = scratch[:15]
    line_refs = scratch[15:]
    loads = local_copies(
        ((residual_in, residual), (above_in, above), (gains_in, gains), (mixer_in, mixer)), in_s
    )
    greet(gather_peers() + line_neighbours(length))
    line = Lines(terms, cuts, length, line_refs)
    line.begin()
    starts(loads)
    gain[...] = jnp.zeros_like(gain)

    def body(at):
        grad, gain_part = norm_rows_back(residual[at], gains[1:2], total[at])
        grad = above[at].astype(F32) + grad
        back[at] = grad
        low[at] = grad.astype(BF16)
        gain[...] += gain_part

    half = low.shape[0] // 2
    gather = Gather(low, low_o, loc, gs, gr)
    for name in scatter_steps(p, total, *scatter_refs):
        if name in ("early", "late"):
            line.start()
        if name == "low half":
            waits(loads)
            rows_loop(half, body)
            gather.begin_half(0)
        if name == "high half":
            rows_loop(half, body, half)
            gather.begin_half(1)
            line.start()
    keeps = starts(local_copies(((back, back_o),), keep_s))
    rows = low.shape[0]
    part = mixer.shape[1] // 3
    y, c, z, x = place()
    near = (gather.me, gather.bx), (gather.by, rank(y, 1 - c, x))
    rest = (gather.bd, rank(1 - y, 1 - c, x)), (rank(y, 1 - c, 1 - x), rank(1 - y, 1 - c, 1 - x))

    def fetch(blocks, slot):
        copies = []
        for n in (0, 1):
            copies.append(
                pltpu.make_async_copy(low_o.at[blocks[n]], parts_in.at[slot, n], load_s.at[slot, n])
            )
        return copies

    def mix(blocks, slot):
        waits(fetch(blocks, slot))
        lines = parts_in[slot].reshape(2 * rows, parts_in.shape[3])
        both = jnp.dot(lines, mixer[:, 2 * part :], preferred_element_type=F32)
        none = jnp.zeros((rows, dmix.shape[2] - part), F32)
        for n in (0, 1):
            dmix[blocks[n]] = jnp.concatenate([both[n * rows : (n + 1) * rows], none], axis=1)
            pltpu.make_async_copy(dmix.at[blocks[n]], dmix_o.at[blocks[n]], keep_s.at[1 + n + 2 * slot]).start()

    def mixed(blocks, slot):
        for n in (0, 1):
            pltpu.make_async_copy(dmix.at[blocks[n]], dmix_o.at[blocks[n]], keep_s.at[1 + n + 2 * slot]).wait()

    def near_blocks():
        gather.own.wait()
        for copy in gather.last[:2]:
            copy.wait_recv()
        starts(fetch(near[0], 0))
        starts(fetch(near[1], 1))
        mix(near[0], 0)
        mix(near[1], 1)

    gather.middle()
    line.start()
    gather.relays(near_blocks)
    gather.finish(2, own=False)
    for n in (0, 1):
        mixed(near[n], n)
        starts(fetch(rest[n], n))
    for n in (0, 1):
        mix(rest[n], n)
    waits(keeps)
    line.end(sums, squares)
    for n in (0, 1):
        mixed(rest[n], n)


def turn(p, residual, above, gains, mixer, rc, terms, cuts, length, collective_id):
    rows, width = residual.shape
    line_rows, columns = terms[0].shape[1], sum(cut[2] for cut in cuts)
    return pl.pallas_call(
        functools.partial(turn_kernel, length, cuts),
        out_shape=(
            jax.ShapeDtypeStruct((rows, width), F32),
            jax.ShapeDtypeStruct((8, width), F32),
            jax.ShapeDtypeStruct((8, rows, width), BF16),
            jax.ShapeDtypeStruct((8, rows, rc), F32),
            jax.ShapeDtypeStruct((line_rows, columns), BF16),
            TILE,
        ),
        in_specs=[ANY] * (5 + len(terms)),
        out_specs=(ANY, VM, ANY, ANY, VM, VM),
        scratch_shapes=scatter_scratch(rows // 2, width)
        + [pltpu.VMEM((rows, width), F32), pltpu.VMEM((rows, width), BF16), DMA, DMA((14,)), DMA((14,))]
        + [pltpu.VMEM((2, 2, rows, width), BF16), DMA((2, 2))]
        + held(residual, above, gains, mixer)
        + [pltpu.VMEM((rows, width), F32), pltpu.VMEM((8, rows, rc), F32), DMA((4,)), DMA((5,))]
        + lines_scratch(length, line_rows, cuts),
        compiler_params=params(collective_id),
        cost_estimate=pl.CostEstimate(flops=0, bytes_accessed=300 * 2**20, transcendentals=0),
    )(p.reshape(8, rows, width), residual, above, gains, mixer, *terms)


def closing_kernel(
    length, x_in, dmz_in, dproj_in, mixed_in, mixer_in, q, residual_in, block, inputs_in, above_in, gains_in, gp_in,
    grad_out, gain, gates_o, out_out, e_o, sums, squares,
    x_part, dmz_part, g, back, total, o, up_a, down_a, up_b, down_b, gp_got, gp_sum,
    ls, lr, load_s, free, loc, es, er, gate_s, gate_r, move_s, move_r,
    dproj, mixed, mixer, residual, inputs, above, gains, gp, grad_o, out, in_s, keep_s, *scatter_refs,
):
    inflow = starts(
        local_copies(
            (
                (gp_in, gp), (dproj_in, dproj), (mixed_in, mixed), (mixer_in, mixer), (residual_in, residual),
                (inputs_in, inputs), (above_in, above), (gains_in, gains),
            ),
            in_s,
        )
    )
    y, c, z, x = place()
    others = line_peers(length)
    s = 2 * z + x
    owner = x * length + z
    to_z = owner // 2
    to_x = owner - 2 * to_z
    from_z, from_x = lax.rem(s, length), s // length
    moves = jnp.where(jnp.logical_and(to_z == z, to_x == x), 0, 1)
    barrier = pltpu.get_barrier_semaphore()
    for peer in others + plane_peers():
        pl.semaphore_signal(barrier, inc=1, device_id=peer, device_id_type=MESH)

    @pl.when(moves == 1)
    def _():
        pl.semaphore_signal(barrier, inc=1, device_id=device(y, c, to_z, to_x), device_id_type=MESH)
        pl.semaphore_signal(barrier, inc=1, device_id=device(y, c, from_z, from_x), device_id_type=MESH)

    pl.semaphore_wait(barrier, len(others) + 7 + 2 * moves)
    model = mixer.shape[0]
    tokens = dproj.shape[0]
    part = mixed.shape[1]
    columns = x_part.shape[2]
    steps = model // columns
    rows = tokens // steps
    line_rows = g.shape[1]

    def loads(i, slot):
        at = pl.ds(pl.multiple_of(i * columns, columns), columns)
        return (
            pltpu.make_async_copy(x_in.at[:, at], x_part.at[slot], load_s.at[0, slot]),
            pltpu.make_async_copy(dmz_in.at[:, at], dmz_part.at[slot], load_s.at[1, slot]),
        )

    group = steps // 4
    order = (3, 1, 2, 0)

    def fetch(i, slot):
        for copy in loads(i, slot):
            copy.start()

    fetch(order[0] * group, 0)
    inflow[0].wait()
    gate = [
        remote(gp.at[lax.rem(z + k + 1, length)], gp_got.at[k], gate_s.at[k], gate_r.at[k], others[k])
        for k in range(length - 1)
    ]
    split = up_a.shape[2]
    line_a = HeldLine(g, 0, up_a, down_a, ls.at[0], lr.at[0])
    line_b = HeldLine(g, split, up_b, down_b, ls.at[1], lr.at[1])
    queue = [chain for _ in range(1, length) for chain in (line_a, line_b)]

    def advance(times=1):
        for _ in range(times):
            if queue:
                queue.pop(0).start()

    output = scatter_steps(q, total, *scatter_refs)
    next(output)
    copies, own = exchange_steps(block, e_o, loc, es, er)

    def compute(n):
        @pl.loop(0, group)
        def _(j):
            count = n * group + j
            slot = count - count // 2 * 2
            i = order[n] * group + j

            @pl.when(j + 1 < group)
            def _():
                fetch(i + 1, 1 - slot)

            if n < 3:

                @pl.when(j + 1 == group)
                def _():
                    fetch(order[n + 1] * group, 1 - slot)

            for copy in loads(i, slot):
                copy.wait()
            front = contract_first(x_part[slot], dproj[...])
            tail = contract_first(dmz_part[slot], mixed[...])
            k = i * columns // line_rows
            at = pl.ds(pl.multiple_of(i * columns - k * line_rows, columns), columns)
            g[k, at] = jnp.concatenate([front, tail], axis=1).astype(BF16)
            block_of = i * rows // 256
            at = pl.ds(pl.multiple_of(i * rows - block_of * 256, rows), rows)
            mine = dproj[pl.ds(pl.multiple_of(i * rows, rows), rows)]
            for first_column in range(0, model, 512):
                cols = slice(first_column, first_column + 512)
                back[block_of, at, cols] = contract_last(mine, mixer[cols, : 2 * part]).astype(BF16)

    waits(inflow[1:4])
    compute(0)
    next(output)
    compute(1)
    if length == 4:
        advance(2)
    next(output)
    compute(2)
    next(output)
    compute(3)
    if length != 4:
        advance(2)
    for _ in output:
        pass
    for peer in gather_peers():
        pl.semaphore_signal(free, inc=1, device_id=peer, device_id_type=MESH)
    advance()
    pl.semaphore_wait(free, 3)
    incoming = scatter_steps(back, o, *scatter_refs)
    next(incoming)
    pair = out.shape[1] // (4 * length)

    def finish_output(at):
        store_turned(out, at, (residual[at] + total[at]).astype(BF16), length, pair)

    waits(inflow[4:])
    rows_loop(out.shape[0], finish_output)
    keeps = local_copies(((out, out_out), (grad_o, grad_out)), keep_s)
    keeps[0].start()
    for copy in gate:
        copy.wait()
    rows_sum = gp[z]
    for k in range(length - 1):
        rows_sum = rows_sum + gp_got[k]
    gp_sum[...] = rows_sum
    move = pltpu.make_async_remote_copy(
        src_ref=gp_sum, dst_ref=gates_o, send_sem=move_s, recv_sem=move_r,
        device_id=device(y, c, to_z, to_x), device_id_type=MESH,
    )
    pl.when(moves == 1)(lambda: move.start())

    @pl.when(moves == 0)
    def _():
        gates_o[...] = rows_sum

    gain[...] = jnp.zeros_like(gain)

    def finish_grad(at):
        grad, gain_part = norm_rows_back(inputs[at].astype(F32), gains[0:1], o[at])
        store_turned(grad_o, at, above[at] + grad, length, pair)
        gain[...] += gain_part

    half = grad_o.shape[0] // 2
    for name in incoming:
        if name in ("sent", "early", "late"):
            advance()
        if name == "low half":
            rows_loop(half, finish_grad)
        if name == "high half":
            rows_loop(half, finish_grad, half)
            keeps[1].start()
    while queue:
        advance()
    squares[...] = jnp.zeros_like(squares)
    line_a.end(sums, 0, squares)
    line_b.end(sums, split, squares)
    pl.when(moves == 1)(lambda: move.wait())
    waits(keeps)
    for copy in copies:
        copy.wait()
    own.wait()


def closing(x, dmz, dproj, mixed, mixer, q, residual, block, inputs, above, gains, gp, length, collective_id):
    rows, width = residual.shape
    tokens, model = x.shape
    part = mixed.shape[1]
    share = block.shape[0] // 8
    block = block.reshape(8, share, block.shape[1])
    line_rows = model // length
    columns = min(256, line_rows)
    split = -(-3 * part // 256) * 128
    slots_a, slots_b = (pltpu.VMEM((length - 1, line_rows, n), BF16) for n in (split, 3 * part - split))
    pack = gp.shape[1:]
    return pl.pallas_call(
        functools.partial(closing_kernel, length),
        out_shape=(
            jax.ShapeDtypeStruct((rows, width), F32),
            jax.ShapeDtypeStruct((8, width), F32),
            jax.ShapeDtypeStruct(pack, F32),
            jax.ShapeDtypeStruct((rows, width), BF16),
            jax.ShapeDtypeStruct(block.shape, BF16),
            jax.ShapeDtypeStruct((line_rows, 3 * part), BF16),
            TILE,
        ),
        in_specs=[ANY] * 12,
        out_specs=(ANY, VM, VM, ANY, ANY, VM, VM),
        scratch_shapes=[
            pltpu.VMEM((2, tokens, columns), BF16),
            pltpu.VMEM((2, tokens, columns), BF16),
            pltpu.VMEM((length, line_rows, 3 * part), BF16),
            pltpu.VMEM((8, rows, width), BF16),
            pltpu.VMEM((rows, width), F32),
            pltpu.VMEM((rows, width), F32),
            slots_a, slots_a, slots_b, slots_b,
            pltpu.VMEM((length - 1,) + pack, F32),
            pltpu.VMEM(pack, F32),
            DMA((2, 2, length)), DMA((2, 2, length)), DMA((2, 2)), pltpu.SemaphoreType.REGULAR,
            DMA, DMA((7,)), DMA((7,)), DMA((length,)), DMA((length,)), DMA, DMA,
            *held(dproj, mixed, mixer, residual, inputs, above, gains, gp),
            pltpu.VMEM((rows, width), F32),
            pltpu.VMEM((rows, width), BF16),
            DMA((8,)), DMA((2,)),
        ]
        + scatter_scratch(rows // 2, width),
        compiler_params=params(collective_id),
        cost_estimate=pl.CostEstimate(
            flops=10 * tokens * model * dproj.shape[1] // 2, bytes_accessed=350 * 2**20, transcendentals=0
        ),
    )(x, dmz, dproj, mixed, mixer, q.reshape(8, rows, width), residual, block, inputs, above, gains, gp)


def first_kernel(
    length, inputs_in, above_in, mixer_in, mlp_in, gains_in, gate_in, chan_in,
    normed_o, wm_o, wf_o, wd_o, w2, gains_o, gate_o, chan_o, inputs_o, above_o,
    inputs, above, mixer_w, mlp_w, gains_w, gate_w, chan_w, load_s,
    gp_o, gn, gp, normed, gn_all, wm, wf, wd, loc, ms, mr, fs, fr, line_s, line_r, gain_s, gain_r, move_s, move_r,
    gather_s, gather_r, hop_s, hop_r,
):
    loads = [
        pltpu.make_async_copy(src, dst, load_s.at[n])
        for n, (src, dst) in enumerate(
            (
                (gains_in, gains_w), (gate_in, gate_w), (chan_in, chan_w), (mixer_in, mixer_w),
                (mlp_in, mlp_w), (inputs_in, inputs), (above_in, above),
            )
        )
    ]
    for copy in loads:
        copy.start()
    y, c, z, x = place()
    s = 2 * z + x
    me = rank(y, c, x)
    rows, width = inputs.shape
    pair = width // (4 * length)
    line = line_peers(length)
    plane = plane_peers()
    to_z, to_x = lax.rem(s, length), s // length
    moves = jnp.where(jnp.logical_and(to_z == z, to_x == x), 0, 1)
    src = x * length + z
    from_z = src // 2
    from_x = src - 2 * from_z
    barrier = pltpu.get_barrier_semaphore()
    for peer in line + plane:
        pl.semaphore_signal(barrier, inc=1, device_id=peer, device_id_type=MESH)

    @pl.when(moves == 1)
    def _():
        pl.semaphore_signal(barrier, inc=1, device_id=device(y, c, to_z, to_x), device_id_type=MESH)
        pl.semaphore_signal(barrier, inc=1, device_id=device(y, c, from_z, from_x), device_id_type=MESH)

    def fill(pack, source, js, offset=0):
        part = pack.shape[2] // len(js)
        whole = source.shape[1] // 24
        for t in range(8):
            for n, j in enumerate(js):
                start = (j * 8 + t) * whole + offset
                pack[t, :, n * part : (n + 1) * part] = source[:, start : start + part].astype(BF16)

    loads[3].wait()
    fill(wm, mixer_w, (0, 1, 2))
    for copy in loads[:3]:
        copy.wait()
    share = gains_w.shape[1]
    gn[...] = jnp.zeros_like(gn)
    for n in (0, 1):

        @pl.when(x == n)
        def _():
            gn[:2, n * share : (n + 1) * share] = gains_w[...]

    gp[...] = jnp.zeros_like(gp)
    channels = contract_first(chan_w[...].astype(BF16), unit(8))
    gp[: gate_w.shape[0]] = jnp.concatenate(
        [
            gate_w[...],
            channels,
            jnp.zeros((gate_w.shape[0], gp.shape[1] - gate_w.shape[1] - 8), F32),
        ],
        axis=1,
    ).astype(BF16)
    gn_all[me, z] = gn[...]
    pl.semaphore_wait(barrier, len(line) + len(plane) + 2 * moves)
    gains = [
        remote(gn, gn_all.at[me, z], line_s.at[0, k], line_r.at[0, k], line[k]) for k in range(length - 1)
    ]
    gate_move = pltpu.make_async_remote_copy(
        src_ref=gp, dst_ref=gp_o.at[to_z], send_sem=move_s, recv_sem=move_r,
        device_id=device(y, c, to_z, to_x), device_id_type=MESH,
    )
    gate_stay = pltpu.make_async_copy(gp, gp_o.at[z], loc.at[2])
    pl.when(moves == 1)(lambda: gate_move.start())
    pl.when(moves == 0)(lambda: gate_stay.start())

    mixer, mixer_own = exchange_steps(wm, wm_o.at[0], loc.at[0], ms, mr)
    hops = LineGather(wm_o, length, hop_s, hop_r)
    mixer_own.wait()
    hops.start_piece(me)

    def pass_piece(n):
        fy, fc, fx = FLIPS[n]
        mixer[n].wait_recv()
        hops.start_piece(rank(flip(y, fy), flip(c, fc), flip(x, fx)))

    pass_piece(1)
    for copy in gains:
        copy.wait()
    spread = [
        remote(gn_all.at[me], gn_all.at[me], gain_s.at[n], gain_r.at[n], plane[n]) for n in range(7)
    ]
    loads[4].wait()
    fill(wd, mlp_w, (2,))
    down, down_own = exchange_steps(wd, wd_o.at[0], loc.at[4], fs.at[1], fr.at[1])
    for n in (0, 2, 3, 5, 4, 6):
        pass_piece(n)
    fill(wf, mlp_w, (0, 1))
    feed, feed_own = exchange_steps(wf, wf_o.at[0], loc.at[3], fs.at[0], fr.at[0])
    pl.when(moves == 1)(lambda: gate_move.wait())
    pl.when(moves == 0)(lambda: gate_stay.wait())
    gates = [
        remote(gp_o.at[z], gp_o.at[z], line_s.at[1, k], line_r.at[1, k], line[k])
        for k in range(length - 1)
    ]
    fill(w2, mlp_w, (0, 1, 2), wd.shape[2])
    for copy in spread:
        copy.wait()
    for k in range(length):
        other = lax.rem(z + k, length)
        for b in range(4):
            at = slice((4 * k + b) * pair, (4 * k + b + 1) * pair)
            tile = (gn_all[2 * b, other] + gn_all[2 * b + 1, other])[:, :pair]
            gains_o[:, at] = tile.astype(BF16).astype(F32)
    for copy in mixer:
        copy.wait_send()

    def body(at):
        v = load_turned(inputs, at, length, pair)
        inputs_o[at] = v
        v = v.astype(F32)
        normed[at] = (v * inverse_rms(v) * gains_o[0:1]).astype(BF16)
        above_o[at] = load_turned(above, at, length, pair)

    for copy in loads[5:]:
        copy.wait()
    half = rows // 2
    gather = Gather(normed, normed_o, loc.at[1], gather_s, gather_r)
    rows_loop(half, body)
    gather.begin_half(0)
    rows_loop(half, body, half)
    gather.begin_half(1)
    hops.arrive(1)
    if length > 2:
        hops.start(2)
    gather.middle()
    if length > 3:
        hops.arrive(2)
        hops.start(3)
    gather.relays()
    for hop in range(min(3, length - 1), length):
        hops.arrive(hop)
        if hop + 1 < length:
            hops.start(hop + 1)
    gather.finish()
    for copy in gates:
        copy.wait()
    gate_rows, columns = gate_w.shape
    head = columns // 2
    own = jnp.concatenate([gp_o[n, :gate_rows].astype(F32) for n in range(length)]).astype(BF16)
    part, rc = own.shape[0], gate_o.shape[0]
    gate_o[...] = jnp.zeros_like(gate_o)
    for first_row in range(0, part, head):
        at = slice(first_row, first_row + head)
        wide = [jnp.zeros((head, first_row), F32)] if first_row else []
        for n in (0, 1):
            block = own[at, n * head : (n + 1) * head].astype(F32)
            rest = jnp.zeros((head, rc - first_row - head), F32)
            gate_o[at, n * rc : (n + 1) * rc] = jnp.concatenate([*wide, block, rest], axis=1).astype(BF16)
    rows_of = contract_last(unit(8), own[:, columns : columns + 8])
    lam = rows_of[7:8]
    u = jnp.exp(-jnp.abs(lam))
    t = u / (2.0 + u)
    series = jnp.full_like(t, 1.0 / 17.0)
    for n in range(15, 0, -2):
        series = series * t * t + 1.0 / n
    rate = 8.0 * (jnp.maximum(-lam, 0.0) + 2.0 * t * series)
    fill_rows = jnp.concatenate([jnp.zeros((7, rc - part), F32), jnp.ones((1, rc - part), F32)])
    chan_o[...] = jnp.concatenate([jnp.concatenate([rows_of[:7], rate]), fill_rows], axis=1)
    for copy in down + feed:
        copy.wait()
    down_own.wait()
    feed_own.wait()
    hops.finish()


def early(f8):
    return f8 // 384 * 256


def unit(n):
    return (
        lax.broadcasted_iota(jnp.int32, (n, n), 0) == lax.broadcasted_iota(jnp.int32, (n, n), 1)
    ).astype(BF16)


def first(inputs, above, mixer, mlp, gains, gate, chan, rc, length, collective_id):
    rows, width = inputs.shape
    pack = (-(-gate.shape[0] // 16) * 16, rc)
    share = mixer.shape[0]
    f8 = mlp.shape[1] // 24
    wm, wf, wd, w2 = (
        (8, share, n) for n in (mixer.shape[1] // 8, 2 * early(f8), early(f8), 3 * (f8 - early(f8)))
    )
    low = jax.ShapeDtypeStruct((rows, width), BF16)
    return pl.pallas_call(
        functools.partial(first_kernel, length),
        out_shape=(
            jax.ShapeDtypeStruct((8, rows, width), BF16),
            jax.ShapeDtypeStruct((length,) + wm, BF16),
            jax.ShapeDtypeStruct((length,) + wf, BF16),
            jax.ShapeDtypeStruct((length,) + wd, BF16),
            jax.ShapeDtypeStruct(w2, BF16),
            jax.ShapeDtypeStruct((8, width), F32),
            jax.ShapeDtypeStruct((rc, 2 * rc), BF16),
            jax.ShapeDtypeStruct((8, rc), F32),
            low,
            low,
        ),
        in_specs=[ANY] * 7,
        out_specs=(ANY, ANY, ANY, ANY, VM, VM, VM, VM, VM, VM),
        scratch_shapes=[
            *[pltpu.VMEM(v.shape, v.dtype) for v in (inputs, above, mixer, mlp, gains, gate, chan)],
            DMA((7,)),
            pltpu.VMEM((length,) + pack, BF16),
            pltpu.VMEM((8, 128), F32),
            pltpu.VMEM(pack, BF16),
            pltpu.VMEM((rows, width), BF16),
            pltpu.VMEM((8, length, 8, 128), F32),
            pltpu.VMEM(wm, BF16),
            pltpu.VMEM(wf, BF16),
            pltpu.VMEM(wd, BF16),
            DMA((5,)), DMA((7,)), DMA((7,)), DMA((2, 7)), DMA((2, 7)),
            DMA((2, length)), DMA((2, length)), DMA((7,)), DMA((7,)), DMA, DMA,
            DMA((14,)), DMA((14,)), DMA((2, length)), DMA((2, length)),
        ],
        compiler_params=params(collective_id),
        cost_estimate=pl.CostEstimate(flops=0, bytes_accessed=300 * 2**20, transcendentals=0),
    )(inputs, above, mixer, mlp, gains, gate, chan)


def last_kernel(
    length, share, wm, gain, gain_two, gates, sq_a, sq_b, sq_c, sq_d,
    wm_o, gains_o, norm_o, factor_o, by_plane, by_line, loc, ss, rs, gs, gr, ls, lr,
):
    y, c, z, x = place()
    me = rank(y, c, x)
    line = line_peers(length)
    plane = plane_peers()
    width = gain.shape[1]
    pair = width // (4 * length)
    squares = sq_a[...] + sq_b[...] + sq_c[...] + sq_d[...] + tile_of_squares(gates[...])
    squares = jnp.concatenate([squares, jnp.zeros((8, width - 128), F32)], axis=1)
    rows = [jnp.sum(v, axis=0, keepdims=True) for v in (gain[...], gain_two[...], squares)]
    by_plane[me] = jnp.concatenate(rows + [jnp.zeros((1, width), F32)])
    greet(line + plane)
    sends = [
        remote(by_plane.at[me], by_plane.at[me], gs.at[n], gr.at[n], plane[n]) for n in range(7)
    ]
    copies, own = exchange_steps(wm, wm_o, loc, ss, rs)
    for copy in sends:
        copy.wait()
    total = by_plane[0]
    for n in range(1, 8):
        total = total + by_plane[n]
    group = 4 * pair
    for k in range(length):
        at = pl.ds(pl.multiple_of(lax.rem(z + k, length) * group, group), group)
        by_line[z, :, at] = total[:, k * group : (k + 1) * group]
    sends = [
        remote(by_line.at[z], by_line.at[z], ls.at[k], lr.at[k], line[k]) for k in range(length - 1)
    ]
    for copy in sends:
        copy.wait()
    total = by_line[0]
    for n in range(1, length):
        total = total + by_line[n]
    squares = jnp.sum(total[:2] * total[:2], axis=0, keepdims=True) + total[2:3]
    norm = jnp.broadcast_to(jnp.sqrt(jnp.sum(squares, axis=1, keepdims=True)), (8, 128))
    norm_o[...] = norm
    factor_o[...] = clip_limit / jnp.maximum(norm, clip_limit)
    gains = jnp.zeros((2, pair), F32)
    for there in range(length):
        for b in range(4):
            first_lane = (there * 4 + b) * pair
            mine = jnp.logical_and(there == z, b == 2 * y + c)
            gains = jnp.where(mine, total[:2, first_lane : first_lane + pair], gains)
    gains_o[...] = jnp.where(x == 0, gains[:, :share], gains[:, share:])
    for copy in copies:
        copy.wait()
    own.wait()


def last(wm, gain, gain_two, gates, squares, length, collective_id):
    width = gain.shape[1]
    share = wm.shape[1]
    return pl.pallas_call(
        functools.partial(last_kernel, length, share),
        out_shape=(
            jax.ShapeDtypeStruct(wm.shape, wm.dtype),
            jax.ShapeDtypeStruct((2, share), F32),
            TILE, TILE,
        ),
        in_specs=[ANY] + [VM] * 7,
        out_specs=(ANY,) + (VM,) * 3,
        scratch_shapes=[
            pltpu.VMEM((8, 4, width), F32),
            pltpu.VMEM((length, 4, width), F32),
            DMA, DMA((7,)), DMA((7,)), DMA((7,)), DMA((7,)),
            DMA((length,)), DMA((length,)),
        ],
        compiler_params=params(collective_id),
    )(wm, gain, gain_two, gates, *squares)


def minus_expm1(v):
    series = 1.0 + v * (1.0 / 8.0)
    for n in (7.0, 6.0, 5.0, 4.0, 3.0, 2.0):
        series = 1.0 + series * v * (1.0 / n)
    return jnp.where(v > -0.5, -v * series, 1.0 - jnp.exp(v))


def gelu_parts(v):
    inner = jnp.tanh(GELU_SCALE * (v + 0.044715 * v * v * v))
    return 0.5 * v * (1.0 + inner), inner


def gelu_slope(v, inner):
    return 0.5 * (1.0 + inner) + 0.5 * v * (1.0 - inner * inner) * GELU_SCALE * (
        1.0 + 3.0 * 0.044715 * v * v
    )


CHUNK = 64


def forward_kernel(
    length, x_in, mixer, gate, chan, above, w2, w_in,
    mixed, branch_o, decay_o, width_o, recur_o, enter_o, conv_o, xe_o, se_o, ends_o, above_o, w2_o, w,
    x_part, pre, loc_h, ends, carry, hs, hr, es, er, gather_l, gather_s, gather_r, hop_s, hop_r, load_s, keep_s, w2_l, w2_s, w2_r,
    branch, decay_k, width_k, recur_k, enter_k, conv_k, xe, se,
):
    keeps = [
        pltpu.make_async_copy(src, dst, keep_s.at[n])
        for n, (src, dst) in enumerate(
            (
                (branch, branch_o), (decay_k, decay_o), (width_k, width_o), (recur_k, recur_o),
                (enter_k, enter_o), (conv_k, conv_o), (xe, xe_o), (se, se_o),
            )
        )
    ]
    y, c, z, x = place()
    line = line_peers(length)
    seqs, span, rc = branch.shape
    part = mixed.shape[2]
    rows = x_part.shape[1]
    chunks = span // CHUNK

    def load(n, slot):
        half = 1 - n // seqs
        b = n - n // seqs * seqs
        at = pl.ds(pl.multiple_of((b * 2 + half) * rows, rows), rows)
        return pltpu.make_async_copy(x_in.at[at], x_part.at[slot], load_s.at[slot])

    load(0, 0).start()
    greet(line + plane_peers())
    hops = LineGather(w, length, hop_s, hop_r)
    hops.start(1)
    gather = Gather(above, above_o, gather_l, gather_s, gather_r)
    gather.begin()
    shares, share_own = exchange_steps(w2, w2_o.at[0], w2_l, w2_s, w2_r)

    def project(n):
        slot = n - n // 2 * 2

        @pl.when(n + 1 < 2 * seqs)
        def _():
            load(n + 1, 1 - slot).start()

        load(n, slot).wait()
        both = jnp.dot(x_part[slot], mixer[:, : 2 * part], preferred_element_type=F32)
        none = jnp.zeros((rows, rc - part), F32)
        half = 1 - n // seqs
        b = n - n // seqs * seqs
        at = pl.multiple_of(half * rows, rows)
        branch[b, pl.ds(at, rows)] = jnp.concatenate([both[:, :part], none], axis=1)
        low = both[:, part:].astype(BF16).astype(F32)
        xe[b, pl.ds(at + 8, rows)] = jnp.concatenate([low, none], axis=1)

    pl.loop(0, seqs)(project)
    ahead = device(y, c, lax.rem(z + 1, length), x)
    halo = remote(xe.at[:, pl.ds(span, 8)], xe.at[:, pl.ds(0, 8)], hs, hr, ahead)
    pl.loop(seqs, 2 * seqs)(project)

    def coefficients(b, chunk):
        r = pl.multiple_of(chunk * CHUNK, CHUNK)
        at = pl.ds(r, CHUNK)
        window = xe[b, pl.ds(r, CHUNK + 8)]
        total = chan[4:5] + chan[0:1] * window[8:]
        for k in (1, 2, 3):
            total = total + chan[k : k + 1] * pltpu.roll(window, k, 0)[8:]
        low = total.astype(BF16)
        conv_k[b, at] = low
        value = low.astype(F32)
        gates = jnp.dot(low, gate[...], preferred_element_type=F32)
        recur = jax.nn.sigmoid(gates[:, :rc] + chan[5:6])
        enter = jax.nn.sigmoid(gates[:, rc:] + chan[6:7])
        log_decay = -chan[7:8] * recur
        decay = jnp.exp(log_decay)
        width = jnp.sqrt(minus_expm1(2.0 * log_decay))
        recur_k[b, at] = recur
        enter_k[b, at] = enter
        decay_k[b, at] = decay
        width_k[b, at] = width
        loc_h[b, at] = width * enter * value

    def later_chunks(i):
        b = i // (chunks - 1)
        coefficients(b, 1 + i - b * (chunks - 1))

    many = seqs * (chunks - 1)
    pl.loop(0, many // 2)(later_chunks)
    hops.arrive(1)
    if length > 2:
        hops.start(2)
    pl.loop(many // 2, many)(later_chunks)
    halo.wait()

    @pl.when(z == 0)
    def _():
        xe[:, 0:8] = jnp.zeros((seqs, 8, rc), F32)

    @pl.loop(0, seqs)
    def _(b):
        coefficients(b, 0)

    for copy in keeps[:-1]:
        copy.start()
    row = lax.broadcasted_iota(jnp.int32, (8, rc), 0)

    def tile(i, held):
        at = pl.ds(pl.multiple_of(i * 8, 8), 8)
        new = []
        for b in range(seqs):
            a, h = decay_k[b, at], loc_h[b, at]
            for n in (1, 2, 4):
                keep = row >= n
                h = h + jnp.where(keep, a * pltpu.roll(h, n, 0), 0.0)
                a = jnp.where(keep, a * pltpu.roll(a, n, 0), a)
            h = h + a * held[b][1]
            a = a * held[b][0]
            loc_h[b, at] = h
            pre[b, at] = a
            new.append((a[7:8], h[7:8]))
        return tuple(new)

    one, zero = jnp.ones((1, rc), F32), jnp.zeros((1, rc), F32)
    final = lax.fori_loop(0, span // 8, tile, ((one, zero),) * seqs)
    for b in range(seqs):
        ends[z, 0, b] = jnp.broadcast_to(final[b][0], (8, rc))
        ends[z, 1, b] = jnp.broadcast_to(final[b][1], (8, rc))
        ends_o[b] = jnp.broadcast_to(final[b][0], (8, rc))
    moves = [remote(ends.at[z], ends.at[z], es.at[k], er.at[k], line[k]) for k in range(length - 1)]
    if length > 3:
        hops.arrive(2)
        hops.start(3)
    for copy in moves:
        copy.wait()
    gather.middle()
    carry[...] = jnp.zeros_like(carry)
    for k in range(length):
        carry[...] = jnp.where(k < z, ends[k, 0] * carry[...] + ends[k, 1], carry[...])

    for b in range(seqs):
        se[b, 0:8] = carry[b]

    @pl.loop(0, seqs * chunks)
    def _(i):
        b = i // chunks
        r = pl.multiple_of((i - b * chunks) * CHUNK, CHUNK)
        at = pl.ds(r, CHUNK)
        state = loc_h[b, at] + pre[b, at] * carry[b, 0:1]
        se[b, pl.ds(r + 8, CHUNK)] = state
        gelu, _ = gelu_parts(branch[b, at])
        mixed[b, at] = (state * gelu)[:, :part].astype(BF16)

    keeps[-1].start()
    gather.end()
    for hop in range(min(3, length - 1), length):
        hops.arrive(hop)
        if hop + 1 < length:
            hops.start(hop + 1)
    hops.finish()
    for copy in keeps + shares:
        copy.wait()
    share_own.wait()


def recur_forward(x, mixer, gate, chan, above, w2, w, length, collective_id):
    rc = gate.shape[0]
    part = mixer.shape[1] // 3
    rows = x.shape[0] // 8
    seqs, span = 4, 2 * rows
    full = jax.ShapeDtypeStruct((seqs, span, rc), F32)
    longer = jax.ShapeDtypeStruct((seqs, span + 8, rc), F32)
    kept = (full, full, full, full, full, jax.ShapeDtypeStruct((seqs, span, rc), BF16), longer, longer)
    return pl.pallas_call(
        functools.partial(forward_kernel, length),
        out_shape=(
            jax.ShapeDtypeStruct((seqs, span, part), BF16),
            *kept,
            jax.ShapeDtypeStruct((seqs, 8, rc), F32),
            jax.ShapeDtypeStruct((8,) + above.shape, above.dtype),
            jax.ShapeDtypeStruct((length,) + w2.shape, w2.dtype),
            jax.ShapeDtypeStruct(w.shape, w.dtype),
        ),
        in_specs=[ANY, VM, VM, VM, ANY, ANY, ANY],
        out_specs=(VM,) + (ANY,) * 8 + (VM, ANY, ANY, ANY),
        scratch_shapes=[
            pltpu.VMEM((2, rows, x.shape[1]), BF16),
            pltpu.VMEM((seqs, span, rc), F32),
            pltpu.VMEM((seqs, span, rc), F32),
            pltpu.VMEM((length, 2, seqs, 8, rc), F32),
            pltpu.VMEM((seqs, 8, rc), F32),
            DMA, DMA, DMA((length,)), DMA((length,)),
            DMA, DMA((14,)), DMA((14,)), DMA((2, length)), DMA((2, length)),
            DMA((2,)), DMA((8,)), DMA, DMA((7,)), DMA((7,)),
            *[pltpu.VMEM(v.shape, v.dtype) for v in kept],
        ],
        input_output_aliases={6: 12},
        compiler_params=params(collective_id),
        cost_estimate=pl.CostEstimate(
            flops=2 * seqs * span * rc * rc * 2, bytes_accessed=100 * 2**20, transcendentals=0
        ),
    )(x, mixer, gate, chan, above, w2, w)


def backward_kernel(
    length, cuts, head, dmix, gate, chan, decay, width, recur, enter, conv, xe, se, ends_f, proj, block_a, block_b, *refs
):
    parts = 1 + max(cut[0] for cut in cuts)
    terms, refs = refs[:parts], refs[parts:]
    dproj, gates_o, sums, squares, block_ao, block_bo, *refs = refs
    dgate, gchan, *refs = refs
    suffix, grad, de, ends, carry, hs, hr, es, er, keep_s, move_l, move_s, move_r, *refs = refs
    kept, line_refs = refs[:8], refs[8:]
    loads = [
        pltpu.make_async_copy(src, dst, keep_s.at[n])
        for n, (src, dst) in enumerate(
            zip((dmix, proj, se, decay, width, recur, enter, conv, xe), (de.at[:, pl.ds(0, decay.shape[1])], *kept))
        )
    ]
    proj, se, decay, width, recur, enter, conv, xe = kept
    y, c, z, x = place()
    line = line_peers(length)
    greet(line + plane_peers())
    scatter = Lines(terms, cuts, length, line_refs)
    scatter.begin()
    for copy in loads:
        copy.start()
    moves = [
        exchange_steps(block_a, block_ao, move_l.at[0], move_s.at[0], move_r.at[0]),
        exchange_steps(block_b, block_bo, move_l.at[1], move_s.at[1], move_r.at[1]),
    ]
    seqs, span, rc = decay.shape
    part = dproj.shape[2] // 2
    chunks = span // CHUNK
    for copy in loads[:3]:
        copy.wait()

    @pl.loop(0, seqs * chunks)
    def _(i):
        b = i // chunks
        r = pl.multiple_of((i - b * chunks) * CHUNK, CHUNK)
        at = pl.ds(r, CHUNK)
        branch = proj[b, at]
        gelu, inner = gelu_parts(branch)
        above = de[b, at]
        state = se[b, pl.ds(r + 8, CHUNK)]
        grad[b, at] = above * gelu
        proj[b, at] = above * state * gelu_slope(branch, inner)

    loads[3].wait()
    row = lax.broadcasted_iota(jnp.int32, (8, rc), 0)

    def tile(i, held):
        at = pl.ds(pl.multiple_of(span - 8 - i * 8, 8), 8)
        new = []
        for b in range(seqs):
            product, total, following = held[b]
            plain, h = decay[b, at], grad[b, at]
            a = jnp.where(row == 7, following, pltpu.roll(plain, 7, 0))
            for n in (1, 2, 4):
                keep = row < 8 - n
                h = h + jnp.where(keep, a * pltpu.roll(h, 8 - n, 0), 0.0)
                a = jnp.where(keep, a * pltpu.roll(a, 8 - n, 0), a)
            h = h + a * total
            a = a * product
            grad[b, at] = h
            suffix[b, at] = a
            new.append((a[0:1], h[0:1], plain[0:1]))
        return tuple(new)

    one, zero = jnp.ones((1, rc), F32), jnp.zeros((1, rc), F32)
    final = lax.fori_loop(0, span // 8, tile, ((one, zero, one),) * seqs)
    for b in range(seqs):
        ends[z, 0, b] = ends_f[b]
        ends[z, 1, b] = jnp.broadcast_to(final[b][1] * final[b][2], (8, rc))
    tails = [remote(ends.at[z], ends.at[z], es.at[k], er.at[k], line[k]) for k in range(length - 1)]
    for copy in tails:
        copy.wait()
    scatter.start()
    scatter.start()
    for copy in loads[4:]:
        copy.wait()
    carry[...] = jnp.zeros_like(carry)
    for k in reversed(range(length)):
        carry[...] = jnp.where(k > z, ends[k, 0] * carry[...] + ends[k, 1], carry[...])

    gchan[...] = jnp.zeros_like(gchan)

    @pl.loop(0, seqs * chunks)
    def _(i):
        b = i // chunks
        r = pl.multiple_of((i - b * chunks) * CHUNK, CHUNK)
        at = pl.ds(r, CHUNK)
        g = grad[b, at] + suffix[b, at] * carry[b, 0:1]
        a, w, ra, ri = decay[b, at], width[b, at], recur[b, at], enter[b, at]
        value = conv[b, at].astype(F32)
        before = pltpu.roll(se[b, pl.ds(r, CHUNK + 8)], 1, 0)[8:]
        dla = g * before * a - g * ri * value * (a * a) / w
        slope = dla * ra * (1.0 - ra)
        dpa = (-chan[7:8] * slope).astype(BF16)
        dpi = (g * w * value * ri * (1.0 - ri)).astype(BF16)
        dgate[b, at, :rc] = dpa
        dgate[b, at, rc:] = dpi
        gchan[5] += fold(dpa.astype(F32))
        gchan[6] += fold(dpi.astype(F32))
        gchan[7] += fold(dla * ra)
        back = lax.dot_general(
            dgate[b, at], gate[...], (((1,), (1,)), ((), ())), preferred_element_type=F32
        )
        dcv = (g * w * ri + back).astype(BF16).astype(F32)
        de[b, at] = dcv
        gchan[4] += fold(dcv)

    behind = device(y, c, lax.rem(z + length - 1, length), x)
    halo = remote(de.at[:, pl.ds(0, 8)], de.at[:, pl.ds(span, 8)], hs, hr, behind)
    halo.wait()
    scatter.start()
    scatter.start()
    low = conv[...].reshape(seqs * span, rc)
    recur_grad, enter_grad = (
        contract_first(low, dgate[:, :, at].reshape(seqs * span, rc)) for at in (slice(0, rc), slice(rc, 2 * rc))
    )

    @pl.when(z == length - 1)
    def _():
        de[:, span:] = jnp.zeros((seqs, 8, rc), F32)

    @pl.loop(0, seqs * chunks)
    def _(i):
        b = i // chunks
        r = pl.multiple_of((i - b * chunks) * CHUNK, CHUNK)
        at = pl.ds(r, CHUNK)
        window = de[b, pl.ds(r, CHUNK + 8)]
        inputs = xe[b, pl.ds(r, CHUNK + 8)]
        dcv = window[:CHUNK]
        total = chan[0:1] * dcv
        gchan[0] += fold(dcv * inputs[8:])
        for k in (1, 2, 3):
            total = total + chan[k : k + 1] * pltpu.roll(window, CHUNK + 8 - k, 0)[:CHUNK]
            gchan[k] += fold(dcv * pltpu.roll(inputs, k, 0)[8:])
        dproj[b, at] = jnp.concatenate([proj[b, at, :part], total[:, :part]], axis=1).astype(BF16)

    rates = 8.0 * minus_expm1(chan[7:8] * (-1.0 / 8.0))
    channels = [jnp.sum(gchan[n], axis=0, keepdims=True) for n in range(8)]
    channels[7] = channels[7] * rates
    channels = lax.dot_general(
        jnp.concatenate(channels), unit(8).astype(F32), (((0,), (0,)), ((), ())),
        precision=lax.Precision.HIGHEST, preferred_element_type=F32,
    )
    blocks = []
    for first_row in range(0, part, head):
        at = slice(first_row, first_row + head)
        blocks.append(jnp.concatenate([recur_grad[at, at], enter_grad[at, at]], axis=1))
    pack = jnp.concatenate(
        [jnp.concatenate(blocks), channels[:part], jnp.zeros((part, rc - 2 * head - 8), F32)], axis=1
    )
    rows = part // length
    if rows < gates_o.shape[1]:
        gates_o[...] = jnp.zeros_like(gates_o)
    for n in range(length):
        gates_o[n, :rows] = pack[n * rows : (n + 1) * rows]
    scatter.end(sums, squares)
    for copies, own in moves:
        for copy in copies:
            copy.wait()
        own.wait()


def recur_backward(dmix, gate, chan, kept, part, head, blocks, terms, cuts, length, collective_id):
    proj, decay, width, recur, enter, conv, xe, se, ends = kept
    seqs, span, rc = decay.shape
    gate_pad = -(-(part // length) // 16) * 16
    line_rows, columns = terms[0].shape[1], sum(cut[2] for cut in cuts)
    return pl.pallas_call(
        functools.partial(backward_kernel, length, cuts, head),
        out_shape=(
            jax.ShapeDtypeStruct((seqs, span, 2 * part), BF16),
            jax.ShapeDtypeStruct((length, gate_pad, rc), F32),
            jax.ShapeDtypeStruct((line_rows, columns), BF16), TILE,
            *[jax.ShapeDtypeStruct(block.shape, BF16) for block in blocks],
        ),
        in_specs=[ANY, VM, VM] + [ANY] * 7 + [VM] + [ANY] * (3 + len(terms)),
        out_specs=(VM,) * 4 + (ANY, ANY),
        scratch_shapes=[
            pltpu.VMEM((seqs, span, 2 * rc), BF16),
            pltpu.VMEM((8, 8, rc), F32),
            pltpu.VMEM((seqs, span, rc), F32),
            pltpu.VMEM((seqs, span, rc), F32),
            pltpu.VMEM((seqs, span + 8, rc), F32),
            pltpu.VMEM((length, 2, seqs, 8, rc), F32),
            pltpu.VMEM((seqs, 8, rc), F32),
            DMA, DMA, DMA((length,)), DMA((length,)),
            DMA((9,)), DMA((2,)), DMA((2, 7)), DMA((2, 7)),
            *[
                pltpu.VMEM(shape, dtype)
                for shape, dtype in (
                    (decay.shape, F32), (se.shape, F32), (decay.shape, F32), (decay.shape, F32),
                    (decay.shape, F32), (decay.shape, F32), (decay.shape, BF16), (xe.shape, F32),
                )
            ],
        ]
        + lines_scratch(length, line_rows, cuts),
        compiler_params=params(collective_id),
        cost_estimate=pl.CostEstimate(
            flops=2 * seqs * span * rc * rc * 2, bytes_accessed=120 * 2**20, transcendentals=0
        ),
    )(dmix, gate, chan, decay, width, recur, enter, conv, xe, se, ends, proj, *blocks, *terms)


def contract_last(left, right):
    return lax.dot_general(
        left, right, (((1,), (1,)), ((), ())), preferred_element_type=F32
    )


def contract_first(left, right):
    return lax.dot_general(
        left, right, (((0,), (0,)), ((), ())), preferred_element_type=F32
    )


def resident(shape):
    return pl.BlockSpec(shape, lambda i: (0, 0), pipeline_mode=pl.Buffered(1))


def feed_forward(x, above, gate_up, down, hid, dgate, dup):
    f = hid.shape[1]
    for first_column in range(0, f, 256):
        at = slice(first_column, first_column + 256)
        gg = jnp.dot(x[...], gate_up[:, at], preferred_element_type=F32)
        uu = jnp.dot(x[...], gate_up[:, f + first_column : f + first_column + 256], preferred_element_type=F32)
        dhid = jnp.dot(above[...], down[:, at], preferred_element_type=F32)
        gelu, inner = gelu_parts(gg)
        hid[:, at] = (gelu * uu).astype(BF16)
        dgate[:, at] = (dhid * uu * gelu_slope(gg, inner)).astype(BF16)
        dup[:, at] = (dhid * gelu).astype(BF16)


def grads_compute(x, above, hid, dgate, dup, gate_o, up_o, down_o):
    gate_o[...] = contract_first(x[...], dgate[...]).astype(BF16)
    up_o[...] = contract_first(x[...], dup[...]).astype(BF16)
    down_o[...] = contract_first(above[...], hid[...]).astype(BF16)


def mlp_specs(tokens, model, f):
    def rows(width):
        return pl.BlockSpec((tokens // 8, width), lambda i: (jnp.minimum(i, 7), 0))

    columns = pl.BlockSpec((tokens, model // 8), lambda i: (0, jnp.maximum(i - 8, 0)))
    grads = pl.BlockSpec((model // 8, f), lambda i: (jnp.maximum(i - 8, 0), 0))
    return rows, columns, grads


def keep_units(step, held, outs):
    at = pl.ds(pl.multiple_of(step * outs[0].shape[0], outs[0].shape[0]), outs[0].shape[0])
    for kept, out in zip(held, outs):
        kept[at] = out[...]


def early_mlp_kernel(
    length, x, above, x_columns, above_columns, gate_up, down, w_in,
    hid, dgate, dup, gate_o, up_o, down_o, w, hid_all, dgate_all, dup_all, ss, rs
):
    step = pl.program_id(0)
    hops = LineGather(w, length, ss, rs)

    @pl.when(step == 0)
    def _():
        greet(line_neighbours(length))
        if length > 2:
            hops.start(2)

    @pl.when(step == 7)
    def _():
        for hop in range(2, length - 1):
            hops.arrive(hop)
            hops.start(hop + 1)

    @pl.when(step < 8)
    def _():
        feed_forward(x, above, gate_up, down, hid, dgate, dup)
        keep_units(step, (hid_all, dgate_all, dup_all), (hid, dgate, dup))

    @pl.when(step >= 8)
    def _():
        grads_compute(x_columns, above_columns, hid_all, dgate_all, dup_all, gate_o, up_o, down_o)

    @pl.when(step == 15)
    def _():
        hops.arrive(length - 1)
        hops.finish(2, length - 1)


def early_mlp(x, above, gate_up, down, w, length, collective_id):
    tokens, model = x.shape
    f = down.shape[1]
    rows, columns, grads = mlp_specs(tokens, model, f)
    unit_shape = jax.ShapeDtypeStruct((tokens, f), BF16)
    grad_shape = jax.ShapeDtypeStruct((model, f), BF16)
    return pl.pallas_call(
        functools.partial(early_mlp_kernel, length),
        grid=(16,),
        out_shape=(unit_shape,) * 3 + (grad_shape,) * 3 + (jax.ShapeDtypeStruct(w.shape, w.dtype),),
        in_specs=[rows(model), rows(model), columns, columns, resident(gate_up.shape), resident(down.shape), ANY],
        out_specs=(rows(f),) * 3 + (grads,) * 3 + (ANY,),
        scratch_shapes=[pltpu.VMEM((tokens, f), BF16)] * 3 + [DMA((2, length)), DMA((2, length))],
        input_output_aliases={6: 6},
        compiler_params=params(collective_id),
        cost_estimate=pl.CostEstimate(flops=12 * tokens * model * f, bytes_accessed=50 * 2**20, transcendentals=0),
    )(x, above, x, above, gate_up, down, w)


def late_mlp_kernel(
    length, cuts, x, above, x_columns, above_columns, hid_one, dgate_one, dup_one, gate_up, down, late, *refs
):
    terms, refs = refs[: len(cuts)], refs[len(cuts) :]
    out, back, gate_o, up_o, down_o, sums, squares, hid, dgate, dup, *refs = refs
    (hid_all, dgate_all, dup_all), line_refs = refs[:3], refs[3:]
    step = pl.program_id(0)
    line = LineScatter([(ref, *cut) for ref, cut in zip(terms, cuts)], length, *line_refs)

    @pl.when(step == 0)
    def _():
        greet(line_neighbours(length))
        line.load((1,))
        line.start()
        line.load((*range(2, length), 0))

    for hop in range(2, length):

        @pl.when(step == min(10, 4 * (hop - 1)))
        def _():
            line.next = hop
            line.start()

    f, g = down.shape[1], hid.shape[1]

    @pl.when(step < 8)
    def _():
        feed_forward(x, above, late.at[:, : 2 * g], late.at[:, 2 * g :], hid, dgate, dup)
        keep_units(step, (hid_all, dgate_all, dup_all), (hid, dgate, dup))
        for first_column in range(0, x.shape[1], 512):
            at = slice(first_column, first_column + 512)
            ahead = contract_last(hid_one[...], down[at]) + contract_last(hid[...], late[at, 2 * g :])
            out[:, at] = ahead.astype(BF16)
            both = contract_last(dgate_one[...], gate_up[at, :f]) + contract_last(dup_one[...], gate_up[at, f:])
            both = both + contract_last(dgate[...], late[at, :g]) + contract_last(dup[...], late[at, g : 2 * g])
            back[:, at] = both.astype(BF16)

    @pl.when(step >= 8)
    def _():
        grads_compute(x_columns, above_columns, hid_all, dgate_all, dup_all, gate_o, up_o, down_o)

    @pl.when(step == 15)
    def _():
        squares[...] = jnp.zeros_like(squares)
        line.end(sums, 0, squares)


def late_mlp(x, above, early_units, gate_up, down, late, terms, cuts, length, collective_id):
    tokens, model = x.shape
    f, g = down.shape[1], late.shape[1] // 3
    line_rows = terms[0].shape[1]
    cut = sum(columns for _, columns in cuts)
    rows, columns, grads = mlp_specs(tokens, model, g)

    def whole(shape):
        return pl.BlockSpec(shape, lambda i: (0, 0))

    return pl.pallas_call(
        functools.partial(late_mlp_kernel, length, cuts),
        grid=(16,),
        out_shape=(jax.ShapeDtypeStruct((tokens, model), BF16),) * 2
        + (jax.ShapeDtypeStruct((model, g), BF16),) * 3
        + (jax.ShapeDtypeStruct((line_rows, cut), BF16), TILE),
        in_specs=[rows(model), rows(model), columns, columns]
        + [rows(f)] * 3
        + [resident(v.shape) for v in (gate_up, down, late)]
        + [ANY] * len(terms),
        out_specs=(rows(model),) * 2 + (grads,) * 3 + (whole((line_rows, cut)), whole((8, 128))),
        scratch_shapes=[pltpu.VMEM((tokens // 8, g), BF16)] * 3
        + [pltpu.VMEM((tokens, g), BF16)] * 3
        + line_scratch(length, line_rows, cut, len(cuts)),
        compiler_params=params(collective_id),
        cost_estimate=pl.CostEstimate(
            flops=6 * tokens * model * (f + 3 * g), bytes_accessed=70 * 2**20, transcendentals=0
        ),
    )(x, above, x, above, *early_units, gate_up, down, late, *terms)


def adam_step(weight, grad, first, second, factor, rate, decay_rate):
    clipped = grad * factor
    first_new = beta_first * first + (1.0 - beta_first) * clipped
    second_new = beta_second * second + (1.0 - beta_second) * clipped * clipped
    first_hat = first_new / (1.0 - beta_first**STEP)
    second_hat = second_new / (1.0 - beta_second**STEP)
    weight_new = weight - rate * (
        first_hat / (jnp.sqrt(second_hat) + adam_eps) + decay_rate * weight
    )
    return (first_new, second_new, weight_new)


def small_steps(factor, refs, outs):
    gains_sum, gates_sum, *states = refs
    rows, columns = states[3].shape
    channels = lax.dot_general(
        unit(8).astype(F32), gates_sum[:rows, columns : columns + 8], (((1,), (1,)), ((), ())),
        precision=lax.Precision.HIGHEST, preferred_element_type=F32,
    )
    grads = gains_sum[...], gates_sum[:rows, :columns], channels
    rates = (rate_gains, 0.0), (rate_matrix, decay_matrix), (rate_channel, 0.0)
    for n in range(3):
        w, m, v = states[3 * n : 3 * n + 3]
        results = adam_step(w[...], grads[n], m[...], v[...], factor, *rates[n])
        for out, result in zip(outs[3 * n : 3 * n + 3], results):
            out[...] = result


def adam_kernel(sources, factor, *refs):
    states, refs = refs[: 3 * len(sources)], refs[3 * len(sources) :]
    count = sum(len(source) for source in sources)
    grads, small, refs = refs[:count], refs[count : count + 11], refs[count + 11 :]
    results, outs = refs[:2], refs[2:]
    for result, out in zip(results, outs[-2:]):
        out[...] = result[...]
    one = factor[0:1, 0:1]
    pl.when(pl.program_id(0) == 0)(lambda: small_steps(one, small, outs[3 * len(sources) : -2]))
    for n, source in enumerate(sources):
        parts = []
        for pieces in source:
            ref, *grads = grads
            for first, columns, at, stride in pieces:
                for t in range(8):
                    parts.append((at + t * stride, columns, ref, t, first))
        parts.sort(key=lambda part: part[0])
        w, m, v = states[3 * n : 3 * n + 3]
        m_o, v_o, w_o = outs[3 * n : 3 * n + 3]
        run = []
        for at, columns, ref, t, first in parts:
            run.append((at, columns, ref[t, :, first : first + columns].astype(F32)))
            end = at + columns
            if end % 128:
                continue
            grad = jnp.concatenate([piece for _, _, piece in run], axis=1) if len(run) > 1 else run[0][2]
            cols = slice(run[0][0], end)
            run = []
            first_new, second_new, weight_new = adam_step(
                w[:, cols], grad, m[:, cols], v[:, cols], one, rate_matrix, decay_matrix
            )
            m_o[:, cols] = first_new
            v_o[:, cols] = second_new
            w_o[:, cols] = weight_new


def adam(matrices, small, factor, passed):
    rows = matrices[0][0].shape[0]
    step = min(rows, 16)

    def block(v):
        return pl.BlockSpec((step, v.shape[1]), lambda i: (i, 0))

    def whole(v):
        return pl.BlockSpec(v.shape, lambda i: (0, 0))

    states = [v for matrix in matrices for v in matrix[:3]]
    grads = [g for matrix in matrices for g in matrix[3]]
    results = [*states, *small[2:], *passed]
    steps = rows // step

    def slab(v):
        return pl.BlockSpec((v.shape[0] // steps, v.shape[1]), lambda i: (i, 0))

    return pl.pallas_call(
        functools.partial(adam_kernel, [matrix[4] for matrix in matrices]),
        grid=(steps,),
        out_shape=tuple(jax.ShapeDtypeStruct(v.shape, v.dtype) for v in results),
        in_specs=[pl.BlockSpec((8, 128), lambda i: (0, 0))]
        + [block(v) for v in states]
        + [pl.BlockSpec((8, step, g.shape[2]), lambda i: (0, i, 0)) for g in grads]
        + [whole(v) for v in small]
        + [slab(v) for v in passed],
        out_specs=tuple(block(v) for v in states)
        + tuple(whole(v) for v in small[2:])
        + tuple(slab(v) for v in passed),
        compiler_params=pltpu.CompilerParams(vmem_limit_bytes=VMEM_BYTES),
        cost_estimate=pl.CostEstimate(
            flops=0, bytes_accessed=sum(8 * v.size for v in states), transcendentals=0
        ),
    )(factor, *states, *grads, *small, *passed)


def on_device(
    block_input,
    out_grad,
    norm_gains,
    mixer_weight,
    gate_weight,
    chan_params,
    mlp_weight,
    first_gains,
    first_mixer,
    first_gate,
    first_chan,
    first_mlp,
    second_gains,
    second_mixer,
    second_gate,
    second_chan,
    second_mlp,
):
    length = lax.axis_size("seq") // 2
    z = lax.axis_index("seq") // 2
    tokens, model = block_input.shape[1:]
    share = mixer_weight.shape[0]
    pair = 2 * share
    lru = mixer_weight.shape[1] // 3
    hidden = mlp_weight.shape[1] // 3
    r8, f8 = lru // 8, hidden // 8
    rc = -(-r8 // 128) * 128
    head = gate_weight.shape[1] // 2
    heads = r8 // head
    gate_rows = gate_weight.shape[0]
    gate_pad = -(-gate_rows // 16) * 16

    x = lax.axis_index("seq") - 2 * z
    batch = lax.axis_index("batch")
    plain = pair % 128 == 0

    def turned(v):
        if plain:
            return v
        v = v.reshape(v.shape[0], 4, length, pair).swapaxes(1, 2)
        return jnp.roll(v, -z, axis=1).reshape(v.shape[0], model)

    def turned_back(v):
        if plain:
            return v
        v = jnp.roll(v.reshape(v.shape[0], length, 4, pair), z, axis=1)
        return v.swapaxes(1, 2).reshape(v.shape[0], model)

    normed_one, mixer_full, mlp_gu, mlp_down, late_pack, gains, gate, chan, inputs, above = first(
        turned(block_input[0]),
        turned(out_grad[0]),
        mixer_weight,
        mlp_weight,
        norm_gains,
        gate_weight,
        chan_params,
        rc,
        length,
        1,
    )
    normed_one = normed_one.reshape(8 * tokens, model)
    mixer_full = mixer_full.reshape(model, 3 * r8)
    mixed, *kept, grad_out, late, mlp_down = recur_forward(
        normed_one, mixer_full, gate, chan, above, late_pack, mlp_down, length, 2
    )
    grad_out = grad_out.reshape(8 * tokens, model)
    mixed = mixed.reshape(8 * tokens, r8)
    residual, normed_two, mlp_gu, late = middle(mixed, mixer_full, inputs, gains, mlp_gu, late, length, 3)
    normed_two = normed_two.reshape(8 * tokens, model)
    h1 = early(f8)
    h2 = f8 - h1
    mlp_gu = mlp_gu.reshape(model, 2 * h1)
    mlp_down = mlp_down.reshape(model, h1)
    hid, dgg, duu, *early_terms, late = early_mlp(normed_two, grad_out, mlp_gu, mlp_down, late, length, 9)
    gate_one, up_one, down_one = (v.reshape(length, 8 * share, h1) for v in early_terms)
    cut = h1 // 4
    mlp_part, dnormed_two, *late_terms, sums_zero, squares_zero = late_mlp(
        normed_two, grad_out, (hid, dgg, duu), mlp_gu, mlp_down, late.reshape(model, 3 * h2),
        (gate_one, up_one), ((0, h1), (0, cut)), length, 11,
    )
    gate_two, up_two, down_two = (v.reshape(length, 8 * share, h2) for v in late_terms)

    grad_residual, gain_two, dmz, dmix, sums_one, squares_one = turn(
        dnormed_two, residual, above, gains, mixer_full, rc,
        (up_one, down_one, gate_two), ((0, cut, h1 - cut), (1, 0, h1), (2, 0, h2)),
        length, 4,
    )
    dmz = dmz.reshape(8 * tokens, model)
    span = 2 * tokens
    dmix = dmix.reshape(4, span, rc)
    sums_zero, sums_one = (v.reshape(8, share, v.shape[1]) for v in (sums_zero, sums_one))
    dproj, gate_back, sums_two, squares_two, back_zero, back_one = recur_backward(
        dmix, gate, chan, kept, r8, head, (sums_zero, sums_one),
        (up_two, down_two), ((0, 0, h2), (1, 0, h2)), length, 6,
    )
    dproj = dproj.reshape(4 * span, 2 * r8)
    input_grad, gain_one, gates_sum, block_output, back_two, mixer_sums, squares_three = closing(
        normed_one, dmz, dproj, mixed, mixer_full, mlp_part, residual, sums_two,
        inputs, grad_residual, gains, gate_back, length, 7,
    )
    mixer_back, gains_sum, norm, factor = last(
        mixer_sums.reshape(8, share, 3 * r8), gain_one, gain_two, gates_sum,
        (squares_zero, squares_one, squares_two, squares_three), length, 8,
    )
    mlp_sources = (
        [(0, h1, 0, f8), (h1, cut, hidden, f8)],
        [
            (0, h1 - cut, hidden + cut, f8),
            (h1 - cut, h1, 2 * hidden, f8),
            (2 * h1 - cut, h2, h1, f8),
        ],
        [(0, h2, hidden + h1, f8), (h2, h2, 2 * hidden + h1, f8)],
    )
    states = adam(
        (
            (
                mixer_weight, first_mixer, second_mixer, (mixer_back,),
                ([(n * r8, r8, n * lru, r8) for n in range(3)],),
            ),
            (mlp_weight, first_mlp, second_mlp, (back_zero, back_one, back_two), mlp_sources),
        ),
        (
            gains_sum, gates_sum, norm_gains, first_gains, second_gains, gate_weight, first_gate, second_gate,
            chan_params, first_chan, second_chan,
        ),
        factor,
        (block_output, input_grad),
    )
    *states, block_output, input_grad = states
    mixer_up, mlp_up, gains_up, gate_up, chan_up = (states[3 * n : 3 * n + 3] for n in range(5))
    return (
        turned_back(block_output)[None],
        turned_back(input_grad)[None],
        norm[0, 0],
        *gains_up,
        *mixer_up,
        *gate_up,
        *chan_up,
        *mlp_up,
    )


def solution(mesh):
    rows = P(("batch", "seq"), None)
    columns = P(None, ("batch", "seq"))
    data = P("batch", "seq", None)
    weights = (columns, rows, rows, columns, rows)
    in_specs = (data, data) + weights * 3
    triples = tuple(spec for spec in weights for _ in range(3))
    return jax.shard_map(
        on_device,
        mesh=mesh,
        in_specs=in_specs,
        out_specs=(data, data, P()) + triples,
        check_vma=False,
    )
```

```python
import functools
import math

import jax
import jax.numpy as jnp
from jax import lax
from jax.experimental import pallas as pl
from jax.experimental.pallas import tpu as pltpu
from jax.sharding import PartitionSpec as P

STEP = 10
norm_eps = 1e-06
clip_limit = 1.0
beta_first = 0.9
beta_second = 0.999
adam_eps = 1e-08
rate_matrix = 0.05
rate_gains = 0.8
rate_channel = 2.0
decay_matrix = 0.1

MESH = pl.DeviceIdType.MESH
F32 = jnp.float32
BF16 = jnp.bfloat16
ANY = pl.BlockSpec(memory_space=pl.ANY)
VM = pl.BlockSpec(memory_space=pltpu.VMEM)
FLIPS = [(fy, fc, fx) for fy in (0, 1) for fc in (0, 1) for fx in (0, 1) if fy + fc + fx]
GELU_SCALE = math.sqrt(2.0 / math.pi)
GELU_CUBE = 0.044715 * GELU_SCALE


def place():
    b = lax.axis_index("batch")
    s = lax.axis_index("seq")
    y, z = b // 2, s // 2
    return y, b - 2 * y, z, s - 2 * z


def device(y, c, z, x):
    return (y * 2 + c, z * 2 + x)


def rank(y, c, x):
    return (y * 2 + c) * 2 + x


def flip(v, f):
    return 1 - v if f else v


def greet(peers):
    barrier = pltpu.get_barrier_semaphore()
    for peer in peers:
        pl.semaphore_signal(barrier, inc=1, device_id=peer, device_id_type=MESH)
    pl.semaphore_wait(barrier, len(peers))


def remote(src, dst, send, recv, to):
    copy = pltpu.make_async_remote_copy(
        src_ref=src, dst_ref=dst, send_sem=send, recv_sem=recv, device_id=to, device_id_type=MESH
    )
    copy.start()
    return copy


VMEM_BYTES = 63 * 2**20


def params(collective_id):
    return pltpu.CompilerParams(
        collective_id=collective_id, has_side_effects=True, vmem_limit_bytes=VMEM_BYTES
    )


DMA = pltpu.SemaphoreType.DMA


def gather_peers():
    y, c, z, x = place()
    return [device(y, c, z, 1 - x), device(1 - y, c, z, x), device(y, 1 - c, z, x)]


class Gather:
    def __init__(self, a, o, loc, ss, rs):
        y, c, z, x = place()
        self.to_x, self.to_y, self.to_c = gather_peers()
        self.me, self.bx = rank(y, c, x), rank(y, c, 1 - x)
        self.by, self.bd = rank(1 - y, c, x), rank(1 - y, c, 1 - x)
        half = a.shape[0] // 2
        self.lo, self.hi = pl.ds(0, half), pl.ds(half, half)
        self.a, self.o, self.loc, self.ss, self.rs = a, o, loc, ss, rs
        self.done, self.last = [], []

    def send(self, src, dst, k, to):
        copy = remote(src, dst, self.ss.at[k], self.rs.at[k], to)
        self.done.append(copy)
        return copy

    def relay(self, block, part, k, to):
        return self.send(self.o.at[block, part], self.o.at[block, part], k, to)

    def begin_half(self, half):
        a, o, me = self.a, self.o, self.me
        part = (self.lo, self.hi)[half]
        if half == 0:
            self.s0 = self.send(a.at[part], o.at[me, part], 0, self.to_x)
            self.s3 = self.send(a.at[part], o.at[me, part], 3, self.to_y)
        else:
            self.s1 = self.send(a.at[part], o.at[me, part], 1, self.to_y)
            self.s2 = self.send(a.at[part], o.at[me, part], 2, self.to_x)
        self.last.append(self.send(a.at[part], o.at[me, part], (4, 13)[half], self.to_c))
        if half == 1:
            self.own = pltpu.make_async_copy(a, o.at[me], self.loc)
            self.own.start()

    def begin(self):
        a, o, me, lo, hi = self.a, self.o, self.me, self.lo, self.hi
        self.s0 = self.send(a.at[lo], o.at[me, lo], 0, self.to_x)
        self.s1 = self.send(a.at[hi], o.at[me, hi], 1, self.to_y)
        self.s2 = self.send(a.at[hi], o.at[me, hi], 2, self.to_x)
        self.s3 = self.send(a.at[lo], o.at[me, lo], 3, self.to_y)
        self.last += [self.send(a.at[part], o.at[me, part], k, self.to_c) for part, k in ((lo, 4), (hi, 13))]
        self.own = pltpu.make_async_copy(a, o.at[me], self.loc)
        self.own.start()

    def middle(self):
        self.s0.wait_recv()
        self.s5 = self.relay(self.bx, self.lo, 5, self.to_y)
        self.last.append(self.relay(self.bx, self.lo, 7, self.to_c))
        self.s1.wait_recv()
        self.s6 = self.relay(self.by, self.hi, 6, self.to_x)
        self.last.append(self.relay(self.by, self.hi, 8, self.to_c))

    def relays(self, mark=lambda: None):
        self.s2.wait_recv()
        self.last.append(self.relay(self.bx, self.hi, 9, self.to_c))
        self.s3.wait_recv()
        self.last.append(self.relay(self.by, self.lo, 10, self.to_c))
        mark()
        self.s5.wait_recv()
        self.last.append(self.relay(self.bd, self.lo, 11, self.to_c))
        self.s6.wait_recv()
        self.last.append(self.relay(self.bd, self.hi, 12, self.to_c))

    def finish(self, skip=0, own=True):
        for copy in self.last[skip:]:
            copy.wait_recv()
        for copy in self.done:
            copy.wait_send()
        if own:
            self.own.wait()

    def end(self, mark=lambda: None):
        self.relays(mark)
        self.finish()


def scatter_steps(p, o, mine, sib, part, got, loc, ss, rs, prepare=None):
    y, c, z, x = place()
    to_x, to_y, to_c = gather_peers()
    half = o.shape[0] // 2
    step = 16
    cut = (pl.ds(0, half), pl.ds(half, half))
    where = ((1 - y, 1 - x), (1 - y, x), (y, 1 - x), (y, x))
    order = [(0, 0), (0, 1), (1, 0), (2, 1), (2, 0), (1, 1), (3, 0), (3, 1)]
    from_c, own, sends = {}, {}, []
    for n, (t, h) in enumerate(order):
        ty, tx = where[t]
        if prepare and all(key[0] != t for key in own):
            prepare(rank(ty, c, tx))
            prepare(rank(ty, 1 - c, tx))
        own[t, h] = pltpu.make_async_copy(
            p.at[rank(ty, c, tx), cut[h]], mine.at[t, h], loc.at[n]
        )
        own[t, h].start()
        from_c[t, h] = remote(
            p.at[rank(ty, 1 - c, tx), cut[h]], sib.at[t, h], ss.at[n], rs.at[n], to_c
        )
        sends.append(from_c[t, h])
    yield "begun"

    def add(dst, t, h, extra):
        own[t, h].wait()
        from_c[t, h].wait_recv()

        @pl.loop(0, half // step)
        def _(i):
            at = pl.ds(pl.multiple_of(i * step, step), step)
            total = mine[t, h, at].astype(F32) + sib[t, h, at].astype(F32)
            for ref in extra:
                total = total + ref[at].astype(F32)
            dst[at] = total.astype(dst.dtype)

    def send(k, slot, to):
        copy = remote(part.at[k], got.at[slot], ss.at[8 + k], rs.at[8 + slot], to)
        sends.append(copy)
        return copy

    def arrival(slot):
        return pltpu.make_async_remote_copy(
            src_ref=part.at[0], dst_ref=got.at[slot], send_sem=ss.at[8], recv_sem=rs.at[8 + slot],
            device_id=to_x, device_id_type=MESH,
        )

    add(part.at[0], 0, 0, ())
    send(0, 1, to_y)
    add(part.at[1], 0, 1, ())
    send(1, 3, to_x)
    add(part.at[2], 1, 0, ())
    send(2, 0, to_y)
    add(part.at[3], 2, 1, ())
    send(3, 2, to_x)
    yield "sent"
    arrival(1).wait_recv()
    add(part.at[4], 2, 0, (got.at[1],))
    send(4, 4, to_x)
    yield "early"
    arrival(3).wait_recv()
    add(part.at[5], 1, 1, (got.at[3],))
    send(5, 5, to_y)
    yield "late"
    arrival(0).wait_recv()
    arrival(4).wait_recv()
    add(o.at[cut[0]], 3, 0, (got.at[0], got.at[4]))
    yield "low half"
    arrival(2).wait_recv()
    arrival(5).wait_recv()
    add(o.at[cut[1]], 3, 1, (got.at[2], got.at[5]))
    yield "high half"
    for copy in sends:
        copy.wait_send()


def scatter_scratch(half, width):
    return [
        pltpu.VMEM((4, 2, half, width), BF16),
        pltpu.VMEM((4, 2, half, width), BF16),
        pltpu.VMEM((6, half, width), BF16),
        pltpu.VMEM((6, half, width), BF16),
        DMA((8,)),
        DMA((14,)),
        DMA((14,)),
    ]


def exchange_steps(a, o, loc, ss, rs, columns=None):
    y, c, z, x = place()
    me = rank(y, c, x)
    dst = o.at[me] if columns is None else o.at[me, :, columns]
    copies = []
    for n, (fy, fc, fx) in enumerate(FLIPS):
        ty, tc, tx = flip(y, fy), flip(c, fc), flip(x, fx)
        copies.append(remote(a.at[rank(ty, tc, tx)], dst, ss.at[n], rs.at[n], device(ty, tc, z, tx)))
    own = pltpu.make_async_copy(a.at[me], dst, loc)
    own.start()
    return copies, own


def plane_peers():
    y, c, z, x = place()
    return [device(flip(y, fy), flip(c, fc), z, flip(x, fx)) for fy, fc, fx in FLIPS]


def line_peers(length):
    y, c, z, x = place()
    return [device(y, c, lax.rem(z + k, length), x) for k in range(1, length)]


class LineGather:
    def __init__(self, buf, length, ss, rs):
        y, c, z, x = place()
        self.z, self.length, self.buf, self.ss, self.rs = z, length, buf, ss, rs
        self.up = device(y, c, lax.rem(z + 1, length), x)
        self.down = device(y, c, lax.rem(z + length - 1, length), x)

    def copy(self, hop, upward):
        length, buf = self.length, self.buf
        src, dst = ((length - hop + 1) % length, length - hop) if upward else (hop - 1, hop)
        way = 0 if upward else 1
        return pltpu.make_async_remote_copy(
            src_ref=buf.at[src], dst_ref=buf.at[dst], send_sem=self.ss.at[way, hop - 1],
            recv_sem=self.rs.at[way, hop - 1], device_id=self.up if upward else self.down,
            device_id_type=MESH,
        )

    def sends(self, hop, act):
        z, length = self.z, self.length

        @pl.when(jnp.logical_and(z + 1 < length, z >= hop - 1))
        def _():
            act(self.copy(hop, True))

        @pl.when(jnp.logical_and(z >= 1, z + hop - 1 < length))
        def _():
            act(self.copy(hop, False))

    def start(self, hop):
        self.sends(hop, lambda copy: copy.start())

    def start_piece(self, n):
        for way, last, dst in ((0, self.z + 1 < self.length, self.length - 1), (1, self.z >= 1, 1)):

            @pl.when(last)
            def _():
                remote(
                    self.buf.at[0, n], self.buf.at[dst, n], self.ss.at[way, 0], self.rs.at[way, 0],
                    (self.up, self.down)[way],
                )

    def arrive(self, hop):
        z, length = self.z, self.length

        @pl.when(z >= hop)
        def _():
            self.copy(hop, True).wait_recv()

        @pl.when(z + hop < length)
        def _():
            self.copy(hop, False).wait_recv()

    def finish(self, first_hop=1, last_hop=None):
        for hop in range(first_hop, (last_hop or self.length - 1) + 1):
            self.sends(hop, lambda copy: copy.wait_send())


class LineScatter:
    def __init__(self, sources, length, total, up_mine, down_mine, up_got, down_got, loc, ss, rs):
        y, c, z, x = place()
        self.sources, self.length, self.total = sources, length, total
        self.mine, self.got = (up_mine, down_mine), (up_got, down_got)
        self.loc, self.ss, self.rs = loc, ss, rs
        self.to = (device(y, c, lax.rem(z + 1, length), x), device(y, c, lax.rem(z + length - 1, length), x))
        self.far = (z, length - 1 - z)
        self.next = 1

    def loads(self, way, hop):
        k = 0 if hop == 0 else self.length - hop if way == 0 else hop
        copies, at = [], 0
        for n, (ref, first, columns) in enumerate(self.sources):
            dst = self.term(way, hop) if hop else self.total
            copies.append(
                pltpu.make_async_copy(
                    ref.at[k, :, pl.ds(first, columns)], dst.at[:, pl.ds(at, columns)],
                    self.loc.at[way, hop, n],
                )
            )
            at += columns
        return copies

    def term(self, way, hop):
        return self.mine[way].at[hop - 1]

    def copy(self, way, hop):
        return pltpu.make_async_remote_copy(
            src_ref=self.term(way, hop), dst_ref=self.got[way].at[hop - 1],
            send_sem=self.ss.at[way, hop - 1], recv_sem=self.rs.at[way, hop - 1],
            device_id=self.to[way], device_id_type=MESH,
        )

    def load(self, hops):
        for hop in hops:
            for way in (0, 1) if hop else (0,):
                for copy in self.loads(way, hop):
                    copy.start()

    def start(self):
        hop = self.next
        if hop >= self.length:
            return
        self.next += 1
        for way in (0, 1):
            far = self.far[way]
            for copy in self.loads(way, hop):
                copy.wait()
            if hop > 1:

                @pl.when(jnp.logical_and(far >= 1, far <= hop - 1))
                def _():
                    self.copy(way, hop - 1).wait_recv()
                    dst, src = self.term(way, hop), self.got[way].at[hop - 2]

                    def add(at):
                        dst[at] = dst[at] + src[at]

                    rows_loop(dst.shape[0], add, unroll=4)

            @pl.when(far <= hop - 1)
            def _():
                self.copy(way, hop).start()

    def end(self, result, first_column, squares):
        last = self.length - 1
        for copy in self.loads(0, 0):
            copy.wait()
        columns = pl.ds(first_column, self.total.shape[1])

        def finish(ways):
            for way in ways:
                self.copy(way, last).wait_recv()

            def add(at):
                total = self.total[at].astype(F32)
                for way in ways:
                    total = total + self.got[way][last - 1, at].astype(F32)
                result[at, columns] = total.astype(result.dtype)
                squares[...] += tile_of_squares(total)

            rows_loop(result.shape[0], add)

        above, below = self.far[0] >= 1, self.far[1] >= 1
        pl.when(jnp.logical_and(above, below))(lambda: finish((0, 1)))
        pl.when(jnp.logical_not(above))(lambda: finish((1,)))
        pl.when(jnp.logical_not(below))(lambda: finish((0,)))
        for hop in range(1, self.length):
            for way in (0, 1):

                @pl.when(self.far[way] <= hop - 1)
                def _():
                    self.copy(way, hop).wait_send()


class HeldLine(LineScatter):
    def __init__(self, g, first_column, up_got, down_got, ss, rs):
        y, c, z, x = place()
        self.length = length = g.shape[0]
        self.columns = pl.ds(first_column, up_got.shape[2])
        self.sources, self.g, self.total = (), g, g.at[0, :, self.columns]
        self.got, self.ss, self.rs = (up_got, down_got), ss, rs
        self.to = line_neighbours(length)
        self.far = (z, length - 1 - z)
        self.next = 1

    def term(self, way, hop):
        return self.g.at[self.length - hop if way == 0 else hop, :, self.columns]


def chains_of(cuts):
    whole = sum(cut[2] for cut in cuts)
    left = -(-whole // 256) * 128
    lists = [], []
    for which, first_column, columns in cuts:
        taken = min(columns, left)
        if taken:
            lists[0].append((which, first_column, taken))
        if columns > taken:
            lists[1].append((which, first_column + taken, columns - taken))
        left -= taken
    return lists


class Lines:
    def __init__(self, terms, cuts, length, refs):
        self.chains, self.length = [], length
        for n, cut in enumerate(chains_of(cuts)):
            sources = [(terms[which], first_column, columns) for which, first_column, columns in cut]
            self.chains.append(
                LineScatter(sources, length, *refs[n * LINE_REFS : (n + 1) * LINE_REFS])
            )
        self.queue = [chain for _ in range(1, length) for chain in self.chains]

    def begin(self):
        for chain in self.chains:
            chain.load((1,))
        self.start()
        self.start()
        for chain in self.chains:
            chain.load((*range(2, self.length), 0))

    def start(self):
        if self.queue:
            self.queue.pop(0).start()

    def end(self, result, squares):
        while self.queue:
            self.start()
        squares[...] = jnp.zeros_like(squares)
        at = 0
        for chain in self.chains:
            chain.end(result, at, squares)
            at += chain.total.shape[1]


def lines_scratch(length, rows, cuts):
    return sum(
        (line_scratch(length, rows, sum(cut[2] for cut in chain), len(chain)) for chain in chains_of(cuts)), []
    )


def fold(v):
    return jnp.sum(v.reshape(v.shape[0] // 8, 8, v.shape[1]), axis=0)


def tile_of_squares(v):
    v = fold(v * v)
    part = v[:, :128]
    for n in range(1, v.shape[1] // 128):
        part = part + v[:, n * 128 : (n + 1) * 128]
    if v.shape[1] % 128:
        rest = v[:, v.shape[1] // 128 * 128 :]
        part = part + jnp.concatenate([rest, jnp.zeros((8, 128 - rest.shape[1]), F32)], axis=1)
    return part


def line_scratch(length, rows, columns, sources):
    slots = pltpu.VMEM((length - 1, rows, columns), BF16)
    return [pltpu.VMEM((rows, columns), BF16)] + [slots] * 4 + [
        DMA((2, length, sources)), DMA((2, length)), DMA((2, length))
    ]


def starts(copies):
    for copy in copies:
        copy.start()
    return copies


def waits(copies):
    for copy in copies:
        copy.wait()


def local_copies(pairs, sems):
    return [pltpu.make_async_copy(src, dst, sems.at[n]) for n, (src, dst) in enumerate(pairs)]


def held(*arrays):
    return [pltpu.VMEM(v.shape, v.dtype) for v in arrays]


LINE_REFS = 8
SCATTER_REFS = 7
TILE = jax.ShapeDtypeStruct((8, 128), F32)


def line_neighbours(length):
    y, c, z, x = place()
    return [device(y, c, lax.rem(z + 1, length), x), device(y, c, lax.rem(z + length - 1, length), x)]


def rows_loop(rows, body, start=0, unroll=2):
    @pl.loop(start // 16, (start + rows) // 16, unroll=unroll)
    def _(i):
        body(pl.ds(pl.multiple_of(i * 16, 16), 16))


def turned_tiles(length, pair):
    _, _, z, _ = place()
    for k in range(length):
        for b in range(4):
            yield k * 4 + b, pl.multiple_of((b * length + lax.rem(z + k, length)) * pair, pair)


def load_turned(ref, at, length, pair):
    if pair % 128:
        return ref[at]
    return jnp.concatenate([ref[at, pl.ds(src, pair)] for _, src in turned_tiles(length, pair)], axis=1)


def store_turned(ref, at, value, length, pair):
    if pair % 128:
        ref[at] = value
        return
    for n, dst in turned_tiles(length, pair):
        ref[at, pl.ds(dst, pair)] = value[:, n * pair : (n + 1) * pair]


def inverse_rms(v):
    return lax.rsqrt(jnp.sum(v * v, axis=-1, keepdims=True) * (1.0 / v.shape[-1]) + norm_eps)


def norm_rows_back(v, gain, grad):
    inverse = inverse_rms(v)
    scaled = v * inverse
    moved = grad * gain
    inner = jnp.sum(moved * scaled, axis=-1, keepdims=True) * (1.0 / v.shape[-1])
    return inverse * (moved - scaled * inner), fold(grad * scaled)


def middle_kernel(length, mixed_in, mixer_in, inputs_in, gains_in, w_in, late_in, residual_o, normed_o, w, late, *scratch):
    scatter_refs, (p, low, loc, gs, gr, hs, hr, late_s, late_r, *scratch) = scratch[:SCATTER_REFS], scratch[SCATTER_REFS:]
    mixed, mixer, inputs, gains, residual, load_s, keep_s = scratch
    loads = starts(
        local_copies(
            ((mixed_in, mixed), (mixer_in, mixer), (inputs_in, inputs), (gains_in, gains)), load_s
        )
    )
    greet(gather_peers() + line_neighbours(length))
    hops = LineGather(w, length, hs, hr)
    hops.start(1)
    late_hops = LineGather(late, length, late_s, late_r)
    late_hops.start(1)
    started = [1]
    part = mixed.shape[1]
    rows, width = low.shape

    waits(loads[:2])

    def prepare(i):
        mine = mixed[pl.ds(pl.multiple_of(i * rows, rows), rows)]
        p[i] = contract_last(mine, mixer[:, 2 * part :]).astype(BF16)

    def advance():
        if started[0] < length - 1:
            hops.arrive(started[0])
            started[0] += 1
            hops.start(started[0])

    def body(at):
        v = inputs[at].astype(F32) + residual[at]
        residual[at] = v
        low[at] = (v * inverse_rms(v) * gains[1:2]).astype(BF16)

    half = low.shape[0] // 2
    gather = Gather(low, normed_o, loc, gs, gr)
    for name in scatter_steps(p, residual, *scatter_refs, prepare=prepare):
        if name == "late":
            advance()
        if name == "low half":
            waits(loads[2:])
            rows_loop(half, body)
            gather.begin_half(0)
        if name == "high half":
            rows_loop(half, body, half)
            gather.begin_half(1)
    keeps = starts(local_copies(((residual, residual_o),), keep_s))
    gather.middle()
    advance()
    gather.end()
    waits(keeps)
    while started[0] < length - 1:
        advance()
    hops.arrive(length - 1)
    hops.finish()
    late_hops.arrive(1)
    late_hops.finish(1, 1)


def middle(mixed, mixer, inputs, gains, w, late, length, collective_id):
    rows, width = inputs.shape
    return pl.pallas_call(
        functools.partial(middle_kernel, length),
        out_shape=(
            jax.ShapeDtypeStruct((rows, width), F32),
            jax.ShapeDtypeStruct((8, rows, width), BF16),
            jax.ShapeDtypeStruct(w.shape, w.dtype),
            jax.ShapeDtypeStruct(late.shape, late.dtype),
        ),
        in_specs=[ANY] * 6,
        out_specs=(ANY,) * 4,
        scratch_shapes=scatter_scratch(rows // 2, width)
        + [pltpu.VMEM((8, rows, width), BF16), pltpu.VMEM((rows, width), BF16), DMA, DMA((14,)), DMA((14,))]
        + [DMA((2, length))] * 4
        + held(mixed, mixer, inputs, gains)
        + [pltpu.VMEM((rows, width), F32), DMA((4,)), DMA((1,))],
        input_output_aliases={4: 2, 5: 3},
        compiler_params=params(collective_id),
        cost_estimate=pl.CostEstimate(flops=0, bytes_accessed=300 * 2**20, transcendentals=0),
    )(mixed, mixer, inputs, gains, w, late)


def turn_kernel(length, cuts, p, residual_in, above_in, gains_in, mixer_in, *refs):
    parts = 1 + max(cut[0] for cut in cuts)
    terms, refs = refs[:parts], refs[parts:]
    back_o, gain, low_o, dmix_o, sums, squares, *scratch = refs
    scatter_refs, scratch = scratch[:SCATTER_REFS], scratch[SCATTER_REFS:]
    total, low, loc, gs, gr, parts_in, load_s, residual, above, gains, mixer, back, dmix, in_s, keep_s = scratch[:15]
    line_refs = scratch[15:]
    loads = local_copies(
        ((residual_in, residual), (above_in, above), (gains_in, gains), (mixer_in, mixer)), in_s
    )
    greet(gather_peers() + line_neighbours(length))
    line = Lines(terms, cuts, length, line_refs)
    line.begin()
    starts(loads)
    gain[...] = jnp.zeros_like(gain)

    def body(at):
        grad, gain_part = norm_rows_back(residual[at], gains[1:2], total[at])
        grad = above[at].astype(F32) + grad
        back[at] = grad
        low[at] = grad.astype(BF16)
        gain[...] += gain_part

    half = low.shape[0] // 2
    gather = Gather(low, low_o, loc, gs, gr)
    for name in scatter_steps(p, total, *scatter_refs):
        if name in ("early", "late"):
            line.start()
        if name == "low half":
            waits(loads)
            rows_loop(half, body)
            gather.begin_half(0)
        if name == "high half":
            rows_loop(half, body, half)
            gather.begin_half(1)
            line.start()
    keeps = starts(local_copies(((back, back_o),), keep_s))
    rows = low.shape[0]
    part = mixer.shape[1] // 3
    y, c, z, x = place()
    near = (gather.me, gather.bx), (gather.by, rank(y, 1 - c, x))
    rest = (gather.bd, rank(1 - y, 1 - c, x)), (rank(y, 1 - c, 1 - x), rank(1 - y, 1 - c, 1 - x))

    def fetch(blocks, slot):
        copies = []
        for n in (0, 1):
            copies.append(
                pltpu.make_async_copy(low_o.at[blocks[n]], parts_in.at[slot, n], load_s.at[slot, n])
            )
        return copies

    def mix(blocks, slot):
        waits(fetch(blocks, slot))
        lines = parts_in[slot].reshape(2 * rows, parts_in.shape[3])
        both = jnp.dot(lines, mixer[:, 2 * part :], preferred_element_type=F32)
        none = jnp.zeros((rows, dmix.shape[2] - part), F32)
        for n in (0, 1):
            dmix[blocks[n]] = jnp.concatenate([both[n * rows : (n + 1) * rows], none], axis=1)
            pltpu.make_async_copy(dmix.at[blocks[n]], dmix_o.at[blocks[n]], keep_s.at[1 + n + 2 * slot]).start()

    def mixed(blocks, slot):
        for n in (0, 1):
            pltpu.make_async_copy(dmix.at[blocks[n]], dmix_o.at[blocks[n]], keep_s.at[1 + n + 2 * slot]).wait()

    def near_blocks():
        gather.own.wait()
        for copy in gather.last[:2]:
            copy.wait_recv()
        starts(fetch(near[0], 0))
        starts(fetch(near[1], 1))
        mix(near[0], 0)
        mix(near[1], 1)

    gather.middle()
    line.start()
    gather.relays(near_blocks)
    gather.finish(2, own=False)
    for n in (0, 1):
        mixed(near[n], n)
        starts(fetch(rest[n], n))
    for n in (0, 1):
        mix(rest[n], n)
    waits(keeps)
    line.end(sums, squares)
    for n in (0, 1):
        mixed(rest[n], n)


def turn(p, residual, above, gains, mixer, rc, terms, cuts, length, collective_id):
    rows, width = residual.shape
    line_rows, columns = terms[0].shape[1], sum(cut[2] for cut in cuts)
    return pl.pallas_call(
        functools.partial(turn_kernel, length, cuts),
        out_shape=(
            jax.ShapeDtypeStruct((rows, width), F32),
            jax.ShapeDtypeStruct((8, width), F32),
            jax.ShapeDtypeStruct((8, rows, width), BF16),
            jax.ShapeDtypeStruct((8, rows, rc), F32),
            jax.ShapeDtypeStruct((line_rows, columns), BF16),
            TILE,
        ),
        in_specs=[ANY] * (5 + len(terms)),
        out_specs=(ANY, VM, ANY, ANY, VM, VM),
        scratch_shapes=scatter_scratch(rows // 2, width)
        + [pltpu.VMEM((rows, width), F32), pltpu.VMEM((rows, width), BF16), DMA, DMA((14,)), DMA((14,))]
        + [pltpu.VMEM((2, 2, rows, width), BF16), DMA((2, 2))]
        + held(residual, above, gains, mixer)
        + [pltpu.VMEM((rows, width), F32), pltpu.VMEM((8, rows, rc), F32), DMA((4,)), DMA((5,))]
        + lines_scratch(length, line_rows, cuts),
        compiler_params=params(collective_id),
        cost_estimate=pl.CostEstimate(flops=0, bytes_accessed=300 * 2**20, transcendentals=0),
    )(p.reshape(8, rows, width), residual, above, gains, mixer, *terms)


def closing_kernel(
    length, x_in, dmz_in, dproj_in, mixed_in, mixer_in, q, residual_in, block, inputs_in, above_in, gains_in, gp_in,
    grad_out, gain, gates_o, out_out, e_o, sums, squares,
    x_part, dmz_part, g, back, total, o, up_a, down_a, up_b, down_b, gp_got, gp_sum,
    ls, lr, load_s, free, loc, es, er, gate_s, gate_r, move_s, move_r,
    dproj, mixed, mixer, residual, inputs, above, gains, gp, grad_o, out, in_s, keep_s, *scatter_refs,
):
    inflow = starts(
        local_copies(
            (
                (gp_in, gp), (dproj_in, dproj), (mixed_in, mixed), (mixer_in, mixer), (residual_in, residual),
                (inputs_in, inputs), (above_in, above), (gains_in, gains),
            ),
            in_s,
        )
    )
    y, c, z, x = place()
    others = line_peers(length)
    s = 2 * z + x
    owner = x * length + z
    to_z = owner // 2
    to_x = owner - 2 * to_z
    from_z, from_x = lax.rem(s, length), s // length
    moves = jnp.where(jnp.logical_and(to_z == z, to_x == x), 0, 1)
    barrier = pltpu.get_barrier_semaphore()
    for peer in others + plane_peers():
        pl.semaphore_signal(barrier, inc=1, device_id=peer, device_id_type=MESH)

    @pl.when(moves == 1)
    def _():
        pl.semaphore_signal(barrier, inc=1, device_id=device(y, c, to_z, to_x), device_id_type=MESH)
        pl.semaphore_signal(barrier, inc=1, device_id=device(y, c, from_z, from_x), device_id_type=MESH)

    pl.semaphore_wait(barrier, len(others) + 7 + 2 * moves)
    model = mixer.shape[0]
    tokens = dproj.shape[0]
    part = mixed.shape[1]
    columns = x_part.shape[2]
    steps = model // columns
    rows = tokens // steps
    line_rows = g.shape[1]

    def loads(i, slot):
        at = pl.ds(pl.multiple_of(i * columns, columns), columns)
        return (
            pltpu.make_async_copy(x_in.at[:, at], x_part.at[slot], load_s.at[0, slot]),
            pltpu.make_async_copy(dmz_in.at[:, at], dmz_part.at[slot], load_s.at[1, slot]),
        )

    group = steps // 4
    order = (3, 1, 2, 0)

    def fetch(i, slot):
        for copy in loads(i, slot):
            copy.start()

    fetch(order[0] * group, 0)
    inflow[0].wait()
    gate = [
        remote(gp.at[lax.rem(z + k + 1, length)], gp_got.at[k], gate_s.at[k], gate_r.at[k], others[k])
        for k in range(length - 1)
    ]
    split = up_a.shape[2]
    line_a = HeldLine(g, 0, up_a, down_a, ls.at[0], lr.at[0])
    line_b = HeldLine(g, split, up_b, down_b, ls.at[1], lr.at[1])
    queue = [chain for _ in range(1, length) for chain in (line_a, line_b)]

    def advance(times=1):
        for _ in range(times):
            if queue:
                queue.pop(0).start()

    output = scatter_steps(q, total, *scatter_refs)
    next(output)
    copies, own = exchange_steps(block, e_o, loc, es, er)

    def compute(n):
        @pl.loop(0, group)
        def _(j):
            count = n * group + j
            slot = count - count // 2 * 2
            i = order[n] * group + j

            @pl.when(j + 1 < group)
            def _():
                fetch(i + 1, 1 - slot)

            if n < 3:

                @pl.when(j + 1 == group)
                def _():
                    fetch(order[n + 1] * group, 1 - slot)

            for copy in loads(i, slot):
                copy.wait()
            front = contract_first(x_part[slot], dproj[...])
            tail = contract_first(dmz_part[slot], mixed[...])
            k = i * columns // line_rows
            at = pl.ds(pl.multiple_of(i * columns - k * line_rows, columns), columns)
            g[k, at] = jnp.concatenate([front, tail], axis=1).astype(BF16)
            block_of = i * rows // 256
            at = pl.ds(pl.multiple_of(i * rows - block_of * 256, rows), rows)
            mine = dproj[pl.ds(pl.multiple_of(i * rows, rows), rows)]
            back[block_of, at] = contract_last(mine, mixer[:, : 2 * part]).astype(BF16)

    waits(inflow[1:4])
    compute(0)
    next(output)
    compute(1)
    if length == 4:
        advance(2)
    next(output)
    compute(2)
    next(output)
    compute(3)
    if length != 4:
        advance(2)
    for _ in output:
        pass
    for peer in gather_peers():
        pl.semaphore_signal(free, inc=1, device_id=peer, device_id_type=MESH)
    advance()
    pl.semaphore_wait(free, 3)
    incoming = scatter_steps(back, o, *scatter_refs)
    next(incoming)
    pair = out.shape[1] // (4 * length)

    def finish_output(at):
        store_turned(out, at, (residual[at] + total[at]).astype(BF16), length, pair)

    waits(inflow[4:])
    rows_loop(out.shape[0], finish_output)
    keeps = local_copies(((out, out_out), (grad_o, grad_out)), keep_s)
    keeps[0].start()
    for copy in gate:
        copy.wait()
    rows_sum = gp[z]
    for k in range(length - 1):
        rows_sum = rows_sum + gp_got[k]
    gp_sum[...] = rows_sum
    move = pltpu.make_async_remote_copy(
        src_ref=gp_sum, dst_ref=gates_o, send_sem=move_s, recv_sem=move_r,
        device_id=device(y, c, to_z, to_x), device_id_type=MESH,
    )
    pl.when(moves == 1)(lambda: move.start())

    @pl.when(moves == 0)
    def _():
        gates_o[...] = rows_sum

    gain[...] = jnp.zeros_like(gain)

    def finish_grad(at):
        grad, gain_part = norm_rows_back(inputs[at].astype(F32), gains[0:1], o[at])
        store_turned(grad_o, at, above[at] + grad, length, pair)
        gain[...] += gain_part

    half = grad_o.shape[0] // 2
    for name in incoming:
        if name in ("sent", "early", "late"):
            advance()
        if name == "low half":
            rows_loop(half, finish_grad)
        if name == "high half":
            rows_loop(half, finish_grad, half)
            keeps[1].start()
    while queue:
        advance()
    squares[...] = jnp.zeros_like(squares)
    line_a.end(sums, 0, squares)
    line_b.end(sums, split, squares)
    pl.when(moves == 1)(lambda: move.wait())
    waits(keeps)
    for copy in copies:
        copy.wait()
    own.wait()


def closing(x, dmz, dproj, mixed, mixer, q, residual, block, inputs, above, gains, gp, length, collective_id):
    rows, width = residual.shape
    tokens, model = x.shape
    part = mixed.shape[1]
    share = block.shape[0] // 8
    block = block.reshape(8, share, block.shape[1])
    line_rows = model // length
    columns = min(256, line_rows)
    split = -(-3 * part // 256) * 128
    slots_a, slots_b = (pltpu.VMEM((length - 1, line_rows, n), BF16) for n in (split, 3 * part - split))
    pack = gp.shape[1:]
    return pl.pallas_call(
        functools.partial(closing_kernel, length),
        out_shape=(
            jax.ShapeDtypeStruct((rows, width), F32),
            jax.ShapeDtypeStruct((8, width), F32),
            jax.ShapeDtypeStruct(pack, F32),
            jax.ShapeDtypeStruct((rows, width), BF16),
            jax.ShapeDtypeStruct(block.shape, BF16),
            jax.ShapeDtypeStruct((line_rows, 3 * part), BF16),
            TILE,
        ),
        in_specs=[ANY] * 12,
        out_specs=(ANY, VM, VM, ANY, ANY, VM, VM),
        scratch_shapes=[
            pltpu.VMEM((2, tokens, columns), BF16),
            pltpu.VMEM((2, tokens, columns), BF16),
            pltpu.VMEM((length, line_rows, 3 * part), BF16),
            pltpu.VMEM((8, rows, width), BF16),
            pltpu.VMEM((rows, width), F32),
            pltpu.VMEM((rows, width), F32),
            slots_a, slots_a, slots_b, slots_b,
            pltpu.VMEM((length - 1,) + pack, F32),
            pltpu.VMEM(pack, F32),
            DMA((2, 2, length)), DMA((2, 2, length)), DMA((2, 2)), pltpu.SemaphoreType.REGULAR,
            DMA, DMA((7,)), DMA((7,)), DMA((length,)), DMA((length,)), DMA, DMA,
            *held(dproj, mixed, mixer, residual, inputs, above, gains, gp),
            pltpu.VMEM((rows, width), F32),
            pltpu.VMEM((rows, width), BF16),
            DMA((8,)), DMA((2,)),
        ]
        + scatter_scratch(rows // 2, width),
        compiler_params=params(collective_id),
        cost_estimate=pl.CostEstimate(
            flops=10 * tokens * model * dproj.shape[1] // 2, bytes_accessed=350 * 2**20, transcendentals=0
        ),
    )(x, dmz, dproj, mixed, mixer, q.reshape(8, rows, width), residual, block, inputs, above, gains, gp)


def first_kernel(
    length, inputs_in, above_in, mixer_in, mlp_in, gains_in, gate_in, chan_in,
    normed_o, wm_o, wf_o, wd_o, w2_o, gains_o, gate_o, chan_o, inputs_o, above_o,
    inputs, above, mixer_w, mlp_w, gains_w, gate_w, chan_w, load_s,
    inputs_k, above_k, w2, keep_s, gp_o, gn, gp, normed, gn_all, wm, wf, wd, loc, ms, mr, fs, fr, line_s, line_r, gain_s, gain_r, move_s, move_r,
    gather_s, gather_r, hop_s, hop_r,
):
    loads = [
        pltpu.make_async_copy(src, dst, load_s.at[n])
        for n, (src, dst) in enumerate(
            (
                (gains_in, gains_w), (gate_in, gate_w), (chan_in, chan_w), (mixer_in, mixer_w),
                (mlp_in, mlp_w), (inputs_in, inputs), (above_in, above),
            )
        )
    ]
    for copy in loads:
        copy.start()
    y, c, z, x = place()
    s = 2 * z + x
    me = rank(y, c, x)
    rows, width = inputs.shape
    pair = width // (4 * length)
    line = line_peers(length)
    plane = plane_peers()
    to_z, to_x = lax.rem(s, length), s // length
    moves = jnp.where(jnp.logical_and(to_z == z, to_x == x), 0, 1)
    src = x * length + z
    from_z = src // 2
    from_x = src - 2 * from_z
    barrier = pltpu.get_barrier_semaphore()
    for peer in line + plane:
        pl.semaphore_signal(barrier, inc=1, device_id=peer, device_id_type=MESH)

    @pl.when(moves == 1)
    def _():
        pl.semaphore_signal(barrier, inc=1, device_id=device(y, c, to_z, to_x), device_id_type=MESH)
        pl.semaphore_signal(barrier, inc=1, device_id=device(y, c, from_z, from_x), device_id_type=MESH)

    def fill(pack, source, js, offset=0):
        part = pack.shape[2] // len(js)
        whole = source.shape[1] // 24
        for t in range(8):
            for n, j in enumerate(js):
                start = (j * 8 + t) * whole + offset
                pack[t, :, n * part : (n + 1) * part] = source[:, start : start + part].astype(BF16)

    loads[3].wait()
    fill(wm, mixer_w, (0, 1, 2))
    for copy in loads[:3]:
        copy.wait()
    share = gains_w.shape[1]
    gn[...] = jnp.zeros_like(gn)
    for n in (0, 1):

        @pl.when(x == n)
        def _():
            gn[:2, n * share : (n + 1) * share] = gains_w[...]

    gp[...] = jnp.zeros_like(gp)
    channels = contract_first(chan_w[...].astype(BF16), unit(8))
    gp[: gate_w.shape[0]] = jnp.concatenate(
        [
            gate_w[...],
            channels,
            jnp.zeros((gate_w.shape[0], gp.shape[1] - gate_w.shape[1] - 8), F32),
        ],
        axis=1,
    ).astype(BF16)
    gn_all[me, z] = gn[...]
    pl.semaphore_wait(barrier, len(line) + len(plane) + 2 * moves)
    gains = [
        remote(gn, gn_all.at[me, z], line_s.at[0, k], line_r.at[0, k], line[k]) for k in range(length - 1)
    ]
    gate_move = pltpu.make_async_remote_copy(
        src_ref=gp, dst_ref=gp_o.at[to_z], send_sem=move_s, recv_sem=move_r,
        device_id=device(y, c, to_z, to_x), device_id_type=MESH,
    )
    gate_stay = pltpu.make_async_copy(gp, gp_o.at[z], loc.at[2])
    pl.when(moves == 1)(lambda: gate_move.start())
    pl.when(moves == 0)(lambda: gate_stay.start())

    mixer, mixer_own = exchange_steps(wm, wm_o.at[0], loc.at[0], ms, mr)
    hops = LineGather(wm_o, length, hop_s, hop_r)
    mixer_own.wait()
    hops.start_piece(me)

    def pass_piece(n):
        fy, fc, fx = FLIPS[n]
        mixer[n].wait_recv()
        hops.start_piece(rank(flip(y, fy), flip(c, fc), flip(x, fx)))

    pass_piece(1)
    for copy in gains:
        copy.wait()
    spread = [
        remote(gn_all.at[me], gn_all.at[me], gain_s.at[n], gain_r.at[n], plane[n]) for n in range(7)
    ]
    loads[4].wait()
    fill(wd, mlp_w, (2,))
    down, down_own = exchange_steps(wd, wd_o.at[0], loc.at[4], fs.at[1], fr.at[1])
    for n in (0, 2, 3, 5, 4, 6):
        pass_piece(n)
    fill(wf, mlp_w, (0, 1))
    feed, feed_own = exchange_steps(wf, wf_o.at[0], loc.at[3], fs.at[0], fr.at[0])
    pl.when(moves == 1)(lambda: gate_move.wait())
    pl.when(moves == 0)(lambda: gate_stay.wait())
    gates = [
        remote(gp_o.at[z], gp_o.at[z], line_s.at[1, k], line_r.at[1, k], line[k])
        for k in range(length - 1)
    ]
    fill(w2, mlp_w, (0, 1, 2), wd.shape[2])
    for copy in spread:
        copy.wait()
    for k in range(length):
        other = lax.rem(z + k, length)
        for b in range(4):
            at = slice((4 * k + b) * pair, (4 * k + b + 1) * pair)
            tile = (gn_all[2 * b, other] + gn_all[2 * b + 1, other])[:, :pair]
            gains_o[:, at] = tile.astype(BF16).astype(F32)
    for copy in mixer:
        copy.wait_send()

    def body(at):
        v = load_turned(inputs, at, length, pair)
        inputs_k[at] = v
        v = v.astype(F32)
        normed[at] = (v * inverse_rms(v) * gains_o[0:1]).astype(BF16)
        above_k[at] = load_turned(above, at, length, pair)

    for copy in loads[5:]:
        copy.wait()
    half = rows // 2
    gather = Gather(normed, normed_o, loc.at[1], gather_s, gather_r)
    rows_loop(half, body)
    gather.begin_half(0)
    hops.arrive(1)
    if length > 2:
        hops.start(2)
    rows_loop(half, body, half)
    gather.begin_half(1)
    keeps = starts(local_copies(((inputs_k, inputs_o), (above_k, above_o)), keep_s))
    gather.middle()
    late, late_own = exchange_steps(w2, w2_o.at[0], loc.at[0], fs.at[2], fr.at[2])
    if length > 3:
        hops.arrive(2)
        hops.start(3)
    for copy in gates:
        copy.wait()
    gate_rows, columns = gate_w.shape
    head = columns // 2
    own = jnp.concatenate([gp_o[n, :gate_rows].astype(F32) for n in range(length)]).astype(BF16)
    part, rc = own.shape[0], gate_o.shape[0]
    gate_o[...] = jnp.zeros_like(gate_o)
    for first_row in range(0, part, head):
        at = slice(first_row, first_row + head)
        wide = [jnp.zeros((head, first_row), F32)] if first_row else []
        for n in (0, 1):
            block = own[at, n * head : (n + 1) * head].astype(F32)
            rest = jnp.zeros((head, rc - first_row - head), F32)
            gate_o[at, n * rc : (n + 1) * rc] = jnp.concatenate([*wide, block, rest], axis=1).astype(BF16)
    rows_of = contract_last(unit(8), own[:, columns : columns + 8])
    lam = rows_of[7:8]
    u = jnp.exp(-jnp.abs(lam))
    t = u / (2.0 + u)
    series = jnp.full_like(t, 1.0 / 17.0)
    for n in range(15, 0, -2):
        series = series * t * t + 1.0 / n
    rate = 8.0 * (jnp.maximum(-lam, 0.0) + 2.0 * t * series)
    fill_rows = jnp.concatenate([jnp.zeros((7, rc - part), F32), jnp.ones((1, rc - part), F32)])
    chan_o[...] = jnp.concatenate([jnp.concatenate([rows_of[:7], rate]), fill_rows], axis=1)
    gather.relays()
    for hop in range(min(3, length - 1), length):
        hops.arrive(hop)
        if hop + 1 < length:
            hops.start(hop + 1)
    gather.finish()
    waits(keeps)
    for copy in down + feed + late:
        copy.wait()
    late_own.wait()
    down_own.wait()
    feed_own.wait()
    hops.finish()


def early(f8):
    return f8 // 384 * 256


def unit(n):
    return (
        lax.broadcasted_iota(jnp.int32, (n, n), 0) == lax.broadcasted_iota(jnp.int32, (n, n), 1)
    ).astype(BF16)


def first(inputs, above, mixer, mlp, gains, gate, chan, rc, length, collective_id):
    rows, width = inputs.shape
    pack = (-(-gate.shape[0] // 16) * 16, rc)
    share = mixer.shape[0]
    f8 = mlp.shape[1] // 24
    wm, wf, wd, w2 = (
        (8, share, n) for n in (mixer.shape[1] // 8, 2 * early(f8), early(f8), 3 * (f8 - early(f8)))
    )
    low = jax.ShapeDtypeStruct((rows, width), BF16)
    return pl.pallas_call(
        functools.partial(first_kernel, length),
        out_shape=(
            jax.ShapeDtypeStruct((8, rows, width), BF16),
            jax.ShapeDtypeStruct((length,) + wm, BF16),
            jax.ShapeDtypeStruct((length,) + wf, BF16),
            jax.ShapeDtypeStruct((length,) + wd, BF16),
            jax.ShapeDtypeStruct((length,) + w2, BF16),
            jax.ShapeDtypeStruct((8, width), F32),
            jax.ShapeDtypeStruct((rc, 2 * rc), BF16),
            jax.ShapeDtypeStruct((8, rc), F32),
            low,
            low,
        ),
        in_specs=[ANY] * 7,
        out_specs=(ANY, ANY, ANY, ANY, ANY, VM, VM, VM, ANY, ANY),
        scratch_shapes=[
            *[pltpu.VMEM(v.shape, v.dtype) for v in (inputs, above, mixer, mlp, gains, gate, chan)],
            DMA((7,)),
            pltpu.VMEM((rows, width), BF16),
            pltpu.VMEM((rows, width), BF16),
            pltpu.VMEM(w2, BF16),
            DMA((2,)),
            pltpu.VMEM((length,) + pack, BF16),
            pltpu.VMEM((8, 128), F32),
            pltpu.VMEM(pack, BF16),
            pltpu.VMEM((rows, width), BF16),
            pltpu.VMEM((8, length, 8, 128), F32),
            pltpu.VMEM(wm, BF16),
            pltpu.VMEM(wf, BF16),
            pltpu.VMEM(wd, BF16),
            DMA((5,)), DMA((7,)), DMA((7,)), DMA((3, 7)), DMA((3, 7)),
            DMA((2, length)), DMA((2, length)), DMA((7,)), DMA((7,)), DMA, DMA,
            DMA((14,)), DMA((14,)), DMA((2, length)), DMA((2, length)),
        ],
        compiler_params=params(collective_id),
        cost_estimate=pl.CostEstimate(flops=0, bytes_accessed=300 * 2**20, transcendentals=0),
    )(inputs, above, mixer, mlp, gains, gate, chan)


def last_kernel(
    length, share, wm, gain, gain_two, gates, sq_a, sq_b, sq_c, sq_d,
    wm_o, gains_o, norm_o, factor_o, by_plane, by_line, loc, ss, rs, gs, gr, ls, lr,
):
    y, c, z, x = place()
    me = rank(y, c, x)
    line = line_peers(length)
    plane = plane_peers()
    width = gain.shape[1]
    pair = width // (4 * length)
    squares = sq_a[...] + sq_b[...] + sq_c[...] + sq_d[...] + tile_of_squares(gates[...])
    squares = jnp.concatenate([squares, jnp.zeros((8, width - 128), F32)], axis=1)
    rows = [jnp.sum(v, axis=0, keepdims=True) for v in (gain[...], gain_two[...], squares)]
    by_plane[me] = jnp.concatenate(rows + [jnp.zeros((1, width), F32)])
    greet(line + plane)
    sends = [
        remote(by_plane.at[me], by_plane.at[me], gs.at[n], gr.at[n], plane[n]) for n in range(7)
    ]
    copies, own = exchange_steps(wm, wm_o, loc, ss, rs)
    for copy in sends:
        copy.wait()
    total = by_plane[0]
    for n in range(1, 8):
        total = total + by_plane[n]
    group = 4 * pair
    for k in range(length):
        at = pl.ds(pl.multiple_of(lax.rem(z + k, length) * group, group), group)
        by_line[z, :, at] = total[:, k * group : (k + 1) * group]
    sends = [
        remote(by_line.at[z], by_line.at[z], ls.at[k], lr.at[k], line[k]) for k in range(length - 1)
    ]
    for copy in sends:
        copy.wait()
    total = by_line[0]
    for n in range(1, length):
        total = total + by_line[n]
    squares = jnp.sum(total[:2] * total[:2], axis=0, keepdims=True) + total[2:3]
    norm = jnp.broadcast_to(jnp.sqrt(jnp.sum(squares, axis=1, keepdims=True)), (8, 128))
    norm_o[...] = norm
    factor_o[...] = clip_limit / jnp.maximum(norm, clip_limit)
    gains = jnp.zeros((2, pair), F32)
    for there in range(length):
        for b in range(4):
            first_lane = (there * 4 + b) * pair
            mine = jnp.logical_and(there == z, b == 2 * y + c)
            gains = jnp.where(mine, total[:2, first_lane : first_lane + pair], gains)
    gains_o[...] = jnp.where(x == 0, gains[:, :share], gains[:, share:])
    for copy in copies:
        copy.wait()
    own.wait()


def last(wm, gain, gain_two, gates, squares, length, collective_id):
    width = gain.shape[1]
    share = wm.shape[1]
    return pl.pallas_call(
        functools.partial(last_kernel, length, share),
        out_shape=(
            jax.ShapeDtypeStruct(wm.shape, wm.dtype),
            jax.ShapeDtypeStruct((2, share), F32),
            TILE, TILE,
        ),
        in_specs=[ANY] + [VM] * 7,
        out_specs=(ANY,) + (VM,) * 3,
        scratch_shapes=[
            pltpu.VMEM((8, 4, width), F32),
            pltpu.VMEM((length, 4, width), F32),
            DMA, DMA((7,)), DMA((7,)), DMA((7,)), DMA((7,)),
            DMA((length,)), DMA((length,)),
        ],
        compiler_params=params(collective_id),
    )(wm, gain, gain_two, gates, *squares)


def minus_expm1(v):
    series = 1.0 + v * (1.0 / 8.0)
    for n in (7.0, 6.0, 5.0, 4.0, 3.0, 2.0):
        series = 1.0 + series * v * (1.0 / n)
    return jnp.where(v > -0.5, -v * series, 1.0 - jnp.exp(v))


def gelu_parts(v):
    square = v * v
    h = 0.5 * jnp.tanh(v * (GELU_CUBE * square + GELU_SCALE)) + 0.5
    return v * h, h, square


def gelu_slope(gelu, h, square):
    return h + gelu * (1.0 - h) * (6.0 * GELU_CUBE * square + 2.0 * GELU_SCALE)


CHUNK = 128


def forward_kernel(
    length, x_in, mixer, gate, chan, above, w_in,
    mixed, branch_o, decay_o, width_o, recur_o, enter_o, conv_o, xe_o, se_o, ends_o, above_o, w,
    x_part, pre, loc_h, ends, carry, hs, hr, es, er, gather_l, gather_s, gather_r, hop_s, hop_r, load_s, keep_s,
    branch, decay_k, width_k, recur_k, enter_k, conv_k, xe, se,
):
    keeps = [
        pltpu.make_async_copy(src, dst, keep_s.at[n])
        for n, (src, dst) in enumerate(
            (
                (branch, branch_o), (decay_k, decay_o), (width_k, width_o), (recur_k, recur_o),
                (enter_k, enter_o), (conv_k, conv_o), (xe, xe_o), (se, se_o),
            )
        )
    ]
    y, c, z, x = place()
    line = line_peers(length)
    seqs, span, rc = branch.shape
    part = mixed.shape[2]
    chunks = span // CHUNK

    def load(b, slot):
        at = pl.ds(pl.multiple_of(b * span, span), span)
        return pltpu.make_async_copy(x_in.at[at], x_part.at[slot], load_s.at[slot])

    load(0, 0).start()
    greet(line + gather_peers())
    hops = LineGather(w, length, hop_s, hop_r)
    hops.start(1)
    gather = Gather(above, above_o, gather_l, gather_s, gather_r)
    gather.begin()

    @pl.loop(0, seqs)
    def _(b):
        slot = b - b // 2 * 2

        @pl.when(b + 1 < seqs)
        def _():
            load(b + 1, 1 - slot).start()

        load(b, slot).wait()
        both = jnp.dot(x_part[slot], mixer[:, : 2 * part], preferred_element_type=F32)
        none = jnp.zeros((span, rc - part), F32)
        branch[b] = jnp.concatenate([both[:, :part], none], axis=1)
        low = both[:, part:].astype(BF16).astype(F32)
        xe[b, 8:] = jnp.concatenate([low, none], axis=1)

    ahead = device(y, c, lax.rem(z + 1, length), x)
    halo = remote(xe.at[:, pl.ds(span, 8)], xe.at[:, pl.ds(0, 8)], hs, hr, ahead)

    def coefficients(b, chunk):
        r = pl.multiple_of(chunk * CHUNK, CHUNK)
        at = pl.ds(r, CHUNK)
        window = xe[b, pl.ds(r, CHUNK + 8)]
        total = chan[4:5] + chan[0:1] * window[8:]
        for k in (1, 2, 3):
            total = total + chan[k : k + 1] * pltpu.roll(window, k, 0)[8:]
        low = total.astype(BF16)
        conv_k[b, at] = low
        value = low.astype(F32)
        gates = jnp.dot(low, gate[...], preferred_element_type=F32)
        recur = jax.nn.sigmoid(gates[:, :rc] + chan[5:6])
        enter = jax.nn.sigmoid(gates[:, rc:] + chan[6:7])
        log_decay = -chan[7:8] * recur
        decay = jnp.exp(log_decay)
        width = jnp.sqrt(minus_expm1(2.0 * log_decay))
        recur_k[b, at] = recur
        enter_k[b, at] = enter
        decay_k[b, at] = decay
        width_k[b, at] = width
        loc_h[b, at] = width * enter * value

    def later_chunks(i):
        b = i // (chunks - 1)
        coefficients(b, 1 + i - b * (chunks - 1))

    many = seqs * (chunks - 1)
    pl.loop(0, many // 2)(later_chunks)
    hops.arrive(1)
    if length > 2:
        hops.start(2)
    gather.middle()
    pl.loop(many // 2, many)(later_chunks)
    halo.wait()

    @pl.when(z == 0)
    def _():
        xe[:, 0:8] = jnp.zeros((seqs, 8, rc), F32)

    @pl.loop(0, seqs)
    def _(b):
        coefficients(b, 0)

    for copy in keeps[:-1]:
        copy.start()
    row = lax.broadcasted_iota(jnp.int32, (8, rc), 0)

    def tile(i, held):
        at = pl.ds(pl.multiple_of(i * 8, 8), 8)
        new = []
        for b in range(seqs):
            a, h = decay_k[b, at], loc_h[b, at]
            for n in (1, 2, 4):
                keep = row >= n
                h = h + jnp.where(keep, a * pltpu.roll(h, n, 0), 0.0)
                a = jnp.where(keep, a * pltpu.roll(a, n, 0), a)
            h = h + a * held[b][1]
            a = a * held[b][0]
            loc_h[b, at] = h
            pre[b, at] = a
            new.append((a[7:8], h[7:8]))
        return tuple(new)

    one, zero = jnp.ones((1, rc), F32), jnp.zeros((1, rc), F32)
    final = lax.fori_loop(0, span // 8, tile, ((one, zero),) * seqs)
    for b in range(seqs):
        ends[z, 0, b] = jnp.broadcast_to(final[b][0], (8, rc))
        ends[z, 1, b] = jnp.broadcast_to(final[b][1], (8, rc))
        ends_o[b] = jnp.broadcast_to(final[b][0], (8, rc))
    moves = [remote(ends.at[z], ends.at[z], es.at[k], er.at[k], line[k]) for k in range(length - 1)]
    if length > 3:
        hops.arrive(2)
        hops.start(3)
    for copy in moves:
        copy.wait()
    carry[...] = jnp.zeros_like(carry)
    for k in range(length):
        carry[...] = jnp.where(k < z, ends[k, 0] * carry[...] + ends[k, 1], carry[...])

    for b in range(seqs):
        se[b, 0:8] = carry[b]

    @pl.loop(0, seqs * chunks)
    def _(i):
        b = i // chunks
        r = pl.multiple_of((i - b * chunks) * CHUNK, CHUNK)
        at = pl.ds(r, CHUNK)
        state = loc_h[b, at] + pre[b, at] * carry[b, 0:1]
        se[b, pl.ds(r + 8, CHUNK)] = state
        gelu, _, _ = gelu_parts(branch[b, at])
        mixed[b, at] = (state * gelu)[:, :part].astype(BF16)

    keeps[-1].start()
    gather.end()
    for hop in range(min(3, length - 1), length):
        hops.arrive(hop)
        if hop + 1 < length:
            hops.start(hop + 1)
    hops.finish()
    waits(keeps)


def recur_forward(x, mixer, gate, chan, above, w, length, collective_id):
    rc = gate.shape[0]
    part = mixer.shape[1] // 3
    rows = x.shape[0] // 8
    seqs, span = 4, 2 * rows
    full = jax.ShapeDtypeStruct((seqs, span, rc), F32)
    longer = jax.ShapeDtypeStruct((seqs, span + 8, rc), F32)
    kept = (full, full, full, full, full, jax.ShapeDtypeStruct((seqs, span, rc), BF16), longer, longer)
    return pl.pallas_call(
        functools.partial(forward_kernel, length),
        out_shape=(
            jax.ShapeDtypeStruct((seqs, span, part), BF16),
            *kept,
            jax.ShapeDtypeStruct((seqs, 8, rc), F32),
            jax.ShapeDtypeStruct((8,) + above.shape, above.dtype),
            jax.ShapeDtypeStruct(w.shape, w.dtype),
        ),
        in_specs=[ANY, VM, VM, VM, ANY, ANY],
        out_specs=(VM,) + (ANY,) * 8 + (VM, ANY, ANY),
        scratch_shapes=[
            pltpu.VMEM((2, span, x.shape[1]), BF16),
            pltpu.VMEM((seqs, span, rc), F32),
            pltpu.VMEM((seqs, span, rc), F32),
            pltpu.VMEM((length, 2, seqs, 8, rc), F32),
            pltpu.VMEM((seqs, 8, rc), F32),
            DMA, DMA, DMA((length,)), DMA((length,)),
            DMA, DMA((14,)), DMA((14,)), DMA((2, length)), DMA((2, length)),
            DMA((2,)), DMA((8,)),
            *[pltpu.VMEM(v.shape, v.dtype) for v in kept],
        ],
        input_output_aliases={5: 11},
        compiler_params=params(collective_id),
        cost_estimate=pl.CostEstimate(
            flops=2 * seqs * span * rc * rc * 2, bytes_accessed=100 * 2**20, transcendentals=0
        ),
    )(x, mixer, gate, chan, above, w)


def backward_kernel(
    length, cuts, head, dmix, gate, chan, decay, width, recur, enter, conv, xe, se, ends_f, proj, block_a, block_b, *refs
):
    parts = 1 + max(cut[0] for cut in cuts)
    terms, refs = refs[:parts], refs[parts:]
    dproj, gates_o, sums, squares, block_ao, block_bo, *refs = refs
    dgate, gchan, *refs = refs
    suffix, grad, de, ends, carry, hs, hr, es, er, keep_s, move_l, move_s, move_r, *refs = refs
    kept, line_refs = refs[:8], refs[8:]
    loads = [
        pltpu.make_async_copy(src, dst, keep_s.at[n])
        for n, (src, dst) in enumerate(
            zip((dmix, proj, se, decay, width, recur, enter, conv, xe), (de.at[:, pl.ds(0, decay.shape[1])], *kept))
        )
    ]
    proj, se, decay, width, recur, enter, conv, xe = kept
    y, c, z, x = place()
    line = line_peers(length)
    greet(line + plane_peers())
    scatter = Lines(terms, cuts, length, line_refs)
    scatter.begin()
    for copy in loads:
        copy.start()
    moves = [
        exchange_steps(block_a, block_ao, move_l.at[0], move_s.at[0], move_r.at[0]),
        exchange_steps(block_b, block_bo, move_l.at[1], move_s.at[1], move_r.at[1]),
    ]
    seqs, span, rc = decay.shape
    part = dproj.shape[2] // 2
    chunks = span // CHUNK
    for copy in loads[:3]:
        copy.wait()

    @pl.loop(0, seqs * chunks)
    def _(i):
        b = i // chunks
        r = pl.multiple_of((i - b * chunks) * CHUNK, CHUNK)
        at = pl.ds(r, CHUNK)
        branch = proj[b, at]
        gelu, h, square = gelu_parts(branch)
        above = de[b, at]
        state = se[b, pl.ds(r + 8, CHUNK)]
        grad[b, at] = above * gelu
        proj[b, at] = above * state * gelu_slope(gelu, h, square)

    loads[3].wait()
    row = lax.broadcasted_iota(jnp.int32, (8, rc), 0)

    def tile(i, held):
        at = pl.ds(pl.multiple_of(span - 8 - i * 8, 8), 8)
        new = []
        for b in range(seqs):
            product, total, following = held[b]
            plain, h = decay[b, at], grad[b, at]
            a = jnp.where(row == 7, following, pltpu.roll(plain, 7, 0))
            for n in (1, 2, 4):
                keep = row < 8 - n
                h = h + jnp.where(keep, a * pltpu.roll(h, 8 - n, 0), 0.0)
                a = jnp.where(keep, a * pltpu.roll(a, 8 - n, 0), a)
            h = h + a * total
            a = a * product
            grad[b, at] = h
            suffix[b, at] = a
            new.append((a[0:1], h[0:1], plain[0:1]))
        return tuple(new)

    one, zero = jnp.ones((1, rc), F32), jnp.zeros((1, rc), F32)
    final = lax.fori_loop(0, span // 8, tile, ((one, zero, one),) * seqs)
    for b in range(seqs):
        ends[z, 0, b] = ends_f[b]
        ends[z, 1, b] = jnp.broadcast_to(final[b][1] * final[b][2], (8, rc))
    tails = [remote(ends.at[z], ends.at[z], es.at[k], er.at[k], line[k]) for k in range(length - 1)]
    for copy in tails:
        copy.wait()
    scatter.start()
    scatter.start()
    for copy in loads[4:]:
        copy.wait()
    carry[...] = jnp.zeros_like(carry)
    for k in reversed(range(length)):
        carry[...] = jnp.where(k > z, ends[k, 0] * carry[...] + ends[k, 1], carry[...])

    gchan[...] = jnp.zeros_like(gchan)

    @pl.loop(0, seqs * chunks)
    def _(i):
        b = i // chunks
        r = pl.multiple_of((i - b * chunks) * CHUNK, CHUNK)
        at = pl.ds(r, CHUNK)
        g = grad[b, at] + suffix[b, at] * carry[b, 0:1]
        a, w, ra, ri = decay[b, at], width[b, at], recur[b, at], enter[b, at]
        value = conv[b, at].astype(F32)
        before = pltpu.roll(se[b, pl.ds(r, CHUNK + 8)], 1, 0)[8:]
        dla = g * before * a - g * ri * value * (a * a) / w
        slope = dla * ra * (1.0 - ra)
        dpa = (-chan[7:8] * slope).astype(BF16)
        dpi = (g * w * value * ri * (1.0 - ri)).astype(BF16)
        dgate[b, at, :rc] = dpa
        dgate[b, at, rc:] = dpi
        gchan[5] += fold(dpa.astype(F32))
        gchan[6] += fold(dpi.astype(F32))
        gchan[7] += fold(dla * ra)
        back = lax.dot_general(
            dgate[b, at], gate[...], (((1,), (1,)), ((), ())), preferred_element_type=F32
        )
        dcv = (g * w * ri + back).astype(BF16).astype(F32)
        de[b, at] = dcv
        gchan[4] += fold(dcv)

    behind = device(y, c, lax.rem(z + length - 1, length), x)
    halo = remote(de.at[:, pl.ds(0, 8)], de.at[:, pl.ds(span, 8)], hs, hr, behind)
    halo.wait()
    scatter.start()
    scatter.start()
    low = conv[...].reshape(seqs * span, rc)
    recur_grad, enter_grad = (
        contract_first(low, dgate[:, :, at].reshape(seqs * span, rc)) for at in (slice(0, rc), slice(rc, 2 * rc))
    )

    @pl.when(z == length - 1)
    def _():
        de[:, span:] = jnp.zeros((seqs, 8, rc), F32)

    @pl.loop(0, seqs * chunks)
    def _(i):
        b = i // chunks
        r = pl.multiple_of((i - b * chunks) * CHUNK, CHUNK)
        at = pl.ds(r, CHUNK)
        window = de[b, pl.ds(r, CHUNK + 8)]
        inputs = xe[b, pl.ds(r, CHUNK + 8)]
        dcv = window[:CHUNK]
        total = chan[0:1] * dcv
        gchan[0] += fold(dcv * inputs[8:])
        for k in (1, 2, 3):
            total = total + chan[k : k + 1] * pltpu.roll(window, CHUNK + 8 - k, 0)[:CHUNK]
            gchan[k] += fold(dcv * pltpu.roll(inputs, k, 0)[8:])
        dproj[b, at] = jnp.concatenate([proj[b, at, :part], total[:, :part]], axis=1).astype(BF16)

    rates = 8.0 * minus_expm1(chan[7:8] * (-1.0 / 8.0))
    channels = [jnp.sum(gchan[n], axis=0, keepdims=True) for n in range(8)]
    channels[7] = channels[7] * rates
    channels = lax.dot_general(
        jnp.concatenate(channels), unit(8).astype(F32), (((0,), (0,)), ((), ())),
        precision=lax.Precision.HIGHEST, preferred_element_type=F32,
    )
    blocks = []
    for first_row in range(0, part, head):
        at = slice(first_row, first_row + head)
        blocks.append(jnp.concatenate([recur_grad[at, at], enter_grad[at, at]], axis=1))
    pack = jnp.concatenate(
        [jnp.concatenate(blocks), channels[:part], jnp.zeros((part, rc - 2 * head - 8), F32)], axis=1
    )
    rows = part // length
    if rows < gates_o.shape[1]:
        gates_o[...] = jnp.zeros_like(gates_o)
    for n in range(length):
        gates_o[n, :rows] = pack[n * rows : (n + 1) * rows]
    scatter.end(sums, squares)
    for copies, own in moves:
        for copy in copies:
            copy.wait()
        own.wait()


def recur_backward(dmix, gate, chan, kept, part, head, blocks, terms, cuts, length, collective_id):
    proj, decay, width, recur, enter, conv, xe, se, ends = kept
    seqs, span, rc = decay.shape
    gate_pad = -(-(part // length) // 16) * 16
    line_rows, columns = terms[0].shape[1], sum(cut[2] for cut in cuts)
    return pl.pallas_call(
        functools.partial(backward_kernel, length, cuts, head),
        out_shape=(
            jax.ShapeDtypeStruct((seqs, span, 2 * part), BF16),
            jax.ShapeDtypeStruct((length, gate_pad, rc), F32),
            jax.ShapeDtypeStruct((line_rows, columns), BF16), TILE,
            *[jax.ShapeDtypeStruct(block.shape, BF16) for block in blocks],
        ),
        in_specs=[ANY, VM, VM] + [ANY] * 7 + [VM] + [ANY] * (3 + len(terms)),
        out_specs=(VM,) * 4 + (ANY, ANY),
        scratch_shapes=[
            pltpu.VMEM((seqs, span, 2 * rc), BF16),
            pltpu.VMEM((8, 8, rc), F32),
            pltpu.VMEM((seqs, span, rc), F32),
            pltpu.VMEM((seqs, span, rc), F32),
            pltpu.VMEM((seqs, span + 8, rc), F32),
            pltpu.VMEM((length, 2, seqs, 8, rc), F32),
            pltpu.VMEM((seqs, 8, rc), F32),
            DMA, DMA, DMA((length,)), DMA((length,)),
            DMA((9,)), DMA((2,)), DMA((2, 7)), DMA((2, 7)),
            *[
                pltpu.VMEM(shape, dtype)
                for shape, dtype in (
                    (decay.shape, F32), (se.shape, F32), (decay.shape, F32), (decay.shape, F32),
                    (decay.shape, F32), (decay.shape, F32), (decay.shape, BF16), (xe.shape, F32),
                )
            ],
        ]
        + lines_scratch(length, line_rows, cuts),
        compiler_params=params(collective_id),
        cost_estimate=pl.CostEstimate(
            flops=2 * seqs * span * rc * rc * 2, bytes_accessed=120 * 2**20, transcendentals=0
        ),
    )(dmix, gate, chan, decay, width, recur, enter, conv, xe, se, ends, proj, *blocks, *terms)


def contract_last(left, right):
    return lax.dot_general(
        left, right, (((1,), (1,)), ((), ())), preferred_element_type=F32
    )


def contract_first(left, right):
    return lax.dot_general(
        left, right, (((0,), (0,)), ((), ())), preferred_element_type=F32
    )


def resident(shape):
    return pl.BlockSpec(shape, lambda i: (0, 0), pipeline_mode=pl.Buffered(1))


STEPS = 4


def feed_forward(x, above, gate_up, down, hid, dboth):
    f = hid.shape[1]
    both = jnp.dot(x[...], gate_up, preferred_element_type=F32)
    gg, uu = both[:, :f], both[:, f:]
    dhid = jnp.dot(above[...], down, preferred_element_type=F32)
    gelu, h, square = gelu_parts(gg)
    hid[...] = (gelu * uu).astype(BF16)
    dboth[:, :f] = (dhid * uu * gelu_slope(gelu, h, square)).astype(BF16)
    dboth[:, f:] = (dhid * gelu).astype(BF16)


def grads_compute(x, above, hid, dboth, gate_o, up_o, down_o):
    f = hid.shape[1]
    both = contract_first(x[...], dboth[...]).astype(BF16)
    gate_o[...] = both[:, :f]
    up_o[...] = both[:, f:]
    down_o[...] = contract_first(above[...], hid[...]).astype(BF16)


def mlp_specs(tokens, model, f):
    def rows(width):
        return pl.BlockSpec((tokens // STEPS, width), lambda i: (jnp.minimum(i, STEPS - 1), 0))

    columns = pl.BlockSpec((tokens, model // STEPS), lambda i: (0, jnp.maximum(i - STEPS, 0)))
    grads = pl.BlockSpec((model // STEPS, f), lambda i: (jnp.maximum(i - STEPS, 0), 0))
    return rows, columns, grads


def keep_units(step, hid_all, dboth_all, hid, dboth):
    rows = hid.shape[0]
    at = pl.ds(pl.multiple_of(step * rows, rows), rows)
    hid_all[at] = hid[...]
    dboth_all[at] = dboth[...]


def early_mlp_kernel(
    length, x, above, x_columns, above_columns, gate_up, down, w_in,
    hid, dboth, gate_o, up_o, down_o, w, hid_all, dboth_all, ss, rs
):
    step = pl.program_id(0)
    hops = LineGather(w, length, ss, rs)

    @pl.when(step == 0)
    def _():
        greet(line_neighbours(length))
        if length > 2:
            hops.start(2)

    @pl.when(step == STEPS)
    def _():
        for hop in range(2, length - 1):
            hops.arrive(hop)
            hops.start(hop + 1)

    @pl.when(step < STEPS)
    def _():
        feed_forward(x, above, gate_up[...], down[...], hid, dboth)
        keep_units(step, hid_all, dboth_all, hid, dboth)

    @pl.when(step >= STEPS)
    def _():
        grads_compute(x_columns, above_columns, hid_all, dboth_all, gate_o, up_o, down_o)

    @pl.when(step == 2 * STEPS - 1)
    def _():
        hops.arrive(length - 1)
        hops.finish(2, length - 1)


def early_mlp(x, above, gate_up, down, w, length, collective_id):
    tokens, model = x.shape
    f = down.shape[1]
    rows, columns, grads = mlp_specs(tokens, model, f)
    grad_shape = jax.ShapeDtypeStruct((model, f), BF16)
    return pl.pallas_call(
        functools.partial(early_mlp_kernel, length),
        grid=(2 * STEPS,),
        out_shape=(
            jax.ShapeDtypeStruct((tokens, f), BF16),
            jax.ShapeDtypeStruct((tokens, 2 * f), BF16),
            grad_shape, grad_shape, grad_shape,
            jax.ShapeDtypeStruct(w.shape, w.dtype),
        ),
        in_specs=[rows(model), rows(model), columns, columns, resident(gate_up.shape), resident(down.shape), ANY],
        out_specs=(rows(f), rows(2 * f)) + (grads,) * 3 + (ANY,),
        scratch_shapes=[pltpu.VMEM((tokens, f), BF16), pltpu.VMEM((tokens, 2 * f), BF16)]
        + [DMA((2, length)), DMA((2, length))],
        input_output_aliases={6: 5},
        compiler_params=params(collective_id),
        cost_estimate=pl.CostEstimate(flops=12 * tokens * model * f, bytes_accessed=50 * 2**20, transcendentals=0),
    )(x, above, x, above, gate_up, down, w)


def late_mlp_kernel(
    length, cuts, x, above, x_columns, above_columns, hid_one, dboth_one, gate_up_in, down_in, late_in, *refs
):
    terms, refs = refs[: len(cuts)], refs[len(cuts) :]
    out, back, gate_o, up_o, down_o, sums, squares, *refs = refs
    gate_up, down, hid, dboth, hid_all, dboth_all, load_s, *line_refs = refs
    step = pl.program_id(0)
    line = LineScatter([(ref, *cut) for ref, cut in zip(terms, cuts)], length, *line_refs)
    f, g = hid_one.shape[1], hid.shape[1]
    loads = local_copies(
        (
            (late_in.at[:, pl.ds(0, 2 * g)], gate_up.at[:, pl.ds(2 * f, 2 * g)]),
            (late_in.at[:, pl.ds(2 * g, g)], down.at[:, pl.ds(f, g)]),
            (down_in, down.at[:, pl.ds(0, f)]),
            (gate_up_in, gate_up.at[:, pl.ds(0, 2 * f)]),
        ),
        load_s,
    )

    @pl.when(step == 0)
    def _():
        starts(loads)
        greet(line_neighbours(length))
        line.load((1,))
        line.start()
        line.load((*range(2, length), 0))
        waits(loads)

    for hop in range(2, length):

        @pl.when(step == min(2 * STEPS - 2, 2 * (hop - 1)))
        def _():
            line.next = hop
            line.start()

    @pl.when(step < STEPS)
    def _():
        feed_forward(x, above, gate_up[:, 2 * f :], down[:, f:], hid, dboth)
        keep_units(step, hid_all, dboth_all, hid, dboth)
        units = jnp.concatenate([hid_one[...], hid[...]], axis=1)
        out[...] = contract_last(units, down[...]).astype(BF16)
        units = jnp.concatenate([dboth_one[...], dboth[...]], axis=1)
        back[...] = contract_last(units, gate_up[...]).astype(BF16)

    @pl.when(step >= STEPS)
    def _():
        grads_compute(x_columns, above_columns, hid_all, dboth_all, gate_o, up_o, down_o)

    @pl.when(step == 2 * STEPS - 1)
    def _():
        squares[...] = jnp.zeros_like(squares)
        line.end(sums, 0, squares)


def late_mlp(x, above, early_units, gate_up, down, late, terms, cuts, length, collective_id):
    tokens, model = x.shape
    f, g = down.shape[1], late.shape[1] // 3
    line_rows = terms[0].shape[1]
    cut = sum(columns for _, columns in cuts)
    rows, columns, grads = mlp_specs(tokens, model, g)

    def whole(shape):
        return pl.BlockSpec(shape, lambda i: (0, 0))

    return pl.pallas_call(
        functools.partial(late_mlp_kernel, length, cuts),
        grid=(2 * STEPS,),
        out_shape=(jax.ShapeDtypeStruct((tokens, model), BF16),) * 2
        + (jax.ShapeDtypeStruct((model, g), BF16),) * 3
        + (jax.ShapeDtypeStruct((line_rows, cut), BF16), TILE),
        in_specs=[rows(model), rows(model), columns, columns, rows(f), rows(2 * f)]
        + [ANY] * (3 + len(terms)),
        out_specs=(rows(model),) * 2 + (grads,) * 3 + (whole((line_rows, cut)), whole((8, 128))),
        scratch_shapes=[
            pltpu.VMEM((model, 2 * f + 2 * g), BF16),
            pltpu.VMEM((model, f + g), BF16),
            pltpu.VMEM((tokens // STEPS, g), BF16),
            pltpu.VMEM((tokens // STEPS, 2 * g), BF16),
            pltpu.VMEM((tokens, g), BF16),
            pltpu.VMEM((tokens, 2 * g), BF16),
            DMA((4,)),
        ]
        + line_scratch(length, line_rows, cut, len(cuts)),
        compiler_params=params(collective_id),
        cost_estimate=pl.CostEstimate(
            flops=6 * tokens * model * (f + 3 * g), bytes_accessed=70 * 2**20, transcendentals=0
        ),
    )(x, above, x, above, *early_units, gate_up, down, late, *terms)


def adam_step(weight, grad, first, second, factor, rate, decay_rate):
    clipped = grad * factor
    first_new = beta_first * first + (1.0 - beta_first) * clipped
    second_new = beta_second * second + (1.0 - beta_second) * clipped * clipped
    first_hat = first_new / (1.0 - beta_first**STEP)
    second_hat = second_new / (1.0 - beta_second**STEP)
    weight_new = weight - rate * (
        first_hat / (jnp.sqrt(second_hat) + adam_eps) + decay_rate * weight
    )
    return (first_new, second_new, weight_new)


def small_steps(factor, refs, outs):
    gains_sum, gates_sum, *states = refs
    rows, columns = states[3].shape
    channels = lax.dot_general(
        unit(8).astype(F32), gates_sum[:rows, columns : columns + 8], (((1,), (1,)), ((), ())),
        precision=lax.Precision.HIGHEST, preferred_element_type=F32,
    )
    grads = gains_sum[...], gates_sum[:rows, :columns], channels
    rates = (rate_gains, 0.0), (rate_matrix, decay_matrix), (rate_channel, 0.0)
    for n in range(3):
        w, m, v = states[3 * n : 3 * n + 3]
        results = adam_step(w[...], grads[n], m[...], v[...], factor, *rates[n])
        for out, result in zip(outs[3 * n : 3 * n + 3], results):
            out[...] = result


def adam_kernel(sources, factor, *refs):
    states, refs = refs[: 3 * len(sources)], refs[3 * len(sources) :]
    count = sum(len(source) for source in sources)
    grads, small, refs = refs[:count], refs[count : count + 11], refs[count + 11 :]
    results, outs = refs[:2], refs[2:]
    for result, out in zip(results, outs[-2:]):
        out[...] = result[...]
    one = factor[0:1, 0:1]
    pl.when(pl.program_id(0) == 0)(lambda: small_steps(one, small, outs[3 * len(sources) : -2]))
    for n, source in enumerate(sources):
        parts = []
        for pieces in source:
            ref, *grads = grads
            for first, columns, at, stride in pieces:
                for t in range(8):
                    parts.append((at + t * stride, columns, ref, t, first))
        parts.sort(key=lambda part: part[0])
        w, m, v = states[3 * n : 3 * n + 3]
        m_o, v_o, w_o = outs[3 * n : 3 * n + 3]
        run = []
        for at, columns, ref, t, first in parts:
            run.append((at, columns, ref[t, :, first : first + columns].astype(F32)))
            end = at + columns
            if end % 128:
                continue
            grad = jnp.concatenate([piece for _, _, piece in run], axis=1) if len(run) > 1 else run[0][2]
            cols = slice(run[0][0], end)
            run = []
            first_new, second_new, weight_new = adam_step(
                w[:, cols], grad, m[:, cols], v[:, cols], one, rate_matrix, decay_matrix
            )
            m_o[:, cols] = first_new
            v_o[:, cols] = second_new
            w_o[:, cols] = weight_new


def adam(matrices, small, factor, passed):
    rows = matrices[0][0].shape[0]
    step = min(rows, 16)

    def block(v):
        return pl.BlockSpec((step, v.shape[1]), lambda i: (i, 0))

    def whole(v):
        return pl.BlockSpec(v.shape, lambda i: (0, 0))

    states = [v for matrix in matrices for v in matrix[:3]]
    grads = [g for matrix in matrices for g in matrix[3]]
    results = [*states, *small[2:], *passed]
    steps = rows // step

    def slab(v):
        return pl.BlockSpec((v.shape[0] // steps, v.shape[1]), lambda i: (i, 0))

    return pl.pallas_call(
        functools.partial(adam_kernel, [matrix[4] for matrix in matrices]),
        grid=(steps,),
        out_shape=tuple(jax.ShapeDtypeStruct(v.shape, v.dtype) for v in results),
        in_specs=[pl.BlockSpec((8, 128), lambda i: (0, 0))]
        + [block(v) for v in states]
        + [pl.BlockSpec((8, step, g.shape[2]), lambda i: (0, i, 0)) for g in grads]
        + [whole(v) for v in small]
        + [slab(v) for v in passed],
        out_specs=tuple(block(v) for v in states)
        + tuple(whole(v) for v in small[2:])
        + tuple(slab(v) for v in passed),
        compiler_params=pltpu.CompilerParams(vmem_limit_bytes=VMEM_BYTES),
        cost_estimate=pl.CostEstimate(
            flops=0, bytes_accessed=sum(8 * v.size for v in states), transcendentals=0
        ),
    )(factor, *states, *grads, *small, *passed)


def on_device(
    block_input,
    out_grad,
    norm_gains,
    mixer_weight,
    gate_weight,
    chan_params,
    mlp_weight,
    first_gains,
    first_mixer,
    first_gate,
    first_chan,
    first_mlp,
    second_gains,
    second_mixer,
    second_gate,
    second_chan,
    second_mlp,
):
    length = lax.axis_size("seq") // 2
    z = lax.axis_index("seq") // 2
    tokens, model = block_input.shape[1:]
    share = mixer_weight.shape[0]
    pair = 2 * share
    lru = mixer_weight.shape[1] // 3
    hidden = mlp_weight.shape[1] // 3
    r8, f8 = lru // 8, hidden // 8
    rc = -(-r8 // 128) * 128
    head = gate_weight.shape[1] // 2
    heads = r8 // head
    gate_rows = gate_weight.shape[0]
    gate_pad = -(-gate_rows // 16) * 16

    x = lax.axis_index("seq") - 2 * z
    batch = lax.axis_index("batch")
    plain = pair % 128 == 0

    def turned(v):
        if plain:
            return v
        v = v.reshape(v.shape[0], 4, length, pair).swapaxes(1, 2)
        return jnp.roll(v, -z, axis=1).reshape(v.shape[0], model)

    def turned_back(v):
        if plain:
            return v
        v = jnp.roll(v.reshape(v.shape[0], length, 4, pair), z, axis=1)
        return v.swapaxes(1, 2).reshape(v.shape[0], model)

    normed_one, mixer_full, mlp_gu, mlp_down, late, gains, gate, chan, inputs, above = first(
        turned(block_input[0]),
        turned(out_grad[0]),
        mixer_weight,
        mlp_weight,
        norm_gains,
        gate_weight,
        chan_params,
        rc,
        length,
        1,
    )
    normed_one = normed_one.reshape(8 * tokens, model)
    mixer_full = mixer_full.reshape(model, 3 * r8)
    mixed, *kept, grad_out, mlp_down = recur_forward(
        normed_one, mixer_full, gate, chan, above, mlp_down, length, 2
    )
    grad_out = grad_out.reshape(8 * tokens, model)
    mixed = mixed.reshape(8 * tokens, r8)
    residual, normed_two, mlp_gu, late = middle(mixed, mixer_full, inputs, gains, mlp_gu, late, length, 3)
    normed_two = normed_two.reshape(8 * tokens, model)
    h1 = early(f8)
    h2 = f8 - h1
    mlp_gu = mlp_gu.reshape(model, 2 * h1)
    mlp_down = mlp_down.reshape(model, h1)
    hid, dboth, *early_terms, late = early_mlp(normed_two, grad_out, mlp_gu, mlp_down, late, length, 9)
    gate_one, up_one, down_one = (v.reshape(length, 8 * share, h1) for v in early_terms)
    cut = h1 // 4
    mlp_part, dnormed_two, *late_terms, sums_zero, squares_zero = late_mlp(
        normed_two, grad_out, (hid, dboth), mlp_gu, mlp_down, late.reshape(model, 3 * h2),
        (gate_one, up_one), ((0, h1), (0, cut)), length, 11,
    )
    gate_two, up_two, down_two = (v.reshape(length, 8 * share, h2) for v in late_terms)

    grad_residual, gain_two, dmz, dmix, sums_one, squares_one = turn(
        dnormed_two, residual, above, gains, mixer_full, rc,
        (up_one, down_one, gate_two), ((0, cut, h1 - cut), (1, 0, h1), (2, 0, h2)),
        length, 4,
    )
    dmz = dmz.reshape(8 * tokens, model)
    span = 2 * tokens
    dmix = dmix.reshape(4, span, rc)
    sums_zero, sums_one = (v.reshape(8, share, v.shape[1]) for v in (sums_zero, sums_one))
    dproj, gate_back, sums_two, squares_two, back_zero, back_one = recur_backward(
        dmix, gate, chan, kept, r8, head, (sums_zero, sums_one),
        (up_two, down_two), ((0, 0, h2), (1, 0, h2)), length, 6,
    )
    dproj = dproj.reshape(4 * span, 2 * r8)
    input_grad, gain_one, gates_sum, block_output, back_two, mixer_sums, squares_three = closing(
        normed_one, dmz, dproj, mixed, mixer_full, mlp_part, residual, sums_two,
        inputs, grad_residual, gains, gate_back, length, 7,
    )
    mixer_back, gains_sum, norm, factor = last(
        mixer_sums.reshape(8, share, 3 * r8), gain_one, gain_two, gates_sum,
        (squares_zero, squares_one, squares_two, squares_three), length, 8,
    )
    mlp_sources = (
        [(0, h1, 0, f8), (h1, cut, hidden, f8)],
        [
            (0, h1 - cut, hidden + cut, f8),
            (h1 - cut, h1, 2 * hidden, f8),
            (2 * h1 - cut, h2, h1, f8),
        ],
        [(0, h2, hidden + h1, f8), (h2, h2, 2 * hidden + h1, f8)],
    )
    states = adam(
        (
            (
                mixer_weight, first_mixer, second_mixer, (mixer_back,),
                ([(n * r8, r8, n * lru, r8) for n in range(3)],),
            ),
            (mlp_weight, first_mlp, second_mlp, (back_zero, back_one, back_two), mlp_sources),
        ),
        (
            gains_sum, gates_sum, norm_gains, first_gains, second_gains, gate_weight, first_gate, second_gate,
            chan_params, first_chan, second_chan,
        ),
        factor,
        (block_output, input_grad),
    )
    *states, block_output, input_grad = states
    mixer_up, mlp_up, gains_up, gate_up, chan_up = (states[3 * n : 3 * n + 3] for n in range(5))
    return (
        turned_back(block_output)[None],
        turned_back(input_grad)[None],
        norm[0, 0],
        *gains_up,
        *mixer_up,
        *gate_up,
        *chan_up,
        *mlp_up,
    )


def solution(mesh):
    rows = P(("batch", "seq"), None)
    columns = P(None, ("batch", "seq"))
    data = P("batch", "seq", None)
    weights = (columns, rows, rows, columns, rows)
    in_specs = (data, data) + weights * 3
    triples = tuple(spec for spec in weights for _ in range(3))
    return jax.shard_map(
        on_device,
        mesh=mesh,
        in_specs=in_specs,
        out_specs=(data, data, P()) + triples,
        check_vma=False,
    )
```

```python
import functools
import math

import jax
import jax.numpy as jnp
from jax import lax
from jax.experimental import pallas as pl
from jax.experimental.pallas import tpu as pltpu
from jax.sharding import PartitionSpec as P

STEP = 10
norm_eps = 1e-06
clip_limit = 1.0
beta_first = 0.9
beta_second = 0.999
adam_eps = 1e-08
rate_matrix = 0.05
rate_gains = 0.8
rate_channel = 2.0
decay_matrix = 0.1

MESH = pl.DeviceIdType.MESH
F32 = jnp.float32
BF16 = jnp.bfloat16
ANY = pl.BlockSpec(memory_space=pl.ANY)
VM = pl.BlockSpec(memory_space=pltpu.VMEM)
FLIPS = [(fy, fc, fx) for fy in (0, 1) for fc in (0, 1) for fx in (0, 1) if fy + fc + fx]
GELU_SCALE = math.sqrt(2.0 / math.pi)
GELU_CUBE = 0.044715 * GELU_SCALE


def place():
    b = lax.axis_index("batch")
    s = lax.axis_index("seq")
    y, z = b // 2, s // 2
    return y, b - 2 * y, z, s - 2 * z


def device(y, c, z, x):
    return (y * 2 + c, z * 2 + x)


def rank(y, c, x):
    return (y * 2 + c) * 2 + x


def flip(v, f):
    return 1 - v if f else v


def greet(peers):
    barrier = pltpu.get_barrier_semaphore()
    for peer in peers:
        pl.semaphore_signal(barrier, inc=1, device_id=peer, device_id_type=MESH)
    pl.semaphore_wait(barrier, len(peers))


def remote(src, dst, send, recv, to):
    copy = pltpu.make_async_remote_copy(
        src_ref=src, dst_ref=dst, send_sem=send, recv_sem=recv, device_id=to, device_id_type=MESH
    )
    copy.start()
    return copy


VMEM_BYTES = 63 * 2**20


def params(collective_id):
    return pltpu.CompilerParams(
        collective_id=collective_id, has_side_effects=True, vmem_limit_bytes=VMEM_BYTES
    )


DMA = pltpu.SemaphoreType.DMA


def gather_peers():
    y, c, z, x = place()
    return [device(y, c, z, 1 - x), device(1 - y, c, z, x), device(y, 1 - c, z, x)]


class Gather:
    def __init__(self, a, o, loc, ss, rs):
        y, c, z, x = place()
        self.to_x, self.to_y, self.to_c = gather_peers()
        self.me, self.bx = rank(y, c, x), rank(y, c, 1 - x)
        self.by, self.bd = rank(1 - y, c, x), rank(1 - y, c, 1 - x)
        half = a.shape[0] // 2
        self.lo, self.hi = pl.ds(0, half), pl.ds(half, half)
        self.a, self.o, self.loc, self.ss, self.rs = a, o, loc, ss, rs
        self.done, self.last = [], []

    def send(self, src, dst, k, to):
        copy = remote(src, dst, self.ss.at[k], self.rs.at[k], to)
        self.done.append(copy)
        return copy

    def relay(self, block, part, k, to):
        return self.send(self.o.at[block, part], self.o.at[block, part], k, to)

    def begin_half(self, half):
        a, o, me = self.a, self.o, self.me
        part = (self.lo, self.hi)[half]
        if half == 0:
            self.s0 = self.send(a.at[part], o.at[me, part], 0, self.to_x)
            self.s3 = self.send(a.at[part], o.at[me, part], 3, self.to_y)
        else:
            self.s1 = self.send(a.at[part], o.at[me, part], 1, self.to_y)
            self.s2 = self.send(a.at[part], o.at[me, part], 2, self.to_x)
        self.last.append(self.send(a.at[part], o.at[me, part], (4, 13)[half], self.to_c))
        if half == 1:
            self.own = pltpu.make_async_copy(a, o.at[me], self.loc)
            self.own.start()

    def begin(self):
        a, o, me, lo, hi = self.a, self.o, self.me, self.lo, self.hi
        self.s0 = self.send(a.at[lo], o.at[me, lo], 0, self.to_x)
        self.s1 = self.send(a.at[hi], o.at[me, hi], 1, self.to_y)
        self.s2 = self.send(a.at[hi], o.at[me, hi], 2, self.to_x)
        self.s3 = self.send(a.at[lo], o.at[me, lo], 3, self.to_y)
        self.last += [self.send(a.at[part], o.at[me, part], k, self.to_c) for part, k in ((lo, 4), (hi, 13))]
        self.own = pltpu.make_async_copy(a, o.at[me], self.loc)
        self.own.start()

    def middle(self):
        self.s0.wait_recv()
        self.s5 = self.relay(self.bx, self.lo, 5, self.to_y)
        self.last.append(self.relay(self.bx, self.lo, 7, self.to_c))
        self.s1.wait_recv()
        self.s6 = self.relay(self.by, self.hi, 6, self.to_x)
        self.last.append(self.relay(self.by, self.hi, 8, self.to_c))

    def relays(self, mark=lambda: None):
        self.s2.wait_recv()
        self.last.append(self.relay(self.bx, self.hi, 9, self.to_c))
        self.s3.wait_recv()
        self.last.append(self.relay(self.by, self.lo, 10, self.to_c))
        mark()
        self.s5.wait_recv()
        self.last.append(self.relay(self.bd, self.lo, 11, self.to_c))
        self.s6.wait_recv()
        self.last.append(self.relay(self.bd, self.hi, 12, self.to_c))

    def finish(self, skip=0, own=True):
        for copy in self.last[skip:]:
            copy.wait_recv()
        for copy in self.done:
            copy.wait_send()
        if own:
            self.own.wait()

    def end(self, mark=lambda: None):
        self.relays(mark)
        self.finish()


def scatter_steps(p, o, mine, sib, part, got, loc, ss, rs, prepare=None):
    y, c, z, x = place()
    to_x, to_y, to_c = gather_peers()
    half = o.shape[0] // 2
    step = 16
    cut = (pl.ds(0, half), pl.ds(half, half))
    where = ((1 - y, 1 - x), (1 - y, x), (y, 1 - x), (y, x))
    order = [(0, 0), (0, 1), (1, 0), (2, 1), (2, 0), (1, 1), (3, 0), (3, 1)]
    from_c, own, sends = {}, {}, []
    for n, (t, h) in enumerate(order):
        ty, tx = where[t]
        if prepare and all(key[0] != t for key in own):
            prepare(rank(ty, c, tx))
            prepare(rank(ty, 1 - c, tx))
        own[t, h] = pltpu.make_async_copy(
            p.at[rank(ty, c, tx), cut[h]], mine.at[t, h], loc.at[n]
        )
        own[t, h].start()
        from_c[t, h] = remote(
            p.at[rank(ty, 1 - c, tx), cut[h]], sib.at[t, h], ss.at[n], rs.at[n], to_c
        )
        sends.append(from_c[t, h])
    yield "begun"

    def add(dst, t, h, extra):
        own[t, h].wait()
        from_c[t, h].wait_recv()

        @pl.loop(0, half // step)
        def _(i):
            at = pl.ds(pl.multiple_of(i * step, step), step)
            total = mine[t, h, at].astype(F32) + sib[t, h, at].astype(F32)
            for ref in extra:
                total = total + ref[at].astype(F32)
            dst[at] = total.astype(dst.dtype)

    def send(k, slot, to):
        copy = remote(part.at[k], got.at[slot], ss.at[8 + k], rs.at[8 + slot], to)
        sends.append(copy)
        return copy

    def arrival(slot):
        return pltpu.make_async_remote_copy(
            src_ref=part.at[0], dst_ref=got.at[slot], send_sem=ss.at[8], recv_sem=rs.at[8 + slot],
            device_id=to_x, device_id_type=MESH,
        )

    add(part.at[0], 0, 0, ())
    send(0, 1, to_y)
    add(part.at[1], 0, 1, ())
    send(1, 3, to_x)
    add(part.at[2], 1, 0, ())
    send(2, 0, to_y)
    add(part.at[3], 2, 1, ())
    send(3, 2, to_x)
    yield "sent"
    arrival(1).wait_recv()
    add(part.at[4], 2, 0, (got.at[1],))
    send(4, 4, to_x)
    yield "early"
    arrival(3).wait_recv()
    add(part.at[5], 1, 1, (got.at[3],))
    send(5, 5, to_y)
    yield "late"
    arrival(0).wait_recv()
    arrival(4).wait_recv()
    add(o.at[cut[0]], 3, 0, (got.at[0], got.at[4]))
    yield "low half"
    arrival(2).wait_recv()
    arrival(5).wait_recv()
    add(o.at[cut[1]], 3, 1, (got.at[2], got.at[5]))
    yield "high half"
    for copy in sends:
        copy.wait_send()


def scatter_scratch(half, width):
    return [
        pltpu.VMEM((4, 2, half, width), BF16),
        pltpu.VMEM((4, 2, half, width), BF16),
        pltpu.VMEM((6, half, width), BF16),
        pltpu.VMEM((6, half, width), BF16),
        DMA((8,)),
        DMA((14,)),
        DMA((14,)),
    ]


def exchange_steps(a, o, loc, ss, rs):
    y, c, z, x = place()
    me = rank(y, c, x)
    dst = o.at[me]
    rows = o.shape[1]

    def block(t):
        if len(a.shape) == 3:
            return a.at[t]
        return a.at[pl.ds(pl.multiple_of(t * rows, rows), rows)]

    copies = []
    for n, (fy, fc, fx) in enumerate(FLIPS):
        ty, tc, tx = flip(y, fy), flip(c, fc), flip(x, fx)
        copies.append(remote(block(rank(ty, tc, tx)), dst, ss.at[n], rs.at[n], device(ty, tc, z, tx)))
    own = pltpu.make_async_copy(block(me), dst, loc)
    own.start()
    return copies, own


def plane_peers():
    y, c, z, x = place()
    return [device(flip(y, fy), flip(c, fc), z, flip(x, fx)) for fy, fc, fx in FLIPS]


def line_peers(length):
    y, c, z, x = place()
    return [device(y, c, lax.rem(z + k, length), x) for k in range(1, length)]


class LineGather:
    def __init__(self, buf, length, ss, rs):
        y, c, z, x = place()
        self.z, self.length, self.buf, self.ss, self.rs = z, length, buf, ss, rs
        self.up = device(y, c, lax.rem(z + 1, length), x)
        self.down = device(y, c, lax.rem(z + length - 1, length), x)

    def copy(self, hop, upward):
        length, buf = self.length, self.buf
        src, dst = ((length - hop + 1) % length, length - hop) if upward else (hop - 1, hop)
        way = 0 if upward else 1
        return pltpu.make_async_remote_copy(
            src_ref=buf.at[src], dst_ref=buf.at[dst], send_sem=self.ss.at[way, hop - 1],
            recv_sem=self.rs.at[way, hop - 1], device_id=self.up if upward else self.down,
            device_id_type=MESH,
        )

    def sends(self, hop, act):
        z, length = self.z, self.length

        @pl.when(jnp.logical_and(z + 1 < length, z >= hop - 1))
        def _():
            act(self.copy(hop, True))

        @pl.when(jnp.logical_and(z >= 1, z + hop - 1 < length))
        def _():
            act(self.copy(hop, False))

    def start(self, hop):
        self.sends(hop, lambda copy: copy.start())

    def start_piece(self, n):
        for way, last, dst in ((0, self.z + 1 < self.length, self.length - 1), (1, self.z >= 1, 1)):

            @pl.when(last)
            def _():
                remote(
                    self.buf.at[0, n], self.buf.at[dst, n], self.ss.at[way, 0], self.rs.at[way, 0],
                    (self.up, self.down)[way],
                )

    def arrive(self, hop):
        z, length = self.z, self.length

        @pl.when(z >= hop)
        def _():
            self.copy(hop, True).wait_recv()

        @pl.when(z + hop < length)
        def _():
            self.copy(hop, False).wait_recv()

    def finish(self, first_hop=1, last_hop=None):
        for hop in range(first_hop, (last_hop or self.length - 1) + 1):
            self.sends(hop, lambda copy: copy.wait_send())


class LineScatter:
    def __init__(self, sources, length, total, up_mine, down_mine, up_got, down_got, loc, ss, rs):
        y, c, z, x = place()
        self.sources, self.length, self.total = sources, length, total
        self.mine, self.got = (up_mine, down_mine), (up_got, down_got)
        self.loc, self.ss, self.rs = loc, ss, rs
        self.to = (device(y, c, lax.rem(z + 1, length), x), device(y, c, lax.rem(z + length - 1, length), x))
        self.far = (z, length - 1 - z)
        self.next = 1

    def loads(self, way, hop):
        k = 0 if hop == 0 else self.length - hop if way == 0 else hop
        copies, at = [], 0
        for n, (ref, first, columns) in enumerate(self.sources):
            dst = self.term(way, hop) if hop else self.total
            copies.append(
                pltpu.make_async_copy(
                    ref.at[k, :, pl.ds(first, columns)], dst.at[:, pl.ds(at, columns)],
                    self.loc.at[way, hop, n],
                )
            )
            at += columns
        return copies

    def term(self, way, hop):
        return self.mine[way].at[hop - 1]

    def copy(self, way, hop):
        return pltpu.make_async_remote_copy(
            src_ref=self.term(way, hop), dst_ref=self.got[way].at[hop - 1],
            send_sem=self.ss.at[way, hop - 1], recv_sem=self.rs.at[way, hop - 1],
            device_id=self.to[way], device_id_type=MESH,
        )

    def load(self, hops):
        for hop in hops:
            for way in (0, 1) if hop else (0,):
                for copy in self.loads(way, hop):
                    copy.start()

    def start(self):
        hop = self.next
        if hop >= self.length:
            return
        self.next += 1
        for way in (0, 1):
            far = self.far[way]
            for copy in self.loads(way, hop):
                copy.wait()
            if hop > 1:

                @pl.when(jnp.logical_and(far >= 1, far <= hop - 1))
                def _():
                    self.copy(way, hop - 1).wait_recv()
                    dst, src = self.term(way, hop), self.got[way].at[hop - 2]

                    def add(at):
                        dst[at] = dst[at] + src[at]

                    rows_loop(dst.shape[0], add, unroll=4)

            @pl.when(far <= hop - 1)
            def _():
                self.copy(way, hop).start()

    def end(self, result, first_column, squares):
        last = self.length - 1
        for copy in self.loads(0, 0):
            copy.wait()
        columns = pl.ds(first_column, self.total.shape[1])

        def finish(ways):
            for way in ways:
                self.copy(way, last).wait_recv()

            def add(at):
                total = self.total[at].astype(F32)
                for way in ways:
                    total = total + self.got[way][last - 1, at].astype(F32)
                result[at, columns] = total.astype(result.dtype)
                squares[...] += tile_of_squares(total)

            rows_loop(result.shape[0], add)

        above, below = self.far[0] >= 1, self.far[1] >= 1
        pl.when(jnp.logical_and(above, below))(lambda: finish((0, 1)))
        pl.when(jnp.logical_not(above))(lambda: finish((1,)))
        pl.when(jnp.logical_not(below))(lambda: finish((0,)))
        for hop in range(1, self.length):
            for way in (0, 1):

                @pl.when(self.far[way] <= hop - 1)
                def _():
                    self.copy(way, hop).wait_send()


class HeldLine(LineScatter):
    def __init__(self, g, first_column, up_got, down_got, ss, rs):
        y, c, z, x = place()
        self.length = length = g.shape[0]
        self.columns = pl.ds(first_column, up_got.shape[2])
        self.sources, self.g, self.total = (), g, g.at[0, :, self.columns]
        self.got, self.ss, self.rs = (up_got, down_got), ss, rs
        self.to = line_neighbours(length)
        self.far = (z, length - 1 - z)
        self.next = 1

    def term(self, way, hop):
        return self.g.at[self.length - hop if way == 0 else hop, :, self.columns]


def chains_of(cuts):
    whole = sum(cut[2] for cut in cuts)
    left = -(-whole // 256) * 128
    lists = [], []
    for which, first_column, columns in cuts:
        taken = min(columns, left)
        if taken:
            lists[0].append((which, first_column, taken))
        if columns > taken:
            lists[1].append((which, first_column + taken, columns - taken))
        left -= taken
    return lists


class Lines:
    def __init__(self, terms, cuts, length, refs):
        self.chains, self.length = [], length
        for n, cut in enumerate(chains_of(cuts)):
            sources = [(terms[which], first_column, columns) for which, first_column, columns in cut]
            self.chains.append(
                LineScatter(sources, length, *refs[n * LINE_REFS : (n + 1) * LINE_REFS])
            )
        self.queue = [chain for _ in range(1, length) for chain in self.chains]

    def begin(self):
        for chain in self.chains:
            chain.load((1,))
        self.start()
        self.start()
        for chain in self.chains:
            chain.load((*range(2, self.length), 0))

    def start(self):
        if self.queue:
            self.queue.pop(0).start()

    def end(self, result, squares):
        while self.queue:
            self.start()
        squares[...] = jnp.zeros_like(squares)
        at = 0
        for chain in self.chains:
            chain.end(result, at, squares)
            at += chain.total.shape[1]


def lines_scratch(length, rows, cuts):
    return sum(
        (line_scratch(length, rows, sum(cut[2] for cut in chain), len(chain)) for chain in chains_of(cuts)), []
    )


def fold(v):
    return jnp.sum(v.reshape(v.shape[0] // 8, 8, v.shape[1]), axis=0)


def tile_of_squares(v):
    v = fold(v * v)
    part = v[:, :128]
    for n in range(1, v.shape[1] // 128):
        part = part + v[:, n * 128 : (n + 1) * 128]
    if v.shape[1] % 128:
        rest = v[:, v.shape[1] // 128 * 128 :]
        part = part + jnp.concatenate([rest, jnp.zeros((8, 128 - rest.shape[1]), F32)], axis=1)
    return part


def line_scratch(length, rows, columns, sources):
    slots = pltpu.VMEM((length - 1, rows, columns), BF16)
    return [pltpu.VMEM((rows, columns), BF16)] + [slots] * 4 + [
        DMA((2, length, sources)), DMA((2, length)), DMA((2, length))
    ]


def starts(copies):
    for copy in copies:
        copy.start()
    return copies


def waits(copies):
    for copy in copies:
        copy.wait()


def local_copies(pairs, sems):
    return [pltpu.make_async_copy(src, dst, sems.at[n]) for n, (src, dst) in enumerate(pairs)]


def held(*arrays):
    return [pltpu.VMEM(v.shape, v.dtype) for v in arrays]


LINE_REFS = 8
SCATTER_REFS = 7
TILE = jax.ShapeDtypeStruct((8, 128), F32)


def line_neighbours(length):
    y, c, z, x = place()
    return [device(y, c, lax.rem(z + 1, length), x), device(y, c, lax.rem(z + length - 1, length), x)]


def rows_loop(rows, body, start=0, unroll=2):
    @pl.loop(start // 16, (start + rows) // 16, unroll=unroll)
    def _(i):
        body(pl.ds(pl.multiple_of(i * 16, 16), 16))


def turned_tiles(length, pair):
    _, _, z, _ = place()
    for k in range(length):
        for b in range(4):
            yield k * 4 + b, pl.multiple_of((b * length + lax.rem(z + k, length)) * pair, pair)


def load_turned(ref, at, length, pair):
    if pair % 128:
        return ref[at]
    return jnp.concatenate([ref[at, pl.ds(src, pair)] for _, src in turned_tiles(length, pair)], axis=1)


def store_turned(ref, at, value, length, pair):
    if pair % 128:
        ref[at] = value
        return
    for n, dst in turned_tiles(length, pair):
        ref[at, pl.ds(dst, pair)] = value[:, n * pair : (n + 1) * pair]


def inverse_rms(v):
    return lax.rsqrt(jnp.sum(v * v, axis=-1, keepdims=True) * (1.0 / v.shape[-1]) + norm_eps)


def norm_rows_back(v, gain, grad):
    inverse = inverse_rms(v)
    scaled = v * inverse
    moved = grad * gain
    inner = jnp.sum(moved * scaled, axis=-1, keepdims=True) * (1.0 / v.shape[-1])
    return inverse * (moved - scaled * inner), fold(grad * scaled)


def middle_kernel(length, mixed_in, mixer_in, inputs_in, gains_in, w_in, late_in, residual_o, normed_o, w, late, *scratch):
    scatter_refs, (p, low, loc, gs, gr, hs, hr, late_s, late_r, *scratch) = scratch[:SCATTER_REFS], scratch[SCATTER_REFS:]
    mixed, mixer, inputs, gains, residual, load_s, keep_s = scratch
    loads = starts(
        local_copies(
            ((mixed_in, mixed), (mixer_in, mixer), (inputs_in, inputs), (gains_in, gains)), load_s
        )
    )
    greet(gather_peers() + line_neighbours(length))
    hops = LineGather(w, length, hs, hr)
    hops.start(1)
    late_hops = LineGather(late, length, late_s, late_r)
    late_hops.start(1)
    started = [1]
    part = mixed.shape[1]
    rows, width = low.shape

    waits(loads[:2])

    def prepare(i):
        mine = mixed[pl.ds(pl.multiple_of(i * rows, rows), rows)]
        p[i] = contract_last(mine, mixer[:, 2 * part :]).astype(BF16)

    def advance():
        if started[0] < length - 1:
            hops.arrive(started[0])
            started[0] += 1
            hops.start(started[0])

    def body(at):
        v = inputs[at].astype(F32) + residual[at]
        residual[at] = v
        low[at] = (v * inverse_rms(v) * gains[1:2]).astype(BF16)

    half = low.shape[0] // 2
    gather = Gather(low, normed_o, loc, gs, gr)
    for name in scatter_steps(p, residual, *scatter_refs, prepare=prepare):
        if name == "late":
            advance()
        if name == "low half":
            waits(loads[2:])
            rows_loop(half, body)
            gather.begin_half(0)
        if name == "high half":
            rows_loop(half, body, half)
            gather.begin_half(1)
    keeps = starts(local_copies(((residual, residual_o),), keep_s))
    gather.middle()
    advance()
    gather.end()
    waits(keeps)
    while started[0] < length - 1:
        advance()
    hops.arrive(length - 1)
    hops.finish()
    late_hops.arrive(1)
    late_hops.finish(1, 1)


def middle(mixed, mixer, inputs, gains, w, late, length, collective_id):
    rows, width = inputs.shape
    return pl.pallas_call(
        functools.partial(middle_kernel, length),
        out_shape=(
            jax.ShapeDtypeStruct((rows, width), F32),
            jax.ShapeDtypeStruct((8, rows, width), BF16),
            jax.ShapeDtypeStruct(w.shape, w.dtype),
            jax.ShapeDtypeStruct(late.shape, late.dtype),
        ),
        in_specs=[ANY] * 6,
        out_specs=(ANY,) * 4,
        scratch_shapes=scatter_scratch(rows // 2, width)
        + [pltpu.VMEM((8, rows, width), BF16), pltpu.VMEM((rows, width), BF16), DMA, DMA((14,)), DMA((14,))]
        + [DMA((2, length))] * 4
        + held(mixed, mixer, inputs, gains)
        + [pltpu.VMEM((rows, width), F32), DMA((4,)), DMA((1,))],
        input_output_aliases={4: 2, 5: 3},
        compiler_params=params(collective_id),
        cost_estimate=pl.CostEstimate(flops=0, bytes_accessed=300 * 2**20, transcendentals=0),
    )(mixed, mixer, inputs, gains, w, late)


def turn_kernel(length, cuts, p, residual_in, above_in, gains_in, mixer_in, *refs):
    parts = 1 + max(cut[0] for cut in cuts)
    terms, refs = refs[:parts], refs[parts:]
    back_o, gain, low_o, dmix_o, sums, squares, *scratch = refs
    scatter_refs, scratch = scratch[:SCATTER_REFS], scratch[SCATTER_REFS:]
    total, low, loc, gs, gr, parts_in, load_s, residual, above, gains, mixer, back, dmix, in_s, keep_s = scratch[:15]
    line_refs = scratch[15:]
    loads = local_copies(
        ((residual_in, residual), (above_in, above), (gains_in, gains), (mixer_in, mixer)), in_s
    )
    greet(gather_peers() + line_neighbours(length))
    line = Lines(terms, cuts, length, line_refs)
    line.begin()
    starts(loads)
    gain[...] = jnp.zeros_like(gain)

    def body(at):
        grad, gain_part = norm_rows_back(residual[at], gains[1:2], total[at])
        grad = above[at].astype(F32) + grad
        back[at] = grad
        low[at] = grad.astype(BF16)
        gain[...] += gain_part

    half = low.shape[0] // 2
    gather = Gather(low, low_o, loc, gs, gr)
    for name in scatter_steps(p, total, *scatter_refs):
        if name in ("early", "late"):
            line.start()
        if name == "low half":
            waits(loads)
            rows_loop(half, body)
            gather.begin_half(0)
        if name == "high half":
            rows_loop(half, body, half)
            gather.begin_half(1)
            line.start()
    keeps = starts(local_copies(((back, back_o),), keep_s))
    rows = low.shape[0]
    part = mixer.shape[1] // 3
    y, c, z, x = place()
    near = (gather.me, gather.bx), (gather.by, rank(y, 1 - c, x))
    rest = (gather.bd, rank(1 - y, 1 - c, x)), (rank(y, 1 - c, 1 - x), rank(1 - y, 1 - c, 1 - x))

    def fetch(blocks, slot):
        copies = []
        for n in (0, 1):
            copies.append(
                pltpu.make_async_copy(low_o.at[blocks[n]], parts_in.at[slot, n], load_s.at[slot, n])
            )
        return copies

    def mix(blocks, slot):
        waits(fetch(blocks, slot))
        lines = parts_in[slot].reshape(2 * rows, parts_in.shape[3])
        both = jnp.dot(lines, mixer[:, 2 * part :], preferred_element_type=F32)
        none = jnp.zeros((rows, dmix.shape[2] - part), F32)
        for n in (0, 1):
            dmix[blocks[n]] = jnp.concatenate([both[n * rows : (n + 1) * rows], none], axis=1)
            pltpu.make_async_copy(dmix.at[blocks[n]], dmix_o.at[blocks[n]], keep_s.at[1 + n + 2 * slot]).start()

    def mixed(blocks, slot):
        for n in (0, 1):
            pltpu.make_async_copy(dmix.at[blocks[n]], dmix_o.at[blocks[n]], keep_s.at[1 + n + 2 * slot]).wait()

    def near_blocks():
        gather.own.wait()
        for copy in gather.last[:2]:
            copy.wait_recv()
        starts(fetch(near[0], 0))
        starts(fetch(near[1], 1))
        mix(near[0], 0)
        mix(near[1], 1)

    gather.middle()
    line.start()
    gather.relays(near_blocks)
    gather.finish(2, own=False)
    for n in (0, 1):
        mixed(near[n], n)
        starts(fetch(rest[n], n))
    for n in (0, 1):
        mix(rest[n], n)
    waits(keeps)
    line.end(sums, squares)
    for n in (0, 1):
        mixed(rest[n], n)


def turn(p, residual, above, gains, mixer, rc, terms, cuts, length, collective_id):
    rows, width = residual.shape
    line_rows, columns = terms[0].shape[1], sum(cut[2] for cut in cuts)
    return pl.pallas_call(
        functools.partial(turn_kernel, length, cuts),
        out_shape=(
            jax.ShapeDtypeStruct((rows, width), F32),
            jax.ShapeDtypeStruct((8, width), F32),
            jax.ShapeDtypeStruct((8, rows, width), BF16),
            jax.ShapeDtypeStruct((8, rows, rc), F32),
            jax.ShapeDtypeStruct((line_rows, columns), BF16),
            TILE,
        ),
        in_specs=[ANY] * (5 + len(terms)),
        out_specs=(ANY, VM, ANY, ANY, VM, VM),
        scratch_shapes=scatter_scratch(rows // 2, width)
        + [pltpu.VMEM((rows, width), F32), pltpu.VMEM((rows, width), BF16), DMA, DMA((14,)), DMA((14,))]
        + [pltpu.VMEM((2, 2, rows, width), BF16), DMA((2, 2))]
        + held(residual, above, gains, mixer)
        + [pltpu.VMEM((rows, width), F32), pltpu.VMEM((8, rows, rc), F32), DMA((4,)), DMA((5,))]
        + lines_scratch(length, line_rows, cuts),
        compiler_params=params(collective_id),
        cost_estimate=pl.CostEstimate(flops=0, bytes_accessed=300 * 2**20, transcendentals=0),
    )(p.reshape(8, rows, width), residual, above, gains, mixer, *terms)


def closing_kernel(
    length, x_in, dmz_in, dproj_in, mixed_in, mixer_in, q, residual_in, block, inputs_in, above_in, gains_in, gp_in,
    grad_out, gain, gates_o, out_out, e_o, early_o, sums, squares,
    early_sums, early_l, early_s, early_r, x_part, dmz_part, g, back, total, o, up_a, down_a, up_b, down_b, gp_got, gp_sum,
    ls, lr, load_s, free, loc, es, er, gate_s, gate_r, move_s, move_r,
    dproj, mixed, mixer, residual, inputs, above, gains, gp, grad_o, out, in_s, keep_s, *scatter_refs,
):
    inflow = starts(
        local_copies(
            (
                (gp_in, gp), (dproj_in, dproj), (mixed_in, mixed), (mixer_in, mixer), (residual_in, residual),
                (inputs_in, inputs), (above_in, above), (gains_in, gains),
            ),
            in_s,
        )
    )
    y, c, z, x = place()
    others = line_peers(length)
    s = 2 * z + x
    owner = x * length + z
    to_z = owner // 2
    to_x = owner - 2 * to_z
    from_z, from_x = lax.rem(s, length), s // length
    moves = jnp.where(jnp.logical_and(to_z == z, to_x == x), 0, 1)
    barrier = pltpu.get_barrier_semaphore()
    for peer in others + plane_peers():
        pl.semaphore_signal(barrier, inc=1, device_id=peer, device_id_type=MESH)

    @pl.when(moves == 1)
    def _():
        pl.semaphore_signal(barrier, inc=1, device_id=device(y, c, to_z, to_x), device_id_type=MESH)
        pl.semaphore_signal(barrier, inc=1, device_id=device(y, c, from_z, from_x), device_id_type=MESH)

    pl.semaphore_wait(barrier, len(others) + 7 + 2 * moves)
    model = mixer.shape[0]
    tokens = dproj.shape[0]
    part = mixed.shape[1]
    columns = x_part.shape[2]
    steps = model // columns
    rows = tokens // steps
    line_rows = g.shape[1]

    def loads(i, slot):
        at = pl.ds(pl.multiple_of(i * columns, columns), columns)
        return (
            pltpu.make_async_copy(x_in.at[:, at], x_part.at[slot], load_s.at[0, slot]),
            pltpu.make_async_copy(dmz_in.at[:, at], dmz_part.at[slot], load_s.at[1, slot]),
        )

    group = steps // 4
    order = (3, 1, 2, 0)

    def fetch(i, slot):
        for copy in loads(i, slot):
            copy.start()

    fetch(order[0] * group, 0)
    inflow[0].wait()
    gate = [
        remote(gp.at[lax.rem(z + k + 1, length)], gp_got.at[k], gate_s.at[k], gate_r.at[k], others[k])
        for k in range(length - 1)
    ]
    split = up_a.shape[2]
    line_a = HeldLine(g, 0, up_a, down_a, ls.at[0], lr.at[0])
    line_b = HeldLine(g, split, up_b, down_b, ls.at[1], lr.at[1])
    queue = [chain for _ in range(1, length) for chain in (line_a, line_b)]

    def advance(times=1):
        for _ in range(times):
            if queue:
                queue.pop(0).start()

    output = scatter_steps(q, total, *scatter_refs)
    next(output)
    copies, own = exchange_steps(block, e_o, loc, es, er)

    def compute(n):
        @pl.loop(0, group)
        def _(j):
            count = n * group + j
            slot = count - count // 2 * 2
            i = order[n] * group + j

            @pl.when(j + 1 < group)
            def _():
                fetch(i + 1, 1 - slot)

            if n < 3:

                @pl.when(j + 1 == group)
                def _():
                    fetch(order[n + 1] * group, 1 - slot)

            for copy in loads(i, slot):
                copy.wait()
            front = contract_first(x_part[slot], dproj[...])
            tail = contract_first(dmz_part[slot], mixed[...])
            k = i * columns // line_rows
            at = pl.ds(pl.multiple_of(i * columns - k * line_rows, columns), columns)
            g[k, at] = jnp.concatenate([front, tail], axis=1).astype(BF16)
            block_of = i * rows // 256
            at = pl.ds(pl.multiple_of(i * rows - block_of * 256, rows), rows)
            mine = dproj[pl.ds(pl.multiple_of(i * rows, rows), rows)]
            back[block_of, at] = contract_last(mine, mixer[:, : 2 * part]).astype(BF16)

    waits(inflow[1:4])
    compute(0)
    next(output)
    compute(1)
    if length == 4:
        advance(2)
    next(output)
    compute(2)
    next(output)
    compute(3)
    if length != 4:
        advance(2)
    for _ in output:
        pass
    for peer in gather_peers():
        pl.semaphore_signal(free, inc=1, device_id=peer, device_id_type=MESH)
    advance()
    pl.semaphore_wait(free, 3)
    incoming = scatter_steps(back, o, *scatter_refs)
    next(incoming)
    pair = out.shape[1] // (4 * length)

    def finish_output(at):
        store_turned(out, at, (residual[at] + total[at]).astype(BF16), length, pair)

    waits(inflow[4:])
    rows_loop(out.shape[0], finish_output)
    keeps = local_copies(((out, out_out), (grad_o, grad_out)), keep_s)
    keeps[0].start()
    for copy in gate:
        copy.wait()
    rows_sum = gp[z]
    for k in range(length - 1):
        rows_sum = rows_sum + gp_got[k]
    gp_sum[...] = rows_sum
    move = pltpu.make_async_remote_copy(
        src_ref=gp_sum, dst_ref=gates_o, send_sem=move_s, recv_sem=move_r,
        device_id=device(y, c, to_z, to_x), device_id_type=MESH,
    )
    pl.when(moves == 1)(lambda: move.start())

    @pl.when(moves == 0)
    def _():
        gates_o[...] = rows_sum

    gain[...] = jnp.zeros_like(gain)

    def finish_grad(at):
        grad, gain_part = norm_rows_back(inputs[at].astype(F32), gains[0:1], o[at])
        store_turned(grad_o, at, above[at] + grad, length, pair)
        gain[...] += gain_part

    half = grad_o.shape[0] // 2
    for name in incoming:
        if name in ("sent", "early", "late"):
            advance()
        if name == "low half":
            rows_loop(half, finish_grad)
        if name == "high half":
            rows_loop(half, finish_grad, half)
            keeps[1].start()
    while queue:
        advance()
    squares[...] = jnp.zeros_like(squares)
    line_a.end(early_sums, 0, squares)
    early_copies, early_own = exchange_steps(early_sums, early_o, early_l, early_s, early_r)
    line_b.end(sums, 0, squares)
    pl.when(moves == 1)(lambda: move.wait())
    waits(keeps)
    for copy in copies + early_copies:
        copy.wait()
    own.wait()
    early_own.wait()


def closing(x, dmz, dproj, mixed, mixer, q, residual, block, inputs, above, gains, gp, length, collective_id):
    rows, width = residual.shape
    tokens, model = x.shape
    part = mixed.shape[1]
    share = block.shape[0] // 8
    block = block.reshape(8, share, block.shape[1])
    line_rows = model // length
    columns = min(256, line_rows)
    split = -(-3 * part // 256) * 128
    slots_a, slots_b = (pltpu.VMEM((length - 1, line_rows, n), BF16) for n in (split, 3 * part - split))
    pack = gp.shape[1:]
    return pl.pallas_call(
        functools.partial(closing_kernel, length),
        out_shape=(
            jax.ShapeDtypeStruct((rows, width), F32),
            jax.ShapeDtypeStruct((8, width), F32),
            jax.ShapeDtypeStruct(pack, F32),
            jax.ShapeDtypeStruct((rows, width), BF16),
            jax.ShapeDtypeStruct(block.shape, BF16),
            jax.ShapeDtypeStruct((8, share, split), BF16),
            jax.ShapeDtypeStruct((line_rows, 3 * part - split), BF16),
            TILE,
        ),
        in_specs=[ANY] * 12,
        out_specs=(ANY, VM, VM, ANY, ANY, ANY, VM, VM),
        scratch_shapes=[
            pltpu.VMEM((line_rows, split), BF16), DMA, DMA((7,)), DMA((7,)),
            pltpu.VMEM((2, tokens, columns), BF16),
            pltpu.VMEM((2, tokens, columns), BF16),
            pltpu.VMEM((length, line_rows, 3 * part), BF16),
            pltpu.VMEM((8, rows, width), BF16),
            pltpu.VMEM((rows, width), F32),
            pltpu.VMEM((rows, width), F32),
            slots_a, slots_a, slots_b, slots_b,
            pltpu.VMEM((length - 1,) + pack, F32),
            pltpu.VMEM(pack, F32),
            DMA((2, 2, length)), DMA((2, 2, length)), DMA((2, 2)), pltpu.SemaphoreType.REGULAR,
            DMA, DMA((7,)), DMA((7,)), DMA((length,)), DMA((length,)), DMA, DMA,
            *held(dproj, mixed, mixer, residual, inputs, above, gains, gp),
            pltpu.VMEM((rows, width), F32),
            pltpu.VMEM((rows, width), BF16),
            DMA((8,)), DMA((2,)),
        ]
        + scatter_scratch(rows // 2, width),
        compiler_params=params(collective_id),
        cost_estimate=pl.CostEstimate(
            flops=10 * tokens * model * dproj.shape[1] // 2, bytes_accessed=350 * 2**20, transcendentals=0
        ),
    )(x, dmz, dproj, mixed, mixer, q.reshape(8, rows, width), residual, block, inputs, above, gains, gp)


def first_kernel(
    length, inputs_in, above_in, mixer_in, mlp_in, gains_in, gate_in, chan_in,
    normed_o, wm_o, wf_o, wd_o, w2_o, gains_o, gate_o, chan_o, inputs_o, above_o,
    inputs, above, mixer_w, mlp_w, gains_w, gate_w, chan_w, load_s,
    inputs_k, above_k, w2, keep_s, gp_o, gn, gp, normed, gn_all, wm, wf, wd, loc, ms, mr, fs, fr, line_s, line_r, gain_s, gain_r, move_s, move_r,
    gather_s, gather_r, hop_s, hop_r,
):
    loads = [
        pltpu.make_async_copy(src, dst, load_s.at[n])
        for n, (src, dst) in enumerate(
            (
                (gains_in, gains_w), (gate_in, gate_w), (chan_in, chan_w), (mixer_in, mixer_w),
                (mlp_in, mlp_w), (inputs_in, inputs), (above_in, above),
            )
        )
    ]
    for copy in loads:
        copy.start()
    y, c, z, x = place()
    s = 2 * z + x
    me = rank(y, c, x)
    rows, width = inputs.shape
    pair = width // (4 * length)
    line = line_peers(length)
    plane = plane_peers()
    to_z, to_x = lax.rem(s, length), s // length
    moves = jnp.where(jnp.logical_and(to_z == z, to_x == x), 0, 1)
    src = x * length + z
    from_z = src // 2
    from_x = src - 2 * from_z
    barrier = pltpu.get_barrier_semaphore()
    for peer in line + plane:
        pl.semaphore_signal(barrier, inc=1, device_id=peer, device_id_type=MESH)

    @pl.when(moves == 1)
    def _():
        pl.semaphore_signal(barrier, inc=1, device_id=device(y, c, to_z, to_x), device_id_type=MESH)
        pl.semaphore_signal(barrier, inc=1, device_id=device(y, c, from_z, from_x), device_id_type=MESH)

    def fill(pack, source, js, offset=0):
        part = pack.shape[2] // len(js)
        whole = source.shape[1] // 24
        for t in range(8):
            for n, j in enumerate(js):
                start = (j * 8 + t) * whole + offset
                pack[t, :, n * part : (n + 1) * part] = source[:, start : start + part].astype(BF16)

    loads[3].wait()
    fill(wm, mixer_w, (0, 1, 2))
    for copy in loads[:3]:
        copy.wait()
    share = gains_w.shape[1]
    gn[...] = jnp.zeros_like(gn)
    for n in (0, 1):

        @pl.when(x == n)
        def _():
            gn[:2, n * share : (n + 1) * share] = gains_w[...]

    gp[...] = jnp.zeros_like(gp)
    channels = contract_first(chan_w[...].astype(BF16), unit(8))
    gp[: gate_w.shape[0]] = jnp.concatenate(
        [
            gate_w[...],
            channels,
            jnp.zeros((gate_w.shape[0], gp.shape[1] - gate_w.shape[1] - 8), F32),
        ],
        axis=1,
    ).astype(BF16)
    gn_all[me, z] = gn[...]
    pl.semaphore_wait(barrier, len(line) + len(plane) + 2 * moves)
    gains = [
        remote(gn, gn_all.at[me, z], line_s.at[0, k], line_r.at[0, k], line[k]) for k in range(length - 1)
    ]
    gate_move = pltpu.make_async_remote_copy(
        src_ref=gp, dst_ref=gp_o.at[to_z], send_sem=move_s, recv_sem=move_r,
        device_id=device(y, c, to_z, to_x), device_id_type=MESH,
    )
    gate_stay = pltpu.make_async_copy(gp, gp_o.at[z], loc.at[2])
    pl.when(moves == 1)(lambda: gate_move.start())
    pl.when(moves == 0)(lambda: gate_stay.start())

    mixer, mixer_own = exchange_steps(wm, wm_o.at[0], loc.at[0], ms, mr)
    hops = LineGather(wm_o, length, hop_s, hop_r)
    mixer_own.wait()
    hops.start_piece(me)

    def pass_piece(n):
        fy, fc, fx = FLIPS[n]
        mixer[n].wait_recv()
        hops.start_piece(rank(flip(y, fy), flip(c, fc), flip(x, fx)))

    pass_piece(1)
    for copy in gains:
        copy.wait()
    spread = [
        remote(gn_all.at[me], gn_all.at[me], gain_s.at[n], gain_r.at[n], plane[n]) for n in range(7)
    ]
    loads[4].wait()
    fill(wd, mlp_w, (2,))
    down, down_own = exchange_steps(wd, wd_o.at[0], loc.at[4], fs.at[1], fr.at[1])
    for n in (0, 2, 3, 5, 4, 6):
        pass_piece(n)
    fill(wf, mlp_w, (0, 1))
    feed, feed_own = exchange_steps(wf, wf_o.at[0], loc.at[3], fs.at[0], fr.at[0])
    pl.when(moves == 1)(lambda: gate_move.wait())
    pl.when(moves == 0)(lambda: gate_stay.wait())
    gates = [
        remote(gp_o.at[z], gp_o.at[z], line_s.at[1, k], line_r.at[1, k], line[k])
        for k in range(length - 1)
    ]
    fill(w2, mlp_w, (0, 1, 2), wd.shape[2])
    for copy in spread:
        copy.wait()
    for k in range(length):
        other = lax.rem(z + k, length)
        for b in range(4):
            at = slice((4 * k + b) * pair, (4 * k + b + 1) * pair)
            tile = (gn_all[2 * b, other] + gn_all[2 * b + 1, other])[:, :pair]
            gains_o[:, at] = tile.astype(BF16).astype(F32)
    for copy in mixer:
        copy.wait_send()

    def body(at):
        v = load_turned(inputs, at, length, pair)
        inputs_k[at] = v
        v = v.astype(F32)
        normed[at] = (v * inverse_rms(v) * gains_o[0:1]).astype(BF16)
        above_k[at] = load_turned(above, at, length, pair)

    for copy in loads[5:]:
        copy.wait()
    half = rows // 2
    gather = Gather(normed, normed_o, loc.at[1], gather_s, gather_r)
    rows_loop(half, body)
    gather.begin_half(0)
    hops.arrive(1)
    if length > 2:
        hops.start(2)
    rows_loop(half, body, half)
    gather.begin_half(1)
    keeps = starts(local_copies(((inputs_k, inputs_o), (above_k, above_o)), keep_s))
    for copy in gates:
        copy.wait()
    gate_rows, columns = gate_w.shape
    head = columns // 2
    own = jnp.concatenate([gp_o[n, :gate_rows].astype(F32) for n in range(length)]).astype(BF16)
    part, rc = own.shape[0], gate_o.shape[0]
    gate_o[...] = jnp.zeros_like(gate_o)
    for first_row in range(0, part, head):
        at = slice(first_row, first_row + head)
        wide = [jnp.zeros((head, first_row), F32)] if first_row else []
        for n in (0, 1):
            block = own[at, n * head : (n + 1) * head].astype(F32)
            rest = jnp.zeros((head, rc - first_row - head), F32)
            gate_o[at, n * rc : (n + 1) * rc] = jnp.concatenate([*wide, block, rest], axis=1).astype(BF16)
    rows_of = contract_last(unit(8), own[:, columns : columns + 8])
    lam = rows_of[7:8]
    u = jnp.exp(-jnp.abs(lam))
    t = u / (2.0 + u)
    series = jnp.full_like(t, 1.0 / 17.0)
    for n in range(15, 0, -2):
        series = series * t * t + 1.0 / n
    rate = 8.0 * (jnp.maximum(-lam, 0.0) + 2.0 * t * series)
    fill_rows = jnp.concatenate([jnp.zeros((7, rc - part), F32), jnp.ones((1, rc - part), F32)])
    chan_o[...] = jnp.concatenate([jnp.concatenate([rows_of[:7], rate]), fill_rows], axis=1)
    if length > 3:
        hops.arrive(2)
        hops.start(3)
    gather.middle()
    late, late_own = exchange_steps(w2, w2_o.at[0], loc.at[0], fs.at[2], fr.at[2])
    gather.relays()
    for hop in range(min(3, length - 1), length):
        hops.arrive(hop)
        if hop + 1 < length:
            hops.start(hop + 1)
    gather.finish()
    waits(keeps)
    for copy in down + feed + late:
        copy.wait()
    late_own.wait()
    down_own.wait()
    feed_own.wait()
    hops.finish()


def early(f8):
    return f8 // 384 * 256


def unit(n):
    return (
        lax.broadcasted_iota(jnp.int32, (n, n), 0) == lax.broadcasted_iota(jnp.int32, (n, n), 1)
    ).astype(BF16)


def first(inputs, above, mixer, mlp, gains, gate, chan, rc, length, collective_id):
    rows, width = inputs.shape
    pack = (-(-gate.shape[0] // 16) * 16, rc)
    share = mixer.shape[0]
    f8 = mlp.shape[1] // 24
    wm, wf, wd, w2 = (
        (8, share, n) for n in (mixer.shape[1] // 8, 2 * early(f8), early(f8), 3 * (f8 - early(f8)))
    )
    low = jax.ShapeDtypeStruct((rows, width), BF16)
    return pl.pallas_call(
        functools.partial(first_kernel, length),
        out_shape=(
            jax.ShapeDtypeStruct((8, rows, width), BF16),
            jax.ShapeDtypeStruct((length,) + wm, BF16),
            jax.ShapeDtypeStruct((length,) + wf, BF16),
            jax.ShapeDtypeStruct((length,) + wd, BF16),
            jax.ShapeDtypeStruct((length,) + w2, BF16),
            jax.ShapeDtypeStruct((8, width), F32),
            jax.ShapeDtypeStruct((rc, 2 * rc), BF16),
            jax.ShapeDtypeStruct((8, rc), F32),
            low,
            low,
        ),
        in_specs=[ANY] * 7,
        out_specs=(ANY, ANY, ANY, ANY, ANY, VM, VM, VM, ANY, ANY),
        scratch_shapes=[
            *[pltpu.VMEM(v.shape, v.dtype) for v in (inputs, above, mixer, mlp, gains, gate, chan)],
            DMA((7,)),
            pltpu.VMEM((rows, width), BF16),
            pltpu.VMEM((rows, width), BF16),
            pltpu.VMEM(w2, BF16),
            DMA((2,)),
            pltpu.VMEM((length,) + pack, BF16),
            pltpu.VMEM((8, 128), F32),
            pltpu.VMEM(pack, BF16),
            pltpu.VMEM((rows, width), BF16),
            pltpu.VMEM((8, length, 8, 128), F32),
            pltpu.VMEM(wm, BF16),
            pltpu.VMEM(wf, BF16),
            pltpu.VMEM(wd, BF16),
            DMA((5,)), DMA((7,)), DMA((7,)), DMA((3, 7)), DMA((3, 7)),
            DMA((2, length)), DMA((2, length)), DMA((7,)), DMA((7,)), DMA, DMA,
            DMA((14,)), DMA((14,)), DMA((2, length)), DMA((2, length)),
        ],
        compiler_params=params(collective_id),
        cost_estimate=pl.CostEstimate(flops=0, bytes_accessed=300 * 2**20, transcendentals=0),
    )(inputs, above, mixer, mlp, gains, gate, chan)


def last_kernel(
    length, share, wm, gain, gain_two, gates, sq_a, sq_b, sq_c, sq_d,
    wm_o, gains_o, norm_o, factor_o, by_plane, by_line, loc, ss, rs, gs, gr, ls, lr,
):
    y, c, z, x = place()
    me = rank(y, c, x)
    line = line_peers(length)
    plane = plane_peers()
    width = gain.shape[1]
    pair = width // (4 * length)
    squares = sq_a[...] + sq_b[...] + sq_c[...] + sq_d[...] + tile_of_squares(gates[...])
    squares = jnp.concatenate([squares, jnp.zeros((8, width - 128), F32)], axis=1)
    rows = [jnp.sum(v, axis=0, keepdims=True) for v in (gain[...], gain_two[...], squares)]
    by_plane[me] = jnp.concatenate(rows + [jnp.zeros((1, width), F32)])
    greet(line + plane)
    sends = [
        remote(by_plane.at[me], by_plane.at[me], gs.at[n], gr.at[n], plane[n]) for n in range(7)
    ]
    copies, own = exchange_steps(wm, wm_o, loc, ss, rs)
    for copy in sends:
        copy.wait()
    total = by_plane[0]
    for n in range(1, 8):
        total = total + by_plane[n]
    group = 4 * pair
    for k in range(length):
        at = pl.ds(pl.multiple_of(lax.rem(z + k, length) * group, group), group)
        by_line[z, :, at] = total[:, k * group : (k + 1) * group]
    sends = [
        remote(by_line.at[z], by_line.at[z], ls.at[k], lr.at[k], line[k]) for k in range(length - 1)
    ]
    for copy in sends:
        copy.wait()
    total = by_line[0]
    for n in range(1, length):
        total = total + by_line[n]
    squares = jnp.sum(total[:2] * total[:2], axis=0, keepdims=True) + total[2:3]
    norm = jnp.broadcast_to(jnp.sqrt(jnp.sum(squares, axis=1, keepdims=True)), (8, 128))
    norm_o[...] = norm
    factor_o[...] = clip_limit / jnp.maximum(norm, clip_limit)
    gains = jnp.zeros((2, pair), F32)
    for there in range(length):
        for b in range(4):
            first_lane = (there * 4 + b) * pair
            mine = jnp.logical_and(there == z, b == 2 * y + c)
            gains = jnp.where(mine, total[:2, first_lane : first_lane + pair], gains)
    gains_o[...] = jnp.where(x == 0, gains[:, :share], gains[:, share:])
    for copy in copies:
        copy.wait()
    own.wait()


def last(wm, gain, gain_two, gates, squares, length, collective_id):
    width = gain.shape[1]
    share = wm.shape[1]
    return pl.pallas_call(
        functools.partial(last_kernel, length, share),
        out_shape=(
            jax.ShapeDtypeStruct(wm.shape, wm.dtype),
            jax.ShapeDtypeStruct((2, share), F32),
            TILE, TILE,
        ),
        in_specs=[ANY] + [VM] * 7,
        out_specs=(ANY,) + (VM,) * 3,
        scratch_shapes=[
            pltpu.VMEM((8, 4, width), F32),
            pltpu.VMEM((length, 4, width), F32),
            DMA, DMA((7,)), DMA((7,)), DMA((7,)), DMA((7,)),
            DMA((length,)), DMA((length,)),
        ],
        compiler_params=params(collective_id),
    )(wm, gain, gain_two, gates, *squares)


def minus_expm1(v):
    series = 1.0 + v * (1.0 / 8.0)
    for n in (7.0, 6.0, 5.0, 4.0, 3.0, 2.0):
        series = 1.0 + series * v * (1.0 / n)
    return jnp.where(v > -0.5, -v * series, 1.0 - jnp.exp(v))


def gelu_parts(v):
    square = v * v
    h = 0.5 * jnp.tanh(v * (GELU_CUBE * square + GELU_SCALE)) + 0.5
    return v * h, h, square


def gelu_slope(gelu, h, square):
    return h + gelu * (1.0 - h) * (6.0 * GELU_CUBE * square + 2.0 * GELU_SCALE)


CHUNK = 128


def forward_kernel(
    length, x_in, mixer_in, gate, chan, above, w_in,
    mixed, branch_o, decay_o, width_o, recur_o, enter_o, conv_o, xe_o, se_o, ends_o, above_o, w,
    x_part, pre, loc_h, ends, carry, hs, hr, es, er, gather_l, gather_s, gather_r, hop_s, hop_r, load_s, keep_s, mixer,
    branch, decay_k, width_k, recur_k, enter_k, conv_k, xe, se,
):
    keeps = [
        pltpu.make_async_copy(src, dst, keep_s.at[n])
        for n, (src, dst) in enumerate(
            (
                (branch, branch_o), (decay_k, decay_o), (width_k, width_o), (recur_k, recur_o),
                (enter_k, enter_o), (conv_k, conv_o), (xe, xe_o), (se, se_o),
            )
        )
    ]
    y, c, z, x = place()
    line = line_peers(length)
    seqs, span, rc = branch.shape
    part = mixed.shape[2]
    chunks = span // CHUNK

    def load(b, slot):
        at = pl.ds(pl.multiple_of(b * span, span), span)
        return pltpu.make_async_copy(x_in.at[at], x_part.at[slot], load_s.at[slot])

    load(0, 0).start()
    mixer_load = pltpu.make_async_copy(mixer_in, mixer, load_s.at[2])
    mixer_load.start()
    greet(line + gather_peers())
    hops = LineGather(w, length, hop_s, hop_r)
    hops.start(1)
    gather = Gather(above, above_o, gather_l, gather_s, gather_r)
    gather.begin()

    mixer_load.wait()

    @pl.loop(0, seqs)
    def _(b):
        slot = b - b // 2 * 2

        @pl.when(b + 1 < seqs)
        def _():
            load(b + 1, 1 - slot).start()

        load(b, slot).wait()
        both = jnp.dot(x_part[slot], mixer[:, : 2 * part], preferred_element_type=F32)
        none = jnp.zeros((span, rc - part), F32)
        branch[b] = jnp.concatenate([both[:, :part], none], axis=1)
        low = both[:, part:].astype(BF16).astype(F32)
        xe[b, 8:] = jnp.concatenate([low, none], axis=1)

    ahead = device(y, c, lax.rem(z + 1, length), x)
    halo = remote(xe.at[:, pl.ds(span, 8)], xe.at[:, pl.ds(0, 8)], hs, hr, ahead)

    def coefficients(b, chunk):
        r = pl.multiple_of(chunk * CHUNK, CHUNK)
        at = pl.ds(r, CHUNK)
        window = xe[b, pl.ds(r, CHUNK + 8)]
        total = chan[4:5] + chan[0:1] * window[8:]
        for k in (1, 2, 3):
            total = total + chan[k : k + 1] * pltpu.roll(window, k, 0)[8:]
        low = total.astype(BF16)
        conv_k[b, at] = low
        value = low.astype(F32)
        gates = jnp.dot(low, gate[...], preferred_element_type=F32)
        recur = jax.nn.sigmoid(gates[:, :rc] + chan[5:6])
        enter = jax.nn.sigmoid(gates[:, rc:] + chan[6:7])
        log_decay = -chan[7:8] * recur
        decay = jnp.exp(log_decay)
        width = jnp.sqrt(minus_expm1(2.0 * log_decay))
        recur_k[b, at] = recur
        enter_k[b, at] = enter
        decay_k[b, at] = decay
        width_k[b, at] = width
        loc_h[b, at] = width * enter * value

    def later_chunks(i):
        b = i // (chunks - 1)
        coefficients(b, 1 + i - b * (chunks - 1))

    many = seqs * (chunks - 1)
    pl.loop(0, many // 2)(later_chunks)
    hops.arrive(1)
    if length > 2:
        hops.start(2)
    gather.middle()
    pl.loop(many // 2, many)(later_chunks)
    halo.wait()

    @pl.when(z == 0)
    def _():
        xe[:, 0:8] = jnp.zeros((seqs, 8, rc), F32)

    @pl.loop(0, seqs)
    def _(b):
        coefficients(b, 0)

    for copy in keeps[:-1]:
        copy.start()
    row = lax.broadcasted_iota(jnp.int32, (8, rc), 0)

    def tile(i, held):
        at = pl.ds(pl.multiple_of(i * 8, 8), 8)
        new = []
        for b in range(seqs):
            a, h = decay_k[b, at], loc_h[b, at]
            for n in (1, 2, 4):
                keep = row >= n
                h = h + jnp.where(keep, a * pltpu.roll(h, n, 0), 0.0)
                a = jnp.where(keep, a * pltpu.roll(a, n, 0), a)
            h = h + a * held[b][1]
            a = a * held[b][0]
            loc_h[b, at] = h
            pre[b, at] = a
            new.append((a[7:8], h[7:8]))
        return tuple(new)

    one, zero = jnp.ones((1, rc), F32), jnp.zeros((1, rc), F32)
    final = lax.fori_loop(0, span // 8, tile, ((one, zero),) * seqs)
    for b in range(seqs):
        ends[z, 0, b] = jnp.broadcast_to(final[b][0], (8, rc))
        ends[z, 1, b] = jnp.broadcast_to(final[b][1], (8, rc))
        ends_o[b] = jnp.broadcast_to(final[b][0], (8, rc))
    moves = [remote(ends.at[z], ends.at[z], es.at[k], er.at[k], line[k]) for k in range(length - 1)]
    if length > 3:
        hops.arrive(2)
        hops.start(3)
    for copy in moves:
        copy.wait()
    carry[...] = jnp.zeros_like(carry)
    for k in range(length):
        carry[...] = jnp.where(k < z, ends[k, 0] * carry[...] + ends[k, 1], carry[...])

    for b in range(seqs):
        se[b, 0:8] = carry[b]

    @pl.loop(0, seqs * chunks)
    def _(i):
        b = i // chunks
        r = pl.multiple_of((i - b * chunks) * CHUNK, CHUNK)
        at = pl.ds(r, CHUNK)
        state = loc_h[b, at] + pre[b, at] * carry[b, 0:1]
        se[b, pl.ds(r + 8, CHUNK)] = state
        gelu, _, _ = gelu_parts(branch[b, at])
        mixed[b, at] = (state * gelu)[:, :part].astype(BF16)

    keeps[-1].start()
    gather.end()
    for hop in range(min(3, length - 1), length):
        hops.arrive(hop)
        if hop + 1 < length:
            hops.start(hop + 1)
    hops.finish()
    waits(keeps)


def recur_forward(x, mixer, gate, chan, above, w, length, collective_id):
    rc = gate.shape[0]
    part = mixer.shape[1] // 3
    rows = x.shape[0] // 8
    seqs, span = 4, 2 * rows
    full = jax.ShapeDtypeStruct((seqs, span, rc), F32)
    longer = jax.ShapeDtypeStruct((seqs, span + 8, rc), F32)
    kept = (full, full, full, full, full, jax.ShapeDtypeStruct((seqs, span, rc), BF16), longer, longer)
    return pl.pallas_call(
        functools.partial(forward_kernel, length),
        out_shape=(
            jax.ShapeDtypeStruct((seqs, span, part), BF16),
            *kept,
            jax.ShapeDtypeStruct((seqs, 8, rc), F32),
            jax.ShapeDtypeStruct((8,) + above.shape, above.dtype),
            jax.ShapeDtypeStruct(w.shape, w.dtype),
        ),
        in_specs=[ANY, ANY, VM, VM, ANY, ANY],
        out_specs=(VM,) + (ANY,) * 8 + (VM, ANY, ANY),
        scratch_shapes=[
            pltpu.VMEM((2, span, x.shape[1]), BF16),
            pltpu.VMEM((seqs, span, rc), F32),
            pltpu.VMEM((seqs, span, rc), F32),
            pltpu.VMEM((length, 2, seqs, 8, rc), F32),
            pltpu.VMEM((seqs, 8, rc), F32),
            DMA, DMA, DMA((length,)), DMA((length,)),
            DMA, DMA((14,)), DMA((14,)), DMA((2, length)), DMA((2, length)),
            DMA((3,)), DMA((8,)),
            *held(mixer),
            *[pltpu.VMEM(v.shape, v.dtype) for v in kept],
        ],
        input_output_aliases={5: 11},
        compiler_params=params(collective_id),
        cost_estimate=pl.CostEstimate(
            flops=2 * seqs * span * rc * rc * 2, bytes_accessed=100 * 2**20, transcendentals=0
        ),
    )(x, mixer, gate, chan, above, w)


def backward_kernel(
    length, cuts, head, dmix, gate, chan, decay, width, recur, enter, conv, xe, se, ends_f, proj, block_a, block_b, *refs
):
    parts = 1 + max(cut[0] for cut in cuts)
    terms, refs = refs[:parts], refs[parts:]
    dproj, gates_o, sums, squares, block_ao, block_bo, *refs = refs
    dgate, gchan, *refs = refs
    suffix, grad, de, ends, carry, hs, hr, es, er, keep_s, move_l, move_s, move_r, *refs = refs
    kept, line_refs = refs[:8], refs[8:]
    loads = [
        pltpu.make_async_copy(src, dst, keep_s.at[n])
        for n, (src, dst) in enumerate(
            zip((dmix, proj, se, decay, width, recur, enter, conv, xe), (de.at[:, pl.ds(0, decay.shape[1])], *kept))
        )
    ]
    proj, se, decay, width, recur, enter, conv, xe = kept
    y, c, z, x = place()
    line = line_peers(length)
    greet(line + plane_peers())
    scatter = Lines(terms, cuts, length, line_refs)
    scatter.begin()
    for copy in loads:
        copy.start()
    moves = [
        exchange_steps(block_a, block_ao, move_l.at[0], move_s.at[0], move_r.at[0]),
        exchange_steps(block_b, block_bo, move_l.at[1], move_s.at[1], move_r.at[1]),
    ]
    seqs, span, rc = decay.shape
    part = dproj.shape[2] // 2
    chunks = span // CHUNK
    for copy in loads[:3]:
        copy.wait()

    @pl.loop(0, seqs * chunks)
    def _(i):
        b = i // chunks
        r = pl.multiple_of((i - b * chunks) * CHUNK, CHUNK)
        at = pl.ds(r, CHUNK)
        branch = proj[b, at]
        gelu, h, square = gelu_parts(branch)
        above = de[b, at]
        state = se[b, pl.ds(r + 8, CHUNK)]
        grad[b, at] = above * gelu
        proj[b, at] = above * state * gelu_slope(gelu, h, square)

    loads[3].wait()
    row = lax.broadcasted_iota(jnp.int32, (8, rc), 0)

    def tile(i, held):
        at = pl.ds(pl.multiple_of(span - 8 - i * 8, 8), 8)
        new = []
        for b in range(seqs):
            product, total, following = held[b]
            plain, h = decay[b, at], grad[b, at]
            a = jnp.where(row == 7, following, pltpu.roll(plain, 7, 0))
            for n in (1, 2, 4):
                keep = row < 8 - n
                h = h + jnp.where(keep, a * pltpu.roll(h, 8 - n, 0), 0.0)
                a = jnp.where(keep, a * pltpu.roll(a, 8 - n, 0), a)
            h = h + a * total
            a = a * product
            grad[b, at] = h
            suffix[b, at] = a
            new.append((a[0:1], h[0:1], plain[0:1]))
        return tuple(new)

    one, zero = jnp.ones((1, rc), F32), jnp.zeros((1, rc), F32)
    final = lax.fori_loop(0, span // 8, tile, ((one, zero, one),) * seqs)
    for b in range(seqs):
        ends[z, 0, b] = ends_f[b]
        ends[z, 1, b] = jnp.broadcast_to(final[b][1] * final[b][2], (8, rc))
    tails = [remote(ends.at[z], ends.at[z], es.at[k], er.at[k], line[k]) for k in range(length - 1)]
    for copy in tails:
        copy.wait()
    for copy in loads[4:]:
        copy.wait()
    carry[...] = jnp.zeros_like(carry)
    for k in reversed(range(length)):
        carry[...] = jnp.where(k > z, ends[k, 0] * carry[...] + ends[k, 1], carry[...])

    gchan[...] = jnp.zeros_like(gchan)

    def gradients(b, chunk):
        r = pl.multiple_of(chunk * CHUNK, CHUNK)
        at = pl.ds(r, CHUNK)
        g = grad[b, at] + suffix[b, at] * carry[b, 0:1]
        a, w, ra, ri = decay[b, at], width[b, at], recur[b, at], enter[b, at]
        value = conv[b, at].astype(F32)
        before = pltpu.roll(se[b, pl.ds(r, CHUNK + 8)], 1, 0)[8:]
        dla = g * before * a - g * ri * value * (a * a) / w
        slope = dla * ra * (1.0 - ra)
        dpa = (-chan[7:8] * slope).astype(BF16)
        dpi = (g * w * value * ri * (1.0 - ri)).astype(BF16)
        dgate[b, at, :rc] = dpa
        dgate[b, at, rc:] = dpi
        gchan[5] += fold(dpa.astype(F32))
        gchan[6] += fold(dpi.astype(F32))
        gchan[7] += fold(dla * ra)
        back = lax.dot_general(
            dgate[b, at], gate[...], (((1,), (1,)), ((), ())), preferred_element_type=F32
        )
        dcv = (g * w * ri + back).astype(BF16).astype(F32)
        de[b, at] = dcv
        gchan[4] += fold(dcv)

    pl.loop(0, seqs)(lambda b: gradients(b, 0))
    behind = device(y, c, lax.rem(z + length - 1, length), x)
    halo = remote(de.at[:, pl.ds(0, 8)], de.at[:, pl.ds(span, 8)], hs, hr, behind)
    scatter.start()
    scatter.start()

    @pl.loop(0, seqs * (chunks - 1))
    def _(i):
        b = i // (chunks - 1)
        gradients(b, 1 + i - b * (chunks - 1))

    scatter.start()
    scatter.start()
    halo.wait()
    low = conv[...].reshape(seqs * span, rc)
    recur_grad, enter_grad = (
        contract_first(low, dgate[:, :, at].reshape(seqs * span, rc)) for at in (slice(0, rc), slice(rc, 2 * rc))
    )

    @pl.when(z == length - 1)
    def _():
        de[:, span:] = jnp.zeros((seqs, 8, rc), F32)

    @pl.loop(0, seqs * chunks)
    def _(i):
        b = i // chunks
        r = pl.multiple_of((i - b * chunks) * CHUNK, CHUNK)
        at = pl.ds(r, CHUNK)
        window = de[b, pl.ds(r, CHUNK + 8)]
        inputs = xe[b, pl.ds(r, CHUNK + 8)]
        dcv = window[:CHUNK]
        total = chan[0:1] * dcv
        gchan[0] += fold(dcv * inputs[8:])
        for k in (1, 2, 3):
            total = total + chan[k : k + 1] * pltpu.roll(window, CHUNK + 8 - k, 0)[:CHUNK]
            gchan[k] += fold(dcv * pltpu.roll(inputs, k, 0)[8:])
        dproj[b, at] = jnp.concatenate([proj[b, at, :part], total[:, :part]], axis=1).astype(BF16)

    rates = 8.0 * minus_expm1(chan[7:8] * (-1.0 / 8.0))
    channels = [jnp.sum(gchan[n], axis=0, keepdims=True) for n in range(8)]
    channels[7] = channels[7] * rates
    channels = lax.dot_general(
        jnp.concatenate(channels), unit(8).astype(F32), (((0,), (0,)), ((), ())),
        precision=lax.Precision.HIGHEST, preferred_element_type=F32,
    )
    blocks = []
    for first_row in range(0, part, head):
        at = slice(first_row, first_row + head)
        blocks.append(jnp.concatenate([recur_grad[at, at], enter_grad[at, at]], axis=1))
    pack = jnp.concatenate(
        [jnp.concatenate(blocks), channels[:part], jnp.zeros((part, rc - 2 * head - 8), F32)], axis=1
    )
    rows = part // length
    if rows < gates_o.shape[1]:
        gates_o[...] = jnp.zeros_like(gates_o)
    for n in range(length):
        gates_o[n, :rows] = pack[n * rows : (n + 1) * rows]
    scatter.end(sums, squares)
    for copies, own in moves:
        for copy in copies:
            copy.wait()
        own.wait()


def recur_backward(dmix, gate, chan, kept, part, head, blocks, terms, cuts, length, collective_id):
    proj, decay, width, recur, enter, conv, xe, se, ends = kept
    seqs, span, rc = decay.shape
    gate_pad = -(-(part // length) // 16) * 16
    line_rows, columns = terms[0].shape[1], sum(cut[2] for cut in cuts)
    return pl.pallas_call(
        functools.partial(backward_kernel, length, cuts, head),
        out_shape=(
            jax.ShapeDtypeStruct((seqs, span, 2 * part), BF16),
            jax.ShapeDtypeStruct((length, gate_pad, rc), F32),
            jax.ShapeDtypeStruct((line_rows, columns), BF16), TILE,
            *[jax.ShapeDtypeStruct(block.shape, BF16) for block in blocks],
        ),
        in_specs=[ANY, VM, VM] + [ANY] * 7 + [VM] + [ANY] * (3 + len(terms)),
        out_specs=(VM,) * 4 + (ANY, ANY),
        scratch_shapes=[
            pltpu.VMEM((seqs, span, 2 * rc), BF16),
            pltpu.VMEM((8, 8, rc), F32),
            pltpu.VMEM((seqs, span, rc), F32),
            pltpu.VMEM((seqs, span, rc), F32),
            pltpu.VMEM((seqs, span + 8, rc), F32),
            pltpu.VMEM((length, 2, seqs, 8, rc), F32),
            pltpu.VMEM((seqs, 8, rc), F32),
            DMA, DMA, DMA((length,)), DMA((length,)),
            DMA((9,)), DMA((2,)), DMA((2, 7)), DMA((2, 7)),
            *[
                pltpu.VMEM(shape, dtype)
                for shape, dtype in (
                    (decay.shape, F32), (se.shape, F32), (decay.shape, F32), (decay.shape, F32),
                    (decay.shape, F32), (decay.shape, F32), (decay.shape, BF16), (xe.shape, F32),
                )
            ],
        ]
        + lines_scratch(length, line_rows, cuts),
        compiler_params=params(collective_id),
        cost_estimate=pl.CostEstimate(
            flops=2 * seqs * span * rc * rc * 2, bytes_accessed=120 * 2**20, transcendentals=0
        ),
    )(dmix, gate, chan, decay, width, recur, enter, conv, xe, se, ends, proj, *blocks, *terms)


def contract_last(left, right):
    return lax.dot_general(
        left, right, (((1,), (1,)), ((), ())), preferred_element_type=F32
    )


def contract_first(left, right):
    return lax.dot_general(
        left, right, (((0,), (0,)), ((), ())), preferred_element_type=F32
    )


def resident(shape):
    return pl.BlockSpec(shape, lambda i: (0, 0), pipeline_mode=pl.Buffered(1))


STEPS = 4


def feed_forward(x, above, gate_up, down, hid, dboth):
    f = hid.shape[1]
    both = jnp.dot(x[...], gate_up, preferred_element_type=F32)
    gg, uu = both[:, :f], both[:, f:]
    dhid = jnp.dot(above[...], down, preferred_element_type=F32)
    gelu, h, square = gelu_parts(gg)
    hid[...] = (gelu * uu).astype(BF16)
    dboth[:, :f] = (dhid * uu * gelu_slope(gelu, h, square)).astype(BF16)
    dboth[:, f:] = (dhid * gelu).astype(BF16)


def grads_compute(x, above, hid, dboth, gate_o, up_o, down_o):
    f = hid.shape[1]
    both = contract_first(x[...], dboth[...]).astype(BF16)
    gate_o[...] = both[:, :f]
    up_o[...] = both[:, f:]
    down_o[...] = contract_first(above[...], hid[...]).astype(BF16)


def mlp_specs(tokens, model, f):
    def rows(width):
        return pl.BlockSpec((tokens // STEPS, width), lambda i: (jnp.minimum(i, STEPS - 1), 0))

    columns = pl.BlockSpec((tokens, model // STEPS), lambda i: (0, jnp.maximum(i - STEPS, 0)))
    grads = pl.BlockSpec((model // STEPS, f), lambda i: (jnp.maximum(i - STEPS, 0), 0))
    return rows, columns, grads


def keep_units(step, hid_all, dboth_all, hid, dboth):
    rows = hid.shape[0]
    at = pl.ds(pl.multiple_of(step * rows, rows), rows)
    hid_all[at] = hid[...]
    dboth_all[at] = dboth[...]


def early_mlp_kernel(
    length, x, above, x_columns, above_columns, gate_up, down, w_in,
    hid, dboth, gate_o, up_o, down_o, w, hid_all, dboth_all, ss, rs
):
    step = pl.program_id(0)
    hops = LineGather(w, length, ss, rs)

    @pl.when(step == 0)
    def _():
        greet(line_neighbours(length))
        if length > 2:
            hops.start(2)

    @pl.when(step == STEPS)
    def _():
        for hop in range(2, length - 1):
            hops.arrive(hop)
            hops.start(hop + 1)

    @pl.when(step < STEPS)
    def _():
        feed_forward(x, above, gate_up[...], down[...], hid, dboth)
        keep_units(step, hid_all, dboth_all, hid, dboth)

    @pl.when(step >= STEPS)
    def _():
        grads_compute(x_columns, above_columns, hid_all, dboth_all, gate_o, up_o, down_o)

    @pl.when(step == 2 * STEPS - 1)
    def _():
        hops.arrive(length - 1)
        hops.finish(2, length - 1)


def early_mlp(x, above, gate_up, down, w, length, collective_id):
    tokens, model = x.shape
    f = down.shape[1]
    rows, columns, grads = mlp_specs(tokens, model, f)
    grad_shape = jax.ShapeDtypeStruct((model, f), BF16)
    return pl.pallas_call(
        functools.partial(early_mlp_kernel, length),
        grid=(2 * STEPS,),
        out_shape=(
            jax.ShapeDtypeStruct((tokens, f), BF16),
            jax.ShapeDtypeStruct((tokens, 2 * f), BF16),
            grad_shape, grad_shape, grad_shape,
            jax.ShapeDtypeStruct(w.shape, w.dtype),
        ),
        in_specs=[rows(model), rows(model), columns, columns, resident(gate_up.shape), resident(down.shape), ANY],
        out_specs=(rows(f), rows(2 * f)) + (grads,) * 3 + (ANY,),
        scratch_shapes=[pltpu.VMEM((tokens, f), BF16), pltpu.VMEM((tokens, 2 * f), BF16)]
        + [DMA((2, length)), DMA((2, length))],
        input_output_aliases={6: 5},
        compiler_params=params(collective_id),
        cost_estimate=pl.CostEstimate(flops=12 * tokens * model * f, bytes_accessed=50 * 2**20, transcendentals=0),
    )(x, above, x, above, gate_up, down, w)


def late_mlp_kernel(
    length, cuts, x, above, x_columns, above_columns, hid_one, dboth_one, gate_up_in, down_in, late_in, *refs
):
    terms, refs = refs[: len(cuts)], refs[len(cuts) :]
    out, back, gate_o, up_o, down_o, sums, squares, *refs = refs
    gate_up, down, hid, dboth, hid_all, dboth_all, load_s, *line_refs = refs
    step = pl.program_id(0)
    line = LineScatter([(ref, *cut) for ref, cut in zip(terms, cuts)], length, *line_refs)
    f, g = hid_one.shape[1], hid.shape[1]
    loads = local_copies(
        (
            (late_in.at[:, pl.ds(0, 2 * g)], gate_up.at[:, pl.ds(2 * f, 2 * g)]),
            (late_in.at[:, pl.ds(2 * g, g)], down.at[:, pl.ds(f, g)]),
            (down_in, down.at[:, pl.ds(0, f)]),
            (gate_up_in, gate_up.at[:, pl.ds(0, 2 * f)]),
        ),
        load_s,
    )

    @pl.when(step == 0)
    def _():
        starts(loads)
        greet(line_neighbours(length))
        line.load((1,))
        line.start()
        line.load((*range(2, length), 0))
        waits(loads)

    for hop in range(2, length):

        @pl.when(step == min(2 * STEPS - 2, 2 * (hop - 1)))
        def _():
            line.next = hop
            line.start()

    @pl.when(step < STEPS)
    def _():
        feed_forward(x, above, gate_up[:, 2 * f :], down[:, f:], hid, dboth)
        keep_units(step, hid_all, dboth_all, hid, dboth)
        units = jnp.concatenate([hid_one[...], hid[...]], axis=1)
        out[...] = contract_last(units, down[...]).astype(BF16)
        units = jnp.concatenate([dboth_one[...], dboth[...]], axis=1)
        back[...] = contract_last(units, gate_up[...]).astype(BF16)

    @pl.when(step >= STEPS)
    def _():
        grads_compute(x_columns, above_columns, hid_all, dboth_all, gate_o, up_o, down_o)

    @pl.when(step == 2 * STEPS - 1)
    def _():
        squares[...] = jnp.zeros_like(squares)
        line.end(sums, 0, squares)


def late_mlp(x, above, early_units, gate_up, down, late, terms, cuts, length, collective_id):
    tokens, model = x.shape
    f, g = down.shape[1], late.shape[1] // 3
    line_rows = terms[0].shape[1]
    cut = sum(columns for _, columns in cuts)
    rows, columns, grads = mlp_specs(tokens, model, g)

    def whole(shape):
        return pl.BlockSpec(shape, lambda i: (0, 0))

    return pl.pallas_call(
        functools.partial(late_mlp_kernel, length, cuts),
        grid=(2 * STEPS,),
        out_shape=(jax.ShapeDtypeStruct((tokens, model), BF16),) * 2
        + (jax.ShapeDtypeStruct((model, g), BF16),) * 3
        + (jax.ShapeDtypeStruct((line_rows, cut), BF16), TILE),
        in_specs=[rows(model), rows(model), columns, columns, rows(f), rows(2 * f)]
        + [ANY] * (3 + len(terms)),
        out_specs=(rows(model),) * 2 + (grads,) * 3 + (whole((line_rows, cut)), whole((8, 128))),
        scratch_shapes=[
            pltpu.VMEM((model, 2 * f + 2 * g), BF16),
            pltpu.VMEM((model, f + g), BF16),
            pltpu.VMEM((tokens // STEPS, g), BF16),
            pltpu.VMEM((tokens // STEPS, 2 * g), BF16),
            pltpu.VMEM((tokens, g), BF16),
            pltpu.VMEM((tokens, 2 * g), BF16),
            DMA((4,)),
        ]
        + line_scratch(length, line_rows, cut, len(cuts)),
        compiler_params=params(collective_id),
        cost_estimate=pl.CostEstimate(
            flops=6 * tokens * model * (f + 3 * g), bytes_accessed=70 * 2**20, transcendentals=0
        ),
    )(x, above, x, above, *early_units, gate_up, down, late, *terms)


def adam_step(weight, grad, first, second, factor, rate, decay_rate):
    clipped = grad * factor
    first_new = beta_first * first + (1.0 - beta_first) * clipped
    second_new = beta_second * second + (1.0 - beta_second) * clipped * clipped
    first_hat = first_new / (1.0 - beta_first**STEP)
    second_hat = second_new / (1.0 - beta_second**STEP)
    weight_new = weight - rate * (
        first_hat / (jnp.sqrt(second_hat) + adam_eps) + decay_rate * weight
    )
    return (first_new, second_new, weight_new)


def small_steps(factor, refs, outs):
    gains_sum, gates_sum, *states = refs
    rows, columns = states[3].shape
    channels = lax.dot_general(
        unit(8).astype(F32), gates_sum[:rows, columns : columns + 8], (((1,), (1,)), ((), ())),
        precision=lax.Precision.HIGHEST, preferred_element_type=F32,
    )
    grads = gains_sum[...], gates_sum[:rows, :columns], channels
    rates = (rate_gains, 0.0), (rate_matrix, decay_matrix), (rate_channel, 0.0)
    for n in range(3):
        w, m, v = states[3 * n : 3 * n + 3]
        results = adam_step(w[...], grads[n], m[...], v[...], factor, *rates[n])
        for out, result in zip(outs[3 * n : 3 * n + 3], results):
            out[...] = result


def adam_kernel(sources, factor, *refs):
    states, refs = refs[: 3 * len(sources)], refs[3 * len(sources) :]
    count = sum(len(source) for source in sources)
    grads, small, refs = refs[:count], refs[count : count + 11], refs[count + 11 :]
    results, norm, outs = refs[:2], refs[2], refs[3:]
    for result, out in zip(results, outs[-3:]):
        out[...] = result[...]
    outs[-1][...] = norm[0:1, 0:1]
    one = factor[0:1, 0:1]
    pl.when(pl.program_id(0) == 0)(lambda: small_steps(one, small, outs[3 * len(sources) : -3]))
    for n, source in enumerate(sources):
        parts = []
        for pieces in source:
            ref, *grads = grads
            for first, columns, at, stride in pieces:
                for t in range(8):
                    parts.append((at + t * stride, columns, ref, t, first))
        parts.sort(key=lambda part: part[0])
        w, m, v = states[3 * n : 3 * n + 3]
        m_o, v_o, w_o = outs[3 * n : 3 * n + 3]
        run = []
        for at, columns, ref, t, first in parts:
            run.append((at, columns, ref[t, :, first : first + columns].astype(F32)))
            end = at + columns
            if end % 128:
                continue
            grad = jnp.concatenate([piece for _, _, piece in run], axis=1) if len(run) > 1 else run[0][2]
            cols = slice(run[0][0], end)
            run = []
            first_new, second_new, weight_new = adam_step(
                w[:, cols], grad, m[:, cols], v[:, cols], one, rate_matrix, decay_matrix
            )
            m_o[:, cols] = first_new
            v_o[:, cols] = second_new
            w_o[:, cols] = weight_new


def adam(matrices, small, factor, norm, passed):
    rows = matrices[0][0].shape[0]
    step = min(rows, 16)

    def block(v):
        return pl.BlockSpec((step, v.shape[1]), lambda i: (i, 0))

    def whole(v):
        return pl.BlockSpec(v.shape, lambda i: (0, 0))

    states = [v for matrix in matrices for v in matrix[:3]]
    grads = [g for matrix in matrices for g in matrix[3]]
    results = [*states, *small[2:], *passed]
    steps = rows // step

    def slab(v):
        return pl.BlockSpec((v.shape[0] // steps, v.shape[1]), lambda i: (i, 0))

    return pl.pallas_call(
        functools.partial(adam_kernel, [matrix[4] for matrix in matrices]),
        grid=(steps,),
        out_shape=tuple(jax.ShapeDtypeStruct(v.shape, v.dtype) for v in results)
        + (jax.ShapeDtypeStruct((1, 1), F32),),
        in_specs=[pl.BlockSpec((8, 128), lambda i: (0, 0))]
        + [block(v) for v in states]
        + [pl.BlockSpec((8, step, g.shape[2]), lambda i: (0, i, 0)) for g in grads]
        + [whole(v) for v in small]
        + [slab(v) for v in passed]
        + [whole(norm)],
        out_specs=tuple(block(v) for v in states)
        + tuple(whole(v) for v in small[2:])
        + tuple(slab(v) for v in passed)
        + (pl.BlockSpec((1, 1), lambda i: (0, 0)),),
        compiler_params=pltpu.CompilerParams(vmem_limit_bytes=VMEM_BYTES),
        cost_estimate=pl.CostEstimate(
            flops=0, bytes_accessed=sum(8 * v.size for v in states), transcendentals=0
        ),
    )(factor, *states, *grads, *small, *passed, norm)


def on_device(
    block_input,
    out_grad,
    norm_gains,
    mixer_weight,
    gate_weight,
    chan_params,
    mlp_weight,
    first_gains,
    first_mixer,
    first_gate,
    first_chan,
    first_mlp,
    second_gains,
    second_mixer,
    second_gate,
    second_chan,
    second_mlp,
):
    length = lax.axis_size("seq") // 2
    z = lax.axis_index("seq") // 2
    tokens, model = block_input.shape[1:]
    share = mixer_weight.shape[0]
    pair = 2 * share
    lru = mixer_weight.shape[1] // 3
    hidden = mlp_weight.shape[1] // 3
    r8, f8 = lru // 8, hidden // 8
    rc = -(-r8 // 128) * 128
    head = gate_weight.shape[1] // 2
    heads = r8 // head
    gate_rows = gate_weight.shape[0]
    gate_pad = -(-gate_rows // 16) * 16

    x = lax.axis_index("seq") - 2 * z
    batch = lax.axis_index("batch")
    plain = pair % 128 == 0

    def turned(v):
        if plain:
            return v
        v = v.reshape(v.shape[0], 4, length, pair).swapaxes(1, 2)
        return jnp.roll(v, -z, axis=1).reshape(v.shape[0], model)

    def turned_back(v):
        if plain:
            return v
        v = jnp.roll(v.reshape(v.shape[0], length, 4, pair), z, axis=1)
        return v.swapaxes(1, 2).reshape(v.shape[0], model)

    normed_one, mixer_full, mlp_gu, mlp_down, late, gains, gate, chan, inputs, above = first(
        turned(block_input[0]),
        turned(out_grad[0]),
        mixer_weight,
        mlp_weight,
        norm_gains,
        gate_weight,
        chan_params,
        rc,
        length,
        1,
    )
    normed_one = normed_one.reshape(8 * tokens, model)
    mixer_full = mixer_full.reshape(model, 3 * r8)
    mixed, *kept, grad_out, mlp_down = recur_forward(
        normed_one, mixer_full, gate, chan, above, mlp_down, length, 2
    )
    grad_out = grad_out.reshape(8 * tokens, model)
    mixed = mixed.reshape(8 * tokens, r8)
    residual, normed_two, mlp_gu, late = middle(mixed, mixer_full, inputs, gains, mlp_gu, late, length, 3)
    normed_two = normed_two.reshape(8 * tokens, model)
    h1 = early(f8)
    h2 = f8 - h1
    mlp_gu = mlp_gu.reshape(model, 2 * h1)
    mlp_down = mlp_down.reshape(model, h1)
    hid, dboth, *early_terms, late = early_mlp(normed_two, grad_out, mlp_gu, mlp_down, late, length, 9)
    gate_one, up_one, down_one = (v.reshape(length, 8 * share, h1) for v in early_terms)
    cut = h1 // 4
    mlp_part, dnormed_two, *late_terms, sums_zero, squares_zero = late_mlp(
        normed_two, grad_out, (hid, dboth), mlp_gu, mlp_down, late.reshape(model, 3 * h2),
        (gate_one, up_one), ((0, h1), (0, cut)), length, 11,
    )
    gate_two, up_two, down_two = (v.reshape(length, 8 * share, h2) for v in late_terms)

    grad_residual, gain_two, dmz, dmix, sums_one, squares_one = turn(
        dnormed_two, residual, above, gains, mixer_full, rc,
        (up_one, down_one, gate_two), ((0, cut, h1 - cut), (1, 0, h1), (2, 0, h2)),
        length, 4,
    )
    dmz = dmz.reshape(8 * tokens, model)
    span = 2 * tokens
    dmix = dmix.reshape(4, span, rc)
    sums_zero, sums_one = (v.reshape(8, share, v.shape[1]) for v in (sums_zero, sums_one))
    dproj, gate_back, sums_two, squares_two, back_zero, back_one = recur_backward(
        dmix, gate, chan, kept, r8, head, (sums_zero, sums_one),
        (up_two, down_two), ((0, 0, h2), (1, 0, h2)), length, 6,
    )
    dproj = dproj.reshape(4 * span, 2 * r8)
    input_grad, gain_one, gates_sum, block_output, back_two, mixer_early, mixer_sums, squares_three = closing(
        normed_one, dmz, dproj, mixed, mixer_full, mlp_part, residual, sums_two,
        inputs, grad_residual, gains, gate_back, length, 7,
    )
    mixer_back, gains_sum, norm, factor = last(
        mixer_sums.reshape(8, share, mixer_sums.shape[1]), gain_one, gain_two, gates_sum,
        (squares_zero, squares_one, squares_two, squares_three), length, 8,
    )
    split = mixer_early.shape[2]
    mlp_sources = (
        [(0, h1, 0, f8), (h1, cut, hidden, f8)],
        [
            (0, h1 - cut, hidden + cut, f8),
            (h1 - cut, h1, 2 * hidden, f8),
            (2 * h1 - cut, h2, h1, f8),
        ],
        [(0, h2, hidden + h1, f8), (h2, h2, 2 * hidden + h1, f8)],
    )
    states = adam(
        (
            (
                mixer_weight, first_mixer, second_mixer, (mixer_early, mixer_back),
                (
                    [(0, r8, 0, r8), (r8, split - r8, lru, r8)],
                    [(0, 2 * r8 - split, lru + split - r8, r8), (2 * r8 - split, r8, 2 * lru, r8)],
                ),
            ),
            (mlp_weight, first_mlp, second_mlp, (back_zero, back_one, back_two), mlp_sources),
        ),
        (
            gains_sum, gates_sum, norm_gains, first_gains, second_gains, gate_weight, first_gate, second_gate,
            chan_params, first_chan, second_chan,
        ),
        factor,
        norm,
        (block_output, input_grad),
    )
    *states, block_output, input_grad, norm = states
    mixer_up, mlp_up, gains_up, gate_up, chan_up = (states[3 * n : 3 * n + 3] for n in range(5))
    return (
        turned_back(block_output)[None],
        turned_back(input_grad)[None],
        norm.reshape(()),
        *gains_up,
        *mixer_up,
        *gate_up,
        *chan_up,
        *mlp_up,
    )


def solution(mesh):
    rows = P(("batch", "seq"), None)
    columns = P(None, ("batch", "seq"))
    data = P("batch", "seq", None)
    weights = (columns, rows, rows, columns, rows)
    in_specs = (data, data) + weights * 3
    triples = tuple(spec for spec in weights for _ in range(3))
    return jax.shard_map(
        on_device,
        mesh=mesh,
        in_specs=in_specs,
        out_specs=(data, data, P()) + triples,
        check_vma=False,
    )
```

```python
import functools
import math

import jax
import jax.numpy as jnp
from jax import lax
from jax.experimental import pallas as pl
from jax.experimental.pallas import tpu as pltpu
from jax.sharding import PartitionSpec as P

STEP = 10
norm_eps = 1e-06
clip_limit = 1.0
beta_first = 0.9
beta_second = 0.999
adam_eps = 1e-08
rate_matrix = 0.05
rate_gains = 0.8
rate_channel = 2.0
decay_matrix = 0.1

MESH = pl.DeviceIdType.MESH
F32 = jnp.float32
BF16 = jnp.bfloat16
ANY = pl.BlockSpec(memory_space=pl.ANY)
VM = pl.BlockSpec(memory_space=pltpu.VMEM)
FLIPS = [(fy, fc, fx) for fy in (0, 1) for fc in (0, 1) for fx in (0, 1) if fy + fc + fx]
GELU_SCALE = math.sqrt(2.0 / math.pi)
GELU_CUBE = 0.044715 * GELU_SCALE


def place():
    b = lax.axis_index("batch")
    s = lax.axis_index("seq")
    y, z = b // 2, s // 2
    return y, b - 2 * y, z, s - 2 * z


def device(y, c, z, x):
    return (y * 2 + c, z * 2 + x)


def rank(y, c, x):
    return (y * 2 + c) * 2 + x


def flip(v, f):
    return 1 - v if f else v


def greet(peers):
    barrier = pltpu.get_barrier_semaphore()
    for peer in peers:
        pl.semaphore_signal(barrier, inc=1, device_id=peer, device_id_type=MESH)
    pl.semaphore_wait(barrier, len(peers))


def remote(src, dst, send, recv, to):
    copy = pltpu.make_async_remote_copy(
        src_ref=src, dst_ref=dst, send_sem=send, recv_sem=recv, device_id=to, device_id_type=MESH
    )
    copy.start()
    return copy


VMEM_BYTES = 63 * 2**20


def params(collective_id):
    return pltpu.CompilerParams(
        collective_id=collective_id, has_side_effects=True, vmem_limit_bytes=VMEM_BYTES
    )


DMA = pltpu.SemaphoreType.DMA


def gather_peers():
    y, c, z, x = place()
    return [device(y, c, z, 1 - x), device(1 - y, c, z, x), device(y, 1 - c, z, x)]


class Gather:
    def __init__(self, a, o, loc, ss, rs):
        y, c, z, x = place()
        self.to_x, self.to_y, self.to_c = gather_peers()
        self.me, self.bx = rank(y, c, x), rank(y, c, 1 - x)
        self.by, self.bd = rank(1 - y, c, x), rank(1 - y, c, 1 - x)
        half = a.shape[0] // 2
        self.lo, self.hi = pl.ds(0, half), pl.ds(half, half)
        self.a, self.o, self.loc, self.ss, self.rs = a, o, loc, ss, rs
        self.done, self.last = [], []

    def send(self, src, dst, k, to):
        copy = remote(src, dst, self.ss.at[k], self.rs.at[k], to)
        self.done.append(copy)
        return copy

    def relay(self, block, part, k, to):
        return self.send(self.o.at[block, part], self.o.at[block, part], k, to)

    def begin_half(self, half):
        a, o, me = self.a, self.o, self.me
        part = (self.lo, self.hi)[half]
        if half == 0:
            self.s0 = self.send(a.at[part], o.at[me, part], 0, self.to_x)
            self.s3 = self.send(a.at[part], o.at[me, part], 3, self.to_y)
        else:
            self.s1 = self.send(a.at[part], o.at[me, part], 1, self.to_y)
            self.s2 = self.send(a.at[part], o.at[me, part], 2, self.to_x)
        self.last.append(self.send(a.at[part], o.at[me, part], (4, 13)[half], self.to_c))
        if half == 1:
            self.own = pltpu.make_async_copy(a, o.at[me], self.loc)
            self.own.start()

    def begin(self):
        a, o, me, lo, hi = self.a, self.o, self.me, self.lo, self.hi
        self.s0 = self.send(a.at[lo], o.at[me, lo], 0, self.to_x)
        self.s1 = self.send(a.at[hi], o.at[me, hi], 1, self.to_y)
        self.s2 = self.send(a.at[hi], o.at[me, hi], 2, self.to_x)
        self.s3 = self.send(a.at[lo], o.at[me, lo], 3, self.to_y)
        self.last += [self.send(a.at[part], o.at[me, part], k, self.to_c) for part, k in ((lo, 4), (hi, 13))]
        self.own = pltpu.make_async_copy(a, o.at[me], self.loc)
        self.own.start()

    def middle(self):
        self.s0.wait_recv()
        self.s5 = self.relay(self.bx, self.lo, 5, self.to_y)
        self.last.append(self.relay(self.bx, self.lo, 7, self.to_c))
        self.s1.wait_recv()
        self.s6 = self.relay(self.by, self.hi, 6, self.to_x)
        self.last.append(self.relay(self.by, self.hi, 8, self.to_c))

    def relays(self, mark=lambda: None):
        self.s2.wait_recv()
        self.last.append(self.relay(self.bx, self.hi, 9, self.to_c))
        self.s3.wait_recv()
        self.last.append(self.relay(self.by, self.lo, 10, self.to_c))
        mark()
        self.s5.wait_recv()
        self.last.append(self.relay(self.bd, self.lo, 11, self.to_c))
        self.s6.wait_recv()
        self.last.append(self.relay(self.bd, self.hi, 12, self.to_c))

    def finish(self, skip=0, own=True):
        for copy in self.last[skip:]:
            copy.wait_recv()
        for copy in self.done:
            copy.wait_send()
        if own:
            self.own.wait()

    def end(self, mark=lambda: None):
        self.relays(mark)
        self.finish()


def scatter_steps(p, o, mine, sib, part, got, loc, ss, rs, prepare=None):
    y, c, z, x = place()
    to_x, to_y, to_c = gather_peers()
    half = o.shape[0] // 2
    step = 16
    cut = (pl.ds(0, half), pl.ds(half, half))
    where = ((1 - y, 1 - x), (1 - y, x), (y, 1 - x), (y, x))
    order = [(0, 0), (0, 1), (1, 0), (2, 1), (2, 0), (1, 1), (3, 0), (3, 1)]
    from_c, own, sends = {}, {}, []
    for n, (t, h) in enumerate(order):
        ty, tx = where[t]
        if mine is not None and prepare and all(key[0] != t for key in own):
            prepare(rank(ty, c, tx))
            prepare(rank(ty, 1 - c, tx))
        if mine is None:
            own[t, h] = None
        else:
            own[t, h] = pltpu.make_async_copy(
                p.at[rank(ty, c, tx), cut[h]], mine.at[t, h], loc.at[n]
            )
            own[t, h].start()
        from_c[t, h] = remote(
            p.at[rank(ty, 1 - c, tx), cut[h]], sib.at[t, h], ss.at[n], rs.at[n], to_c
        )
        sends.append(from_c[t, h])
    yield "begun"

    def own_ref(t, h):
        return p.at[rank(where[t][0], c, where[t][1]), cut[h]] if mine is None else mine.at[t, h]

    pieces = ((0, 0), (0, 1), (1, 0), (2, 1), (2, 0), (1, 1))

    def part_ref(k):
        return own_ref(*pieces[k]) if part is None else part.at[k]

    def add(dst, t, h, extra):
        if own[t, h] is not None:
            own[t, h].wait()
        term = own_ref(t, h)
        from_c[t, h].wait_recv()

        @pl.loop(0, half // step)
        def _(i):
            at = pl.ds(pl.multiple_of(i * step, step), step)
            total = term[at].astype(F32) + sib[t, h, at].astype(F32)
            for ref in extra:
                total = total + ref[at].astype(F32)
            dst[at] = total.astype(dst.dtype)

    def send(k, slot, to):
        copy = remote(part_ref(k), got.at[slot], ss.at[8 + k], rs.at[8 + slot], to)
        sends.append(copy)
        return copy

    def arrival(slot):
        return pltpu.make_async_remote_copy(
            src_ref=got.at[slot], dst_ref=got.at[slot], send_sem=ss.at[8], recv_sem=rs.at[8 + slot],
            device_id=to_x, device_id_type=MESH,
        )

    add(part_ref(0), 0, 0, ())
    send(0, 1, to_y)
    add(part_ref(1), 0, 1, ())
    send(1, 3, to_x)
    add(part_ref(2), 1, 0, ())
    send(2, 0, to_y)
    add(part_ref(3), 2, 1, ())
    send(3, 2, to_x)
    yield "sent"
    arrival(1).wait_recv()
    add(part_ref(4), 2, 0, (got.at[1],))
    send(4, 4, to_x)
    yield "early"
    arrival(3).wait_recv()
    add(part_ref(5), 1, 1, (got.at[3],))
    send(5, 5, to_y)
    yield "late"
    arrival(0).wait_recv()
    arrival(4).wait_recv()
    add(o.at[cut[0]], 3, 0, (got.at[0], got.at[4]))
    yield "low half"
    arrival(2).wait_recv()
    arrival(5).wait_recv()
    add(o.at[cut[1]], 3, 1, (got.at[2], got.at[5]))
    yield "high half"
    for copy in sends:
        copy.wait_send()


def scatter_scratch(half, width):
    return [
        pltpu.VMEM((4, 2, half, width), BF16),
        pltpu.VMEM((4, 2, half, width), BF16),
        pltpu.VMEM((6, half, width), BF16),
        pltpu.VMEM((6, half, width), BF16),
        DMA((8,)),
        DMA((14,)),
        DMA((14,)),
    ]


def exchange_steps(a, o, loc, ss, rs):
    y, c, z, x = place()
    me = rank(y, c, x)
    dst = o.at[me]
    rows = o.shape[1]

    def block(t):
        if len(a.shape) == 3:
            return a.at[t]
        return a.at[pl.ds(pl.multiple_of(t * rows, rows), rows)]

    copies = []
    for n, (fy, fc, fx) in enumerate(FLIPS):
        ty, tc, tx = flip(y, fy), flip(c, fc), flip(x, fx)
        copies.append(remote(block(rank(ty, tc, tx)), dst, ss.at[n], rs.at[n], device(ty, tc, z, tx)))
    own = pltpu.make_async_copy(block(me), dst, loc)
    own.start()
    return copies, own


def plane_peers():
    y, c, z, x = place()
    return [device(flip(y, fy), flip(c, fc), z, flip(x, fx)) for fy, fc, fx in FLIPS]


def line_peers(length):
    y, c, z, x = place()
    return [device(y, c, lax.rem(z + k, length), x) for k in range(1, length)]


class LineGather:
    def __init__(self, buf, length, ss, rs):
        y, c, z, x = place()
        self.z, self.length, self.buf, self.ss, self.rs = z, length, buf, ss, rs
        self.up = device(y, c, lax.rem(z + 1, length), x)
        self.down = device(y, c, lax.rem(z + length - 1, length), x)

    def copy(self, hop, upward):
        length, buf = self.length, self.buf
        src, dst = ((length - hop + 1) % length, length - hop) if upward else (hop - 1, hop)
        way = 0 if upward else 1
        return pltpu.make_async_remote_copy(
            src_ref=buf.at[src], dst_ref=buf.at[dst], send_sem=self.ss.at[way, hop - 1],
            recv_sem=self.rs.at[way, hop - 1], device_id=self.up if upward else self.down,
            device_id_type=MESH,
        )

    def sends(self, hop, act):
        z, length = self.z, self.length

        @pl.when(jnp.logical_and(z + 1 < length, z >= hop - 1))
        def _():
            act(self.copy(hop, True))

        @pl.when(jnp.logical_and(z >= 1, z + hop - 1 < length))
        def _():
            act(self.copy(hop, False))

    def start(self, hop):
        self.sends(hop, lambda copy: copy.start())

    def start_piece(self, n):
        for way, last, dst in ((0, self.z + 1 < self.length, self.length - 1), (1, self.z >= 1, 1)):

            @pl.when(last)
            def _():
                remote(
                    self.buf.at[0, n], self.buf.at[dst, n], self.ss.at[way, 0], self.rs.at[way, 0],
                    (self.up, self.down)[way],
                )

    def arrive(self, hop):
        z, length = self.z, self.length

        @pl.when(z >= hop)
        def _():
            self.copy(hop, True).wait_recv()

        @pl.when(z + hop < length)
        def _():
            self.copy(hop, False).wait_recv()

    def finish(self, first_hop=1, last_hop=None):
        for hop in range(first_hop, (last_hop or self.length - 1) + 1):
            self.sends(hop, lambda copy: copy.wait_send())


class LineScatter:
    def __init__(self, sources, length, total, up_mine, down_mine, up_got, down_got, loc, ss, rs):
        y, c, z, x = place()
        self.sources, self.length, self.total = sources, length, total
        self.mine, self.got = (up_mine, down_mine), (up_got, down_got)
        self.loc, self.ss, self.rs = loc, ss, rs
        self.to = (device(y, c, lax.rem(z + 1, length), x), device(y, c, lax.rem(z + length - 1, length), x))
        self.far = (z, length - 1 - z)
        self.next = 1

    def loads(self, way, hop):
        k = 0 if hop == 0 else self.length - hop if way == 0 else hop
        copies, at = [], 0
        for n, (ref, first, columns) in enumerate(self.sources):
            dst = self.term(way, hop) if hop else self.total
            copies.append(
                pltpu.make_async_copy(
                    ref.at[k, :, pl.ds(first, columns)], dst.at[:, pl.ds(at, columns)],
                    self.loc.at[way, hop, n],
                )
            )
            at += columns
        return copies

    def term(self, way, hop):
        return self.mine[way].at[hop - 1]

    def copy(self, way, hop):
        return pltpu.make_async_remote_copy(
            src_ref=self.term(way, hop), dst_ref=self.got[way].at[hop - 1],
            send_sem=self.ss.at[way, hop - 1], recv_sem=self.rs.at[way, hop - 1],
            device_id=self.to[way], device_id_type=MESH,
        )

    def load(self, hops):
        for hop in hops:
            for way in (0, 1) if hop else (0,):
                for copy in self.loads(way, hop):
                    copy.start()

    def start(self):
        hop = self.next
        if hop >= self.length:
            return
        self.next += 1
        for way in (0, 1):
            far = self.far[way]
            for copy in self.loads(way, hop):
                copy.wait()
            if hop > 1:

                @pl.when(jnp.logical_and(far >= 1, far <= hop - 1))
                def _():
                    self.copy(way, hop - 1).wait_recv()
                    dst, src = self.term(way, hop), self.got[way].at[hop - 2]

                    def add(at):
                        dst[at] = dst[at] + src[at]

                    rows_loop(dst.shape[0], add, unroll=4)

            @pl.when(far <= hop - 1)
            def _():
                self.copy(way, hop).start()

    def end(self, result, first_column, squares):
        last = self.length - 1
        for copy in self.loads(0, 0):
            copy.wait()
        columns = pl.ds(first_column, self.total.shape[1])

        def finish(ways):
            for way in ways:
                self.copy(way, last).wait_recv()

            def add(at):
                total = self.total[at].astype(F32)
                for way in ways:
                    total = total + self.got[way][last - 1, at].astype(F32)
                result[at, columns] = total.astype(result.dtype)
                squares[...] += tile_of_squares(total)

            rows_loop(result.shape[0], add)

        above, below = self.far[0] >= 1, self.far[1] >= 1
        pl.when(jnp.logical_and(above, below))(lambda: finish((0, 1)))
        pl.when(jnp.logical_not(above))(lambda: finish((1,)))
        pl.when(jnp.logical_not(below))(lambda: finish((0,)))
        for hop in range(1, self.length):
            for way in (0, 1):

                @pl.when(self.far[way] <= hop - 1)
                def _():
                    self.copy(way, hop).wait_send()


class HeldLine(LineScatter):
    def __init__(self, g, first_column, up_got, down_got, ss, rs):
        y, c, z, x = place()
        self.length = length = g.shape[0]
        self.columns = pl.ds(first_column, up_got.shape[2])
        self.sources, self.g, self.total = (), g, g.at[0, :, self.columns]
        self.got, self.ss, self.rs = (up_got, down_got), ss, rs
        self.to = line_neighbours(length)
        self.far = (z, length - 1 - z)
        self.next = 1

    def term(self, way, hop):
        return self.g.at[self.length - hop if way == 0 else hop, :, self.columns]


def chains_of(cuts):
    whole = sum(cut[2] for cut in cuts)
    left = -(-whole // 256) * 128
    lists = [], []
    for which, first_column, columns in cuts:
        taken = min(columns, left)
        if taken:
            lists[0].append((which, first_column, taken))
        if columns > taken:
            lists[1].append((which, first_column + taken, columns - taken))
        left -= taken
    return lists


class Lines:
    def __init__(self, terms, cuts, length, refs):
        self.chains, self.length = [], length
        for n, cut in enumerate(chains_of(cuts)):
            sources = [(terms[which], first_column, columns) for which, first_column, columns in cut]
            self.chains.append(
                LineScatter(sources, length, *refs[n * LINE_REFS : (n + 1) * LINE_REFS])
            )
        self.queue = [chain for _ in range(1, length) for chain in self.chains]

    def begin(self):
        for chain in self.chains:
            chain.load((1,))
        self.start()
        self.start()
        for chain in self.chains:
            chain.load((*range(2, self.length), 0))

    def start(self):
        if self.queue:
            self.queue.pop(0).start()

    def end(self, result, squares):
        while self.queue:
            self.start()
        squares[...] = jnp.zeros_like(squares)
        at = 0
        for chain in self.chains:
            chain.end(result, at, squares)
            at += chain.total.shape[1]


def lines_scratch(length, rows, cuts):
    return sum(
        (line_scratch(length, rows, sum(cut[2] for cut in chain), len(chain)) for chain in chains_of(cuts)), []
    )


def fold(v):
    return jnp.sum(v.reshape(v.shape[0] // 8, 8, v.shape[1]), axis=0)


def tile_of_squares(v):
    v = fold(v * v)
    part = v[:, :128]
    for n in range(1, v.shape[1] // 128):
        part = part + v[:, n * 128 : (n + 1) * 128]
    if v.shape[1] % 128:
        rest = v[:, v.shape[1] // 128 * 128 :]
        part = part + jnp.concatenate([rest, jnp.zeros((8, 128 - rest.shape[1]), F32)], axis=1)
    return part


def line_scratch(length, rows, columns, sources):
    slots = pltpu.VMEM((length - 1, rows, columns), BF16)
    return [pltpu.VMEM((rows, columns), BF16)] + [slots] * 4 + [
        DMA((2, length, sources)), DMA((2, length)), DMA((2, length))
    ]


def starts(copies):
    for copy in copies:
        copy.start()
    return copies


def waits(copies):
    for copy in copies:
        copy.wait()


def local_copies(pairs, sems):
    return [pltpu.make_async_copy(src, dst, sems.at[n]) for n, (src, dst) in enumerate(pairs)]


def held(*arrays):
    return [pltpu.VMEM(v.shape, v.dtype) for v in arrays]


LINE_REFS = 8
SCATTER_REFS = 7
TILE = jax.ShapeDtypeStruct((8, 128), F32)


def line_neighbours(length):
    y, c, z, x = place()
    return [device(y, c, lax.rem(z + 1, length), x), device(y, c, lax.rem(z + length - 1, length), x)]


def rows_loop(rows, body, start=0, unroll=2):
    @pl.loop(start // 16, (start + rows) // 16, unroll=unroll)
    def _(i):
        body(pl.ds(pl.multiple_of(i * 16, 16), 16))


def turned_tiles(length, pair):
    _, _, z, _ = place()
    for k in range(length):
        for b in range(4):
            yield k * 4 + b, pl.multiple_of((b * length + lax.rem(z + k, length)) * pair, pair)


def load_turned(ref, at, length, pair):
    if pair % 128:
        return ref[at]
    return jnp.concatenate([ref[at, pl.ds(src, pair)] for _, src in turned_tiles(length, pair)], axis=1)


def store_turned(ref, at, value, length, pair):
    if pair % 128:
        ref[at] = value
        return
    for n, dst in turned_tiles(length, pair):
        ref[at, pl.ds(dst, pair)] = value[:, n * pair : (n + 1) * pair]


def inverse_rms(v):
    return lax.rsqrt(jnp.sum(v * v, axis=-1, keepdims=True) * (1.0 / v.shape[-1]) + norm_eps)


def norm_rows_back(v, gain, grad):
    inverse = inverse_rms(v)
    scaled = v * inverse
    moved = grad * gain
    inner = jnp.sum(moved * scaled, axis=-1, keepdims=True) * (1.0 / v.shape[-1])
    return inverse * (moved - scaled * inner), fold(grad * scaled)


def middle_kernel(length, mixed_in, mixer_in, inputs_in, gains_in, w_in, late_in, residual_o, normed_o, w, late, *scratch):
    scatter_refs, (p, low, loc, gs, gr, hs, hr, late_s, late_r, *scratch) = scratch[:SCATTER_REFS], scratch[SCATTER_REFS:]
    mixed, mixer, inputs, gains, residual, load_s, keep_s = scratch
    loads = starts(
        local_copies(
            ((mixed_in, mixed), (mixer_in, mixer), (inputs_in, inputs), (gains_in, gains)), load_s
        )
    )
    greet(gather_peers() + line_neighbours(length))
    hops = LineGather(w, length, hs, hr)
    hops.start(1)
    late_hops = LineGather(late, length, late_s, late_r)
    late_hops.start(1)
    started = [1]
    part = mixed.shape[1]
    rows, width = low.shape

    waits(loads[:2])

    def prepare(i):
        mine = mixed[pl.ds(pl.multiple_of(i * rows, rows), rows)]
        p[i] = contract_last(mine, mixer[:, 2 * part :]).astype(BF16)

    def advance():
        if started[0] < length - 1:
            hops.arrive(started[0])
            started[0] += 1
            hops.start(started[0])

    def body(at):
        v = inputs[at].astype(F32) + residual[at]
        residual[at] = v
        low[at] = (v * inverse_rms(v) * gains[1:2]).astype(BF16)

    half = low.shape[0] // 2
    gather = Gather(low, normed_o, loc, gs, gr)
    for name in scatter_steps(p, residual, *scatter_refs, prepare=prepare):
        if name == "late":
            advance()
        if name == "low half":
            waits(loads[2:])
            rows_loop(half, body)
            gather.begin_half(0)
        if name == "high half":
            rows_loop(half, body, half)
            gather.begin_half(1)
    keeps = starts(local_copies(((residual, residual_o),), keep_s))
    gather.middle()
    advance()
    gather.end()
    waits(keeps)
    while started[0] < length - 1:
        advance()
    hops.arrive(length - 1)
    hops.finish()
    late_hops.arrive(1)
    late_hops.finish(1, 1)


def middle(mixed, mixer, inputs, gains, w, late, length, collective_id):
    rows, width = inputs.shape
    return pl.pallas_call(
        functools.partial(middle_kernel, length),
        out_shape=(
            jax.ShapeDtypeStruct((rows, width), F32),
            jax.ShapeDtypeStruct((8, rows, width), BF16),
            jax.ShapeDtypeStruct(w.shape, w.dtype),
            jax.ShapeDtypeStruct(late.shape, late.dtype),
        ),
        in_specs=[ANY] * 6,
        out_specs=(ANY,) * 4,
        scratch_shapes=scatter_scratch(rows // 2, width)
        + [pltpu.VMEM((8, rows, width), BF16), pltpu.VMEM((rows, width), BF16), DMA, DMA((14,)), DMA((14,))]
        + [DMA((2, length))] * 4
        + held(mixed, mixer, inputs, gains)
        + [pltpu.VMEM((rows, width), F32), DMA((4,)), DMA((1,))],
        input_output_aliases={4: 2, 5: 3},
        compiler_params=params(collective_id),
        cost_estimate=pl.CostEstimate(flops=0, bytes_accessed=300 * 2**20, transcendentals=0),
    )(mixed, mixer, inputs, gains, w, late)


def turn_kernel(length, cuts, p, residual_in, above_in, gains_in, mixer_in, *refs):
    parts = 1 + max(cut[0] for cut in cuts)
    terms, refs = refs[:parts], refs[parts:]
    back_o, gain, low_o, dmix_o, sums, squares, *scratch = refs
    scatter_refs, scratch = scratch[:SCATTER_REFS], scratch[SCATTER_REFS:]
    total, low, loc, gs, gr, parts_in, load_s, residual, above, gains, mixer, back, dmix, in_s, keep_s = scratch[:15]
    line_refs = scratch[15:]
    loads = local_copies(
        ((residual_in, residual), (above_in, above), (gains_in, gains), (mixer_in, mixer)), in_s
    )
    greet(gather_peers() + line_neighbours(length))
    line = Lines(terms, cuts, length, line_refs)
    line.begin()
    starts(loads)
    gain[...] = jnp.zeros_like(gain)

    def body(at):
        grad, gain_part = norm_rows_back(residual[at], gains[1:2], total[at])
        grad = above[at].astype(F32) + grad
        back[at] = grad
        low[at] = grad.astype(BF16)
        gain[...] += gain_part

    half = low.shape[0] // 2
    gather = Gather(low, low_o, loc, gs, gr)
    for name in scatter_steps(p, total, *scatter_refs):
        if name in ("early", "late"):
            line.start()
        if name == "low half":
            waits(loads)
            rows_loop(half, body)
            gather.begin_half(0)
        if name == "high half":
            rows_loop(half, body, half)
            gather.begin_half(1)
            line.start()
    keeps = starts(local_copies(((back, back_o),), keep_s))
    rows = low.shape[0]
    part = mixer.shape[1] // 3
    y, c, z, x = place()
    near = (gather.me, gather.bx), (gather.by, rank(y, 1 - c, x))
    rest = (gather.bd, rank(1 - y, 1 - c, x)), (rank(y, 1 - c, 1 - x), rank(1 - y, 1 - c, 1 - x))

    def fetch(blocks, slot):
        copies = []
        for n in (0, 1):
            copies.append(
                pltpu.make_async_copy(low_o.at[blocks[n]], parts_in.at[slot, n], load_s.at[slot, n])
            )
        return copies

    def mix(blocks, slot):
        waits(fetch(blocks, slot))
        lines = parts_in[slot].reshape(2 * rows, parts_in.shape[3])
        both = jnp.dot(lines, mixer[:, 2 * part :], preferred_element_type=F32)
        none = jnp.zeros((rows, dmix.shape[2] - part), F32)
        for n in (0, 1):
            dmix[blocks[n]] = jnp.concatenate([both[n * rows : (n + 1) * rows], none], axis=1)
            pltpu.make_async_copy(dmix.at[blocks[n]], dmix_o.at[blocks[n]], keep_s.at[1 + n + 2 * slot]).start()

    def mixed(blocks, slot):
        for n in (0, 1):
            pltpu.make_async_copy(dmix.at[blocks[n]], dmix_o.at[blocks[n]], keep_s.at[1 + n + 2 * slot]).wait()

    def near_blocks():
        gather.own.wait()
        for copy in gather.last[:2]:
            copy.wait_recv()
        starts(fetch(near[0], 0))
        starts(fetch(near[1], 1))
        mix(near[0], 0)
        mix(near[1], 1)

    gather.middle()
    line.start()
    gather.relays(near_blocks)
    gather.finish(2, own=False)
    for n in (0, 1):
        mixed(near[n], n)
        starts(fetch(rest[n], n))
    for n in (0, 1):
        mix(rest[n], n)
    waits(keeps)
    line.end(sums, squares)
    for n in (0, 1):
        mixed(rest[n], n)


def turn(p, residual, above, gains, mixer, rc, terms, cuts, length, collective_id):
    rows, width = residual.shape
    line_rows, columns = terms[0].shape[1], sum(cut[2] for cut in cuts)
    return pl.pallas_call(
        functools.partial(turn_kernel, length, cuts),
        out_shape=(
            jax.ShapeDtypeStruct((rows, width), F32),
            jax.ShapeDtypeStruct((8, width), F32),
            jax.ShapeDtypeStruct((8, rows, width), BF16),
            jax.ShapeDtypeStruct((8, rows, rc), F32),
            jax.ShapeDtypeStruct((line_rows, columns), BF16),
            TILE,
        ),
        in_specs=[ANY] * (5 + len(terms)),
        out_specs=(ANY, VM, ANY, ANY, VM, VM),
        scratch_shapes=scatter_scratch(rows // 2, width)
        + [pltpu.VMEM((rows, width), F32), pltpu.VMEM((rows, width), BF16), DMA, DMA((14,)), DMA((14,))]
        + [pltpu.VMEM((2, 2, rows, width), BF16), DMA((2, 2))]
        + held(residual, above, gains, mixer)
        + [pltpu.VMEM((rows, width), F32), pltpu.VMEM((8, rows, rc), F32), DMA((4,)), DMA((5,))]
        + lines_scratch(length, line_rows, cuts),
        compiler_params=params(collective_id),
        cost_estimate=pl.CostEstimate(flops=0, bytes_accessed=300 * 2**20, transcendentals=0),
    )(p.reshape(8, rows, width), residual, above, gains, mixer, *terms)


def closing_kernel(
    length, x_in, dmz_in, dproj_in, mixed_in, mixer_in, q, residual_in, block, inputs_in, above_in, gains_in, gp_in,
    grad_out, gain, gates_o, out_out, e_o, early_o, sums, squares,
    early_sums, early_l, early_s, early_r, x_part, dmz_part, g, back, total, o, up_a, down_a, up_b, down_b, gp_got, gp_sum,
    ls, lr, load_s, loc, es, er, gate_s, gate_r, move_s, move_r,
    dproj, mixed, mixer, residual, inputs, above, gains, gp, in_s, keep_s,
    mine, sib_q, got_q, loc_q, ss_q, rs_q, sib_p, got_p, ss_p, rs_p,
):
    inflow = starts(
        local_copies(
            (
                (gp_in, gp), (dproj_in, dproj), (mixed_in, mixed), (mixer_in, mixer), (residual_in, residual),
                (inputs_in, inputs), (above_in, above), (gains_in, gains),
            ),
            in_s,
        )
    )
    y, c, z, x = place()
    others = line_peers(length)
    s = 2 * z + x
    owner = x * length + z
    to_z = owner // 2
    to_x = owner - 2 * to_z
    from_z, from_x = lax.rem(s, length), s // length
    moves = jnp.where(jnp.logical_and(to_z == z, to_x == x), 0, 1)
    barrier = pltpu.get_barrier_semaphore()
    for peer in others + plane_peers():
        pl.semaphore_signal(barrier, inc=1, device_id=peer, device_id_type=MESH)

    @pl.when(moves == 1)
    def _():
        pl.semaphore_signal(barrier, inc=1, device_id=device(y, c, to_z, to_x), device_id_type=MESH)
        pl.semaphore_signal(barrier, inc=1, device_id=device(y, c, from_z, from_x), device_id_type=MESH)

    pl.semaphore_wait(barrier, len(others) + 7 + 2 * moves)
    model = mixer.shape[0]
    tokens = dproj.shape[0]
    part = mixed.shape[1]
    columns = x_part.shape[2]
    steps = model // columns
    rows, width = residual.shape
    half = rows // 2
    line_rows = g.shape[1]

    def loads(i, slot):
        at = pl.ds(pl.multiple_of(i * columns, columns), columns)
        return (
            pltpu.make_async_copy(x_in.at[:, at], x_part.at[slot], load_s.at[0, slot]),
            pltpu.make_async_copy(dmz_in.at[:, at], dmz_part.at[slot], load_s.at[1, slot]),
        )

    group = steps // 4
    order = (3, 1, 2, 0)

    def fetch(i, slot):
        for copy in loads(i, slot):
            copy.start()

    fetch(order[0] * group, 0)
    inflow[0].wait()
    gate = [
        remote(gp.at[lax.rem(z + k + 1, length)], gp_got.at[k], gate_s.at[k], gate_r.at[k], others[k])
        for k in range(length - 1)
    ]
    split = up_a.shape[2]
    line_a = HeldLine(g, 0, up_a, down_a, ls.at[0], lr.at[0])
    line_b = HeldLine(g, split, up_b, down_b, ls.at[1], lr.at[1])
    queue = [chain for _ in range(1, length) for chain in (line_a, line_b)]

    def advance(times=1):
        for _ in range(times):
            if queue:
                queue.pop(0).start()

    output = scatter_steps(q, total, mine, sib_q, None, got_q, loc_q, ss_q, rs_q)
    next(output)
    copies, own = exchange_steps(block, e_o, loc, es, er)

    def compute(n, start=0, stop=None):
        @pl.loop(start, group if stop is None else stop)
        def _(j):
            count = n * group + j
            slot = count - count // 2 * 2
            i = order[n] * group + j

            @pl.when(j + 1 < group)
            def _():
                fetch(i + 1, 1 - slot)

            if n < 3:

                @pl.when(j + 1 == group)
                def _():
                    fetch(order[n + 1] * group, 1 - slot)

            for copy in loads(i, slot):
                copy.wait()
            front = contract_first(x_part[slot], dproj[...])
            tail = contract_first(dmz_part[slot], mixed[...])
            k = i * columns // line_rows
            at = pl.ds(pl.multiple_of(i * columns - k * line_rows, columns), columns)
            g[k, at] = jnp.concatenate([front, tail], axis=1).astype(BF16)

    waits(inflow[1:4])
    compute(0, 0, group // 2)
    next(output)
    compute(0, group // 2)
    compute(1)
    if length == 4:
        advance(2)
    next(output)

    @pl.loop(0, 8)
    def _(i):
        lines = dproj[pl.ds(pl.multiple_of(i * rows, rows), rows)]
        back[i] = contract_last(lines, mixer[:, : 2 * part]).astype(BF16)

    incoming = scatter_steps(back, o, None, sib_p, None, got_p, None, ss_p, rs_p)
    next(incoming)
    next(output)
    next(incoming)
    compute(2)
    advance(1 if length == 4 else 0)
    for _ in output:
        pass
    next(incoming)
    compute(3)
    advance(1 if length == 4 else 2)
    pair = width // (4 * length)
    waits(inflow[4:])
    keeps = []
    for n in (0, 1):

        def finish_output(at):
            whole = pl.ds(pl.multiple_of(at.start + n * half, 16), 16)
            store_turned(mine.at[0, n], at, (residual[whole] + total[whole]).astype(BF16), length, pair)

        rows_loop(half, finish_output)
        keeps.append(
            pltpu.make_async_copy(mine.at[0, n], out_out.at[pl.ds(n * half, half)], keep_s.at[n])
        )
        keeps[n].start()
    keeps.append(pltpu.make_async_copy(above, grad_out, keep_s.at[2]))
    advance()
    for copy in gate:
        copy.wait()
    rows_sum = gp[z]
    for k in range(length - 1):
        rows_sum = rows_sum + gp_got[k]
    gp_sum[...] = rows_sum
    move = pltpu.make_async_remote_copy(
        src_ref=gp_sum, dst_ref=gates_o, send_sem=move_s, recv_sem=move_r,
        device_id=device(y, c, to_z, to_x), device_id_type=MESH,
    )
    pl.when(moves == 1)(lambda: move.start())

    @pl.when(moves == 0)
    def _():
        gates_o[...] = rows_sum

    gain[...] = jnp.zeros_like(gain)

    def finish_grad(at):
        grad, gain_part = norm_rows_back(inputs[at].astype(F32), gains[0:1], o[at])
        store_turned(above, at, above[at] + grad, length, pair)
        gain[...] += gain_part

    for name in incoming:
        if name == "late":
            advance()
        if name == "low half":
            rows_loop(half, finish_grad)
        if name == "high half":
            rows_loop(half, finish_grad, half)
            keeps[2].start()
    while queue:
        advance()
    squares[...] = jnp.zeros_like(squares)
    line_a.end(early_sums, 0, squares)
    early_copies, early_own = exchange_steps(early_sums, early_o, early_l, early_s, early_r)
    line_b.end(sums, 0, squares)
    pl.when(moves == 1)(lambda: move.wait())
    waits(keeps)
    for copy in copies + early_copies:
        copy.wait()
    own.wait()
    early_own.wait()


def closing(x, dmz, dproj, mixed, mixer, q, residual, block, inputs, above, gains, gp, length, collective_id):
    rows, width = residual.shape
    tokens, model = x.shape
    part = mixed.shape[1]
    share = block.shape[0] // 8
    block = block.reshape(8, share, block.shape[1])
    line_rows = model // length
    columns = min(256, line_rows)
    split = -(-3 * part // 256) * 128
    slots_a, slots_b = (pltpu.VMEM((length - 1, line_rows, n), BF16) for n in (split, 3 * part - split))
    pack = gp.shape[1:]
    return pl.pallas_call(
        functools.partial(closing_kernel, length),
        out_shape=(
            jax.ShapeDtypeStruct((rows, width), F32),
            jax.ShapeDtypeStruct((8, width), F32),
            jax.ShapeDtypeStruct(pack, F32),
            jax.ShapeDtypeStruct((rows, width), BF16),
            jax.ShapeDtypeStruct(block.shape, BF16),
            jax.ShapeDtypeStruct((8, share, split), BF16),
            jax.ShapeDtypeStruct((line_rows, 3 * part - split), BF16),
            TILE,
        ),
        in_specs=[ANY] * 12,
        out_specs=(ANY, VM, VM, ANY, ANY, ANY, VM, VM),
        scratch_shapes=[
            pltpu.VMEM((line_rows, split), BF16), DMA, DMA((7,)), DMA((7,)),
            pltpu.VMEM((2, tokens, columns), BF16),
            pltpu.VMEM((2, tokens, columns), BF16),
            pltpu.VMEM((length, line_rows, 3 * part), BF16),
            pltpu.VMEM((8, rows, width), BF16),
            pltpu.VMEM((rows, width), F32),
            pltpu.VMEM((rows, width), F32),
            slots_a, slots_a, slots_b, slots_b,
            pltpu.VMEM((length - 1,) + pack, F32),
            pltpu.VMEM(pack, F32),
            DMA((2, 2, length)), DMA((2, 2, length)), DMA((2, 2)),
            DMA, DMA((7,)), DMA((7,)), DMA((length,)), DMA((length,)), DMA, DMA,
            *held(dproj, mixed, mixer, residual, inputs, above, gains, gp),
            DMA((8,)), DMA((3,)),
            pltpu.VMEM((4, 2, rows // 2, width), BF16),
            pltpu.VMEM((4, 2, rows // 2, width), BF16),
            pltpu.VMEM((6, rows // 2, width), BF16),
            DMA((8,)), DMA((14,)), DMA((14,)),
            pltpu.VMEM((4, 2, rows // 2, width), BF16),
            pltpu.VMEM((6, rows // 2, width), BF16),
            DMA((14,)), DMA((14,)),
        ],
        compiler_params=params(collective_id),
        cost_estimate=pl.CostEstimate(
            flops=10 * tokens * model * dproj.shape[1] // 2, bytes_accessed=350 * 2**20, transcendentals=0
        ),
    )(x, dmz, dproj, mixed, mixer, q.reshape(8, rows, width), residual, block, inputs, above, gains, gp)


def first_kernel(
    length, inputs_in, above_in, mixer_in, mlp_in, gains_in, gate_in, chan_in,
    normed_o, wm_o, wf_o, wd_o, w2_o, gains_o, gate_o, chan_o, inputs_o, above_o,
    inputs, above, mixer_w, mlp_w, gains_w, gate_w, chan_w, load_s,
    inputs_k, above_k, w2, keep_s, gp_o, gn, gp, normed, gn_all, wm, wf, wd, loc, ms, mr, fs, fr, line_s, line_r, gain_s, gain_r, move_s, move_r,
    gather_s, gather_r, hop_s, hop_r,
):
    loads = [
        pltpu.make_async_copy(src, dst, load_s.at[n])
        for n, (src, dst) in enumerate(
            (
                (gains_in, gains_w), (gate_in, gate_w), (chan_in, chan_w), (mixer_in, mixer_w),
                (mlp_in, mlp_w), (inputs_in, inputs), (above_in, above),
            )
        )
    ]
    for copy in loads:
        copy.start()
    y, c, z, x = place()
    s = 2 * z + x
    me = rank(y, c, x)
    rows, width = inputs.shape
    pair = width // (4 * length)
    line = line_peers(length)
    plane = plane_peers()
    to_z, to_x = lax.rem(s, length), s // length
    moves = jnp.where(jnp.logical_and(to_z == z, to_x == x), 0, 1)
    src = x * length + z
    from_z = src // 2
    from_x = src - 2 * from_z
    barrier = pltpu.get_barrier_semaphore()
    for peer in line + plane:
        pl.semaphore_signal(barrier, inc=1, device_id=peer, device_id_type=MESH)

    @pl.when(moves == 1)
    def _():
        pl.semaphore_signal(barrier, inc=1, device_id=device(y, c, to_z, to_x), device_id_type=MESH)
        pl.semaphore_signal(barrier, inc=1, device_id=device(y, c, from_z, from_x), device_id_type=MESH)

    def fill(pack, source, js, offset=0):
        part = pack.shape[2] // len(js)
        whole = source.shape[1] // 24
        for t in range(8):
            for n, j in enumerate(js):
                start = (j * 8 + t) * whole + offset
                pack[t, :, n * part : (n + 1) * part] = source[:, start : start + part].astype(BF16)

    loads[3].wait()
    fill(wm, mixer_w, (0, 1, 2))
    for copy in loads[:3]:
        copy.wait()
    share = gains_w.shape[1]
    gn[...] = jnp.zeros_like(gn)
    for n in (0, 1):

        @pl.when(x == n)
        def _():
            gn[:2, n * share : (n + 1) * share] = gains_w[...]

    gp[...] = jnp.zeros_like(gp)
    channels = contract_first(chan_w[...].astype(BF16), unit(8))
    gp[: gate_w.shape[0]] = jnp.concatenate(
        [
            gate_w[...],
            channels,
            jnp.zeros((gate_w.shape[0], gp.shape[1] - gate_w.shape[1] - 8), F32),
        ],
        axis=1,
    ).astype(BF16)
    gn_all[me, z] = gn[...]
    pl.semaphore_wait(barrier, len(line) + len(plane) + 2 * moves)
    gains = [
        remote(gn, gn_all.at[me, z], line_s.at[0, k], line_r.at[0, k], line[k]) for k in range(length - 1)
    ]
    gate_move = pltpu.make_async_remote_copy(
        src_ref=gp, dst_ref=gp_o.at[to_z], send_sem=move_s, recv_sem=move_r,
        device_id=device(y, c, to_z, to_x), device_id_type=MESH,
    )
    gate_stay = pltpu.make_async_copy(gp, gp_o.at[z], loc.at[2])
    pl.when(moves == 1)(lambda: gate_move.start())
    pl.when(moves == 0)(lambda: gate_stay.start())

    mixer, mixer_own = exchange_steps(wm, wm_o.at[0], loc.at[0], ms, mr)
    hops = LineGather(wm_o, length, hop_s, hop_r)
    mixer_own.wait()
    hops.start_piece(me)

    def pass_piece(n):
        fy, fc, fx = FLIPS[n]
        mixer[n].wait_recv()
        hops.start_piece(rank(flip(y, fy), flip(c, fc), flip(x, fx)))

    pass_piece(1)
    for copy in gains:
        copy.wait()
    spread = [
        remote(gn_all.at[me], gn_all.at[me], gain_s.at[n], gain_r.at[n], plane[n]) for n in range(7)
    ]
    loads[4].wait()
    fill(wd, mlp_w, (2,))
    down, down_own = exchange_steps(wd, wd_o.at[0], loc.at[4], fs.at[1], fr.at[1])
    for n in (0, 2, 3, 5, 4, 6):
        pass_piece(n)
    fill(wf, mlp_w, (0, 1))
    feed, feed_own = exchange_steps(wf, wf_o.at[0], loc.at[3], fs.at[0], fr.at[0])
    pl.when(moves == 1)(lambda: gate_move.wait())
    pl.when(moves == 0)(lambda: gate_stay.wait())
    gates = [
        remote(gp_o.at[z], gp_o.at[z], line_s.at[1, k], line_r.at[1, k], line[k])
        for k in range(length - 1)
    ]
    fill(w2, mlp_w, (0, 1, 2), wd.shape[2])
    for copy in spread:
        copy.wait()
    for k in range(length):
        other = lax.rem(z + k, length)
        for b in range(4):
            at = slice((4 * k + b) * pair, (4 * k + b + 1) * pair)
            tile = (gn_all[2 * b, other] + gn_all[2 * b + 1, other])[:, :pair]
            gains_o[:, at] = tile.astype(BF16).astype(F32)
    for copy in mixer:
        copy.wait_send()

    def body(at):
        v = load_turned(inputs, at, length, pair)
        inputs_k[at] = v
        v = v.astype(F32)
        normed[at] = (v * inverse_rms(v) * gains_o[0:1]).astype(BF16)
        above_k[at] = load_turned(above, at, length, pair)

    for copy in loads[5:]:
        copy.wait()
    half = rows // 2
    gather = Gather(normed, normed_o, loc.at[1], gather_s, gather_r)
    rows_loop(half, body)
    gather.begin_half(0)
    hops.arrive(1)
    if length > 2:
        hops.start(2)
    rows_loop(half, body, half)
    gather.begin_half(1)
    keeps = starts(local_copies(((inputs_k, inputs_o), (above_k, above_o)), keep_s))
    for copy in gates:
        copy.wait()
    gate_rows, columns = gate_w.shape
    head = columns // 2
    own = jnp.concatenate([gp_o[n, :gate_rows].astype(F32) for n in range(length)]).astype(BF16)
    part, rc = own.shape[0], gate_o.shape[0]
    gate_o[...] = jnp.zeros_like(gate_o)
    for first_row in range(0, part, head):
        at = slice(first_row, first_row + head)
        wide = [jnp.zeros((head, first_row), F32)] if first_row else []
        for n in (0, 1):
            block = own[at, n * head : (n + 1) * head].astype(F32)
            rest = jnp.zeros((head, rc - first_row - head), F32)
            gate_o[at, n * rc : (n + 1) * rc] = jnp.concatenate([*wide, block, rest], axis=1).astype(BF16)
    rows_of = contract_last(unit(8), own[:, columns : columns + 8])
    lam = rows_of[7:8]
    u = jnp.exp(-jnp.abs(lam))
    t = u / (2.0 + u)
    series = jnp.full_like(t, 1.0 / 17.0)
    for n in range(15, 0, -2):
        series = series * t * t + 1.0 / n
    rate = 8.0 * (jnp.maximum(-lam, 0.0) + 2.0 * t * series)
    fill_rows = jnp.concatenate([jnp.zeros((7, rc - part), F32), jnp.ones((1, rc - part), F32)])
    chan_o[...] = jnp.concatenate([jnp.concatenate([rows_of[:7], rate]), fill_rows], axis=1)
    if length > 3:
        hops.arrive(2)
        hops.start(3)
    gather.middle()
    late, late_own = exchange_steps(w2, w2_o.at[0], loc.at[0], fs.at[2], fr.at[2])
    gather.relays()
    for hop in range(min(3, length - 1), length):
        hops.arrive(hop)
        if hop + 1 < length:
            hops.start(hop + 1)
    gather.finish()
    waits(keeps)
    for copy in down + feed + late:
        copy.wait()
    late_own.wait()
    down_own.wait()
    feed_own.wait()
    hops.finish()


def early(f8):
    return f8 // 384 * 256


def unit(n):
    return (
        lax.broadcasted_iota(jnp.int32, (n, n), 0) == lax.broadcasted_iota(jnp.int32, (n, n), 1)
    ).astype(BF16)


def first(inputs, above, mixer, mlp, gains, gate, chan, rc, length, collective_id):
    rows, width = inputs.shape
    pack = (-(-gate.shape[0] // 16) * 16, rc)
    share = mixer.shape[0]
    f8 = mlp.shape[1] // 24
    wm, wf, wd, w2 = (
        (8, share, n) for n in (mixer.shape[1] // 8, 2 * early(f8), early(f8), 3 * (f8 - early(f8)))
    )
    low = jax.ShapeDtypeStruct((rows, width), BF16)
    return pl.pallas_call(
        functools.partial(first_kernel, length),
        out_shape=(
            jax.ShapeDtypeStruct((8, rows, width), BF16),
            jax.ShapeDtypeStruct((length,) + wm, BF16),
            jax.ShapeDtypeStruct((length,) + wf, BF16),
            jax.ShapeDtypeStruct((length,) + wd, BF16),
            jax.ShapeDtypeStruct((length,) + w2, BF16),
            jax.ShapeDtypeStruct((8, width), F32),
            jax.ShapeDtypeStruct((rc, 2 * rc), BF16),
            jax.ShapeDtypeStruct((8, rc), F32),
            low,
            low,
        ),
        in_specs=[ANY] * 7,
        out_specs=(ANY, ANY, ANY, ANY, ANY, VM, VM, VM, ANY, ANY),
        scratch_shapes=[
            *[pltpu.VMEM(v.shape, v.dtype) for v in (inputs, above, mixer, mlp, gains, gate, chan)],
            DMA((7,)),
            pltpu.VMEM((rows, width), BF16),
            pltpu.VMEM((rows, width), BF16),
            pltpu.VMEM(w2, BF16),
            DMA((2,)),
            pltpu.VMEM((length,) + pack, BF16),
            pltpu.VMEM((8, 128), F32),
            pltpu.VMEM(pack, BF16),
            pltpu.VMEM((rows, width), BF16),
            pltpu.VMEM((8, length, 8, 128), F32),
            pltpu.VMEM(wm, BF16),
            pltpu.VMEM(wf, BF16),
            pltpu.VMEM(wd, BF16),
            DMA((5,)), DMA((7,)), DMA((7,)), DMA((3, 7)), DMA((3, 7)),
            DMA((2, length)), DMA((2, length)), DMA((7,)), DMA((7,)), DMA, DMA,
            DMA((14,)), DMA((14,)), DMA((2, length)), DMA((2, length)),
        ],
        compiler_params=params(collective_id),
        cost_estimate=pl.CostEstimate(flops=0, bytes_accessed=300 * 2**20, transcendentals=0),
    )(inputs, above, mixer, mlp, gains, gate, chan)


def last_kernel(
    length, share, wm, gain, gain_two, gates, sq_a, sq_b, sq_c, sq_d,
    wm_o, gains_o, norm_o, factor_o, by_plane, by_line, loc, ss, rs, gs, gr, ls, lr,
):
    y, c, z, x = place()
    me = rank(y, c, x)
    line = line_peers(length)
    plane = plane_peers()
    width = gain.shape[1]
    pair = width // (4 * length)
    squares = sq_a[...] + sq_b[...] + sq_c[...] + sq_d[...] + tile_of_squares(gates[...])
    squares = jnp.concatenate([squares, jnp.zeros((8, width - 128), F32)], axis=1)
    rows = [jnp.sum(v, axis=0, keepdims=True) for v in (gain[...], gain_two[...], squares)]
    by_plane[me] = jnp.concatenate(rows + [jnp.zeros((1, width), F32)])
    greet(line + plane)
    sends = [
        remote(by_plane.at[me], by_plane.at[me], gs.at[n], gr.at[n], plane[n]) for n in range(7)
    ]
    copies, own = exchange_steps(wm, wm_o, loc, ss, rs)
    for copy in sends:
        copy.wait()
    total = by_plane[0]
    for n in range(1, 8):
        total = total + by_plane[n]
    group = 4 * pair
    for k in range(length):
        at = pl.ds(pl.multiple_of(lax.rem(z + k, length) * group, group), group)
        by_line[z, :, at] = total[:, k * group : (k + 1) * group]
    sends = [
        remote(by_line.at[z], by_line.at[z], ls.at[k], lr.at[k], line[k]) for k in range(length - 1)
    ]
    for copy in sends:
        copy.wait()
    total = by_line[0]
    for n in range(1, length):
        total = total + by_line[n]
    squares = jnp.sum(total[:2] * total[:2], axis=0, keepdims=True) + total[2:3]
    norm = jnp.broadcast_to(jnp.sqrt(jnp.sum(squares, axis=1, keepdims=True)), (8, 128))
    norm_o[...] = norm
    factor_o[...] = clip_limit / jnp.maximum(norm, clip_limit)
    gains = jnp.zeros((2, pair), F32)
    for there in range(length):
        for b in range(4):
            first_lane = (there * 4 + b) * pair
            mine = jnp.logical_and(there == z, b == 2 * y + c)
            gains = jnp.where(mine, total[:2, first_lane : first_lane + pair], gains)
    gains_o[...] = jnp.where(x == 0, gains[:, :share], gains[:, share:])
    for copy in copies:
        copy.wait()
    own.wait()


def last(wm, gain, gain_two, gates, squares, length, collective_id):
    width = gain.shape[1]
    share = wm.shape[1]
    return pl.pallas_call(
        functools.partial(last_kernel, length, share),
        out_shape=(
            jax.ShapeDtypeStruct(wm.shape, wm.dtype),
            jax.ShapeDtypeStruct((2, share), F32),
            TILE, TILE,
        ),
        in_specs=[ANY] + [VM] * 7,
        out_specs=(ANY,) + (VM,) * 3,
        scratch_shapes=[
            pltpu.VMEM((8, 4, width), F32),
            pltpu.VMEM((length, 4, width), F32),
            DMA, DMA((7,)), DMA((7,)), DMA((7,)), DMA((7,)),
            DMA((length,)), DMA((length,)),
        ],
        compiler_params=params(collective_id),
    )(wm, gain, gain_two, gates, *squares)


def minus_expm1(v):
    series = 1.0 + v * (1.0 / 8.0)
    for n in (7.0, 6.0, 5.0, 4.0, 3.0, 2.0):
        series = 1.0 + series * v * (1.0 / n)
    return jnp.where(v > -0.5, -v * series, 1.0 - jnp.exp(v))


def gelu_parts(v):
    square = v * v
    h = 0.5 * jnp.tanh(v * (GELU_CUBE * square + GELU_SCALE)) + 0.5
    return v * h, h, square


def gelu_slope(gelu, h, square):
    return h + gelu * (1.0 - h) * (6.0 * GELU_CUBE * square + 2.0 * GELU_SCALE)


CHUNK = 128


def forward_kernel(
    length, x_in, mixer_in, gate, chan, above, w_in,
    mixed, branch_o, decay_o, width_o, recur_o, enter_o, conv_o, xe_o, se_o, ends_o, above_o, w,
    x_part, pre, loc_h, ends, carry, hs, hr, es, er, gather_l, gather_s, gather_r, hop_s, hop_r, load_s, keep_s, mixer,
    branch, decay_k, width_k, recur_k, enter_k, conv_k, xe, se,
):
    keeps = [
        pltpu.make_async_copy(src, dst, keep_s.at[n])
        for n, (src, dst) in enumerate(
            (
                (branch, branch_o), (decay_k, decay_o), (width_k, width_o), (recur_k, recur_o),
                (enter_k, enter_o), (conv_k, conv_o), (xe, xe_o), (se, se_o),
            )
        )
    ]
    y, c, z, x = place()
    line = line_peers(length)
    seqs, span, rc = branch.shape
    part = mixed.shape[2]
    chunks = span // CHUNK

    def load(b, slot):
        at = pl.ds(pl.multiple_of(b * span, span), span)
        return pltpu.make_async_copy(x_in.at[at], x_part.at[slot], load_s.at[slot])

    load(0, 0).start()
    mixer_load = pltpu.make_async_copy(mixer_in, mixer, load_s.at[2])
    mixer_load.start()
    greet(line + gather_peers())
    hops = LineGather(w, length, hop_s, hop_r)
    hops.start(1)
    gather = Gather(above, above_o, gather_l, gather_s, gather_r)
    gather.begin()

    mixer_load.wait()

    @pl.loop(0, seqs)
    def _(b):
        slot = b - b // 2 * 2

        @pl.when(b + 1 < seqs)
        def _():
            load(b + 1, 1 - slot).start()

        load(b, slot).wait()
        both = jnp.dot(x_part[slot], mixer[:, : 2 * part], preferred_element_type=F32)
        none = jnp.zeros((span, rc - part), F32)
        branch[b] = jnp.concatenate([both[:, :part], none], axis=1)
        low = both[:, part:].astype(BF16).astype(F32)
        xe[b, 8:] = jnp.concatenate([low, none], axis=1)

    ahead = device(y, c, lax.rem(z + 1, length), x)
    halo = remote(xe.at[:, pl.ds(span, 8)], xe.at[:, pl.ds(0, 8)], hs, hr, ahead)

    def coefficients(b, chunk):
        r = pl.multiple_of(chunk * CHUNK, CHUNK)
        at = pl.ds(r, CHUNK)
        window = xe[b, pl.ds(r, CHUNK + 8)]
        total = chan[4:5] + chan[0:1] * window[8:]
        for k in (1, 2, 3):
            total = total + chan[k : k + 1] * pltpu.roll(window, k, 0)[8:]
        low = total.astype(BF16)
        conv_k[b, at] = low
        value = low.astype(F32)
        gates = jnp.dot(low, gate[...], preferred_element_type=F32)
        recur = jax.nn.sigmoid(gates[:, :rc] + chan[5:6])
        enter = jax.nn.sigmoid(gates[:, rc:] + chan[6:7])
        log_decay = -chan[7:8] * recur
        decay = jnp.exp(log_decay)
        width = jnp.sqrt(minus_expm1(2.0 * log_decay))
        recur_k[b, at] = recur
        enter_k[b, at] = enter
        decay_k[b, at] = decay
        width_k[b, at] = width
        loc_h[b, at] = width * enter * value

    def later_chunks(i):
        b = i // (chunks - 1)
        coefficients(b, 1 + i - b * (chunks - 1))

    many = seqs * (chunks - 1)
    pl.loop(0, many // 2)(later_chunks)
    hops.arrive(1)
    if length > 2:
        hops.start(2)
    gather.middle()
    pl.loop(many // 2, many)(later_chunks)
    halo.wait()

    @pl.when(z == 0)
    def _():
        xe[:, 0:8] = jnp.zeros((seqs, 8, rc), F32)

    @pl.loop(0, seqs)
    def _(b):
        coefficients(b, 0)

    for copy in keeps[:-1]:
        copy.start()
    row = lax.broadcasted_iota(jnp.int32, (8, rc), 0)

    def tile(i, held):
        at = pl.ds(pl.multiple_of(i * 8, 8), 8)
        new = []
        for b in range(seqs):
            a, h = decay_k[b, at], loc_h[b, at]
            for n in (1, 2, 4):
                keep = row >= n
                h = h + jnp.where(keep, a * pltpu.roll(h, n, 0), 0.0)
                a = jnp.where(keep, a * pltpu.roll(a, n, 0), a)
            h = h + a * held[b][1]
            a = a * held[b][0]
            loc_h[b, at] = h
            pre[b, at] = a
            new.append((a[7:8], h[7:8]))
        return tuple(new)

    one, zero = jnp.ones((1, rc), F32), jnp.zeros((1, rc), F32)
    final = lax.fori_loop(0, span // 8, tile, ((one, zero),) * seqs)
    for b in range(seqs):
        ends[z, 0, b] = jnp.broadcast_to(final[b][0], (8, rc))
        ends[z, 1, b] = jnp.broadcast_to(final[b][1], (8, rc))
        ends_o[b] = jnp.broadcast_to(final[b][0], (8, rc))
    moves = [remote(ends.at[z], ends.at[z], es.at[k], er.at[k], line[k]) for k in range(length - 1)]
    if length > 3:
        hops.arrive(2)
        hops.start(3)
    for copy in moves:
        copy.wait()
    carry[...] = jnp.zeros_like(carry)
    for k in range(length):
        carry[...] = jnp.where(k < z, ends[k, 0] * carry[...] + ends[k, 1], carry[...])

    for b in range(seqs):
        se[b, 0:8] = carry[b]

    @pl.loop(0, seqs * chunks)
    def _(i):
        b = i // chunks
        r = pl.multiple_of((i - b * chunks) * CHUNK, CHUNK)
        at = pl.ds(r, CHUNK)
        state = loc_h[b, at] + pre[b, at] * carry[b, 0:1]
        se[b, pl.ds(r + 8, CHUNK)] = state
        gelu, _, _ = gelu_parts(branch[b, at])
        mixed[b, at] = (state * gelu)[:, :part].astype(BF16)

    keeps[-1].start()
    gather.end()
    for hop in range(min(3, length - 1), length):
        hops.arrive(hop)
        if hop + 1 < length:
            hops.start(hop + 1)
    hops.finish()
    waits(keeps)


def recur_forward(x, mixer, gate, chan, above, w, length, collective_id):
    rc = gate.shape[0]
    part = mixer.shape[1] // 3
    rows = x.shape[0] // 8
    seqs, span = 4, 2 * rows
    full = jax.ShapeDtypeStruct((seqs, span, rc), F32)
    longer = jax.ShapeDtypeStruct((seqs, span + 8, rc), F32)
    kept = (full, full, full, full, full, jax.ShapeDtypeStruct((seqs, span, rc), BF16), longer, longer)
    return pl.pallas_call(
        functools.partial(forward_kernel, length),
        out_shape=(
            jax.ShapeDtypeStruct((seqs, span, part), BF16),
            *kept,
            jax.ShapeDtypeStruct((seqs, 8, rc), F32),
            jax.ShapeDtypeStruct((8,) + above.shape, above.dtype),
            jax.ShapeDtypeStruct(w.shape, w.dtype),
        ),
        in_specs=[ANY, ANY, VM, VM, ANY, ANY],
        out_specs=(VM,) + (ANY,) * 8 + (VM, ANY, ANY),
        scratch_shapes=[
            pltpu.VMEM((2, span, x.shape[1]), BF16),
            pltpu.VMEM((seqs, span, rc), F32),
            pltpu.VMEM((seqs, span, rc), F32),
            pltpu.VMEM((length, 2, seqs, 8, rc), F32),
            pltpu.VMEM((seqs, 8, rc), F32),
            DMA, DMA, DMA((length,)), DMA((length,)),
            DMA, DMA((14,)), DMA((14,)), DMA((2, length)), DMA((2, length)),
            DMA((3,)), DMA((8,)),
            *held(mixer),
            *[pltpu.VMEM(v.shape, v.dtype) for v in kept],
        ],
        input_output_aliases={5: 11},
        compiler_params=params(collective_id),
        cost_estimate=pl.CostEstimate(
            flops=2 * seqs * span * rc * rc * 2, bytes_accessed=100 * 2**20, transcendentals=0
        ),
    )(x, mixer, gate, chan, above, w)


def backward_kernel(
    length, cuts, head, dmix, gate, chan, decay, width, recur, enter, conv, xe, se, ends_f, proj, block_a, block_b, *refs
):
    parts = 1 + max(cut[0] for cut in cuts)
    terms, refs = refs[:parts], refs[parts:]
    dproj, gates_o, sums, squares, block_ao, block_bo, *refs = refs
    dgate, gchan, *refs = refs
    suffix, grad, de, ends, carry, hs, hr, es, er, keep_s, move_l, move_s, move_r, *refs = refs
    kept, line_refs = refs[:8], refs[8:]
    loads = [
        pltpu.make_async_copy(src, dst, keep_s.at[n])
        for n, (src, dst) in enumerate(
            zip((dmix, proj, se, decay, width, recur, enter, conv, xe), (de.at[:, pl.ds(0, decay.shape[1])], *kept))
        )
    ]
    proj, se, decay, width, recur, enter, conv, xe = kept
    y, c, z, x = place()
    line = line_peers(length)
    greet(line + plane_peers())
    scatter = Lines(terms, cuts, length, line_refs)
    scatter.begin()
    for copy in loads:
        copy.start()
    moves = [
        exchange_steps(block_a, block_ao, move_l.at[0], move_s.at[0], move_r.at[0]),
        exchange_steps(block_b, block_bo, move_l.at[1], move_s.at[1], move_r.at[1]),
    ]
    seqs, span, rc = decay.shape
    part = dproj.shape[2] // 2
    chunks = span // CHUNK
    for copy in loads[:3]:
        copy.wait()

    @pl.loop(0, seqs * chunks)
    def _(i):
        b = i // chunks
        r = pl.multiple_of((i - b * chunks) * CHUNK, CHUNK)
        at = pl.ds(r, CHUNK)
        branch = proj[b, at]
        gelu, h, square = gelu_parts(branch)
        above = de[b, at]
        state = se[b, pl.ds(r + 8, CHUNK)]
        grad[b, at] = above * gelu
        proj[b, at] = above * state * gelu_slope(gelu, h, square)

    loads[3].wait()
    row = lax.broadcasted_iota(jnp.int32, (8, rc), 0)

    def tile(i, held):
        at = pl.ds(pl.multiple_of(span - 8 - i * 8, 8), 8)
        new = []
        for b in range(seqs):
            product, total, following = held[b]
            plain, h = decay[b, at], grad[b, at]
            a = jnp.where(row == 7, following, pltpu.roll(plain, 7, 0))
            for n in (1, 2, 4):
                keep = row < 8 - n
                h = h + jnp.where(keep, a * pltpu.roll(h, 8 - n, 0), 0.0)
                a = jnp.where(keep, a * pltpu.roll(a, 8 - n, 0), a)
            h = h + a * total
            a = a * product
            grad[b, at] = h
            suffix[b, at] = a
            new.append((a[0:1], h[0:1], plain[0:1]))
        return tuple(new)

    one, zero = jnp.ones((1, rc), F32), jnp.zeros((1, rc), F32)
    final = lax.fori_loop(0, span // 8, tile, ((one, zero, one),) * seqs)
    for b in range(seqs):
        ends[z, 0, b] = ends_f[b]
        ends[z, 1, b] = jnp.broadcast_to(final[b][1] * final[b][2], (8, rc))
    tails = [remote(ends.at[z], ends.at[z], es.at[k], er.at[k], line[k]) for k in range(length - 1)]
    for copy in tails:
        copy.wait()
    for copy in loads[4:]:
        copy.wait()
    carry[...] = jnp.zeros_like(carry)
    for k in reversed(range(length)):
        carry[...] = jnp.where(k > z, ends[k, 0] * carry[...] + ends[k, 1], carry[...])

    gchan[...] = jnp.zeros_like(gchan)

    def gradients(b, chunk):
        r = pl.multiple_of(chunk * CHUNK, CHUNK)
        at = pl.ds(r, CHUNK)
        g = grad[b, at] + suffix[b, at] * carry[b, 0:1]
        a, w, ra, ri = decay[b, at], width[b, at], recur[b, at], enter[b, at]
        value = conv[b, at].astype(F32)
        before = pltpu.roll(se[b, pl.ds(r, CHUNK + 8)], 1, 0)[8:]
        dla = g * before * a - g * ri * value * (a * a) / w
        slope = dla * ra * (1.0 - ra)
        dpa = (-chan[7:8] * slope).astype(BF16)
        dpi = (g * w * value * ri * (1.0 - ri)).astype(BF16)
        dgate[b, at, :rc] = dpa
        dgate[b, at, rc:] = dpi
        gchan[5] += fold(dpa.astype(F32))
        gchan[6] += fold(dpi.astype(F32))
        gchan[7] += fold(dla * ra)
        back = lax.dot_general(
            dgate[b, at], gate[...], (((1,), (1,)), ((), ())), preferred_element_type=F32
        )
        dcv = (g * w * ri + back).astype(BF16).astype(F32)
        de[b, at] = dcv
        gchan[4] += fold(dcv)

    pl.loop(0, seqs)(lambda b: gradients(b, 0))
    behind = device(y, c, lax.rem(z + length - 1, length), x)
    halo = remote(de.at[:, pl.ds(0, 8)], de.at[:, pl.ds(span, 8)], hs, hr, behind)
    scatter.start()
    scatter.start()

    @pl.loop(0, seqs * (chunks - 1))
    def _(i):
        b = i // (chunks - 1)
        gradients(b, 1 + i - b * (chunks - 1))

    scatter.start()
    scatter.start()
    halo.wait()
    low = conv[...].reshape(seqs * span, rc)
    recur_grad, enter_grad = (
        contract_first(low, dgate[:, :, at].reshape(seqs * span, rc)) for at in (slice(0, rc), slice(rc, 2 * rc))
    )

    @pl.when(z == length - 1)
    def _():
        de[:, span:] = jnp.zeros((seqs, 8, rc), F32)

    @pl.loop(0, seqs * chunks)
    def _(i):
        b = i // chunks
        r = pl.multiple_of((i - b * chunks) * CHUNK, CHUNK)
        at = pl.ds(r, CHUNK)
        window = de[b, pl.ds(r, CHUNK + 8)]
        inputs = xe[b, pl.ds(r, CHUNK + 8)]
        dcv = window[:CHUNK]
        total = chan[0:1] * dcv
        gchan[0] += fold(dcv * inputs[8:])
        for k in (1, 2, 3):
            total = total + chan[k : k + 1] * pltpu.roll(window, CHUNK + 8 - k, 0)[:CHUNK]
            gchan[k] += fold(dcv * pltpu.roll(inputs, k, 0)[8:])
        dproj[b, at] = jnp.concatenate([proj[b, at, :part], total[:, :part]], axis=1).astype(BF16)

    rates = 8.0 * minus_expm1(chan[7:8] * (-1.0 / 8.0))
    channels = [jnp.sum(gchan[n], axis=0, keepdims=True) for n in range(8)]
    channels[7] = channels[7] * rates
    channels = lax.dot_general(
        jnp.concatenate(channels), unit(8).astype(F32), (((0,), (0,)), ((), ())),
        precision=lax.Precision.HIGHEST, preferred_element_type=F32,
    )
    blocks = []
    for first_row in range(0, part, head):
        at = slice(first_row, first_row + head)
        blocks.append(jnp.concatenate([recur_grad[at, at], enter_grad[at, at]], axis=1))
    pack = jnp.concatenate(
        [jnp.concatenate(blocks), channels[:part], jnp.zeros((part, rc - 2 * head - 8), F32)], axis=1
    )
    rows = part // length
    if rows < gates_o.shape[1]:
        gates_o[...] = jnp.zeros_like(gates_o)
    for n in range(length):
        gates_o[n, :rows] = pack[n * rows : (n + 1) * rows]
    scatter.end(sums, squares)
    for copies, own in moves:
        for copy in copies:
            copy.wait()
        own.wait()


def recur_backward(dmix, gate, chan, kept, part, head, blocks, terms, cuts, length, collective_id):
    proj, decay, width, recur, enter, conv, xe, se, ends = kept
    seqs, span, rc = decay.shape
    gate_pad = -(-(part // length) // 16) * 16
    line_rows, columns = terms[0].shape[1], sum(cut[2] for cut in cuts)
    return pl.pallas_call(
        functools.partial(backward_kernel, length, cuts, head),
        out_shape=(
            jax.ShapeDtypeStruct((seqs, span, 2 * part), BF16),
            jax.ShapeDtypeStruct((length, gate_pad, rc), F32),
            jax.ShapeDtypeStruct((line_rows, columns), BF16), TILE,
            *[jax.ShapeDtypeStruct(block.shape, BF16) for block in blocks],
        ),
        in_specs=[ANY, VM, VM] + [ANY] * 7 + [VM] + [ANY] * (3 + len(terms)),
        out_specs=(VM,) * 4 + (ANY, ANY),
        scratch_shapes=[
            pltpu.VMEM((seqs, span, 2 * rc), BF16),
            pltpu.VMEM((8, 8, rc), F32),
            pltpu.VMEM((seqs, span, rc), F32),
            pltpu.VMEM((seqs, span, rc), F32),
            pltpu.VMEM((seqs, span + 8, rc), F32),
            pltpu.VMEM((length, 2, seqs, 8, rc), F32),
            pltpu.VMEM((seqs, 8, rc), F32),
            DMA, DMA, DMA((length,)), DMA((length,)),
            DMA((9,)), DMA((2,)), DMA((2, 7)), DMA((2, 7)),
            *[
                pltpu.VMEM(shape, dtype)
                for shape, dtype in (
                    (decay.shape, F32), (se.shape, F32), (decay.shape, F32), (decay.shape, F32),
                    (decay.shape, F32), (decay.shape, F32), (decay.shape, BF16), (xe.shape, F32),
                )
            ],
        ]
        + lines_scratch(length, line_rows, cuts),
        compiler_params=params(collective_id),
        cost_estimate=pl.CostEstimate(
            flops=2 * seqs * span * rc * rc * 2, bytes_accessed=120 * 2**20, transcendentals=0
        ),
    )(dmix, gate, chan, decay, width, recur, enter, conv, xe, se, ends, proj, *blocks, *terms)


def contract_last(left, right):
    return lax.dot_general(
        left, right, (((1,), (1,)), ((), ())), preferred_element_type=F32
    )


def contract_first(left, right):
    return lax.dot_general(
        left, right, (((0,), (0,)), ((), ())), preferred_element_type=F32
    )


def resident(shape):
    return pl.BlockSpec(shape, lambda i: (0, 0), pipeline_mode=pl.Buffered(1))


STEPS = 4


def feed_forward(x, above, gate_up, down, hid, dboth):
    f = hid.shape[1]
    both = jnp.dot(x[...], gate_up, preferred_element_type=F32)
    gg, uu = both[:, :f], both[:, f:]
    dhid = jnp.dot(above[...], down, preferred_element_type=F32)
    gelu, h, square = gelu_parts(gg)
    hid[...] = (gelu * uu).astype(BF16)
    dboth[:, :f] = (dhid * uu * gelu_slope(gelu, h, square)).astype(BF16)
    dboth[:, f:] = (dhid * gelu).astype(BF16)


def grads_compute(x, above, hid, dboth, gate_o, up_o, down_o):
    f = hid.shape[1]
    both = contract_first(x[...], dboth[...]).astype(BF16)
    gate_o[...] = both[:, :f]
    up_o[...] = both[:, f:]
    down_o[...] = contract_first(above[...], hid[...]).astype(BF16)


def mlp_specs(tokens, model, f):
    def rows(width):
        return pl.BlockSpec((tokens // STEPS, width), lambda i: (jnp.minimum(i, STEPS - 1), 0))

    columns = pl.BlockSpec((tokens, model // STEPS), lambda i: (0, jnp.maximum(i - STEPS, 0)))
    grads = pl.BlockSpec((model // STEPS, f), lambda i: (jnp.maximum(i - STEPS, 0), 0))
    return rows, columns, grads


def keep_units(step, hid_all, dboth_all, hid, dboth):
    rows = hid.shape[0]
    at = pl.ds(pl.multiple_of(step * rows, rows), rows)
    hid_all[at] = hid[...]
    dboth_all[at] = dboth[...]


def early_mlp_kernel(
    length, x, above, x_columns, above_columns, gate_up, down, w_in,
    hid, dboth, gate_o, up_o, down_o, w, hid_all, dboth_all, ss, rs
):
    step = pl.program_id(0)
    hops = LineGather(w, length, ss, rs)

    @pl.when(step == 0)
    def _():
        greet(line_neighbours(length))
        if length > 2:
            hops.start(2)

    @pl.when(step == STEPS)
    def _():
        for hop in range(2, length - 1):
            hops.arrive(hop)
            hops.start(hop + 1)

    @pl.when(step < STEPS)
    def _():
        feed_forward(x, above, gate_up[...], down[...], hid, dboth)
        keep_units(step, hid_all, dboth_all, hid, dboth)

    @pl.when(step >= STEPS)
    def _():
        grads_compute(x_columns, above_columns, hid_all, dboth_all, gate_o, up_o, down_o)

    @pl.when(step == 2 * STEPS - 1)
    def _():
        hops.arrive(length - 1)
        hops.finish(2, length - 1)


def early_mlp(x, above, gate_up, down, w, length, collective_id):
    tokens, model = x.shape
    f = down.shape[1]
    rows, columns, grads = mlp_specs(tokens, model, f)
    grad_shape = jax.ShapeDtypeStruct((model, f), BF16)
    return pl.pallas_call(
        functools.partial(early_mlp_kernel, length),
        grid=(2 * STEPS,),
        out_shape=(
            jax.ShapeDtypeStruct((tokens, f), BF16),
            jax.ShapeDtypeStruct((tokens, 2 * f), BF16),
            grad_shape, grad_shape, grad_shape,
            jax.ShapeDtypeStruct(w.shape, w.dtype),
        ),
        in_specs=[rows(model), rows(model), columns, columns, resident(gate_up.shape), resident(down.shape), ANY],
        out_specs=(rows(f), rows(2 * f)) + (grads,) * 3 + (ANY,),
        scratch_shapes=[pltpu.VMEM((tokens, f), BF16), pltpu.VMEM((tokens, 2 * f), BF16)]
        + [DMA((2, length)), DMA((2, length))],
        input_output_aliases={6: 5},
        compiler_params=params(collective_id),
        cost_estimate=pl.CostEstimate(flops=12 * tokens * model * f, bytes_accessed=50 * 2**20, transcendentals=0),
    )(x, above, x, above, gate_up, down, w)


def late_mlp_kernel(
    length, cuts, x, above, x_columns, above_columns, hid_one, dboth_one, gate_up_in, down_in, late_in, *refs
):
    terms, refs = refs[: len(cuts)], refs[len(cuts) :]
    out, back, gate_o, up_o, down_o, sums, squares, *refs = refs
    gate_up, down, hid, dboth, hid_all, dboth_all, load_s, *line_refs = refs
    step = pl.program_id(0)
    line = LineScatter([(ref, *cut) for ref, cut in zip(terms, cuts)], length, *line_refs)
    f, g = hid_one.shape[1], hid.shape[1]
    loads = local_copies(
        (
            (late_in.at[:, pl.ds(0, 2 * g)], gate_up.at[:, pl.ds(2 * f, 2 * g)]),
            (late_in.at[:, pl.ds(2 * g, g)], down.at[:, pl.ds(f, g)]),
            (down_in, down.at[:, pl.ds(0, f)]),
            (gate_up_in, gate_up.at[:, pl.ds(0, 2 * f)]),
        ),
        load_s,
    )

    @pl.when(step == 0)
    def _():
        starts(loads)
        greet(line_neighbours(length))
        line.load((1,))
        line.start()
        line.load((*range(2, length), 0))
        waits(loads)

    for hop in range(2, length):

        @pl.when(step == min(2 * STEPS - 2, 2 * (hop - 1)))
        def _():
            line.next = hop
            line.start()

    @pl.when(step < STEPS)
    def _():
        feed_forward(x, above, gate_up[:, 2 * f :], down[:, f:], hid, dboth)
        keep_units(step, hid_all, dboth_all, hid, dboth)
        units = jnp.concatenate([hid_one[...], hid[...]], axis=1)
        out[...] = contract_last(units, down[...]).astype(BF16)
        units = jnp.concatenate([dboth_one[...], dboth[...]], axis=1)
        back[...] = contract_last(units, gate_up[...]).astype(BF16)

    @pl.when(step >= STEPS)
    def _():
        grads_compute(x_columns, above_columns, hid_all, dboth_all, gate_o, up_o, down_o)

    @pl.when(step == 2 * STEPS - 1)
    def _():
        squares[...] = jnp.zeros_like(squares)
        line.end(sums, 0, squares)


def late_mlp(x, above, early_units, gate_up, down, late, terms, cuts, length, collective_id):
    tokens, model = x.shape
    f, g = down.shape[1], late.shape[1] // 3
    line_rows = terms[0].shape[1]
    cut = sum(columns for _, columns in cuts)
    rows, columns, grads = mlp_specs(tokens, model, g)

    def whole(shape):
        return pl.BlockSpec(shape, lambda i: (0, 0))

    return pl.pallas_call(
        functools.partial(late_mlp_kernel, length, cuts),
        grid=(2 * STEPS,),
        out_shape=(jax.ShapeDtypeStruct((tokens, model), BF16),) * 2
        + (jax.ShapeDtypeStruct((model, g), BF16),) * 3
        + (jax.ShapeDtypeStruct((line_rows, cut), BF16), TILE),
        in_specs=[rows(model), rows(model), columns, columns, rows(f), rows(2 * f)]
        + [ANY] * (3 + len(terms)),
        out_specs=(rows(model),) * 2 + (grads,) * 3 + (whole((line_rows, cut)), whole((8, 128))),
        scratch_shapes=[
            pltpu.VMEM((model, 2 * f + 2 * g), BF16),
            pltpu.VMEM((model, f + g), BF16),
            pltpu.VMEM((tokens // STEPS, g), BF16),
            pltpu.VMEM((tokens // STEPS, 2 * g), BF16),
            pltpu.VMEM((tokens, g), BF16),
            pltpu.VMEM((tokens, 2 * g), BF16),
            DMA((4,)),
        ]
        + line_scratch(length, line_rows, cut, len(cuts)),
        compiler_params=params(collective_id),
        cost_estimate=pl.CostEstimate(
            flops=6 * tokens * model * (f + 3 * g), bytes_accessed=70 * 2**20, transcendentals=0
        ),
    )(x, above, x, above, *early_units, gate_up, down, late, *terms)


def adam_step(weight, grad, first, second, factor, rate, decay_rate):
    clipped = grad * factor
    first_new = beta_first * first + (1.0 - beta_first) * clipped
    second_new = beta_second * second + (1.0 - beta_second) * clipped * clipped
    first_hat = first_new / (1.0 - beta_first**STEP)
    second_hat = second_new / (1.0 - beta_second**STEP)
    weight_new = weight - rate * (
        first_hat / (jnp.sqrt(second_hat) + adam_eps) + decay_rate * weight
    )
    return (first_new, second_new, weight_new)


def small_steps(factor, refs, outs):
    gains_sum, gates_sum, *states = refs
    rows, columns = states[3].shape
    channels = lax.dot_general(
        unit(8).astype(F32), gates_sum[:rows, columns : columns + 8], (((1,), (1,)), ((), ())),
        precision=lax.Precision.HIGHEST, preferred_element_type=F32,
    )
    grads = gains_sum[...], gates_sum[:rows, :columns], channels
    rates = (rate_gains, 0.0), (rate_matrix, decay_matrix), (rate_channel, 0.0)
    for n in range(3):
        w, m, v = states[3 * n : 3 * n + 3]
        results = adam_step(w[...], grads[n], m[...], v[...], factor, *rates[n])
        for out, result in zip(outs[3 * n : 3 * n + 3], results):
            out[...] = result


def adam_kernel(sources, factor, *refs):
    states, refs = refs[: 3 * len(sources)], refs[3 * len(sources) :]
    count = sum(len(source) for source in sources)
    grads, small, refs = refs[:count], refs[count : count + 11], refs[count + 11 :]
    results, norm, outs = refs[:2], refs[2], refs[3:]
    for result, out in zip(results, outs[-3:]):
        out[...] = result[...]
    outs[-1][...] = norm[0:1, 0:1]
    one = factor[0:1, 0:1]
    pl.when(pl.program_id(0) == 0)(lambda: small_steps(one, small, outs[3 * len(sources) : -3]))
    for n, source in enumerate(sources):
        parts = []
        for pieces in source:
            ref, *grads = grads
            for first, columns, at, stride in pieces:
                for t in range(8):
                    parts.append((at + t * stride, columns, ref, t, first))
        parts.sort(key=lambda part: part[0])
        w, m, v = states[3 * n : 3 * n + 3]
        m_o, v_o, w_o = outs[3 * n : 3 * n + 3]
        run = []
        for at, columns, ref, t, first in parts:
            run.append((at, columns, ref[t, :, first : first + columns].astype(F32)))
            end = at + columns
            if end % 128:
                continue
            grad = jnp.concatenate([piece for _, _, piece in run], axis=1) if len(run) > 1 else run[0][2]
            cols = slice(run[0][0], end)
            run = []
            first_new, second_new, weight_new = adam_step(
                w[:, cols], grad, m[:, cols], v[:, cols], one, rate_matrix, decay_matrix
            )
            m_o[:, cols] = first_new
            v_o[:, cols] = second_new
            w_o[:, cols] = weight_new


def adam(matrices, small, factor, norm, passed):
    rows = matrices[0][0].shape[0]
    step = min(rows, 16)

    def block(v):
        return pl.BlockSpec((step, v.shape[1]), lambda i: (i, 0))

    def whole(v):
        return pl.BlockSpec(v.shape, lambda i: (0, 0))

    states = [v for matrix in matrices for v in matrix[:3]]
    grads = [g for matrix in matrices for g in matrix[3]]
    results = [*states, *small[2:], *passed]
    steps = rows // step

    def slab(v):
        return pl.BlockSpec((v.shape[0] // steps, v.shape[1]), lambda i: (i, 0))

    return pl.pallas_call(
        functools.partial(adam_kernel, [matrix[4] for matrix in matrices]),
        grid=(steps,),
        out_shape=tuple(jax.ShapeDtypeStruct(v.shape, v.dtype) for v in results)
        + (jax.ShapeDtypeStruct((1, 1), F32),),
        in_specs=[pl.BlockSpec((8, 128), lambda i: (0, 0))]
        + [block(v) for v in states]
        + [pl.BlockSpec((8, step, g.shape[2]), lambda i: (0, i, 0)) for g in grads]
        + [whole(v) for v in small]
        + [slab(v) for v in passed]
        + [whole(norm)],
        out_specs=tuple(block(v) for v in states)
        + tuple(whole(v) for v in small[2:])
        + tuple(slab(v) for v in passed)
        + (pl.BlockSpec((1, 1), lambda i: (0, 0)),),
        compiler_params=pltpu.CompilerParams(vmem_limit_bytes=VMEM_BYTES),
        cost_estimate=pl.CostEstimate(
            flops=0, bytes_accessed=sum(8 * v.size for v in states), transcendentals=0
        ),
    )(factor, *states, *grads, *small, *passed, norm)


def on_device(
    block_input,
    out_grad,
    norm_gains,
    mixer_weight,
    gate_weight,
    chan_params,
    mlp_weight,
    first_gains,
    first_mixer,
    first_gate,
    first_chan,
    first_mlp,
    second_gains,
    second_mixer,
    second_gate,
    second_chan,
    second_mlp,
):
    length = lax.axis_size("seq") // 2
    z = lax.axis_index("seq") // 2
    tokens, model = block_input.shape[1:]
    share = mixer_weight.shape[0]
    pair = 2 * share
    lru = mixer_weight.shape[1] // 3
    hidden = mlp_weight.shape[1] // 3
    r8, f8 = lru // 8, hidden // 8
    rc = -(-r8 // 128) * 128
    head = gate_weight.shape[1] // 2
    heads = r8 // head
    gate_rows = gate_weight.shape[0]
    gate_pad = -(-gate_rows // 16) * 16

    x = lax.axis_index("seq") - 2 * z
    batch = lax.axis_index("batch")
    plain = pair % 128 == 0

    def turned(v):
        if plain:
            return v
        v = v.reshape(v.shape[0], 4, length, pair).swapaxes(1, 2)
        return jnp.roll(v, -z, axis=1).reshape(v.shape[0], model)

    def turned_back(v):
        if plain:
            return v
        v = jnp.roll(v.reshape(v.shape[0], length, 4, pair), z, axis=1)
        return v.swapaxes(1, 2).reshape(v.shape[0], model)

    normed_one, mixer_full, mlp_gu, mlp_down, late, gains, gate, chan, inputs, above = first(
        turned(block_input[0]),
        turned(out_grad[0]),
        mixer_weight,
        mlp_weight,
        norm_gains,
        gate_weight,
        chan_params,
        rc,
        length,
        1,
    )
    normed_one = normed_one.reshape(8 * tokens, model)
    mixer_full = mixer_full.reshape(model, 3 * r8)
    mixed, *kept, grad_out, mlp_down = recur_forward(
        normed_one, mixer_full, gate, chan, above, mlp_down, length, 2
    )
    grad_out = grad_out.reshape(8 * tokens, model)
    mixed = mixed.reshape(8 * tokens, r8)
    residual, normed_two, mlp_gu, late = middle(mixed, mixer_full, inputs, gains, mlp_gu, late, length, 3)
    normed_two = normed_two.reshape(8 * tokens, model)
    h1 = early(f8)
    h2 = f8 - h1
    mlp_gu = mlp_gu.reshape(model, 2 * h1)
    mlp_down = mlp_down.reshape(model, h1)
    hid, dboth, *early_terms, late = early_mlp(normed_two, grad_out, mlp_gu, mlp_down, late, length, 9)
    gate_one, up_one, down_one = (v.reshape(length, 8 * share, h1) for v in early_terms)
    cut = h1 // 4
    mlp_part, dnormed_two, *late_terms, sums_zero, squares_zero = late_mlp(
        normed_two, grad_out, (hid, dboth), mlp_gu, mlp_down, late.reshape(model, 3 * h2),
        (gate_one, up_one), ((0, h1), (0, cut)), length, 11,
    )
    gate_two, up_two, down_two = (v.reshape(length, 8 * share, h2) for v in late_terms)

    grad_residual, gain_two, dmz, dmix, sums_one, squares_one = turn(
        dnormed_two, residual, above, gains, mixer_full, rc,
        (up_one, down_one, gate_two), ((0, cut, h1 - cut), (1, 0, h1), (2, 0, h2)),
        length, 4,
    )
    dmz = dmz.reshape(8 * tokens, model)
    span = 2 * tokens
    dmix = dmix.reshape(4, span, rc)
    sums_zero, sums_one = (v.reshape(8, share, v.shape[1]) for v in (sums_zero, sums_one))
    dproj, gate_back, sums_two, squares_two, back_zero, back_one = recur_backward(
        dmix, gate, chan, kept, r8, head, (sums_zero, sums_one),
        (up_two, down_two), ((0, 0, h2), (1, 0, h2)), length, 6,
    )
    dproj = dproj.reshape(4 * span, 2 * r8)
    input_grad, gain_one, gates_sum, block_output, back_two, mixer_early, mixer_sums, squares_three = closing(
        normed_one, dmz, dproj, mixed, mixer_full, mlp_part, residual, sums_two,
        inputs, grad_residual, gains, gate_back, length, 7,
    )
    mixer_back, gains_sum, norm, factor = last(
        mixer_sums.reshape(8, share, mixer_sums.shape[1]), gain_one, gain_two, gates_sum,
        (squares_zero, squares_one, squares_two, squares_three), length, 8,
    )
    split = mixer_early.shape[2]
    mlp_sources = (
        [(0, h1, 0, f8), (h1, cut, hidden, f8)],
        [
            (0, h1 - cut, hidden + cut, f8),
            (h1 - cut, h1, 2 * hidden, f8),
            (2 * h1 - cut, h2, h1, f8),
        ],
        [(0, h2, hidden + h1, f8), (h2, h2, 2 * hidden + h1, f8)],
    )
    states = adam(
        (
            (
                mixer_weight, first_mixer, second_mixer, (mixer_early, mixer_back),
                (
                    [(0, r8, 0, r8), (r8, split - r8, lru, r8)],
                    [(0, 2 * r8 - split, lru + split - r8, r8), (2 * r8 - split, r8, 2 * lru, r8)],
                ),
            ),
            (mlp_weight, first_mlp, second_mlp, (back_zero, back_one, back_two), mlp_sources),
        ),
        (
            gains_sum, gates_sum, norm_gains, first_gains, second_gains, gate_weight, first_gate, second_gate,
            chan_params, first_chan, second_chan,
        ),
        factor,
        norm,
        (block_output, input_grad),
    )
    *states, block_output, input_grad, norm = states
    mixer_up, mlp_up, gains_up, gate_up, chan_up = (states[3 * n : 3 * n + 3] for n in range(5))
    return (
        turned_back(block_output)[None],
        turned_back(input_grad)[None],
        norm.reshape(()),
        *gains_up,
        *mixer_up,
        *gate_up,
        *chan_up,
        *mlp_up,
    )


def solution(mesh):
    rows = P(("batch", "seq"), None)
    columns = P(None, ("batch", "seq"))
    data = P("batch", "seq", None)
    weights = (columns, rows, rows, columns, rows)
    in_specs = (data, data) + weights * 3
    triples = tuple(spec for spec in weights for _ in range(3))
    return jax.shard_map(
        on_device,
        mesh=mesh,
        in_specs=in_specs,
        out_specs=(data, data, P()) + triples,
        check_vma=False,
    )
```

```python
import functools
import math

import jax
import jax.numpy as jnp
from jax import lax
from jax.experimental import pallas as pl
from jax.experimental.pallas import tpu as pltpu
from jax.sharding import PartitionSpec as P

STEP = 10
norm_eps = 1e-06
clip_limit = 1.0
beta_first = 0.9
beta_second = 0.999
adam_eps = 1e-08
rate_matrix = 0.05
rate_gains = 0.8
rate_channel = 2.0
decay_matrix = 0.1

MESH = pl.DeviceIdType.MESH
F32 = jnp.float32
BF16 = jnp.bfloat16
ANY = pl.BlockSpec(memory_space=pl.ANY)
VM = pl.BlockSpec(memory_space=pltpu.VMEM)
FLIPS = [(fy, fc, fx) for fy in (0, 1) for fc in (0, 1) for fx in (0, 1) if fy + fc + fx]
GELU_SCALE = math.sqrt(2.0 / math.pi)
GELU_CUBE = 0.044715 * GELU_SCALE


def place():
    b = lax.axis_index("batch")
    s = lax.axis_index("seq")
    y, z = b // 2, s // 2
    return y, b - 2 * y, z, s - 2 * z


def device(y, c, z, x):
    return (y * 2 + c, z * 2 + x)


def rank(y, c, x):
    return (y * 2 + c) * 2 + x


def flip(v, f):
    return 1 - v if f else v


def greet(peers):
    barrier = pltpu.get_barrier_semaphore()
    for peer in peers:
        pl.semaphore_signal(barrier, inc=1, device_id=peer, device_id_type=MESH)
    pl.semaphore_wait(barrier, len(peers))


def remote(src, dst, send, recv, to):
    copy = pltpu.make_async_remote_copy(
        src_ref=src, dst_ref=dst, send_sem=send, recv_sem=recv, device_id=to, device_id_type=MESH
    )
    copy.start()
    return copy


VMEM_BYTES = 63 * 2**20


def params(collective_id):
    return pltpu.CompilerParams(
        collective_id=collective_id, has_side_effects=True, vmem_limit_bytes=VMEM_BYTES
    )


DMA = pltpu.SemaphoreType.DMA


def gather_peers():
    y, c, z, x = place()
    return [device(y, c, z, 1 - x), device(1 - y, c, z, x), device(y, 1 - c, z, x)]


class Gather:
    def __init__(self, a, o, loc, ss, rs):
        y, c, z, x = place()
        self.to_x, self.to_y, self.to_c = gather_peers()
        self.me, self.bx = rank(y, c, x), rank(y, c, 1 - x)
        self.by, self.bd = rank(1 - y, c, x), rank(1 - y, c, 1 - x)
        half = a.shape[0] // 2
        self.lo, self.hi = pl.ds(0, half), pl.ds(half, half)
        self.a, self.o, self.loc, self.ss, self.rs = a, o, loc, ss, rs
        self.done, self.last = [], []

    def send(self, src, dst, k, to):
        copy = remote(src, dst, self.ss.at[k], self.rs.at[k], to)
        self.done.append(copy)
        return copy

    def relay(self, block, part, k, to):
        return self.send(self.o.at[block, part], self.o.at[block, part], k, to)

    def begin_half(self, half):
        a, o, me = self.a, self.o, self.me
        part = (self.lo, self.hi)[half]
        if half == 0:
            self.s0 = self.send(a.at[part], o.at[me, part], 0, self.to_x)
            self.s3 = self.send(a.at[part], o.at[me, part], 3, self.to_y)
        else:
            self.s1 = self.send(a.at[part], o.at[me, part], 1, self.to_y)
            self.s2 = self.send(a.at[part], o.at[me, part], 2, self.to_x)
        self.last.append(self.send(a.at[part], o.at[me, part], (4, 13)[half], self.to_c))
        if half == 1:
            self.own = pltpu.make_async_copy(a, o.at[me], self.loc)
            self.own.start()

    def begin(self):
        a, o, me, lo, hi = self.a, self.o, self.me, self.lo, self.hi
        self.s0 = self.send(a.at[lo], o.at[me, lo], 0, self.to_x)
        self.s1 = self.send(a.at[hi], o.at[me, hi], 1, self.to_y)
        self.s2 = self.send(a.at[hi], o.at[me, hi], 2, self.to_x)
        self.s3 = self.send(a.at[lo], o.at[me, lo], 3, self.to_y)
        self.last += [self.send(a.at[part], o.at[me, part], k, self.to_c) for part, k in ((lo, 4), (hi, 13))]
        self.own = pltpu.make_async_copy(a, o.at[me], self.loc)
        self.own.start()

    def middle(self):
        self.s0.wait_recv()
        self.s5 = self.relay(self.bx, self.lo, 5, self.to_y)
        self.last.append(self.relay(self.bx, self.lo, 7, self.to_c))
        self.s1.wait_recv()
        self.s6 = self.relay(self.by, self.hi, 6, self.to_x)
        self.last.append(self.relay(self.by, self.hi, 8, self.to_c))

    def relays(self, mark=lambda: None):
        self.s2.wait_recv()
        self.last.append(self.relay(self.bx, self.hi, 9, self.to_c))
        self.s3.wait_recv()
        self.last.append(self.relay(self.by, self.lo, 10, self.to_c))
        mark()
        self.s5.wait_recv()
        self.last.append(self.relay(self.bd, self.lo, 11, self.to_c))
        self.s6.wait_recv()
        self.last.append(self.relay(self.bd, self.hi, 12, self.to_c))

    def finish(self, skip=0, own=True):
        for copy in self.last[skip:]:
            copy.wait_recv()
        for copy in self.done:
            copy.wait_send()
        if own:
            self.own.wait()

    def end(self, mark=lambda: None):
        self.relays(mark)
        self.finish()


def scatter_steps(p, o, mine, sib, part, got, loc, ss, rs, prepare=None):
    y, c, z, x = place()
    to_x, to_y, to_c = gather_peers()
    half = o.shape[0] // 2
    step = 16
    cut = (pl.ds(0, half), pl.ds(half, half))
    where = ((1 - y, 1 - x), (1 - y, x), (y, 1 - x), (y, x))
    order = [(0, 0), (0, 1), (1, 0), (2, 1), (2, 0), (1, 1), (3, 0), (3, 1)]
    from_c, own, sends = {}, {}, []
    for n, (t, h) in enumerate(order):
        ty, tx = where[t]
        if mine is not None and prepare and all(key[0] != t for key in own):
            prepare(rank(ty, c, tx))
            prepare(rank(ty, 1 - c, tx))
        if mine is None:
            own[t, h] = None
        else:
            own[t, h] = pltpu.make_async_copy(
                p.at[rank(ty, c, tx), cut[h]], mine.at[t, h], loc.at[n]
            )
            own[t, h].start()
        from_c[t, h] = remote(
            p.at[rank(ty, 1 - c, tx), cut[h]], sib.at[t, h], ss.at[n], rs.at[n], to_c
        )
        sends.append(from_c[t, h])
    yield "begun"

    def own_ref(t, h):
        return p.at[rank(where[t][0], c, where[t][1]), cut[h]] if mine is None else mine.at[t, h]

    pieces = ((0, 0), (0, 1), (1, 0), (2, 1), (2, 0), (1, 1))

    def part_ref(k):
        return own_ref(*pieces[k]) if part is None else part.at[k]

    def add(dst, t, h, extra):
        if own[t, h] is not None:
            own[t, h].wait()
        term = own_ref(t, h)
        from_c[t, h].wait_recv()

        @pl.loop(0, half // step)
        def _(i):
            at = pl.ds(pl.multiple_of(i * step, step), step)
            total = term[at].astype(F32) + sib[t, h, at].astype(F32)
            for ref in extra:
                total = total + ref[at].astype(F32)
            dst[at] = total.astype(dst.dtype)

    def send(k, slot, to):
        copy = remote(part_ref(k), got.at[slot], ss.at[8 + k], rs.at[8 + slot], to)
        sends.append(copy)
        return copy

    def arrival(slot):
        return pltpu.make_async_remote_copy(
            src_ref=got.at[slot], dst_ref=got.at[slot], send_sem=ss.at[8], recv_sem=rs.at[8 + slot],
            device_id=to_x, device_id_type=MESH,
        )

    add(part_ref(0), 0, 0, ())
    send(0, 1, to_y)
    add(part_ref(1), 0, 1, ())
    send(1, 3, to_x)
    add(part_ref(2), 1, 0, ())
    send(2, 0, to_y)
    add(part_ref(3), 2, 1, ())
    send(3, 2, to_x)
    yield "sent"
    arrival(1).wait_recv()
    add(part_ref(4), 2, 0, (got.at[1],))
    send(4, 4, to_x)
    yield "early"
    arrival(3).wait_recv()
    add(part_ref(5), 1, 1, (got.at[3],))
    send(5, 5, to_y)
    yield "late"
    arrival(0).wait_recv()
    arrival(4).wait_recv()
    add(o.at[cut[0]], 3, 0, (got.at[0], got.at[4]))
    yield "low half"
    arrival(2).wait_recv()
    arrival(5).wait_recv()
    add(o.at[cut[1]], 3, 1, (got.at[2], got.at[5]))
    yield "high half"
    for copy in sends:
        copy.wait_send()


def scatter_scratch(half, width):
    return [
        pltpu.VMEM((4, 2, half, width), BF16),
        pltpu.VMEM((4, 2, half, width), BF16),
        pltpu.VMEM((6, half, width), BF16),
        pltpu.VMEM((6, half, width), BF16),
        DMA((8,)),
        DMA((14,)),
        DMA((14,)),
    ]


def exchange_steps(a, o, loc, ss, rs):
    y, c, z, x = place()
    me = rank(y, c, x)
    dst = o.at[me]
    rows = o.shape[1]

    def block(t):
        if len(a.shape) == 3:
            return a.at[t]
        return a.at[pl.ds(pl.multiple_of(t * rows, rows), rows)]

    copies = []
    for n, (fy, fc, fx) in enumerate(FLIPS):
        ty, tc, tx = flip(y, fy), flip(c, fc), flip(x, fx)
        copies.append(remote(block(rank(ty, tc, tx)), dst, ss.at[n], rs.at[n], device(ty, tc, z, tx)))
    own = pltpu.make_async_copy(block(me), dst, loc)
    own.start()
    return copies, own


def plane_peers():
    y, c, z, x = place()
    return [device(flip(y, fy), flip(c, fc), z, flip(x, fx)) for fy, fc, fx in FLIPS]


def line_peers(length):
    y, c, z, x = place()
    return [device(y, c, lax.rem(z + k, length), x) for k in range(1, length)]


class LineGather:
    def __init__(self, buf, length, ss, rs):
        y, c, z, x = place()
        self.z, self.length, self.buf, self.ss, self.rs = z, length, buf, ss, rs
        self.up = device(y, c, lax.rem(z + 1, length), x)
        self.down = device(y, c, lax.rem(z + length - 1, length), x)

    def copy(self, hop, upward):
        length, buf = self.length, self.buf
        src, dst = ((length - hop + 1) % length, length - hop) if upward else (hop - 1, hop)
        way = 0 if upward else 1
        return pltpu.make_async_remote_copy(
            src_ref=buf.at[src], dst_ref=buf.at[dst], send_sem=self.ss.at[way, hop - 1],
            recv_sem=self.rs.at[way, hop - 1], device_id=self.up if upward else self.down,
            device_id_type=MESH,
        )

    def sends(self, hop, act):
        z, length = self.z, self.length

        @pl.when(jnp.logical_and(z + 1 < length, z >= hop - 1))
        def _():
            act(self.copy(hop, True))

        @pl.when(jnp.logical_and(z >= 1, z + hop - 1 < length))
        def _():
            act(self.copy(hop, False))

    def start(self, hop):
        self.sends(hop, lambda copy: copy.start())

    def start_piece(self, n):
        for way, last, dst in ((0, self.z + 1 < self.length, self.length - 1), (1, self.z >= 1, 1)):

            @pl.when(last)
            def _():
                remote(
                    self.buf.at[0, n], self.buf.at[dst, n], self.ss.at[way, 0], self.rs.at[way, 0],
                    (self.up, self.down)[way],
                )

    def arrive(self, hop):
        z, length = self.z, self.length

        @pl.when(z >= hop)
        def _():
            self.copy(hop, True).wait_recv()

        @pl.when(z + hop < length)
        def _():
            self.copy(hop, False).wait_recv()

    def finish(self, first_hop=1, last_hop=None):
        for hop in range(first_hop, (last_hop or self.length - 1) + 1):
            self.sends(hop, lambda copy: copy.wait_send())


class LineScatter:
    def __init__(self, sources, length, total, up_mine, down_mine, up_got, down_got, loc, ss, rs):
        y, c, z, x = place()
        self.sources, self.length, self.total = sources, length, total
        self.mine, self.got = (up_mine, down_mine), (up_got, down_got)
        self.loc, self.ss, self.rs = loc, ss, rs
        self.to = (device(y, c, lax.rem(z + 1, length), x), device(y, c, lax.rem(z + length - 1, length), x))
        self.far = (z, length - 1 - z)
        self.next = 1

    def loads(self, way, hop):
        k = 0 if hop == 0 else self.length - hop if way == 0 else hop
        copies, at = [], 0
        for n, (ref, first, columns) in enumerate(self.sources):
            dst = self.term(way, hop) if hop else self.total
            copies.append(
                pltpu.make_async_copy(
                    ref.at[k, :, pl.ds(first, columns)], dst.at[:, pl.ds(at, columns)],
                    self.loc.at[way, hop, n],
                )
            )
            at += columns
        return copies

    def term(self, way, hop):
        return self.mine[way].at[hop - 1]

    def copy(self, way, hop):
        return pltpu.make_async_remote_copy(
            src_ref=self.term(way, hop), dst_ref=self.got[way].at[hop - 1],
            send_sem=self.ss.at[way, hop - 1], recv_sem=self.rs.at[way, hop - 1],
            device_id=self.to[way], device_id_type=MESH,
        )

    def load(self, hops):
        for hop in hops:
            for way in (0, 1) if hop else (0,):
                for copy in self.loads(way, hop):
                    copy.start()

    def start(self):
        hop = self.next
        if hop >= self.length:
            return
        self.next += 1
        for way in (0, 1):
            far = self.far[way]
            for copy in self.loads(way, hop):
                copy.wait()
            if hop > 1:

                @pl.when(jnp.logical_and(far >= 1, far <= hop - 1))
                def _():
                    self.copy(way, hop - 1).wait_recv()
                    dst, src = self.term(way, hop), self.got[way].at[hop - 2]

                    def add(at):
                        dst[at] = dst[at] + src[at]

                    rows_loop(dst.shape[0], add, unroll=4)

            @pl.when(far <= hop - 1)
            def _():
                self.copy(way, hop).start()

    def end(self, result, first_column, squares):
        last = self.length - 1
        for copy in self.loads(0, 0):
            copy.wait()
        columns = pl.ds(first_column, self.total.shape[1])

        def finish(ways):
            for way in ways:
                self.copy(way, last).wait_recv()

            def add(at):
                total = self.total[at].astype(F32)
                for way in ways:
                    total = total + self.got[way][last - 1, at].astype(F32)
                result[at, columns] = total.astype(result.dtype)
                squares[...] += tile_of_squares(total)

            rows_loop(result.shape[0], add)

        above, below = self.far[0] >= 1, self.far[1] >= 1
        pl.when(jnp.logical_and(above, below))(lambda: finish((0, 1)))
        pl.when(jnp.logical_not(above))(lambda: finish((1,)))
        pl.when(jnp.logical_not(below))(lambda: finish((0,)))
        for hop in range(1, self.length):
            for way in (0, 1):

                @pl.when(self.far[way] <= hop - 1)
                def _():
                    self.copy(way, hop).wait_send()


class HeldLine(LineScatter):
    def __init__(self, g, first_column, up_got, down_got, ss, rs):
        y, c, z, x = place()
        self.length = length = g.shape[0]
        self.columns = pl.ds(first_column, up_got.shape[2])
        self.sources, self.g, self.total = (), g, g.at[0, :, self.columns]
        self.got, self.ss, self.rs = (up_got, down_got), ss, rs
        self.to = line_neighbours(length)
        self.far = (z, length - 1 - z)
        self.next = 1

    def term(self, way, hop):
        return self.g.at[self.length - hop if way == 0 else hop, :, self.columns]


def chains_of(cuts):
    whole = sum(cut[2] for cut in cuts)
    left = -(-whole // 256) * 128
    lists = [], []
    for which, first_column, columns in cuts:
        taken = min(columns, left)
        if taken:
            lists[0].append((which, first_column, taken))
        if columns > taken:
            lists[1].append((which, first_column + taken, columns - taken))
        left -= taken
    return lists


class Lines:
    def __init__(self, terms, cuts, length, refs):
        self.chains, self.length = [], length
        for n, cut in enumerate(chains_of(cuts)):
            sources = [(terms[which], first_column, columns) for which, first_column, columns in cut]
            self.chains.append(
                LineScatter(sources, length, *refs[n * LINE_REFS : (n + 1) * LINE_REFS])
            )
        self.queue = [chain for _ in range(1, length) for chain in self.chains]

    def begin(self):
        for chain in self.chains:
            chain.load((1,))
        self.start()
        self.start()
        for chain in self.chains:
            chain.load((*range(2, self.length), 0))

    def start(self):
        if self.queue:
            self.queue.pop(0).start()

    def end(self, result, squares):
        while self.queue:
            self.start()
        squares[...] = jnp.zeros_like(squares)
        at = 0
        for chain in self.chains:
            chain.end(result, at, squares)
            at += chain.total.shape[1]


def lines_scratch(length, rows, cuts):
    return sum(
        (line_scratch(length, rows, sum(cut[2] for cut in chain), len(chain)) for chain in chains_of(cuts)), []
    )


def fold(v):
    return jnp.sum(v.reshape(v.shape[0] // 8, 8, v.shape[1]), axis=0)


def tile_of_squares(v):
    v = fold(v * v)
    part = v[:, :128]
    for n in range(1, v.shape[1] // 128):
        part = part + v[:, n * 128 : (n + 1) * 128]
    if v.shape[1] % 128:
        rest = v[:, v.shape[1] // 128 * 128 :]
        part = part + jnp.concatenate([rest, jnp.zeros((8, 128 - rest.shape[1]), F32)], axis=1)
    return part


def line_scratch(length, rows, columns, sources):
    slots = pltpu.VMEM((length - 1, rows, columns), BF16)
    return [pltpu.VMEM((rows, columns), BF16)] + [slots] * 4 + [
        DMA((2, length, sources)), DMA((2, length)), DMA((2, length))
    ]


def starts(copies):
    for copy in copies:
        copy.start()
    return copies


def waits(copies):
    for copy in copies:
        copy.wait()


def local_copies(pairs, sems):
    return [pltpu.make_async_copy(src, dst, sems.at[n]) for n, (src, dst) in enumerate(pairs)]


def held(*arrays):
    return [pltpu.VMEM(v.shape, v.dtype) for v in arrays]


LINE_REFS = 8
SCATTER_REFS = 7
TILE = jax.ShapeDtypeStruct((8, 128), F32)


def line_neighbours(length):
    y, c, z, x = place()
    return [device(y, c, lax.rem(z + 1, length), x), device(y, c, lax.rem(z + length - 1, length), x)]


def rows_loop(rows, body, start=0, unroll=2):
    @pl.loop(start // 16, (start + rows) // 16, unroll=unroll)
    def _(i):
        body(pl.ds(pl.multiple_of(i * 16, 16), 16))


def turned_tiles(length, pair):
    _, _, z, _ = place()
    for k in range(length):
        for b in range(4):
            yield k * 4 + b, pl.multiple_of((b * length + lax.rem(z + k, length)) * pair, pair)


def load_turned(ref, at, length, pair):
    if pair % 128:
        return ref[at]
    return jnp.concatenate([ref[at, pl.ds(src, pair)] for _, src in turned_tiles(length, pair)], axis=1)


def store_turned(ref, at, value, length, pair):
    if pair % 128:
        ref[at] = value
        return
    for n, dst in turned_tiles(length, pair):
        ref[at, pl.ds(dst, pair)] = value[:, n * pair : (n + 1) * pair]


def inverse_rms(v):
    return lax.rsqrt(jnp.sum(v * v, axis=-1, keepdims=True) * (1.0 / v.shape[-1]) + norm_eps)


def norm_rows_back(v, gain, grad):
    inverse = inverse_rms(v)
    scaled = v * inverse
    moved = grad * gain
    inner = jnp.sum(moved * scaled, axis=-1, keepdims=True) * (1.0 / v.shape[-1])
    return inverse * (moved - scaled * inner), fold(grad * scaled)


def middle_kernel(length, mixed_in, mixer_in, inputs_in, gains_in, w_in, late_in, residual_o, normed_o, w, late, *scratch):
    scatter_refs, (p, low, loc, gs, gr, hs, hr, late_s, late_r, *scratch) = scratch[:SCATTER_REFS], scratch[SCATTER_REFS:]
    mixed, mixer, inputs, gains, residual, load_s, keep_s = scratch
    loads = starts(
        local_copies(
            ((mixed_in, mixed), (mixer_in, mixer), (inputs_in, inputs), (gains_in, gains)), load_s
        )
    )
    greet(gather_peers() + line_neighbours(length))
    hops = LineGather(w, length, hs, hr)
    hops.start(1)
    late_hops = LineGather(late, length, late_s, late_r)
    late_hops.start(1)
    started = [1]
    part = mixed.shape[1]
    rows, width = low.shape

    waits(loads[:2])

    def prepare(i):
        mine = mixed[pl.ds(pl.multiple_of(i * rows, rows), rows)]
        p[i] = contract_last(mine, mixer[:, 2 * part :]).astype(BF16)

    def advance():
        if started[0] < length - 1:
            hops.arrive(started[0])
            started[0] += 1
            hops.start(started[0])

    def body(at):
        v = inputs[at].astype(F32) + residual[at]
        residual[at] = v
        low[at] = (v * inverse_rms(v) * gains[1:2]).astype(BF16)

    half = low.shape[0] // 2
    gather = Gather(low, normed_o, loc, gs, gr)
    for name in scatter_steps(p, residual, *scatter_refs, prepare=prepare):
        if name == "late":
            advance()
        if name == "low half":
            waits(loads[2:])
            rows_loop(half, body)
            gather.begin_half(0)
        if name == "high half":
            rows_loop(half, body, half)
            gather.begin_half(1)
    keeps = starts(local_copies(((residual, residual_o),), keep_s))
    gather.middle()
    advance()
    gather.end()
    waits(keeps)
    while started[0] < length - 1:
        advance()
    hops.arrive(length - 1)
    hops.finish()
    late_hops.arrive(1)
    late_hops.finish(1, 1)


def middle(mixed, mixer, inputs, gains, w, late, length, collective_id):
    rows, width = inputs.shape
    return pl.pallas_call(
        functools.partial(middle_kernel, length),
        out_shape=(
            jax.ShapeDtypeStruct((rows, width), F32),
            jax.ShapeDtypeStruct((8, rows, width), BF16),
            jax.ShapeDtypeStruct(w.shape, w.dtype),
            jax.ShapeDtypeStruct(late.shape, late.dtype),
        ),
        in_specs=[ANY] * 6,
        out_specs=(ANY,) * 4,
        scratch_shapes=scatter_scratch(rows // 2, width)
        + [pltpu.VMEM((8, rows, width), BF16), pltpu.VMEM((rows, width), BF16), DMA, DMA((14,)), DMA((14,))]
        + [DMA((2, length))] * 4
        + held(mixed, mixer, inputs, gains)
        + [pltpu.VMEM((rows, width), F32), DMA((4,)), DMA((1,))],
        input_output_aliases={4: 2, 5: 3},
        compiler_params=params(collective_id),
        cost_estimate=pl.CostEstimate(flops=0, bytes_accessed=300 * 2**20, transcendentals=0),
    )(mixed, mixer, inputs, gains, w, late)


def turn_kernel(length, cuts, p, residual_in, above_in, gains_in, mixer_in, *refs):
    parts = 1 + max(cut[0] for cut in cuts)
    terms, refs = refs[:parts], refs[parts:]
    back_o, gain, low_o, dmix_o, sums, squares, *scratch = refs
    scatter_refs, scratch = scratch[:SCATTER_REFS], scratch[SCATTER_REFS:]
    total, low, loc, gs, gr, parts_in, load_s, residual, above, gains, mixer, back, dmix, in_s, keep_s = scratch[:15]
    line_refs = scratch[15:]
    loads = local_copies(
        ((residual_in, residual), (above_in, above), (gains_in, gains), (mixer_in, mixer)), in_s
    )
    greet(gather_peers() + line_neighbours(length))
    line = Lines(terms, cuts, length, line_refs)
    line.begin()
    starts(loads)
    gain[...] = jnp.zeros_like(gain)

    def body(at):
        grad, gain_part = norm_rows_back(residual[at], gains[1:2], total[at])
        grad = above[at].astype(F32) + grad
        back[at] = grad
        low[at] = grad.astype(BF16)
        gain[...] += gain_part

    half = low.shape[0] // 2
    gather = Gather(low, low_o, loc, gs, gr)
    for name in scatter_steps(p, total, *scatter_refs):
        if name in ("early", "late"):
            line.start()
        if name == "low half":
            waits(loads)
            rows_loop(half, body)
            gather.begin_half(0)
        if name == "high half":
            rows_loop(half, body, half)
            gather.begin_half(1)
            line.start()
    keeps = starts(local_copies(((back, back_o),), keep_s))
    rows = low.shape[0]
    part = mixer.shape[1] // 3
    y, c, z, x = place()
    near = (gather.me, gather.bx), (gather.by, rank(y, 1 - c, x))
    rest = (gather.bd, rank(1 - y, 1 - c, x)), (rank(y, 1 - c, 1 - x), rank(1 - y, 1 - c, 1 - x))

    def fetch(blocks, slot):
        copies = []
        for n in (0, 1):
            copies.append(
                pltpu.make_async_copy(low_o.at[blocks[n]], parts_in.at[slot, n], load_s.at[slot, n])
            )
        return copies

    def mix(blocks, slot):
        waits(fetch(blocks, slot))
        lines = parts_in[slot].reshape(2 * rows, parts_in.shape[3])
        both = jnp.dot(lines, mixer[:, 2 * part :], preferred_element_type=F32)
        none = jnp.zeros((rows, dmix.shape[2] - part), F32)
        for n in (0, 1):
            dmix[blocks[n]] = jnp.concatenate([both[n * rows : (n + 1) * rows], none], axis=1)
            pltpu.make_async_copy(dmix.at[blocks[n]], dmix_o.at[blocks[n]], keep_s.at[1 + n + 2 * slot]).start()

    def mixed(blocks, slot):
        for n in (0, 1):
            pltpu.make_async_copy(dmix.at[blocks[n]], dmix_o.at[blocks[n]], keep_s.at[1 + n + 2 * slot]).wait()

    def near_blocks():
        gather.own.wait()
        for copy in gather.last[:2]:
            copy.wait_recv()
        starts(fetch(near[0], 0))
        starts(fetch(near[1], 1))
        mix(near[0], 0)
        mix(near[1], 1)

    gather.middle()
    line.start()
    gather.relays(near_blocks)
    gather.finish(2, own=False)
    for n in (0, 1):
        mixed(near[n], n)
        starts(fetch(rest[n], n))
    for n in (0, 1):
        mix(rest[n], n)
    waits(keeps)
    line.end(sums, squares)
    for n in (0, 1):
        mixed(rest[n], n)


def turn(p, residual, above, gains, mixer, rc, terms, cuts, length, collective_id):
    rows, width = residual.shape
    line_rows, columns = terms[0].shape[1], sum(cut[2] for cut in cuts)
    return pl.pallas_call(
        functools.partial(turn_kernel, length, cuts),
        out_shape=(
            jax.ShapeDtypeStruct((rows, width), F32),
            jax.ShapeDtypeStruct((8, width), F32),
            jax.ShapeDtypeStruct((8, rows, width), BF16),
            jax.ShapeDtypeStruct((8, rows, rc), F32),
            jax.ShapeDtypeStruct((line_rows, columns), BF16),
            TILE,
        ),
        in_specs=[ANY] * (5 + len(terms)),
        out_specs=(ANY, VM, ANY, ANY, VM, VM),
        scratch_shapes=scatter_scratch(rows // 2, width)
        + [pltpu.VMEM((rows, width), F32), pltpu.VMEM((rows, width), BF16), DMA, DMA((14,)), DMA((14,))]
        + [pltpu.VMEM((2, 2, rows, width), BF16), DMA((2, 2))]
        + held(residual, above, gains, mixer)
        + [pltpu.VMEM((rows, width), F32), pltpu.VMEM((8, rows, rc), F32), DMA((4,)), DMA((5,))]
        + lines_scratch(length, line_rows, cuts),
        compiler_params=params(collective_id),
        cost_estimate=pl.CostEstimate(flops=0, bytes_accessed=300 * 2**20, transcendentals=0),
    )(p.reshape(8, rows, width), residual, above, gains, mixer, *terms)


def closing_kernel(
    length, x_in, dmz_in, dproj_in, mixed_in, mixer_in, q, residual_in, block, inputs_in, above_in, gains_in, gp_in,
    grad_out, gain, gates_o, out_out, e_o, sums, squares,
    x_part, dmz_part, g, back, total, o, up_a, down_a, up_b, down_b, gp_got, gp_sum,
    ls, lr, load_s, loc, es, er, gate_s, gate_r, move_s, move_r,
    dproj, mixed, mixer, residual, inputs, above, gains, gp, in_s, keep_s,
    mine, sib_q, got_q, loc_q, ss_q, rs_q, sib_p, got_p, ss_p, rs_p,
):
    inflow = starts(
        local_copies(
            (
                (gp_in, gp), (dproj_in, dproj), (mixed_in, mixed), (mixer_in, mixer), (residual_in, residual),
                (inputs_in, inputs), (above_in, above), (gains_in, gains),
            ),
            in_s,
        )
    )
    y, c, z, x = place()
    others = line_peers(length)
    s = 2 * z + x
    owner = x * length + z
    to_z = owner // 2
    to_x = owner - 2 * to_z
    from_z, from_x = lax.rem(s, length), s // length
    moves = jnp.where(jnp.logical_and(to_z == z, to_x == x), 0, 1)
    barrier = pltpu.get_barrier_semaphore()
    for peer in others + plane_peers():
        pl.semaphore_signal(barrier, inc=1, device_id=peer, device_id_type=MESH)

    @pl.when(moves == 1)
    def _():
        pl.semaphore_signal(barrier, inc=1, device_id=device(y, c, to_z, to_x), device_id_type=MESH)
        pl.semaphore_signal(barrier, inc=1, device_id=device(y, c, from_z, from_x), device_id_type=MESH)

    pl.semaphore_wait(barrier, len(others) + 7 + 2 * moves)
    model = mixer.shape[0]
    tokens = dproj.shape[0]
    part = mixed.shape[1]
    columns = x_part.shape[2]
    steps = model // columns
    rows, width = residual.shape
    half = rows // 2
    line_rows = g.shape[1]

    def loads(i, slot):
        at = pl.ds(pl.multiple_of(i * columns, columns), columns)
        return (
            pltpu.make_async_copy(x_in.at[:, at], x_part.at[slot], load_s.at[0, slot]),
            pltpu.make_async_copy(dmz_in.at[:, at], dmz_part.at[slot], load_s.at[1, slot]),
        )

    group = steps // 4
    order = (3, 1, 2, 0)

    def fetch(i, slot):
        for copy in loads(i, slot):
            copy.start()

    fetch(order[0] * group, 0)
    inflow[0].wait()
    gate = [
        remote(gp.at[lax.rem(z + k + 1, length)], gp_got.at[k], gate_s.at[k], gate_r.at[k], others[k])
        for k in range(length - 1)
    ]
    split = up_a.shape[2]
    line_a = HeldLine(g, 0, up_a, down_a, ls.at[0], lr.at[0])
    line_b = HeldLine(g, split, up_b, down_b, ls.at[1], lr.at[1])
    queue = [chain for _ in range(1, length) for chain in (line_a, line_b)]

    def advance(times=1):
        for _ in range(times):
            if queue:
                queue.pop(0).start()

    output = scatter_steps(q, total, mine, sib_q, None, got_q, loc_q, ss_q, rs_q)
    next(output)
    copies, own = exchange_steps(block, e_o, loc, es, er)

    def compute(n, start=0, stop=None):
        @pl.loop(start, group if stop is None else stop)
        def _(j):
            count = n * group + j
            slot = count - count // 2 * 2
            i = order[n] * group + j

            @pl.when(j + 1 < group)
            def _():
                fetch(i + 1, 1 - slot)

            if n < 3:

                @pl.when(j + 1 == group)
                def _():
                    fetch(order[n + 1] * group, 1 - slot)

            for copy in loads(i, slot):
                copy.wait()
            front = contract_first(x_part[slot], dproj[...])
            tail = contract_first(dmz_part[slot], mixed[...])
            k = i * columns // line_rows
            at = pl.ds(pl.multiple_of(i * columns - k * line_rows, columns), columns)
            g[k, at] = jnp.concatenate([front, tail], axis=1).astype(BF16)

    waits(inflow[1:4])
    compute(0, 0, group // 2)
    next(output)
    compute(0, group // 2)
    compute(1)
    if length == 4:
        advance(2)
    next(output)

    @pl.loop(0, 8)
    def _(i):
        lines = dproj[pl.ds(pl.multiple_of(i * rows, rows), rows)]
        back[i] = contract_last(lines, mixer[:, : 2 * part]).astype(BF16)

    incoming = scatter_steps(back, o, None, sib_p, None, got_p, None, ss_p, rs_p)
    next(incoming)
    next(output)
    next(incoming)
    compute(2)
    advance(1 if length == 4 else 0)
    for _ in output:
        pass
    next(incoming)
    compute(3)
    advance(1 if length == 4 else 2)
    pair = width // (4 * length)
    waits(inflow[4:])
    keeps = []
    for n in (0, 1):

        def finish_output(at):
            whole = pl.ds(pl.multiple_of(at.start + n * half, 16), 16)
            store_turned(mine.at[0, n], at, (residual[whole] + total[whole]).astype(BF16), length, pair)

        rows_loop(half, finish_output)
        keeps.append(
            pltpu.make_async_copy(mine.at[0, n], out_out.at[pl.ds(n * half, half)], keep_s.at[n])
        )
        keeps[n].start()
    keeps.append(pltpu.make_async_copy(above, grad_out, keep_s.at[2]))
    advance()
    for copy in gate:
        copy.wait()
    rows_sum = gp[z]
    for k in range(length - 1):
        rows_sum = rows_sum + gp_got[k]
    gp_sum[...] = rows_sum
    move = pltpu.make_async_remote_copy(
        src_ref=gp_sum, dst_ref=gates_o, send_sem=move_s, recv_sem=move_r,
        device_id=device(y, c, to_z, to_x), device_id_type=MESH,
    )
    pl.when(moves == 1)(lambda: move.start())

    @pl.when(moves == 0)
    def _():
        gates_o[...] = rows_sum

    gain[...] = jnp.zeros_like(gain)

    def finish_grad(at):
        grad, gain_part = norm_rows_back(inputs[at].astype(F32), gains[0:1], o[at])
        store_turned(above, at, above[at] + grad, length, pair)
        gain[...] += gain_part

    for name in incoming:
        if name == "late":
            advance()
        if name == "low half":
            rows_loop(half, finish_grad)
        if name == "high half":
            rows_loop(half, finish_grad, half)
            keeps[2].start()
    while queue:
        advance()
    squares[...] = jnp.zeros_like(squares)
    line_a.end(sums, 0, squares)
    line_b.end(sums, split, squares)
    pl.when(moves == 1)(lambda: move.wait())
    waits(keeps)
    waits(copies)
    own.wait()


def closing(x, dmz, dproj, mixed, mixer, q, residual, block, inputs, above, gains, gp, length, collective_id):
    rows, width = residual.shape
    tokens, model = x.shape
    part = mixed.shape[1]
    share = block.shape[0] // 8
    block = block.reshape(8, share, block.shape[1])
    line_rows = model // length
    columns = min(256, line_rows)
    split = -(-3 * part // 256) * 128
    slots_a, slots_b = (pltpu.VMEM((length - 1, line_rows, n), BF16) for n in (split, 3 * part - split))
    pack = gp.shape[1:]
    return pl.pallas_call(
        functools.partial(closing_kernel, length),
        out_shape=(
            jax.ShapeDtypeStruct((rows, width), F32),
            jax.ShapeDtypeStruct((8, width), F32),
            jax.ShapeDtypeStruct(pack, F32),
            jax.ShapeDtypeStruct((rows, width), BF16),
            jax.ShapeDtypeStruct(block.shape, BF16),
            jax.ShapeDtypeStruct((line_rows, 3 * part), BF16),
            TILE,
        ),
        in_specs=[ANY] * 12,
        out_specs=(ANY, VM, VM, ANY, ANY, VM, VM),
        scratch_shapes=[
            pltpu.VMEM((2, tokens, columns), BF16),
            pltpu.VMEM((2, tokens, columns), BF16),
            pltpu.VMEM((length, line_rows, 3 * part), BF16),
            pltpu.VMEM((8, rows, width), BF16),
            pltpu.VMEM((rows, width), F32),
            pltpu.VMEM((rows, width), F32),
            slots_a, slots_a, slots_b, slots_b,
            pltpu.VMEM((length - 1,) + pack, F32),
            pltpu.VMEM(pack, F32),
            DMA((2, 2, length)), DMA((2, 2, length)), DMA((2, 2)),
            DMA, DMA((7,)), DMA((7,)), DMA((length,)), DMA((length,)), DMA, DMA,
            *held(dproj, mixed, mixer, residual, inputs, above, gains, gp),
            DMA((8,)), DMA((3,)),
            pltpu.VMEM((4, 2, rows // 2, width), BF16),
            pltpu.VMEM((4, 2, rows // 2, width), BF16),
            pltpu.VMEM((6, rows // 2, width), BF16),
            DMA((8,)), DMA((14,)), DMA((14,)),
            pltpu.VMEM((4, 2, rows // 2, width), BF16),
            pltpu.VMEM((6, rows // 2, width), BF16),
            DMA((14,)), DMA((14,)),
        ],
        compiler_params=params(collective_id),
        cost_estimate=pl.CostEstimate(
            flops=10 * tokens * model * dproj.shape[1] // 2, bytes_accessed=350 * 2**20, transcendentals=0
        ),
    )(x, dmz, dproj, mixed, mixer, q.reshape(8, rows, width), residual, block, inputs, above, gains, gp)


def first_kernel(
    length, inputs_in, above_in, mixer_in, mlp_in, gains_in, gate_in, chan_in,
    normed_o, wm_o, wf_o, wd_o, w2_o, gains_o, gate_o, chan_o, inputs_o, above_o,
    inputs, above, mixer_w, mlp_w, gains_w, gate_w, chan_w, load_s,
    inputs_k, above_k, w2, keep_s, gp_o, gn, gp, normed, gn_all, wm, wf, wd, loc, ms, mr, fs, fr, line_s, line_r, gain_s, gain_r, move_s, move_r,
    gather_s, gather_r, hop_s, hop_r,
):
    loads = [
        pltpu.make_async_copy(src, dst, load_s.at[n])
        for n, (src, dst) in enumerate(
            (
                (gains_in, gains_w), (gate_in, gate_w), (chan_in, chan_w), (mixer_in, mixer_w),
                (mlp_in, mlp_w), (inputs_in, inputs), (above_in, above),
            )
        )
    ]
    for copy in loads:
        copy.start()
    y, c, z, x = place()
    s = 2 * z + x
    me = rank(y, c, x)
    rows, width = inputs.shape
    pair = width // (4 * length)
    line = line_peers(length)
    plane = plane_peers()
    to_z, to_x = lax.rem(s, length), s // length
    moves = jnp.where(jnp.logical_and(to_z == z, to_x == x), 0, 1)
    src = x * length + z
    from_z = src // 2
    from_x = src - 2 * from_z
    barrier = pltpu.get_barrier_semaphore()
    for peer in line + plane:
        pl.semaphore_signal(barrier, inc=1, device_id=peer, device_id_type=MESH)

    @pl.when(moves == 1)
    def _():
        pl.semaphore_signal(barrier, inc=1, device_id=device(y, c, to_z, to_x), device_id_type=MESH)
        pl.semaphore_signal(barrier, inc=1, device_id=device(y, c, from_z, from_x), device_id_type=MESH)

    def fill(pack, source, js, offset=0):
        part = pack.shape[2] // len(js)
        whole = source.shape[1] // 24
        for t in range(8):
            for n, j in enumerate(js):
                start = (j * 8 + t) * whole + offset
                pack[t, :, n * part : (n + 1) * part] = source[:, start : start + part].astype(BF16)

    loads[3].wait()
    fill(wm, mixer_w, (0, 1, 2))
    for copy in loads[:3]:
        copy.wait()
    share = gains_w.shape[1]
    gn[...] = jnp.zeros_like(gn)
    for n in (0, 1):

        @pl.when(x == n)
        def _():
            gn[:2, n * share : (n + 1) * share] = gains_w[...]

    gp[...] = jnp.zeros_like(gp)
    channels = contract_first(chan_w[...].astype(BF16), unit(8))
    gp[: gate_w.shape[0]] = jnp.concatenate(
        [
            gate_w[...],
            channels,
            jnp.zeros((gate_w.shape[0], gp.shape[1] - gate_w.shape[1] - 8), F32),
        ],
        axis=1,
    ).astype(BF16)
    gn_all[me, z] = gn[...]
    pl.semaphore_wait(barrier, len(line) + len(plane) + 2 * moves)
    gains = [
        remote(gn, gn_all.at[me, z], line_s.at[0, k], line_r.at[0, k], line[k]) for k in range(length - 1)
    ]
    gate_move = pltpu.make_async_remote_copy(
        src_ref=gp, dst_ref=gp_o.at[to_z], send_sem=move_s, recv_sem=move_r,
        device_id=device(y, c, to_z, to_x), device_id_type=MESH,
    )
    gate_stay = pltpu.make_async_copy(gp, gp_o.at[z], loc.at[2])
    pl.when(moves == 1)(lambda: gate_move.start())
    pl.when(moves == 0)(lambda: gate_stay.start())

    mixer, mixer_own = exchange_steps(wm, wm_o.at[0], loc.at[0], ms, mr)
    hops = LineGather(wm_o, length, hop_s, hop_r)
    mixer_own.wait()
    hops.start_piece(me)

    def pass_piece(n):
        fy, fc, fx = FLIPS[n]
        mixer[n].wait_recv()
        hops.start_piece(rank(flip(y, fy), flip(c, fc), flip(x, fx)))

    pass_piece(1)
    for copy in gains:
        copy.wait()
    spread = [
        remote(gn_all.at[me], gn_all.at[me], gain_s.at[n], gain_r.at[n], plane[n]) for n in range(7)
    ]
    loads[4].wait()
    fill(wd, mlp_w, (2,))
    down, down_own = exchange_steps(wd, wd_o.at[0], loc.at[4], fs.at[1], fr.at[1])
    for n in (0, 2, 3, 5, 4, 6):
        pass_piece(n)
    fill(wf, mlp_w, (0, 1))
    feed, feed_own = exchange_steps(wf, wf_o.at[0], loc.at[3], fs.at[0], fr.at[0])
    pl.when(moves == 1)(lambda: gate_move.wait())
    pl.when(moves == 0)(lambda: gate_stay.wait())
    gates = [
        remote(gp_o.at[z], gp_o.at[z], line_s.at[1, k], line_r.at[1, k], line[k])
        for k in range(length - 1)
    ]
    fill(w2, mlp_w, (0, 1, 2), wd.shape[2])
    for copy in spread:
        copy.wait()
    for k in range(length):
        other = lax.rem(z + k, length)
        for b in range(4):
            at = slice((4 * k + b) * pair, (4 * k + b + 1) * pair)
            tile = (gn_all[2 * b, other] + gn_all[2 * b + 1, other])[:, :pair]
            gains_o[:, at] = tile.astype(BF16).astype(F32)
    for copy in mixer:
        copy.wait_send()

    def body(at):
        v = load_turned(inputs, at, length, pair)
        inputs_k[at] = v
        v = v.astype(F32)
        normed[at] = (v * inverse_rms(v) * gains_o[0:1]).astype(BF16)
        above_k[at] = load_turned(above, at, length, pair)

    for copy in loads[5:]:
        copy.wait()
    half = rows // 2
    gather = Gather(normed, normed_o, loc.at[1], gather_s, gather_r)
    rows_loop(half, body)
    gather.begin_half(0)
    hops.arrive(1)
    if length > 2:
        hops.start(2)
    rows_loop(half, body, half)
    gather.begin_half(1)
    keeps = starts(local_copies(((inputs_k, inputs_o), (above_k, above_o)), keep_s))
    for copy in gates:
        copy.wait()
    gate_rows, columns = gate_w.shape
    head = columns // 2
    own = jnp.concatenate([gp_o[n, :gate_rows].astype(F32) for n in range(length)]).astype(BF16)
    part, rc = own.shape[0], gate_o.shape[0]
    gate_o[...] = jnp.zeros_like(gate_o)
    for first_row in range(0, part, head):
        at = slice(first_row, first_row + head)
        wide = [jnp.zeros((head, first_row), F32)] if first_row else []
        for n in (0, 1):
            block = own[at, n * head : (n + 1) * head].astype(F32)
            rest = jnp.zeros((head, rc - first_row - head), F32)
            gate_o[at, n * rc : (n + 1) * rc] = jnp.concatenate([*wide, block, rest], axis=1).astype(BF16)
    rows_of = contract_last(unit(8), own[:, columns : columns + 8])
    lam = rows_of[7:8]
    u = jnp.exp(-jnp.abs(lam))
    t = u / (2.0 + u)
    series = jnp.full_like(t, 1.0 / 17.0)
    for n in range(15, 0, -2):
        series = series * t * t + 1.0 / n
    rate = 8.0 * (jnp.maximum(-lam, 0.0) + 2.0 * t * series)
    fill_rows = jnp.concatenate([jnp.zeros((7, rc - part), F32), jnp.ones((1, rc - part), F32)])
    chan_o[...] = jnp.concatenate([jnp.concatenate([rows_of[:7], rate]), fill_rows], axis=1)
    if length > 3:
        hops.arrive(2)
        hops.start(3)
    gather.middle()
    late, late_own = exchange_steps(w2, w2_o.at[0], loc.at[0], fs.at[2], fr.at[2])
    gather.relays()
    for hop in range(min(3, length - 1), length):
        hops.arrive(hop)
        if hop + 1 < length:
            hops.start(hop + 1)
    gather.finish()
    waits(keeps)
    for copy in down + feed + late:
        copy.wait()
    late_own.wait()
    down_own.wait()
    feed_own.wait()
    hops.finish()


def early(f8):
    return f8 // 384 * 256


def unit(n):
    return (
        lax.broadcasted_iota(jnp.int32, (n, n), 0) == lax.broadcasted_iota(jnp.int32, (n, n), 1)
    ).astype(BF16)


def first(inputs, above, mixer, mlp, gains, gate, chan, rc, length, collective_id):
    rows, width = inputs.shape
    pack = (-(-gate.shape[0] // 16) * 16, rc)
    share = mixer.shape[0]
    f8 = mlp.shape[1] // 24
    wm, wf, wd, w2 = (
        (8, share, n) for n in (mixer.shape[1] // 8, 2 * early(f8), early(f8), 3 * (f8 - early(f8)))
    )
    low = jax.ShapeDtypeStruct((rows, width), BF16)
    return pl.pallas_call(
        functools.partial(first_kernel, length),
        out_shape=(
            jax.ShapeDtypeStruct((8, rows, width), BF16),
            jax.ShapeDtypeStruct((length,) + wm, BF16),
            jax.ShapeDtypeStruct((length,) + wf, BF16),
            jax.ShapeDtypeStruct((length,) + wd, BF16),
            jax.ShapeDtypeStruct((length,) + w2, BF16),
            jax.ShapeDtypeStruct((8, width), F32),
            jax.ShapeDtypeStruct((rc, 2 * rc), BF16),
            jax.ShapeDtypeStruct((8, rc), F32),
            low,
            low,
        ),
        in_specs=[ANY] * 7,
        out_specs=(ANY, ANY, ANY, ANY, ANY, VM, VM, VM, ANY, ANY),
        scratch_shapes=[
            *[pltpu.VMEM(v.shape, v.dtype) for v in (inputs, above, mixer, mlp, gains, gate, chan)],
            DMA((7,)),
            pltpu.VMEM((rows, width), BF16),
            pltpu.VMEM((rows, width), BF16),
            pltpu.VMEM(w2, BF16),
            DMA((2,)),
            pltpu.VMEM((length,) + pack, BF16),
            pltpu.VMEM((8, 128), F32),
            pltpu.VMEM(pack, BF16),
            pltpu.VMEM((rows, width), BF16),
            pltpu.VMEM((8, length, 8, 128), F32),
            pltpu.VMEM(wm, BF16),
            pltpu.VMEM(wf, BF16),
            pltpu.VMEM(wd, BF16),
            DMA((5,)), DMA((7,)), DMA((7,)), DMA((3, 7)), DMA((3, 7)),
            DMA((2, length)), DMA((2, length)), DMA((7,)), DMA((7,)), DMA, DMA,
            DMA((14,)), DMA((14,)), DMA((2, length)), DMA((2, length)),
        ],
        compiler_params=params(collective_id),
        cost_estimate=pl.CostEstimate(flops=0, bytes_accessed=300 * 2**20, transcendentals=0),
    )(inputs, above, mixer, mlp, gains, gate, chan)


def last_kernel(
    length, share, wm, gain, gain_two, gates, sq_a, sq_b, sq_c, sq_d,
    wm_o, gains_o, norm_o, factor_o, by_plane, by_line, loc, ss, rs, gs, gr, ls, lr,
):
    y, c, z, x = place()
    me = rank(y, c, x)
    line = line_peers(length)
    plane = plane_peers()
    width = gain.shape[1]
    pair = width // (4 * length)
    squares = sq_a[...] + sq_b[...] + sq_c[...] + sq_d[...] + tile_of_squares(gates[...])
    squares = jnp.concatenate([squares, jnp.zeros((8, width - 128), F32)], axis=1)
    rows = [jnp.sum(v, axis=0, keepdims=True) for v in (gain[...], gain_two[...], squares)]
    by_plane[me] = jnp.concatenate(rows + [jnp.zeros((1, width), F32)])
    greet(line + plane)
    sends = [
        remote(by_plane.at[me], by_plane.at[me], gs.at[n], gr.at[n], plane[n]) for n in range(7)
    ]
    copies, own = exchange_steps(wm, wm_o, loc, ss, rs)
    for copy in sends:
        copy.wait()
    total = by_plane[0]
    for n in range(1, 8):
        total = total + by_plane[n]
    group = 4 * pair
    for k in range(length):
        at = pl.ds(pl.multiple_of(lax.rem(z + k, length) * group, group), group)
        by_line[z, :, at] = total[:, k * group : (k + 1) * group]
    sends = [
        remote(by_line.at[z], by_line.at[z], ls.at[k], lr.at[k], line[k]) for k in range(length - 1)
    ]
    for copy in sends:
        copy.wait()
    total = by_line[0]
    for n in range(1, length):
        total = total + by_line[n]
    squares = jnp.sum(total[:2] * total[:2], axis=0, keepdims=True) + total[2:3]
    norm = jnp.broadcast_to(jnp.sqrt(jnp.sum(squares, axis=1, keepdims=True)), (8, 128))
    norm_o[...] = norm
    factor_o[...] = clip_limit / jnp.maximum(norm, clip_limit)
    gains = jnp.zeros((2, pair), F32)
    for there in range(length):
        for b in range(4):
            first_lane = (there * 4 + b) * pair
            mine = jnp.logical_and(there == z, b == 2 * y + c)
            gains = jnp.where(mine, total[:2, first_lane : first_lane + pair], gains)
    gains_o[...] = jnp.where(x == 0, gains[:, :share], gains[:, share:])
    for copy in copies:
        copy.wait()
    own.wait()


def last(wm, gain, gain_two, gates, squares, length, collective_id):
    width = gain.shape[1]
    share = wm.shape[1]
    return pl.pallas_call(
        functools.partial(last_kernel, length, share),
        out_shape=(
            jax.ShapeDtypeStruct(wm.shape, wm.dtype),
            jax.ShapeDtypeStruct((2, share), F32),
            TILE, TILE,
        ),
        in_specs=[ANY] + [VM] * 7,
        out_specs=(ANY,) + (VM,) * 3,
        scratch_shapes=[
            pltpu.VMEM((8, 4, width), F32),
            pltpu.VMEM((length, 4, width), F32),
            DMA, DMA((7,)), DMA((7,)), DMA((7,)), DMA((7,)),
            DMA((length,)), DMA((length,)),
        ],
        compiler_params=params(collective_id),
    )(wm, gain, gain_two, gates, *squares)


def minus_expm1(v):
    series = 1.0 + v * (1.0 / 8.0)
    for n in (7.0, 6.0, 5.0, 4.0, 3.0, 2.0):
        series = 1.0 + series * v * (1.0 / n)
    return jnp.where(v > -0.5, -v * series, 1.0 - jnp.exp(v))


def gelu_parts(v):
    square = v * v
    h = 0.5 * jnp.tanh(v * (GELU_CUBE * square + GELU_SCALE)) + 0.5
    return v * h, h, square


def gelu_slope(gelu, h, square):
    return h + gelu * (1.0 - h) * (6.0 * GELU_CUBE * square + 2.0 * GELU_SCALE)


CHUNK = 128


def forward_kernel(
    length, x_in, mixer_in, gate, chan, above, w_in,
    mixed, branch_o, decay_o, width_o, recur_o, enter_o, conv_o, xe_o, se_o, ends_o, above_o, w,
    x_part, pre, loc_h, ends, carry, hs, hr, es, er, gather_l, gather_s, gather_r, hop_s, hop_r, load_s, keep_s, mixer,
    branch, decay_k, width_k, recur_k, enter_k, conv_k, xe, se,
):
    keeps = [
        pltpu.make_async_copy(src, dst, keep_s.at[n])
        for n, (src, dst) in enumerate(
            (
                (branch, branch_o), (decay_k, decay_o), (width_k, width_o), (recur_k, recur_o),
                (enter_k, enter_o), (conv_k, conv_o), (xe, xe_o), (se, se_o),
            )
        )
    ]
    y, c, z, x = place()
    line = line_peers(length)
    seqs, span, rc = branch.shape
    part = mixed.shape[2]
    chunks = span // CHUNK

    def load(b, slot):
        at = pl.ds(pl.multiple_of(b * span, span), span)
        return pltpu.make_async_copy(x_in.at[at], x_part.at[slot], load_s.at[slot])

    load(0, 0).start()
    mixer_load = pltpu.make_async_copy(mixer_in, mixer, load_s.at[2])
    mixer_load.start()
    greet(line + gather_peers())
    hops = LineGather(w, length, hop_s, hop_r)
    hops.start(1)
    gather = Gather(above, above_o, gather_l, gather_s, gather_r)
    gather.begin()

    mixer_load.wait()

    @pl.loop(0, seqs)
    def _(b):
        slot = b - b // 2 * 2

        @pl.when(b + 1 < seqs)
        def _():
            load(b + 1, 1 - slot).start()

        load(b, slot).wait()
        both = jnp.dot(x_part[slot], mixer[:, : 2 * part], preferred_element_type=F32)
        none = jnp.zeros((span, rc - part), F32)
        branch[b] = jnp.concatenate([both[:, :part], none], axis=1)
        low = both[:, part:].astype(BF16).astype(F32)
        xe[b, 8:] = jnp.concatenate([low, none], axis=1)

    ahead = device(y, c, lax.rem(z + 1, length), x)
    halo = remote(xe.at[:, pl.ds(span, 8)], xe.at[:, pl.ds(0, 8)], hs, hr, ahead)

    def coefficients(b, chunk):
        r = pl.multiple_of(chunk * CHUNK, CHUNK)
        at = pl.ds(r, CHUNK)
        window = xe[b, pl.ds(r, CHUNK + 8)]
        total = chan[4:5] + chan[0:1] * window[8:]
        for k in (1, 2, 3):
            total = total + chan[k : k + 1] * pltpu.roll(window, k, 0)[8:]
        low = total.astype(BF16)
        conv_k[b, at] = low
        value = low.astype(F32)
        gates = jnp.dot(low, gate[...], preferred_element_type=F32)
        recur = jax.nn.sigmoid(gates[:, :rc] + chan[5:6])
        enter = jax.nn.sigmoid(gates[:, rc:] + chan[6:7])
        log_decay = -chan[7:8] * recur
        decay = jnp.exp(log_decay)
        width = jnp.sqrt(minus_expm1(2.0 * log_decay))
        recur_k[b, at] = recur
        enter_k[b, at] = enter
        decay_k[b, at] = decay
        width_k[b, at] = width
        loc_h[b, at] = width * enter * value

    def later_chunks(i):
        b = i // (chunks - 1)
        coefficients(b, 1 + i - b * (chunks - 1))

    many = seqs * (chunks - 1)
    pl.loop(0, many // 2)(later_chunks)
    hops.arrive(1)
    if length > 2:
        hops.start(2)
    gather.middle()
    pl.loop(many // 2, many)(later_chunks)
    halo.wait()

    @pl.when(z == 0)
    def _():
        xe[:, 0:8] = jnp.zeros((seqs, 8, rc), F32)

    @pl.loop(0, seqs)
    def _(b):
        coefficients(b, 0)

    for copy in keeps[:-1]:
        copy.start()
    row = lax.broadcasted_iota(jnp.int32, (8, rc), 0)

    def tile(i, held):
        at = pl.ds(pl.multiple_of(i * 8, 8), 8)
        new = []
        for b in range(seqs):
            a, h = decay_k[b, at], loc_h[b, at]
            for n in (1, 2, 4):
                keep = row >= n
                h = h + jnp.where(keep, a * pltpu.roll(h, n, 0), 0.0)
                a = jnp.where(keep, a * pltpu.roll(a, n, 0), a)
            h = h + a * held[b][1]
            a = a * held[b][0]
            loc_h[b, at] = h
            pre[b, at] = a
            new.append((a[7:8], h[7:8]))
        return tuple(new)

    one, zero = jnp.ones((1, rc), F32), jnp.zeros((1, rc), F32)
    final = lax.fori_loop(0, span // 8, tile, ((one, zero),) * seqs)
    for b in range(seqs):
        ends[z, 0, b] = jnp.broadcast_to(final[b][0], (8, rc))
        ends[z, 1, b] = jnp.broadcast_to(final[b][1], (8, rc))
        ends_o[b] = jnp.broadcast_to(final[b][0], (8, rc))
    moves = [remote(ends.at[z], ends.at[z], es.at[k], er.at[k], line[k]) for k in range(length - 1)]
    if length > 3:
        hops.arrive(2)
        hops.start(3)
    for copy in moves:
        copy.wait()
    carry[...] = jnp.zeros_like(carry)
    for k in range(length):
        carry[...] = jnp.where(k < z, ends[k, 0] * carry[...] + ends[k, 1], carry[...])

    for b in range(seqs):
        se[b, 0:8] = carry[b]

    @pl.loop(0, seqs * chunks)
    def _(i):
        b = i // chunks
        r = pl.multiple_of((i - b * chunks) * CHUNK, CHUNK)
        at = pl.ds(r, CHUNK)
        state = loc_h[b, at] + pre[b, at] * carry[b, 0:1]
        se[b, pl.ds(r + 8, CHUNK)] = state
        gelu, _, _ = gelu_parts(branch[b, at])
        mixed[b, at] = (state * gelu)[:, :part].astype(BF16)

    keeps[-1].start()
    gather.end()
    for hop in range(min(3, length - 1), length):
        hops.arrive(hop)
        if hop + 1 < length:
            hops.start(hop + 1)
    hops.finish()
    waits(keeps)


def recur_forward(x, mixer, gate, chan, above, w, length, collective_id):
    rc = gate.shape[0]
    part = mixer.shape[1] // 3
    rows = x.shape[0] // 8
    seqs, span = 4, 2 * rows
    full = jax.ShapeDtypeStruct((seqs, span, rc), F32)
    longer = jax.ShapeDtypeStruct((seqs, span + 8, rc), F32)
    kept = (full, full, full, full, full, jax.ShapeDtypeStruct((seqs, span, rc), BF16), longer, longer)
    return pl.pallas_call(
        functools.partial(forward_kernel, length),
        out_shape=(
            jax.ShapeDtypeStruct((seqs, span, part), BF16),
            *kept,
            jax.ShapeDtypeStruct((seqs, 8, rc), F32),
            jax.ShapeDtypeStruct((8,) + above.shape, above.dtype),
            jax.ShapeDtypeStruct(w.shape, w.dtype),
        ),
        in_specs=[ANY, ANY, VM, VM, ANY, ANY],
        out_specs=(VM,) + (ANY,) * 8 + (VM, ANY, ANY),
        scratch_shapes=[
            pltpu.VMEM((2, span, x.shape[1]), BF16),
            pltpu.VMEM((seqs, span, rc), F32),
            pltpu.VMEM((seqs, span, rc), F32),
            pltpu.VMEM((length, 2, seqs, 8, rc), F32),
            pltpu.VMEM((seqs, 8, rc), F32),
            DMA, DMA, DMA((length,)), DMA((length,)),
            DMA, DMA((14,)), DMA((14,)), DMA((2, length)), DMA((2, length)),
            DMA((3,)), DMA((8,)),
            *held(mixer),
            *[pltpu.VMEM(v.shape, v.dtype) for v in kept],
        ],
        input_output_aliases={5: 11},
        compiler_params=params(collective_id),
        cost_estimate=pl.CostEstimate(
            flops=2 * seqs * span * rc * rc * 2, bytes_accessed=100 * 2**20, transcendentals=0
        ),
    )(x, mixer, gate, chan, above, w)


def backward_kernel(
    length, cuts, head, dmix, gate, chan, decay, width, recur, enter, conv, xe, se, ends_f, proj, block_a, block_b, *refs
):
    parts = 1 + max(cut[0] for cut in cuts)
    terms, refs = refs[:parts], refs[parts:]
    dproj, gates_o, sums, squares, block_ao, block_bo, *refs = refs
    dgate, gchan, *refs = refs
    suffix, grad, de, ends, carry, hs, hr, es, er, keep_s, move_l, move_s, move_r, *refs = refs
    kept, line_refs = refs[:8], refs[8:]
    loads = [
        pltpu.make_async_copy(src, dst, keep_s.at[n])
        for n, (src, dst) in enumerate(
            zip((dmix, proj, se, decay, width, recur, enter, conv, xe), (de.at[:, pl.ds(0, decay.shape[1])], *kept))
        )
    ]
    proj, se, decay, width, recur, enter, conv, xe = kept
    y, c, z, x = place()
    line = line_peers(length)
    greet(line + plane_peers())
    scatter = Lines(terms, cuts, length, line_refs)
    scatter.begin()
    for copy in loads:
        copy.start()
    moves = [
        exchange_steps(block_a, block_ao, move_l.at[0], move_s.at[0], move_r.at[0]),
        exchange_steps(block_b, block_bo, move_l.at[1], move_s.at[1], move_r.at[1]),
    ]
    seqs, span, rc = decay.shape
    part = dproj.shape[2] // 2
    chunks = span // CHUNK
    for copy in loads[:3]:
        copy.wait()

    @pl.loop(0, seqs * chunks)
    def _(i):
        b = i // chunks
        r = pl.multiple_of((i - b * chunks) * CHUNK, CHUNK)
        at = pl.ds(r, CHUNK)
        branch = proj[b, at]
        gelu, h, square = gelu_parts(branch)
        above = de[b, at]
        state = se[b, pl.ds(r + 8, CHUNK)]
        grad[b, at] = above * gelu
        proj[b, at] = above * state * gelu_slope(gelu, h, square)

    loads[3].wait()
    row = lax.broadcasted_iota(jnp.int32, (8, rc), 0)

    def tile(i, held):
        at = pl.ds(pl.multiple_of(span - 8 - i * 8, 8), 8)
        new = []
        for b in range(seqs):
            product, total, following = held[b]
            plain, h = decay[b, at], grad[b, at]
            a = jnp.where(row == 7, following, pltpu.roll(plain, 7, 0))
            for n in (1, 2, 4):
                keep = row < 8 - n
                h = h + jnp.where(keep, a * pltpu.roll(h, 8 - n, 0), 0.0)
                a = jnp.where(keep, a * pltpu.roll(a, 8 - n, 0), a)
            h = h + a * total
            a = a * product
            grad[b, at] = h
            suffix[b, at] = a
            new.append((a[0:1], h[0:1], plain[0:1]))
        return tuple(new)

    one, zero = jnp.ones((1, rc), F32), jnp.zeros((1, rc), F32)
    final = lax.fori_loop(0, span // 8, tile, ((one, zero, one),) * seqs)
    for b in range(seqs):
        ends[z, 0, b] = ends_f[b]
        ends[z, 1, b] = jnp.broadcast_to(final[b][1] * final[b][2], (8, rc))
    tails = [remote(ends.at[z], ends.at[z], es.at[k], er.at[k], line[k]) for k in range(length - 1)]
    for copy in tails:
        copy.wait()
    for copy in loads[4:]:
        copy.wait()
    carry[...] = jnp.zeros_like(carry)
    for k in reversed(range(length)):
        carry[...] = jnp.where(k > z, ends[k, 0] * carry[...] + ends[k, 1], carry[...])

    gchan[...] = jnp.zeros_like(gchan)

    def gradients(b, chunk):
        r = pl.multiple_of(chunk * CHUNK, CHUNK)
        at = pl.ds(r, CHUNK)
        g = grad[b, at] + suffix[b, at] * carry[b, 0:1]
        a, w, ra, ri = decay[b, at], width[b, at], recur[b, at], enter[b, at]
        value = conv[b, at].astype(F32)
        before = pltpu.roll(se[b, pl.ds(r, CHUNK + 8)], 1, 0)[8:]
        dla = g * before * a - g * ri * value * (a * a) / w
        slope = dla * ra * (1.0 - ra)
        dpa = (-chan[7:8] * slope).astype(BF16)
        dpi = (g * w * value * ri * (1.0 - ri)).astype(BF16)
        dgate[b, at, :rc] = dpa
        dgate[b, at, rc:] = dpi
        gchan[5] += fold(dpa.astype(F32))
        gchan[6] += fold(dpi.astype(F32))
        gchan[7] += fold(dla * ra)
        back = lax.dot_general(
            dgate[b, at], gate[...], (((1,), (1,)), ((), ())), preferred_element_type=F32
        )
        dcv = (g * w * ri + back).astype(BF16).astype(F32)
        de[b, at] = dcv
        gchan[4] += fold(dcv)

    pl.loop(0, seqs)(lambda b: gradients(b, 0))
    behind = device(y, c, lax.rem(z + length - 1, length), x)
    halo = remote(de.at[:, pl.ds(0, 8)], de.at[:, pl.ds(span, 8)], hs, hr, behind)
    scatter.start()
    scatter.start()

    @pl.loop(0, seqs * (chunks - 1))
    def _(i):
        b = i // (chunks - 1)
        gradients(b, 1 + i - b * (chunks - 1))

    scatter.start()
    scatter.start()
    halo.wait()
    low = conv[...].reshape(seqs * span, rc)
    recur_grad, enter_grad = (
        contract_first(low, dgate[:, :, at].reshape(seqs * span, rc)) for at in (slice(0, rc), slice(rc, 2 * rc))
    )

    @pl.when(z == length - 1)
    def _():
        de[:, span:] = jnp.zeros((seqs, 8, rc), F32)

    @pl.loop(0, seqs * chunks)
    def _(i):
        b = i // chunks
        r = pl.multiple_of((i - b * chunks) * CHUNK, CHUNK)
        at = pl.ds(r, CHUNK)
        window = de[b, pl.ds(r, CHUNK + 8)]
        inputs = xe[b, pl.ds(r, CHUNK + 8)]
        dcv = window[:CHUNK]
        total = chan[0:1] * dcv
        gchan[0] += fold(dcv * inputs[8:])
        for k in (1, 2, 3):
            total = total + chan[k : k + 1] * pltpu.roll(window, CHUNK + 8 - k, 0)[:CHUNK]
            gchan[k] += fold(dcv * pltpu.roll(inputs, k, 0)[8:])
        dproj[b, at] = jnp.concatenate([proj[b, at, :part], total[:, :part]], axis=1).astype(BF16)

    rates = 8.0 * minus_expm1(chan[7:8] * (-1.0 / 8.0))
    channels = [jnp.sum(gchan[n], axis=0, keepdims=True) for n in range(8)]
    channels[7] = channels[7] * rates
    channels = lax.dot_general(
        jnp.concatenate(channels), unit(8).astype(F32), (((0,), (0,)), ((), ())),
        precision=lax.Precision.HIGHEST, preferred_element_type=F32,
    )
    blocks = []
    for first_row in range(0, part, head):
        at = slice(first_row, first_row + head)
        blocks.append(jnp.concatenate([recur_grad[at, at], enter_grad[at, at]], axis=1))
    pack = jnp.concatenate(
        [jnp.concatenate(blocks), channels[:part], jnp.zeros((part, rc - 2 * head - 8), F32)], axis=1
    )
    rows = part // length
    if rows < gates_o.shape[1]:
        gates_o[...] = jnp.zeros_like(gates_o)
    for n in range(length):
        gates_o[n, :rows] = pack[n * rows : (n + 1) * rows]
    scatter.end(sums, squares)
    for copies, own in moves:
        for copy in copies:
            copy.wait()
        own.wait()


def recur_backward(dmix, gate, chan, kept, part, head, blocks, terms, cuts, length, collective_id):
    proj, decay, width, recur, enter, conv, xe, se, ends = kept
    seqs, span, rc = decay.shape
    gate_pad = -(-(part // length) // 16) * 16
    line_rows, columns = terms[0].shape[1], sum(cut[2] for cut in cuts)
    return pl.pallas_call(
        functools.partial(backward_kernel, length, cuts, head),
        out_shape=(
            jax.ShapeDtypeStruct((seqs, span, 2 * part), BF16),
            jax.ShapeDtypeStruct((length, gate_pad, rc), F32),
            jax.ShapeDtypeStruct((line_rows, columns), BF16), TILE,
            *[jax.ShapeDtypeStruct(block.shape, BF16) for block in blocks],
        ),
        in_specs=[ANY, VM, VM] + [ANY] * 7 + [VM] + [ANY] * (3 + len(terms)),
        out_specs=(VM,) * 4 + (ANY, ANY),
        scratch_shapes=[
            pltpu.VMEM((seqs, span, 2 * rc), BF16),
            pltpu.VMEM((8, 8, rc), F32),
            pltpu.VMEM((seqs, span, rc), F32),
            pltpu.VMEM((seqs, span, rc), F32),
            pltpu.VMEM((seqs, span + 8, rc), F32),
            pltpu.VMEM((length, 2, seqs, 8, rc), F32),
            pltpu.VMEM((seqs, 8, rc), F32),
            DMA, DMA, DMA((length,)), DMA((length,)),
            DMA((9,)), DMA((2,)), DMA((2, 7)), DMA((2, 7)),
            *[
                pltpu.VMEM(shape, dtype)
                for shape, dtype in (
                    (decay.shape, F32), (se.shape, F32), (decay.shape, F32), (decay.shape, F32),
                    (decay.shape, F32), (decay.shape, F32), (decay.shape, BF16), (xe.shape, F32),
                )
            ],
        ]
        + lines_scratch(length, line_rows, cuts),
        compiler_params=params(collective_id),
        cost_estimate=pl.CostEstimate(
            flops=2 * seqs * span * rc * rc * 2, bytes_accessed=120 * 2**20, transcendentals=0
        ),
    )(dmix, gate, chan, decay, width, recur, enter, conv, xe, se, ends, proj, *blocks, *terms)


def contract_last(left, right):
    return lax.dot_general(
        left, right, (((1,), (1,)), ((), ())), preferred_element_type=F32
    )


def contract_first(left, right):
    return lax.dot_general(
        left, right, (((0,), (0,)), ((), ())), preferred_element_type=F32
    )


def resident(shape):
    return pl.BlockSpec(shape, lambda i: (0, 0), pipeline_mode=pl.Buffered(1))


STEPS = 4


def feed_forward(x, above, gate_up, down, hid, dboth):
    f = hid.shape[1]
    both = jnp.dot(x[...], gate_up, preferred_element_type=F32)
    gg, uu = both[:, :f], both[:, f:]
    dhid = jnp.dot(above[...], down, preferred_element_type=F32)
    gelu, h, square = gelu_parts(gg)
    hid[...] = (gelu * uu).astype(BF16)
    dboth[:, :f] = (dhid * uu * gelu_slope(gelu, h, square)).astype(BF16)
    dboth[:, f:] = (dhid * gelu).astype(BF16)


def grads_compute(x, above, hid, dboth, gate_o, up_o, down_o):
    f = hid.shape[1]
    both = contract_first(x[...], dboth[...]).astype(BF16)
    gate_o[...] = both[:, :f]
    up_o[...] = both[:, f:]
    down_o[...] = contract_first(above[...], hid[...]).astype(BF16)


def mlp_specs(tokens, model, f):
    def rows(width):
        return pl.BlockSpec((tokens // STEPS, width), lambda i: (jnp.minimum(i, STEPS - 1), 0))

    columns = pl.BlockSpec((tokens, model // STEPS), lambda i: (0, jnp.maximum(i - STEPS, 0)))
    grads = pl.BlockSpec((model // STEPS, f), lambda i: (jnp.maximum(i - STEPS, 0), 0))
    return rows, columns, grads


def keep_units(step, hid_all, dboth_all, hid, dboth):
    rows = hid.shape[0]
    at = pl.ds(pl.multiple_of(step * rows, rows), rows)
    hid_all[at] = hid[...]
    dboth_all[at] = dboth[...]


def early_mlp_kernel(
    length, x, above, x_columns, above_columns, gate_up, down, w_in,
    hid, dboth, gate_o, up_o, down_o, w, hid_all, dboth_all, ss, rs
):
    step = pl.program_id(0)
    hops = LineGather(w, length, ss, rs)

    @pl.when(step == 0)
    def _():
        greet(line_neighbours(length))
        if length > 2:
            hops.start(2)

    @pl.when(step == STEPS)
    def _():
        for hop in range(2, length - 1):
            hops.arrive(hop)
            hops.start(hop + 1)

    @pl.when(step < STEPS)
    def _():
        feed_forward(x, above, gate_up[...], down[...], hid, dboth)
        keep_units(step, hid_all, dboth_all, hid, dboth)

    @pl.when(step >= STEPS)
    def _():
        grads_compute(x_columns, above_columns, hid_all, dboth_all, gate_o, up_o, down_o)

    @pl.when(step == 2 * STEPS - 1)
    def _():
        hops.arrive(length - 1)
        hops.finish(2, length - 1)


def early_mlp(x, above, gate_up, down, w, length, collective_id):
    tokens, model = x.shape
    f = down.shape[1]
    rows, columns, grads = mlp_specs(tokens, model, f)
    grad_shape = jax.ShapeDtypeStruct((model, f), BF16)
    return pl.pallas_call(
        functools.partial(early_mlp_kernel, length),
        grid=(2 * STEPS,),
        out_shape=(
            jax.ShapeDtypeStruct((tokens, f), BF16),
            jax.ShapeDtypeStruct((tokens, 2 * f), BF16),
            grad_shape, grad_shape, grad_shape,
            jax.ShapeDtypeStruct(w.shape, w.dtype),
        ),
        in_specs=[rows(model), rows(model), columns, columns, resident(gate_up.shape), resident(down.shape), ANY],
        out_specs=(rows(f), rows(2 * f)) + (grads,) * 3 + (ANY,),
        scratch_shapes=[pltpu.VMEM((tokens, f), BF16), pltpu.VMEM((tokens, 2 * f), BF16)]
        + [DMA((2, length)), DMA((2, length))],
        input_output_aliases={6: 5},
        compiler_params=params(collective_id),
        cost_estimate=pl.CostEstimate(flops=12 * tokens * model * f, bytes_accessed=50 * 2**20, transcendentals=0),
    )(x, above, x, above, gate_up, down, w)


def late_mlp_kernel(
    length, cuts, x, above, x_columns, above_columns, hid_one, dboth_one, gate_up_in, down_in, late_in, *refs
):
    terms, refs = refs[: len(cuts)], refs[len(cuts) :]
    out, back, gate_o, up_o, down_o, sums, squares, *refs = refs
    gate_up, down, hid, dboth, hid_all, dboth_all, load_s, *line_refs = refs
    step = pl.program_id(0)
    line = LineScatter([(ref, *cut) for ref, cut in zip(terms, cuts)], length, *line_refs)
    f, g = hid_one.shape[1], hid.shape[1]
    loads = local_copies(
        (
            (late_in.at[:, pl.ds(0, 2 * g)], gate_up.at[:, pl.ds(2 * f, 2 * g)]),
            (late_in.at[:, pl.ds(2 * g, g)], down.at[:, pl.ds(f, g)]),
            (down_in, down.at[:, pl.ds(0, f)]),
            (gate_up_in, gate_up.at[:, pl.ds(0, 2 * f)]),
        ),
        load_s,
    )

    @pl.when(step == 0)
    def _():
        starts(loads)
        greet(line_neighbours(length))
        line.load((1,))
        line.start()
        line.load((*range(2, length), 0))
        waits(loads)

    for hop in range(2, length):

        @pl.when(step == min(2 * STEPS - 2, 2 * (hop - 1)))
        def _():
            line.next = hop
            line.start()

    @pl.when(step < STEPS)
    def _():
        feed_forward(x, above, gate_up[:, 2 * f :], down[:, f:], hid, dboth)
        keep_units(step, hid_all, dboth_all, hid, dboth)
        units = jnp.concatenate([hid_one[...], hid[...]], axis=1)
        out[...] = contract_last(units, down[...]).astype(BF16)
        units = jnp.concatenate([dboth_one[...], dboth[...]], axis=1)
        back[...] = contract_last(units, gate_up[...]).astype(BF16)

    @pl.when(step >= STEPS)
    def _():
        grads_compute(x_columns, above_columns, hid_all, dboth_all, gate_o, up_o, down_o)

    @pl.when(step == 2 * STEPS - 1)
    def _():
        squares[...] = jnp.zeros_like(squares)
        line.end(sums, 0, squares)


def late_mlp(x, above, early_units, gate_up, down, late, terms, cuts, length, collective_id):
    tokens, model = x.shape
    f, g = down.shape[1], late.shape[1] // 3
    line_rows = terms[0].shape[1]
    cut = sum(columns for _, columns in cuts)
    rows, columns, grads = mlp_specs(tokens, model, g)

    def whole(shape):
        return pl.BlockSpec(shape, lambda i: (0, 0))

    return pl.pallas_call(
        functools.partial(late_mlp_kernel, length, cuts),
        grid=(2 * STEPS,),
        out_shape=(jax.ShapeDtypeStruct((tokens, model), BF16),) * 2
        + (jax.ShapeDtypeStruct((model, g), BF16),) * 3
        + (jax.ShapeDtypeStruct((line_rows, cut), BF16), TILE),
        in_specs=[rows(model), rows(model), columns, columns, rows(f), rows(2 * f)]
        + [ANY] * (3 + len(terms)),
        out_specs=(rows(model),) * 2 + (grads,) * 3 + (whole((line_rows, cut)), whole((8, 128))),
        scratch_shapes=[
            pltpu.VMEM((model, 2 * f + 2 * g), BF16),
            pltpu.VMEM((model, f + g), BF16),
            pltpu.VMEM((tokens // STEPS, g), BF16),
            pltpu.VMEM((tokens // STEPS, 2 * g), BF16),
            pltpu.VMEM((tokens, g), BF16),
            pltpu.VMEM((tokens, 2 * g), BF16),
            DMA((4,)),
        ]
        + line_scratch(length, line_rows, cut, len(cuts)),
        compiler_params=params(collective_id),
        cost_estimate=pl.CostEstimate(
            flops=6 * tokens * model * (f + 3 * g), bytes_accessed=70 * 2**20, transcendentals=0
        ),
    )(x, above, x, above, *early_units, gate_up, down, late, *terms)


def adam_step(weight, grad, first, second, factor, rate, decay_rate):
    clipped = grad * factor
    first_new = beta_first * first + (1.0 - beta_first) * clipped
    second_new = beta_second * second + (1.0 - beta_second) * clipped * clipped
    first_hat = first_new / (1.0 - beta_first**STEP)
    second_hat = second_new / (1.0 - beta_second**STEP)
    weight_new = weight - rate * (
        first_hat / (jnp.sqrt(second_hat) + adam_eps) + decay_rate * weight
    )
    return (first_new, second_new, weight_new)


def small_steps(factor, refs, outs):
    gains_sum, gates_sum, *states = refs
    rows, columns = states[3].shape
    channels = lax.dot_general(
        unit(8).astype(F32), gates_sum[:rows, columns : columns + 8], (((1,), (1,)), ((), ())),
        precision=lax.Precision.HIGHEST, preferred_element_type=F32,
    )
    grads = gains_sum[...], gates_sum[:rows, :columns], channels
    rates = (rate_gains, 0.0), (rate_matrix, decay_matrix), (rate_channel, 0.0)
    for n in range(3):
        w, m, v = states[3 * n : 3 * n + 3]
        results = adam_step(w[...], grads[n], m[...], v[...], factor, *rates[n])
        for out, result in zip(outs[3 * n : 3 * n + 3], results):
            out[...] = result


def adam_kernel(sources, factor, *refs):
    states, refs = refs[: 3 * len(sources)], refs[3 * len(sources) :]
    count = sum(len(source) for source in sources)
    grads, small, refs = refs[:count], refs[count : count + 11], refs[count + 11 :]
    results, norm, outs = refs[:2], refs[2], refs[3:]
    for result, out in zip(results, outs[-3:]):
        out[...] = result[...]
    outs[-1][...] = norm[0:1, 0:1]
    one = factor[0:1, 0:1]
    pl.when(pl.program_id(0) == 0)(lambda: small_steps(one, small, outs[3 * len(sources) : -3]))
    for n, source in enumerate(sources):
        parts = []
        for pieces in source:
            ref, *grads = grads
            for first, columns, at, stride in pieces:
                for t in range(8):
                    parts.append((at + t * stride, columns, ref, t, first))
        parts.sort(key=lambda part: part[0])
        w, m, v = states[3 * n : 3 * n + 3]
        m_o, v_o, w_o = outs[3 * n : 3 * n + 3]
        run = []
        for at, columns, ref, t, first in parts:
            run.append((at, columns, ref[t, :, first : first + columns].astype(F32)))
            end = at + columns
            if end % 128:
                continue
            grad = jnp.concatenate([piece for _, _, piece in run], axis=1) if len(run) > 1 else run[0][2]
            cols = slice(run[0][0], end)
            run = []
            first_new, second_new, weight_new = adam_step(
                w[:, cols], grad, m[:, cols], v[:, cols], one, rate_matrix, decay_matrix
            )
            m_o[:, cols] = first_new
            v_o[:, cols] = second_new
            w_o[:, cols] = weight_new


def adam(matrices, small, factor, norm, passed):
    rows = matrices[0][0].shape[0]
    step = min(rows, 16)

    def block(v):
        return pl.BlockSpec((step, v.shape[1]), lambda i: (i, 0))

    def whole(v):
        return pl.BlockSpec(v.shape, lambda i: (0, 0))

    states = [v for matrix in matrices for v in matrix[:3]]
    grads = [g for matrix in matrices for g in matrix[3]]
    results = [*states, *small[2:], *passed]
    steps = rows // step

    def slab(v):
        return pl.BlockSpec((v.shape[0] // steps, v.shape[1]), lambda i: (i, 0))

    return pl.pallas_call(
        functools.partial(adam_kernel, [matrix[4] for matrix in matrices]),
        grid=(steps,),
        out_shape=tuple(jax.ShapeDtypeStruct(v.shape, v.dtype) for v in results)
        + (jax.ShapeDtypeStruct((1, 1), F32),),
        in_specs=[pl.BlockSpec((8, 128), lambda i: (0, 0))]
        + [block(v) for v in states]
        + [pl.BlockSpec((8, step, g.shape[2]), lambda i: (0, i, 0)) for g in grads]
        + [whole(v) for v in small]
        + [slab(v) for v in passed]
        + [whole(norm)],
        out_specs=tuple(block(v) for v in states)
        + tuple(whole(v) for v in small[2:])
        + tuple(slab(v) for v in passed)
        + (pl.BlockSpec((1, 1), lambda i: (0, 0)),),
        compiler_params=pltpu.CompilerParams(vmem_limit_bytes=VMEM_BYTES),
        cost_estimate=pl.CostEstimate(
            flops=0, bytes_accessed=sum(8 * v.size for v in states), transcendentals=0
        ),
    )(factor, *states, *grads, *small, *passed, norm)


def on_device(
    block_input,
    out_grad,
    norm_gains,
    mixer_weight,
    gate_weight,
    chan_params,
    mlp_weight,
    first_gains,
    first_mixer,
    first_gate,
    first_chan,
    first_mlp,
    second_gains,
    second_mixer,
    second_gate,
    second_chan,
    second_mlp,
):
    length = lax.axis_size("seq") // 2
    z = lax.axis_index("seq") // 2
    tokens, model = block_input.shape[1:]
    share = mixer_weight.shape[0]
    pair = 2 * share
    lru = mixer_weight.shape[1] // 3
    hidden = mlp_weight.shape[1] // 3
    r8, f8 = lru // 8, hidden // 8
    rc = -(-r8 // 128) * 128
    head = gate_weight.shape[1] // 2
    heads = r8 // head
    gate_rows = gate_weight.shape[0]
    gate_pad = -(-gate_rows // 16) * 16

    x = lax.axis_index("seq") - 2 * z
    batch = lax.axis_index("batch")
    plain = pair % 128 == 0

    def turned(v):
        if plain:
            return v
        v = v.reshape(v.shape[0], 4, length, pair).swapaxes(1, 2)
        return jnp.roll(v, -z, axis=1).reshape(v.shape[0], model)

    def turned_back(v):
        if plain:
            return v
        v = jnp.roll(v.reshape(v.shape[0], length, 4, pair), z, axis=1)
        return v.swapaxes(1, 2).reshape(v.shape[0], model)

    normed_one, mixer_full, mlp_gu, mlp_down, late, gains, gate, chan, inputs, above = first(
        turned(block_input[0]),
        turned(out_grad[0]),
        mixer_weight,
        mlp_weight,
        norm_gains,
        gate_weight,
        chan_params,
        rc,
        length,
        1,
    )
    normed_one = normed_one.reshape(8 * tokens, model)
    mixer_full = mixer_full.reshape(model, 3 * r8)
    mixed, *kept, grad_out, mlp_down = recur_forward(
        normed_one, mixer_full, gate, chan, above, mlp_down, length, 2
    )
    grad_out = grad_out.reshape(8 * tokens, model)
    mixed = mixed.reshape(8 * tokens, r8)
    residual, normed_two, mlp_gu, late = middle(mixed, mixer_full, inputs, gains, mlp_gu, late, length, 3)
    normed_two = normed_two.reshape(8 * tokens, model)
    h1 = early(f8)
    h2 = f8 - h1
    mlp_gu = mlp_gu.reshape(model, 2 * h1)
    mlp_down = mlp_down.reshape(model, h1)
    hid, dboth, *early_terms, late = early_mlp(normed_two, grad_out, mlp_gu, mlp_down, late, length, 9)
    gate_one, up_one, down_one = (v.reshape(length, 8 * share, h1) for v in early_terms)
    cut = h1 // 4
    mlp_part, dnormed_two, *late_terms, sums_zero, squares_zero = late_mlp(
        normed_two, grad_out, (hid, dboth), mlp_gu, mlp_down, late.reshape(model, 3 * h2),
        (gate_one, up_one), ((0, h1), (0, cut)), length, 11,
    )
    gate_two, up_two, down_two = (v.reshape(length, 8 * share, h2) for v in late_terms)

    grad_residual, gain_two, dmz, dmix, sums_one, squares_one = turn(
        dnormed_two, residual, above, gains, mixer_full, rc,
        (up_one, down_one, gate_two), ((0, cut, h1 - cut), (1, 0, h1), (2, 0, h2)),
        length, 4,
    )
    dmz = dmz.reshape(8 * tokens, model)
    span = 2 * tokens
    dmix = dmix.reshape(4, span, rc)
    sums_zero, sums_one = (v.reshape(8, share, v.shape[1]) for v in (sums_zero, sums_one))
    dproj, gate_back, sums_two, squares_two, back_zero, back_one = recur_backward(
        dmix, gate, chan, kept, r8, head, (sums_zero, sums_one),
        (up_two, down_two), ((0, 0, h2), (1, 0, h2)), length, 6,
    )
    dproj = dproj.reshape(4 * span, 2 * r8)
    input_grad, gain_one, gates_sum, block_output, back_two, mixer_sums, squares_three = closing(
        normed_one, dmz, dproj, mixed, mixer_full, mlp_part, residual, sums_two,
        inputs, grad_residual, gains, gate_back, length, 7,
    )
    mixer_back, gains_sum, norm, factor = last(
        mixer_sums.reshape(8, share, mixer_sums.shape[1]), gain_one, gain_two, gates_sum,
        (squares_zero, squares_one, squares_two, squares_three), length, 8,
    )
    mlp_sources = (
        [(0, h1, 0, f8), (h1, cut, hidden, f8)],
        [
            (0, h1 - cut, hidden + cut, f8),
            (h1 - cut, h1, 2 * hidden, f8),
            (2 * h1 - cut, h2, h1, f8),
        ],
        [(0, h2, hidden + h1, f8), (h2, h2, 2 * hidden + h1, f8)],
    )
    states = adam(
        (
            (
                mixer_weight, first_mixer, second_mixer, (mixer_back,),
                ([(n * r8, r8, n * lru, r8) for n in range(3)],),
            ),
            (mlp_weight, first_mlp, second_mlp, (back_zero, back_one, back_two), mlp_sources),
        ),
        (
            gains_sum, gates_sum, norm_gains, first_gains, second_gains, gate_weight, first_gate, second_gate,
            chan_params, first_chan, second_chan,
        ),
        factor,
        norm,
        (block_output, input_grad),
    )
    *states, block_output, input_grad, norm = states
    mixer_up, mlp_up, gains_up, gate_up, chan_up = (states[3 * n : 3 * n + 3] for n in range(5))
    return (
        turned_back(block_output)[None],
        turned_back(input_grad)[None],
        norm.reshape(()),
        *gains_up,
        *mixer_up,
        *gate_up,
        *chan_up,
        *mlp_up,
    )


def solution(mesh):
    rows = P(("batch", "seq"), None)
    columns = P(None, ("batch", "seq"))
    data = P("batch", "seq", None)
    weights = (columns, rows, rows, columns, rows)
    in_specs = (data, data) + weights * 3
    triples = tuple(spec for spec in weights for _ in range(3))
    return jax.shard_map(
        on_device,
        mesh=mesh,
        in_specs=in_specs,
        out_specs=(data, data, P()) + triples,
        check_vma=False,
    )
```

```python
import functools
import math

import jax
import jax.numpy as jnp
from jax import lax
from jax.experimental import pallas as pl
from jax.experimental.pallas import tpu as pltpu
from jax.sharding import PartitionSpec as P

STEP = 10
norm_eps = 1e-06
clip_limit = 1.0
beta_first = 0.9
beta_second = 0.999
adam_eps = 1e-08
rate_matrix = 0.05
rate_gains = 0.8
rate_channel = 2.0
decay_matrix = 0.1

MESH = pl.DeviceIdType.MESH
F32 = jnp.float32
BF16 = jnp.bfloat16
ANY = pl.BlockSpec(memory_space=pl.ANY)
VM = pl.BlockSpec(memory_space=pltpu.VMEM)
FLIPS = [(fy, fc, fx) for fy in (0, 1) for fc in (0, 1) for fx in (0, 1) if fy + fc + fx]
GELU_SCALE = math.sqrt(2.0 / math.pi)
GELU_CUBE = 0.044715 * GELU_SCALE


def place():
    b = lax.axis_index("batch")
    s = lax.axis_index("seq")
    y, z = b // 2, s // 2
    return y, b - 2 * y, z, s - 2 * z


def device(y, c, z, x):
    return (y * 2 + c, z * 2 + x)


def rank(y, c, x):
    return (y * 2 + c) * 2 + x


def flip(v, f):
    return 1 - v if f else v


def greet(peers):
    barrier = pltpu.get_barrier_semaphore()
    for peer in peers:
        pl.semaphore_signal(barrier, inc=1, device_id=peer, device_id_type=MESH)
    pl.semaphore_wait(barrier, len(peers))


def remote(src, dst, send, recv, to):
    copy = pltpu.make_async_remote_copy(
        src_ref=src, dst_ref=dst, send_sem=send, recv_sem=recv, device_id=to, device_id_type=MESH
    )
    copy.start()
    return copy


VMEM_BYTES = 63 * 2**20


def params(collective_id):
    return pltpu.CompilerParams(
        collective_id=collective_id, has_side_effects=True, vmem_limit_bytes=VMEM_BYTES
    )


DMA = pltpu.SemaphoreType.DMA


def gather_peers():
    y, c, z, x = place()
    return [device(y, c, z, 1 - x), device(1 - y, c, z, x), device(y, 1 - c, z, x)]


class Gather:
    def __init__(self, a, o, loc, ss, rs):
        y, c, z, x = place()
        self.to_x, self.to_y, self.to_c = gather_peers()
        self.me, self.bx = rank(y, c, x), rank(y, c, 1 - x)
        self.by, self.bd = rank(1 - y, c, x), rank(1 - y, c, 1 - x)
        half = a.shape[0] // 2
        self.lo, self.hi = pl.ds(0, half), pl.ds(half, half)
        self.a, self.o, self.loc, self.ss, self.rs = a, o, loc, ss, rs
        self.done, self.last = [], []

    def send(self, src, dst, k, to):
        copy = remote(src, dst, self.ss.at[k], self.rs.at[k], to)
        self.done.append(copy)
        return copy

    def relay(self, block, part, k, to):
        return self.send(self.o.at[block, part], self.o.at[block, part], k, to)

    def begin_half(self, half):
        a, o, me = self.a, self.o, self.me
        part = (self.lo, self.hi)[half]
        if half == 0:
            self.s0 = self.send(a.at[part], o.at[me, part], 0, self.to_x)
            self.s3 = self.send(a.at[part], o.at[me, part], 3, self.to_y)
        else:
            self.s1 = self.send(a.at[part], o.at[me, part], 1, self.to_y)
            self.s2 = self.send(a.at[part], o.at[me, part], 2, self.to_x)
        self.last.append(self.send(a.at[part], o.at[me, part], (4, 13)[half], self.to_c))
        if half == 1:
            self.own = pltpu.make_async_copy(a, o.at[me], self.loc)
            self.own.start()

    def begin(self):
        a, o, me, lo, hi = self.a, self.o, self.me, self.lo, self.hi
        self.s0 = self.send(a.at[lo], o.at[me, lo], 0, self.to_x)
        self.s1 = self.send(a.at[hi], o.at[me, hi], 1, self.to_y)
        self.s2 = self.send(a.at[hi], o.at[me, hi], 2, self.to_x)
        self.s3 = self.send(a.at[lo], o.at[me, lo], 3, self.to_y)
        self.last += [self.send(a.at[part], o.at[me, part], k, self.to_c) for part, k in ((lo, 4), (hi, 13))]
        self.own = pltpu.make_async_copy(a, o.at[me], self.loc)
        self.own.start()

    def middle(self):
        self.s0.wait_recv()
        self.s5 = self.relay(self.bx, self.lo, 5, self.to_y)
        self.last.append(self.relay(self.bx, self.lo, 7, self.to_c))
        self.s1.wait_recv()
        self.s6 = self.relay(self.by, self.hi, 6, self.to_x)
        self.last.append(self.relay(self.by, self.hi, 8, self.to_c))

    def relays(self, mark=lambda: None):
        self.s2.wait_recv()
        self.last.append(self.relay(self.bx, self.hi, 9, self.to_c))
        self.s3.wait_recv()
        self.last.append(self.relay(self.by, self.lo, 10, self.to_c))
        mark()
        self.s5.wait_recv()
        self.last.append(self.relay(self.bd, self.lo, 11, self.to_c))
        self.s6.wait_recv()
        self.last.append(self.relay(self.bd, self.hi, 12, self.to_c))

    def finish(self, skip=0, own=True):
        for copy in self.last[skip:]:
            copy.wait_recv()
        for copy in self.done:
            copy.wait_send()
        if own:
            self.own.wait()

    def end(self, mark=lambda: None):
        self.relays(mark)
        self.finish()


def scatter_steps(p, o, mine, sib, part, got, loc, ss, rs, prepare=None):
    y, c, z, x = place()
    to_x, to_y, to_c = gather_peers()
    half = o.shape[0] // 2
    step = 16
    cut = (pl.ds(0, half), pl.ds(half, half))
    where = ((1 - y, 1 - x), (1 - y, x), (y, 1 - x), (y, x))
    order = [(0, 0), (0, 1), (1, 0), (2, 1), (2, 0), (1, 1), (3, 0), (3, 1)]
    from_c, own, sends = {}, {}, []
    for n, (t, h) in enumerate(order):
        ty, tx = where[t]
        if mine is not None and prepare and all(key[0] != t for key in own):
            prepare(rank(ty, c, tx))
            prepare(rank(ty, 1 - c, tx))
        if mine is None:
            own[t, h] = None
        else:
            own[t, h] = pltpu.make_async_copy(
                p.at[rank(ty, c, tx), cut[h]], mine.at[t, h], loc.at[n]
            )
            own[t, h].start()
        from_c[t, h] = remote(
            p.at[rank(ty, 1 - c, tx), cut[h]], sib.at[t, h], ss.at[n], rs.at[n], to_c
        )
        sends.append(from_c[t, h])
    yield "begun"

    def own_ref(t, h):
        return p.at[rank(where[t][0], c, where[t][1]), cut[h]] if mine is None else mine.at[t, h]

    pieces = ((0, 0), (0, 1), (1, 0), (2, 1), (2, 0), (1, 1))

    def part_ref(k):
        return own_ref(*pieces[k]) if part is None else part.at[k]

    def add(dst, t, h, extra):
        if own[t, h] is not None:
            own[t, h].wait()
        term = own_ref(t, h)
        from_c[t, h].wait_recv()

        @pl.loop(0, half // step)
        def _(i):
            at = pl.ds(pl.multiple_of(i * step, step), step)
            total = term[at].astype(F32) + sib[t, h, at].astype(F32)
            for ref in extra:
                total = total + ref[at].astype(F32)
            dst[at] = total.astype(dst.dtype)

    def send(k, slot, to):
        copy = remote(part_ref(k), got.at[slot], ss.at[8 + k], rs.at[8 + slot], to)
        sends.append(copy)
        return copy

    def arrival(slot):
        return pltpu.make_async_remote_copy(
            src_ref=got.at[slot], dst_ref=got.at[slot], send_sem=ss.at[8], recv_sem=rs.at[8 + slot],
            device_id=to_x, device_id_type=MESH,
        )

    add(part_ref(0), 0, 0, ())
    send(0, 1, to_y)
    add(part_ref(1), 0, 1, ())
    send(1, 3, to_x)
    add(part_ref(2), 1, 0, ())
    send(2, 0, to_y)
    add(part_ref(3), 2, 1, ())
    send(3, 2, to_x)
    yield "sent"
    arrival(1).wait_recv()
    add(part_ref(4), 2, 0, (got.at[1],))
    send(4, 4, to_x)
    yield "early"
    arrival(3).wait_recv()
    add(part_ref(5), 1, 1, (got.at[3],))
    send(5, 5, to_y)
    yield "late"
    arrival(0).wait_recv()
    arrival(4).wait_recv()
    add(o.at[cut[0]], 3, 0, (got.at[0], got.at[4]))
    yield "low half"
    arrival(2).wait_recv()
    arrival(5).wait_recv()
    add(o.at[cut[1]], 3, 1, (got.at[2], got.at[5]))
    yield "high half"
    for copy in sends:
        copy.wait_send()


def scatter_scratch(half, width):
    return [
        pltpu.VMEM((4, 2, half, width), BF16),
        pltpu.VMEM((4, 2, half, width), BF16),
        pltpu.VMEM((6, half, width), BF16),
        pltpu.VMEM((6, half, width), BF16),
        DMA((8,)),
        DMA((14,)),
        DMA((14,)),
    ]


def exchange_steps(a, o, loc, ss, rs):
    y, c, z, x = place()
    me = rank(y, c, x)
    dst = o.at[me]
    rows = o.shape[1]

    def block(t):
        if len(a.shape) == 3:
            return a.at[t]
        return a.at[pl.ds(pl.multiple_of(t * rows, rows), rows)]

    copies = []
    for n, (fy, fc, fx) in enumerate(FLIPS):
        ty, tc, tx = flip(y, fy), flip(c, fc), flip(x, fx)
        copies.append(remote(block(rank(ty, tc, tx)), dst, ss.at[n], rs.at[n], device(ty, tc, z, tx)))
    own = pltpu.make_async_copy(block(me), dst, loc)
    own.start()
    return copies, own


def plane_peers():
    y, c, z, x = place()
    return [device(flip(y, fy), flip(c, fc), z, flip(x, fx)) for fy, fc, fx in FLIPS]


def line_peers(length):
    y, c, z, x = place()
    return [device(y, c, lax.rem(z + k, length), x) for k in range(1, length)]


class LineGather:
    def __init__(self, buf, length, ss, rs):
        y, c, z, x = place()
        self.z, self.length, self.buf, self.ss, self.rs = z, length, buf, ss, rs
        self.up = device(y, c, lax.rem(z + 1, length), x)
        self.down = device(y, c, lax.rem(z + length - 1, length), x)

    def copy(self, hop, upward):
        length, buf = self.length, self.buf
        src, dst = ((length - hop + 1) % length, length - hop) if upward else (hop - 1, hop)
        way = 0 if upward else 1
        return pltpu.make_async_remote_copy(
            src_ref=buf.at[src], dst_ref=buf.at[dst], send_sem=self.ss.at[way, hop - 1],
            recv_sem=self.rs.at[way, hop - 1], device_id=self.up if upward else self.down,
            device_id_type=MESH,
        )

    def sends(self, hop, act):
        z, length = self.z, self.length

        @pl.when(jnp.logical_and(z + 1 < length, z >= hop - 1))
        def _():
            act(self.copy(hop, True))

        @pl.when(jnp.logical_and(z >= 1, z + hop - 1 < length))
        def _():
            act(self.copy(hop, False))

    def start(self, hop):
        self.sends(hop, lambda copy: copy.start())

    def start_piece(self, n):
        for way, last, dst in ((0, self.z + 1 < self.length, self.length - 1), (1, self.z >= 1, 1)):

            @pl.when(last)
            def _():
                remote(
                    self.buf.at[0, n], self.buf.at[dst, n], self.ss.at[way, 0], self.rs.at[way, 0],
                    (self.up, self.down)[way],
                )

    def arrive(self, hop):
        z, length = self.z, self.length

        @pl.when(z >= hop)
        def _():
            self.copy(hop, True).wait_recv()

        @pl.when(z + hop < length)
        def _():
            self.copy(hop, False).wait_recv()

    def finish(self, first_hop=1, last_hop=None):
        for hop in range(first_hop, (last_hop or self.length - 1) + 1):
            self.sends(hop, lambda copy: copy.wait_send())


class LineScatter:
    def __init__(self, sources, length, total, up_mine, down_mine, up_got, down_got, loc, ss, rs):
        y, c, z, x = place()
        self.sources, self.length, self.total = sources, length, total
        self.mine, self.got = (up_mine, down_mine), (up_got, down_got)
        self.loc, self.ss, self.rs = loc, ss, rs
        self.to = (device(y, c, lax.rem(z + 1, length), x), device(y, c, lax.rem(z + length - 1, length), x))
        self.far = (z, length - 1 - z)
        self.next = 1

    def loads(self, way, hop):
        k = 0 if hop == 0 else self.length - hop if way == 0 else hop
        copies, at = [], 0
        for n, (ref, first, columns) in enumerate(self.sources):
            dst = self.term(way, hop) if hop else self.total
            copies.append(
                pltpu.make_async_copy(
                    ref.at[k, :, pl.ds(first, columns)], dst.at[:, pl.ds(at, columns)],
                    self.loc.at[way, hop, n],
                )
            )
            at += columns
        return copies

    def term(self, way, hop):
        return self.mine[way].at[hop - 1]

    def copy(self, way, hop):
        return pltpu.make_async_remote_copy(
            src_ref=self.term(way, hop), dst_ref=self.got[way].at[hop - 1],
            send_sem=self.ss.at[way, hop - 1], recv_sem=self.rs.at[way, hop - 1],
            device_id=self.to[way], device_id_type=MESH,
        )

    def load(self, hops):
        for hop in hops:
            for way in (0, 1) if hop else (0,):
                for copy in self.loads(way, hop):
                    copy.start()

    def start(self):
        hop = self.next
        if hop >= self.length:
            return
        self.next += 1
        for way in (0, 1):
            far = self.far[way]
            for copy in self.loads(way, hop):
                copy.wait()
            if hop > 1:

                @pl.when(jnp.logical_and(far >= 1, far <= hop - 1))
                def _():
                    self.copy(way, hop - 1).wait_recv()
                    dst, src = self.term(way, hop), self.got[way].at[hop - 2]

                    def add(at):
                        dst[at] = dst[at] + src[at]

                    rows_loop(dst.shape[0], add, unroll=4)

            @pl.when(far <= hop - 1)
            def _():
                self.copy(way, hop).start()

    def end(self, result, first_column, squares):
        last = self.length - 1
        for copy in self.loads(0, 0):
            copy.wait()
        columns = pl.ds(first_column, self.total.shape[1])

        def finish(ways):
            for way in ways:
                self.copy(way, last).wait_recv()

            def add(at):
                total = self.total[at].astype(F32)
                for way in ways:
                    total = total + self.got[way][last - 1, at].astype(F32)
                result[at, columns] = total.astype(result.dtype)
                squares[...] += tile_of_squares(total)

            rows_loop(result.shape[0], add)

        above, below = self.far[0] >= 1, self.far[1] >= 1
        pl.when(jnp.logical_and(above, below))(lambda: finish((0, 1)))
        pl.when(jnp.logical_not(above))(lambda: finish((1,)))
        pl.when(jnp.logical_not(below))(lambda: finish((0,)))
        for hop in range(1, self.length):
            for way in (0, 1):

                @pl.when(self.far[way] <= hop - 1)
                def _():
                    self.copy(way, hop).wait_send()


class HeldLine(LineScatter):
    def __init__(self, g, first_column, up_got, down_got, ss, rs):
        y, c, z, x = place()
        self.length = length = g.shape[0]
        self.columns = pl.ds(first_column, up_got.shape[2])
        self.sources, self.g, self.total = (), g, g.at[0, :, self.columns]
        self.got, self.ss, self.rs = (up_got, down_got), ss, rs
        self.to = line_neighbours(length)
        self.far = (z, length - 1 - z)
        self.next = 1

    def term(self, way, hop):
        return self.g.at[self.length - hop if way == 0 else hop, :, self.columns]


def chains_of(cuts):
    whole = sum(cut[2] for cut in cuts)
    left = -(-whole // 256) * 128
    lists = [], []
    for which, first_column, columns in cuts:
        taken = min(columns, left)
        if taken:
            lists[0].append((which, first_column, taken))
        if columns > taken:
            lists[1].append((which, first_column + taken, columns - taken))
        left -= taken
    return lists


class Lines:
    def __init__(self, terms, cuts, length, refs):
        self.chains, self.length = [], length
        for n, cut in enumerate(chains_of(cuts)):
            sources = [(terms[which], first_column, columns) for which, first_column, columns in cut]
            self.chains.append(
                LineScatter(sources, length, *refs[n * LINE_REFS : (n + 1) * LINE_REFS])
            )
        self.queue = [chain for _ in range(1, length) for chain in self.chains]

    def begin(self):
        for chain in self.chains:
            chain.load((1,))
        self.start()
        self.start()
        for chain in self.chains:
            chain.load((*range(2, self.length), 0))

    def start(self):
        if self.queue:
            self.queue.pop(0).start()

    def end(self, result, squares):
        while self.queue:
            self.start()
        squares[...] = jnp.zeros_like(squares)
        at = 0
        for chain in self.chains:
            chain.end(result, at, squares)
            at += chain.total.shape[1]


def lines_scratch(length, rows, cuts):
    return sum(
        (line_scratch(length, rows, sum(cut[2] for cut in chain), len(chain)) for chain in chains_of(cuts)), []
    )


def fold(v):
    return jnp.sum(v.reshape(v.shape[0] // 8, 8, v.shape[1]), axis=0)


def tile_of_squares(v):
    v = fold(v * v)
    part = v[:, :128]
    for n in range(1, v.shape[1] // 128):
        part = part + v[:, n * 128 : (n + 1) * 128]
    if v.shape[1] % 128:
        rest = v[:, v.shape[1] // 128 * 128 :]
        part = part + jnp.concatenate([rest, jnp.zeros((8, 128 - rest.shape[1]), F32)], axis=1)
    return part


def line_scratch(length, rows, columns, sources):
    slots = pltpu.VMEM((length - 1, rows, columns), BF16)
    return [pltpu.VMEM((rows, columns), BF16)] + [slots] * 4 + [
        DMA((2, length, sources)), DMA((2, length)), DMA((2, length))
    ]


def starts(copies):
    for copy in copies:
        copy.start()
    return copies


def waits(copies):
    for copy in copies:
        copy.wait()


def local_copies(pairs, sems):
    return [pltpu.make_async_copy(src, dst, sems.at[n]) for n, (src, dst) in enumerate(pairs)]


def held(*arrays):
    return [pltpu.VMEM(v.shape, v.dtype) for v in arrays]


LINE_REFS = 8
SCATTER_REFS = 7
TILE = jax.ShapeDtypeStruct((8, 128), F32)


def line_neighbours(length):
    y, c, z, x = place()
    return [device(y, c, lax.rem(z + 1, length), x), device(y, c, lax.rem(z + length - 1, length), x)]


def rows_loop(rows, body, start=0, unroll=4):
    @pl.loop(start // 16, (start + rows) // 16, unroll=unroll)
    def _(i):
        body(pl.ds(pl.multiple_of(i * 16, 16), 16))


def turned_tiles(length, pair):
    _, _, z, _ = place()
    for k in range(length):
        for b in range(4):
            yield k * 4 + b, pl.multiple_of((b * length + lax.rem(z + k, length)) * pair, pair)


def load_turned(ref, at, length, pair):
    if pair % 128:
        return ref[at]
    return jnp.concatenate([ref[at, pl.ds(src, pair)] for _, src in turned_tiles(length, pair)], axis=1)


def store_turned(ref, at, value, length, pair):
    if pair % 128:
        ref[at] = value
        return
    for n, dst in turned_tiles(length, pair):
        ref[at, pl.ds(dst, pair)] = value[:, n * pair : (n + 1) * pair]


def inverse_rms(v):
    return lax.rsqrt(jnp.sum(v * v, axis=-1, keepdims=True) * (1.0 / v.shape[-1]) + norm_eps)


def norm_rows_back(v, gain, grad):
    inverse = inverse_rms(v)
    scaled = v * inverse
    moved = grad * gain
    inner = jnp.sum(moved * scaled, axis=-1, keepdims=True) * (1.0 / v.shape[-1])
    return inverse * (moved - scaled * inner), fold(grad * scaled)


def middle_kernel(length, mixed_in, mixer_in, inputs_in, gains_in, w_in, late_in, residual_o, normed_o, w, late, *scratch):
    scatter_refs, (p, low, loc, gs, gr, hs, hr, late_s, late_r, *scratch) = scratch[:SCATTER_REFS], scratch[SCATTER_REFS:]
    mixed, mixer, inputs, gains, residual, load_s, keep_s = scratch
    loads = starts(
        local_copies(
            ((mixed_in, mixed), (mixer_in, mixer), (inputs_in, inputs), (gains_in, gains)), load_s
        )
    )
    greet(gather_peers() + line_neighbours(length))
    hops = LineGather(w, length, hs, hr)
    hops.start(1)
    late_hops = LineGather(late, length, late_s, late_r)
    late_hops.start(1)
    started = [1]
    part = mixed.shape[1]
    rows, width = low.shape

    waits(loads[:2])

    def prepare(i):
        mine = mixed[pl.ds(pl.multiple_of(i * rows, rows), rows)]
        p[i] = contract_last(mine, mixer[:, 2 * part :]).astype(BF16)

    def advance():
        if started[0] < length - 1:
            hops.arrive(started[0])
            started[0] += 1
            hops.start(started[0])

    def body(at):
        v = inputs[at].astype(F32) + residual[at]
        residual[at] = v
        low[at] = (v * inverse_rms(v) * gains[1:2]).astype(BF16)

    half = low.shape[0] // 2
    gather = Gather(low, normed_o, loc, gs, gr)
    for name in scatter_steps(p, residual, *scatter_refs, prepare=prepare):
        if name == "late":
            advance()
        if name == "low half":
            waits(loads[2:])
            rows_loop(half, body)
            gather.begin_half(0)
        if name == "high half":
            rows_loop(half, body, half)
            gather.begin_half(1)
    keeps = starts(local_copies(((residual, residual_o),), keep_s))
    gather.middle()
    advance()
    gather.end()
    waits(keeps)
    while started[0] < length - 1:
        advance()
    hops.arrive(length - 1)
    hops.finish()
    late_hops.arrive(1)
    late_hops.finish(1, 1)


def middle(mixed, mixer, inputs, gains, w, late, length, collective_id):
    rows, width = inputs.shape
    return pl.pallas_call(
        functools.partial(middle_kernel, length),
        out_shape=(
            jax.ShapeDtypeStruct((rows, width), F32),
            jax.ShapeDtypeStruct((8, rows, width), BF16),
            jax.ShapeDtypeStruct(w.shape, w.dtype),
            jax.ShapeDtypeStruct(late.shape, late.dtype),
        ),
        in_specs=[ANY] * 6,
        out_specs=(ANY,) * 4,
        scratch_shapes=scatter_scratch(rows // 2, width)
        + [pltpu.VMEM((8, rows, width), BF16), pltpu.VMEM((rows, width), BF16), DMA, DMA((14,)), DMA((14,))]
        + [DMA((2, length))] * 4
        + held(mixed, mixer, inputs, gains)
        + [pltpu.VMEM((rows, width), F32), DMA((4,)), DMA((1,))],
        input_output_aliases={4: 2, 5: 3},
        compiler_params=params(collective_id),
        cost_estimate=pl.CostEstimate(flops=0, bytes_accessed=300 * 2**20, transcendentals=0),
    )(mixed, mixer, inputs, gains, w, late)


def turn_kernel(length, cuts, p, residual_in, above_in, gains_in, mixer_in, *refs):
    parts = 1 + max(cut[0] for cut in cuts)
    terms, refs = refs[:parts], refs[parts:]
    back_o, gain, low_o, dmix_o, sums, squares, *scratch = refs
    scatter_refs, scratch = scratch[:SCATTER_REFS], scratch[SCATTER_REFS:]
    total, low, loc, gs, gr, parts_in, load_s, residual, above, gains, mixer, back, dmix, in_s, keep_s = scratch[:15]
    line_refs = scratch[15:]
    loads = local_copies(
        ((residual_in, residual), (above_in, above), (gains_in, gains), (mixer_in, mixer)), in_s
    )
    greet(gather_peers() + line_neighbours(length))
    line = Lines(terms, cuts, length, line_refs)
    line.begin()
    starts(loads)
    gain[...] = jnp.zeros_like(gain)

    def body(at):
        grad, gain_part = norm_rows_back(residual[at], gains[1:2], total[at])
        grad = above[at].astype(F32) + grad
        back[at] = grad
        low[at] = grad.astype(BF16)
        gain[...] += gain_part

    half = low.shape[0] // 2
    gather = Gather(low, low_o, loc, gs, gr)
    for name in scatter_steps(p, total, *scatter_refs):
        if name in ("early", "late"):
            line.start()
        if name == "low half":
            waits(loads)
            rows_loop(half, body)
            gather.begin_half(0)
        if name == "high half":
            rows_loop(half, body, half)
            gather.begin_half(1)
            line.start()
    keeps = starts(local_copies(((back, back_o),), keep_s))
    rows = low.shape[0]
    part = mixer.shape[1] // 3
    y, c, z, x = place()
    near = (gather.me, gather.bx), (gather.by, rank(y, 1 - c, x))
    rest = (gather.bd, rank(1 - y, 1 - c, x)), (rank(y, 1 - c, 1 - x), rank(1 - y, 1 - c, 1 - x))

    def fetch(blocks, slot):
        copies = []
        for n in (0, 1):
            copies.append(
                pltpu.make_async_copy(low_o.at[blocks[n]], parts_in.at[slot, n], load_s.at[slot, n])
            )
        return copies

    def mix(blocks, slot):
        waits(fetch(blocks, slot))
        lines = parts_in[slot].reshape(2 * rows, parts_in.shape[3])
        both = jnp.dot(lines, mixer[:, 2 * part :], preferred_element_type=F32)
        none = jnp.zeros((rows, dmix.shape[2] - part), F32)
        for n in (0, 1):
            dmix[blocks[n]] = jnp.concatenate([both[n * rows : (n + 1) * rows], none], axis=1)
            pltpu.make_async_copy(dmix.at[blocks[n]], dmix_o.at[blocks[n]], keep_s.at[1 + n + 2 * slot]).start()

    def mixed(blocks, slot):
        for n in (0, 1):
            pltpu.make_async_copy(dmix.at[blocks[n]], dmix_o.at[blocks[n]], keep_s.at[1 + n + 2 * slot]).wait()

    def near_blocks():
        gather.own.wait()
        for copy in gather.last[:2]:
            copy.wait_recv()
        starts(fetch(near[0], 0))
        starts(fetch(near[1], 1))
        mix(near[0], 0)
        mix(near[1], 1)

    gather.middle()
    line.start()
    gather.relays(near_blocks)
    gather.finish(2, own=False)
    for n in (0, 1):
        mixed(near[n], n)
        starts(fetch(rest[n], n))
    for n in (0, 1):
        mix(rest[n], n)
    waits(keeps)
    line.end(sums, squares)
    for n in (0, 1):
        mixed(rest[n], n)


def turn(p, residual, above, gains, mixer, rc, terms, cuts, length, collective_id):
    rows, width = residual.shape
    line_rows, columns = terms[0].shape[1], sum(cut[2] for cut in cuts)
    return pl.pallas_call(
        functools.partial(turn_kernel, length, cuts),
        out_shape=(
            jax.ShapeDtypeStruct((rows, width), F32),
            jax.ShapeDtypeStruct((8, width), F32),
            jax.ShapeDtypeStruct((8, rows, width), BF16),
            jax.ShapeDtypeStruct((8, rows, rc), F32),
            jax.ShapeDtypeStruct((line_rows, columns), BF16),
            TILE,
        ),
        in_specs=[ANY] * (5 + len(terms)),
        out_specs=(ANY, VM, ANY, ANY, VM, VM),
        scratch_shapes=scatter_scratch(rows // 2, width)
        + [pltpu.VMEM((rows, width), F32), pltpu.VMEM((rows, width), BF16), DMA, DMA((14,)), DMA((14,))]
        + [pltpu.VMEM((2, 2, rows, width), BF16), DMA((2, 2))]
        + held(residual, above, gains, mixer)
        + [pltpu.VMEM((rows, width), F32), pltpu.VMEM((8, rows, rc), F32), DMA((4,)), DMA((5,))]
        + lines_scratch(length, line_rows, cuts),
        compiler_params=params(collective_id),
        cost_estimate=pl.CostEstimate(flops=0, bytes_accessed=300 * 2**20, transcendentals=0),
    )(p.reshape(8, rows, width), residual, above, gains, mixer, *terms)


def closing_kernel(
    length, x_in, dmz_in, dproj_in, mixed_in, mixer_in, q, residual_in, block, inputs_in, above_in, gains_in, gp_in,
    grad_out, gain, gates_o, out_out, e_o, early_o, sums, squares,
    early_sums, early_l, early_s, early_r, x_part, dmz_part, g, back, total, o, up_a, down_a, up_b, down_b, gp_got, gp_sum,
    ls, lr, load_s, loc, es, er, gate_s, gate_r, move_s, move_r,
    dproj, mixed, mixer, residual, inputs, above, gains, gp, in_s, keep_s,
    mine, sib_q, got_q, loc_q, ss_q, rs_q, sib_p, got_p, ss_p, rs_p,
):
    inflow = starts(
        local_copies(
            (
                (gp_in, gp), (dproj_in, dproj), (mixed_in, mixed), (mixer_in, mixer), (residual_in, residual),
                (inputs_in, inputs), (above_in, above), (gains_in, gains),
            ),
            in_s,
        )
    )
    y, c, z, x = place()
    others = line_peers(length)
    s = 2 * z + x
    owner = x * length + z
    to_z = owner // 2
    to_x = owner - 2 * to_z
    from_z, from_x = lax.rem(s, length), s // length
    moves = jnp.where(jnp.logical_and(to_z == z, to_x == x), 0, 1)
    barrier = pltpu.get_barrier_semaphore()
    for peer in others + plane_peers():
        pl.semaphore_signal(barrier, inc=1, device_id=peer, device_id_type=MESH)

    @pl.when(moves == 1)
    def _():
        pl.semaphore_signal(barrier, inc=1, device_id=device(y, c, to_z, to_x), device_id_type=MESH)
        pl.semaphore_signal(barrier, inc=1, device_id=device(y, c, from_z, from_x), device_id_type=MESH)

    pl.semaphore_wait(barrier, len(others) + 7 + 2 * moves)
    model = mixer.shape[0]
    tokens = dproj.shape[0]
    part = mixed.shape[1]
    columns = x_part.shape[2]
    steps = model // columns
    rows, width = residual.shape
    half = rows // 2
    line_rows = g.shape[1]

    def loads(i, slot):
        at = pl.ds(pl.multiple_of(i * columns, columns), columns)
        return (
            pltpu.make_async_copy(x_in.at[:, at], x_part.at[slot], load_s.at[0, slot]),
            pltpu.make_async_copy(dmz_in.at[:, at], dmz_part.at[slot], load_s.at[1, slot]),
        )

    group = steps // 4
    order = (3, 1, 2, 0)

    def fetch(i, slot):
        for copy in loads(i, slot):
            copy.start()

    fetch(order[0] * group, 0)
    inflow[0].wait()
    gate = [
        remote(gp.at[lax.rem(z + k + 1, length)], gp_got.at[k], gate_s.at[k], gate_r.at[k], others[k])
        for k in range(length - 1)
    ]
    split = up_a.shape[2]
    line_a = HeldLine(g, 0, up_a, down_a, ls.at[0], lr.at[0])
    line_b = HeldLine(g, split, up_b, down_b, ls.at[1], lr.at[1])
    queue = [chain for _ in range(1, length) for chain in (line_a, line_b)]

    def advance(times=1):
        for _ in range(times):
            if queue:
                queue.pop(0).start()

    output = scatter_steps(q, total, mine, sib_q, None, got_q, loc_q, ss_q, rs_q)
    next(output)
    copies, own = exchange_steps(block, e_o, loc, es, er)

    def compute(n, start=0, stop=None):
        @pl.loop(start, group if stop is None else stop)
        def _(j):
            count = n * group + j
            slot = count - count // 2 * 2
            i = order[n] * group + j

            @pl.when(j + 1 < group)
            def _():
                fetch(i + 1, 1 - slot)

            if n < 3:

                @pl.when(j + 1 == group)
                def _():
                    fetch(order[n + 1] * group, 1 - slot)

            for copy in loads(i, slot):
                copy.wait()
            front = contract_first(x_part[slot], dproj[...])
            tail = contract_first(dmz_part[slot], mixed[...])
            k = i * columns // line_rows
            at = pl.ds(pl.multiple_of(i * columns - k * line_rows, columns), columns)
            g[k, at] = jnp.concatenate([front, tail], axis=1).astype(BF16)

    waits(inflow[1:4])
    compute(0, 0, group // 2)
    next(output)
    compute(0, group // 2)
    compute(1)
    if length == 4:
        advance(2)
    next(output)

    @pl.loop(0, 8)
    def _(i):
        lines = dproj[pl.ds(pl.multiple_of(i * rows, rows), rows)]
        back[i] = contract_last(lines, mixer[:, : 2 * part]).astype(BF16)

    incoming = scatter_steps(back, o, None, sib_p, None, got_p, None, ss_p, rs_p)
    next(incoming)
    next(output)
    next(incoming)
    compute(2)
    advance(1 if length == 4 else 0)
    for _ in output:
        pass
    next(incoming)
    compute(3)
    advance(1 if length == 4 else 2)
    pair = width // (4 * length)
    waits(inflow[4:])
    keeps = []
    for n in (0, 1):

        def finish_output(at):
            whole = pl.ds(pl.multiple_of(at.start + n * half, 16), 16)
            store_turned(mine.at[0, n], at, (residual[whole] + total[whole]).astype(BF16), length, pair)

        rows_loop(half, finish_output)
        keeps.append(
            pltpu.make_async_copy(mine.at[0, n], out_out.at[pl.ds(n * half, half)], keep_s.at[n])
        )
        keeps[n].start()
    keeps.append(pltpu.make_async_copy(above, grad_out, keep_s.at[2]))
    advance()
    for copy in gate:
        copy.wait()
    rows_sum = gp[z]
    for k in range(length - 1):
        rows_sum = rows_sum + gp_got[k]
    gp_sum[...] = rows_sum
    move = pltpu.make_async_remote_copy(
        src_ref=gp_sum, dst_ref=gates_o, send_sem=move_s, recv_sem=move_r,
        device_id=device(y, c, to_z, to_x), device_id_type=MESH,
    )
    pl.when(moves == 1)(lambda: move.start())

    @pl.when(moves == 0)
    def _():
        gates_o[...] = rows_sum

    gain[...] = jnp.zeros_like(gain)

    def finish_grad(at):
        grad, gain_part = norm_rows_back(inputs[at].astype(F32), gains[0:1], o[at])
        store_turned(above, at, above[at] + grad, length, pair)
        gain[...] += gain_part

    for name in incoming:
        if name == "late":
            advance()
        if name == "low half":
            rows_loop(half, finish_grad)
        if name == "high half":
            rows_loop(half, finish_grad, half)
            keeps[2].start()
    while queue:
        advance()
    squares[...] = jnp.zeros_like(squares)
    line_a.end(early_sums, 0, squares)
    early_copies, early_own = exchange_steps(early_sums, early_o, early_l, early_s, early_r)
    line_b.end(sums, 0, squares)
    pl.when(moves == 1)(lambda: move.wait())
    waits(keeps)
    for copy in copies + early_copies:
        copy.wait()
    own.wait()
    early_own.wait()


def closing(x, dmz, dproj, mixed, mixer, q, residual, block, inputs, above, gains, gp, length, collective_id):
    rows, width = residual.shape
    tokens, model = x.shape
    part = mixed.shape[1]
    share = block.shape[0] // 8
    block = block.reshape(8, share, block.shape[1])
    line_rows = model // length
    columns = min(256, line_rows)
    split = -(-3 * part // 256) * 128
    slots_a, slots_b = (pltpu.VMEM((length - 1, line_rows, n), BF16) for n in (split, 3 * part - split))
    pack = gp.shape[1:]
    return pl.pallas_call(
        functools.partial(closing_kernel, length),
        out_shape=(
            jax.ShapeDtypeStruct((rows, width), F32),
            jax.ShapeDtypeStruct((8, width), F32),
            jax.ShapeDtypeStruct(pack, F32),
            jax.ShapeDtypeStruct((rows, width), BF16),
            jax.ShapeDtypeStruct(block.shape, BF16),
            jax.ShapeDtypeStruct((8, share, split), BF16),
            jax.ShapeDtypeStruct((line_rows, 3 * part - split), BF16),
            TILE,
        ),
        in_specs=[ANY] * 12,
        out_specs=(ANY, VM, VM, ANY, ANY, ANY, VM, VM),
        scratch_shapes=[
            pltpu.VMEM((line_rows, split), BF16), DMA, DMA((7,)), DMA((7,)),
            pltpu.VMEM((2, tokens, columns), BF16),
            pltpu.VMEM((2, tokens, columns), BF16),
            pltpu.VMEM((length, line_rows, 3 * part), BF16),
            pltpu.VMEM((8, rows, width), BF16),
            pltpu.VMEM((rows, width), F32),
            pltpu.VMEM((rows, width), F32),
            slots_a, slots_a, slots_b, slots_b,
            pltpu.VMEM((length - 1,) + pack, F32),
            pltpu.VMEM(pack, F32),
            DMA((2, 2, length)), DMA((2, 2, length)), DMA((2, 2)),
            DMA, DMA((7,)), DMA((7,)), DMA((length,)), DMA((length,)), DMA, DMA,
            *held(dproj, mixed, mixer, residual, inputs, above, gains, gp),
            DMA((8,)), DMA((3,)),
            pltpu.VMEM((4, 2, rows // 2, width), BF16),
            pltpu.VMEM((4, 2, rows // 2, width), BF16),
            pltpu.VMEM((6, rows // 2, width), BF16),
            DMA((8,)), DMA((14,)), DMA((14,)),
            pltpu.VMEM((4, 2, rows // 2, width), BF16),
            pltpu.VMEM((6, rows // 2, width), BF16),
            DMA((14,)), DMA((14,)),
        ],
        compiler_params=params(collective_id),
        cost_estimate=pl.CostEstimate(
            flops=10 * tokens * model * dproj.shape[1] // 2, bytes_accessed=350 * 2**20, transcendentals=0
        ),
    )(x, dmz, dproj, mixed, mixer, q.reshape(8, rows, width), residual, block, inputs, above, gains, gp)


def first_kernel(
    length, inputs_in, above_in, mixer_in, mlp_in, gains_in, gate_in, chan_in,
    normed_o, wm_o, wf_o, wd_o, w2_o, gains_o, gate_o, chan_o, inputs_o, above_o,
    inputs, above, mixer_w, mlp_w, gains_w, gate_w, chan_w, load_s,
    inputs_k, above_k, w2, keep_s, gp_o, gn, gp, normed, gn_all, wm, wf, wd, loc, ms, mr, fs, fr, line_s, line_r, gain_s, gain_r, move_s, move_r,
    gather_s, gather_r, hop_s, hop_r,
):
    loads = [
        pltpu.make_async_copy(src, dst, load_s.at[n])
        for n, (src, dst) in enumerate(
            (
                (gains_in, gains_w), (gate_in, gate_w), (chan_in, chan_w), (mixer_in, mixer_w),
                (mlp_in, mlp_w), (inputs_in, inputs), (above_in, above),
            )
        )
    ]
    for copy in loads:
        copy.start()
    y, c, z, x = place()
    s = 2 * z + x
    me = rank(y, c, x)
    rows, width = inputs.shape
    pair = width // (4 * length)
    line = line_peers(length)
    plane = plane_peers()
    to_z, to_x = lax.rem(s, length), s // length
    moves = jnp.where(jnp.logical_and(to_z == z, to_x == x), 0, 1)
    src = x * length + z
    from_z = src // 2
    from_x = src - 2 * from_z
    barrier = pltpu.get_barrier_semaphore()
    for peer in line + plane:
        pl.semaphore_signal(barrier, inc=1, device_id=peer, device_id_type=MESH)

    @pl.when(moves == 1)
    def _():
        pl.semaphore_signal(barrier, inc=1, device_id=device(y, c, to_z, to_x), device_id_type=MESH)
        pl.semaphore_signal(barrier, inc=1, device_id=device(y, c, from_z, from_x), device_id_type=MESH)

    def fill(pack, source, js, offset=0):
        part = pack.shape[2] // len(js)
        whole = source.shape[1] // 24
        for t in range(8):
            for n, j in enumerate(js):
                start = (j * 8 + t) * whole + offset
                pack[t, :, n * part : (n + 1) * part] = source[:, start : start + part].astype(BF16)

    loads[3].wait()
    fill(wm, mixer_w, (0, 1, 2))
    for copy in loads[:3]:
        copy.wait()
    share = gains_w.shape[1]
    gn[...] = jnp.zeros_like(gn)
    for n in (0, 1):

        @pl.when(x == n)
        def _():
            gn[:2, n * share : (n + 1) * share] = gains_w[...]

    gp[...] = jnp.zeros_like(gp)
    channels = contract_first(chan_w[...].astype(BF16), unit(8))
    gp[: gate_w.shape[0]] = jnp.concatenate(
        [
            gate_w[...],
            channels,
            jnp.zeros((gate_w.shape[0], gp.shape[1] - gate_w.shape[1] - 8), F32),
        ],
        axis=1,
    ).astype(BF16)
    gn_all[me, z] = gn[...]
    pl.semaphore_wait(barrier, len(line) + len(plane) + 2 * moves)
    gains = [
        remote(gn, gn_all.at[me, z], line_s.at[0, k], line_r.at[0, k], line[k]) for k in range(length - 1)
    ]
    gate_move = pltpu.make_async_remote_copy(
        src_ref=gp, dst_ref=gp_o.at[to_z], send_sem=move_s, recv_sem=move_r,
        device_id=device(y, c, to_z, to_x), device_id_type=MESH,
    )
    gate_stay = pltpu.make_async_copy(gp, gp_o.at[z], loc.at[2])
    pl.when(moves == 1)(lambda: gate_move.start())
    pl.when(moves == 0)(lambda: gate_stay.start())

    mixer, mixer_own = exchange_steps(wm, wm_o.at[0], loc.at[0], ms, mr)
    hops = LineGather(wm_o, length, hop_s, hop_r)
    mixer_own.wait()
    hops.start_piece(me)

    def pass_piece(n):
        fy, fc, fx = FLIPS[n]
        mixer[n].wait_recv()
        hops.start_piece(rank(flip(y, fy), flip(c, fc), flip(x, fx)))

    pass_piece(1)
    for copy in gains:
        copy.wait()
    spread = [
        remote(gn_all.at[me], gn_all.at[me], gain_s.at[n], gain_r.at[n], plane[n]) for n in range(7)
    ]
    loads[4].wait()
    fill(wd, mlp_w, (2,))
    down, down_own = exchange_steps(wd, wd_o.at[0], loc.at[4], fs.at[1], fr.at[1])
    for n in (0, 2, 3, 5, 4, 6):
        pass_piece(n)
    fill(wf, mlp_w, (0, 1))
    feed, feed_own = exchange_steps(wf, wf_o.at[0], loc.at[3], fs.at[0], fr.at[0])
    pl.when(moves == 1)(lambda: gate_move.wait())
    pl.when(moves == 0)(lambda: gate_stay.wait())
    gates = [
        remote(gp_o.at[z], gp_o.at[z], line_s.at[1, k], line_r.at[1, k], line[k])
        for k in range(length - 1)
    ]
    fill(w2, mlp_w, (0, 1, 2), wd.shape[2])
    for copy in spread:
        copy.wait()
    for k in range(length):
        other = lax.rem(z + k, length)
        for b in range(4):
            at = slice((4 * k + b) * pair, (4 * k + b + 1) * pair)
            tile = (gn_all[2 * b, other] + gn_all[2 * b + 1, other])[:, :pair]
            gains_o[:, at] = tile.astype(BF16).astype(F32)
    for copy in mixer:
        copy.wait_send()

    def body(at):
        v = load_turned(inputs, at, length, pair)
        inputs_k[at] = v
        v = v.astype(F32)
        normed[at] = (v * inverse_rms(v) * gains_o[0:1]).astype(BF16)
        above_k[at] = load_turned(above, at, length, pair)

    for copy in loads[5:]:
        copy.wait()
    half = rows // 2
    gather = Gather(normed, normed_o, loc.at[1], gather_s, gather_r)
    rows_loop(half, body)
    gather.begin_half(0)
    hops.arrive(1)
    if length > 2:
        hops.start(2)
    rows_loop(half, body, half)
    gather.begin_half(1)
    keeps = starts(local_copies(((inputs_k, inputs_o), (above_k, above_o)), keep_s))
    for copy in gates:
        copy.wait()
    gate_rows, columns = gate_w.shape
    head = columns // 2
    own = jnp.concatenate([gp_o[n, :gate_rows].astype(F32) for n in range(length)]).astype(BF16)
    part, rc = own.shape[0], gate_o.shape[0]
    gate_o[...] = jnp.zeros_like(gate_o)
    for first_row in range(0, part, head):
        at = slice(first_row, first_row + head)
        wide = [jnp.zeros((head, first_row), F32)] if first_row else []
        for n in (0, 1):
            block = own[at, n * head : (n + 1) * head].astype(F32)
            rest = jnp.zeros((head, rc - first_row - head), F32)
            gate_o[at, n * rc : (n + 1) * rc] = jnp.concatenate([*wide, block, rest], axis=1).astype(BF16)
    rows_of = contract_last(unit(8), own[:, columns : columns + 8])
    lam = rows_of[7:8]
    u = jnp.exp(-jnp.abs(lam))
    t = u / (2.0 + u)
    series = jnp.full_like(t, 1.0 / 17.0)
    for n in range(15, 0, -2):
        series = series * t * t + 1.0 / n
    rate = 8.0 * (jnp.maximum(-lam, 0.0) + 2.0 * t * series)
    fill_rows = jnp.concatenate([jnp.zeros((7, rc - part), F32), jnp.ones((1, rc - part), F32)])
    chan_o[...] = jnp.concatenate([jnp.concatenate([rows_of[:7], rate]), fill_rows], axis=1)
    if length > 3:
        hops.arrive(2)
        hops.start(3)
    gather.middle()
    late, late_own = exchange_steps(w2, w2_o.at[0], loc.at[0], fs.at[2], fr.at[2])
    gather.relays()
    for hop in range(min(3, length - 1), length):
        hops.arrive(hop)
        if hop + 1 < length:
            hops.start(hop + 1)
    gather.finish()
    waits(keeps)
    for copy in down + feed + late:
        copy.wait()
    late_own.wait()
    down_own.wait()
    feed_own.wait()
    hops.finish()


def early(f8):
    return f8 // 384 * 256


def unit(n):
    return (
        lax.broadcasted_iota(jnp.int32, (n, n), 0) == lax.broadcasted_iota(jnp.int32, (n, n), 1)
    ).astype(BF16)


def first(inputs, above, mixer, mlp, gains, gate, chan, rc, length, collective_id):
    rows, width = inputs.shape
    pack = (-(-gate.shape[0] // 16) * 16, rc)
    share = mixer.shape[0]
    f8 = mlp.shape[1] // 24
    wm, wf, wd, w2 = (
        (8, share, n) for n in (mixer.shape[1] // 8, 2 * early(f8), early(f8), 3 * (f8 - early(f8)))
    )
    low = jax.ShapeDtypeStruct((rows, width), BF16)
    return pl.pallas_call(
        functools.partial(first_kernel, length),
        out_shape=(
            jax.ShapeDtypeStruct((8, rows, width), BF16),
            jax.ShapeDtypeStruct((length,) + wm, BF16),
            jax.ShapeDtypeStruct((length,) + wf, BF16),
            jax.ShapeDtypeStruct((length,) + wd, BF16),
            jax.ShapeDtypeStruct((length,) + w2, BF16),
            jax.ShapeDtypeStruct((8, width), F32),
            jax.ShapeDtypeStruct((rc, 2 * rc), BF16),
            jax.ShapeDtypeStruct((8, rc), F32),
            low,
            low,
        ),
        in_specs=[ANY] * 7,
        out_specs=(ANY, ANY, ANY, ANY, ANY, VM, VM, VM, ANY, ANY),
        scratch_shapes=[
            *[pltpu.VMEM(v.shape, v.dtype) for v in (inputs, above, mixer, mlp, gains, gate, chan)],
            DMA((7,)),
            pltpu.VMEM((rows, width), BF16),
            pltpu.VMEM((rows, width), BF16),
            pltpu.VMEM(w2, BF16),
            DMA((2,)),
            pltpu.VMEM((length,) + pack, BF16),
            pltpu.VMEM((8, 128), F32),
            pltpu.VMEM(pack, BF16),
            pltpu.VMEM((rows, width), BF16),
            pltpu.VMEM((8, length, 8, 128), F32),
            pltpu.VMEM(wm, BF16),
            pltpu.VMEM(wf, BF16),
            pltpu.VMEM(wd, BF16),
            DMA((5,)), DMA((7,)), DMA((7,)), DMA((3, 7)), DMA((3, 7)),
            DMA((2, length)), DMA((2, length)), DMA((7,)), DMA((7,)), DMA, DMA,
            DMA((14,)), DMA((14,)), DMA((2, length)), DMA((2, length)),
        ],
        compiler_params=params(collective_id),
        cost_estimate=pl.CostEstimate(flops=0, bytes_accessed=300 * 2**20, transcendentals=0),
    )(inputs, above, mixer, mlp, gains, gate, chan)


def last_kernel(
    length, share, wm, gain, gain_two, gates, sq_a, sq_b, sq_c, sq_d,
    wm_o, gains_o, norm_o, factor_o, by_plane, by_line, loc, ss, rs, gs, gr, ls, lr,
):
    y, c, z, x = place()
    me = rank(y, c, x)
    line = line_peers(length)
    plane = plane_peers()
    width = gain.shape[1]
    pair = width // (4 * length)
    squares = sq_a[...] + sq_b[...] + sq_c[...] + sq_d[...] + tile_of_squares(gates[...])
    squares = jnp.concatenate([squares, jnp.zeros((8, width - 128), F32)], axis=1)
    rows = [jnp.sum(v, axis=0, keepdims=True) for v in (gain[...], gain_two[...], squares)]
    by_plane[me] = jnp.concatenate(rows + [jnp.zeros((1, width), F32)])
    greet(line + plane)
    sends = [
        remote(by_plane.at[me], by_plane.at[me], gs.at[n], gr.at[n], plane[n]) for n in range(7)
    ]
    copies, own = exchange_steps(wm, wm_o, loc, ss, rs)
    for copy in sends:
        copy.wait()
    total = by_plane[0]
    for n in range(1, 8):
        total = total + by_plane[n]
    group = 4 * pair
    for k in range(length):
        at = pl.ds(pl.multiple_of(lax.rem(z + k, length) * group, group), group)
        by_line[z, :, at] = total[:, k * group : (k + 1) * group]
    sends = [
        remote(by_line.at[z], by_line.at[z], ls.at[k], lr.at[k], line[k]) for k in range(length - 1)
    ]
    for copy in sends:
        copy.wait()
    total = by_line[0]
    for n in range(1, length):
        total = total + by_line[n]
    squares = jnp.sum(total[:2] * total[:2], axis=0, keepdims=True) + total[2:3]
    norm = jnp.broadcast_to(jnp.sqrt(jnp.sum(squares, axis=1, keepdims=True)), (8, 128))
    norm_o[...] = norm
    factor_o[...] = clip_limit / jnp.maximum(norm, clip_limit)
    gains = jnp.zeros((2, pair), F32)
    for there in range(length):
        for b in range(4):
            first_lane = (there * 4 + b) * pair
            mine = jnp.logical_and(there == z, b == 2 * y + c)
            gains = jnp.where(mine, total[:2, first_lane : first_lane + pair], gains)
    gains_o[...] = jnp.where(x == 0, gains[:, :share], gains[:, share:])
    for copy in copies:
        copy.wait()
    own.wait()


def last(wm, gain, gain_two, gates, squares, length, collective_id):
    width = gain.shape[1]
    share = wm.shape[1]
    return pl.pallas_call(
        functools.partial(last_kernel, length, share),
        out_shape=(
            jax.ShapeDtypeStruct(wm.shape, wm.dtype),
            jax.ShapeDtypeStruct((2, share), F32),
            TILE, TILE,
        ),
        in_specs=[ANY] + [VM] * 7,
        out_specs=(ANY,) + (VM,) * 3,
        scratch_shapes=[
            pltpu.VMEM((8, 4, width), F32),
            pltpu.VMEM((length, 4, width), F32),
            DMA, DMA((7,)), DMA((7,)), DMA((7,)), DMA((7,)),
            DMA((length,)), DMA((length,)),
        ],
        compiler_params=params(collective_id),
    )(wm, gain, gain_two, gates, *squares)


def minus_expm1(v):
    series = 1.0 + v * (1.0 / 8.0)
    for n in (7.0, 6.0, 5.0, 4.0, 3.0, 2.0):
        series = 1.0 + series * v * (1.0 / n)
    return jnp.where(v > -0.5, -v * series, 1.0 - jnp.exp(v))


def gelu_parts(v):
    square = v * v
    h = 0.5 * jnp.tanh(v * (GELU_CUBE * square + GELU_SCALE)) + 0.5
    return v * h, h, square


def gelu_slope(gelu, h, square):
    return h + gelu * (1.0 - h) * (6.0 * GELU_CUBE * square + 2.0 * GELU_SCALE)


CHUNK = 128


def forward_kernel(
    length, x_in, mixer_in, gate, chan, above, w_in,
    mixed, branch_o, decay_o, width_o, recur_o, enter_o, conv_o, xe_o, se_o, ends_o, above_o, w,
    x_part, pre, loc_h, ends, carry, hs, hr, es, er, gather_l, gather_s, gather_r, hop_s, hop_r, load_s, keep_s, mixer,
    branch, decay_k, width_k, recur_k, enter_k, conv_k, xe, se,
):
    keeps = [
        pltpu.make_async_copy(src, dst, keep_s.at[n])
        for n, (src, dst) in enumerate(
            (
                (branch, branch_o), (decay_k, decay_o), (width_k, width_o), (recur_k, recur_o),
                (enter_k, enter_o), (conv_k, conv_o), (xe, xe_o), (se, se_o),
            )
        )
    ]
    y, c, z, x = place()
    line = line_peers(length)
    seqs, span, rc = branch.shape
    part = mixed.shape[2]
    chunks = span // CHUNK

    def load(b, slot):
        at = pl.ds(pl.multiple_of(b * span, span), span)
        return pltpu.make_async_copy(x_in.at[at], x_part.at[slot], load_s.at[slot])

    load(0, 0).start()
    mixer_load = pltpu.make_async_copy(mixer_in, mixer, load_s.at[2])
    mixer_load.start()
    greet(line + gather_peers())
    hops = LineGather(w, length, hop_s, hop_r)
    hops.start(1)
    gather = Gather(above, above_o, gather_l, gather_s, gather_r)
    gather.begin()

    mixer_load.wait()

    @pl.loop(0, seqs)
    def _(b):
        slot = b - b // 2 * 2

        @pl.when(b + 1 < seqs)
        def _():
            load(b + 1, 1 - slot).start()

        load(b, slot).wait()
        both = jnp.dot(x_part[slot], mixer[:, : 2 * part], preferred_element_type=F32)
        none = jnp.zeros((span, rc - part), F32)
        branch[b] = jnp.concatenate([both[:, :part], none], axis=1)
        low = both[:, part:].astype(BF16).astype(F32)
        xe[b, 8:] = jnp.concatenate([low, none], axis=1)

    ahead = device(y, c, lax.rem(z + 1, length), x)
    halo = remote(xe.at[:, pl.ds(span, 8)], xe.at[:, pl.ds(0, 8)], hs, hr, ahead)

    def coefficients(b, chunk):
        r = pl.multiple_of(chunk * CHUNK, CHUNK)
        at = pl.ds(r, CHUNK)
        window = xe[b, pl.ds(r, CHUNK + 8)]
        total = chan[4:5] + chan[0:1] * window[8:]
        for k in (1, 2, 3):
            total = total + chan[k : k + 1] * pltpu.roll(window, k, 0)[8:]
        low = total.astype(BF16)
        conv_k[b, at] = low
        value = low.astype(F32)
        gates = jnp.dot(low, gate[...], preferred_element_type=F32)
        recur = jax.nn.sigmoid(gates[:, :rc] + chan[5:6])
        enter = jax.nn.sigmoid(gates[:, rc:] + chan[6:7])
        log_decay = -chan[7:8] * recur
        decay = jnp.exp(log_decay)
        width = jnp.sqrt(minus_expm1(2.0 * log_decay))
        recur_k[b, at] = recur
        enter_k[b, at] = enter
        decay_k[b, at] = decay
        width_k[b, at] = width
        loc_h[b, at] = width * enter * value

    def later_chunks(i):
        b = i // (chunks - 1)
        coefficients(b, 1 + i - b * (chunks - 1))

    many = seqs * (chunks - 1)
    pl.loop(0, many // 2)(later_chunks)
    hops.arrive(1)
    if length > 2:
        hops.start(2)
    gather.middle()
    pl.loop(many // 2, many)(later_chunks)
    halo.wait()

    @pl.when(z == 0)
    def _():
        xe[:, 0:8] = jnp.zeros((seqs, 8, rc), F32)

    @pl.loop(0, seqs)
    def _(b):
        coefficients(b, 0)

    for copy in keeps[:-1]:
        copy.start()
    row = lax.broadcasted_iota(jnp.int32, (8, rc), 0)

    def tile(i, held):
        at = pl.ds(pl.multiple_of(i * 8, 8), 8)
        new = []
        for b in range(seqs):
            a, h = decay_k[b, at], loc_h[b, at]
            for n in (1, 2, 4):
                keep = row >= n
                h = h + jnp.where(keep, a * pltpu.roll(h, n, 0), 0.0)
                a = jnp.where(keep, a * pltpu.roll(a, n, 0), a)
            h = h + a * held[b][1]
            a = a * held[b][0]
            loc_h[b, at] = h
            pre[b, at] = a
            new.append((a[7:8], h[7:8]))
        return tuple(new)

    one, zero = jnp.ones((1, rc), F32), jnp.zeros((1, rc), F32)
    final = lax.fori_loop(0, span // 8, tile, ((one, zero),) * seqs)
    for b in range(seqs):
        ends[z, 0, b] = jnp.broadcast_to(final[b][0], (8, rc))
        ends[z, 1, b] = jnp.broadcast_to(final[b][1], (8, rc))
        ends_o[b] = jnp.broadcast_to(final[b][0], (8, rc))
    moves = [remote(ends.at[z], ends.at[z], es.at[k], er.at[k], line[k]) for k in range(length - 1)]
    if length > 3:
        hops.arrive(2)
        hops.start(3)
    for copy in moves:
        copy.wait()
    carry[...] = jnp.zeros_like(carry)
    for k in range(length):
        carry[...] = jnp.where(k < z, ends[k, 0] * carry[...] + ends[k, 1], carry[...])

    for b in range(seqs):
        se[b, 0:8] = carry[b]

    @pl.loop(0, seqs * chunks)
    def _(i):
        b = i // chunks
        r = pl.multiple_of((i - b * chunks) * CHUNK, CHUNK)
        at = pl.ds(r, CHUNK)
        state = loc_h[b, at] + pre[b, at] * carry[b, 0:1]
        se[b, pl.ds(r + 8, CHUNK)] = state
        gelu, _, _ = gelu_parts(branch[b, at])
        mixed[b, at] = (state * gelu)[:, :part].astype(BF16)

    keeps[-1].start()
    gather.end()
    for hop in range(min(3, length - 1), length):
        hops.arrive(hop)
        if hop + 1 < length:
            hops.start(hop + 1)
    hops.finish()
    waits(keeps)


def recur_forward(x, mixer, gate, chan, above, w, length, collective_id):
    rc = gate.shape[0]
    part = mixer.shape[1] // 3
    rows = x.shape[0] // 8
    seqs, span = 4, 2 * rows
    full = jax.ShapeDtypeStruct((seqs, span, rc), F32)
    longer = jax.ShapeDtypeStruct((seqs, span + 8, rc), F32)
    kept = (full, full, full, full, full, jax.ShapeDtypeStruct((seqs, span, rc), BF16), longer, longer)
    return pl.pallas_call(
        functools.partial(forward_kernel, length),
        out_shape=(
            jax.ShapeDtypeStruct((seqs, span, part), BF16),
            *kept,
            jax.ShapeDtypeStruct((seqs, 8, rc), F32),
            jax.ShapeDtypeStruct((8,) + above.shape, above.dtype),
            jax.ShapeDtypeStruct(w.shape, w.dtype),
        ),
        in_specs=[ANY, ANY, VM, VM, ANY, ANY],
        out_specs=(VM,) + (ANY,) * 8 + (VM, ANY, ANY),
        scratch_shapes=[
            pltpu.VMEM((2, span, x.shape[1]), BF16),
            pltpu.VMEM((seqs, span, rc), F32),
            pltpu.VMEM((seqs, span, rc), F32),
            pltpu.VMEM((length, 2, seqs, 8, rc), F32),
            pltpu.VMEM((seqs, 8, rc), F32),
            DMA, DMA, DMA((length,)), DMA((length,)),
            DMA, DMA((14,)), DMA((14,)), DMA((2, length)), DMA((2, length)),
            DMA((3,)), DMA((8,)),
            *held(mixer),
            *[pltpu.VMEM(v.shape, v.dtype) for v in kept],
        ],
        input_output_aliases={5: 11},
        compiler_params=params(collective_id),
        cost_estimate=pl.CostEstimate(
            flops=2 * seqs * span * rc * rc * 2, bytes_accessed=100 * 2**20, transcendentals=0
        ),
    )(x, mixer, gate, chan, above, w)


def backward_kernel(
    length, cuts, head, dmix, gate, chan, decay, width, recur, enter, conv, xe, se, ends_f, proj, block_a, block_b, *refs
):
    parts = 1 + max(cut[0] for cut in cuts)
    terms, refs = refs[:parts], refs[parts:]
    dproj, gates_o, sums, squares, block_ao, block_bo, *refs = refs
    dgate, gchan, *refs = refs
    suffix, grad, de, ends, carry, hs, hr, es, er, keep_s, move_l, move_s, move_r, *refs = refs
    kept, line_refs = refs[:8], refs[8:]
    loads = [
        pltpu.make_async_copy(src, dst, keep_s.at[n])
        for n, (src, dst) in enumerate(
            zip((dmix, proj, se, decay, width, recur, enter, conv, xe), (de.at[:, pl.ds(0, decay.shape[1])], *kept))
        )
    ]
    proj, se, decay, width, recur, enter, conv, xe = kept
    y, c, z, x = place()
    line = line_peers(length)
    greet(line + plane_peers())
    scatter = Lines(terms, cuts, length, line_refs)
    scatter.begin()
    for copy in loads:
        copy.start()
    moves = [
        exchange_steps(block_a, block_ao, move_l.at[0], move_s.at[0], move_r.at[0]),
        exchange_steps(block_b, block_bo, move_l.at[1], move_s.at[1], move_r.at[1]),
    ]
    seqs, span, rc = decay.shape
    part = dproj.shape[2] // 2
    chunks = span // CHUNK
    for copy in loads[:3]:
        copy.wait()

    @pl.loop(0, seqs * chunks)
    def _(i):
        b = i // chunks
        r = pl.multiple_of((i - b * chunks) * CHUNK, CHUNK)
        at = pl.ds(r, CHUNK)
        branch = proj[b, at]
        gelu, h, square = gelu_parts(branch)
        above = de[b, at]
        state = se[b, pl.ds(r + 8, CHUNK)]
        grad[b, at] = above * gelu
        proj[b, at] = above * state * gelu_slope(gelu, h, square)

    loads[3].wait()
    row = lax.broadcasted_iota(jnp.int32, (8, rc), 0)

    def tile(i, held):
        at = pl.ds(pl.multiple_of(span - 8 - i * 8, 8), 8)
        new = []
        for b in range(seqs):
            product, total, following = held[b]
            plain, h = decay[b, at], grad[b, at]
            a = jnp.where(row == 7, following, pltpu.roll(plain, 7, 0))
            for n in (1, 2, 4):
                keep = row < 8 - n
                h = h + jnp.where(keep, a * pltpu.roll(h, 8 - n, 0), 0.0)
                a = jnp.where(keep, a * pltpu.roll(a, 8 - n, 0), a)
            h = h + a * total
            a = a * product
            grad[b, at] = h
            suffix[b, at] = a
            new.append((a[0:1], h[0:1], plain[0:1]))
        return tuple(new)

    one, zero = jnp.ones((1, rc), F32), jnp.zeros((1, rc), F32)
    final = lax.fori_loop(0, span // 8, tile, ((one, zero, one),) * seqs)
    for b in range(seqs):
        ends[z, 0, b] = ends_f[b]
        ends[z, 1, b] = jnp.broadcast_to(final[b][1] * final[b][2], (8, rc))
    tails = [remote(ends.at[z], ends.at[z], es.at[k], er.at[k], line[k]) for k in range(length - 1)]
    for copy in tails:
        copy.wait()
    for copy in loads[4:]:
        copy.wait()
    carry[...] = jnp.zeros_like(carry)
    for k in reversed(range(length)):
        carry[...] = jnp.where(k > z, ends[k, 0] * carry[...] + ends[k, 1], carry[...])

    gchan[...] = jnp.zeros_like(gchan)

    def gradients(b, chunk):
        r = pl.multiple_of(chunk * CHUNK, CHUNK)
        at = pl.ds(r, CHUNK)
        g = grad[b, at] + suffix[b, at] * carry[b, 0:1]
        a, w, ra, ri = decay[b, at], width[b, at], recur[b, at], enter[b, at]
        value = conv[b, at].astype(F32)
        before = pltpu.roll(se[b, pl.ds(r, CHUNK + 8)], 1, 0)[8:]
        dla = g * before * a - g * ri * value * (a * a) / w
        slope = dla * ra * (1.0 - ra)
        dpa = (-chan[7:8] * slope).astype(BF16)
        dpi = (g * w * value * ri * (1.0 - ri)).astype(BF16)
        dgate[b, at, :rc] = dpa
        dgate[b, at, rc:] = dpi
        gchan[5] += fold(dpa.astype(F32))
        gchan[6] += fold(dpi.astype(F32))
        gchan[7] += fold(dla * ra)
        back = lax.dot_general(
            dgate[b, at], gate[...], (((1,), (1,)), ((), ())), preferred_element_type=F32
        )
        dcv = (g * w * ri + back).astype(BF16).astype(F32)
        de[b, at] = dcv
        gchan[4] += fold(dcv)

    pl.loop(0, seqs)(lambda b: gradients(b, 0))
    behind = device(y, c, lax.rem(z + length - 1, length), x)
    halo = remote(de.at[:, pl.ds(0, 8)], de.at[:, pl.ds(span, 8)], hs, hr, behind)
    scatter.start()
    scatter.start()

    @pl.loop(0, seqs * (chunks - 1))
    def _(i):
        b = i // (chunks - 1)
        gradients(b, 1 + i - b * (chunks - 1))

    scatter.start()
    scatter.start()
    halo.wait()
    low = conv[...].reshape(seqs * span, rc)
    recur_grad, enter_grad = (
        contract_first(low, dgate[:, :, at].reshape(seqs * span, rc)) for at in (slice(0, rc), slice(rc, 2 * rc))
    )

    @pl.when(z == length - 1)
    def _():
        de[:, span:] = jnp.zeros((seqs, 8, rc), F32)

    @pl.loop(0, seqs * chunks)
    def _(i):
        b = i // chunks
        r = pl.multiple_of((i - b * chunks) * CHUNK, CHUNK)
        at = pl.ds(r, CHUNK)
        window = de[b, pl.ds(r, CHUNK + 8)]
        inputs = xe[b, pl.ds(r, CHUNK + 8)]
        dcv = window[:CHUNK]
        total = chan[0:1] * dcv
        gchan[0] += fold(dcv * inputs[8:])
        for k in (1, 2, 3):
            total = total + chan[k : k + 1] * pltpu.roll(window, CHUNK + 8 - k, 0)[:CHUNK]
            gchan[k] += fold(dcv * pltpu.roll(inputs, k, 0)[8:])
        dproj[b, at] = jnp.concatenate([proj[b, at, :part], total[:, :part]], axis=1).astype(BF16)

    rates = 8.0 * minus_expm1(chan[7:8] * (-1.0 / 8.0))
    channels = [jnp.sum(gchan[n], axis=0, keepdims=True) for n in range(8)]
    channels[7] = channels[7] * rates
    channels = lax.dot_general(
        jnp.concatenate(channels), unit(8).astype(F32), (((0,), (0,)), ((), ())),
        precision=lax.Precision.HIGHEST, preferred_element_type=F32,
    )
    blocks = []
    for first_row in range(0, part, head):
        at = slice(first_row, first_row + head)
        blocks.append(jnp.concatenate([recur_grad[at, at], enter_grad[at, at]], axis=1))
    pack = jnp.concatenate(
        [jnp.concatenate(blocks), channels[:part], jnp.zeros((part, rc - 2 * head - 8), F32)], axis=1
    )
    rows = part // length
    if rows < gates_o.shape[1]:
        gates_o[...] = jnp.zeros_like(gates_o)
    for n in range(length):
        gates_o[n, :rows] = pack[n * rows : (n + 1) * rows]
    scatter.end(sums, squares)
    for copies, own in moves:
        for copy in copies:
            copy.wait()
        own.wait()


def recur_backward(dmix, gate, chan, kept, part, head, blocks, terms, cuts, length, collective_id):
    proj, decay, width, recur, enter, conv, xe, se, ends = kept
    seqs, span, rc = decay.shape
    gate_pad = -(-(part // length) // 16) * 16
    line_rows, columns = terms[0].shape[1], sum(cut[2] for cut in cuts)
    return pl.pallas_call(
        functools.partial(backward_kernel, length, cuts, head),
        out_shape=(
            jax.ShapeDtypeStruct((seqs, span, 2 * part), BF16),
            jax.ShapeDtypeStruct((length, gate_pad, rc), F32),
            jax.ShapeDtypeStruct((line_rows, columns), BF16), TILE,
            *[jax.ShapeDtypeStruct(block.shape, BF16) for block in blocks],
        ),
        in_specs=[ANY, VM, VM] + [ANY] * 7 + [VM] + [ANY] * (3 + len(terms)),
        out_specs=(VM,) * 4 + (ANY, ANY),
        scratch_shapes=[
            pltpu.VMEM((seqs, span, 2 * rc), BF16),
            pltpu.VMEM((8, 8, rc), F32),
            pltpu.VMEM((seqs, span, rc), F32),
            pltpu.VMEM((seqs, span, rc), F32),
            pltpu.VMEM((seqs, span + 8, rc), F32),
            pltpu.VMEM((length, 2, seqs, 8, rc), F32),
            pltpu.VMEM((seqs, 8, rc), F32),
            DMA, DMA, DMA((length,)), DMA((length,)),
            DMA((9,)), DMA((2,)), DMA((2, 7)), DMA((2, 7)),
            *[
                pltpu.VMEM(shape, dtype)
                for shape, dtype in (
                    (decay.shape, F32), (se.shape, F32), (decay.shape, F32), (decay.shape, F32),
                    (decay.shape, F32), (decay.shape, F32), (decay.shape, BF16), (xe.shape, F32),
                )
            ],
        ]
        + lines_scratch(length, line_rows, cuts),
        compiler_params=params(collective_id),
        cost_estimate=pl.CostEstimate(
            flops=2 * seqs * span * rc * rc * 2, bytes_accessed=120 * 2**20, transcendentals=0
        ),
    )(dmix, gate, chan, decay, width, recur, enter, conv, xe, se, ends, proj, *blocks, *terms)


def contract_last(left, right):
    return lax.dot_general(
        left, right, (((1,), (1,)), ((), ())), preferred_element_type=F32
    )


def contract_first(left, right):
    return lax.dot_general(
        left, right, (((0,), (0,)), ((), ())), preferred_element_type=F32
    )


def resident(shape):
    return pl.BlockSpec(shape, lambda i: (0, 0), pipeline_mode=pl.Buffered(1))


STEPS = 4


def feed_forward(x, above, gate_up, down, hid, dboth):
    f = hid.shape[1]
    both = jnp.dot(x[...], gate_up, preferred_element_type=F32)
    gg, uu = both[:, :f], both[:, f:]
    dhid = jnp.dot(above[...], down, preferred_element_type=F32)
    gelu, h, square = gelu_parts(gg)
    hid[...] = (gelu * uu).astype(BF16)
    dboth[:, :f] = (dhid * uu * gelu_slope(gelu, h, square)).astype(BF16)
    dboth[:, f:] = (dhid * gelu).astype(BF16)


def grads_compute(x, above, hid, dboth, gate_o, up_o, down_o):
    f = hid.shape[1]
    both = contract_first(x[...], dboth[...]).astype(BF16)
    gate_o[...] = both[:, :f]
    up_o[...] = both[:, f:]
    down_o[...] = contract_first(above[...], hid[...]).astype(BF16)


def mlp_specs(tokens, model, f):
    def rows(width):
        return pl.BlockSpec((tokens // STEPS, width), lambda i: (jnp.minimum(i, STEPS - 1), 0))

    columns = pl.BlockSpec((tokens, model // STEPS), lambda i: (0, jnp.maximum(i - STEPS, 0)))
    grads = pl.BlockSpec((model // STEPS, f), lambda i: (jnp.maximum(i - STEPS, 0), 0))
    return rows, columns, grads


def keep_units(step, hid_all, dboth_all, hid, dboth):
    rows = hid.shape[0]
    at = pl.ds(pl.multiple_of(step * rows, rows), rows)
    hid_all[at] = hid[...]
    dboth_all[at] = dboth[...]


def early_mlp_kernel(
    length, x, above, x_columns, above_columns, gate_up, down, w_in,
    hid, dboth, gate_o, up_o, down_o, w, hid_all, dboth_all, ss, rs
):
    step = pl.program_id(0)
    hops = LineGather(w, length, ss, rs)

    @pl.when(step == 0)
    def _():
        greet(line_neighbours(length))
        if length > 2:
            hops.start(2)

    @pl.when(step == STEPS)
    def _():
        for hop in range(2, length - 1):
            hops.arrive(hop)
            hops.start(hop + 1)

    @pl.when(step < STEPS)
    def _():
        feed_forward(x, above, gate_up[...], down[...], hid, dboth)
        keep_units(step, hid_all, dboth_all, hid, dboth)

    @pl.when(step >= STEPS)
    def _():
        grads_compute(x_columns, above_columns, hid_all, dboth_all, gate_o, up_o, down_o)

    @pl.when(step == 2 * STEPS - 1)
    def _():
        hops.arrive(length - 1)
        hops.finish(2, length - 1)


def early_mlp(x, above, gate_up, down, w, length, collective_id):
    tokens, model = x.shape
    f = down.shape[1]
    rows, columns, grads = mlp_specs(tokens, model, f)
    grad_shape = jax.ShapeDtypeStruct((model, f), BF16)
    return pl.pallas_call(
        functools.partial(early_mlp_kernel, length),
        grid=(2 * STEPS,),
        out_shape=(
            jax.ShapeDtypeStruct((tokens, f), BF16),
            jax.ShapeDtypeStruct((tokens, 2 * f), BF16),
            grad_shape, grad_shape, grad_shape,
            jax.ShapeDtypeStruct(w.shape, w.dtype),
        ),
        in_specs=[rows(model), rows(model), columns, columns, resident(gate_up.shape), resident(down.shape), ANY],
        out_specs=(rows(f), rows(2 * f)) + (grads,) * 3 + (ANY,),
        scratch_shapes=[pltpu.VMEM((tokens, f), BF16), pltpu.VMEM((tokens, 2 * f), BF16)]
        + [DMA((2, length)), DMA((2, length))],
        input_output_aliases={6: 5},
        compiler_params=params(collective_id),
        cost_estimate=pl.CostEstimate(flops=12 * tokens * model * f, bytes_accessed=50 * 2**20, transcendentals=0),
    )(x, above, x, above, gate_up, down, w)


def late_mlp_kernel(
    length, cuts, x, above, x_columns, above_columns, hid_one, dboth_one, gate_up_in, down_in, late_in, *refs
):
    terms, refs = refs[: len(cuts)], refs[len(cuts) :]
    out, back, gate_o, up_o, down_o, sums, squares, *refs = refs
    gate_up, down, hid, dboth, hid_all, dboth_all, load_s, *line_refs = refs
    step = pl.program_id(0)
    line = LineScatter([(ref, *cut) for ref, cut in zip(terms, cuts)], length, *line_refs)
    f, g = hid_one.shape[1], hid.shape[1]
    loads = local_copies(
        (
            (late_in.at[:, pl.ds(0, 2 * g)], gate_up.at[:, pl.ds(2 * f, 2 * g)]),
            (late_in.at[:, pl.ds(2 * g, g)], down.at[:, pl.ds(f, g)]),
            (down_in, down.at[:, pl.ds(0, f)]),
            (gate_up_in, gate_up.at[:, pl.ds(0, 2 * f)]),
        ),
        load_s,
    )

    @pl.when(step == 0)
    def _():
        starts(loads)
        greet(line_neighbours(length))
        line.load((1,))
        line.start()
        line.load((*range(2, length), 0))
        waits(loads)

    for hop in range(2, length):

        @pl.when(step == min(2 * STEPS - 2, 2 * (hop - 1)))
        def _():
            line.next = hop
            line.start()

    @pl.when(step < STEPS)
    def _():
        feed_forward(x, above, gate_up[:, 2 * f :], down[:, f:], hid, dboth)
        keep_units(step, hid_all, dboth_all, hid, dboth)
        units = jnp.concatenate([hid_one[...], hid[...]], axis=1)
        out[...] = contract_last(units, down[...]).astype(BF16)
        units = jnp.concatenate([dboth_one[...], dboth[...]], axis=1)
        back[...] = contract_last(units, gate_up[...]).astype(BF16)

    @pl.when(step >= STEPS)
    def _():
        grads_compute(x_columns, above_columns, hid_all, dboth_all, gate_o, up_o, down_o)

    @pl.when(step == 2 * STEPS - 1)
    def _():
        squares[...] = jnp.zeros_like(squares)
        line.end(sums, 0, squares)


def late_mlp(x, above, early_units, gate_up, down, late, terms, cuts, length, collective_id):
    tokens, model = x.shape
    f, g = down.shape[1], late.shape[1] // 3
    line_rows = terms[0].shape[1]
    cut = sum(columns for _, columns in cuts)
    rows, columns, grads = mlp_specs(tokens, model, g)

    def whole(shape):
        return pl.BlockSpec(shape, lambda i: (0, 0))

    return pl.pallas_call(
        functools.partial(late_mlp_kernel, length, cuts),
        grid=(2 * STEPS,),
        out_shape=(jax.ShapeDtypeStruct((tokens, model), BF16),) * 2
        + (jax.ShapeDtypeStruct((model, g), BF16),) * 3
        + (jax.ShapeDtypeStruct((line_rows, cut), BF16), TILE),
        in_specs=[rows(model), rows(model), columns, columns, rows(f), rows(2 * f)]
        + [ANY] * (3 + len(terms)),
        out_specs=(rows(model),) * 2 + (grads,) * 3 + (whole((line_rows, cut)), whole((8, 128))),
        scratch_shapes=[
            pltpu.VMEM((model, 2 * f + 2 * g), BF16),
            pltpu.VMEM((model, f + g), BF16),
            pltpu.VMEM((tokens // STEPS, g), BF16),
            pltpu.VMEM((tokens // STEPS, 2 * g), BF16),
            pltpu.VMEM((tokens, g), BF16),
            pltpu.VMEM((tokens, 2 * g), BF16),
            DMA((4,)),
        ]
        + line_scratch(length, line_rows, cut, len(cuts)),
        compiler_params=params(collective_id),
        cost_estimate=pl.CostEstimate(
            flops=6 * tokens * model * (f + 3 * g), bytes_accessed=70 * 2**20, transcendentals=0
        ),
    )(x, above, x, above, *early_units, gate_up, down, late, *terms)


def adam_step(weight, grad, first, second, factor, rate, decay_rate):
    clipped = grad * factor
    first_new = beta_first * first + (1.0 - beta_first) * clipped
    second_new = beta_second * second + (1.0 - beta_second) * clipped * clipped
    first_hat = first_new / (1.0 - beta_first**STEP)
    second_hat = second_new / (1.0 - beta_second**STEP)
    weight_new = weight - rate * (
        first_hat / (jnp.sqrt(second_hat) + adam_eps) + decay_rate * weight
    )
    return (first_new, second_new, weight_new)


def small_steps(factor, refs, outs):
    gains_sum, gates_sum, *states = refs
    rows, columns = states[3].shape
    channels = lax.dot_general(
        unit(8).astype(F32), gates_sum[:rows, columns : columns + 8], (((1,), (1,)), ((), ())),
        precision=lax.Precision.HIGHEST, preferred_element_type=F32,
    )
    grads = gains_sum[...], gates_sum[:rows, :columns], channels
    rates = (rate_gains, 0.0), (rate_matrix, decay_matrix), (rate_channel, 0.0)
    for n in range(3):
        w, m, v = states[3 * n : 3 * n + 3]
        results = adam_step(w[...], grads[n], m[...], v[...], factor, *rates[n])
        for out, result in zip(outs[3 * n : 3 * n + 3], results):
            out[...] = result


def adam_kernel(sources, factor, *refs):
    states, refs = refs[: 3 * len(sources)], refs[3 * len(sources) :]
    count = sum(len(source) for source in sources)
    grads, small, refs = refs[:count], refs[count : count + 11], refs[count + 11 :]
    results, norm, outs = refs[:2], refs[2], refs[3:]
    for result, out in zip(results, outs[-3:]):
        out[...] = result[...]
    outs[-1][...] = norm[0:1, 0:1]
    one = factor[0:1, 0:1]
    pl.when(pl.program_id(0) == 0)(lambda: small_steps(one, small, outs[3 * len(sources) : -3]))
    for n, source in enumerate(sources):
        parts = []
        for pieces in source:
            ref, *grads = grads
            for first, columns, at, stride in pieces:
                for t in range(8):
                    parts.append((at + t * stride, columns, ref, t, first))
        parts.sort(key=lambda part: part[0])
        w, m, v = states[3 * n : 3 * n + 3]
        m_o, v_o, w_o = outs[3 * n : 3 * n + 3]
        run = []
        for at, columns, ref, t, first in parts:
            run.append((at, columns, ref[t, :, first : first + columns].astype(F32)))
            end = at + columns
            if end % 128:
                continue
            grad = jnp.concatenate([piece for _, _, piece in run], axis=1) if len(run) > 1 else run[0][2]
            cols = slice(run[0][0], end)
            run = []
            first_new, second_new, weight_new = adam_step(
                w[:, cols], grad, m[:, cols], v[:, cols], one, rate_matrix, decay_matrix
            )
            m_o[:, cols] = first_new
            v_o[:, cols] = second_new
            w_o[:, cols] = weight_new


def adam(matrices, small, factor, norm, passed):
    rows = matrices[0][0].shape[0]
    step = min(rows, 16)

    def block(v):
        return pl.BlockSpec((step, v.shape[1]), lambda i: (i, 0))

    def whole(v):
        return pl.BlockSpec(v.shape, lambda i: (0, 0))

    states = [v for matrix in matrices for v in matrix[:3]]
    grads = [g for matrix in matrices for g in matrix[3]]
    results = [*states, *small[2:], *passed]
    steps = rows // step

    def slab(v):
        return pl.BlockSpec((v.shape[0] // steps, v.shape[1]), lambda i: (i, 0))

    return pl.pallas_call(
        functools.partial(adam_kernel, [matrix[4] for matrix in matrices]),
        grid=(steps,),
        out_shape=tuple(jax.ShapeDtypeStruct(v.shape, v.dtype) for v in results)
        + (jax.ShapeDtypeStruct((1, 1), F32),),
        in_specs=[pl.BlockSpec((8, 128), lambda i: (0, 0))]
        + [block(v) for v in states]
        + [pl.BlockSpec((8, step, g.shape[2]), lambda i: (0, i, 0)) for g in grads]
        + [whole(v) for v in small]
        + [slab(v) for v in passed]
        + [whole(norm)],
        out_specs=tuple(block(v) for v in states)
        + tuple(whole(v) for v in small[2:])
        + tuple(slab(v) for v in passed)
        + (pl.BlockSpec((1, 1), lambda i: (0, 0)),),
        compiler_params=pltpu.CompilerParams(vmem_limit_bytes=VMEM_BYTES),
        cost_estimate=pl.CostEstimate(
            flops=0, bytes_accessed=sum(8 * v.size for v in states), transcendentals=0
        ),
    )(factor, *states, *grads, *small, *passed, norm)


def on_device(
    block_input,
    out_grad,
    norm_gains,
    mixer_weight,
    gate_weight,
    chan_params,
    mlp_weight,
    first_gains,
    first_mixer,
    first_gate,
    first_chan,
    first_mlp,
    second_gains,
    second_mixer,
    second_gate,
    second_chan,
    second_mlp,
):
    length = lax.axis_size("seq") // 2
    z = lax.axis_index("seq") // 2
    tokens, model = block_input.shape[1:]
    share = mixer_weight.shape[0]
    pair = 2 * share
    lru = mixer_weight.shape[1] // 3
    hidden = mlp_weight.shape[1] // 3
    r8, f8 = lru // 8, hidden // 8
    rc = -(-r8 // 128) * 128
    head = gate_weight.shape[1] // 2
    heads = r8 // head
    gate_rows = gate_weight.shape[0]
    gate_pad = -(-gate_rows // 16) * 16

    x = lax.axis_index("seq") - 2 * z
    batch = lax.axis_index("batch")
    plain = pair % 128 == 0

    def turned(v):
        if plain:
            return v
        v = v.reshape(v.shape[0], 4, length, pair).swapaxes(1, 2)
        return jnp.roll(v, -z, axis=1).reshape(v.shape[0], model)

    def turned_back(v):
        if plain:
            return v
        v = jnp.roll(v.reshape(v.shape[0], length, 4, pair), z, axis=1)
        return v.swapaxes(1, 2).reshape(v.shape[0], model)

    normed_one, mixer_full, mlp_gu, mlp_down, late, gains, gate, chan, inputs, above = first(
        turned(block_input[0]),
        turned(out_grad[0]),
        mixer_weight,
        mlp_weight,
        norm_gains,
        gate_weight,
        chan_params,
        rc,
        length,
        1,
    )
    normed_one = normed_one.reshape(8 * tokens, model)
    mixer_full = mixer_full.reshape(model, 3 * r8)
    mixed, *kept, grad_out, mlp_down = recur_forward(
        normed_one, mixer_full, gate, chan, above, mlp_down, length, 2
    )
    grad_out = grad_out.reshape(8 * tokens, model)
    mixed = mixed.reshape(8 * tokens, r8)
    residual, normed_two, mlp_gu, late = middle(mixed, mixer_full, inputs, gains, mlp_gu, late, length, 3)
    normed_two = normed_two.reshape(8 * tokens, model)
    h1 = early(f8)
    h2 = f8 - h1
    mlp_gu = mlp_gu.reshape(model, 2 * h1)
    mlp_down = mlp_down.reshape(model, h1)
    hid, dboth, *early_terms, late = early_mlp(normed_two, grad_out, mlp_gu, mlp_down, late, length, 9)
    gate_one, up_one, down_one = (v.reshape(length, 8 * share, h1) for v in early_terms)
    cut = h1 // 4
    mlp_part, dnormed_two, *late_terms, sums_zero, squares_zero = late_mlp(
        normed_two, grad_out, (hid, dboth), mlp_gu, mlp_down, late.reshape(model, 3 * h2),
        (gate_one, up_one), ((0, h1), (0, cut)), length, 11,
    )
    gate_two, up_two, down_two = (v.reshape(length, 8 * share, h2) for v in late_terms)

    grad_residual, gain_two, dmz, dmix, sums_one, squares_one = turn(
        dnormed_two, residual, above, gains, mixer_full, rc,
        (up_one, down_one, gate_two), ((0, cut, h1 - cut), (1, 0, h1), (2, 0, h2)),
        length, 4,
    )
    dmz = dmz.reshape(8 * tokens, model)
    span = 2 * tokens
    dmix = dmix.reshape(4, span, rc)
    sums_zero, sums_one = (v.reshape(8, share, v.shape[1]) for v in (sums_zero, sums_one))
    dproj, gate_back, sums_two, squares_two, back_zero, back_one = recur_backward(
        dmix, gate, chan, kept, r8, head, (sums_zero, sums_one),
        (up_two, down_two), ((0, 0, h2), (1, 0, h2)), length, 6,
    )
    dproj = dproj.reshape(4 * span, 2 * r8)
    input_grad, gain_one, gates_sum, block_output, back_two, mixer_early, mixer_sums, squares_three = closing(
        normed_one, dmz, dproj, mixed, mixer_full, mlp_part, residual, sums_two,
        inputs, grad_residual, gains, gate_back, length, 7,
    )
    mixer_back, gains_sum, norm, factor = last(
        mixer_sums.reshape(8, share, mixer_sums.shape[1]), gain_one, gain_two, gates_sum,
        (squares_zero, squares_one, squares_two, squares_three), length, 8,
    )
    split = mixer_early.shape[2]
    mlp_sources = (
        [(0, h1, 0, f8), (h1, cut, hidden, f8)],
        [
            (0, h1 - cut, hidden + cut, f8),
            (h1 - cut, h1, 2 * hidden, f8),
            (2 * h1 - cut, h2, h1, f8),
        ],
        [(0, h2, hidden + h1, f8), (h2, h2, 2 * hidden + h1, f8)],
    )
    states = adam(
        (
            (
                mixer_weight, first_mixer, second_mixer, (mixer_early, mixer_back),
                (
                    [(0, r8, 0, r8), (r8, split - r8, lru, r8)],
                    [(0, 2 * r8 - split, lru + split - r8, r8), (2 * r8 - split, r8, 2 * lru, r8)],
                ),
            ),
            (mlp_weight, first_mlp, second_mlp, (back_zero, back_one, back_two), mlp_sources),
        ),
        (
            gains_sum, gates_sum, norm_gains, first_gains, second_gains, gate_weight, first_gate, second_gate,
            chan_params, first_chan, second_chan,
        ),
        factor,
        norm,
        (block_output, input_grad),
    )
    *states, block_output, input_grad, norm = states
    mixer_up, mlp_up, gains_up, gate_up, chan_up = (states[3 * n : 3 * n + 3] for n in range(5))
    return (
        turned_back(block_output)[None],
        turned_back(input_grad)[None],
        norm.reshape(()),
        *gains_up,
        *mixer_up,
        *gate_up,
        *chan_up,
        *mlp_up,
    )


def solution(mesh):
    rows = P(("batch", "seq"), None)
    columns = P(None, ("batch", "seq"))
    data = P("batch", "seq", None)
    weights = (columns, rows, rows, columns, rows)
    in_specs = (data, data) + weights * 3
    triples = tuple(spec for spec in weights for _ in range(3))
    return jax.shard_map(
        on_device,
        mesh=mesh,
        in_specs=in_specs,
        out_specs=(data, data, P()) + triples,
        check_vma=False,
    )
```
